32 devices in a mesh: section: 2 (over x), dp: 16 (over z, y, core).
Axes of the slice: x: 2, y: 2, z: 4, core: 2. Of those that a mesh axis runs over, the one named last changes fastest.
Arguments:
- sources: bfloat16 [13824, 1024], P('dp'), may hold values from -6 to 6
- targets: bfloat16 [8192, 1024], P('dp'), may hold values from -6 to 6
- cotangent: bfloat16 [8192, 1024], P('dp'), may hold values from -6 to 6
- source_lengths: int32 [16, 2], P('dp'), may hold values from 48 to 768, as said below
- target_lengths: int32 [16, 2], P('dp'), may hold values from 128 to 256, as said below
- attn_qkv: bfloat16 [2, 1024, 3072], P('section'), may hold values from -0.1875 to 0.1875
- attn_out: bfloat16 [2, 1024, 1024], P('section'), may hold values from -0.75 to 0.75
- ffn_in: bfloat16 [2, 1024, 4096], P('section'), may hold values from -0.1875 to 0.1875
- ffn_out: bfloat16 [2, 4096, 1024], P('section'), may hold values from -0.09375 to 0.09375
- norm_gains: float32 [2, 2, 1024], P('section'), may hold values from 0.5 to 1.5
- prefix_pairs: bfloat16 [2, 2, 30, 1024], P('section'), may hold values from -6 to 6
- adapt_down: bfloat16 [2, 1024, 512], P('section'), may hold values from -0.1875 to 0.1875
- adapt_down_bias: float32 [2, 512], P('section'), may hold values from -3 to 3
- adapt_up: bfloat16 [2, 512, 1024], P('section'), may hold values from -0.0625 to 0.0625
- adapt_up_bias: float32 [2, 1024], P('section'), may hold values from -0.6 to 0.6
- cross_query: bfloat16 [1024, 1024], replicated, may hold values from -0.1875 to 0.1875
- cross_pairs: bfloat16 [1024, 2048], replicated, may hold values from -0.1875 to 0.1875
- cross_out: bfloat16 [1024, 1024], replicated, may hold values from -0.75 to 0.75
- cross_gain: float32 [1024], replicated, may hold values from 0.5 to 1.5
Outputs:
- decoder_output: bfloat16 [8192, 1024], P('dp', 'section')
- source_grad: bfloat16 [13824, 1024], P('dp', 'section')
- target_grad: bfloat16 [8192, 1024], P('dp', 'section')
- prefix_grad: float32 [2, 2, 30, 1024], P('section')
- down_grad: float32 [2, 1024, 512], P('section')
- down_bias_grad: float32 [2, 512], P('section')
- up_grad: float32 [2, 512, 1024], P('section')
- up_bias_grad: float32 [2, 1024], P('section')
The draws below stay inside these ranges and needn't reach their ends.
Inputs may be any that keep to these rules, and one draw needn't show every extreme that they name: `source_lengths`: row i holds data index i's lengths: the first column (long bucket) lies from 97 to 768 and equals 768 for some i; the second (short bucket) lies from 48 to 96 and equals 96 for some i. `target_lengths`: each column equals 256 for some row.
All inputs are finite; a program needn't handle non-finite values.
Results may differ from the reference program's by a relative error of at most 0.023.
Values may be sent and summed in bfloat16 or wider, within the bound.
A program may use at most 448 MiB of HBM per device.

```python
import jax
import jax.numpy as jnp
from jax import lax

D = 1024
FF = 4096
HD = 64
AD = 512
PRE = 30
SRC_LONG = 768
SRC_SHORT = 96
TGT = 256
SRC_DEV = 864
SOURCES = 13824
TARGETS = 8192
N_DP = 16


def bucket_lengths(key, low_end, high_end, most):
    drawn_values = jax.random.randint(key, (N_DP,), low_end, high_end + 1)
    chosen = jax.random.randint(jax.random.fold_in(key, 7), (), 0, N_DP)
    return drawn_values.at[chosen].set(most)


def draw_source_lengths(key, part):
    key = jax.random.fold_in(key, 11)
    long_part = bucket_lengths(jax.random.fold_in(key, 1), SRC_SHORT + 1, SRC_LONG, SRC_LONG)
    short_part = bucket_lengths(jax.random.fold_in(key, 2), SRC_SHORT // 2, SRC_SHORT, SRC_SHORT)
    return jnp.stack([long_part, short_part], 1).astype(jnp.int32)


def draw_target_lengths(key, part):
    key = jax.random.fold_in(key, 13)
    first_part = bucket_lengths(jax.random.fold_in(key, 1), TGT // 2, TGT, TGT)
    second_part = bucket_lengths(jax.random.fold_in(key, 2), TGT // 2, TGT, TGT)
    return jnp.stack([first_part, second_part], 1).astype(jnp.int32)


def shard_levels(stream_key, dims, pieces, low, top_value):
    def one(axis_at, blocks):
        draws = jax.random.uniform(jax.random.fold_in(jax.random.fold_in(stream_key, 6), axis_at), (blocks,), jnp.float32, low / len(pieces), top_value / len(pieces))
        return jnp.repeat(jnp.exp(draws), dims[axis_at] // blocks).reshape((-1,) + (1,) * (len(dims) - axis_at - 1))

    level = one(*pieces[0])
    for cut in pieces[1:]:
        level = level * one(*cut)
    return level


def bell_draw(own_key, shape, spread, bound, shards=(), kind=jnp.bfloat16):
    values = jax.random.normal(own_key, shape, jnp.float32) * spread
    if len(shards) > 0:
        values = shard_levels(own_key, shape, shards, -0.22, 0.18) * values
    return jnp.clip(values, min=-bound, max=bound).astype(kind)


def setup_inputs(seed: int = 0) -> dict:
    keys = jax.random.split(jax.random.key(seed), 20)
    return {
        "sources": bell_draw(keys[0], (SOURCES, D), 1.0, 6.0, ((0, 16),)),
        "targets": bell_draw(keys[1], (TARGETS, D), 1.0, 6.0, ((0, 16),)),
        "cotangent": bell_draw(keys[2], (TARGETS, D), 1.0, 6.0, ((0, 16),)),
        "source_lengths": draw_source_lengths(jax.random.fold_in(keys[19], 71), 0),
        "target_lengths": draw_target_lengths(jax.random.fold_in(keys[19], 71), 0),
        "attn_qkv": bell_draw(keys[5], (2, D, 3 * D), D ** -0.5, 0.1875, ((0, 2),)),
        "attn_out": bell_draw(keys[6], (2, D, D), (D // 16) ** -0.5, 0.75, ((0, 2),)),
        "ffn_in": bell_draw(keys[7], (2, D, FF), D ** -0.5, 0.1875, ((0, 2),)),
        "ffn_out": bell_draw(keys[8], (2, FF, D), FF ** -0.5, 0.09375, ((0, 2),)),
        "norm_gains": jnp.clip(1.0 + 0.1 * jax.random.normal(keys[9], (2, 2, D), jnp.float32), 0.5, 1.5),
        "prefix_pairs": bell_draw(keys[10], (2, 2, PRE, D), 1.0, 6.0, ((0, 2),)),
        "adapt_down": bell_draw(keys[11], (2, D, AD), D ** -0.5, 0.1875, ((0, 2),)),
        "adapt_down_bias": bell_draw(keys[12], (2, AD), 0.5, 3.0, ((0, 2),), jnp.float32),
        "adapt_up": bell_draw(keys[13], (2, AD, D), (16 * AD) ** -0.5, 0.0625, ((0, 2),)),
        "adapt_up_bias": bell_draw(keys[14], (2, D), 0.1, 0.6, ((0, 2),), jnp.float32),
        "cross_query": bell_draw(keys[15], (D, D), D ** -0.5, 0.1875),
        "cross_pairs": bell_draw(keys[16], (D, 2 * D), D ** -0.5, 0.1875),
        "cross_out": bell_draw(keys[17], (D, D), (D // 16) ** -0.5, 0.75),
        "cross_gain": jnp.clip(1.0 + 0.1 * jax.random.normal(keys[18], (D,), jnp.float32), 0.5, 1.5),
    }


@jax.custom_vjp
def low(v):
    return lax.optimization_barrier(v.astype(jnp.bfloat16)).astype(jnp.float32)

@jax.custom_vjp
def low_back(v):
    return v

def low_keep(v):
    return (low(v), None)

def low_pass(kept, grad):
    return (grad,)

def back_keep(v):
    return (v, None)

def back_low(kept, grad):
    return (low(grad),)
low.defvjp(low_keep, low_pass)
low_back.defvjp(back_keep, back_low)
precise = lax.Precision.HIGHEST
norm_eps = 1e-05
big_negative = -1e+30
adapter_scale = 4.0

def product(left_side, right_side):
    return jnp.dot(left_side, right_side, precision=precise)

def layer_norm(values, weight):
    centered = values - lax.optimization_barrier(jnp.mean(values, axis=-1, keepdims=True))
    return centered * lax.rsqrt(lax.optimization_barrier(jnp.mean(centered * centered, axis=-1, keepdims=True)) + norm_eps) * weight

def exact_gelu(values):
    return jax.nn.gelu(values, approximate=False)

def key_allowed(row_start, row_count, prefix_len, key_rows, length, causal):
    grid_shape = (row_count, prefix_len + key_rows)
    query_pos = row_start + lax.broadcasted_iota(jnp.int32, grid_shape, 0)
    key_pos = lax.broadcasted_iota(jnp.int32, grid_shape, 1) - prefix_len
    allowed = key_pos < length
    if causal:
        allowed = jnp.logical_and(allowed, key_pos <= query_pos)
    return allowed

def attend(queries, keys_all, values_all, prefix_len, length, causal):
    row_count = queries.shape[0]
    key_count = keys_all.shape[0]
    head_count = queries.shape[1] // HD
    query_heads = queries.reshape(row_count, head_count, HD)
    key_heads = keys_all.reshape(key_count, head_count, HD)
    value_heads = values_all.reshape(key_count, head_count, HD)
    raw_scores = low_back(jnp.einsum('qhd,khd->hqk', query_heads, key_heads, precision=precise))
    allowed = key_allowed(0, row_count, prefix_len, key_count - prefix_len, length, causal)
    scores = jnp.where(allowed[None], raw_scores * HD ** (-0.5), big_negative)
    soft_weights = low(jax.nn.softmax(scores, axis=-1))
    mixed_heads = jnp.einsum('hqk,khd->qhd', soft_weights, value_heads, precision=precise)
    return low_back(low(mixed_heads.reshape(row_count, head_count * HD)))

def self_block(tokens, length, causal, params):
    model_width = tokens.shape[1]
    qkv_rows = low_back(low(product(tokens, params['qkv'])))
    keys_all = jnp.concatenate([params['prefix'][0], qkv_rows[:, model_width:2 * model_width]], 0)
    values_all = jnp.concatenate([params['prefix'][1], qkv_rows[:, 2 * model_width:]], 0)
    attended = attend(qkv_rows[:, :model_width], keys_all, values_all, PRE, length, causal)
    return tokens + low_back(product(attended, params['out']))

def feed_forward(normed, params):
    normed_low = low(normed)
    hidden = low_back(product(normed_low, params['ffn_in']))
    active = low(exact_gelu(hidden))
    branch_out = low_back(product(active, params['ffn_out']))
    adapter_pre = low_back(product(normed_low, params['down']) + params['down_bias'])
    adapter_act = low(exact_gelu(adapter_pre))
    adapter_out = low_back(product(adapter_act, params['up']) + params['up_bias'])
    return normed + branch_out + adapter_scale * adapter_out

def encoder_layer(tokens, length, params):
    first_sum = self_block(tokens, length, False, params)
    normed = layer_norm(first_sum, params['gains'][0])
    second_sum = feed_forward(normed, params)
    return low_back(low(layer_norm(second_sum, params['gains'][1])))

def decoder_layer(targets, memory, target_len, source_len, params, cross_params):
    model_width = targets.shape[1]
    first_sum = self_block(targets, target_len, True, params)
    normed = layer_norm(first_sum, params['gains'][0])
    cross_queries = low_back(low(product(low(normed), cross_params['query'])))
    pair_rows = low_back(low(product(memory, cross_params['pairs'])))
    attended = attend(cross_queries, pair_rows[:, :model_width], pair_rows[:, model_width:], 0, source_len, False)
    second_sum = normed + low_back(product(attended, cross_params['out']))
    middle = layer_norm(second_sum, cross_params['gain'])
    third_sum = feed_forward(middle, params)
    final_norm = layer_norm(third_sum, params['gains'][1])
    valid_rows = lax.broadcasted_iota(jnp.int32, (targets.shape[0], 1), 0) < target_len
    return jnp.where(valid_rows, final_norm, 0.0)

def joined(frozen_part, trained_part):
    return dict(list(frozen_part.items()) + list(trained_part.items()))

def reference(sources, targets, cotangent, source_lengths, target_lengths, attn_qkv, attn_out, ffn_in, ffn_out, norm_gains, prefix_pairs, adapt_down, adapt_down_bias, adapt_up, adapt_up_bias, cross_query, cross_pairs, cross_out, cross_gain):
    frozen = [dict(qkv=attn_qkv[section_index].astype(jnp.float32), out=attn_out[section_index].astype(jnp.float32), ffn_in=ffn_in[section_index].astype(jnp.float32), ffn_out=ffn_out[section_index].astype(jnp.float32), gains=norm_gains[section_index].astype(jnp.float32)) for section_index in range(2)]
    trained = [dict(prefix=prefix_pairs[section_index].astype(jnp.float32), down=adapt_down[section_index].astype(jnp.float32), down_bias=adapt_down_bias[section_index].astype(jnp.float32), up=adapt_up[section_index].astype(jnp.float32), up_bias=adapt_up_bias[section_index].astype(jnp.float32)) for section_index in range(2)]
    cross_params = dict(query=cross_query.astype(jnp.float32), pairs=cross_pairs.astype(jnp.float32), out=cross_out.astype(jnp.float32), gain=cross_gain.astype(jnp.float32))

    def device_step(grad_totals, inputs):
        source_rows, target_rows, cot_rows, source_len, target_len = inputs
        outputs, target_grads, source_grads = ([], [], [])
        offset = 0
        for bucket, row_count in enumerate((SRC_LONG, SRC_SHORT)):
            source_part = source_rows[offset:offset + row_count].astype(jnp.float32)
            offset = offset + row_count
            target_part = target_rows[bucket * TGT:(bucket + 1) * TGT].astype(jnp.float32)
            cot_part = cot_rows[bucket * TGT:(bucket + 1) * TGT].astype(jnp.float32)

            def forward(source_in, target_in, encoder_trained, decoder_trained):
                memory = encoder_layer(source_in, source_len[bucket], joined(frozen[0], encoder_trained))
                return decoder_layer(target_in, memory, target_len[bucket], source_len[bucket], joined(frozen[1], decoder_trained), cross_params)
            result, pull_back = jax.vjp(forward, source_part, target_part, trained[0], trained[1])
            source_grad, target_grad, encoder_grad, decoder_grad = pull_back(cot_part)
            grad_totals = jax.tree.map(jnp.add, grad_totals, (encoder_grad, decoder_grad))
            outputs.append(result)
            target_grads.append(target_grad)
            source_grads.append(source_grad)
        return (grad_totals, (jnp.concatenate(outputs, 0), jnp.concatenate(target_grads, 0), jnp.concatenate(source_grads, 0)))
    initial = jax.tree.map(jnp.zeros_like, (trained[0], trained[1]))
    scanned_inputs = (sources.reshape(N_DP, SRC_DEV, D), targets.reshape(N_DP, 2 * TGT, D), cotangent.reshape(N_DP, 2 * TGT, D), source_lengths, target_lengths)
    grad_totals, stacked = lax.scan(device_step, initial, scanned_inputs)
    encoder_total, decoder_total = grad_totals
    decoder_output = stacked[0].reshape(TARGETS, D).astype(jnp.bfloat16)
    target_grad = stacked[1].reshape(TARGETS, D).astype(jnp.bfloat16)
    source_grad = stacked[2].reshape(SOURCES, D).astype(jnp.bfloat16)
    prefix_grad = jnp.stack([encoder_total['prefix'], decoder_total['prefix']]) / N_DP
    down_grad = jnp.stack([encoder_total['down'], decoder_total['down']]) / N_DP
    down_bias_grad = jnp.stack([encoder_total['down_bias'], decoder_total['down_bias']]) / N_DP
    up_grad = jnp.stack([encoder_total['up'], decoder_total['up']]) / N_DP
    up_bias_grad = jnp.stack([encoder_total['up_bias'], decoder_total['up_bias']]) / N_DP
    return (decoder_output, source_grad, target_grad, prefix_grad, down_grad, down_bias_grad, up_grad, up_bias_grad)
```

```python
import functools

import jax
import jax.numpy as jnp
from jax import lax
from jax.experimental import pallas as pl
from jax.experimental.pallas import tpu as pltpu
from jax.sharding import PartitionSpec as P

HD = 64
PRE = 30
PRE_PAD = 32
SRC_LONG = 768
SRC_SHORT = 96
TGT = 256
LANES = 128

BF = jnp.bfloat16
F32 = jnp.float32
norm_eps = 1e-05
big_negative = -1e30
adapter_scale = 4.0
chunk = 512
vmem_bytes = 56 * 2**20

phi_poly = (
    0.797869713181688,
    0.036392283539041996,
    -8.782472977701046e-05,
    -3.669384069669515e-05,
    1.4250308145882202e-06,
)


def nn(left, right):
    return lax.dot_general(left, right, (((1,), (0,)), ((), ())), preferred_element_type=F32)


def nt(left, right):
    return lax.dot_general(left, right, (((1,), (1,)), ((), ())), preferred_element_type=F32)


def tn(left, right):
    return lax.dot_general(left, right, (((0,), (0,)), ((), ())), preferred_element_type=F32)


def gelu_pair(values):
    square = values * values
    poly = phi_poly[4]
    for coefficient in phi_poly[3::-1]:
        poly = poly * square + coefficient
    half = 0.5 * jnp.tanh(values * poly) + 0.5
    density = jnp.exp(square * -0.5) * 0.3989422804014327
    return values * half, half + values * density


def row_tiles(rows, most=288):
    count = -(-rows // most)
    size = rows // count
    return [(i * size, size) for i in range(count)]


def norm_rows(values):
    centered = values - jnp.mean(values, axis=-1, keepdims=True)
    scale = lax.rsqrt(jnp.mean(centered * centered, axis=-1, keepdims=True) + norm_eps)
    return centered * scale, scale


def norm_rows_back(hat, scale, grad_hat):
    mean_grad = jnp.mean(grad_hat, axis=-1, keepdims=True)
    mean_dot = jnp.mean(grad_hat * hat, axis=-1, keepdims=True)
    return scale * (grad_hat - mean_grad - hat * mean_dot)


def params(limit=vmem_bytes):
    return pltpu.CompilerParams(vmem_limit_bytes=limit)


def whole(shape):
    return pl.BlockSpec(shape, lambda *g: (0,) * len(shape))


def product_kernel(x_ref, w_ref, o_ref):
    o_ref[...] = nn(x_ref[...], w_ref[...]).astype(BF)


def product(x, w, tile=512):
    rows, depth = x.shape
    width = w.shape[1]
    return pl.pallas_call(
        product_kernel,
        grid=(width // tile,),
        in_specs=[whole((rows, depth)), pl.BlockSpec((depth, tile), lambda i: (0, i))],
        out_specs=pl.BlockSpec((rows, tile), lambda i: (0, i)),
        out_shape=jax.ShapeDtypeStruct((rows, width), BF),
        compiler_params=params(),
        name="product",
    )(x, w)


def back_product_kernel(*refs, parts, residual):
    grads = refs[:parts]
    w_ref = refs[parts]
    o_ref = refs[-1]
    total = None
    width = grads[0].shape[1]
    for i, grad in enumerate(grads):
        term = nt(grad[...], w_ref[:, i * width : (i + 1) * width])
        total = term if total is None else total + term
    if residual:
        total = total + refs[parts + 1][...]
    o_ref[...] = total.astype(BF)


def back_product(grads, w, residual=None, tile=256):
    rows, width = grads[0].shape
    depth = w.shape[0]
    parts = len(grads)
    specs = [whole((rows, width))] * parts + [
        pl.BlockSpec((tile, parts * width), lambda i: (i, 0))
    ]
    args = list(grads) + [w]
    if residual is not None:
        specs.append(pl.BlockSpec((rows, tile), lambda i: (0, i)))
        args.append(residual)
    return pl.pallas_call(
        functools.partial(back_product_kernel, parts=parts, residual=residual is not None),
        grid=(depth // tile,),
        in_specs=specs,
        out_specs=pl.BlockSpec((rows, tile), lambda i: (0, i)),
        out_shape=jax.ShapeDtypeStruct((rows, depth), BF),
        compiler_params=params(),
        name="back_product",
    )(*args)


def head_lanes(head):
    lane = lax.broadcasted_iota(jnp.int32, (1, LANES), 1)
    own = (lane < HD) if head == 0 else (lane >= HD)
    first = HD if head == 0 else 0
    return own, lane == first, lane == first + 1


def bf(value):
    return jnp.asarray(value, BF)


def stacked(rows_ref, prefix_ref, start, count):
    rows = rows_ref[start : start + count]
    if prefix_ref is None:
        return rows
    return jnp.concatenate([rows, prefix_ref[...]], 0)


def attend_kernel(*refs, segs, prefix, causal):
    len_ref, q_ref, k_ref, v_ref = refs[:4]
    at = 4
    pk_ref = pv_ref = None
    if prefix:
        pk_ref, pv_ref = refs[4:6]
        at = 6
    o_ref, inv_ref = refs[at : at + 2]
    p_refs = refs[at + 2 :]
    for seg, (q0, nq, k0, nk) in enumerate(segs):
        keys = stacked(k_ref, pk_ref, k0, nk)
        values = stacked(v_ref, pv_ref, k0, nk)
        count = keys.shape[0]
        row = lax.broadcasted_iota(jnp.int32, (count, 1), 0)
        seen = row < jnp.minimum(len_ref[0, seg], nk)
        if prefix:
            seen = seen | ((row >= nk) & (row < nk + PRE))
        queries = q_ref[q0 : q0 + nq] * bf(HD**-0.5)
        out = inv = None
        for head in range(2):
            own, first, _ = head_lanes(head)
            k_own = jnp.where(own, keys, jnp.where(first & ~seen, bf(big_negative), bf(0)))
            q_own = jnp.where(own, queries, jnp.where(first, bf(1), bf(0)))
            v_own = jnp.where(own, values, bf(1))
            scores = nt(k_own, q_own)
            if causal:
                key_at = lax.broadcasted_iota(jnp.int32, scores.shape, 0)
                query_at = lax.broadcasted_iota(jnp.int32, scores.shape, 1)
                allowed = (key_at <= query_at) | (key_at >= nk)
                scores = jnp.where(allowed, scores, big_negative)
            peak = jnp.max(scores, axis=0, keepdims=True)
            weights = jnp.exp(scores - peak).astype(BF)
            p_refs[seg][head] = weights
            mixed = tn(weights, v_own)
            inverse = 1.0 / pltpu.roll(mixed, HD, 1)
            mixed = mixed * inverse
            out = mixed if out is None else jnp.where(own, mixed, out)
            inv = inverse if inv is None else jnp.where(own, inverse, inv)
        o_ref[q0 : q0 + nq] = out.astype(BF)
        inv_ref[q0 : q0 + nq] = inv


def column_spec(rows, offset):
    return pl.BlockSpec((rows, LANES), lambda h: (0, h + offset))


def attend(lengths, q, k, v, prefixes, segs, causal):
    pairs = 8
    q_rows, k_rows = q[0].shape[0], k[0].shape[0]
    prefix = prefixes is not None
    extra = PRE_PAD if prefix else 0
    specs = [
        pl.BlockSpec(memory_space=pltpu.SMEM),
        column_spec(q_rows, q[1]),
        column_spec(k_rows, k[1]),
        column_spec(k_rows, v[1]),
    ]
    args = [lengths, q[0], k[0], v[0]]
    if prefix:
        specs += [column_spec(PRE_PAD, 0)] * 2
        args += list(prefixes)
    weight_shapes = [(2 * pairs, nk + extra, nq) for _, nq, _, nk in segs]
    return pl.pallas_call(
        functools.partial(attend_kernel, segs=segs, prefix=prefix, causal=causal),
        grid=(pairs,),
        in_specs=specs,
        out_specs=[column_spec(q_rows, 0), column_spec(q_rows, 0)]
        + [pl.BlockSpec((2,) + s[1:], lambda h: (h, 0, 0)) for s in weight_shapes],
        out_shape=[
            jax.ShapeDtypeStruct((q_rows, pairs * LANES), BF),
            jax.ShapeDtypeStruct((q_rows, pairs * LANES), F32),
        ]
        + [jax.ShapeDtypeStruct(s, BF) for s in weight_shapes],
        compiler_params=params(),
        name="attend",
    )(*args)


def attend_back_kernel(*refs, segs, prefix):
    q_ref, k_ref, v_ref, o_ref, inv_ref, g_ref = refs[:6]
    at = 6
    pk_ref = pv_ref = None
    if prefix:
        pk_ref, pv_ref = refs[6:8]
        at = 8
    p_refs = refs[at : at + len(segs)]
    outs = refs[at + len(segs) :]
    dq_ref, dk_ref, dv_ref = outs[:3]
    prefix_totals = [None, None]
    scale = HD**-0.5
    for seg, (q0, nq, k0, nk) in enumerate(segs):
        keys = stacked(k_ref, pk_ref, k0, nk)
        values = stacked(v_ref, pv_ref, k0, nk)
        queries = q_ref[q0 : q0 + nq]
        grads = g_ref[q0 : q0 + nq].astype(F32) * inv_ref[q0 : q0 + nq]
        grads_low = grads.astype(BF)
        dots = grads * o_ref[q0 : q0 + nq].astype(F32)
        dq = dk = dv = None
        for head in range(2):
            own, first, second = head_lanes(head)
            row_dot = -jnp.sum(jnp.where(own, dots, 0.0), axis=1, keepdims=True)
            high = row_dot.astype(BF)
            rest = (row_dot - high.astype(F32)).astype(BF)
            g_own = jnp.where(
                own, grads_low, jnp.where(first, high, jnp.where(second, rest, bf(0)))
            )
            v_own = jnp.where(own, values, jnp.where(first | second, bf(1), bf(0)))
            weights = p_refs[seg][head]
            score_grad = (weights.astype(F32) * nt(v_own, g_own)).astype(BF)
            dv_head = nn(weights, grads_low)
            dk_head = nn(score_grad, queries)
            dq_head = tn(score_grad, keys)
            dq = dq_head if dq is None else jnp.where(own, dq_head, dq)
            dk = dk_head if dk is None else jnp.where(own, dk_head, dk)
            dv = dv_head if dv is None else jnp.where(own, dv_head, dv)
        dk = dk * scale
        dq_ref[q0 : q0 + nq] = (dq * scale).astype(BF)
        dk_ref[k0 : k0 + nk] = dk[:nk].astype(BF)
        dv_ref[k0 : k0 + nk] = dv[:nk].astype(BF)
        if prefix:
            for i, grad in enumerate((dk, dv)):
                part = grad[nk:]
                prefix_totals[i] = part if seg == 0 else prefix_totals[i] + part
    if prefix:
        outs[3][...] = prefix_totals[0]
        outs[4][...] = prefix_totals[1]


def attend_back(q, k, v, prefixes, attended, inverse, grad, weights, segs):
    pairs = 8
    q_rows, k_rows = q[0].shape[0], k[0].shape[0]
    prefix = prefixes is not None
    specs = [
        column_spec(q_rows, q[1]),
        column_spec(k_rows, k[1]),
        column_spec(k_rows, v[1]),
        column_spec(q_rows, 0),
        column_spec(q_rows, 0),
        column_spec(q_rows, 0),
    ]
    args = [q[0], k[0], v[0], attended, inverse, grad]
    if prefix:
        specs += [column_spec(PRE_PAD, 0)] * 2
        args += list(prefixes)
    specs += [pl.BlockSpec((2,) + w.shape[1:], lambda h: (h, 0, 0)) for w in weights]
    args += list(weights)
    out_specs = [column_spec(q_rows, 0), column_spec(k_rows, 0), column_spec(k_rows, 0)]
    out_shape = [
        jax.ShapeDtypeStruct((q_rows, pairs * LANES), BF),
        jax.ShapeDtypeStruct((k_rows, pairs * LANES), BF),
        jax.ShapeDtypeStruct((k_rows, pairs * LANES), BF),
    ]
    if prefix:
        out_specs += [column_spec(PRE_PAD, 0)] * 2
        out_shape += [jax.ShapeDtypeStruct((PRE_PAD, pairs * LANES), F32)] * 2
    return pl.pallas_call(
        functools.partial(attend_back_kernel, segs=segs, prefix=prefix),
        grid=(pairs,),
        in_specs=specs,
        out_specs=out_specs,
        out_shape=out_shape,
        compiler_params=params(),
        name="attend_back",
    )(*args)


def ffn_step(low_ref, acc_ref, in_ref, out_ref, slope_ref, act_ref, bias_ref, scale):
    for start, size in row_tiles(low_ref.shape[0]):
        rows = slice(start, start + size)
        hidden = nn(low_ref[rows], in_ref[...])
        if bias_ref is not None:
            hidden = hidden + bias_ref[...]
        active, slope = gelu_pair(hidden)
        slope_ref[rows] = slope.astype(BF)
        active = active.astype(BF)
        if act_ref is not None:
            act_ref[rows] = active
        term = nn(active, out_ref[...])
        acc_ref[rows] += term if scale is None else scale * term


def enc_ffn_kernel(
    x_ref, att_ref, wo_ref, gain_ref, in_ref, out_ref, down_ref, downb_ref, up_ref, upb_ref,
    mem_ref, slope_ref, act_ref, low_ref, scales_ref, acc_ref,
):
    step = pl.program_id(0)
    last = pl.num_programs(0) - 1

    @pl.when(step == 0)
    def _():
        for start, size in row_tiles(x_ref.shape[0]):
            rows = slice(start, start + size)
            first = x_ref[rows].astype(F32) + nn(att_ref[rows], wo_ref[...])
            hat, scale = norm_rows(first)
            normed = hat * gain_ref[0:1]
            acc_ref[rows] = normed
            low_ref[rows] = normed.astype(BF)
            scales_ref[rows, 0:1] = scale

    @pl.when((step > 0) & (step < last))
    def _():
        ffn_step(low_ref, acc_ref, in_ref, out_ref, slope_ref, None, None, None)

    @pl.when(step == last)
    def _():
        ffn_step(low_ref, acc_ref, down_ref, up_ref, slope_ref, act_ref, downb_ref, adapter_scale)
        for start, size in row_tiles(x_ref.shape[0]):
            rows = slice(start, start + size)
            hat, scale = norm_rows(acc_ref[rows] + adapter_scale * upb_ref[...])
            mem_ref[rows] = (hat * gain_ref[1:2]).astype(BF)
            scales_ref[rows, 1:2] = scale


def enc_ffn(x, att, w):
    rows, width = x.shape
    hidden = w["ffn_in"].shape[1]
    steps = hidden // chunk

    def at(i):
        return jnp.clip(i - 1, 0, steps - 1)

    return pl.pallas_call(
        enc_ffn_kernel,
        grid=(steps + 2,),
        in_specs=[
            whole((rows, width)),
            whole((rows, width)),
            whole((width, width)),
            whole((2, width)),
            pl.BlockSpec((width, chunk), lambda i: (0, at(i))),
            pl.BlockSpec((chunk, width), lambda i: (at(i), 0)),
            whole((width, chunk)),
            whole((1, chunk)),
            whole((chunk, width)),
            whole((1, width)),
        ],
        out_specs=[
            whole((rows, width)),
            pl.BlockSpec((rows, chunk), lambda i: (0, jnp.clip(i - 1, 0, steps))),
            whole((rows, chunk)),
            whole((rows, width)),
            whole((rows, LANES)),
        ],
        out_shape=[
            jax.ShapeDtypeStruct((rows, width), BF),
            jax.ShapeDtypeStruct((rows, hidden + chunk), BF),
            jax.ShapeDtypeStruct((rows, chunk), BF),
            jax.ShapeDtypeStruct((rows, width), BF),
            jax.ShapeDtypeStruct((rows, LANES), F32),
        ],
        scratch_shapes=[pltpu.VMEM((rows, width), F32)],
        compiler_params=params(),
        name="enc_ffn",
    )(
        x, att, w["out"], w["gains"], w["ffn_in"], w["ffn_out"],
        w["down"], w["down_bias"], w["up"], w["up_bias"],
    )


def ffn_back_step(grad_ref, acc_ref, in_ref, out_ref, slope_ref):
    for start, size in row_tiles(grad_ref.shape[0]):
        rows = slice(start, start + size)
        pre = (nt(grad_ref[rows], out_ref[...]) * slope_ref[rows].astype(F32)).astype(BF)
        acc_ref[rows] += nt(pre, in_ref[...])


def adapter_back(grad_ref, acc_ref, low_ref, act_ref, slope_ref, down_ref, up_ref, outs, pre_ref):
    ddown_ref, ddownb_ref, dup_ref, dupb_ref = outs
    total = None
    for start, size in row_tiles(grad_ref.shape[0]):
        rows = slice(start, start + size)
        back = adapter_scale * nt(grad_ref[rows], up_ref[...])
        pre = (back * slope_ref[rows].astype(F32)).astype(BF)
        pre_ref[rows] = pre
        sums = jnp.sum(pre.astype(F32), axis=0, keepdims=True)
        total = sums if total is None else total + sums
        acc_ref[rows] += nt(pre, down_ref[...])
    ddownb_ref[...] = total
    ddown_ref[...] = tn(low_ref[...], pre_ref[...])
    dup_ref[...] = adapter_scale * tn(act_ref[...], grad_ref[...])
    dupb_ref[...] = adapter_scale * jnp.sum(grad_ref[...].astype(F32), axis=0, keepdims=True)


def enc_ffn_back_kernel(
    dmem_ref, mem_ref, low_ref, scales_ref, gain_ref, slope_ref, act_ref,
    in_ref, out_ref, down_ref, up_ref, wo_ref,
    dfirst_ref, datt_ref, ddown_ref, ddownb_ref, dup_ref, dupb_ref,
    acc_ref, grad_ref, pre_ref,
):
    step = pl.program_id(0)
    last = pl.num_programs(0) - 1

    @pl.when(step == 0)
    def _():
        for start, size in row_tiles(dmem_ref.shape[0]):
            rows = slice(start, start + size)
            gain = gain_ref[1:2]
            hat = mem_ref[rows].astype(F32) / gain
            grad = norm_rows_back(
                hat, scales_ref[rows, 1:2], dmem_ref[rows].astype(F32) * gain
            )
            acc_ref[rows] = grad
            grad_ref[rows] = grad.astype(BF)
        adapter_back(
            grad_ref, acc_ref, low_ref, act_ref, slope_ref, down_ref, up_ref,
            (ddown_ref, ddownb_ref, dup_ref, dupb_ref), pre_ref,
        )

    @pl.when(step > 0)
    def _():
        ffn_back_step(grad_ref, acc_ref, in_ref, out_ref, slope_ref)

    @pl.when(step == last)
    def _():
        for start, size in row_tiles(dmem_ref.shape[0]):
            rows = slice(start, start + size)
            gain = gain_ref[0:1]
            hat = low_ref[rows].astype(F32) / gain
            grad = norm_rows_back(hat, scales_ref[rows, 0:1], acc_ref[rows] * gain)
            dfirst_ref[rows] = grad
            datt_ref[rows] = nt(grad.astype(BF), wo_ref[...]).astype(BF)


def enc_ffn_back(dmem, mem, low, scales, slope, act, w):
    rows, width = dmem.shape
    hidden = w["ffn_in"].shape[1]
    steps = hidden // chunk

    def at(i):
        return jnp.clip(i - 1, 0, steps - 1)

    return pl.pallas_call(
        enc_ffn_back_kernel,
        grid=(steps + 1,),
        in_specs=[
            whole((rows, width)),
            whole((rows, width)),
            whole((rows, width)),
            whole((rows, LANES)),
            whole((2, width)),
            pl.BlockSpec((rows, chunk), lambda i: (0, jnp.where(i == 0, steps, i - 1))),
            whole((rows, chunk)),
            pl.BlockSpec((width, chunk), lambda i: (0, at(i))),
            pl.BlockSpec((chunk, width), lambda i: (at(i), 0)),
            whole((width, chunk)),
            whole((chunk, width)),
            whole((width, width)),
        ],
        out_specs=[
            whole((rows, width)),
            whole((rows, width)),
            whole((width, chunk)),
            whole((1, chunk)),
            whole((chunk, width)),
            whole((1, width)),
        ],
        out_shape=[
            jax.ShapeDtypeStruct((rows, width), F32),
            jax.ShapeDtypeStruct((rows, width), BF),
            jax.ShapeDtypeStruct((width, chunk), F32),
            jax.ShapeDtypeStruct((1, chunk), F32),
            jax.ShapeDtypeStruct((chunk, width), F32),
            jax.ShapeDtypeStruct((1, width), F32),
        ],
        scratch_shapes=[
            pltpu.VMEM((rows, width), F32),
            pltpu.VMEM((rows, width), BF),
            pltpu.VMEM((rows, chunk), BF),
        ],
        compiler_params=params(),
        name="enc_ffn_back",
    )(
        dmem, mem, low, scales, w["gains"], slope, act,
        w["ffn_in"], w["ffn_out"], w["down"], w["up"], w["out"],
    )


def dec_mid_kernel(x_ref, att_ref, wo_ref, gain_ref, wq_ref, n_ref, scale_ref, cq_ref):
    for start, size in row_tiles(x_ref.shape[0], 256):
        rows = slice(start, start + size)
        first = x_ref[rows].astype(F32) + nn(att_ref[rows], wo_ref[...])
        hat, scale = norm_rows(first)
        normed = hat * gain_ref[0:1]
        n_ref[rows] = normed
        scale_ref[rows, 0:1] = scale
        cq_ref[rows] = nn(normed.astype(BF), wq_ref[...]).astype(BF)


def dec_mid(x, att, w, cross):
    rows, width = x.shape
    return pl.pallas_call(
        dec_mid_kernel,
        out_shape=[
            jax.ShapeDtypeStruct((rows, width), F32),
            jax.ShapeDtypeStruct((rows, LANES), F32),
            jax.ShapeDtypeStruct((rows, width), BF),
        ],
        compiler_params=params(),
        name="dec_mid",
    )(x, att, w["out"], w["gains"], cross["query"])


def dec_ffn_kernel(
    len_ref, n_ref, catt_ref, cot_ref, wco_ref, cgain_ref, gain_ref,
    in_ref, out_ref, down_ref, downb_ref, up_ref, upb_ref,
    y_ref, dsecond_ref, dcatt_ref, ddown_ref, ddownb_ref, dup_ref, dupb_ref,
    acc_ref, low_ref, grad_ref, slope_ref, act_ref, pre_ref, scale_ref,
    *, steps,
):
    step = pl.program_id(0)
    tiles = row_tiles(n_ref.shape[0], TGT)

    @pl.when(step == 0)
    def _():
        for start, size in tiles:
            rows = slice(start, start + size)
            second = n_ref[rows] + nn(catt_ref[rows], wco_ref[...])
            hat, scale = norm_rows(second)
            middle = hat * cgain_ref[...]
            acc_ref[rows] = middle
            low_ref[rows] = middle.astype(BF)
            scale_ref[rows, 0:1] = scale

    @pl.when((step > 0) & (step <= steps))
    def _():
        ffn_step(low_ref, acc_ref, in_ref, out_ref, slope_ref.at[step - 1], None, None, None)

    @pl.when(step == steps + 1)
    def _():
        ffn_step(
            low_ref, acc_ref, down_ref, up_ref, slope_ref.at[steps], act_ref, downb_ref,
            adapter_scale,
        )
        for tile, (start, size) in enumerate(tiles):
            rows = slice(start, start + size)
            gain = gain_ref[1:2]
            hat, scale = norm_rows(acc_ref[rows] + adapter_scale * upb_ref[...])
            valid = lax.broadcasted_iota(jnp.int32, (size, 1), 0) < len_ref[0, tile]
            y_ref[rows] = jnp.where(valid, hat * gain, 0.0).astype(BF)
            cot = jnp.where(valid, cot_ref[rows].astype(F32), 0.0)
            grad = norm_rows_back(hat, scale, cot * gain)
            acc_ref[rows] = grad
            grad_ref[rows] = grad.astype(BF)
        adapter_back(
            grad_ref, acc_ref, low_ref, act_ref, slope_ref.at[steps], down_ref, up_ref,
            (ddown_ref, ddownb_ref, dup_ref, dupb_ref), pre_ref,
        )

    @pl.when(step > steps + 1)
    def _():
        ffn_back_step(grad_ref, acc_ref, in_ref, out_ref, slope_ref.at[2 * steps + 1 - step])

    @pl.when(step == 2 * steps + 1)
    def _():
        for start, size in tiles:
            rows = slice(start, start + size)
            gain = cgain_ref[...]
            hat = low_ref[rows].astype(F32) / gain
            grad = norm_rows_back(hat, scale_ref[rows, 0:1], acc_ref[rows] * gain)
            dsecond_ref[rows] = grad
            dcatt_ref[rows] = nt(grad.astype(BF), wco_ref[...]).astype(BF)


def dec_ffn(lengths, n, catt, cot, w, cross):
    rows, width = n.shape
    hidden = w["ffn_in"].shape[1]
    steps = hidden // chunk

    def at(i):
        return jnp.where(i <= steps, jnp.clip(i - 1, 0, steps - 1), jnp.clip(2 * steps + 1 - i, 0, steps - 1))

    return pl.pallas_call(
        functools.partial(dec_ffn_kernel, steps=steps),
        grid=(2 * steps + 2,),
        in_specs=[
            pl.BlockSpec(memory_space=pltpu.SMEM),
            whole((rows, width)),
            whole((rows, width)),
            whole((rows, width)),
            whole((width, width)),
            whole((1, width)),
            whole((2, width)),
            pl.BlockSpec((width, chunk), lambda i: (0, at(i))),
            pl.BlockSpec((chunk, width), lambda i: (at(i), 0)),
            whole((width, chunk)),
            whole((1, chunk)),
            whole((chunk, width)),
            whole((1, width)),
        ],
        out_specs=[
            whole((rows, width)),
            whole((rows, width)),
            whole((rows, width)),
            whole((width, chunk)),
            whole((1, chunk)),
            whole((chunk, width)),
            whole((1, width)),
        ],
        out_shape=[
            jax.ShapeDtypeStruct((rows, width), BF),
            jax.ShapeDtypeStruct((rows, width), F32),
            jax.ShapeDtypeStruct((rows, width), BF),
            jax.ShapeDtypeStruct((width, chunk), F32),
            jax.ShapeDtypeStruct((1, chunk), F32),
            jax.ShapeDtypeStruct((chunk, width), F32),
            jax.ShapeDtypeStruct((1, width), F32),
        ],
        scratch_shapes=[
            pltpu.VMEM((rows, width), F32),
            pltpu.VMEM((rows, width), BF),
            pltpu.VMEM((rows, width), BF),
            pltpu.VMEM((steps + 1, rows, chunk), BF),
            pltpu.VMEM((rows, chunk), BF),
            pltpu.VMEM((rows, chunk), BF),
            pltpu.VMEM((rows, LANES), F32),
        ],
        compiler_params=params(),
        name="dec_ffn",
    )(
        lengths, n, catt, cot, cross["out"], cross["gain"], w["gains"],
        w["ffn_in"], w["ffn_out"], w["down"], w["down_bias"], w["up"], w["up_bias"],
    )


def dec_mid_back_kernel(
    dsecond_ref, dcq_ref, wq_ref, n_ref, scale_ref, gain_ref, wo_ref, dfirst_ref, datt_ref
):
    for start, size in row_tiles(n_ref.shape[0], 256):
        rows = slice(start, start + size)
        gain = gain_ref[0:1]
        total = dsecond_ref[rows] + nt(dcq_ref[rows], wq_ref[...])
        grad = norm_rows_back(n_ref[rows] / gain, scale_ref[rows, 0:1], total * gain)
        dfirst_ref[rows] = grad
        datt_ref[rows] = nt(grad.astype(BF), wo_ref[...]).astype(BF)


def dec_mid_back(dsecond, dcq, n, scale, w, cross):
    rows, width = n.shape
    return pl.pallas_call(
        dec_mid_back_kernel,
        out_shape=[
            jax.ShapeDtypeStruct((rows, width), F32),
            jax.ShapeDtypeStruct((rows, width), BF),
        ],
        compiler_params=params(),
        name="dec_mid_back",
    )(dsecond, dcq, cross["query"], n, scale, w["gains"], w["out"])


enc_segs = ((0, SRC_LONG, 0, SRC_LONG), (SRC_LONG, SRC_SHORT, SRC_LONG, SRC_SHORT))
dec_segs = ((0, TGT, 0, TGT), (TGT, TGT, TGT, TGT))
cross_segs = ((0, TGT, 0, SRC_LONG), (TGT, TGT, SRC_LONG, SRC_SHORT))


def encoder_forward(x, lengths, w):
    qkv = product(x, w["qkv"])
    att, inv, *weights = attend(
        lengths, (qkv, 0), (qkv, 8), (qkv, 16), w["prefix"], enc_segs, False
    )
    mem, slope, act, low, scales = enc_ffn(x, att, w)
    return mem, (qkv, att, inv, weights, mem, slope, act, low, scales)


def encoder_back_ffn(saved, dmem, w):
    mem, slope, act, low, scales = saved[4:]
    dfirst, datt, *adapter = enc_ffn_back(dmem, mem, low, scales, slope, act, w)
    return dfirst, datt, adapter


def encoder_back_self(saved, dfirst, datt, w):
    qkv, att, inv, weights = saved[:4]
    dq, dk, dv, *dprefix = attend_back(
        (qkv, 0), (qkv, 8), (qkv, 16), w["prefix"], att, inv, datt, weights, enc_segs
    )
    return back_product([dq, dk, dv], w["qkv"], dfirst), dprefix


def decoder_self(t, lengths, w, cross):
    qkv = product(t, w["qkv"])
    att, inv, *weights = attend(
        lengths, (qkv, 0), (qkv, 8), (qkv, 16), w["prefix"], dec_segs, True
    )
    n, scale, cq = dec_mid(t, att, w, cross)
    return cq, (qkv, att, inv, weights, n, scale)


def decoder_cross(kept, mem, cq, cot, src_lengths, tgt_lengths, w, cross):
    n = kept[4]
    kv = product(mem, cross["pairs"])
    catt, cinv, *cweights = attend(
        src_lengths, (cq, 0), (kv, 0), (kv, 8), None, cross_segs, False
    )
    y, dsecond, dcatt, *adapter = dec_ffn(tgt_lengths, n, catt, cot, w, cross)
    dcq, dck, dcv = attend_back(
        (cq, 0), (kv, 0), (kv, 8), None, catt, cinv, dcatt, cweights, cross_segs
    )
    dmem = back_product([dck, dcv], cross["pairs"])
    return y, dmem, dcq, dsecond, adapter


def decoder_self_back(kept, dsecond, dcq, w, cross):
    qkv, att, inv, weights, n, scale = kept
    dfirst, datt = dec_mid_back(dsecond, dcq, n, scale, w, cross)
    dq, dk, dv, *dprefix = attend_back(
        (qkv, 0), (qkv, 8), (qkv, 16), w["prefix"], att, inv, datt, weights, dec_segs
    )
    return back_product([dq, dk, dv], w["qkv"], dfirst), dprefix


def blank_kernel(*refs):
    pass


def blanks(shapes):
    return pl.pallas_call(
        blank_kernel,
        out_shape=list(shapes),
        out_specs=[pl.BlockSpec(memory_space=pl.ANY)] * len(shapes),
        name="blank",
    )()


def on_section(is_encoder, encoder_work, decoder_work, *operands):
    enc_shapes = jax.eval_shape(encoder_work, *operands)
    dec_shapes = jax.eval_shape(decoder_work, *operands)

    def blank_like(shapes):
        leaves, tree = jax.tree.flatten(shapes)
        if not leaves:
            return shapes
        return jax.tree.unflatten(tree, blanks(leaves))

    return lax.cond(
        is_encoder,
        lambda *a: (encoder_work(*a), blank_like(dec_shapes)),
        lambda *a: (blank_like(enc_shapes), decoder_work(*a)),
        *operands,
    )


def to_decoder(block):
    return lax.ppermute(block, "section", [(0, 1)])


def to_encoder(block):
    return lax.ppermute(block, "section", [(1, 0)])


def per_device(
    sources, targets, cotangent, source_lengths, target_lengths,
    attn_qkv, attn_out, ffn_in, ffn_out, norm_gains, prefix_pairs,
    adapt_down, adapt_down_bias, adapt_up, adapt_up_bias,
    cross_query, cross_pairs, cross_out, cross_gain,
):
    is_encoder = lax.axis_index("section") == 0
    prefix = jnp.pad(prefix_pairs[0], ((0, 0), (0, PRE_PAD - PRE), (0, 0)))
    w = dict(
        qkv=attn_qkv[0], out=attn_out[0], ffn_in=ffn_in[0], ffn_out=ffn_out[0],
        gains=norm_gains[0], prefix=(prefix[0], prefix[1]),
        down=adapt_down[0], down_bias=adapt_down_bias,
        up=adapt_up[0], up_bias=adapt_up_bias,
    )
    cross = dict(query=cross_query, pairs=cross_pairs, out=cross_out, gain=cross_gain[None])
    half = sources.shape[1] // 2
    replicas = lax.axis_size("dp")

    (mem, saved), (cq, kept) = on_section(
        is_encoder,
        lambda: encoder_forward(sources, source_lengths, w),
        lambda: decoder_self(targets, target_lengths, w, cross),
    )
    mem_here = to_decoder(mem)
    _, (y, dmem, dcq, dsecond, dec_adapter) = on_section(
        is_encoder,
        lambda *a: (),
        lambda *a: decoder_cross(*a, cotangent, source_lengths, target_lengths, w, cross),
        kept, mem_here, cq,
    )
    dmem_here = to_encoder(dmem)
    y_low = to_encoder(y[:, :half])
    (dfirst, datt, enc_adapter), (dt, dec_prefix) = on_section(
        is_encoder,
        lambda *a: encoder_back_ffn(a[0], a[1], w),
        lambda *a: decoder_self_back(a[2], a[3], a[4], w, cross),
        saved, dmem_here, kept, dsecond, dcq,
    )
    dt_low = to_encoder(dt[:, :half])
    adapter = [
        jnp.where(is_encoder, a, b) / replicas for a, b in zip(enc_adapter, dec_adapter)
    ]
    down, down_bias, up, up_bias = lax.psum(adapter, "dp")
    (dx, enc_prefix), _ = on_section(
        is_encoder,
        lambda *a: encoder_back_self(*a, w),
        lambda *a: (),
        saved, dfirst, datt,
    )
    dx_high = to_decoder(dx[:, half:])
    prefix_grad = jnp.stack(
        [jnp.where(is_encoder, a, b)[:PRE] for a, b in zip(enc_prefix, dec_prefix)]
    )
    prefix_grad, down, up = lax.optimization_barrier((prefix_grad, down, up))
    prefix_grad = lax.psum(prefix_grad / replicas, "dp")
    return (
        jnp.where(is_encoder, y_low, y[:, half:]),
        jnp.where(is_encoder, dx[:, :half], dx_high),
        jnp.where(is_encoder, dt_low, dt[:, half:]),
        prefix_grad[None],
        down[None],
        down_bias,
        up[None],
        up_bias,
    )


def solution(mesh):
    layer2, layer3, rows = P("section", None), P("section", None, None), P("dp", None)
    return jax.shard_map(
        per_device,
        mesh=mesh,
        in_specs=(
            rows, rows, rows, rows, rows,
            layer3, layer3, layer3, layer3, layer3,
            P("section", None, None, None),
            layer3, layer2, layer3, layer2,
            P(), P(), P(), P(),
        ),
        out_specs=(
            P("dp", "section"), P("dp", "section"), P("dp", "section"),
            P("section", None, None, None), layer3, layer2, layer3, layer2,
        ),
        check_vma=False,
    )
```

```python
import functools

import jax
import jax.numpy as jnp
from jax import lax
from jax.experimental import pallas as pl
from jax.experimental.pallas import tpu as pltpu
from jax.sharding import PartitionSpec as P

HD = 64
PRE = 30
PRE_PAD = 32
SRC_LONG = 768
SRC_SHORT = 96
TGT = 256
LANES = 128

BF = jnp.bfloat16
F32 = jnp.float32
norm_eps = 1e-05
big_negative = -1e30
adapter_scale = 4.0
chunk = 512
vmem_bytes = 56 * 2**20

phi_poly = (
    0.797869713181688,
    0.036392283539041996,
    -8.782472977701046e-05,
    -3.669384069669515e-05,
    1.4250308145882202e-06,
)


def nn(left, right):
    return lax.dot_general(left, right, (((1,), (0,)), ((), ())), preferred_element_type=F32)


def nt(left, right):
    return lax.dot_general(left, right, (((1,), (1,)), ((), ())), preferred_element_type=F32)


def tn(left, right):
    return lax.dot_general(left, right, (((0,), (0,)), ((), ())), preferred_element_type=F32)


def gelu_pair(values):
    square = values * values
    poly = phi_poly[4]
    for coefficient in phi_poly[3::-1]:
        poly = poly * square + coefficient
    half = 0.5 * jnp.tanh(values * poly) + 0.5
    density = jnp.exp(square * -0.5) * 0.3989422804014327
    return values * half, half + values * density


def row_tiles(rows, most=288):
    count = -(-rows // most)
    size = rows // count
    return [(i * size, size) for i in range(count)]


def norm_rows(values):
    centered = values - jnp.mean(values, axis=-1, keepdims=True)
    scale = lax.rsqrt(jnp.mean(centered * centered, axis=-1, keepdims=True) + norm_eps)
    return centered * scale, scale


def norm_rows_back(hat, scale, grad_hat):
    mean_grad = jnp.mean(grad_hat, axis=-1, keepdims=True)
    mean_dot = jnp.mean(grad_hat * hat, axis=-1, keepdims=True)
    return scale * (grad_hat - mean_grad - hat * mean_dot)


def params(limit=vmem_bytes):
    return pltpu.CompilerParams(vmem_limit_bytes=limit)


def whole(shape):
    return pl.BlockSpec(shape, lambda *g: (0,) * len(shape))


def product_kernel(x_ref, w_ref, o_ref):
    o_ref[...] = nn(x_ref[...], w_ref[...]).astype(BF)


def product(x, w, tile=512):
    rows, depth = x.shape
    width = w.shape[1]
    return pl.pallas_call(
        product_kernel,
        grid=(width // tile,),
        in_specs=[whole((rows, depth)), pl.BlockSpec((depth, tile), lambda i: (0, i))],
        out_specs=pl.BlockSpec((rows, tile), lambda i: (0, i)),
        out_shape=jax.ShapeDtypeStruct((rows, width), BF),
        compiler_params=params(),
        name="product",
    )(x, w)


def back_product_kernel(*refs, parts, residual):
    grads = refs[:parts]
    w_ref = refs[parts]
    o_ref = refs[-1]
    total = None
    width = grads[0].shape[1]
    for i, grad in enumerate(grads):
        term = nt(grad[...], w_ref[:, i * width : (i + 1) * width])
        total = term if total is None else total + term
    if residual:
        total = total + refs[parts + 1][...]
    o_ref[...] = total.astype(BF)


def back_product(grads, w, residual=None, tile=256):
    rows, width = grads[0].shape
    depth = w.shape[0]
    parts = len(grads)
    specs = [whole((rows, width))] * parts + [
        pl.BlockSpec((tile, parts * width), lambda i: (i, 0))
    ]
    args = list(grads) + [w]
    if residual is not None:
        specs.append(pl.BlockSpec((rows, tile), lambda i: (0, i)))
        args.append(residual)
    return pl.pallas_call(
        functools.partial(back_product_kernel, parts=parts, residual=residual is not None),
        grid=(depth // tile,),
        in_specs=specs,
        out_specs=pl.BlockSpec((rows, tile), lambda i: (0, i)),
        out_shape=jax.ShapeDtypeStruct((rows, depth), BF),
        compiler_params=params(),
        name="back_product",
    )(*args)


def head_lanes(head):
    lane = lax.broadcasted_iota(jnp.int32, (1, LANES), 1)
    own = (lane < HD) if head == 0 else (lane >= HD)
    first = HD if head == 0 else 0
    return own, lane == first, lane == first + 1


def bf(value):
    return jnp.asarray(value, BF)


def stacked(rows_ref, prefix_ref, start, count):
    rows = rows_ref[start : start + count]
    if prefix_ref is None:
        return rows
    return jnp.concatenate([rows, prefix_ref[...]], 0)


def attend_kernel(*refs, segs, prefix, causal):
    len_ref, q_ref, k_ref, v_ref = refs[:4]
    at = 4
    pk_ref = pv_ref = None
    if prefix:
        pk_ref, pv_ref = refs[4:6]
        at = 6
    o_ref, inv_ref = refs[at : at + 2]
    p_refs = refs[at + 2 :]
    for seg, (q0, nq, k0, nk) in enumerate(segs):
        keys = stacked(k_ref, pk_ref, k0, nk)
        values = stacked(v_ref, pv_ref, k0, nk)
        count = keys.shape[0]
        row = lax.broadcasted_iota(jnp.int32, (count, 1), 0)
        seen = row < jnp.minimum(len_ref[0, seg], nk)
        if prefix:
            seen = seen | ((row >= nk) & (row < nk + PRE))
        queries = q_ref[q0 : q0 + nq] * bf(HD**-0.5)
        out = inv = None
        for head in range(2):
            own, first, _ = head_lanes(head)
            k_own = jnp.where(own, keys, jnp.where(first & ~seen, bf(big_negative), bf(0)))
            q_own = jnp.where(own, queries, jnp.where(first, bf(1), bf(0)))
            v_own = jnp.where(own, values, bf(1))
            scores = nt(k_own, q_own)
            if causal:
                key_at = lax.broadcasted_iota(jnp.int32, scores.shape, 0)
                query_at = lax.broadcasted_iota(jnp.int32, scores.shape, 1)
                allowed = (key_at <= query_at) | (key_at >= nk)
                scores = jnp.where(allowed, scores, big_negative)
            peak = jnp.max(scores, axis=0, keepdims=True)
            weights = jnp.exp(scores - peak).astype(BF)
            p_refs[seg][head] = weights
            mixed = tn(weights, v_own)
            inverse = 1.0 / pltpu.roll(mixed, HD, 1)
            mixed = mixed * inverse
            out = mixed if out is None else jnp.where(own, mixed, out)
            inv = inverse if inv is None else jnp.where(own, inverse, inv)
        o_ref[q0 : q0 + nq] = out.astype(BF)
        inv_ref[q0 : q0 + nq] = inv


def column_spec(rows, offset):
    return pl.BlockSpec((rows, LANES), lambda h: (0, h + offset))


def attend(lengths, q, k, v, prefixes, segs, causal):
    pairs = 8
    q_rows, k_rows = q[0].shape[0], k[0].shape[0]
    prefix = prefixes is not None
    extra = PRE_PAD if prefix else 0
    specs = [
        pl.BlockSpec(memory_space=pltpu.SMEM),
        column_spec(q_rows, q[1]),
        column_spec(k_rows, k[1]),
        column_spec(k_rows, v[1]),
    ]
    args = [lengths, q[0], k[0], v[0]]
    if prefix:
        specs += [column_spec(PRE_PAD, 0)] * 2
        args += list(prefixes)
    weight_shapes = [(2 * pairs, nk + extra, nq) for _, nq, _, nk in segs]
    return pl.pallas_call(
        functools.partial(attend_kernel, segs=segs, prefix=prefix, causal=causal),
        grid=(pairs,),
        in_specs=specs,
        out_specs=[column_spec(q_rows, 0), column_spec(q_rows, 0)]
        + [pl.BlockSpec((2,) + s[1:], lambda h: (h, 0, 0)) for s in weight_shapes],
        out_shape=[
            jax.ShapeDtypeStruct((q_rows, pairs * LANES), BF),
            jax.ShapeDtypeStruct((q_rows, pairs * LANES), F32),
        ]
        + [jax.ShapeDtypeStruct(s, BF) for s in weight_shapes],
        compiler_params=params(),
        name="attend",
    )(*args)


def attend_back_kernel(*refs, segs, prefix):
    q_ref, k_ref, v_ref, o_ref, inv_ref, g_ref = refs[:6]
    at = 6
    pk_ref = pv_ref = None
    if prefix:
        pk_ref, pv_ref = refs[6:8]
        at = 8
    p_refs = refs[at : at + len(segs)]
    outs = refs[at + len(segs) :]
    dq_ref, dk_ref, dv_ref = outs[:3]
    prefix_totals = [None, None]
    scale = HD**-0.5
    for seg, (q0, nq, k0, nk) in enumerate(segs):
        keys = stacked(k_ref, pk_ref, k0, nk)
        values = stacked(v_ref, pv_ref, k0, nk)
        queries = q_ref[q0 : q0 + nq]
        grads = g_ref[q0 : q0 + nq].astype(F32) * inv_ref[q0 : q0 + nq]
        grads_low = grads.astype(BF)
        dots = grads * o_ref[q0 : q0 + nq].astype(F32)
        dq = dk = dv = None
        for head in range(2):
            own, first, second = head_lanes(head)
            row_dot = -jnp.sum(jnp.where(own, dots, 0.0), axis=1, keepdims=True)
            high = row_dot.astype(BF)
            rest = (row_dot - high.astype(F32)).astype(BF)
            g_own = jnp.where(
                own, grads_low, jnp.where(first, high, jnp.where(second, rest, bf(0)))
            )
            v_own = jnp.where(own, values, jnp.where(first | second, bf(1), bf(0)))
            weights = p_refs[seg][head]
            score_grad = (weights.astype(F32) * nt(v_own, g_own)).astype(BF)
            dv_head = nn(weights, grads_low)
            dk_head = nn(score_grad, queries)
            dq_head = tn(score_grad, keys)
            dq = dq_head if dq is None else jnp.where(own, dq_head, dq)
            dk = dk_head if dk is None else jnp.where(own, dk_head, dk)
            dv = dv_head if dv is None else jnp.where(own, dv_head, dv)
        dk = dk * scale
        dq_ref[q0 : q0 + nq] = (dq * scale).astype(BF)
        dk_ref[k0 : k0 + nk] = dk[:nk].astype(BF)
        dv_ref[k0 : k0 + nk] = dv[:nk].astype(BF)
        if prefix:
            for i, grad in enumerate((dk, dv)):
                part = grad[nk:]
                prefix_totals[i] = part if seg == 0 else prefix_totals[i] + part
    if prefix:
        outs[3][...] = prefix_totals[0]
        outs[4][...] = prefix_totals[1]


def attend_back(q, k, v, prefixes, attended, inverse, grad, weights, segs):
    pairs = 8
    q_rows, k_rows = q[0].shape[0], k[0].shape[0]
    prefix = prefixes is not None
    specs = [
        column_spec(q_rows, q[1]),
        column_spec(k_rows, k[1]),
        column_spec(k_rows, v[1]),
        column_spec(q_rows, 0),
        column_spec(q_rows, 0),
        column_spec(q_rows, 0),
    ]
    args = [q[0], k[0], v[0], attended, inverse, grad]
    if prefix:
        specs += [column_spec(PRE_PAD, 0)] * 2
        args += list(prefixes)
    specs += [pl.BlockSpec((2,) + w.shape[1:], lambda h: (h, 0, 0)) for w in weights]
    args += list(weights)
    out_specs = [column_spec(q_rows, 0), column_spec(k_rows, 0), column_spec(k_rows, 0)]
    out_shape = [
        jax.ShapeDtypeStruct((q_rows, pairs * LANES), BF),
        jax.ShapeDtypeStruct((k_rows, pairs * LANES), BF),
        jax.ShapeDtypeStruct((k_rows, pairs * LANES), BF),
    ]
    if prefix:
        out_specs += [column_spec(PRE_PAD, 0)] * 2
        out_shape += [jax.ShapeDtypeStruct((PRE_PAD, pairs * LANES), F32)] * 2
    return pl.pallas_call(
        functools.partial(attend_back_kernel, segs=segs, prefix=prefix),
        grid=(pairs,),
        in_specs=specs,
        out_specs=out_specs,
        out_shape=out_shape,
        compiler_params=params(),
        name="attend_back",
    )(*args)


def ffn_step(low_ref, acc_ref, in_ref, out_ref, slope_ref, act_ref, bias_ref, scale):
    for start, size in row_tiles(low_ref.shape[0]):
        rows = slice(start, start + size)
        hidden = nn(low_ref[rows], in_ref[...])
        if bias_ref is not None:
            hidden = hidden + bias_ref[...]
        active, slope = gelu_pair(hidden)
        slope_ref[rows] = slope.astype(BF)
        active = active.astype(BF)
        if act_ref is not None:
            act_ref[rows] = active
        term = nn(active, out_ref[...])
        acc_ref[rows] += term if scale is None else scale * term


def enc_ffn_kernel(
    x_ref, att_ref, wo_ref, gain_ref, in_ref, out_ref, down_ref, downb_ref, up_ref, upb_ref,
    mem_ref, slope_ref, act_ref, low_ref, scales_ref, acc_ref,
):
    step = pl.program_id(0)
    last = pl.num_programs(0) - 1

    @pl.when(step == 0)
    def _():
        for start, size in row_tiles(x_ref.shape[0]):
            rows = slice(start, start + size)
            first = x_ref[rows].astype(F32) + nn(att_ref[rows], wo_ref[...])
            hat, scale = norm_rows(first)
            normed = hat * gain_ref[0:1]
            acc_ref[rows] = normed
            low_ref[rows] = normed.astype(BF)
            scales_ref[rows, 0:1] = scale

    @pl.when((step > 0) & (step < last))
    def _():
        ffn_step(low_ref, acc_ref, in_ref, out_ref, slope_ref, None, None, None)

    @pl.when(step == last)
    def _():
        ffn_step(low_ref, acc_ref, down_ref, up_ref, slope_ref, act_ref, downb_ref, adapter_scale)
        for start, size in row_tiles(x_ref.shape[0]):
            rows = slice(start, start + size)
            hat, scale = norm_rows(acc_ref[rows] + adapter_scale * upb_ref[...])
            mem_ref[rows] = (hat * gain_ref[1:2]).astype(BF)
            scales_ref[rows, 1:2] = scale


def enc_ffn(x, att, w):
    rows, width = x.shape
    hidden = w["ffn_in"].shape[1]
    steps = hidden // chunk

    def at(i):
        return jnp.clip(i - 1, 0, steps - 1)

    return pl.pallas_call(
        enc_ffn_kernel,
        grid=(steps + 2,),
        in_specs=[
            whole((rows, width)),
            whole((rows, width)),
            whole((width, width)),
            whole((2, width)),
            pl.BlockSpec((width, chunk), lambda i: (0, at(i))),
            pl.BlockSpec((chunk, width), lambda i: (at(i), 0)),
            whole((width, chunk)),
            whole((1, chunk)),
            whole((chunk, width)),
            whole((1, width)),
        ],
        out_specs=[
            whole((rows, width)),
            pl.BlockSpec((rows, chunk), lambda i: (0, jnp.clip(i - 1, 0, steps))),
            whole((rows, chunk)),
            whole((rows, width)),
            whole((rows, LANES)),
        ],
        out_shape=[
            jax.ShapeDtypeStruct((rows, width), BF),
            jax.ShapeDtypeStruct((rows, hidden + chunk), BF),
            jax.ShapeDtypeStruct((rows, chunk), BF),
            jax.ShapeDtypeStruct((rows, width), BF),
            jax.ShapeDtypeStruct((rows, LANES), F32),
        ],
        scratch_shapes=[pltpu.VMEM((rows, width), F32)],
        compiler_params=params(),
        name="enc_ffn",
    )(
        x, att, w["out"], w["gains"], w["ffn_in"], w["ffn_out"],
        w["down"], w["down_bias"], w["up"], w["up_bias"],
    )


def ffn_back_step(grad_ref, acc_ref, in_ref, out_ref, slope_ref):
    for start, size in row_tiles(grad_ref.shape[0]):
        rows = slice(start, start + size)
        pre = (nt(grad_ref[rows], out_ref[...]) * slope_ref[rows].astype(F32)).astype(BF)
        acc_ref[rows] += nt(pre, in_ref[...])


def adapter_back(grad_ref, acc_ref, low_ref, act_ref, slope_ref, down_ref, up_ref, outs, pre_ref):
    ddown_ref, ddownb_ref, dup_ref, dupb_ref = outs
    total = None
    for start, size in row_tiles(grad_ref.shape[0]):
        rows = slice(start, start + size)
        back = adapter_scale * nt(grad_ref[rows], up_ref[...])
        pre = (back * slope_ref[rows].astype(F32)).astype(BF)
        pre_ref[rows] = pre
        sums = jnp.sum(pre.astype(F32), axis=0, keepdims=True)
        total = sums if total is None else total + sums
        acc_ref[rows] += nt(pre, down_ref[...])
    ddownb_ref[...] = total
    ddown_ref[...] = tn(low_ref[...], pre_ref[...])
    dup_ref[...] = adapter_scale * tn(act_ref[...], grad_ref[...])
    dupb_ref[...] = adapter_scale * jnp.sum(grad_ref[...].astype(F32), axis=0, keepdims=True)


def enc_ffn_back_kernel(
    dmem_ref, mem_ref, low_ref, scales_ref, gain_ref, slope_ref, act_ref,
    in_ref, out_ref, down_ref, up_ref, wo_ref,
    dfirst_ref, datt_ref, ddown_ref, ddownb_ref, dup_ref, dupb_ref,
    acc_ref, grad_ref, pre_ref,
):
    step = pl.program_id(0)
    last = pl.num_programs(0) - 1

    @pl.when(step == 0)
    def _():
        for start, size in row_tiles(dmem_ref.shape[0]):
            rows = slice(start, start + size)
            gain = gain_ref[1:2]
            hat = mem_ref[rows].astype(F32) / gain
            grad = norm_rows_back(
                hat, scales_ref[rows, 1:2], dmem_ref[rows].astype(F32) * gain
            )
            acc_ref[rows] = grad
            grad_ref[rows] = grad.astype(BF)
        adapter_back(
            grad_ref, acc_ref, low_ref, act_ref, slope_ref, down_ref, up_ref,
            (ddown_ref, ddownb_ref, dup_ref, dupb_ref), pre_ref,
        )

    @pl.when(step > 0)
    def _():
        ffn_back_step(grad_ref, acc_ref, in_ref, out_ref, slope_ref)

    @pl.when(step == last)
    def _():
        for start, size in row_tiles(dmem_ref.shape[0]):
            rows = slice(start, start + size)
            gain = gain_ref[0:1]
            hat = low_ref[rows].astype(F32) / gain
            grad = norm_rows_back(hat, scales_ref[rows, 0:1], acc_ref[rows] * gain)
            dfirst_ref[rows] = grad
            datt_ref[rows] = nt(grad.astype(BF), wo_ref[...]).astype(BF)


def enc_ffn_back(dmem, mem, low, scales, slope, act, w):
    rows, width = dmem.shape
    hidden = w["ffn_in"].shape[1]
    steps = hidden // chunk

    def at(i):
        return jnp.clip(i - 1, 0, steps - 1)

    return pl.pallas_call(
        enc_ffn_back_kernel,
        grid=(steps + 1,),
        in_specs=[
            whole((rows, width)),
            whole((rows, width)),
            whole((rows, width)),
            whole((rows, LANES)),
            whole((2, width)),
            pl.BlockSpec((rows, chunk), lambda i: (0, jnp.where(i == 0, steps, i - 1))),
            whole((rows, chunk)),
            pl.BlockSpec((width, chunk), lambda i: (0, at(i))),
            pl.BlockSpec((chunk, width), lambda i: (at(i), 0)),
            whole((width, chunk)),
            whole((chunk, width)),
            whole((width, width)),
        ],
        out_specs=[
            whole((rows, width)),
            whole((rows, width)),
            whole((width, chunk)),
            whole((1, chunk)),
            whole((chunk, width)),
            whole((1, width)),
        ],
        out_shape=[
            jax.ShapeDtypeStruct((rows, width), F32),
            jax.ShapeDtypeStruct((rows, width), BF),
            jax.ShapeDtypeStruct((width, chunk), F32),
            jax.ShapeDtypeStruct((1, chunk), F32),
            jax.ShapeDtypeStruct((chunk, width), F32),
            jax.ShapeDtypeStruct((1, width), F32),
        ],
        scratch_shapes=[
            pltpu.VMEM((rows, width), F32),
            pltpu.VMEM((rows, width), BF),
            pltpu.VMEM((rows, chunk), BF),
        ],
        compiler_params=params(),
        name="enc_ffn_back",
    )(
        dmem, mem, low, scales, w["gains"], slope, act,
        w["ffn_in"], w["ffn_out"], w["down"], w["up"], w["out"],
    )


def dec_mid_kernel(x_ref, att_ref, wo_ref, gain_ref, wq_ref, n_ref, scale_ref, cq_ref):
    for start, size in row_tiles(x_ref.shape[0], 256):
        rows = slice(start, start + size)
        first = x_ref[rows].astype(F32) + nn(att_ref[rows], wo_ref[...])
        hat, scale = norm_rows(first)
        normed = hat * gain_ref[0:1]
        n_ref[rows] = normed
        scale_ref[rows, 0:1] = scale
        cq_ref[rows] = nn(normed.astype(BF), wq_ref[...]).astype(BF)


def dec_mid(x, att, w, cross):
    rows, width = x.shape
    return pl.pallas_call(
        dec_mid_kernel,
        out_shape=[
            jax.ShapeDtypeStruct((rows, width), F32),
            jax.ShapeDtypeStruct((rows, LANES), F32),
            jax.ShapeDtypeStruct((rows, width), BF),
        ],
        compiler_params=params(),
        name="dec_mid",
    )(x, att, w["out"], w["gains"], cross["query"])


def dec_ffn_kernel(
    len_ref, n_ref, catt_ref, cot_ref, wco_ref, cgain_ref, gain_ref,
    in_ref, out_ref, down_ref, downb_ref, up_ref, upb_ref,
    y_ref, dsecond_ref, dcatt_ref, ddown_ref, ddownb_ref, dup_ref, dupb_ref,
    acc_ref, low_ref, grad_ref, slope_ref, act_ref, pre_ref, scale_ref,
    *, steps,
):
    step = pl.program_id(0)
    tiles = row_tiles(n_ref.shape[0], TGT)

    @pl.when(step == 0)
    def _():
        for start, size in tiles:
            rows = slice(start, start + size)
            second = n_ref[rows] + nn(catt_ref[rows], wco_ref[...])
            hat, scale = norm_rows(second)
            middle = hat * cgain_ref[...]
            acc_ref[rows] = middle
            low_ref[rows] = middle.astype(BF)
            scale_ref[rows, 0:1] = scale

    @pl.when((step > 0) & (step <= steps))
    def _():
        ffn_step(low_ref, acc_ref, in_ref, out_ref, slope_ref.at[step - 1], None, None, None)

    @pl.when(step == steps + 1)
    def _():
        ffn_step(
            low_ref, acc_ref, down_ref, up_ref, slope_ref.at[steps], act_ref, downb_ref,
            adapter_scale,
        )
        for tile, (start, size) in enumerate(tiles):
            rows = slice(start, start + size)
            gain = gain_ref[1:2]
            hat, scale = norm_rows(acc_ref[rows] + adapter_scale * upb_ref[...])
            valid = lax.broadcasted_iota(jnp.int32, (size, 1), 0) < len_ref[0, tile]
            y_ref[rows] = jnp.where(valid, hat * gain, 0.0).astype(BF)
            cot = jnp.where(valid, cot_ref[rows].astype(F32), 0.0)
            grad = norm_rows_back(hat, scale, cot * gain)
            acc_ref[rows] = grad
            grad_ref[rows] = grad.astype(BF)
        adapter_back(
            grad_ref, acc_ref, low_ref, act_ref, slope_ref.at[steps], down_ref, up_ref,
            (ddown_ref, ddownb_ref, dup_ref, dupb_ref), pre_ref,
        )

    @pl.when(step > steps + 1)
    def _():
        ffn_back_step(grad_ref, acc_ref, in_ref, out_ref, slope_ref.at[2 * steps + 1 - step])

    @pl.when(step == 2 * steps + 1)
    def _():
        for start, size in tiles:
            rows = slice(start, start + size)
            gain = cgain_ref[...]
            hat = low_ref[rows].astype(F32) / gain
            grad = norm_rows_back(hat, scale_ref[rows, 0:1], acc_ref[rows] * gain)
            dsecond_ref[rows] = grad
            dcatt_ref[rows] = nt(grad.astype(BF), wco_ref[...]).astype(BF)


def dec_ffn(lengths, n, catt, cot, w, cross):
    rows, width = n.shape
    hidden = w["ffn_in"].shape[1]
    steps = hidden // chunk

    def at(i):
        return jnp.where(i <= steps, jnp.clip(i - 1, 0, steps - 1), jnp.clip(2 * steps + 1 - i, 0, steps - 1))

    return pl.pallas_call(
        functools.partial(dec_ffn_kernel, steps=steps),
        grid=(2 * steps + 2,),
        in_specs=[
            pl.BlockSpec(memory_space=pltpu.SMEM),
            whole((rows, width)),
            whole((rows, width)),
            whole((rows, width)),
            whole((width, width)),
            whole((1, width)),
            whole((2, width)),
            pl.BlockSpec((width, chunk), lambda i: (0, at(i))),
            pl.BlockSpec((chunk, width), lambda i: (at(i), 0)),
            whole((width, chunk)),
            whole((1, chunk)),
            whole((chunk, width)),
            whole((1, width)),
        ],
        out_specs=[
            whole((rows, width)),
            whole((rows, width)),
            whole((rows, width)),
            whole((width, chunk)),
            whole((1, chunk)),
            whole((chunk, width)),
            whole((1, width)),
        ],
        out_shape=[
            jax.ShapeDtypeStruct((rows, width), BF),
            jax.ShapeDtypeStruct((rows, width), F32),
            jax.ShapeDtypeStruct((rows, width), BF),
            jax.ShapeDtypeStruct((width, chunk), F32),
            jax.ShapeDtypeStruct((1, chunk), F32),
            jax.ShapeDtypeStruct((chunk, width), F32),
            jax.ShapeDtypeStruct((1, width), F32),
        ],
        scratch_shapes=[
            pltpu.VMEM((rows, width), F32),
            pltpu.VMEM((rows, width), BF),
            pltpu.VMEM((rows, width), BF),
            pltpu.VMEM((steps + 1, rows, chunk), BF),
            pltpu.VMEM((rows, chunk), BF),
            pltpu.VMEM((rows, chunk), BF),
            pltpu.VMEM((rows, LANES), F32),
        ],
        compiler_params=params(),
        name="dec_ffn",
    )(
        lengths, n, catt, cot, cross["out"], cross["gain"], w["gains"],
        w["ffn_in"], w["ffn_out"], w["down"], w["down_bias"], w["up"], w["up_bias"],
    )


def dec_mid_back_kernel(
    dsecond_ref, dcq_ref, wq_ref, n_ref, scale_ref, gain_ref, wo_ref, dfirst_ref, datt_ref
):
    for start, size in row_tiles(n_ref.shape[0], 256):
        rows = slice(start, start + size)
        gain = gain_ref[0:1]
        total = dsecond_ref[rows] + nt(dcq_ref[rows], wq_ref[...])
        grad = norm_rows_back(n_ref[rows] / gain, scale_ref[rows, 0:1], total * gain)
        dfirst_ref[rows] = grad
        datt_ref[rows] = nt(grad.astype(BF), wo_ref[...]).astype(BF)


def dec_mid_back(dsecond, dcq, n, scale, w, cross):
    rows, width = n.shape
    return pl.pallas_call(
        dec_mid_back_kernel,
        out_shape=[
            jax.ShapeDtypeStruct((rows, width), F32),
            jax.ShapeDtypeStruct((rows, width), BF),
        ],
        compiler_params=params(),
        name="dec_mid_back",
    )(dsecond, dcq, cross["query"], n, scale, w["gains"], w["out"])


enc_segs = ((0, SRC_LONG, 0, SRC_LONG), (SRC_LONG, SRC_SHORT, SRC_LONG, SRC_SHORT))
dec_segs = ((0, TGT, 0, TGT), (TGT, TGT, TGT, TGT))
cross_segs = ((0, TGT, 0, SRC_LONG), (TGT, TGT, SRC_LONG, SRC_SHORT))


def encoder_forward(x, lengths, w):
    qkv = product(x, w["qkv"])
    att, inv, *weights = attend(
        lengths, (qkv, 0), (qkv, 8), (qkv, 16), w["prefix"], enc_segs, False
    )
    mem, slope, act, low, scales = enc_ffn(x, att, w)
    return mem, (qkv, att, inv, weights, mem, slope, act, low, scales)


def encoder_back_ffn(saved, dmem, w):
    mem, slope, act, low, scales = saved[4:]
    dfirst, datt, *adapter = enc_ffn_back(dmem, mem, low, scales, slope, act, w)
    return dfirst, datt, adapter


def encoder_back_self(saved, dfirst, datt, w):
    qkv, att, inv, weights = saved[:4]
    dq, dk, dv, *dprefix = attend_back(
        (qkv, 0), (qkv, 8), (qkv, 16), w["prefix"], att, inv, datt, weights, enc_segs
    )
    return back_product([dq, dk, dv], w["qkv"], dfirst), dprefix


def decoder_self(t, lengths, w, cross):
    qkv = product(t, w["qkv"])
    att, inv, *weights = attend(
        lengths, (qkv, 0), (qkv, 8), (qkv, 16), w["prefix"], dec_segs, True
    )
    n, scale, cq = dec_mid(t, att, w, cross)
    return cq, (qkv, att, inv, weights, n, scale)


def decoder_cross(kept, mem, cq, cot, src_lengths, tgt_lengths, w, cross):
    n = kept[4]
    kv = product(mem, cross["pairs"])
    catt, cinv, *cweights = attend(
        src_lengths, (cq, 0), (kv, 0), (kv, 8), None, cross_segs, False
    )
    y, dsecond, dcatt, *adapter = dec_ffn(tgt_lengths, n, catt, cot, w, cross)
    dcq, dck, dcv = attend_back(
        (cq, 0), (kv, 0), (kv, 8), None, catt, cinv, dcatt, cweights, cross_segs
    )
    dmem = back_product([dck, dcv], cross["pairs"])
    return y, dmem, dcq, dsecond, adapter


def decoder_self_back(kept, dsecond, dcq, w, cross):
    qkv, att, inv, weights, n, scale = kept
    dfirst, datt = dec_mid_back(dsecond, dcq, n, scale, w, cross)
    dq, dk, dv, *dprefix = attend_back(
        (qkv, 0), (qkv, 8), (qkv, 16), w["prefix"], att, inv, datt, weights, dec_segs
    )
    return back_product([dq, dk, dv], w["qkv"], dfirst), dprefix


def packed_rows(devices):
    unit = 16 * devices
    return -(-(2 * chunk + 2 * PRE_PAD + 16) // unit) * unit


def group_sum_kernel(
    up_ref, down_ref, pk_ref, pv_ref, upb_ref, downb_ref,
    o_up_ref, o_down_ref, o_pk_ref, o_pv_ref, o_bias_ref,
    mine, theirs, half_sum, landed, total, result,
    pair_sems, spread_sems, gather_sems, back_sems,
    *, devices,
):
    chips = devices // 2
    rows = packed_rows(devices)
    half, part = rows // 2, rows // devices
    place = lax.axis_index("dp")
    core, chip = lax.rem(place, 2), place // 2
    partner = place + 1 - 2 * core

    def peer(distance):
        return lax.rem(chip + distance, chips) * 2 + core

    barrier = pltpu.get_barrier_semaphore()
    for other in [partner] + [peer(s) for s in range(1, chips)]:
        pl.semaphore_signal(barrier, inc=1, device_id={"dp": other}, device_id_type=pl.DeviceIdType.MESH)

    width = 2 * chunk
    scale = 1.0 / devices
    mine[0:chunk] = (up_ref[...] * scale).astype(BF)
    mine[chunk:width, 0:chunk] = (down_ref[0:chunk] * scale).astype(BF)
    mine[chunk:width, chunk:width] = (down_ref[chunk:width] * scale).astype(BF)
    mine[width : width + PRE_PAD] = (pk_ref[...] * scale).astype(BF)
    mine[width + PRE_PAD : width + 2 * PRE_PAD] = (pv_ref[...] * scale).astype(BF)
    at = width + 2 * PRE_PAD
    row = lax.broadcasted_iota(jnp.int32, (16, width), 0)
    down_row = jnp.concatenate([downb_ref[...], jnp.zeros_like(downb_ref)], 1)
    bias = jnp.where(row == 0, upb_ref[...], jnp.where(row == 1, down_row, 0.0)) * scale
    mine[at : at + 16] = bias.astype(BF)
    if rows > at + 16:
        mine[at + 16 : rows] = jnp.zeros((rows - at - 16, width), BF)
    pl.semaphore_wait(barrier, chips)

    def remote(source, target, send_sem, recv_sem, other):
        return pltpu.make_async_remote_copy(
            src_ref=source, dst_ref=target, send_sem=send_sem, recv_sem=recv_sem,
            device_id={"dp": other}, device_id_type=pl.DeviceIdType.MESH,
        )

    kept = pl.multiple_of(core * half, 16)
    given = pl.multiple_of((1 - core) * half, 16)
    swap = remote(
        mine.at[pl.ds(given, half)], theirs, pair_sems.at[0], pair_sems.at[1], partner
    )
    swap.start()
    swap.wait()
    half_sum[...] = (
        mine[pl.ds(kept, half)].astype(F32) + theirs[...].astype(F32)
    ).astype(BF)
    spread = []
    for s in range(1, chips):
        other_chip = lax.rem(chip + s, chips)
        copy = remote(
            half_sum.at[pl.ds(pl.multiple_of(other_chip * part, 16), part)],
            landed.at[s - 1],
            spread_sems.at[0, s - 1], spread_sems.at[1, s - 1], peer(s),
        )
        copy.start()
        spread.append(copy)
    summed = half_sum[pl.ds(pl.multiple_of(chip * part, 16), part)].astype(F32)
    for s in range(1, chips):
        spread[s - 1].wait()
        summed = summed + landed[s - 1].astype(F32)
    total[...] = summed.astype(BF)

    here = pl.multiple_of(kept + chip * part, 16)
    result[pl.ds(here, part)] = total[...]
    gather = []
    for s in range(1, chips):
        copy = remote(
            total, result.at[pl.ds(here, part)],
            gather_sems.at[0, s - 1], gather_sems.at[1, s - 1], peer(s),
        )
        copy.start()
        gather.append(copy)
    back = [
        remote(
            total, result.at[pl.ds(here, part)], back_sems.at[0, 0], back_sems.at[1, 0], partner
        )
    ]
    back[0].start()
    for s in range(1, chips):
        gather[s - 1].wait()
        source = lax.rem(chip + chips - s, chips)
        rows_there = pl.ds(pl.multiple_of(kept + source * part, 16), part)
        copy = remote(
            result.at[rows_there], result.at[rows_there],
            back_sems.at[0, s], back_sems.at[1, s], partner,
        )
        copy.start()
        back.append(copy)
    for copy in back:
        copy.wait()
    o_up_ref[...] = result[0:chunk].astype(F32)
    o_down_ref[0:chunk] = result[chunk:width, 0:chunk].astype(F32)
    o_down_ref[chunk:width] = result[chunk:width, chunk:width].astype(F32)
    o_pk_ref[...] = result[width : width + PRE_PAD].astype(F32)
    o_pv_ref[...] = result[width + PRE_PAD : width + 2 * PRE_PAD].astype(F32)
    o_bias_ref[...] = result[at : at + 16].astype(F32)


def group_sum(up, down, pk, pv, up_bias, down_bias):
    devices = lax.axis_size("dp")
    rows = packed_rows(devices)
    chips = devices // 2
    width = up.shape[1]
    part = rows // devices
    return pl.pallas_call(
        functools.partial(group_sum_kernel, devices=devices),
        out_shape=[
            jax.ShapeDtypeStruct(up.shape, F32),
            jax.ShapeDtypeStruct(down.shape, F32),
            jax.ShapeDtypeStruct(pk.shape, F32),
            jax.ShapeDtypeStruct(pv.shape, F32),
            jax.ShapeDtypeStruct((16, width), F32),
        ],
        scratch_shapes=[
            pltpu.VMEM((rows, width), BF),
            pltpu.VMEM((rows // 2, width), BF),
            pltpu.VMEM((rows // 2, width), BF),
            pltpu.VMEM((chips - 1, part, width), BF),
            pltpu.VMEM((part, width), BF),
            pltpu.VMEM((rows, width), BF),
            pltpu.SemaphoreType.DMA((2,)),
            pltpu.SemaphoreType.DMA((2, chips - 1)),
            pltpu.SemaphoreType.DMA((2, chips - 1)),
            pltpu.SemaphoreType.DMA((2, chips)),
        ],
        compiler_params=pltpu.CompilerParams(
            vmem_limit_bytes=vmem_bytes, collective_id=0, has_side_effects=True
        ),
        name="group_sum",
    )(up, down, pk, pv, up_bias, down_bias)


def blank_kernel(*refs):
    pass


def blanks(shapes):
    return pl.pallas_call(
        blank_kernel,
        out_shape=list(shapes),
        out_specs=[pl.BlockSpec(memory_space=pl.ANY)] * len(shapes),
        name="blank",
    )()


def on_section(is_encoder, encoder_work, decoder_work, *operands):
    enc_shapes, _ = jax.eval_shape(encoder_work, *operands)
    dec_shapes, _ = jax.eval_shape(decoder_work, *operands)

    def blank_like(shapes):
        leaves, tree = jax.tree.flatten(shapes)
        if not leaves:
            return shapes
        return jax.tree.unflatten(tree, blanks(leaves))

    def encoder_branch(*a):
        own, shared = encoder_work(*a)
        return own, blank_like(dec_shapes), shared

    def decoder_branch(*a):
        own, shared = decoder_work(*a)
        return blank_like(enc_shapes), own, shared

    return lax.cond(is_encoder, encoder_branch, decoder_branch, *operands)


def to_decoder(block):
    return lax.ppermute(block, "section", [(0, 1)])


def to_encoder(block):
    return lax.ppermute(block, "section", [(1, 0)])


def per_device(
    sources, targets, cotangent, source_lengths, target_lengths,
    attn_qkv, attn_out, ffn_in, ffn_out, norm_gains, prefix_pairs,
    adapt_down, adapt_down_bias, adapt_up, adapt_up_bias,
    cross_query, cross_pairs, cross_out, cross_gain,
):
    is_encoder = lax.axis_index("section") == 0
    prefix = jnp.pad(prefix_pairs[0], ((0, 0), (0, PRE_PAD - PRE), (0, 0)))
    w = dict(
        qkv=attn_qkv[0], out=attn_out[0], ffn_in=ffn_in[0], ffn_out=ffn_out[0],
        gains=norm_gains[0], prefix=(prefix[0], prefix[1]),
        down=adapt_down[0], down_bias=adapt_down_bias,
        up=adapt_up[0], up_bias=adapt_up_bias,
    )
    cross = dict(query=cross_query, pairs=cross_pairs, out=cross_out, gain=cross_gain[None])
    half = sources.shape[1] // 2

    (mem, saved), (cq, kept), _ = on_section(
        is_encoder,
        lambda: (encoder_forward(sources, source_lengths, w), ()),
        lambda: (decoder_self(targets, target_lengths, w, cross), ()),
    )
    mem_here = to_decoder(mem)
    _, (y, dmem, dcq, dsecond, dec_adapter), _ = on_section(
        is_encoder,
        lambda *a: ((), ()),
        lambda *a: (decoder_cross(*a, cotangent, source_lengths, target_lengths, w, cross), ()),
        kept, mem_here, cq,
    )
    dmem_here = to_encoder(dmem)

    def encoder_c1(saved, dmem, kept, dsecond, dcq, dec_adapter):
        dfirst, datt, adapter = encoder_back_ffn(saved, dmem, w)
        return (dfirst, datt), adapter

    def decoder_c1(saved, dmem, kept, dsecond, dcq, dec_adapter):
        return decoder_self_back(kept, dsecond, dcq, w, cross), dec_adapter

    (dfirst, datt), (dt, dec_prefix), adapter = on_section(
        is_encoder, encoder_c1, decoder_c1, saved, dmem_here, kept, dsecond, dcq, dec_adapter
    )
    low_halves = to_encoder(jnp.concatenate([y[:, :half], dt[:, :half]], 0))
    dx, _, prefix_grads = on_section(
        is_encoder,
        lambda saved, dfirst, datt, dec_prefix: encoder_back_self(saved, dfirst, datt, w),
        lambda saved, dfirst, datt, dec_prefix: ((), dec_prefix),
        saved, dfirst, datt, dec_prefix,
    )
    dx_high = to_decoder(dx[:, half:])
    ddown, ddownb, dup, dupb = adapter
    up, down, pk, pv, bias = group_sum(dup, ddown, *prefix_grads, dupb, ddownb)
    targets_rows = y.shape[0]
    return (
        jnp.where(is_encoder, low_halves[:targets_rows], y[:, half:]),
        jnp.where(is_encoder, dx[:, :half], dx_high),
        jnp.where(is_encoder, low_halves[targets_rows:], dt[:, half:]),
        jnp.stack([pk[:PRE], pv[:PRE]])[None],
        down[None],
        bias[1:2, : down.shape[1]],
        up[None],
        bias[0:1],
    )


def solution(mesh):
    layer2, layer3, rows = P("section", None), P("section", None, None), P("dp", None)
    return jax.shard_map(
        per_device,
        mesh=mesh,
        in_specs=(
            rows, rows, rows, rows, rows,
            layer3, layer3, layer3, layer3, layer3,
            P("section", None, None, None),
            layer3, layer2, layer3, layer2,
            P(), P(), P(), P(),
        ),
        out_specs=(
            P("dp", "section"), P("dp", "section"), P("dp", "section"),
            P("section", None, None, None), layer3, layer2, layer3, layer2,
        ),
        check_vma=False,
    )
```

```python
import functools

import jax
import jax.numpy as jnp
from jax import lax
from jax.experimental import pallas as pl
from jax.experimental.pallas import tpu as pltpu
from jax.sharding import PartitionSpec as P

HD = 64
PRE = 30
PRE_PAD = 32
SRC_LONG = 768
SRC_SHORT = 96
TGT = 256
LANES = 128

BF = jnp.bfloat16
F32 = jnp.float32
norm_eps = 1e-05
big_negative = -1e30
adapter_scale = 4.0
chunk = 512
vmem_bytes = 56 * 2**20

phi_poly = (
    0.797869713181688,
    0.036392283539041996,
    -8.782472977701046e-05,
    -3.669384069669515e-05,
    1.4250308145882202e-06,
)


def nn(left, right):
    return lax.dot_general(left, right, (((1,), (0,)), ((), ())), preferred_element_type=F32)


def nt(left, right):
    return lax.dot_general(left, right, (((1,), (1,)), ((), ())), preferred_element_type=F32)


def tn(left, right):
    return lax.dot_general(left, right, (((0,), (0,)), ((), ())), preferred_element_type=F32)


def gelu_pair(values):
    square = values * values
    poly = phi_poly[4]
    for coefficient in phi_poly[3::-1]:
        poly = poly * square + coefficient
    half = 0.5 * jnp.tanh(values * poly) + 0.5
    density = jnp.exp(square * -0.5) * 0.3989422804014327
    return values * half, half + values * density


def row_tiles(rows, most=288):
    count = -(-rows // most)
    size = rows // count
    return [(i * size, size) for i in range(count)]


def norm_rows(values):
    centered = values - jnp.mean(values, axis=-1, keepdims=True)
    scale = lax.rsqrt(jnp.mean(centered * centered, axis=-1, keepdims=True) + norm_eps)
    return centered * scale, scale


def norm_rows_back(hat, scale, grad_hat):
    mean_grad = jnp.mean(grad_hat, axis=-1, keepdims=True)
    mean_dot = jnp.mean(grad_hat * hat, axis=-1, keepdims=True)
    return scale * (grad_hat - mean_grad - hat * mean_dot)


def params(limit=vmem_bytes):
    return pltpu.CompilerParams(vmem_limit_bytes=limit)


def whole(shape):
    return pl.BlockSpec(shape, lambda *g: (0,) * len(shape))


def product_kernel(x_ref, w_ref, o_ref):
    o_ref[...] = nn(x_ref[...], w_ref[...]).astype(BF)


def product(x, w, tile=512):
    rows, depth = x.shape
    width = w.shape[1]
    return pl.pallas_call(
        product_kernel,
        grid=(width // tile,),
        in_specs=[whole((rows, depth)), pl.BlockSpec((depth, tile), lambda i: (0, i))],
        out_specs=pl.BlockSpec((rows, tile), lambda i: (0, i)),
        out_shape=jax.ShapeDtypeStruct((rows, width), BF),
        compiler_params=params(),
        name="product",
    )(x, w)


def back_product_kernel(*refs, parts, residual):
    grads = refs[:parts]
    w_ref = refs[parts]
    o_ref = refs[-1]
    total = None
    width = grads[0].shape[1]
    for i, grad in enumerate(grads):
        term = nt(grad[...], w_ref[:, i * width : (i + 1) * width])
        total = term if total is None else total + term
    if residual:
        total = total + refs[parts + 1][...]
    o_ref[...] = total.astype(BF)


def back_product(grads, w, residual=None, tile=256):
    rows, width = grads[0].shape
    depth = w.shape[0]
    parts = len(grads)
    specs = [whole((rows, width))] * parts + [
        pl.BlockSpec((tile, parts * width), lambda i: (i, 0))
    ]
    args = list(grads) + [w]
    if residual is not None:
        specs.append(pl.BlockSpec((rows, tile), lambda i: (0, i)))
        args.append(residual)
    return pl.pallas_call(
        functools.partial(back_product_kernel, parts=parts, residual=residual is not None),
        grid=(depth // tile,),
        in_specs=specs,
        out_specs=pl.BlockSpec((rows, tile), lambda i: (0, i)),
        out_shape=jax.ShapeDtypeStruct((rows, depth), BF),
        compiler_params=params(),
        name="back_product",
    )(*args)


def head_lanes(head):
    lane = lax.broadcasted_iota(jnp.int32, (1, LANES), 1)
    own = (lane < HD) if head == 0 else (lane >= HD)
    first = HD if head == 0 else 0
    return own, lane == first, lane == first + 1


def bf(value):
    return jnp.asarray(value, BF)


def stacked(rows_ref, prefix_ref, start, count):
    rows = rows_ref[start : start + count]
    if prefix_ref is None:
        return rows
    return jnp.concatenate([rows, prefix_ref[...]], 0)


def attend_kernel(*refs, segs, prefix, causal):
    len_ref, q_ref, k_ref, v_ref = refs[:4]
    at = 4
    pk_ref = pv_ref = None
    if prefix:
        pk_ref, pv_ref = refs[4:6]
        at = 6
    o_ref, inv_ref = refs[at : at + 2]
    p_refs = refs[at + 2 :]
    for seg, (q0, nq, k0, nk) in enumerate(segs):
        keys = stacked(k_ref, pk_ref, k0, nk)
        values = stacked(v_ref, pv_ref, k0, nk)
        count = keys.shape[0]
        row = lax.broadcasted_iota(jnp.int32, (count, 1), 0)
        seen = row < jnp.minimum(len_ref[0, seg], nk)
        if prefix:
            seen = seen | ((row >= nk) & (row < nk + PRE))
        queries = q_ref[q0 : q0 + nq] * bf(HD**-0.5)
        out = inv = None
        for head in range(2):
            own, first, _ = head_lanes(head)
            k_own = jnp.where(own, keys, jnp.where(first & ~seen, bf(big_negative), bf(0)))
            q_own = jnp.where(own, queries, jnp.where(first, bf(1), bf(0)))
            v_own = jnp.where(own, values, bf(1))
            scores = nt(k_own, q_own)
            if causal:
                key_at = lax.broadcasted_iota(jnp.int32, scores.shape, 0)
                query_at = lax.broadcasted_iota(jnp.int32, scores.shape, 1)
                allowed = (key_at <= query_at) | (key_at >= nk)
                scores = jnp.where(allowed, scores, big_negative)
            peak = jnp.max(scores, axis=0, keepdims=True)
            weights = jnp.exp(scores - peak).astype(BF)
            p_refs[seg][head] = weights
            mixed = tn(weights, v_own)
            inverse = 1.0 / pltpu.roll(mixed, HD, 1)
            mixed = mixed * inverse
            out = mixed if out is None else jnp.where(own, mixed, out)
            inv = inverse if inv is None else jnp.where(own, inverse, inv)
        o_ref[q0 : q0 + nq] = out.astype(BF)
        inv_ref[q0 : q0 + nq] = inv


def column_spec(rows, offset):
    return pl.BlockSpec((rows, LANES), lambda h: (0, h + offset))


def attend(lengths, q, k, v, prefixes, segs, causal):
    pairs = 8
    q_rows, k_rows = q[0].shape[0], k[0].shape[0]
    prefix = prefixes is not None
    extra = PRE_PAD if prefix else 0
    specs = [
        pl.BlockSpec(memory_space=pltpu.SMEM),
        column_spec(q_rows, q[1]),
        column_spec(k_rows, k[1]),
        column_spec(k_rows, v[1]),
    ]
    args = [lengths, q[0], k[0], v[0]]
    if prefix:
        specs += [column_spec(PRE_PAD, 0)] * 2
        args += list(prefixes)
    weight_shapes = [(2 * pairs, nk + extra, nq) for _, nq, _, nk in segs]
    return pl.pallas_call(
        functools.partial(attend_kernel, segs=segs, prefix=prefix, causal=causal),
        grid=(pairs,),
        in_specs=specs,
        out_specs=[column_spec(q_rows, 0), column_spec(q_rows, 0)]
        + [pl.BlockSpec((2,) + s[1:], lambda h: (h, 0, 0)) for s in weight_shapes],
        out_shape=[
            jax.ShapeDtypeStruct((q_rows, pairs * LANES), BF),
            jax.ShapeDtypeStruct((q_rows, pairs * LANES), F32),
        ]
        + [jax.ShapeDtypeStruct(s, BF) for s in weight_shapes],
        compiler_params=params(),
        name="attend",
    )(*args)


def attend_back_pair(
    q_ref, k_ref, v_ref, o_ref, inv_ref, g_ref, pk_ref, pv_ref, p_refs, dq_ref, dk_ref, dv_ref, segs
):
    prefix_totals = [None, None]
    scale = HD**-0.5
    for seg, (q0, nq, k0, nk) in enumerate(segs):
        keys = stacked(k_ref, pk_ref, k0, nk)
        values = stacked(v_ref, pv_ref, k0, nk)
        queries = q_ref[q0 : q0 + nq]
        grads = g_ref[q0 : q0 + nq].astype(F32) * inv_ref[q0 : q0 + nq]
        grads_low = grads.astype(BF)
        dots = grads * o_ref[q0 : q0 + nq].astype(F32)
        dq = dk = dv = None
        for head in range(2):
            own, first, second = head_lanes(head)
            row_dot = -jnp.sum(jnp.where(own, dots, 0.0), axis=1, keepdims=True)
            high = row_dot.astype(BF)
            rest = (row_dot - high.astype(F32)).astype(BF)
            g_own = jnp.where(
                own, grads_low, jnp.where(first, high, jnp.where(second, rest, bf(0)))
            )
            v_own = jnp.where(own, values, jnp.where(first | second, bf(1), bf(0)))
            weights = p_refs[seg][head]
            score_grad = (weights.astype(F32) * nt(v_own, g_own)).astype(BF)
            dv_head = nn(weights, grads_low)
            dk_head = nn(score_grad, queries)
            dq_head = tn(score_grad, keys)
            dq = dq_head if dq is None else jnp.where(own, dq_head, dq)
            dk = dk_head if dk is None else jnp.where(own, dk_head, dk)
            dv = dv_head if dv is None else jnp.where(own, dv_head, dv)
        dk = dk * scale
        dq_ref[q0 : q0 + nq] = (dq * scale).astype(BF)
        dk_ref[k0 : k0 + nk] = dk[:nk].astype(BF)
        dv_ref[k0 : k0 + nk] = dv[:nk].astype(BF)
        if pk_ref is not None:
            for i, grad in enumerate((dk, dv)):
                part = grad[nk:]
                prefix_totals[i] = part if seg == 0 else prefix_totals[i] + part
    return prefix_totals


def attend_back_kernel(*refs, segs, prefix):
    at = 8 if prefix else 6
    pk_ref, pv_ref = refs[6:8] if prefix else (None, None)
    outs = refs[at + len(segs) :]
    totals = attend_back_pair(
        *refs[:6], pk_ref, pv_ref, refs[at : at + len(segs)], *outs[:3], segs
    )
    if prefix:
        outs[3][...] = totals[0]
        outs[4][...] = totals[1]


def attend_back(q, k, v, prefixes, attended, inverse, grad, weights, segs):
    pairs = 8
    q_rows, k_rows = q[0].shape[0], k[0].shape[0]
    prefix = prefixes is not None
    specs = [
        column_spec(q_rows, q[1]),
        column_spec(k_rows, k[1]),
        column_spec(k_rows, v[1]),
        column_spec(q_rows, 0),
        column_spec(q_rows, 0),
        column_spec(q_rows, 0),
    ]
    args = [q[0], k[0], v[0], attended, inverse, grad]
    if prefix:
        specs += [column_spec(PRE_PAD, 0)] * 2
        args += list(prefixes)
    specs += [pl.BlockSpec((2,) + w.shape[1:], lambda h: (h, 0, 0)) for w in weights]
    args += list(weights)
    out_specs = [column_spec(q_rows, 0), column_spec(k_rows, 0), column_spec(k_rows, 0)]
    out_shape = [
        jax.ShapeDtypeStruct((q_rows, pairs * LANES), BF),
        jax.ShapeDtypeStruct((k_rows, pairs * LANES), BF),
        jax.ShapeDtypeStruct((k_rows, pairs * LANES), BF),
    ]
    if prefix:
        out_specs += [column_spec(PRE_PAD, 0)] * 2
        out_shape += [jax.ShapeDtypeStruct((PRE_PAD, pairs * LANES), F32)] * 2
    return pl.pallas_call(
        functools.partial(attend_back_kernel, segs=segs, prefix=prefix),
        grid=(pairs,),
        in_specs=specs,
        out_specs=out_specs,
        out_shape=out_shape,
        compiler_params=params(),
        name="attend_back",
    )(*args)


def ffn_step(low_ref, acc_ref, in_ref, out_ref, slope_ref, act_ref, bias_ref, scale):
    for start, size in row_tiles(low_ref.shape[0]):
        rows = slice(start, start + size)
        hidden = nn(low_ref[rows], in_ref[...])
        if bias_ref is not None:
            hidden = hidden + bias_ref[...]
        active, slope = gelu_pair(hidden)
        slope_ref[rows] = slope.astype(BF)
        active = active.astype(BF)
        if act_ref is not None:
            act_ref[rows] = active
        term = nn(active, out_ref[...])
        acc_ref[rows] += term if scale is None else scale * term


def enc_ffn_kernel(
    x_ref, att_ref, wo_ref, gain_ref, in_ref, out_ref, down_ref, downb_ref, up_ref, upb_ref,
    mem_ref, slope_ref, act_ref, low_ref, scales_ref, acc_ref,
):
    step = pl.program_id(0)
    last = pl.num_programs(0) - 1

    @pl.when(step == 0)
    def _():
        for start, size in row_tiles(x_ref.shape[0]):
            rows = slice(start, start + size)
            first = x_ref[rows].astype(F32) + nn(att_ref[rows], wo_ref[...])
            hat, scale = norm_rows(first)
            normed = hat * gain_ref[0:1]
            acc_ref[rows] = normed
            low_ref[rows] = normed.astype(BF)
            scales_ref[rows, 0:1] = scale

    @pl.when((step > 0) & (step < last))
    def _():
        ffn_step(low_ref, acc_ref, in_ref, out_ref, slope_ref, None, None, None)

    @pl.when(step == last)
    def _():
        ffn_step(low_ref, acc_ref, down_ref, up_ref, slope_ref, act_ref, downb_ref, adapter_scale)
        for start, size in row_tiles(x_ref.shape[0]):
            rows = slice(start, start + size)
            hat, scale = norm_rows(acc_ref[rows] + adapter_scale * upb_ref[...])
            mem_ref[rows] = (hat * gain_ref[1:2]).astype(BF)
            scales_ref[rows, 1:2] = scale


def enc_ffn(x, att, w):
    rows, width = x.shape
    hidden = w["ffn_in"].shape[1]
    steps = hidden // chunk

    def at(i):
        return jnp.clip(i - 1, 0, steps - 1)

    return pl.pallas_call(
        enc_ffn_kernel,
        grid=(steps + 2,),
        in_specs=[
            whole((rows, width)),
            whole((rows, width)),
            whole((width, width)),
            whole((2, width)),
            pl.BlockSpec((width, chunk), lambda i: (0, at(i))),
            pl.BlockSpec((chunk, width), lambda i: (at(i), 0)),
            whole((width, chunk)),
            whole((1, chunk)),
            whole((chunk, width)),
            whole((1, width)),
        ],
        out_specs=[
            whole((rows, width)),
            pl.BlockSpec((rows, chunk), lambda i: (0, jnp.clip(i - 1, 0, steps))),
            whole((rows, chunk)),
            whole((rows, width)),
            whole((rows, LANES)),
        ],
        out_shape=[
            jax.ShapeDtypeStruct((rows, width), BF),
            jax.ShapeDtypeStruct((rows, hidden + chunk), BF),
            jax.ShapeDtypeStruct((rows, chunk), BF),
            jax.ShapeDtypeStruct((rows, width), BF),
            jax.ShapeDtypeStruct((rows, LANES), F32),
        ],
        scratch_shapes=[pltpu.VMEM((rows, width), F32)],
        compiler_params=params(),
        name="enc_ffn",
    )(
        x, att, w["out"], w["gains"], w["ffn_in"], w["ffn_out"],
        w["down"], w["down_bias"], w["up"], w["up_bias"],
    )


def ffn_back_step(grad_ref, acc_ref, in_ref, out_ref, slope_ref):
    for start, size in row_tiles(grad_ref.shape[0]):
        rows = slice(start, start + size)
        pre = (nt(grad_ref[rows], out_ref[...]) * slope_ref[rows].astype(F32)).astype(BF)
        acc_ref[rows] += nt(pre, in_ref[...])


def adapter_back(grad_ref, acc_ref, low_ref, act_ref, slope_ref, down_ref, up_ref, outs, pre_ref):
    ddown_ref, ddownb_ref, dup_ref, dupb_ref = outs
    total = None
    for start, size in row_tiles(grad_ref.shape[0]):
        rows = slice(start, start + size)
        back = adapter_scale * nt(grad_ref[rows], up_ref[...])
        pre = (back * slope_ref[rows].astype(F32)).astype(BF)
        pre_ref[rows] = pre
        sums = jnp.sum(pre.astype(F32), axis=0, keepdims=True)
        total = sums if total is None else total + sums
        acc_ref[rows] += nt(pre, down_ref[...])
    ddownb_ref[...] = total
    ddown_ref[...] = tn(low_ref[...], pre_ref[...])
    dup_ref[...] = adapter_scale * tn(act_ref[...], grad_ref[...])
    dupb_ref[...] = adapter_scale * jnp.sum(grad_ref[...].astype(F32), axis=0, keepdims=True)


def enc_ffn_back_kernel(
    dmem_ref, mem_ref, low_ref, scales_ref, gain_ref, slope_ref, act_ref,
    in_ref, out_ref, down_ref, up_ref, wo_ref,
    dfirst_ref, datt_ref, ddown_ref, ddownb_ref, dup_ref, dupb_ref,
    acc_ref, grad_ref, pre_ref,
):
    step = pl.program_id(0)
    last = pl.num_programs(0) - 1

    @pl.when(step == 0)
    def _():
        for start, size in row_tiles(dmem_ref.shape[0]):
            rows = slice(start, start + size)
            gain = gain_ref[1:2]
            hat = mem_ref[rows].astype(F32) / gain
            grad = norm_rows_back(
                hat, scales_ref[rows, 1:2], dmem_ref[rows].astype(F32) * gain
            )
            acc_ref[rows] = grad
            grad_ref[rows] = grad.astype(BF)
        adapter_back(
            grad_ref, acc_ref, low_ref, act_ref, slope_ref, down_ref, up_ref,
            (ddown_ref, ddownb_ref, dup_ref, dupb_ref), pre_ref,
        )

    @pl.when(step > 0)
    def _():
        ffn_back_step(grad_ref, acc_ref, in_ref, out_ref, slope_ref)

    @pl.when(step == last)
    def _():
        for start, size in row_tiles(dmem_ref.shape[0]):
            rows = slice(start, start + size)
            gain = gain_ref[0:1]
            hat = low_ref[rows].astype(F32) / gain
            grad = norm_rows_back(hat, scales_ref[rows, 0:1], acc_ref[rows] * gain)
            dfirst_ref[rows] = grad
            datt_ref[rows] = nt(grad.astype(BF), wo_ref[...]).astype(BF)


def enc_ffn_back(dmem, mem, low, scales, slope, act, w):
    rows, width = dmem.shape
    hidden = w["ffn_in"].shape[1]
    steps = hidden // chunk

    def at(i):
        return jnp.clip(i - 1, 0, steps - 1)

    return pl.pallas_call(
        enc_ffn_back_kernel,
        grid=(steps + 1,),
        in_specs=[
            whole((rows, width)),
            whole((rows, width)),
            whole((rows, width)),
            whole((rows, LANES)),
            whole((2, width)),
            pl.BlockSpec((rows, chunk), lambda i: (0, jnp.where(i == 0, steps, i - 1))),
            whole((rows, chunk)),
            pl.BlockSpec((width, chunk), lambda i: (0, at(i))),
            pl.BlockSpec((chunk, width), lambda i: (at(i), 0)),
            whole((width, chunk)),
            whole((chunk, width)),
            whole((width, width)),
        ],
        out_specs=[
            whole((rows, width)),
            whole((rows, width)),
            whole((width, chunk)),
            whole((1, chunk)),
            whole((chunk, width)),
            whole((1, width)),
        ],
        out_shape=[
            jax.ShapeDtypeStruct((rows, width), F32),
            jax.ShapeDtypeStruct((rows, width), BF),
            jax.ShapeDtypeStruct((width, chunk), F32),
            jax.ShapeDtypeStruct((1, chunk), F32),
            jax.ShapeDtypeStruct((chunk, width), F32),
            jax.ShapeDtypeStruct((1, width), F32),
        ],
        scratch_shapes=[
            pltpu.VMEM((rows, width), F32),
            pltpu.VMEM((rows, width), BF),
            pltpu.VMEM((rows, chunk), BF),
        ],
        compiler_params=params(),
        name="enc_ffn_back",
    )(
        dmem, mem, low, scales, w["gains"], slope, act,
        w["ffn_in"], w["ffn_out"], w["down"], w["up"], w["out"],
    )


def dec_mid_kernel(x_ref, att_ref, wo_ref, gain_ref, wq_ref, n_ref, scale_ref, cq_ref):
    for start, size in row_tiles(x_ref.shape[0], 256):
        rows = slice(start, start + size)
        first = x_ref[rows].astype(F32) + nn(att_ref[rows], wo_ref[...])
        hat, scale = norm_rows(first)
        normed = hat * gain_ref[0:1]
        n_ref[rows] = normed
        scale_ref[rows, 0:1] = scale
        cq_ref[rows] = nn(normed.astype(BF), wq_ref[...]).astype(BF)


def dec_mid(x, att, w, cross):
    rows, width = x.shape
    return pl.pallas_call(
        dec_mid_kernel,
        out_shape=[
            jax.ShapeDtypeStruct((rows, width), F32),
            jax.ShapeDtypeStruct((rows, LANES), F32),
            jax.ShapeDtypeStruct((rows, width), BF),
        ],
        compiler_params=params(),
        name="dec_mid",
    )(x, att, w["out"], w["gains"], cross["query"])


def dec_ffn_kernel(
    len_ref, n_ref, catt_ref, cot_ref, wco_ref, cgain_ref, gain_ref,
    in_ref, out_ref, down_ref, downb_ref, up_ref, upb_ref,
    y_ref, dsecond_ref, dcatt_ref, ddown_ref, ddownb_ref, dup_ref, dupb_ref,
    acc_ref, low_ref, grad_ref, slope_ref, act_ref, pre_ref, scale_ref,
    *, steps,
):
    step = pl.program_id(0)
    tiles = row_tiles(n_ref.shape[0], TGT)

    @pl.when(step == 0)
    def _():
        for start, size in tiles:
            rows = slice(start, start + size)
            second = n_ref[rows] + nn(catt_ref[rows], wco_ref[...])
            hat, scale = norm_rows(second)
            middle = hat * cgain_ref[...]
            acc_ref[rows] = middle
            low_ref[rows] = middle.astype(BF)
            scale_ref[rows, 0:1] = scale

    @pl.when((step > 0) & (step <= steps))
    def _():
        ffn_step(low_ref, acc_ref, in_ref, out_ref, slope_ref.at[step - 1], None, None, None)

    @pl.when(step == steps + 1)
    def _():
        ffn_step(
            low_ref, acc_ref, down_ref, up_ref, slope_ref.at[steps], act_ref, downb_ref,
            adapter_scale,
        )
        for tile, (start, size) in enumerate(tiles):
            rows = slice(start, start + size)
            gain = gain_ref[1:2]
            hat, scale = norm_rows(acc_ref[rows] + adapter_scale * upb_ref[...])
            valid = lax.broadcasted_iota(jnp.int32, (size, 1), 0) < len_ref[0, tile]
            y_ref[rows] = jnp.where(valid, hat * gain, 0.0).astype(BF)
            cot = jnp.where(valid, cot_ref[rows].astype(F32), 0.0)
            grad = norm_rows_back(hat, scale, cot * gain)
            acc_ref[rows] = grad
            grad_ref[rows] = grad.astype(BF)
        adapter_back(
            grad_ref, acc_ref, low_ref, act_ref, slope_ref.at[steps], down_ref, up_ref,
            (ddown_ref, ddownb_ref, dup_ref, dupb_ref), pre_ref,
        )

    @pl.when(step > steps + 1)
    def _():
        ffn_back_step(grad_ref, acc_ref, in_ref, out_ref, slope_ref.at[2 * steps + 1 - step])

    @pl.when(step == 2 * steps + 1)
    def _():
        for start, size in tiles:
            rows = slice(start, start + size)
            gain = cgain_ref[...]
            hat = low_ref[rows].astype(F32) / gain
            grad = norm_rows_back(hat, scale_ref[rows, 0:1], acc_ref[rows] * gain)
            dsecond_ref[rows] = grad
            dcatt_ref[rows] = nt(grad.astype(BF), wco_ref[...]).astype(BF)


def dec_ffn(lengths, n, catt, cot, w, cross):
    rows, width = n.shape
    hidden = w["ffn_in"].shape[1]
    steps = hidden // chunk

    def at(i):
        return jnp.where(i <= steps, jnp.clip(i - 1, 0, steps - 1), jnp.clip(2 * steps + 1 - i, 0, steps - 1))

    return pl.pallas_call(
        functools.partial(dec_ffn_kernel, steps=steps),
        grid=(2 * steps + 2,),
        in_specs=[
            pl.BlockSpec(memory_space=pltpu.SMEM),
            whole((rows, width)),
            whole((rows, width)),
            whole((rows, width)),
            whole((width, width)),
            whole((1, width)),
            whole((2, width)),
            pl.BlockSpec((width, chunk), lambda i: (0, at(i))),
            pl.BlockSpec((chunk, width), lambda i: (at(i), 0)),
            whole((width, chunk)),
            whole((1, chunk)),
            whole((chunk, width)),
            whole((1, width)),
        ],
        out_specs=[
            whole((rows, width)),
            whole((rows, width)),
            whole((rows, width)),
            whole((width, chunk)),
            whole((1, chunk)),
            whole((chunk, width)),
            whole((1, width)),
        ],
        out_shape=[
            jax.ShapeDtypeStruct((rows, width), BF),
            jax.ShapeDtypeStruct((rows, width), F32),
            jax.ShapeDtypeStruct((rows, width), BF),
            jax.ShapeDtypeStruct((width, chunk), F32),
            jax.ShapeDtypeStruct((1, chunk), F32),
            jax.ShapeDtypeStruct((chunk, width), F32),
            jax.ShapeDtypeStruct((1, width), F32),
        ],
        scratch_shapes=[
            pltpu.VMEM((rows, width), F32),
            pltpu.VMEM((rows, width), BF),
            pltpu.VMEM((rows, width), BF),
            pltpu.VMEM((steps + 1, rows, chunk), BF),
            pltpu.VMEM((rows, chunk), BF),
            pltpu.VMEM((rows, chunk), BF),
            pltpu.VMEM((rows, LANES), F32),
        ],
        compiler_params=params(),
        name="dec_ffn",
    )(
        lengths, n, catt, cot, cross["out"], cross["gain"], w["gains"],
        w["ffn_in"], w["ffn_out"], w["down"], w["down_bias"], w["up"], w["up_bias"],
    )


def dec_mid_back_kernel(
    dsecond_ref, dcq_ref, wq_ref, n_ref, scale_ref, gain_ref, wo_ref, dfirst_ref, datt_ref
):
    for start, size in row_tiles(n_ref.shape[0], 256):
        rows = slice(start, start + size)
        gain = gain_ref[0:1]
        total = dsecond_ref[rows] + nt(dcq_ref[rows], wq_ref[...])
        grad = norm_rows_back(n_ref[rows] / gain, scale_ref[rows, 0:1], total * gain)
        dfirst_ref[rows] = grad
        datt_ref[rows] = nt(grad.astype(BF), wo_ref[...]).astype(BF)


def dec_mid_back(dsecond, dcq, n, scale, w, cross):
    rows, width = n.shape
    return pl.pallas_call(
        dec_mid_back_kernel,
        out_shape=[
            jax.ShapeDtypeStruct((rows, width), F32),
            jax.ShapeDtypeStruct((rows, width), BF),
        ],
        compiler_params=params(),
        name="dec_mid_back",
    )(dsecond, dcq, cross["query"], n, scale, w["gains"], w["out"])


enc_segs = ((0, SRC_LONG, 0, SRC_LONG), (SRC_LONG, SRC_SHORT, SRC_LONG, SRC_SHORT))
dec_segs = ((0, TGT, 0, TGT), (TGT, TGT, TGT, TGT))
cross_segs = ((0, TGT, 0, SRC_LONG), (TGT, TGT, SRC_LONG, SRC_SHORT))


def encoder_forward(x, lengths, w):
    qkv = product(x, w["qkv"])
    att, inv, *weights = attend(
        lengths, (qkv, 0), (qkv, 8), (qkv, 16), w["prefix"], enc_segs, False
    )
    mem, slope, act, low, scales = enc_ffn(x, att, w)
    return mem, (qkv, att, inv, weights, mem, slope, act, low, scales)


def encoder_back_ffn(saved, dmem, w):
    mem, slope, act, low, scales = saved[4:]
    dfirst, datt, *adapter = enc_ffn_back(dmem, mem, low, scales, slope, act, w)
    return dfirst, datt, adapter


def decoder_self(t, lengths, w, cross):
    qkv = product(t, w["qkv"])
    att, inv, *weights = attend(
        lengths, (qkv, 0), (qkv, 8), (qkv, 16), w["prefix"], dec_segs, True
    )
    n, scale, cq = dec_mid(t, att, w, cross)
    return cq, (qkv, att, inv, weights, n, scale)


def decoder_cross(kept, mem, cq, cot, src_lengths, tgt_lengths, w, cross):
    n = kept[4]
    kv = product(mem, cross["pairs"])
    catt, cinv, *cweights = attend(
        src_lengths, (cq, 0), (kv, 0), (kv, 8), None, cross_segs, False
    )
    y, dsecond, dcatt, *adapter = dec_ffn(tgt_lengths, n, catt, cot, w, cross)
    dcq, dck, dcv = attend_back(
        (cq, 0), (kv, 0), (kv, 8), None, catt, cinv, dcatt, cweights, cross_segs
    )
    dmem = back_product([dck, dcv], cross["pairs"])
    return y, dmem, dcq, dsecond, adapter


def decoder_self_back(kept, dsecond, dcq, w, cross):
    qkv, att, inv, weights, n, scale = kept
    dfirst, datt = dec_mid_back(dsecond, dcq, n, scale, w, cross)
    dq, dk, dv, *dprefix = attend_back(
        (qkv, 0), (qkv, 8), (qkv, 16), w["prefix"], att, inv, datt, weights, dec_segs
    )
    return back_product([dq, dk, dv], w["qkv"], dfirst), dprefix


def small_shape(devices):
    return 8, 8 * (2 * chunk) // devices


def finish_kernel(
    q_ref, k_ref, v_ref, o_ref, inv_ref, g_ref, pk_ref, pv_ref, pl_ref, ps_ref,
    dfirst_ref, wqkv_ref, up_ref, down_ref, upb_ref, downb_ref, dpk_ref, dpv_ref,
    y_ref, dt_ref,
    source_ref, low_ref, o_up_ref, o_down_ref, o_small_ref,
    dq, dk, dv, small, mine, theirs, half_sum, landed, total, result,
    small_landed, small_total, small_result, dx_low, dx_high, dx_landed, lows, lows_landed,
    pair_sems, spread_sems, gather_sems, back_sems, small_sems, share_sems, cross_sems,
    *, devices,
):
    step = pl.program_id(0)
    pairs = 8
    is_encoder = lax.axis_index("section") == 0
    section = lax.axis_index("section")
    chips = devices // 2
    rows = 2 * chunk
    half, part = rows // 2, rows // devices
    place = lax.axis_index("dp")
    core, chip = lax.rem(place, 2), place // 2
    partner = place + 1 - 2 * core
    small_rows, small_cols = small_shape(devices)
    tile = 256
    width = 2 * chunk
    scale = 1.0 / devices

    def peer(distance):
        return lax.rem(chip + distance, chips) * 2 + core

    def remote(source, target, send_sem, recv_sem, other):
        return pltpu.make_async_remote_copy(
            src_ref=source, dst_ref=target, send_sem=send_sem, recv_sem=recv_sem,
            device_id=other, device_id_type=pl.DeviceIdType.MESH,
        )

    def in_group(other):
        return {"dp": other}

    across = {"section": 1 - section}
    kept = pl.multiple_of(core * half, 16)
    given = pl.multiple_of((1 - core) * half, 16)
    here = pl.multiple_of(kept + chip * part, 16)

    def swap():
        return remote(
            mine.at[pl.ds(given, half)], theirs, pair_sems.at[0], pair_sems.at[1],
            in_group(partner),
        )

    def spread(s):
        at = pl.multiple_of(lax.rem(chip + s, chips) * part, 16)
        return remote(
            half_sum.at[pl.ds(at, part)], landed.at[s - 1],
            spread_sems.at[0, s - 1], spread_sems.at[1, s - 1], in_group(peer(s)),
        )

    def gather(s):
        return remote(
            total, result.at[pl.ds(here, part)],
            gather_sems.at[0, s - 1], gather_sems.at[1, s - 1], in_group(peer(s)),
        )

    def back(s):
        source = lax.rem(chip + chips - s, chips)
        there = pl.ds(pl.multiple_of(kept + source * part, 16), part)
        return remote(
            total if s == 0 else result.at[there], result.at[there],
            back_sems.at[0, s], back_sems.at[1, s], in_group(partner),
        )

    def piece(index):
        row = pl.multiple_of(lax.rem(index, 8) * small_rows, 8)
        col = pl.multiple_of((index // 8) * small_cols, LANES)
        return pl.ds(row, small_rows), pl.ds(col, small_cols)

    def small_out(s):
        return remote(
            small.at[piece(lax.rem(place + s, devices))], small_landed.at[s - 1],
            small_sems.at[0, s - 1], small_sems.at[1, s - 1],
            in_group(lax.rem(place + s, devices)),
        )

    def small_share(s):
        return remote(
            small_total, small_result.at[piece(place)],
            share_sems.at[0, s - 1], share_sems.at[1, s - 1],
            in_group(lax.rem(place + s, devices)),
        )

    def send_low():
        return remote(lows, lows_landed, cross_sems.at[0, 0], cross_sems.at[1, 0], across)

    def send_high(i):
        return remote(
            dx_high.at[i], dx_landed.at[i], cross_sems.at[0, 1 + i], cross_sems.at[1, 1 + i], across
        )

    @pl.when(step == 0)
    def _():
        barrier = pltpu.get_barrier_semaphore()
        others = [in_group(lax.rem(place + s, devices)) for s in range(1, devices)] + [across]
        for other in others:
            pl.semaphore_signal(
                barrier, inc=1, device_id=other, device_id_type=pl.DeviceIdType.MESH
            )
        mine[0:chunk] = (up_ref[...] * scale).astype(BF)
        mine[chunk:width, 0:chunk] = (down_ref[0:chunk] * scale).astype(BF)
        mine[chunk:width, chunk:width] = (down_ref[chunk:width] * scale).astype(BF)
        pl.semaphore_wait(barrier, devices)
        swap().start()

        @pl.when(jnp.logical_not(is_encoder))
        def _():
            lows[0] = y_ref[...]
            lows[1] = dt_ref[...]
            send_low().start()
            small[0:PRE_PAD] = dpk_ref[...] * scale
            small[PRE_PAD : 2 * PRE_PAD] = dpv_ref[...] * scale

    @pl.when(is_encoder & (step < pairs))
    def _():
        at = pl.multiple_of(step * LANES, LANES)
        lanes = pl.ds(at, LANES)
        prefix_totals = attend_back_pair(
            q_ref, k_ref, v_ref, o_ref, inv_ref, g_ref, pk_ref, pv_ref, (pl_ref, ps_ref),
            dq.at[:, lanes], dk.at[:, lanes], dv.at[:, lanes], enc_segs,
        )
        small[0:PRE_PAD, lanes] = prefix_totals[0] * scale
        small[PRE_PAD : 2 * PRE_PAD, lanes] = prefix_totals[1] * scale

    @pl.when(step == 1)
    def _():
        swap().wait()
        half_sum[...] = (
            mine[pl.ds(kept, half)].astype(F32) + theirs[...].astype(F32)
        ).astype(BF)
        for s in range(1, chips):
            spread(s).start()

    @pl.when(step == pairs - 1)
    def _():
        down_row = jnp.concatenate([downb_ref[...], jnp.zeros_like(downb_ref)], 1)
        small[PRE : PRE + 1] = upb_ref[...] * scale
        small[PRE + 1 : PRE + 2] = down_row * scale
        for s in range(1, devices):
            small_out(s).start()
        summed = half_sum[pl.ds(pl.multiple_of(chip * part, 16), part)].astype(F32)
        for s in range(1, chips):
            spread(s).wait()
            summed = summed + landed[s - 1].astype(F32)
        total[...] = summed.astype(BF)
        result[pl.ds(here, part)] = total[...]
        for s in range(1, chips):
            gather(s).start()
        back(0).start()

    for i in range(4):

        @pl.when(is_encoder & (step == pairs + i))
        def _(i=i):
            acc = dfirst_ref[...]
            for n, grad in enumerate((dq, dk, dv)):
                acc = acc + nt(grad[...], wqkv_ref[:, n * width : (n + 1) * width])
            if i < 2:
                dx_high[i] = acc.astype(BF)
                send_high(i).start()
            else:
                dx_low[:, (i - 2) * tile : (i - 1) * tile] = acc.astype(BF)

    @pl.when(step == pairs + 1)
    def _():
        own_rows, own_cols = piece(place)
        summed = small[own_rows, own_cols]
        for s in range(1, devices):
            small_out(s).wait()
            summed = summed + small_landed[s - 1]
        small_total[...] = summed
        small_result[own_rows, own_cols] = summed
        for s in range(1, devices):
            small_share(s).start()

    @pl.when(step == pairs + 3)
    def _():
        for s in range(1, chips):
            gather(s).wait()
            back(s).start()
        for s in range(1, devices):
            small_share(s).wait()
        for s in range(chips):
            back(s).wait()
        o_small_ref[...] = small_result[...]
        o_up_ref[...] = result[0:chunk].astype(F32)
        o_down_ref[0:chunk] = result[chunk:width, 0:chunk].astype(F32)
        o_down_ref[chunk:width] = result[chunk:width, chunk:width].astype(F32)

        @pl.when(is_encoder)
        def _():
            send_low().wait_recv()
            low_ref[...] = lows_landed[...]
            source_ref[...] = dx_low[...]
            for i in range(2):
                send_high(i).wait_send()

        @pl.when(jnp.logical_not(is_encoder))
        def _():
            send_low().wait_send()
            for i in range(2):
                send_high(i).wait_recv()
                source_ref[:, i * tile : (i + 1) * tile] = dx_landed[i]


def finish(saved, datt, dfirst, w, adapter, dec_prefix, y_low, dt_low):
    qkv, att, inv, weights = saved[:4]
    ddown, ddownb, dup, dupb = adapter
    devices = lax.axis_size("dp")
    chips = devices // 2
    rows, width = dfirst.shape
    targets = y_low.shape[0]
    pairs, tile = 8, 256
    half = width // 2
    part = width // devices
    small_rows, small_cols = small_shape(devices)

    def pair(offset):
        return pl.BlockSpec((rows, LANES), lambda i: (0, jnp.minimum(i, pairs - 1) + offset))

    def at(i):
        return jnp.where(i < pairs + 2, 2 + jnp.maximum(i - pairs, 0), i - pairs - 2)

    def once(shape):
        return pl.BlockSpec(shape, lambda i: (0,) * len(shape), pipeline_mode=pl.Buffered(1))

    prefix_pair = pl.BlockSpec((PRE_PAD, LANES), lambda i: (0, jnp.minimum(i, pairs - 1)))
    vmem = pltpu.VMEM
    dma = pltpu.SemaphoreType.DMA
    return pl.pallas_call(
        functools.partial(finish_kernel, devices=devices),
        grid=(pairs + 4,),
        in_specs=[pair(0), pair(8), pair(16), pair(0), pair(0), pair(0), prefix_pair, prefix_pair]
        + [
            pl.BlockSpec((2,) + p.shape[1:], lambda i: (jnp.minimum(i, pairs - 1), 0, 0))
            for p in weights
        ]
        + [
            pl.BlockSpec((rows, tile), lambda i: (0, at(i))),
            pl.BlockSpec((tile, 3 * width), lambda i: (at(i), 0)),
        ]
        + [once(a.shape) for a in (dup, ddown, dupb, ddownb, *dec_prefix, y_low, dt_low)],
        out_specs=[
            once((rows, half)), once((2, targets, half)), once(dup.shape), once(ddown.shape),
            once((2 * PRE_PAD, width)),
        ],
        out_shape=[
            jax.ShapeDtypeStruct((rows, half), BF),
            jax.ShapeDtypeStruct((2, targets, half), BF),
            jax.ShapeDtypeStruct(dup.shape, F32),
            jax.ShapeDtypeStruct(ddown.shape, F32),
            jax.ShapeDtypeStruct((2 * PRE_PAD, width), F32),
        ],
        scratch_shapes=[
            vmem((rows, width), BF), vmem((rows, width), BF), vmem((rows, width), BF),
            vmem((2 * PRE_PAD, width), F32),
            vmem((width, width), BF), vmem((half, width), BF), vmem((half, width), BF),
            vmem((chips - 1, part, width), BF), vmem((part, width), BF), vmem((width, width), BF),
            vmem((devices - 1, small_rows, small_cols), F32), vmem((small_rows, small_cols), F32),
            vmem((2 * PRE_PAD, width), F32),
            vmem((rows, half), BF), vmem((2, rows, tile), BF), vmem((2, rows, tile), BF),
            vmem((2, targets, half), BF), vmem((2, targets, half), BF),
            dma((2,)), dma((2, chips - 1)), dma((2, chips - 1)), dma((2, chips)),
            dma((2, devices - 1)), dma((2, devices - 1)), dma((2, 3)),
        ],
        compiler_params=pltpu.CompilerParams(
            vmem_limit_bytes=vmem_bytes, collective_id=0, has_side_effects=True
        ),
        name="finish",
    )(
        qkv, qkv, qkv, att, inv, datt, *w["prefix"], *weights,
        dfirst, w["qkv"], dup, ddown, dupb, ddownb, *dec_prefix, y_low, dt_low,
    )


def blank_kernel(*refs):
    pass


def blanks(shapes):
    return pl.pallas_call(
        blank_kernel,
        out_shape=list(shapes),
        out_specs=[pl.BlockSpec(memory_space=pl.ANY)] * len(shapes),
        name="blank",
    )()


def on_section(is_encoder, encoder_work, decoder_work, *operands):
    enc_shapes, _ = jax.eval_shape(encoder_work, *operands)
    dec_shapes, _ = jax.eval_shape(decoder_work, *operands)

    def blank_like(shapes):
        leaves, tree = jax.tree.flatten(shapes)
        if not leaves:
            return shapes
        return jax.tree.unflatten(tree, blanks(leaves))

    def encoder_branch(*a):
        own, shared = encoder_work(*a)
        return own, blank_like(dec_shapes), shared

    def decoder_branch(*a):
        own, shared = decoder_work(*a)
        return blank_like(enc_shapes), own, shared

    return lax.cond(is_encoder, encoder_branch, decoder_branch, *operands)


def to_decoder(block):
    return lax.ppermute(block, "section", [(0, 1)])


def to_encoder(block):
    return lax.ppermute(block, "section", [(1, 0)])


def per_device(
    sources, targets, cotangent, source_lengths, target_lengths,
    attn_qkv, attn_out, ffn_in, ffn_out, norm_gains, prefix_pairs,
    adapt_down, adapt_down_bias, adapt_up, adapt_up_bias,
    cross_query, cross_pairs, cross_out, cross_gain,
):
    is_encoder = lax.axis_index("section") == 0
    prefix = jnp.pad(prefix_pairs[0], ((0, 0), (0, PRE_PAD - PRE), (0, 0)))
    w = dict(
        qkv=attn_qkv[0], out=attn_out[0], ffn_in=ffn_in[0], ffn_out=ffn_out[0],
        gains=norm_gains[0], prefix=(prefix[0], prefix[1]),
        down=adapt_down[0], down_bias=adapt_down_bias,
        up=adapt_up[0], up_bias=adapt_up_bias,
    )
    cross = dict(query=cross_query, pairs=cross_pairs, out=cross_out, gain=cross_gain[None])
    half = sources.shape[1] // 2

    (mem, saved), (cq, kept), _ = on_section(
        is_encoder,
        lambda: (encoder_forward(sources, source_lengths, w), ()),
        lambda: (decoder_self(targets, target_lengths, w, cross), ()),
    )
    mem_here = to_decoder(mem)
    _, (y, dmem, dcq, dsecond, dec_adapter), _ = on_section(
        is_encoder,
        lambda *a: ((), ()),
        lambda *a: (decoder_cross(*a, cotangent, source_lengths, target_lengths, w, cross), ()),
        kept, mem_here, cq,
    )
    dmem_here = to_encoder(dmem)

    def encoder_c1(saved, dmem, kept, dsecond, dcq, dec_adapter):
        dfirst, datt, adapter = encoder_back_ffn(saved, dmem, w)
        return (dfirst, datt), adapter

    def decoder_c1(saved, dmem, kept, dsecond, dcq, dec_adapter):
        return decoder_self_back(kept, dsecond, dcq, w, cross), dec_adapter

    (dfirst, datt), (dt, dec_prefix), adapter = on_section(
        is_encoder, encoder_c1, decoder_c1, saved, dmem_here, kept, dsecond, dcq, dec_adapter
    )
    source_grad, low, up, down, small = finish(
        saved, datt, dfirst, w, adapter, dec_prefix, y[:, :half], dt[:, :half]
    )
    return (
        jnp.where(is_encoder, low[0], y[:, half:]),
        source_grad,
        jnp.where(is_encoder, low[1], dt[:, half:]),
        jnp.stack([small[:PRE], small[PRE_PAD : PRE_PAD + PRE]])[None],
        down[None],
        small[PRE + 1 : PRE + 2, : down.shape[1]],
        up[None],
        small[PRE : PRE + 1],
    )


def solution(mesh):
    layer2, layer3, rows = P("section", None), P("section", None, None), P("dp", None)
    return jax.shard_map(
        per_device,
        mesh=mesh,
        in_specs=(
            rows, rows, rows, rows, rows,
            layer3, layer3, layer3, layer3, layer3,
            P("section", None, None, None),
            layer3, layer2, layer3, layer2,
            P(), P(), P(), P(),
        ),
        out_specs=(
            P("dp", "section"), P("dp", "section"), P("dp", "section"),
            P("section", None, None, None), layer3, layer2, layer3, layer2,
        ),
        check_vma=False,
    )
```

```python
import functools

import jax
import jax.numpy as jnp
from jax import lax
from jax.experimental import pallas as pl
from jax.experimental.pallas import tpu as pltpu
from jax.sharding import PartitionSpec as P

HD = 64
PRE = 30
PRE_PAD = 32
SRC_LONG = 768
SRC_SHORT = 96
TGT = 256
LANES = 128

BF = jnp.bfloat16
F32 = jnp.float32
norm_eps = 1e-05
big_negative = -1e30
adapter_scale = 4.0
chunk = 512
wide = 1024
ENC_ROWS = (SRC_LONG + SRC_SHORT) // 3
vmem_bytes = 56 * 2**20

phi_poly = (
    0.797869713181688,
    0.036392283539041996,
    -8.782472977701046e-05,
    -3.669384069669515e-05,
    1.4250308145882202e-06,
)


def nn(left, right):
    return lax.dot_general(left, right, (((1,), (0,)), ((), ())), preferred_element_type=F32)


def nt(left, right):
    return lax.dot_general(left, right, (((1,), (1,)), ((), ())), preferred_element_type=F32)


def tn(left, right):
    return lax.dot_general(left, right, (((0,), (0,)), ((), ())), preferred_element_type=F32)


def gelu_pair(values):
    square = values * values
    poly = phi_poly[4]
    for coefficient in phi_poly[3::-1]:
        poly = poly * square + coefficient
    half = 0.5 * jnp.tanh(values * poly) + 0.5
    density = jnp.exp(square * -0.5) * 0.3989422804014327
    return values * half, half + values * density


def row_tiles(rows, most=288):
    count = -(-rows // most)
    size = rows // count
    return [(i * size, size) for i in range(count)]


def norm_rows(values):
    centered = values - jnp.mean(values, axis=-1, keepdims=True)
    scale = lax.rsqrt(jnp.mean(centered * centered, axis=-1, keepdims=True) + norm_eps)
    return centered * scale, scale


def norm_rows_back(hat, scale, grad_hat):
    mean_grad = jnp.mean(grad_hat, axis=-1, keepdims=True)
    mean_dot = jnp.mean(grad_hat * hat, axis=-1, keepdims=True)
    return scale * (grad_hat - mean_grad - hat * mean_dot)


def params(limit=vmem_bytes):
    return pltpu.CompilerParams(vmem_limit_bytes=limit)


def whole(shape):
    return pl.BlockSpec(shape, lambda *g: (0,) * len(shape))


def product_kernel(x_ref, w_ref, o_ref):
    o_ref[...] = nn(x_ref[...], w_ref[...]).astype(BF)


def product(x, w, tile=1024):
    rows, depth = x.shape
    width = w.shape[1]
    return pl.pallas_call(
        product_kernel,
        grid=(width // tile,),
        in_specs=[whole((rows, depth)), pl.BlockSpec((depth, tile), lambda i: (0, i))],
        out_specs=pl.BlockSpec((rows, tile), lambda i: (0, i)),
        out_shape=jax.ShapeDtypeStruct((rows, width), BF),
        compiler_params=params(),
        name="product",
    )(x, w)


def back_product_kernel(*refs, parts, residual, cuts):
    grads = refs[:parts]
    w_ref = refs[parts]
    outs = refs[-len(cuts) :]
    total = None
    width = grads[0].shape[1]
    for i, grad in enumerate(grads):
        term = nt(grad[...], w_ref[:, i * width : (i + 1) * width])
        total = term if total is None else total + term
    if residual:
        total = total + refs[parts + 1][...]
    for (start, size), o_ref in zip(cuts, outs):
        o_ref[...] = total[start : start + size].astype(BF)


def back_product(grads, w, residual=None, tile=512, cuts=None):
    rows, width = grads[0].shape
    depth = w.shape[0]
    parts = len(grads)
    cuts = cuts or ((0, rows),)
    specs = [whole((rows, width))] * parts + [
        pl.BlockSpec((tile, parts * width), lambda i: (i, 0))
    ]
    args = list(grads) + [w]
    if residual is not None:
        specs.append(pl.BlockSpec((rows, tile), lambda i: (0, i)))
        args.append(residual)
    return pl.pallas_call(
        functools.partial(
            back_product_kernel, parts=parts, residual=residual is not None, cuts=cuts
        ),
        grid=(depth // tile,),
        in_specs=specs,
        out_specs=[pl.BlockSpec((size, tile), lambda i: (0, i)) for _, size in cuts],
        out_shape=[jax.ShapeDtypeStruct((size, depth), BF) for _, size in cuts],
        compiler_params=params(),
        name="back_product",
    )(*args)


def head_lanes(head):
    lane = lax.broadcasted_iota(jnp.int32, (1, LANES), 1)
    own = (lane < HD) if head == 0 else (lane >= HD)
    first = HD if head == 0 else 0
    return own, lane == first, lane == first + 1


def bf(value):
    return jnp.asarray(value, BF)


def rows_of(refs, start, count):
    parts = []
    for ref in refs:
        size = ref.shape[0]
        low, high = max(start, 0), min(start + count, size)
        if low < high:
            parts.append(ref[low:high])
        start -= size
    return parts


def stacked(refs, prefix_ref, start, count):
    parts = rows_of(refs, start, count)
    if prefix_ref is not None:
        parts.append(prefix_ref[...])
    return parts[0] if len(parts) == 1 else jnp.concatenate(parts, 0)


def attend_kernel(*refs, segs, prefix, causal, pieces, which):
    len_ref, q_ref = refs[:2]
    k_refs, v_refs = refs[2 : 2 + pieces], refs[2 + pieces : 2 + 2 * pieces]
    at = 2 + 2 * pieces
    pk_ref = pv_ref = None
    if prefix:
        pk_ref, pv_ref = refs[at : at + 2]
        at += 2
    o_ref, inv_ref = refs[at : at + 2]
    p_refs = refs[at + 2 :]
    for seg, (q0, nq, k0, nk) in enumerate(segs):
        keys = stacked(k_refs, pk_ref, k0, nk)
        values = stacked(v_refs, pv_ref, k0, nk)
        count = keys.shape[0]
        row = lax.broadcasted_iota(jnp.int32, (count, 1), 0)
        seen = row < jnp.minimum(len_ref[0, which + seg], nk)
        if prefix:
            seen = seen | ((row >= nk) & (row < nk + PRE))
        queries = q_ref[q0 : q0 + nq] * bf(HD**-0.5)
        out = inv = None
        for head in range(2):
            own, first, _ = head_lanes(head)
            k_own = jnp.where(own, keys, jnp.where(first & ~seen, bf(big_negative), bf(0)))
            q_own = jnp.where(own, queries, jnp.where(first, bf(1), bf(0)))
            v_own = jnp.where(own, values, bf(1))
            scores = nt(k_own, q_own)
            if causal:
                key_at = lax.broadcasted_iota(jnp.int32, scores.shape, 0)
                query_at = lax.broadcasted_iota(jnp.int32, scores.shape, 1)
                allowed = (key_at <= query_at) | (key_at >= nk)
                scores = jnp.where(allowed, scores, big_negative)
            peak = jnp.max(scores, axis=0, keepdims=True)
            weights = jnp.exp(scores - peak).astype(BF)
            p_refs[seg][head] = weights
            mixed = tn(weights, v_own)
            inverse = 1.0 / pltpu.roll(mixed, HD, 1)
            mixed = mixed * inverse
            out = mixed if out is None else jnp.where(own, mixed, out)
            inv = inverse if inv is None else jnp.where(own, inverse, inv)
        o_ref[q0 : q0 + nq] = out.astype(BF)
        inv_ref[q0 : q0 + nq] = inv


def column_spec(rows, offset, row_block=0):
    return pl.BlockSpec((rows, LANES), lambda h: (row_block, h + offset))


def attend(lengths, q, keys, values, prefixes, segs, causal, which=0):
    pairs = 8
    q_rows = q[1]
    prefix = prefixes is not None
    extra = PRE_PAD if prefix else 0
    specs = [pl.BlockSpec(memory_space=pltpu.SMEM)]
    args = [lengths]
    for array, rows, block, offset in [q, *keys, *values]:
        specs.append(column_spec(rows, offset, block))
        args.append(array)
    if prefix:
        specs += [column_spec(PRE_PAD, 0)] * 2
        args += list(prefixes)
    weight_shapes = [(2 * pairs, nk + extra, nq) for _, nq, _, nk in segs]
    return pl.pallas_call(
        functools.partial(
            attend_kernel, segs=segs, prefix=prefix, causal=causal, pieces=len(keys), which=which
        ),
        grid=(pairs,),
        in_specs=specs,
        out_specs=[column_spec(q_rows, 0), column_spec(q_rows, 0)]
        + [pl.BlockSpec((2,) + s[1:], lambda h: (h, 0, 0)) for s in weight_shapes],
        out_shape=[
            jax.ShapeDtypeStruct((q_rows, pairs * LANES), BF),
            jax.ShapeDtypeStruct((q_rows, pairs * LANES), F32),
        ]
        + [jax.ShapeDtypeStruct(s, BF) for s in weight_shapes],
        compiler_params=params(),
        name="attend",
    )(*args)


def attend_back_pair(
    q_ref, k_refs, v_refs, o_ref, inv_ref, g_refs, pk_ref, pv_ref, p_refs, dq_ref, dk_ref, dv_ref, segs
):
    prefix_totals = [None, None]
    scale = HD**-0.5
    for seg, (q0, nq, k0, nk) in enumerate(segs):
        keys = stacked(k_refs, pk_ref, k0, nk)
        values = stacked(v_refs, pv_ref, k0, nk)
        queries = q_ref[q0 : q0 + nq]
        grads = stacked(g_refs, None, q0, nq).astype(F32) * inv_ref[q0 : q0 + nq]
        grads_low = grads.astype(BF)
        dots = grads * o_ref[q0 : q0 + nq].astype(F32)
        dq = dk = dv = None
        for head in range(2):
            own, first, second = head_lanes(head)
            row_dot = -jnp.sum(jnp.where(own, dots, 0.0), axis=1, keepdims=True)
            high = row_dot.astype(BF)
            rest = (row_dot - high.astype(F32)).astype(BF)
            g_own = jnp.where(
                own, grads_low, jnp.where(first, high, jnp.where(second, rest, bf(0)))
            )
            v_own = jnp.where(own, values, jnp.where(first | second, bf(1), bf(0)))
            weights = p_refs[seg][head]
            score_grad = (weights.astype(F32) * nt(v_own, g_own)).astype(BF)
            dv_head = nn(weights, grads_low)
            dk_head = nn(score_grad, queries)
            dq_head = tn(score_grad, keys)
            dq = dq_head if dq is None else jnp.where(own, dq_head, dq)
            dk = dk_head if dk is None else jnp.where(own, dk_head, dk)
            dv = dv_head if dv is None else jnp.where(own, dv_head, dv)
        dk = dk * scale
        dq_ref[q0 : q0 + nq] = (dq * scale).astype(BF)
        at = k0 - segs[0][2]
        dk_ref[at : at + nk] = dk[:nk].astype(BF)
        dv_ref[at : at + nk] = dv[:nk].astype(BF)
        if pk_ref is not None:
            for i, grad in enumerate((dk, dv)):
                part = grad[nk:]
                prefix_totals[i] = part if seg == 0 else prefix_totals[i] + part
    return prefix_totals


def attend_back_kernel(*refs, segs, prefix, pieces):
    q_ref, o_ref, inv_ref, g_ref = refs[:4]
    k_refs, v_refs = refs[4 : 4 + pieces], refs[4 + pieces : 4 + 2 * pieces]
    at = 4 + 2 * pieces
    pk_ref = pv_ref = None
    if prefix:
        pk_ref, pv_ref = refs[at : at + 2]
        at += 2
    outs = refs[at + len(segs) :]
    totals = attend_back_pair(
        q_ref, k_refs, v_refs, o_ref, inv_ref, [g_ref], pk_ref, pv_ref,
        refs[at : at + len(segs)], *outs[:3], segs,
    )
    if prefix:
        outs[3][...] = totals[0]
        outs[4][...] = totals[1]


def attend_back(q, keys, values, prefixes, attended, inverse, grad, weights, segs):
    pairs = 8
    q_rows = q[1]
    k_rows = sum(nk for _, _, _, nk in segs)
    prefix = prefixes is not None
    specs, args = [], []
    own = [(a, q_rows, 0, 0) for a in (attended, inverse, grad)]
    for array, rows, block, offset in [q, *own, *keys, *values]:
        specs.append(column_spec(rows, offset, block))
        args.append(array)
    if prefix:
        specs += [column_spec(PRE_PAD, 0)] * 2
        args += list(prefixes)
    specs += [pl.BlockSpec((2,) + w.shape[1:], lambda h: (h, 0, 0)) for w in weights]
    args += list(weights)
    out_specs = [column_spec(q_rows, 0), column_spec(k_rows, 0), column_spec(k_rows, 0)]
    out_shape = [
        jax.ShapeDtypeStruct((q_rows, pairs * LANES), BF),
        jax.ShapeDtypeStruct((k_rows, pairs * LANES), BF),
        jax.ShapeDtypeStruct((k_rows, pairs * LANES), BF),
    ]
    if prefix:
        out_specs += [column_spec(PRE_PAD, 0)] * 2
        out_shape += [jax.ShapeDtypeStruct((PRE_PAD, pairs * LANES), F32)] * 2
    return pl.pallas_call(
        functools.partial(
            attend_back_kernel, segs=segs, prefix=prefix, pieces=len(keys)
        ),
        grid=(pairs,),
        in_specs=specs,
        out_specs=out_specs,
        out_shape=out_shape,
        compiler_params=params(),
        name="attend_back",
    )(*args)


def ffn_step(low_ref, acc_ref, in_ref, out_ref, slope_ref, act_ref, bias_ref, scale):
    for start, size in row_tiles(low_ref.shape[0]):
        rows = slice(start, start + size)
        hidden = nn(low_ref[rows], in_ref[...])
        if bias_ref is not None:
            hidden = hidden + bias_ref[...]
        active, slope = gelu_pair(hidden)
        slope_ref[rows] = slope.astype(BF)
        active = active.astype(BF)
        if act_ref is not None:
            act_ref[rows] = active
        term = nn(active, out_ref[...])
        acc_ref[rows] += term if scale is None else scale * term


def enc_ffn_kernel(
    x_ref, att_ref, wo_ref, gain_ref, in_ref, out_ref, down_ref, downb_ref, up_ref, upb_ref,
    mem_ref, slope_ref, pre_slope_ref, act_ref, low_ref, scales_ref, acc_ref,
):
    step = pl.program_id(0)
    last = pl.num_programs(0) - 1

    @pl.when(step == 0)
    def _():
        first = x_ref[...].astype(F32) + nn(att_ref[...], wo_ref[...])
        hat, scale = norm_rows(first)
        normed = hat * gain_ref[0:1]
        acc_ref[...] = normed
        low_ref[...] = normed.astype(BF)
        scales_ref[:, 0:1] = scale

    @pl.when((step > 0) & (step < last))
    def _():
        ffn_step(low_ref, acc_ref, in_ref, out_ref, slope_ref, None, None, None)

    @pl.when(step == last)
    def _():
        ffn_step(
            low_ref, acc_ref, down_ref, up_ref, pre_slope_ref, act_ref, downb_ref, adapter_scale
        )
        hat, scale = norm_rows(acc_ref[...] + adapter_scale * upb_ref[...])
        mem_ref[...] = (hat * gain_ref[1:2]).astype(BF)
        scales_ref[:, 1:2] = scale


def enc_ffn(x, att, w, part):
    width = x.shape[1]
    rows = ENC_ROWS
    hidden = w["ffn_in"].shape[1]
    steps = hidden // wide

    def at(i):
        return jnp.clip(i - 1, 0, steps - 1)

    return pl.pallas_call(
        enc_ffn_kernel,
        grid=(steps + 2,),
        in_specs=[
            pl.BlockSpec((rows, width), lambda i: (part, 0)),
            pl.BlockSpec((rows, width), lambda i: (part, 0)),
            whole((width, width)),
            whole((2, width)),
            pl.BlockSpec((width, wide), lambda i: (0, at(i))),
            pl.BlockSpec((wide, width), lambda i: (at(i), 0)),
            whole((width, chunk)),
            whole((1, chunk)),
            whole((chunk, width)),
            whole((1, width)),
        ],
        out_specs=[
            whole((rows, width)),
            pl.BlockSpec((rows, wide), lambda i: (0, at(i))),
            whole((rows, chunk)),
            whole((rows, chunk)),
            whole((rows, width)),
            whole((rows, LANES)),
        ],
        out_shape=[
            jax.ShapeDtypeStruct((rows, width), BF),
            jax.ShapeDtypeStruct((rows, hidden), BF),
            jax.ShapeDtypeStruct((rows, chunk), BF),
            jax.ShapeDtypeStruct((rows, chunk), BF),
            jax.ShapeDtypeStruct((rows, width), BF),
            jax.ShapeDtypeStruct((rows, LANES), F32),
        ],
        scratch_shapes=[pltpu.VMEM((rows, width), F32)],
        compiler_params=params(),
        name="enc_ffn",
    )(
        x, att, w["out"], w["gains"], w["ffn_in"], w["ffn_out"],
        w["down"], w["down_bias"], w["up"], w["up_bias"],
    )


def ffn_back_step(grad_ref, acc_ref, in_ref, out_ref, slope_ref):
    for start, size in row_tiles(grad_ref.shape[0]):
        rows = slice(start, start + size)
        pre = (nt(grad_ref[rows], out_ref[...]) * slope_ref[rows].astype(F32)).astype(BF)
        acc_ref[rows] += nt(pre, in_ref[...])


def adapter_back(grad_ref, acc_ref, low_ref, act_ref, slope_ref, down_ref, up_ref, outs, pre_ref):
    ddown_ref, ddownb_ref, dup_ref, dupb_ref = outs
    total = None
    for start, size in row_tiles(grad_ref.shape[0]):
        rows = slice(start, start + size)
        back = adapter_scale * nt(grad_ref[rows], up_ref[...])
        pre = (back * slope_ref[rows].astype(F32)).astype(BF)
        pre_ref[rows] = pre
        sums = jnp.sum(pre.astype(F32), axis=0, keepdims=True)
        total = sums if total is None else total + sums
        acc_ref[rows] += nt(pre, down_ref[...])
    ddownb_ref[...] = total
    ddown_ref[...] = tn(low_ref[...], pre_ref[...])
    dup_ref[...] = adapter_scale * tn(act_ref[...], grad_ref[...])
    dupb_ref[...] = adapter_scale * jnp.sum(grad_ref[...].astype(F32), axis=0, keepdims=True)


def enc_ffn_back_kernel(
    dmem_ref, mem_ref, low_ref, scales_ref, gain_ref, slope_ref, pre_slope_ref,
    in_ref, out_ref, down_ref, up_ref, wo_ref,
    dfirst_ref, datt_ref, grad_ref, pre_ref,
    acc_ref,
):
    step = pl.program_id(0)
    last = pl.num_programs(0) - 1

    @pl.when(step == 0)
    def _():
        gain = gain_ref[1:2]
        hat = mem_ref[...].astype(F32) / gain
        grad = norm_rows_back(hat, scales_ref[:, 1:2], dmem_ref[...].astype(F32) * gain)
        low = grad.astype(BF)
        grad_ref[...] = low
        back = adapter_scale * nt(low, up_ref[...])
        pre = (back * pre_slope_ref[...].astype(F32)).astype(BF)
        pre_ref[...] = pre
        acc_ref[...] = grad + nt(pre, down_ref[...])

    ffn_back_step(grad_ref, acc_ref, in_ref, out_ref, slope_ref)

    @pl.when(step == last)
    def _():
        gain = gain_ref[0:1]
        hat = low_ref[...].astype(F32) / gain
        grad = norm_rows_back(hat, scales_ref[:, 0:1], acc_ref[...] * gain)
        dfirst_ref[...] = grad
        datt_ref[...] = nt(grad.astype(BF), wo_ref[...]).astype(BF)


def enc_ffn_back(dmem, saved, w):
    mem, slope, pre_slope, act, low, scales = saved
    rows, width = dmem.shape
    hidden = w["ffn_in"].shape[1]
    steps = hidden // wide
    return pl.pallas_call(
        enc_ffn_back_kernel,
        grid=(steps,),
        in_specs=[
            whole((rows, width)),
            whole((rows, width)),
            whole((rows, width)),
            whole((rows, LANES)),
            whole((2, width)),
            pl.BlockSpec((rows, wide), lambda i: (0, i)),
            whole((rows, chunk)),
            pl.BlockSpec((width, wide), lambda i: (0, i)),
            pl.BlockSpec((wide, width), lambda i: (i, 0)),
            whole((width, chunk)),
            whole((chunk, width)),
            whole((width, width)),
        ],
        out_specs=[
            whole((rows, width)),
            whole((rows, width)),
            whole((rows, width)),
            whole((rows, chunk)),
        ],
        out_shape=[
            jax.ShapeDtypeStruct((rows, width), F32),
            jax.ShapeDtypeStruct((rows, width), BF),
            jax.ShapeDtypeStruct((rows, width), BF),
            jax.ShapeDtypeStruct((rows, chunk), BF),
        ],
        scratch_shapes=[pltpu.VMEM((rows, width), F32)],
        compiler_params=params(),
        name="enc_ffn_back",
    )(
        dmem, mem, low, scales, w["gains"], slope, pre_slope,
        w["ffn_in"], w["ffn_out"], w["down"], w["up"], w["out"],
    )


def adapter_grads_kernel(*refs, parts):
    groups = [refs[n * parts : (n + 1) * parts] for n in range(4)]
    low, act, grad, pre = [jnp.concatenate([r[...] for r in g], 0) for g in groups]
    ddown_ref, ddownb_ref, dup_ref, dupb_ref = refs[4 * parts :]
    ddown_ref[...] = tn(low, pre)
    ddownb_ref[...] = jnp.sum(pre.astype(F32), axis=0, keepdims=True)
    dup_ref[...] = adapter_scale * tn(act, grad)
    dupb_ref[...] = adapter_scale * jnp.sum(grad.astype(F32), axis=0, keepdims=True)


def adapter_grads(lows, acts, grads, pres):
    width = lows[0].shape[1]
    return pl.pallas_call(
        functools.partial(adapter_grads_kernel, parts=len(lows)),
        out_shape=[
            jax.ShapeDtypeStruct((width, chunk), F32),
            jax.ShapeDtypeStruct((1, chunk), F32),
            jax.ShapeDtypeStruct((chunk, width), F32),
            jax.ShapeDtypeStruct((1, width), F32),
        ],
        compiler_params=params(),
        name="adapter_grads",
    )(*lows, *acts, *grads, *pres)


def dec_mid_kernel(x_ref, att_ref, wo_ref, gain_ref, wq_ref, n_ref, scale_ref, cq_ref):
    for start, size in row_tiles(x_ref.shape[0], 256):
        rows = slice(start, start + size)
        first = x_ref[rows].astype(F32) + nn(att_ref[rows], wo_ref[...])
        hat, scale = norm_rows(first)
        normed = hat * gain_ref[0:1]
        n_ref[rows] = normed
        scale_ref[rows, 0:1] = scale
        cq_ref[rows] = nn(normed.astype(BF), wq_ref[...]).astype(BF)


def dec_mid(x, att, w, cross):
    rows, width = x.shape
    return pl.pallas_call(
        dec_mid_kernel,
        out_shape=[
            jax.ShapeDtypeStruct((rows, width), F32),
            jax.ShapeDtypeStruct((rows, LANES), F32),
            jax.ShapeDtypeStruct((rows, width), BF),
        ],
        compiler_params=params(),
        name="dec_mid",
    )(x, att, w["out"], w["gains"], cross["query"])


def dec_ffn_kernel(
    len_ref, n_ref, catt_ref, cot_ref, wco_ref, cgain_ref, gain_ref,
    in_ref, out_ref, down_ref, downb_ref, up_ref, upb_ref,
    y_ref, dsecond_ref, dcatt_ref, ddown_ref, ddownb_ref, dup_ref, dupb_ref,
    acc_ref, low_ref, grad_ref, slope_ref, pre_slope_ref, act_ref, pre_ref, scale_ref,
    *, steps, which,
):
    step = pl.program_id(0)
    tiles = row_tiles(n_ref.shape[0], TGT)

    @pl.when(step == 0)
    def _():
        for start, size in tiles:
            rows = slice(start, start + size)
            second = n_ref[rows] + nn(catt_ref[rows], wco_ref[...])
            hat, scale = norm_rows(second)
            middle = hat * cgain_ref[...]
            acc_ref[rows] = middle
            low_ref[rows] = middle.astype(BF)
            scale_ref[rows, 0:1] = scale

    @pl.when((step > 0) & (step <= steps))
    def _():
        ffn_step(low_ref, acc_ref, in_ref, out_ref, slope_ref.at[step - 1], None, None, None)

    @pl.when(step == steps + 1)
    def _():
        ffn_step(
            low_ref, acc_ref, down_ref, up_ref, pre_slope_ref, act_ref, downb_ref,
            adapter_scale,
        )
        for start, size in tiles:
            rows = slice(start, start + size)
            gain = gain_ref[1:2]
            hat, scale = norm_rows(acc_ref[rows] + adapter_scale * upb_ref[...])
            valid = lax.broadcasted_iota(jnp.int32, (size, 1), 0) < len_ref[0, which]
            y_ref[rows] = jnp.where(valid, hat * gain, 0.0).astype(BF)
            cot = jnp.where(valid, cot_ref[rows].astype(F32), 0.0)
            grad = norm_rows_back(hat, scale, cot * gain)
            acc_ref[rows] = grad
            grad_ref[rows] = grad.astype(BF)
        adapter_back(
            grad_ref, acc_ref, low_ref, act_ref, pre_slope_ref, down_ref, up_ref,
            (ddown_ref, ddownb_ref, dup_ref, dupb_ref), pre_ref,
        )

    @pl.when(step > steps + 1)
    def _():
        ffn_back_step(grad_ref, acc_ref, in_ref, out_ref, slope_ref.at[2 * steps + 1 - step])

    @pl.when(step == 2 * steps + 1)
    def _():
        for start, size in tiles:
            rows = slice(start, start + size)
            gain = cgain_ref[...]
            hat = low_ref[rows].astype(F32) / gain
            grad = norm_rows_back(hat, scale_ref[rows, 0:1], acc_ref[rows] * gain)
            dsecond_ref[rows] = grad
            dcatt_ref[rows] = nt(grad.astype(BF), wco_ref[...]).astype(BF)


def dec_ffn(lengths, n, catt, cot, w, cross, which):
    rows, width = catt.shape
    hidden = w["ffn_in"].shape[1]
    steps = hidden // wide

    def at(i):
        return jnp.where(i <= steps, jnp.clip(i - 1, 0, steps - 1), jnp.clip(2 * steps + 1 - i, 0, steps - 1))

    return pl.pallas_call(
        functools.partial(dec_ffn_kernel, steps=steps, which=which),
        grid=(2 * steps + 2,),
        in_specs=[
            pl.BlockSpec(memory_space=pltpu.SMEM),
            pl.BlockSpec((rows, width), lambda i: (which, 0)),
            whole((rows, width)),
            pl.BlockSpec((rows, width), lambda i: (which, 0)),
            whole((width, width)),
            whole((1, width)),
            whole((2, width)),
            pl.BlockSpec((width, wide), lambda i: (0, at(i))),
            pl.BlockSpec((wide, width), lambda i: (at(i), 0)),
            whole((width, chunk)),
            whole((1, chunk)),
            whole((chunk, width)),
            whole((1, width)),
        ],
        out_specs=[
            whole((rows, width)),
            whole((rows, width)),
            whole((rows, width)),
            whole((width, chunk)),
            whole((1, chunk)),
            whole((chunk, width)),
            whole((1, width)),
        ],
        out_shape=[
            jax.ShapeDtypeStruct((rows, width), BF),
            jax.ShapeDtypeStruct((rows, width), F32),
            jax.ShapeDtypeStruct((rows, width), BF),
            jax.ShapeDtypeStruct((width, chunk), F32),
            jax.ShapeDtypeStruct((1, chunk), F32),
            jax.ShapeDtypeStruct((chunk, width), F32),
            jax.ShapeDtypeStruct((1, width), F32),
        ],
        scratch_shapes=[
            pltpu.VMEM((rows, width), F32),
            pltpu.VMEM((rows, width), BF),
            pltpu.VMEM((rows, width), BF),
            pltpu.VMEM((steps, rows, wide), BF),
            pltpu.VMEM((rows, chunk), BF),
            pltpu.VMEM((rows, chunk), BF),
            pltpu.VMEM((rows, chunk), BF),
            pltpu.VMEM((rows, LANES), F32),
        ],
        compiler_params=params(),
        name="dec_ffn",
    )(
        lengths, n, catt, cot, cross["out"], cross["gain"], w["gains"],
        w["ffn_in"], w["ffn_out"], w["down"], w["down_bias"], w["up"], w["up_bias"],
    )


def dec_mid_back_kernel(
    dsecond_ref, dcq_ref, wq_ref, n_ref, scale_ref, gain_ref, wo_ref, dfirst_ref, datt_ref
):
    for start, size in row_tiles(n_ref.shape[0], 256):
        rows = slice(start, start + size)
        gain = gain_ref[0:1]
        total = dsecond_ref[rows] + nt(dcq_ref[rows], wq_ref[...])
        grad = norm_rows_back(n_ref[rows] / gain, scale_ref[rows, 0:1], total * gain)
        dfirst_ref[rows] = grad
        datt_ref[rows] = nt(grad.astype(BF), wo_ref[...]).astype(BF)


def dec_mid_back(dsecond, dcq, n, scale, w, cross):
    rows, width = n.shape
    return pl.pallas_call(
        dec_mid_back_kernel,
        out_shape=[
            jax.ShapeDtypeStruct((rows, width), F32),
            jax.ShapeDtypeStruct((rows, width), BF),
        ],
        compiler_params=params(),
        name="dec_mid_back",
    )(dsecond, dcq, cross["query"], n, scale, w["gains"], w["out"])


enc_segs = ((0, SRC_LONG, 0, SRC_LONG), (SRC_LONG, SRC_SHORT, SRC_LONG, SRC_SHORT))
dec_segs = ((0, TGT, 0, TGT), (TGT, TGT, TGT, TGT))
cross_segs = (((0, TGT, 0, SRC_LONG),), ((0, TGT, SRC_LONG % ENC_ROWS, SRC_SHORT),))


def self_columns(qkv):
    rows = qkv.shape[0]
    return (qkv, rows, 0, 0), [(qkv, rows, 0, 8)], [(qkv, rows, 0, 16)]


def cross_columns(cq, kvs, which):
    return (
        (cq, TGT, which, 0),
        [(kv, ENC_ROWS, 0, 0) for kv in kvs],
        [(kv, ENC_ROWS, 0, 8) for kv in kvs],
    )


def decoder_self(t, lengths, w, cross):
    qkv = product(t, w["qkv"])
    att, inv, *weights = attend(lengths, *self_columns(qkv), w["prefix"], dec_segs, True)
    n, scale, cq = dec_mid(t, att, w, cross)
    return cq, (qkv, att, inv, weights, n, scale)


def cross_forward(lengths, cq, kvs, which):
    return attend(
        lengths, *cross_columns(cq, kvs, which), None, cross_segs[which], False, which
    )


def cross_backward(cq, kvs, forward, dcatt, which):
    catt, inv, *weights = forward
    return attend_back(
        *cross_columns(cq, kvs, which), None, catt, inv, dcatt, weights, cross_segs[which]
    )


def decoder_self_back(kept, dsecond, dcq, w, cross):
    qkv, att, inv, weights, n, scale = kept
    dfirst, datt = dec_mid_back(dsecond, dcq, n, scale, w, cross)
    dq, dk, dv, *dprefix = attend_back(
        *self_columns(qkv), w["prefix"], att, inv, datt, weights, dec_segs
    )
    return back_product([dq, dk, dv], w["qkv"], dfirst)[0], dprefix


def small_shape(devices):
    return 8, 8 * (2 * chunk) // devices


def finish_kernel(
    q_ref, k_ref, v_ref, o_ref, inv_ref, g0_ref, g1_ref, g2_ref, pk_ref, pv_ref, pl_ref, ps_ref,
    dfirst0_ref, dfirst1_ref, dfirst2_ref, wqkv_ref, up_ref, down_ref, upb_ref, downb_ref, dpk_ref, dpv_ref,
    lows,
    source_ref, low_ref, o_up_ref, o_down_ref, o_small_ref,
    dq, dk, dv, small, mine, theirs, half_sum, landed, total, result,
    small_landed, small_total, small_result, dx_low, dx_high, dx_landed, lows_landed,
    pair_sems, spread_sems, gather_sems, back_sems, small_sems, share_sems, cross_sems,
    *, devices,
):
    step = pl.program_id(0)
    pairs = 8
    is_encoder = lax.axis_index("section") == 0
    section = lax.axis_index("section")
    chips = devices // 2
    rows = 2 * chunk
    half, part = rows // 2, rows // devices
    place = lax.axis_index("dp")
    core, chip = lax.rem(place, 2), place // 2
    partner = place + 1 - 2 * core
    small_rows, small_cols = small_shape(devices)
    tile = 256
    width = 2 * chunk
    scale = 1.0 / devices

    def peer(distance):
        return lax.rem(chip + distance, chips) * 2 + core

    def remote(source, target, send_sem, recv_sem, other):
        return pltpu.make_async_remote_copy(
            src_ref=source, dst_ref=target, send_sem=send_sem, recv_sem=recv_sem,
            device_id=other, device_id_type=pl.DeviceIdType.MESH,
        )

    def in_group(other):
        return {"dp": other}

    across = {"section": 1 - section}
    kept = pl.multiple_of(core * half, 16)
    given = pl.multiple_of((1 - core) * half, 16)
    here = pl.multiple_of(kept + chip * part, 16)

    def swap():
        return remote(
            mine.at[pl.ds(given, half)], theirs, pair_sems.at[0], pair_sems.at[1],
            in_group(partner),
        )

    def spread(s):
        at = pl.multiple_of(lax.rem(chip + s, chips) * part, 16)
        return remote(
            half_sum.at[pl.ds(at, part)], landed.at[s - 1],
            spread_sems.at[0, s - 1], spread_sems.at[1, s - 1], in_group(peer(s)),
        )

    def gather(s):
        return remote(
            total, result.at[pl.ds(here, part)],
            gather_sems.at[0, s - 1], gather_sems.at[1, s - 1], in_group(peer(s)),
        )

    def back(s):
        source = lax.rem(chip + chips - s, chips)
        there = pl.ds(pl.multiple_of(kept + source * part, 16), part)
        return remote(
            total if s == 0 else result.at[there], result.at[there],
            back_sems.at[0, s], back_sems.at[1, s], in_group(partner),
        )

    def piece(index):
        row = pl.multiple_of(lax.rem(index, 8) * small_rows, 8)
        col = pl.multiple_of((index // 8) * small_cols, LANES)
        return pl.ds(row, small_rows), pl.ds(col, small_cols)

    def small_out(s):
        return remote(
            small.at[piece(lax.rem(place + s, devices))], small_landed.at[s - 1],
            small_sems.at[0, s - 1], small_sems.at[1, s - 1],
            in_group(lax.rem(place + s, devices)),
        )

    def small_share(s):
        return remote(
            small_total, small_result.at[piece(place)],
            share_sems.at[0, s - 1], share_sems.at[1, s - 1],
            in_group(lax.rem(place + s, devices)),
        )

    def send_low():
        return remote(lows, lows_landed, cross_sems.at[0, 0], cross_sems.at[1, 0], across)

    def send_high(i):
        return remote(
            dx_high.at[i], dx_landed.at[i], cross_sems.at[0, 1 + i], cross_sems.at[1, 1 + i], across
        )

    @pl.when(step == 0)
    def _():
        barrier = pltpu.get_barrier_semaphore()
        others = [in_group(lax.rem(place + s, devices)) for s in range(1, devices)] + [across]
        for other in others:
            pl.semaphore_signal(
                barrier, inc=1, device_id=other, device_id_type=pl.DeviceIdType.MESH
            )
        mine[0:chunk] = (up_ref[...] * scale).astype(BF)
        mine[chunk:width, 0:chunk] = (down_ref[0:chunk] * scale).astype(BF)
        mine[chunk:width, chunk:width] = (down_ref[chunk:width] * scale).astype(BF)
        pl.semaphore_wait(barrier, devices)
        swap().start()

        @pl.when(jnp.logical_not(is_encoder))
        def _():
            send_low().start()
            small[0:PRE_PAD] = dpk_ref[...] * scale
            small[PRE_PAD : 2 * PRE_PAD] = dpv_ref[...] * scale

    @pl.when(is_encoder & (step < pairs))
    def _():
        at = pl.multiple_of(step * LANES, LANES)
        lanes = pl.ds(at, LANES)
        prefix_totals = attend_back_pair(
            q_ref, [k_ref], [v_ref], o_ref, inv_ref, [g0_ref, g1_ref, g2_ref], pk_ref, pv_ref,
            (pl_ref, ps_ref),
            dq.at[:, lanes], dk.at[:, lanes], dv.at[:, lanes], enc_segs,
        )
        small[0:PRE_PAD, lanes] = prefix_totals[0] * scale
        small[PRE_PAD : 2 * PRE_PAD, lanes] = prefix_totals[1] * scale

    @pl.when(step == 1)
    def _():
        swap().wait()
        half_sum[...] = (
            mine[pl.ds(kept, half)].astype(F32) + theirs[...].astype(F32)
        ).astype(BF)
        for s in range(1, chips):
            spread(s).start()

    @pl.when(step == pairs - 1)
    def _():
        down_row = jnp.concatenate([downb_ref[...], jnp.zeros_like(downb_ref)], 1)
        small[PRE : PRE + 1] = upb_ref[...] * scale
        small[PRE + 1 : PRE + 2] = down_row * scale
        for s in range(1, devices):
            small_out(s).start()
        summed = half_sum[pl.ds(pl.multiple_of(chip * part, 16), part)].astype(F32)
        for s in range(1, chips):
            spread(s).wait()
            summed = summed + landed[s - 1].astype(F32)
        total[...] = summed.astype(BF)
        result[pl.ds(here, part)] = total[...]
        for s in range(1, chips):
            gather(s).start()
        back(0).start()

    for i in range(4):

        @pl.when(is_encoder & (step == pairs + i))
        def _(i=i):
            acc = jnp.concatenate([dfirst0_ref[...], dfirst1_ref[...], dfirst2_ref[...]], 0)
            for n, grad in enumerate((dq, dk, dv)):
                acc = acc + nt(grad[...], wqkv_ref[:, n * width : (n + 1) * width])
            if i < 2:
                dx_high[i] = acc.astype(BF)
                send_high(i).start()
            else:
                dx_low[:, (i - 2) * tile : (i - 1) * tile] = acc.astype(BF)

    @pl.when(step == pairs + 1)
    def _():
        own_rows, own_cols = piece(place)
        summed = small[own_rows, own_cols]
        for s in range(1, devices):
            small_out(s).wait()
            summed = summed + small_landed[s - 1]
        small_total[...] = summed
        small_result[own_rows, own_cols] = summed
        for s in range(1, devices):
            small_share(s).start()

    @pl.when(step == pairs + 3)
    def _():
        for s in range(1, chips):
            gather(s).wait()
            back(s).start()
        for s in range(1, devices):
            small_share(s).wait()
        for s in range(chips):
            back(s).wait()
        o_small_ref[...] = small_result[...]
        o_up_ref[...] = result[0:chunk].astype(F32)
        o_down_ref[0:chunk] = result[chunk:width, 0:chunk].astype(F32)
        o_down_ref[chunk:width] = result[chunk:width, chunk:width].astype(F32)

        @pl.when(is_encoder)
        def _():
            send_low().wait_recv()
            low_ref[...] = lows_landed[...]
            source_ref[...] = dx_low[...]
            for i in range(2):
                send_high(i).wait_send()

        @pl.when(jnp.logical_not(is_encoder))
        def _():
            send_low().wait_send()
            for i in range(2):
                send_high(i).wait_recv()
                source_ref[:, i * tile : (i + 1) * tile] = dx_landed[i]


def finish(saved, datts, dfirsts, w, adapter, dec_prefix, lows):
    qkv, att, inv, weights = saved
    ddown, ddownb, dup, dupb = adapter
    devices = lax.axis_size("dp")
    chips = devices // 2
    rows, width = att.shape
    targets = lows.shape[1]
    pairs, tile = 8, 256
    half = width // 2
    part = width // devices
    small_rows, small_cols = small_shape(devices)

    def pair(offset):
        return pl.BlockSpec((rows, LANES), lambda i: (0, jnp.minimum(i, pairs - 1) + offset))

    def at(i):
        return jnp.where(i < pairs + 2, 2 + jnp.maximum(i - pairs, 0), i - pairs - 2)

    def once(shape):
        return pl.BlockSpec(shape, lambda i: (0,) * len(shape), pipeline_mode=pl.Buffered(1))

    prefix_pair = pl.BlockSpec((PRE_PAD, LANES), lambda i: (0, jnp.minimum(i, pairs - 1)))
    vmem = pltpu.VMEM
    dma = pltpu.SemaphoreType.DMA
    return pl.pallas_call(
        functools.partial(finish_kernel, devices=devices),
        grid=(pairs + 4,),
        in_specs=[pair(0), pair(8), pair(16), pair(0), pair(0)]
        + [pl.BlockSpec((ENC_ROWS, LANES), lambda i: (0, jnp.minimum(i, pairs - 1)))] * 3
        + [prefix_pair] * 2
        + [
            pl.BlockSpec((2,) + p.shape[1:], lambda i: (jnp.minimum(i, pairs - 1), 0, 0))
            for p in weights
        ]
        + [
            pl.BlockSpec((ENC_ROWS, tile), lambda i: (0, at(i))),
        ]
        * 3
        + [
            pl.BlockSpec((tile, 3 * width), lambda i: (at(i), 0)),
        ]
        + [once(a.shape) for a in (dup, ddown, dupb, ddownb, *dec_prefix)]
        + [pl.BlockSpec(memory_space=pl.ANY)],
        out_specs=[
            once((rows, half)), once((2, targets, half)), once(dup.shape), once(ddown.shape),
            once((2 * PRE_PAD, width)),
        ],
        out_shape=[
            jax.ShapeDtypeStruct((rows, half), BF),
            jax.ShapeDtypeStruct((2, targets, half), BF),
            jax.ShapeDtypeStruct(dup.shape, F32),
            jax.ShapeDtypeStruct(ddown.shape, F32),
            jax.ShapeDtypeStruct((2 * PRE_PAD, width), F32),
        ],
        scratch_shapes=[
            vmem((rows, width), BF), vmem((rows, width), BF), vmem((rows, width), BF),
            vmem((2 * PRE_PAD, width), F32),
            vmem((width, width), BF), vmem((half, width), BF), vmem((half, width), BF),
            vmem((chips - 1, part, width), BF), vmem((part, width), BF), vmem((width, width), BF),
            vmem((devices - 1, small_rows, small_cols), F32), vmem((small_rows, small_cols), F32),
            vmem((2 * PRE_PAD, width), F32),
            vmem((rows, half), BF), vmem((2, rows, tile), BF), vmem((2, rows, tile), BF),
            vmem((2, targets, half), BF),
            dma((2,)), dma((2, chips - 1)), dma((2, chips - 1)), dma((2, chips)),
            dma((2, devices - 1)), dma((2, devices - 1)), dma((2, 3)),
        ],
        compiler_params=pltpu.CompilerParams(
            vmem_limit_bytes=vmem_bytes, collective_id=0, has_side_effects=True
        ),
        name="finish",
    )(
        qkv, qkv, qkv, att, inv, *datts, *w["prefix"], *weights,
        *dfirsts, w["qkv"], dup, ddown, dupb, ddownb, *dec_prefix, lows,
    )


def blank_kernel(*refs):
    pass


def blanks(shapes):
    return pl.pallas_call(
        blank_kernel,
        out_shape=list(shapes),
        out_specs=[pl.BlockSpec(memory_space=pl.ANY)] * len(shapes),
        name="blank",
    )()


def on_section(is_encoder, encoder_work, decoder_work, *operands):
    enc_shapes, _ = jax.eval_shape(encoder_work, *operands)
    dec_shapes, _ = jax.eval_shape(decoder_work, *operands)

    def blank_like(shapes):
        leaves, tree = jax.tree.flatten(shapes)
        if not leaves:
            return shapes
        return jax.tree.unflatten(tree, blanks(leaves))

    def encoder_branch(*a):
        own, shared = encoder_work(*a)
        return own, blank_like(dec_shapes), shared

    def decoder_branch(*a):
        own, shared = decoder_work(*a)
        return blank_like(enc_shapes), own, shared

    return lax.cond(is_encoder, encoder_branch, decoder_branch, *operands)


def to_decoder(block):
    return lax.ppermute(block, "section", [(0, 1)])


def to_encoder(block):
    return lax.ppermute(block, "section", [(1, 0)])


def per_device(
    sources, targets, cotangent, source_lengths, target_lengths,
    attn_qkv, attn_out, ffn_in, ffn_out, norm_gains, prefix_pairs,
    adapt_down, adapt_down_bias, adapt_up, adapt_up_bias,
    cross_query, cross_pairs, cross_out, cross_gain,
):
    is_encoder = lax.axis_index("section") == 0
    prefix = jnp.pad(prefix_pairs[0], ((0, 0), (0, PRE_PAD - PRE), (0, 0)))
    w = dict(
        qkv=attn_qkv[0], out=attn_out[0], ffn_in=ffn_in[0], ffn_out=ffn_out[0],
        gains=norm_gains[0], prefix=(prefix[0], prefix[1]),
        down=adapt_down[0], down_bias=adapt_down_bias,
        up=adapt_up[0], up_bias=adapt_up_bias,
    )
    cross = dict(query=cross_query, pairs=cross_pairs, out=cross_out, gain=cross_gain[None])
    half = sources.shape[1] // 2

    def at_encoder(work, *operands):
        return on_section(is_encoder, lambda *a: (work(*a), ()), lambda *a: ((), ()), *operands)[0]

    def at_decoder(work, *operands):
        return on_section(is_encoder, lambda *a: ((), ()), lambda *a: (work(*a), ()), *operands)[1]

    def at_both(enc_work, dec_work, *operands):
        return on_section(
            is_encoder, lambda *a: (enc_work(*a), ()), lambda *a: (dec_work(*a), ()), *operands
        )[:2]

    def encoder_start():
        qkv = product(sources, w["qkv"])
        att, inv, *weights = attend(
            source_lengths, *self_columns(qkv), w["prefix"], enc_segs, False
        )
        return (qkv, att, inv, weights), enc_ffn(sources, att, w, 2)

    (saved, part2), (cq, kept) = at_both(
        encoder_start, lambda: decoder_self(targets, target_lengths, w, cross)
    )
    mem2 = to_decoder(part2[0])
    part1 = at_encoder(lambda saved: enc_ffn(sources, saved[1], w, 1), saved)
    mem1 = to_decoder(part1[0])

    def decoder_short(saved, mem2, cq):
        kv2 = product(mem2, cross["pairs"])
        return kv2, cross_forward(source_lengths, cq, [kv2], 1)

    part0, (kv2, short) = at_both(
        lambda saved, mem2, cq: enc_ffn(sources, saved[1], w, 0), decoder_short, saved, mem2, cq
    )
    mem0 = to_decoder(part0[0])
    kv1 = at_decoder(lambda mem1: product(mem1, cross["pairs"]), mem1)

    def decoder_long(mem0, kv1, kv2, cq, kept):
        kvs = [product(mem0, cross["pairs"]), kv1, kv2]
        long = cross_forward(source_lengths, cq, kvs, 0)
        y, dsecond, dcatt, *adapter = dec_ffn(
            target_lengths, kept[4], long[0], cotangent, w, cross, 0
        )
        dcq, dck, dcv = cross_backward(cq, kvs, long, dcatt, 0)
        cuts = ((0, ENC_ROWS), (ENC_ROWS, ENC_ROWS), (2 * ENC_ROWS, SRC_LONG - 2 * ENC_ROWS))
        return back_product([dck, dcv], cross["pairs"], cuts=cuts), y, dsecond, dcq, adapter

    dmems, *long = at_decoder(decoder_long, mem0, kv1, kv2, cq, kept)
    dmem0, dmem1, dmem2 = [to_encoder(block) for block in dmems]

    def decoder_short_back(dmem0, part0, kv2, cq, kept, short):
        y, dsecond, dcatt, *adapter = dec_ffn(
            target_lengths, kept[4], short[0], cotangent, w, cross, 1
        )
        dcq, dck, dcv = cross_backward(cq, [kv2], short, dcatt, 1)
        return back_product([dck, dcv], cross["pairs"])[0], y, dsecond, dcq, adapter

    back0, (dmem_short, *short) = at_both(
        lambda dmem0, part0, *a: enc_ffn_back(dmem0, part0, w),
        decoder_short_back, dmem0, part0, kv2, cq, kept, short,
    )
    dmem_short = to_encoder(dmem_short)

    def decoder_end(dmem1, part1, kept, long, short):
        y, dsecond, dcq = [jnp.concatenate([a, b], 0) for a, b in zip(long[:3], short[:3])]
        dt, dprefix = decoder_self_back(kept, dsecond, dcq, w, cross)
        adapter = jax.tree.map(jnp.add, long[3], short[3])
        highs = jnp.stack([y[:, half:], dt[:, half:]])
        return highs, jnp.stack([y[:, :half], dt[:, :half]]), dprefix, adapter

    back1, (highs, lows, dec_prefix, dec_adapter) = at_both(
        lambda dmem1, part1, *a: enc_ffn_back(dmem1, part1, w),
        decoder_end, dmem1, part1, kept, long, short,
    )

    def encoder_end(dmem2, dmem_short, part0, part1, part2, back0, back1, dec_adapter):
        back2 = enc_ffn_back(jnp.concatenate([dmem2, dmem_short], 0), part2, w)
        parts, backs = (part0, part1, part2), (back0, back1, back2)
        adapter = adapter_grads(
            [p[4] for p in parts], [p[3] for p in parts],
            [b[2] for b in backs], [b[3] for b in backs],
        )
        return back2, list(adapter)

    back2, _, adapter = on_section(
        is_encoder, encoder_end, lambda *a: ((), list(a[-1])),
        dmem2, dmem_short, part0, part1, part2, back0, back1, dec_adapter,
    )
    backs = (back0, back1, back2)
    source_grad, low, up, down, small = finish(
        saved, [b[1] for b in backs], [b[0] for b in backs], w, adapter, dec_prefix, lows
    )
    target_halves = jnp.where(is_encoder, low, highs)
    return (
        target_halves[0],
        source_grad,
        target_halves[1],
        jnp.stack([small[:PRE], small[PRE_PAD : PRE_PAD + PRE]])[None],
        down[None],
        small[PRE + 1 : PRE + 2, : down.shape[1]],
        up[None],
        small[PRE : PRE + 1],
    )


def solution(mesh):
    layer2, layer3, rows = P("section", None), P("section", None, None), P("dp", None)
    return jax.shard_map(
        per_device,
        mesh=mesh,
        in_specs=(
            rows, rows, rows, rows, rows,
            layer3, layer3, layer3, layer3, layer3,
            P("section", None, None, None),
            layer3, layer2, layer3, layer2,
            P(), P(), P(), P(),
        ),
        out_specs=(
            P("dp", "section"), P("dp", "section"), P("dp", "section"),
            P("section", None, None, None), layer3, layer2, layer3, layer2,
        ),
        check_vma=False,
    )
```

```python
import functools

import jax
import jax.numpy as jnp
from jax import lax
from jax.experimental import pallas as pl
from jax.experimental.pallas import tpu as pltpu
from jax.sharding import PartitionSpec as P

HD = 64
PRE = 30
PRE_PAD = 32
SRC_LONG = 768
SRC_SHORT = 96
TGT = 256
LANES = 128

BF = jnp.bfloat16
F32 = jnp.float32
norm_eps = 1e-05
big_negative = -1e30
adapter_scale = 4.0
chunk = 512
wide = 1024
ENC_ROWS = (SRC_LONG + SRC_SHORT) // 3
vmem_bytes = 56 * 2**20

phi_poly = (
    0.797869713181688,
    0.036392283539041996,
    -8.782472977701046e-05,
    -3.669384069669515e-05,
    1.4250308145882202e-06,
)


def nn(left, right):
    return lax.dot_general(left, right, (((1,), (0,)), ((), ())), preferred_element_type=F32)


def nt(left, right):
    return lax.dot_general(left, right, (((1,), (1,)), ((), ())), preferred_element_type=F32)


def tn(left, right):
    return lax.dot_general(left, right, (((0,), (0,)), ((), ())), preferred_element_type=F32)


def gelu_pair(values):
    square = values * values
    poly = phi_poly[4]
    for coefficient in phi_poly[3::-1]:
        poly = poly * square + coefficient
    half = 0.5 * jnp.tanh(values * poly) + 0.5
    density = jnp.exp(square * -0.5) * 0.3989422804014327
    return values * half, half + values * density


def row_tiles(rows, most=288):
    count = -(-rows // most)
    size = rows // count
    return [(i * size, size) for i in range(count)]


def norm_rows(values):
    centered = values - jnp.mean(values, axis=-1, keepdims=True)
    scale = lax.rsqrt(jnp.mean(centered * centered, axis=-1, keepdims=True) + norm_eps)
    return centered * scale, scale


def norm_rows_back(hat, scale, grad_hat):
    mean_grad = jnp.mean(grad_hat, axis=-1, keepdims=True)
    mean_dot = jnp.mean(grad_hat * hat, axis=-1, keepdims=True)
    return scale * (grad_hat - mean_grad - hat * mean_dot)


def params(limit=vmem_bytes):
    return pltpu.CompilerParams(vmem_limit_bytes=limit)


def whole(shape):
    return pl.BlockSpec(shape, lambda *g: (0,) * len(shape))


def product_kernel(x_ref, w_ref, o_ref):
    o_ref[...] = nn(x_ref[...], w_ref[...]).astype(BF)


def product(x, w, tile=1024):
    rows, depth = x.shape
    width = w.shape[1]
    return pl.pallas_call(
        product_kernel,
        grid=(width // tile,),
        in_specs=[whole((rows, depth)), pl.BlockSpec((depth, tile), lambda i: (0, i))],
        out_specs=pl.BlockSpec((rows, tile), lambda i: (0, i)),
        out_shape=jax.ShapeDtypeStruct((rows, width), BF),
        compiler_params=params(),
        name="product",
    )(x, w)


def back_product_kernel(*refs, parts, residual, cuts):
    grads = refs[:parts]
    w_ref = refs[parts]
    outs = refs[-len(cuts) :]
    total = None
    width = grads[0].shape[1]
    for i, grad in enumerate(grads):
        term = nt(grad[...], w_ref[:, i * width : (i + 1) * width])
        total = term if total is None else total + term
    if residual:
        total = total + refs[parts + 1][...]
    for (start, size), o_ref in zip(cuts, outs):
        o_ref[...] = total[start : start + size].astype(BF)


def back_product(grads, w, residual=None, tile=512, cuts=None):
    rows, width = grads[0].shape
    depth = w.shape[0]
    parts = len(grads)
    cuts = cuts or ((0, rows),)
    specs = [whole((rows, width))] * parts + [
        pl.BlockSpec((tile, parts * width), lambda i: (i, 0))
    ]
    args = list(grads) + [w]
    if residual is not None:
        specs.append(pl.BlockSpec((rows, tile), lambda i: (0, i)))
        args.append(residual)
    return pl.pallas_call(
        functools.partial(
            back_product_kernel, parts=parts, residual=residual is not None, cuts=cuts
        ),
        grid=(depth // tile,),
        in_specs=specs,
        out_specs=[pl.BlockSpec((size, tile), lambda i: (0, i)) for _, size in cuts],
        out_shape=[jax.ShapeDtypeStruct((size, depth), BF) for _, size in cuts],
        compiler_params=params(),
        name="back_product",
    )(*args)


def head_lanes(head):
    lane = lax.broadcasted_iota(jnp.int32, (1, LANES), 1)
    own = (lane < HD) if head == 0 else (lane >= HD)
    first = HD if head == 0 else 0
    return own, lane == first, lane == first + 1


def bf(value):
    return jnp.asarray(value, BF)


def rows_of(refs, start, count):
    parts = []
    for ref in refs:
        size = ref.shape[0]
        low, high = max(start, 0), min(start + count, size)
        if low < high:
            parts.append(ref[low:high])
        start -= size
    return parts


def stacked(refs, prefix_ref, start, count):
    parts = rows_of(refs, start, count)
    if prefix_ref is not None:
        parts.append(prefix_ref[...])
    return parts[0] if len(parts) == 1 else jnp.concatenate(parts, 0)


def attend_kernel(*refs, segs, prefix, causal, pieces, which):
    len_ref, q_ref = refs[:2]
    k_refs, v_refs = refs[2 : 2 + pieces], refs[2 + pieces : 2 + 2 * pieces]
    at = 2 + 2 * pieces
    pk_ref = pv_ref = None
    if prefix:
        pk_ref, pv_ref = refs[at : at + 2]
        at += 2
    o_ref, inv_ref = refs[at : at + 2]
    p_refs = refs[at + 2 :]
    for seg, (q0, nq, k0, nk) in enumerate(segs):
        keys = stacked(k_refs, pk_ref, k0, nk)
        values = stacked(v_refs, pv_ref, k0, nk)
        count = keys.shape[0]
        row = lax.broadcasted_iota(jnp.int32, (count, 1), 0)
        seen = row < jnp.minimum(len_ref[0, which + seg], nk)
        if prefix:
            seen = seen | ((row >= nk) & (row < nk + PRE))
        queries = q_ref[q0 : q0 + nq] * bf(HD**-0.5)
        out = inv = None
        for head in range(2):
            own, first, _ = head_lanes(head)
            k_own = jnp.where(own, keys, jnp.where(first & ~seen, bf(big_negative), bf(0)))
            q_own = jnp.where(own, queries, jnp.where(first, bf(1), bf(0)))
            v_own = jnp.where(own, values, bf(1))
            scores = nt(k_own, q_own)
            if causal:
                key_at = lax.broadcasted_iota(jnp.int32, scores.shape, 0)
                query_at = lax.broadcasted_iota(jnp.int32, scores.shape, 1)
                allowed = (key_at <= query_at) | (key_at >= nk)
                scores = jnp.where(allowed, scores, big_negative)
            peak = jnp.max(scores, axis=0, keepdims=True)
            weights = jnp.exp(scores - peak).astype(BF)
            p_refs[seg][head] = weights
            mixed = tn(weights, v_own)
            inverse = 1.0 / pltpu.roll(mixed, HD, 1)
            mixed = mixed * inverse
            out = mixed if out is None else jnp.where(own, mixed, out)
            inv = inverse if inv is None else jnp.where(own, inverse, inv)
        o_ref[q0 : q0 + nq] = out.astype(BF)
        inv_ref[q0 : q0 + nq] = inv


def column_spec(rows, offset, row_block=0):
    return pl.BlockSpec((rows, LANES), lambda h: (row_block, h + offset))


def attend(lengths, q, keys, values, prefixes, segs, causal, which=0):
    pairs = 8
    q_rows = q[1]
    prefix = prefixes is not None
    extra = PRE_PAD if prefix else 0
    specs = [pl.BlockSpec(memory_space=pltpu.SMEM)]
    args = [lengths]
    for array, rows, block, offset in [q, *keys, *values]:
        specs.append(column_spec(rows, offset, block))
        args.append(array)
    if prefix:
        specs += [column_spec(PRE_PAD, 0)] * 2
        args += list(prefixes)
    weight_shapes = [(2 * pairs, nk + extra, nq) for _, nq, _, nk in segs]
    return pl.pallas_call(
        functools.partial(
            attend_kernel, segs=segs, prefix=prefix, causal=causal, pieces=len(keys), which=which
        ),
        grid=(pairs,),
        in_specs=specs,
        out_specs=[column_spec(q_rows, 0), column_spec(q_rows, 0)]
        + [pl.BlockSpec((2,) + s[1:], lambda h: (h, 0, 0)) for s in weight_shapes],
        out_shape=[
            jax.ShapeDtypeStruct((q_rows, pairs * LANES), BF),
            jax.ShapeDtypeStruct((q_rows, pairs * LANES), F32),
        ]
        + [jax.ShapeDtypeStruct(s, BF) for s in weight_shapes],
        compiler_params=params(),
        name="attend",
    )(*args)


def attend_back_pair(
    q_ref, k_refs, v_refs, o_ref, inv_ref, g_refs, pk_ref, pv_ref, p_refs, dq_ref, dk_ref, dv_ref, segs
):
    prefix_totals = [None, None]
    scale = HD**-0.5
    for seg, (q0, nq, k0, nk) in enumerate(segs):
        keys = stacked(k_refs, pk_ref, k0, nk)
        values = stacked(v_refs, pv_ref, k0, nk)
        queries = q_ref[q0 : q0 + nq]
        grads = stacked(g_refs, None, q0, nq).astype(F32) * inv_ref[q0 : q0 + nq]
        grads_low = grads.astype(BF)
        dots = grads * o_ref[q0 : q0 + nq].astype(F32)
        dq = dk = dv = None
        for head in range(2):
            own, first, second = head_lanes(head)
            row_dot = -jnp.sum(jnp.where(own, dots, 0.0), axis=1, keepdims=True)
            high = row_dot.astype(BF)
            rest = (row_dot - high.astype(F32)).astype(BF)
            g_own = jnp.where(
                own, grads_low, jnp.where(first, high, jnp.where(second, rest, bf(0)))
            )
            v_own = jnp.where(own, values, jnp.where(first | second, bf(1), bf(0)))
            weights = p_refs[seg][head]
            score_grad = (weights.astype(F32) * nt(v_own, g_own)).astype(BF)
            dv_head = nn(weights, grads_low)
            dk_head = nn(score_grad, queries)
            dq_head = tn(score_grad, keys)
            dq = dq_head if dq is None else jnp.where(own, dq_head, dq)
            dk = dk_head if dk is None else jnp.where(own, dk_head, dk)
            dv = dv_head if dv is None else jnp.where(own, dv_head, dv)
        dk = dk * scale
        dq_ref[q0 : q0 + nq] = (dq * scale).astype(BF)
        at = k0 - segs[0][2]
        dk_ref[at : at + nk] = dk[:nk].astype(BF)
        dv_ref[at : at + nk] = dv[:nk].astype(BF)
        if pk_ref is not None:
            for i, grad in enumerate((dk, dv)):
                part = grad[nk:]
                prefix_totals[i] = part if seg == 0 else prefix_totals[i] + part
    return prefix_totals


def attend_back_kernel(*refs, segs, prefix, pieces):
    q_ref, o_ref, inv_ref, g_ref = refs[:4]
    k_refs, v_refs = refs[4 : 4 + pieces], refs[4 + pieces : 4 + 2 * pieces]
    at = 4 + 2 * pieces
    pk_ref = pv_ref = None
    if prefix:
        pk_ref, pv_ref = refs[at : at + 2]
        at += 2
    outs = refs[at + len(segs) :]
    totals = attend_back_pair(
        q_ref, k_refs, v_refs, o_ref, inv_ref, [g_ref], pk_ref, pv_ref,
        refs[at : at + len(segs)], *outs[:3], segs,
    )
    if prefix:
        outs[3][...] = totals[0]
        outs[4][...] = totals[1]


def attend_back(q, keys, values, prefixes, attended, inverse, grad, weights, segs):
    pairs = 8
    q_rows = q[1]
    k_rows = sum(nk for _, _, _, nk in segs)
    prefix = prefixes is not None
    specs, args = [], []
    own = [(a, q_rows, 0, 0) for a in (attended, inverse, grad)]
    for array, rows, block, offset in [q, *own, *keys, *values]:
        specs.append(column_spec(rows, offset, block))
        args.append(array)
    if prefix:
        specs += [column_spec(PRE_PAD, 0)] * 2
        args += list(prefixes)
    specs += [pl.BlockSpec((2,) + w.shape[1:], lambda h: (h, 0, 0)) for w in weights]
    args += list(weights)
    out_specs = [column_spec(q_rows, 0), column_spec(k_rows, 0), column_spec(k_rows, 0)]
    out_shape = [
        jax.ShapeDtypeStruct((q_rows, pairs * LANES), BF),
        jax.ShapeDtypeStruct((k_rows, pairs * LANES), BF),
        jax.ShapeDtypeStruct((k_rows, pairs * LANES), BF),
    ]
    if prefix:
        out_specs += [column_spec(PRE_PAD, 0)] * 2
        out_shape += [jax.ShapeDtypeStruct((PRE_PAD, pairs * LANES), F32)] * 2
    return pl.pallas_call(
        functools.partial(
            attend_back_kernel, segs=segs, prefix=prefix, pieces=len(keys)
        ),
        grid=(pairs,),
        in_specs=specs,
        out_specs=out_specs,
        out_shape=out_shape,
        compiler_params=params(),
        name="attend_back",
    )(*args)


def ffn_step(low_ref, acc_ref, in_ref, out_ref, slope_ref, act_ref, bias_ref, scale):
    for start, size in row_tiles(low_ref.shape[0]):
        rows = slice(start, start + size)
        hidden = nn(low_ref[rows], in_ref[...])
        if bias_ref is not None:
            hidden = hidden + bias_ref[...]
        active, slope = gelu_pair(hidden)
        slope_ref[rows] = slope.astype(BF)
        active = active.astype(BF)
        if act_ref is not None:
            act_ref[rows] = active
        term = nn(active, out_ref[...])
        acc_ref[rows] += term if scale is None else scale * term


def enc_ffn_kernel(
    x_ref, att_ref, wo_ref, gain_ref, in_ref, out_ref, down_ref, downb_ref, up_ref, upb_ref,
    mem_ref, slope_ref, pre_slope_ref, act_ref, low_ref, scales_ref, acc_ref,
):
    step = pl.program_id(0)
    last = pl.num_programs(0) - 1

    @pl.when(step == 0)
    def _():
        first = x_ref[...].astype(F32) + nn(att_ref[...], wo_ref[...])
        hat, scale = norm_rows(first)
        normed = hat * gain_ref[0:1]
        acc_ref[...] = normed
        low_ref[...] = normed.astype(BF)
        scales_ref[:, 0:1] = scale

    @pl.when((step > 0) & (step < last))
    def _():
        ffn_step(low_ref, acc_ref, in_ref, out_ref, slope_ref, None, None, None)

    @pl.when(step == last)
    def _():
        ffn_step(
            low_ref, acc_ref, down_ref, up_ref, pre_slope_ref, act_ref, downb_ref, adapter_scale
        )
        hat, scale = norm_rows(acc_ref[...] + adapter_scale * upb_ref[...])
        mem_ref[...] = (hat * gain_ref[1:2]).astype(BF)
        scales_ref[:, 1:2] = scale


def enc_ffn(x, att, w, part):
    width = x.shape[1]
    rows = ENC_ROWS
    hidden = w["ffn_in"].shape[1]
    steps = hidden // wide

    def at(i):
        return jnp.clip(i - 1, 0, steps - 1)

    return pl.pallas_call(
        enc_ffn_kernel,
        grid=(steps + 2,),
        in_specs=[
            pl.BlockSpec((rows, width), lambda i: (part, 0)),
            pl.BlockSpec((rows, width), lambda i: (part, 0)),
            whole((width, width)),
            whole((2, width)),
            pl.BlockSpec((width, wide), lambda i: (0, at(i))),
            pl.BlockSpec((wide, width), lambda i: (at(i), 0)),
            whole((width, chunk)),
            whole((1, chunk)),
            whole((chunk, width)),
            whole((1, width)),
        ],
        out_specs=[
            whole((rows, width)),
            pl.BlockSpec((rows, wide), lambda i: (0, at(i))),
            whole((rows, chunk)),
            whole((rows, chunk)),
            whole((rows, width)),
            whole((rows, LANES)),
        ],
        out_shape=[
            jax.ShapeDtypeStruct((rows, width), BF),
            jax.ShapeDtypeStruct((rows, hidden), BF),
            jax.ShapeDtypeStruct((rows, chunk), BF),
            jax.ShapeDtypeStruct((rows, chunk), BF),
            jax.ShapeDtypeStruct((rows, width), BF),
            jax.ShapeDtypeStruct((rows, LANES), F32),
        ],
        scratch_shapes=[pltpu.VMEM((rows, width), F32)],
        compiler_params=params(),
        name="enc_ffn",
    )(
        x, att, w["out"], w["gains"], w["ffn_in"], w["ffn_out"],
        w["down"], w["down_bias"], w["up"], w["up_bias"],
    )


def ffn_back_step(grad_ref, acc_ref, in_ref, out_ref, slope_ref):
    for start, size in row_tiles(grad_ref.shape[0]):
        rows = slice(start, start + size)
        pre = (nt(grad_ref[rows], out_ref[...]) * slope_ref[rows].astype(F32)).astype(BF)
        acc_ref[rows] += nt(pre, in_ref[...])


def adapter_back(grad_ref, acc_ref, low_ref, act_ref, slope_ref, down_ref, up_ref, outs, pre_ref):
    ddown_ref, ddownb_ref, dup_ref, dupb_ref = outs
    total = None
    for start, size in row_tiles(grad_ref.shape[0]):
        rows = slice(start, start + size)
        back = adapter_scale * nt(grad_ref[rows], up_ref[...])
        pre = (back * slope_ref[rows].astype(F32)).astype(BF)
        pre_ref[rows] = pre
        sums = jnp.sum(pre.astype(F32), axis=0, keepdims=True)
        total = sums if total is None else total + sums
        acc_ref[rows] += nt(pre, down_ref[...])
    ddownb_ref[...] = total
    ddown_ref[...] = tn(low_ref[...], pre_ref[...])
    dup_ref[...] = adapter_scale * tn(act_ref[...], grad_ref[...])
    dupb_ref[...] = adapter_scale * jnp.sum(grad_ref[...].astype(F32), axis=0, keepdims=True)


def enc_ffn_back_kernel(
    *refs, pieces,
):
    enc_ffn_back_body(refs[:pieces], *refs[pieces:])


def enc_ffn_back_body(
    dmem_refs, mem_ref, low_ref, scales_ref, gain_ref, slope_ref, pre_slope_ref,
    in_ref, out_ref, down_ref, up_ref, wo_ref,
    dfirst_ref, datt_ref, grad_ref, pre_ref,
    acc_ref,
):
    step = pl.program_id(0)
    last = pl.num_programs(0) - 1

    @pl.when(step == 0)
    def _():
        gain = gain_ref[1:2]
        hat = mem_ref[...].astype(F32) / gain
        grad = norm_rows_back(hat, scales_ref[:, 1:2], stacked(dmem_refs, None, 0, ENC_ROWS).astype(F32) * gain)
        low = grad.astype(BF)
        grad_ref[...] = low
        back = adapter_scale * nt(low, up_ref[...])
        pre = (back * pre_slope_ref[...].astype(F32)).astype(BF)
        pre_ref[...] = pre
        acc_ref[...] = grad + nt(pre, down_ref[...])

    ffn_back_step(grad_ref, acc_ref, in_ref, out_ref, slope_ref)

    @pl.when(step == last)
    def _():
        gain = gain_ref[0:1]
        hat = low_ref[...].astype(F32) / gain
        grad = norm_rows_back(hat, scales_ref[:, 0:1], acc_ref[...] * gain)
        dfirst_ref[...] = grad
        datt_ref[...] = nt(grad.astype(BF), wo_ref[...]).astype(BF)


def enc_ffn_back(dmems, saved, w):
    mem, slope, pre_slope, act, low, scales = saved
    rows, width = mem.shape
    hidden = w["ffn_in"].shape[1]
    steps = hidden // wide
    return pl.pallas_call(
        functools.partial(enc_ffn_back_kernel, pieces=len(dmems)),
        grid=(steps,),
        in_specs=[whole(d.shape) for d in dmems]
        + [
            whole((rows, width)),
            whole((rows, width)),
            whole((rows, LANES)),
            whole((2, width)),
            pl.BlockSpec((rows, wide), lambda i: (0, i)),
            whole((rows, chunk)),
            pl.BlockSpec((width, wide), lambda i: (0, i)),
            pl.BlockSpec((wide, width), lambda i: (i, 0)),
            whole((width, chunk)),
            whole((chunk, width)),
            whole((width, width)),
        ],
        out_specs=[
            whole((rows, width)),
            whole((rows, width)),
            whole((rows, width)),
            whole((rows, chunk)),
        ],
        out_shape=[
            jax.ShapeDtypeStruct((rows, width), F32),
            jax.ShapeDtypeStruct((rows, width), BF),
            jax.ShapeDtypeStruct((rows, width), BF),
            jax.ShapeDtypeStruct((rows, chunk), BF),
        ],
        scratch_shapes=[pltpu.VMEM((rows, width), F32)],
        compiler_params=params(),
        name="enc_ffn_back",
    )(
        *dmems, mem, low, scales, w["gains"], slope, pre_slope,
        w["ffn_in"], w["ffn_out"], w["down"], w["up"], w["out"],
    )


def adapter_grads_kernel(*refs, parts):
    groups = [refs[n * parts : (n + 1) * parts] for n in range(4)]
    low, act, grad, pre = [jnp.concatenate([r[...] for r in g], 0) for g in groups]
    ddown_ref, ddownb_ref, dup_ref, dupb_ref = refs[4 * parts :]
    ddown_ref[...] = tn(low, pre)
    ddownb_ref[...] = jnp.sum(pre.astype(F32), axis=0, keepdims=True)
    dup_ref[...] = adapter_scale * tn(act, grad)
    dupb_ref[...] = adapter_scale * jnp.sum(grad.astype(F32), axis=0, keepdims=True)


def adapter_grads(lows, acts, grads, pres):
    width = lows[0].shape[1]
    return pl.pallas_call(
        functools.partial(adapter_grads_kernel, parts=len(lows)),
        out_shape=[
            jax.ShapeDtypeStruct((width, chunk), F32),
            jax.ShapeDtypeStruct((1, chunk), F32),
            jax.ShapeDtypeStruct((chunk, width), F32),
            jax.ShapeDtypeStruct((1, width), F32),
        ],
        compiler_params=params(),
        name="adapter_grads",
    )(*lows, *acts, *grads, *pres)


def dec_mid_kernel(x_ref, att_ref, wo_ref, gain_ref, wq_ref, n_ref, scale_ref, cq_ref):
    for start, size in row_tiles(x_ref.shape[0], 256):
        rows = slice(start, start + size)
        first = x_ref[rows].astype(F32) + nn(att_ref[rows], wo_ref[...])
        hat, scale = norm_rows(first)
        normed = hat * gain_ref[0:1]
        n_ref[rows] = normed
        scale_ref[rows, 0:1] = scale
        cq_ref[rows] = nn(normed.astype(BF), wq_ref[...]).astype(BF)


def dec_mid(x, att, w, cross):
    rows, width = x.shape
    return pl.pallas_call(
        dec_mid_kernel,
        out_shape=[
            jax.ShapeDtypeStruct((rows, width), F32),
            jax.ShapeDtypeStruct((rows, LANES), F32),
            jax.ShapeDtypeStruct((rows, width), BF),
        ],
        compiler_params=params(),
        name="dec_mid",
    )(x, att, w["out"], w["gains"], cross["query"])


def dec_ffn_kernel(
    len_ref, n_ref, catt_ref, cot_ref, wco_ref, cgain_ref, gain_ref,
    in_ref, out_ref, down_ref, downb_ref, up_ref, upb_ref,
    y_ref, dsecond_ref, dcatt_ref, ddown_ref, ddownb_ref, dup_ref, dupb_ref,
    acc_ref, low_ref, grad_ref, slope_ref, pre_slope_ref, act_ref, pre_ref, scale_ref,
    *, steps, which,
):
    step = pl.program_id(0)
    tiles = row_tiles(n_ref.shape[0], TGT)

    @pl.when(step == 0)
    def _():
        for start, size in tiles:
            rows = slice(start, start + size)
            second = n_ref[rows] + nn(catt_ref[rows], wco_ref[...])
            hat, scale = norm_rows(second)
            middle = hat * cgain_ref[...]
            acc_ref[rows] = middle
            low_ref[rows] = middle.astype(BF)
            scale_ref[rows, 0:1] = scale

    @pl.when((step > 0) & (step <= steps))
    def _():
        ffn_step(low_ref, acc_ref, in_ref, out_ref, slope_ref.at[step - 1], None, None, None)

    @pl.when(step == steps + 1)
    def _():
        ffn_step(
            low_ref, acc_ref, down_ref, up_ref, pre_slope_ref, act_ref, downb_ref,
            adapter_scale,
        )
        for start, size in tiles:
            rows = slice(start, start + size)
            gain = gain_ref[1:2]
            hat, scale = norm_rows(acc_ref[rows] + adapter_scale * upb_ref[...])
            valid = lax.broadcasted_iota(jnp.int32, (size, 1), 0) < len_ref[0, which]
            y_ref[rows] = jnp.where(valid, hat * gain, 0.0).astype(BF)
            cot = jnp.where(valid, cot_ref[rows].astype(F32), 0.0)
            grad = norm_rows_back(hat, scale, cot * gain)
            acc_ref[rows] = grad
            grad_ref[rows] = grad.astype(BF)
        adapter_back(
            grad_ref, acc_ref, low_ref, act_ref, pre_slope_ref, down_ref, up_ref,
            (ddown_ref, ddownb_ref, dup_ref, dupb_ref), pre_ref,
        )

    @pl.when(step > steps + 1)
    def _():
        ffn_back_step(grad_ref, acc_ref, in_ref, out_ref, slope_ref.at[2 * steps + 1 - step])

    @pl.when(step == 2 * steps + 1)
    def _():
        for start, size in tiles:
            rows = slice(start, start + size)
            gain = cgain_ref[...]
            hat = low_ref[rows].astype(F32) / gain
            grad = norm_rows_back(hat, scale_ref[rows, 0:1], acc_ref[rows] * gain)
            dsecond_ref[rows] = grad
            dcatt_ref[rows] = nt(grad.astype(BF), wco_ref[...]).astype(BF)


def dec_ffn(lengths, n, catt, cot, w, cross, which):
    rows, width = catt.shape
    hidden = w["ffn_in"].shape[1]
    steps = hidden // wide

    def at(i):
        return jnp.where(i <= steps, jnp.clip(i - 1, 0, steps - 1), jnp.clip(2 * steps + 1 - i, 0, steps - 1))

    return pl.pallas_call(
        functools.partial(dec_ffn_kernel, steps=steps, which=which),
        grid=(2 * steps + 2,),
        in_specs=[
            pl.BlockSpec(memory_space=pltpu.SMEM),
            pl.BlockSpec((rows, width), lambda i: (which, 0)),
            whole((rows, width)),
            pl.BlockSpec((rows, width), lambda i: (which, 0)),
            whole((width, width)),
            whole((1, width)),
            whole((2, width)),
            pl.BlockSpec((width, wide), lambda i: (0, at(i))),
            pl.BlockSpec((wide, width), lambda i: (at(i), 0)),
            whole((width, chunk)),
            whole((1, chunk)),
            whole((chunk, width)),
            whole((1, width)),
        ],
        out_specs=[
            whole((rows, width)),
            whole((rows, width)),
            whole((rows, width)),
            whole((width, chunk)),
            whole((1, chunk)),
            whole((chunk, width)),
            whole((1, width)),
        ],
        out_shape=[
            jax.ShapeDtypeStruct((rows, width), BF),
            jax.ShapeDtypeStruct((rows, width), F32),
            jax.ShapeDtypeStruct((rows, width), BF),
            jax.ShapeDtypeStruct((width, chunk), F32),
            jax.ShapeDtypeStruct((1, chunk), F32),
            jax.ShapeDtypeStruct((chunk, width), F32),
            jax.ShapeDtypeStruct((1, width), F32),
        ],
        scratch_shapes=[
            pltpu.VMEM((rows, width), F32),
            pltpu.VMEM((rows, width), BF),
            pltpu.VMEM((rows, width), BF),
            pltpu.VMEM((steps, rows, wide), BF),
            pltpu.VMEM((rows, chunk), BF),
            pltpu.VMEM((rows, chunk), BF),
            pltpu.VMEM((rows, chunk), BF),
            pltpu.VMEM((rows, LANES), F32),
        ],
        compiler_params=params(),
        name="dec_ffn",
    )(
        lengths, n, catt, cot, cross["out"], cross["gain"], w["gains"],
        w["ffn_in"], w["ffn_out"], w["down"], w["down_bias"], w["up"], w["up_bias"],
    )


def dec_mid_back_kernel(
    dsecond_ref, dcq_ref, wq_ref, n_ref, scale_ref, gain_ref, wo_ref, dfirst_ref, datt_ref
):
    for start, size in row_tiles(n_ref.shape[0], 256):
        rows = slice(start, start + size)
        gain = gain_ref[0:1]
        total = dsecond_ref[rows] + nt(dcq_ref[rows], wq_ref[...])
        grad = norm_rows_back(n_ref[rows] / gain, scale_ref[rows, 0:1], total * gain)
        dfirst_ref[rows] = grad
        datt_ref[rows] = nt(grad.astype(BF), wo_ref[...]).astype(BF)


def dec_mid_back(dsecond, dcq, n, scale, w, cross):
    rows, width = n.shape
    return pl.pallas_call(
        dec_mid_back_kernel,
        out_shape=[
            jax.ShapeDtypeStruct((rows, width), F32),
            jax.ShapeDtypeStruct((rows, width), BF),
        ],
        compiler_params=params(),
        name="dec_mid_back",
    )(dsecond, dcq, cross["query"], n, scale, w["gains"], w["out"])


enc_segs = ((0, SRC_LONG, 0, SRC_LONG), (SRC_LONG, SRC_SHORT, SRC_LONG, SRC_SHORT))
dec_segs = ((0, TGT, 0, TGT), (TGT, TGT, TGT, TGT))
cross_segs = (((0, TGT, 0, SRC_LONG),), ((0, TGT, SRC_LONG % ENC_ROWS, SRC_SHORT),))


def self_columns(qkv):
    rows = qkv.shape[0]
    return (qkv, rows, 0, 0), [(qkv, rows, 0, 8)], [(qkv, rows, 0, 16)]


def cross_columns(cq, kvs, which):
    return (
        (cq, TGT, which, 0),
        [(kv, ENC_ROWS, 0, 0) for kv in kvs],
        [(kv, ENC_ROWS, 0, 8) for kv in kvs],
    )


def decoder_self(t, lengths, w, cross):
    qkv = product(t, w["qkv"])
    att, inv, *weights = attend(lengths, *self_columns(qkv), w["prefix"], dec_segs, True)
    n, scale, cq = dec_mid(t, att, w, cross)
    return cq, (qkv, att, inv, weights, n, scale)


def cross_forward(lengths, cq, kvs, which):
    return attend(
        lengths, *cross_columns(cq, kvs, which), None, cross_segs[which], False, which
    )


def cross_backward(cq, kvs, forward, dcatt, which):
    catt, inv, *weights = forward
    return attend_back(
        *cross_columns(cq, kvs, which), None, catt, inv, dcatt, weights, cross_segs[which]
    )


def decoder_self_back(kept, dsecond, dcq, w, cross):
    qkv, att, inv, weights, n, scale = kept
    dfirst, datt = dec_mid_back(dsecond, dcq, n, scale, w, cross)
    dq, dk, dv, *dprefix = attend_back(
        *self_columns(qkv), w["prefix"], att, inv, datt, weights, dec_segs
    )
    return back_product([dq, dk, dv], w["qkv"], dfirst)[0], dprefix


def small_shape(devices):
    return 8, 8 * (2 * chunk) // devices


def finish_kernel(
    q_ref, k_ref, v_ref, o_ref, inv_ref, g0_ref, g1_ref, g2_ref, pk_ref, pv_ref, pl_ref, ps_ref,
    dfirst0_ref, dfirst1_ref, dfirst2_ref, wqkv_ref, up_ref, down_ref, upb_ref, downb_ref, dpk_ref, dpv_ref,
    lows,
    source_ref, low_ref, o_sums_ref, o_small_ref,
    dq, dk, dv, small, mine, theirs, half_sum, landed, total, result,
    small_landed, small_total, small_result, dx_low, dx_high, dx_landed, lows_landed,
    pair_sems, spread_sems, gather_sems, back_sems, small_sems, share_sems, cross_sems,
    *, devices,
):
    step = pl.program_id(0)
    pairs = 8
    is_encoder = lax.axis_index("section") == 0
    section = lax.axis_index("section")
    chips = devices // 2
    rows = 2 * chunk
    half, part = rows // 2, rows // devices
    place = lax.axis_index("dp")
    core, chip = lax.rem(place, 2), place // 2
    partner = place + 1 - 2 * core
    small_rows, small_cols = small_shape(devices)
    tile = 256
    width = 2 * chunk
    scale = 1.0 / devices

    def peer(distance):
        return lax.rem(chip + distance, chips) * 2 + core

    def remote(source, target, send_sem, recv_sem, other):
        return pltpu.make_async_remote_copy(
            src_ref=source, dst_ref=target, send_sem=send_sem, recv_sem=recv_sem,
            device_id=other, device_id_type=pl.DeviceIdType.MESH,
        )

    def in_group(other):
        return {"dp": other}

    across = {"section": 1 - section}
    kept = pl.multiple_of(core * half, 16)
    given = pl.multiple_of((1 - core) * half, 16)
    here = pl.multiple_of(kept + chip * part, 16)

    def swap():
        return remote(
            mine.at[pl.ds(given, half)], theirs, pair_sems.at[0], pair_sems.at[1],
            in_group(partner),
        )

    def spread(s):
        at = pl.multiple_of(lax.rem(chip + s, chips) * part, 16)
        return remote(
            half_sum.at[pl.ds(at, part)], landed.at[s - 1],
            spread_sems.at[0, s - 1], spread_sems.at[1, s - 1], in_group(peer(s)),
        )

    def gather(s):
        return remote(
            total, result.at[pl.ds(here, part)],
            gather_sems.at[0, s - 1], gather_sems.at[1, s - 1], in_group(peer(s)),
        )

    def back(s):
        source = lax.rem(chip + chips - s, chips)
        there = pl.ds(pl.multiple_of(kept + source * part, 16), part)
        return remote(
            total if s == 0 else result.at[there], result.at[there],
            back_sems.at[0, s], back_sems.at[1, s], in_group(partner),
        )

    def piece(index):
        row = pl.multiple_of(lax.rem(index, 8) * small_rows, 8)
        col = pl.multiple_of((index // 8) * small_cols, LANES)
        return pl.ds(row, small_rows), pl.ds(col, small_cols)

    def small_out(s):
        return remote(
            small.at[piece(lax.rem(place + s, devices))], small_landed.at[s - 1],
            small_sems.at[0, s - 1], small_sems.at[1, s - 1],
            in_group(lax.rem(place + s, devices)),
        )

    def small_share(s):
        return remote(
            small_total, small_result.at[piece(place)],
            share_sems.at[0, s - 1], share_sems.at[1, s - 1],
            in_group(lax.rem(place + s, devices)),
        )

    def send_low():
        return remote(lows, lows_landed, cross_sems.at[0, 0], cross_sems.at[1, 0], across)

    def send_high(i):
        return remote(
            dx_high.at[i], dx_landed.at[i], cross_sems.at[0, 1 + i], cross_sems.at[1, 1 + i], across
        )

    def greet(barrier, other):
        pl.semaphore_signal(
            barrier, inc=1, device_id=other, device_id_type=pl.DeviceIdType.MESH
        )

    @pl.when(step == 0)
    def _():
        barrier = pltpu.get_barrier_semaphore()
        for s in range(1, devices):
            greet(barrier, in_group(lax.rem(place + s, devices)))
        mine[0:chunk] = (up_ref[...] * scale).astype(BF)
        mine[chunk:width, 0:chunk] = (down_ref[0:chunk] * scale).astype(BF)
        mine[chunk:width, chunk:width] = (down_ref[chunk:width] * scale).astype(BF)
        @pl.when(is_encoder)
        def _():
            pl.semaphore_wait(barrier, devices - 1)
            greet(barrier, across)

        @pl.when(jnp.logical_not(is_encoder))
        def _():
            pl.semaphore_wait(barrier, devices)
            greet(barrier, across)

        swap().start()

        @pl.when(jnp.logical_not(is_encoder))
        def _():
            send_low().start()
            small[0:PRE_PAD] = dpk_ref[...] * scale
            small[PRE_PAD : 2 * PRE_PAD] = dpv_ref[...] * scale

    @pl.when(is_encoder & (step < pairs))
    def _():
        at = pl.multiple_of(step * LANES, LANES)
        lanes = pl.ds(at, LANES)
        prefix_totals = attend_back_pair(
            q_ref, [k_ref], [v_ref], o_ref, inv_ref, [g0_ref, g1_ref, g2_ref], pk_ref, pv_ref,
            (pl_ref, ps_ref),
            dq.at[:, lanes], dk.at[:, lanes], dv.at[:, lanes], enc_segs,
        )
        small[0:PRE_PAD, lanes] = prefix_totals[0] * scale
        small[PRE_PAD : 2 * PRE_PAD, lanes] = prefix_totals[1] * scale

    @pl.when(step == 0)
    def _():
        swap().wait()
        half_sum[...] = (
            mine[pl.ds(kept, half)].astype(F32) + theirs[...].astype(F32)
        ).astype(BF)
        for s in range(1, chips):
            spread(s).start()

    @pl.when(step == pairs - 2)
    def _():
        summed = half_sum[pl.ds(pl.multiple_of(chip * part, 16), part)].astype(F32)
        for s in range(1, chips):
            spread(s).wait()
            summed = summed + landed[s - 1].astype(F32)
        total[...] = summed.astype(BF)
        result[pl.ds(here, part)] = total[...]
        for s in range(1, chips):
            gather(s).start()
        back(0).start()

    @pl.when(step == pairs - 1)
    def _():
        down_row = jnp.concatenate([downb_ref[...], jnp.zeros_like(downb_ref)], 1)
        small[PRE : PRE + 1] = upb_ref[...] * scale
        small[PRE + 1 : PRE + 2] = down_row * scale
        for s in range(1, devices):
            small_out(s).start()

    @pl.when(is_encoder & (step == pairs))
    def _():
        pl.semaphore_wait(pltpu.get_barrier_semaphore(), 1)

    for i in range(4):

        @pl.when(is_encoder & (step == pairs + i))
        def _(i=i):
            acc = jnp.concatenate([dfirst0_ref[...], dfirst1_ref[...], dfirst2_ref[...]], 0)
            for n, grad in enumerate((dq, dk, dv)):
                acc = acc + nt(grad[...], wqkv_ref[:, n * width : (n + 1) * width])
            if i < 2:
                dx_high[i] = acc.astype(BF)
                send_high(i).start()
            else:
                dx_low[:, (i - 2) * tile : (i - 1) * tile] = acc.astype(BF)

    @pl.when(step == pairs + 1)
    def _():
        own_rows, own_cols = piece(place)
        summed = small[own_rows, own_cols]
        for s in range(1, devices):
            small_out(s).wait()
            summed = summed + small_landed[s - 1]
        small_total[...] = summed
        small_result[own_rows, own_cols] = summed
        for s in range(1, devices):
            small_share(s).start()

    @pl.when(step == pairs + 3)
    def _():
        for s in range(1, chips):
            gather(s).wait()
            back(s).start()
        for s in range(1, devices):
            small_share(s).wait()
        for s in range(chips):
            back(s).wait()
        o_small_ref[...] = small_result[...]
        o_sums_ref[...] = result[...]

        @pl.when(is_encoder)
        def _():
            send_low().wait_recv()
            low_ref[...] = lows_landed[...]
            source_ref[...] = dx_low[...]
            for i in range(2):
                send_high(i).wait_send()

        @pl.when(jnp.logical_not(is_encoder))
        def _():
            send_low().wait_send()
            for i in range(2):
                send_high(i).wait_recv()
                source_ref[:, i * tile : (i + 1) * tile] = dx_landed[i]


def finish(saved, datts, dfirsts, w, adapter, dec_prefix, lows):
    qkv, att, inv, weights = saved
    ddown, ddownb, dup, dupb = adapter
    devices = lax.axis_size("dp")
    chips = devices // 2
    rows, width = att.shape
    targets = lows.shape[1]
    pairs, tile = 8, 256
    half = width // 2
    part = width // devices
    small_rows, small_cols = small_shape(devices)

    def pair(offset):
        return pl.BlockSpec((rows, LANES), lambda i: (0, jnp.minimum(i, pairs - 1) + offset))

    def at(i):
        return jnp.where(i < pairs + 2, 2 + jnp.maximum(i - pairs, 0), i - pairs - 2)

    def once(shape):
        return pl.BlockSpec(shape, lambda i: (0,) * len(shape), pipeline_mode=pl.Buffered(1))

    prefix_pair = pl.BlockSpec((PRE_PAD, LANES), lambda i: (0, jnp.minimum(i, pairs - 1)))
    vmem = pltpu.VMEM
    dma = pltpu.SemaphoreType.DMA
    return pl.pallas_call(
        functools.partial(finish_kernel, devices=devices),
        grid=(pairs + 4,),
        in_specs=[pair(0), pair(8), pair(16), pair(0), pair(0)]
        + [pl.BlockSpec((ENC_ROWS, LANES), lambda i: (0, jnp.minimum(i, pairs - 1)))] * 3
        + [prefix_pair] * 2
        + [
            pl.BlockSpec((2,) + p.shape[1:], lambda i: (jnp.minimum(i, pairs - 1), 0, 0))
            for p in weights
        ]
        + [
            pl.BlockSpec((ENC_ROWS, tile), lambda i: (0, at(i))),
        ]
        * 3
        + [
            pl.BlockSpec((tile, 3 * width), lambda i: (at(i), 0)),
        ]
        + [once(a.shape) for a in (dup, ddown, dupb, ddownb, *dec_prefix)]
        + [pl.BlockSpec(memory_space=pl.ANY)],
        out_specs=[
            once((rows, half)), once((2, targets, half)), once((width, width)),
            once((2 * PRE_PAD, width)),
        ],
        out_shape=[
            jax.ShapeDtypeStruct((rows, half), BF),
            jax.ShapeDtypeStruct((2, targets, half), BF),
            jax.ShapeDtypeStruct((width, width), BF),
            jax.ShapeDtypeStruct((2 * PRE_PAD, width), F32),
        ],
        scratch_shapes=[
            vmem((rows, width), BF), vmem((rows, width), BF), vmem((rows, width), BF),
            vmem((2 * PRE_PAD, width), F32),
            vmem((width, width), BF), vmem((half, width), BF), vmem((half, width), BF),
            vmem((chips - 1, part, width), BF), vmem((part, width), BF), vmem((width, width), BF),
            vmem((devices - 1, small_rows, small_cols), F32), vmem((small_rows, small_cols), F32),
            vmem((2 * PRE_PAD, width), F32),
            vmem((rows, half), BF), vmem((2, rows, tile), BF), vmem((2, rows, tile), BF),
            vmem((2, targets, half), BF),
            dma((2,)), dma((2, chips - 1)), dma((2, chips - 1)), dma((2, chips)),
            dma((2, devices - 1)), dma((2, devices - 1)), dma((2, 3)),
        ],
        compiler_params=pltpu.CompilerParams(
            vmem_limit_bytes=vmem_bytes, collective_id=0, has_side_effects=True
        ),
        name="finish",
    )(
        qkv, qkv, qkv, att, inv, *datts, *w["prefix"], *weights,
        *dfirsts, w["qkv"], dup, ddown, dupb, ddownb, *dec_prefix, lows,
    )


def blank_kernel(*refs):
    pass


def blanks(shapes):
    return pl.pallas_call(
        blank_kernel,
        out_shape=list(shapes),
        out_specs=[pl.BlockSpec(memory_space=pl.ANY)] * len(shapes),
        name="blank",
    )()


def on_section(is_encoder, encoder_work, decoder_work, *operands):
    enc_shapes, _ = jax.eval_shape(encoder_work, *operands)
    dec_shapes, _ = jax.eval_shape(decoder_work, *operands)

    def blank_like(shapes):
        leaves, tree = jax.tree.flatten(shapes)
        if not leaves:
            return shapes
        return jax.tree.unflatten(tree, blanks(leaves))

    def encoder_branch(*a):
        own, shared = encoder_work(*a)
        return own, blank_like(dec_shapes), shared

    def decoder_branch(*a):
        own, shared = decoder_work(*a)
        return blank_like(enc_shapes), own, shared

    return lax.cond(is_encoder, encoder_branch, decoder_branch, *operands)


def to_decoder(block):
    return lax.ppermute(block, "section", [(0, 1)])


def to_encoder(block):
    return lax.ppermute(block, "section", [(1, 0)])


def per_device(
    sources, targets, cotangent, source_lengths, target_lengths,
    attn_qkv, attn_out, ffn_in, ffn_out, norm_gains, prefix_pairs,
    adapt_down, adapt_down_bias, adapt_up, adapt_up_bias,
    cross_query, cross_pairs, cross_out, cross_gain,
):
    is_encoder = lax.axis_index("section") == 0
    prefix = jnp.pad(prefix_pairs[0], ((0, 0), (0, PRE_PAD - PRE), (0, 0)))
    w = dict(
        qkv=attn_qkv[0], out=attn_out[0], ffn_in=ffn_in[0], ffn_out=ffn_out[0],
        gains=norm_gains[0], prefix=(prefix[0], prefix[1]),
        down=adapt_down[0], down_bias=adapt_down_bias,
        up=adapt_up[0], up_bias=adapt_up_bias,
    )
    cross = dict(query=cross_query, pairs=cross_pairs, out=cross_out, gain=cross_gain[None])
    half = sources.shape[1] // 2

    def at_encoder(work, *operands):
        return on_section(is_encoder, lambda *a: (work(*a), ()), lambda *a: ((), ()), *operands)[0]

    def at_decoder(work, *operands):
        return on_section(is_encoder, lambda *a: ((), ()), lambda *a: (work(*a), ()), *operands)[1]

    def at_both(enc_work, dec_work, *operands):
        return on_section(
            is_encoder, lambda *a: (enc_work(*a), ()), lambda *a: (dec_work(*a), ()), *operands
        )[:2]

    def encoder_start():
        qkv = product(sources, w["qkv"])
        att, inv, *weights = attend(
            source_lengths, *self_columns(qkv), w["prefix"], enc_segs, False
        )
        return (qkv, att, inv, weights), enc_ffn(sources, att, w, 2)

    (saved, part2), (cq, kept) = at_both(
        encoder_start, lambda: decoder_self(targets, target_lengths, w, cross)
    )
    mem2 = to_decoder(part2[0])
    part1 = at_encoder(lambda saved: enc_ffn(sources, saved[1], w, 1), saved)
    mem1 = to_decoder(part1[0])

    def decoder_short(saved, mem2, cq):
        kv2 = product(mem2, cross["pairs"])
        return kv2, cross_forward(source_lengths, cq, [kv2], 1)

    part0, (kv2, short) = at_both(
        lambda saved, mem2, cq: enc_ffn(sources, saved[1], w, 0), decoder_short, saved, mem2, cq
    )
    mem0 = to_decoder(part0[0])
    kv1 = at_decoder(lambda mem1: product(mem1, cross["pairs"]), mem1)

    def decoder_long(mem0, kv1, kv2, cq, kept):
        kvs = [product(mem0, cross["pairs"]), kv1, kv2]
        long = cross_forward(source_lengths, cq, kvs, 0)
        y, dsecond, dcatt, *adapter = dec_ffn(
            target_lengths, kept[4], long[0], cotangent, w, cross, 0
        )
        dcq, dck, dcv = cross_backward(cq, kvs, long, dcatt, 0)
        cuts = ((0, ENC_ROWS), (ENC_ROWS, ENC_ROWS), (2 * ENC_ROWS, SRC_LONG - 2 * ENC_ROWS))
        return back_product([dck, dcv], cross["pairs"], cuts=cuts), y, dsecond, dcq, adapter

    dmems, *long = at_decoder(decoder_long, mem0, kv1, kv2, cq, kept)
    dmem0, dmem1, dmem2 = [to_encoder(block) for block in dmems]

    def decoder_short_back(kv2, cq, kept, short):
        y, dsecond, dcatt, *adapter = dec_ffn(
            target_lengths, kept[4], short[0], cotangent, w, cross, 1
        )
        dcq, dck, dcv = cross_backward(cq, [kv2], short, dcatt, 1)
        return back_product([dck, dcv], cross["pairs"])[0], y, dsecond, dcq, adapter

    dmem_short, *short = at_decoder(decoder_short_back, kv2, cq, kept, short)
    dmem_short = to_encoder(dmem_short)

    def decoder_end(kept, long, short):
        y, dsecond, dcq = [jnp.concatenate([a, b], 0) for a, b in zip(long[:3], short[:3])]
        dt, dprefix = decoder_self_back(kept, dsecond, dcq, w, cross)
        adapter = jax.tree.map(jnp.add, long[3], short[3])
        highs = jnp.stack([y[:, half:], dt[:, half:]])
        return highs, jnp.stack([y[:, :half], dt[:, :half]]), dprefix, adapter

    highs, lows, dec_prefix, dec_adapter = at_decoder(decoder_end, kept, long, short)
    dmem0, lows = lax.optimization_barrier((dmem0, lows))
    back0 = at_encoder(lambda dmem0, part0: enc_ffn_back([dmem0], part0, w), dmem0, part0)
    back1 = at_encoder(lambda dmem1, part1: enc_ffn_back([dmem1], part1, w), dmem1, part1)

    def encoder_end(dmem2, dmem_short, part0, part1, part2, back0, back1, dec_adapter):
        back2 = enc_ffn_back([dmem2, dmem_short], part2, w)
        parts, backs = (part0, part1, part2), (back0, back1, back2)
        adapter = adapter_grads(
            [p[4] for p in parts], [p[3] for p in parts],
            [b[2] for b in backs], [b[3] for b in backs],
        )
        return back2, list(adapter)

    back2, _, adapter = on_section(
        is_encoder, encoder_end, lambda *a: ((), list(a[-1])),
        dmem2, dmem_short, part0, part1, part2, back0, back1, dec_adapter,
    )
    backs = (back0, back1, back2)
    source_grad, low, sums, small = finish(
        saved, [b[1] for b in backs], [b[0] for b in backs], w, adapter, dec_prefix, lows
    )
    target_halves = jnp.where(is_encoder, low, highs)
    sums = sums.astype(F32)
    return (
        target_halves[0],
        source_grad,
        target_halves[1],
        jnp.stack([small[:PRE], small[PRE_PAD : PRE_PAD + PRE]])[None],
        jnp.concatenate([sums[chunk:, :chunk], sums[chunk:, chunk:]], 0)[None],
        small[PRE + 1 : PRE + 2, :chunk],
        sums[None, :chunk],
        small[PRE : PRE + 1],
    )


def solution(mesh):
    layer2, layer3, rows = P("section", None), P("section", None, None), P("dp", None)
    return jax.shard_map(
        per_device,
        mesh=mesh,
        in_specs=(
            rows, rows, rows, rows, rows,
            layer3, layer3, layer3, layer3, layer3,
            P("section", None, None, None),
            layer3, layer2, layer3, layer2,
            P(), P(), P(), P(),
        ),
        out_specs=(
            P("dp", "section"), P("dp", "section"), P("dp", "section"),
            P("section", None, None, None), layer3, layer2, layer3, layer2,
        ),
        check_vma=False,
    )
```

```python
import functools

import jax
import jax.numpy as jnp
from jax import lax
from jax.experimental import pallas as pl
from jax.experimental.pallas import tpu as pltpu
from jax.sharding import PartitionSpec as P

HD = 64
PRE = 30
PRE_PAD = 32
SRC_LONG = 768
SRC_SHORT = 96
TGT = 256
LANES = 128

BF = jnp.bfloat16
F32 = jnp.float32
norm_eps = 1e-05
big_negative = -1e30
adapter_scale = 4.0
chunk = 512
wide = 1024
ENC_ROWS = (SRC_LONG + SRC_SHORT) // 3
vmem_bytes = 56 * 2**20

phi_poly = (
    0.797869713181688,
    0.036392283539041996,
    -8.782472977701046e-05,
    -3.669384069669515e-05,
    1.4250308145882202e-06,
)


def nn(left, right):
    return lax.dot_general(left, right, (((1,), (0,)), ((), ())), preferred_element_type=F32)


def nt(left, right):
    return lax.dot_general(left, right, (((1,), (1,)), ((), ())), preferred_element_type=F32)


def tn(left, right):
    return lax.dot_general(left, right, (((0,), (0,)), ((), ())), preferred_element_type=F32)


def gelu_pair(values):
    square = values * values
    poly = phi_poly[4]
    for coefficient in phi_poly[3::-1]:
        poly = poly * square + coefficient
    half = 0.5 * jnp.tanh(values * poly) + 0.5
    density = jnp.exp(square * -0.5) * 0.3989422804014327
    return values * half, half + values * density


def row_tiles(rows, most=288):
    count = -(-rows // most)
    size = rows // count
    return [(i * size, size) for i in range(count)]


def norm_rows(values):
    centered = values - jnp.mean(values, axis=-1, keepdims=True)
    scale = lax.rsqrt(jnp.mean(centered * centered, axis=-1, keepdims=True) + norm_eps)
    return centered * scale, scale


def norm_rows_back(hat, scale, grad_hat):
    mean_grad = jnp.mean(grad_hat, axis=-1, keepdims=True)
    mean_dot = jnp.mean(grad_hat * hat, axis=-1, keepdims=True)
    return scale * (grad_hat - mean_grad - hat * mean_dot)


def params(limit=vmem_bytes):
    return pltpu.CompilerParams(vmem_limit_bytes=limit)


def whole(shape):
    return pl.BlockSpec(shape, lambda *g: (0,) * len(shape))


def product_kernel(x_ref, w_ref, o_ref):
    o_ref[...] = nn(x_ref[...], w_ref[...]).astype(BF)


def product(x, w, tile=1024):
    rows, depth = x.shape
    width = w.shape[1]
    return pl.pallas_call(
        product_kernel,
        grid=(width // tile,),
        in_specs=[whole((rows, depth)), pl.BlockSpec((depth, tile), lambda i: (0, i))],
        out_specs=pl.BlockSpec((rows, tile), lambda i: (0, i)),
        out_shape=jax.ShapeDtypeStruct((rows, width), BF),
        compiler_params=params(),
        name="product",
    )(x, w)


def back_product_kernel(*refs, parts, residual, cuts):
    grads = refs[:parts]
    w_ref = refs[parts]
    outs = refs[-len(cuts) :]
    total = None
    width = grads[0].shape[1]
    for i, grad in enumerate(grads):
        term = nt(grad[...], w_ref[:, i * width : (i + 1) * width])
        total = term if total is None else total + term
    if residual:
        total = total + refs[parts + 1][...]
    for (start, size), o_ref in zip(cuts, outs):
        o_ref[...] = total[start : start + size].astype(BF)


def back_product(grads, w, residual=None, tile=512, cuts=None):
    rows, width = grads[0].shape
    depth = w.shape[0]
    parts = len(grads)
    cuts = cuts or ((0, rows),)
    specs = [whole((rows, width))] * parts + [
        pl.BlockSpec((tile, parts * width), lambda i: (i, 0))
    ]
    args = list(grads) + [w]
    if residual is not None:
        specs.append(pl.BlockSpec((rows, tile), lambda i: (0, i)))
        args.append(residual)
    return pl.pallas_call(
        functools.partial(
            back_product_kernel, parts=parts, residual=residual is not None, cuts=cuts
        ),
        grid=(depth // tile,),
        in_specs=specs,
        out_specs=[pl.BlockSpec((size, tile), lambda i: (0, i)) for _, size in cuts],
        out_shape=[jax.ShapeDtypeStruct((size, depth), BF) for _, size in cuts],
        compiler_params=params(),
        name="back_product",
    )(*args)


def head_lanes(head):
    lane = lax.broadcasted_iota(jnp.int32, (1, LANES), 1)
    own = (lane < HD) if head == 0 else (lane >= HD)
    first = HD if head == 0 else 0
    return own, lane == first, lane == first + 1


def bf(value):
    return jnp.asarray(value, BF)


def rows_of(refs, start, count):
    parts = []
    for ref in refs:
        size = ref.shape[0]
        low, high = max(start, 0), min(start + count, size)
        if low < high:
            parts.append(ref[low:high])
        start -= size
    return parts


def stacked(refs, prefix_ref, start, count):
    parts = rows_of(refs, start, count)
    if prefix_ref is not None:
        parts.append(prefix_ref[...])
    return parts[0] if len(parts) == 1 else jnp.concatenate(parts, 0)


def attend_pair(*refs, segs, prefix, causal, pieces, which):
    len_ref, q_ref = refs[:2]
    k_refs, v_refs = refs[2 : 2 + pieces], refs[2 + pieces : 2 + 2 * pieces]
    at = 2 + 2 * pieces
    pk_ref = pv_ref = None
    if prefix:
        pk_ref, pv_ref = refs[at : at + 2]
        at += 2
    o_ref, inv_ref = refs[at : at + 2]
    p_refs = refs[at + 2 :]
    for seg, (q0, nq, k0, nk) in enumerate(segs):
        keys = stacked(k_refs, pk_ref, k0, nk)
        values = stacked(v_refs, pv_ref, k0, nk)
        count = keys.shape[0]
        row = lax.broadcasted_iota(jnp.int32, (count, 1), 0)
        seen = row < jnp.minimum(len_ref[0, which + seg], nk)
        if prefix:
            seen = seen | ((row >= nk) & (row < nk + PRE))
        queries = q_ref[q0 : q0 + nq] * bf(HD**-0.5)
        out = inv = None
        for head in range(2):
            own, first, _ = head_lanes(head)
            k_own = jnp.where(own, keys, jnp.where(first & ~seen, bf(big_negative), bf(0)))
            q_own = jnp.where(own, queries, jnp.where(first, bf(1), bf(0)))
            v_own = jnp.where(own, values, bf(1))
            scores = nt(k_own, q_own)
            if causal:
                key_at = lax.broadcasted_iota(jnp.int32, scores.shape, 0)
                query_at = lax.broadcasted_iota(jnp.int32, scores.shape, 1)
                allowed = (key_at <= query_at) | (key_at >= nk)
                scores = jnp.where(allowed, scores, big_negative)
            peak = jnp.max(scores, axis=0, keepdims=True)
            weights = jnp.exp(scores - peak).astype(BF)
            p_refs[seg][head] = weights
            mixed = tn(weights, v_own)
            inverse = 1.0 / pltpu.roll(mixed, HD, 1)
            mixed = mixed * inverse
            out = mixed if out is None else jnp.where(own, mixed, out)
            inv = inverse if inv is None else jnp.where(own, inverse, inv)
        o_ref[q0 : q0 + nq] = out.astype(BF)
        inv_ref[q0 : q0 + nq] = inv


def lane_views(refs, group, j):
    views = []
    for ref in refs:
        if len(ref.shape) == 2:
            views.append(ref.at[:, j * LANES : (j + 1) * LANES])
        else:
            views.append(ref.at[2 * j : 2 * j + 2])
    return views


def attend_kernel(len_ref, *refs, group, **kw):
    for j in range(group):
        attend_pair(len_ref, *lane_views(refs, group, j), **kw)


def column_spec(rows, offset, row_block=0, group=1):
    return pl.BlockSpec((rows, group * LANES), lambda h: (row_block, h + offset // group))


def attend(lengths, q, keys, values, prefixes, segs, causal, which=0, group=1):
    pairs = 8
    q_rows = q[1]
    prefix = prefixes is not None
    extra = PRE_PAD if prefix else 0
    specs = [pl.BlockSpec(memory_space=pltpu.SMEM)]
    args = [lengths]
    for array, rows, block, offset in [q, *keys, *values]:
        specs.append(column_spec(rows, offset, block, group))
        args.append(array)
    if prefix:
        specs += [column_spec(PRE_PAD, 0, 0, group)] * 2
        args += list(prefixes)
    weight_shapes = [(2 * pairs, nk + extra, nq) for _, nq, _, nk in segs]
    return pl.pallas_call(
        functools.partial(
            attend_kernel, group=group, segs=segs, prefix=prefix, causal=causal, pieces=len(keys), which=which
        ),
        grid=(pairs // group,),
        in_specs=specs,
        out_specs=[column_spec(q_rows, 0, 0, group)] * 2
        + [pl.BlockSpec((2 * group,) + s[1:], lambda h: (h, 0, 0)) for s in weight_shapes],
        out_shape=[
            jax.ShapeDtypeStruct((q_rows, pairs * LANES), BF),
            jax.ShapeDtypeStruct((q_rows, pairs * LANES), F32),
        ]
        + [jax.ShapeDtypeStruct(s, BF) for s in weight_shapes],
        compiler_params=params(),
        name="attend",
    )(*args)


def attend_back_pair(
    q_ref, k_refs, v_refs, o_ref, inv_ref, g_refs, pk_ref, pv_ref, p_refs, dq_ref, dk_ref, dv_ref, segs
):
    prefix_totals = [None, None]
    scale = HD**-0.5
    for seg, (q0, nq, k0, nk) in enumerate(segs):
        keys = stacked(k_refs, pk_ref, k0, nk)
        values = stacked(v_refs, pv_ref, k0, nk)
        queries = q_ref[q0 : q0 + nq]
        grads = stacked(g_refs, None, q0, nq).astype(F32) * inv_ref[q0 : q0 + nq]
        grads_low = grads.astype(BF)
        dots = grads * o_ref[q0 : q0 + nq].astype(F32)
        dq = dk = dv = None
        for head in range(2):
            own, first, second = head_lanes(head)
            row_dot = -jnp.sum(jnp.where(own, dots, 0.0), axis=1, keepdims=True)
            high = row_dot.astype(BF)
            rest = (row_dot - high.astype(F32)).astype(BF)
            g_own = jnp.where(
                own, grads_low, jnp.where(first, high, jnp.where(second, rest, bf(0)))
            )
            v_own = jnp.where(own, values, jnp.where(first | second, bf(1), bf(0)))
            weights = p_refs[seg][head]
            score_grad = (weights.astype(F32) * nt(v_own, g_own)).astype(BF)
            dv_head = nn(weights, grads_low)
            dk_head = nn(score_grad, queries)
            dq_head = tn(score_grad, keys)
            dq = dq_head if dq is None else jnp.where(own, dq_head, dq)
            dk = dk_head if dk is None else jnp.where(own, dk_head, dk)
            dv = dv_head if dv is None else jnp.where(own, dv_head, dv)
        dk = dk * scale
        dq_ref[q0 : q0 + nq] = (dq * scale).astype(BF)
        at = k0 - segs[0][2]
        dk_ref[at : at + nk] = dk[:nk].astype(BF)
        dv_ref[at : at + nk] = dv[:nk].astype(BF)
        if pk_ref is not None:
            for i, grad in enumerate((dk, dv)):
                part = grad[nk:]
                prefix_totals[i] = part if seg == 0 else prefix_totals[i] + part
    return prefix_totals


def attend_back_kernel(*refs, group, **kw):
    for j in range(group):
        attend_back_views(*lane_views(refs, group, j), **kw)


def attend_back_views(*refs, segs, prefix, pieces):
    q_ref, o_ref, inv_ref, g_ref = refs[:4]
    k_refs, v_refs = refs[4 : 4 + pieces], refs[4 + pieces : 4 + 2 * pieces]
    at = 4 + 2 * pieces
    pk_ref = pv_ref = None
    if prefix:
        pk_ref, pv_ref = refs[at : at + 2]
        at += 2
    outs = refs[at + len(segs) :]
    totals = attend_back_pair(
        q_ref, k_refs, v_refs, o_ref, inv_ref, [g_ref], pk_ref, pv_ref,
        refs[at : at + len(segs)], *outs[:3], segs,
    )
    if prefix:
        outs[3][...] = totals[0]
        outs[4][...] = totals[1]


def attend_back(q, keys, values, prefixes, attended, inverse, grad, weights, segs, group=2):
    pairs = 8
    q_rows = q[1]
    k_rows = sum(nk for _, _, _, nk in segs)
    prefix = prefixes is not None
    specs, args = [], []
    own = [(a, q_rows, 0, 0) for a in (attended, inverse, grad)]
    for array, rows, block, offset in [q, *own, *keys, *values]:
        specs.append(column_spec(rows, offset, block, group))
        args.append(array)
    if prefix:
        specs += [column_spec(PRE_PAD, 0, 0, group)] * 2
        args += list(prefixes)
    specs += [pl.BlockSpec((2 * group,) + w.shape[1:], lambda h: (h, 0, 0)) for w in weights]
    args += list(weights)
    out_specs = [column_spec(n, 0, 0, group) for n in (q_rows, k_rows, k_rows)]
    out_shape = [
        jax.ShapeDtypeStruct((q_rows, pairs * LANES), BF),
        jax.ShapeDtypeStruct((k_rows, pairs * LANES), BF),
        jax.ShapeDtypeStruct((k_rows, pairs * LANES), BF),
    ]
    if prefix:
        out_specs += [column_spec(PRE_PAD, 0, 0, group)] * 2
        out_shape += [jax.ShapeDtypeStruct((PRE_PAD, pairs * LANES), F32)] * 2
    return pl.pallas_call(
        functools.partial(
            attend_back_kernel, group=group, segs=segs, prefix=prefix, pieces=len(keys)
        ),
        grid=(pairs // group,),
        in_specs=specs,
        out_specs=out_specs,
        out_shape=out_shape,
        compiler_params=params(),
        name="attend_back",
    )(*args)


def ffn_step(low_ref, acc_ref, in_ref, out_ref, slope_ref, act_ref, bias_ref, scale):
    for start, size in row_tiles(low_ref.shape[0]):
        rows = slice(start, start + size)
        hidden = nn(low_ref[rows], in_ref[...])
        if bias_ref is not None:
            hidden = hidden + bias_ref[...]
        active, slope = gelu_pair(hidden)
        slope_ref[rows] = slope.astype(BF)
        active = active.astype(BF)
        if act_ref is not None:
            act_ref[rows] = active
        term = nn(active, out_ref[...])
        acc_ref[rows] += term if scale is None else scale * term


def enc_ffn_kernel(
    x_ref, att_ref, wo_ref, gain_ref, in_ref, out_ref, down_ref, downb_ref, up_ref, upb_ref,
    mem_ref, slope_ref, pre_slope_ref, act_ref, low_ref, scales_ref, acc_ref,
):
    step = pl.program_id(0)
    last = pl.num_programs(0) - 1

    @pl.when(step == 0)
    def _():
        first = x_ref[...].astype(F32) + nn(att_ref[...], wo_ref[...])
        hat, scale = norm_rows(first)
        normed = hat * gain_ref[0:1]
        acc_ref[...] = normed
        low_ref[...] = normed.astype(BF)
        scales_ref[:, 0:1] = scale

    @pl.when((step > 0) & (step < last))
    def _():
        ffn_step(low_ref, acc_ref, in_ref, out_ref, slope_ref, None, None, None)

    @pl.when(step == last)
    def _():
        ffn_step(
            low_ref, acc_ref, down_ref, up_ref, pre_slope_ref, act_ref, downb_ref, adapter_scale
        )
        hat, scale = norm_rows(acc_ref[...] + adapter_scale * upb_ref[...])
        mem_ref[...] = (hat * gain_ref[1:2]).astype(BF)
        scales_ref[:, 1:2] = scale


def enc_ffn(x, att, w, part):
    width = x.shape[1]
    rows = ENC_ROWS
    hidden = w["ffn_in"].shape[1]
    steps = hidden // wide

    def at(i):
        return jnp.clip(i - 1, 0, steps - 1)

    return pl.pallas_call(
        enc_ffn_kernel,
        grid=(steps + 2,),
        in_specs=[
            pl.BlockSpec((rows, width), lambda i: (part, 0)),
            pl.BlockSpec((rows, width), lambda i: (part, 0)),
            whole((width, width)),
            whole((2, width)),
            pl.BlockSpec((width, wide), lambda i: (0, at(i))),
            pl.BlockSpec((wide, width), lambda i: (at(i), 0)),
            whole((width, chunk)),
            whole((1, chunk)),
            whole((chunk, width)),
            whole((1, width)),
        ],
        out_specs=[
            whole((rows, width)),
            pl.BlockSpec((rows, wide), lambda i: (0, at(i))),
            whole((rows, chunk)),
            whole((rows, chunk)),
            whole((rows, width)),
            whole((rows, LANES)),
        ],
        out_shape=[
            jax.ShapeDtypeStruct((rows, width), BF),
            jax.ShapeDtypeStruct((rows, hidden), BF),
            jax.ShapeDtypeStruct((rows, chunk), BF),
            jax.ShapeDtypeStruct((rows, chunk), BF),
            jax.ShapeDtypeStruct((rows, width), BF),
            jax.ShapeDtypeStruct((rows, LANES), F32),
        ],
        scratch_shapes=[pltpu.VMEM((rows, width), F32)],
        compiler_params=params(),
        name="enc_ffn",
    )(
        x, att, w["out"], w["gains"], w["ffn_in"], w["ffn_out"],
        w["down"], w["down_bias"], w["up"], w["up_bias"],
    )


def ffn_back_step(grad_ref, acc_ref, in_ref, out_ref, slope_ref):
    for start, size in row_tiles(grad_ref.shape[0]):
        rows = slice(start, start + size)
        pre = (nt(grad_ref[rows], out_ref[...]) * slope_ref[rows].astype(F32)).astype(BF)
        acc_ref[rows] += nt(pre, in_ref[...])


def adapter_back(grad_ref, acc_ref, low_ref, act_ref, slope_ref, down_ref, up_ref, outs, pre_ref):
    ddown_ref, ddownb_ref, dup_ref, dupb_ref = outs
    total = None
    for start, size in row_tiles(grad_ref.shape[0]):
        rows = slice(start, start + size)
        back = adapter_scale * nt(grad_ref[rows], up_ref[...])
        pre = (back * slope_ref[rows].astype(F32)).astype(BF)
        pre_ref[rows] = pre
        sums = jnp.sum(pre.astype(F32), axis=0, keepdims=True)
        total = sums if total is None else total + sums
        acc_ref[rows] += nt(pre, down_ref[...])
    ddownb_ref[...] = total
    ddown_ref[...] = tn(low_ref[...], pre_ref[...])
    dup_ref[...] = adapter_scale * tn(act_ref[...], grad_ref[...])
    dupb_ref[...] = adapter_scale * jnp.sum(grad_ref[...].astype(F32), axis=0, keepdims=True)


def enc_ffn_back_kernel(
    *refs, pieces,
):
    enc_ffn_back_body(refs[:pieces], *refs[pieces:])


def enc_ffn_back_body(
    dmem_refs, mem_ref, low_ref, scales_ref, gain_ref, slope_ref, pre_slope_ref,
    in_ref, out_ref, down_ref, up_ref, wo_ref,
    dfirst_ref, datt_ref, grad_ref, pre_ref,
    acc_ref,
):
    step = pl.program_id(0)
    last = pl.num_programs(0) - 1

    @pl.when(step == 0)
    def _():
        gain = gain_ref[1:2]
        hat = mem_ref[...].astype(F32) / gain
        grad = norm_rows_back(hat, scales_ref[:, 1:2], stacked(dmem_refs, None, 0, ENC_ROWS).astype(F32) * gain)
        low = grad.astype(BF)
        grad_ref[...] = low
        back = adapter_scale * nt(low, up_ref[...])
        pre = (back * pre_slope_ref[...].astype(F32)).astype(BF)
        pre_ref[...] = pre
        acc_ref[...] = grad + nt(pre, down_ref[...])

    ffn_back_step(grad_ref, acc_ref, in_ref, out_ref, slope_ref)

    @pl.when(step == last)
    def _():
        gain = gain_ref[0:1]
        hat = low_ref[...].astype(F32) / gain
        grad = norm_rows_back(hat, scales_ref[:, 0:1], acc_ref[...] * gain)
        dfirst_ref[...] = grad
        datt_ref[...] = nt(grad.astype(BF), wo_ref[...]).astype(BF)


def enc_ffn_back(dmems, saved, w):
    mem, slope, pre_slope, act, low, scales = saved
    rows, width = mem.shape
    hidden = w["ffn_in"].shape[1]
    steps = hidden // wide
    return pl.pallas_call(
        functools.partial(enc_ffn_back_kernel, pieces=len(dmems)),
        grid=(steps,),
        in_specs=[whole(d.shape) for d in dmems]
        + [
            whole((rows, width)),
            whole((rows, width)),
            whole((rows, LANES)),
            whole((2, width)),
            pl.BlockSpec((rows, wide), lambda i: (0, i)),
            whole((rows, chunk)),
            pl.BlockSpec((width, wide), lambda i: (0, i)),
            pl.BlockSpec((wide, width), lambda i: (i, 0)),
            whole((width, chunk)),
            whole((chunk, width)),
            whole((width, width)),
        ],
        out_specs=[
            whole((rows, width)),
            whole((rows, width)),
            whole((rows, width)),
            whole((rows, chunk)),
        ],
        out_shape=[
            jax.ShapeDtypeStruct((rows, width), F32),
            jax.ShapeDtypeStruct((rows, width), BF),
            jax.ShapeDtypeStruct((rows, width), BF),
            jax.ShapeDtypeStruct((rows, chunk), BF),
        ],
        scratch_shapes=[pltpu.VMEM((rows, width), F32)],
        compiler_params=params(),
        name="enc_ffn_back",
    )(
        *dmems, mem, low, scales, w["gains"], slope, pre_slope,
        w["ffn_in"], w["ffn_out"], w["down"], w["up"], w["out"],
    )


def adapter_grads_kernel(*refs, parts):
    groups = [refs[n * parts : (n + 1) * parts] for n in range(4)]
    low, act, grad, pre = [jnp.concatenate([r[...] for r in g], 0) for g in groups]
    ddown_ref, ddownb_ref, dup_ref, dupb_ref = refs[4 * parts :]
    ddown_ref[...] = tn(low, pre)
    ddownb_ref[...] = jnp.sum(pre.astype(F32), axis=0, keepdims=True)
    dup_ref[...] = adapter_scale * tn(act, grad)
    dupb_ref[...] = adapter_scale * jnp.sum(grad.astype(F32), axis=0, keepdims=True)


def adapter_grads(lows, acts, grads, pres):
    width = lows[0].shape[1]
    return pl.pallas_call(
        functools.partial(adapter_grads_kernel, parts=len(lows)),
        out_shape=[
            jax.ShapeDtypeStruct((width, chunk), F32),
            jax.ShapeDtypeStruct((1, chunk), F32),
            jax.ShapeDtypeStruct((chunk, width), F32),
            jax.ShapeDtypeStruct((1, width), F32),
        ],
        compiler_params=params(),
        name="adapter_grads",
    )(*lows, *acts, *grads, *pres)


def dec_mid_kernel(x_ref, att_ref, wo_ref, gain_ref, wq_ref, n_ref, scale_ref, cq_ref):
    for start, size in row_tiles(x_ref.shape[0], 256):
        rows = slice(start, start + size)
        first = x_ref[rows].astype(F32) + nn(att_ref[rows], wo_ref[...])
        hat, scale = norm_rows(first)
        normed = hat * gain_ref[0:1]
        n_ref[rows] = normed
        scale_ref[rows, 0:1] = scale
        cq_ref[rows] = nn(normed.astype(BF), wq_ref[...]).astype(BF)


def dec_mid(x, att, w, cross):
    rows, width = x.shape
    return pl.pallas_call(
        dec_mid_kernel,
        out_shape=[
            jax.ShapeDtypeStruct((rows, width), F32),
            jax.ShapeDtypeStruct((rows, LANES), F32),
            jax.ShapeDtypeStruct((rows, width), BF),
        ],
        compiler_params=params(),
        name="dec_mid",
    )(x, att, w["out"], w["gains"], cross["query"])


def dec_ffn_kernel(
    len_ref, n_ref, catt_ref, cot_ref, wco_ref, cgain_ref, gain_ref,
    in_ref, out_ref, down_ref, downb_ref, up_ref, upb_ref,
    y_ref, dsecond_ref, dcatt_ref, ddown_ref, ddownb_ref, dup_ref, dupb_ref,
    acc_ref, low_ref, grad_ref, slope_ref, pre_slope_ref, act_ref, pre_ref, scale_ref,
    *, steps, which,
):
    step = pl.program_id(0)
    tiles = row_tiles(n_ref.shape[0], TGT)

    @pl.when(step == 0)
    def _():
        for start, size in tiles:
            rows = slice(start, start + size)
            second = n_ref[rows] + nn(catt_ref[rows], wco_ref[...])
            hat, scale = norm_rows(second)
            middle = hat * cgain_ref[...]
            acc_ref[rows] = middle
            low_ref[rows] = middle.astype(BF)
            scale_ref[rows, 0:1] = scale

    @pl.when((step > 0) & (step <= steps))
    def _():
        ffn_step(low_ref, acc_ref, in_ref, out_ref, slope_ref.at[step - 1], None, None, None)

    @pl.when(step == steps + 1)
    def _():
        ffn_step(
            low_ref, acc_ref, down_ref, up_ref, pre_slope_ref, act_ref, downb_ref,
            adapter_scale,
        )
        for start, size in tiles:
            rows = slice(start, start + size)
            gain = gain_ref[1:2]
            hat, scale = norm_rows(acc_ref[rows] + adapter_scale * upb_ref[...])
            valid = lax.broadcasted_iota(jnp.int32, (size, 1), 0) < len_ref[0, which]
            y_ref[rows] = jnp.where(valid, hat * gain, 0.0).astype(BF)
            cot = jnp.where(valid, cot_ref[rows].astype(F32), 0.0)
            grad = norm_rows_back(hat, scale, cot * gain)
            acc_ref[rows] = grad
            grad_ref[rows] = grad.astype(BF)
        adapter_back(
            grad_ref, acc_ref, low_ref, act_ref, pre_slope_ref, down_ref, up_ref,
            (ddown_ref, ddownb_ref, dup_ref, dupb_ref), pre_ref,
        )

    @pl.when(step > steps + 1)
    def _():
        ffn_back_step(grad_ref, acc_ref, in_ref, out_ref, slope_ref.at[2 * steps + 1 - step])

    @pl.when(step == 2 * steps + 1)
    def _():
        for start, size in tiles:
            rows = slice(start, start + size)
            gain = cgain_ref[...]
            hat = low_ref[rows].astype(F32) / gain
            grad = norm_rows_back(hat, scale_ref[rows, 0:1], acc_ref[rows] * gain)
            dsecond_ref[rows] = grad
            dcatt_ref[rows] = nt(grad.astype(BF), wco_ref[...]).astype(BF)


def dec_ffn(lengths, n, catt, cot, w, cross, which):
    rows, width = catt.shape
    hidden = w["ffn_in"].shape[1]
    steps = hidden // wide

    def at(i):
        return jnp.where(i <= steps, jnp.clip(i - 1, 0, steps - 1), jnp.clip(2 * steps + 1 - i, 0, steps - 1))

    return pl.pallas_call(
        functools.partial(dec_ffn_kernel, steps=steps, which=which),
        grid=(2 * steps + 2,),
        in_specs=[
            pl.BlockSpec(memory_space=pltpu.SMEM),
            pl.BlockSpec((rows, width), lambda i: (which, 0)),
            whole((rows, width)),
            pl.BlockSpec((rows, width), lambda i: (which, 0)),
            whole((width, width)),
            whole((1, width)),
            whole((2, width)),
            pl.BlockSpec((width, wide), lambda i: (0, at(i))),
            pl.BlockSpec((wide, width), lambda i: (at(i), 0)),
            whole((width, chunk)),
            whole((1, chunk)),
            whole((chunk, width)),
            whole((1, width)),
        ],
        out_specs=[
            whole((rows, width)),
            whole((rows, width)),
            whole((rows, width)),
            whole((width, chunk)),
            whole((1, chunk)),
            whole((chunk, width)),
            whole((1, width)),
        ],
        out_shape=[
            jax.ShapeDtypeStruct((rows, width), BF),
            jax.ShapeDtypeStruct((rows, width), F32),
            jax.ShapeDtypeStruct((rows, width), BF),
            jax.ShapeDtypeStruct((width, chunk), F32),
            jax.ShapeDtypeStruct((1, chunk), F32),
            jax.ShapeDtypeStruct((chunk, width), F32),
            jax.ShapeDtypeStruct((1, width), F32),
        ],
        scratch_shapes=[
            pltpu.VMEM((rows, width), F32),
            pltpu.VMEM((rows, width), BF),
            pltpu.VMEM((rows, width), BF),
            pltpu.VMEM((steps, rows, wide), BF),
            pltpu.VMEM((rows, chunk), BF),
            pltpu.VMEM((rows, chunk), BF),
            pltpu.VMEM((rows, chunk), BF),
            pltpu.VMEM((rows, LANES), F32),
        ],
        compiler_params=params(),
        name="dec_ffn",
    )(
        lengths, n, catt, cot, cross["out"], cross["gain"], w["gains"],
        w["ffn_in"], w["ffn_out"], w["down"], w["down_bias"], w["up"], w["up_bias"],
    )


def dec_mid_back_kernel(
    dsecond0_ref, dsecond1_ref, dcq0_ref, dcq1_ref, wq_ref, n_ref, scale_ref, gain_ref, wo_ref,
    dfirst_ref, datt_ref,
):
    for pair, (dsecond_ref, dcq_ref) in enumerate(
        ((dsecond0_ref, dcq0_ref), (dsecond1_ref, dcq1_ref))
    ):
        rows = slice(pair * TGT, (pair + 1) * TGT)
        gain = gain_ref[0:1]
        total = dsecond_ref[...] + nt(dcq_ref[...], wq_ref[...])
        grad = norm_rows_back(n_ref[rows] / gain, scale_ref[rows, 0:1], total * gain)
        dfirst_ref[rows] = grad
        datt_ref[rows] = nt(grad.astype(BF), wo_ref[...]).astype(BF)


def dec_mid_back(dseconds, dcqs, n, scale, w, cross):
    rows, width = n.shape
    return pl.pallas_call(
        dec_mid_back_kernel,
        out_shape=[
            jax.ShapeDtypeStruct((rows, width), F32),
            jax.ShapeDtypeStruct((rows, width), BF),
        ],
        compiler_params=params(),
        name="dec_mid_back",
    )(*dseconds, *dcqs, cross["query"], n, scale, w["gains"], w["out"])


enc_segs = ((0, SRC_LONG, 0, SRC_LONG), (SRC_LONG, SRC_SHORT, SRC_LONG, SRC_SHORT))
dec_segs = ((0, TGT, 0, TGT), (TGT, TGT, TGT, TGT))
cross_segs = (((0, TGT, 0, SRC_LONG),), ((0, TGT, SRC_LONG % ENC_ROWS, SRC_SHORT),))


def self_columns(qkv):
    rows = qkv.shape[0]
    return (qkv, rows, 0, 0), [(qkv, rows, 0, 8)], [(qkv, rows, 0, 16)]


def cross_columns(cq, kvs, which):
    return (
        (cq, TGT, which, 0),
        [(kv, ENC_ROWS, 0, 0) for kv in kvs],
        [(kv, ENC_ROWS, 0, 8) for kv in kvs],
    )


def decoder_self(t, lengths, w, cross):
    qkv = product(t, w["qkv"])
    att, inv, *weights = attend(lengths, *self_columns(qkv), w["prefix"], dec_segs, True, group=2)
    n, scale, cq = dec_mid(t, att, w, cross)
    return cq, (qkv, att, inv, weights, n, scale)


def cross_forward(lengths, cq, kvs, which):
    return attend(
        lengths, *cross_columns(cq, kvs, which), None, cross_segs[which], False, which, group=2
    )


def cross_backward(cq, kvs, forward, dcatt, which):
    catt, inv, *weights = forward
    return attend_back(
        *cross_columns(cq, kvs, which), None, catt, inv, dcatt, weights, cross_segs[which]
    )


def decoder_self_back(kept, dseconds, dcqs, w, cross):
    qkv, att, inv, weights, n, scale = kept
    dfirst, datt = dec_mid_back(dseconds, dcqs, n, scale, w, cross)
    dq, dk, dv, *dprefix = attend_back(
        *self_columns(qkv), w["prefix"], att, inv, datt, weights, dec_segs
    )
    return back_product([dq, dk, dv], w["qkv"], dfirst)[0], dprefix


def small_shape(devices):
    return 8, 8 * (2 * chunk) // devices


def finish_kernel(
    q_ref, k_ref, v_ref, o_ref, inv_ref, g0_ref, g1_ref, g2_ref, pk_ref, pv_ref, pl_ref, ps_ref,
    dfirst0_ref, dfirst1_ref, dfirst2_ref, wqkv_ref,
    enc_down, enc_downb, enc_up, enc_upb, long_down, long_downb, long_up, long_upb,
    short_down, short_downb, short_up, short_upb, dpk_ref, dpv_ref,
    y0_ref, y1_ref, dt_ref,
    source_ref, y_ref, target_ref, o_sums_ref, o_small_ref,
    dq, dk, dv, small, ups, downs, mine, theirs, half_sum, across_y, y_sum, landed, total, result,
    small_landed, small_total, small_result, dx_low, dx_high, dx_landed, lows, lows_landed,
    load_sems, pair_sems, y_sems, z_sems, gather_sems, share_y_sems, back_sems,
    small_sems, share_sems, cross_sems,
    *, devices,
):
    step = pl.program_id(0)
    pairs = 8
    section = lax.axis_index("section")
    is_encoder = section == 0
    chips = devices // 2
    line = chips // 2
    slices = 16 // line
    rows = 2 * chunk
    half = rows // 2
    size = half // slices
    side = size // 2
    part = side // line
    place = lax.axis_index("dp")
    core, chip = lax.rem(place, 2), place // 2
    bit, at_line = lax.rem(chip, 2), chip // 2
    partner = place + 1 - 2 * core
    beside = place + 2 - 4 * bit
    small_rows, small_cols = small_shape(devices)
    tile = 256
    width = 2 * chunk
    scale = 1.0 / devices

    def aligned(value, unit=16):
        return pl.multiple_of(value, unit)

    def along(distance):
        return (lax.rem(at_line + distance, line) * 2 + bit) * 2 + core

    def remote(source, target, send_sem, recv_sem, other):
        return pltpu.make_async_remote_copy(
            src_ref=source, dst_ref=target, send_sem=send_sem, recv_sem=recv_sem,
            device_id=other, device_id_type=pl.DeviceIdType.MESH,
        )

    def in_group(other):
        return {"dp": other}

    across = {"section": 1 - section}
    kept = aligned(core * half)
    given = aligned((1 - core) * half)

    def swap():
        return remote(
            mine.at[pl.ds(given, half)], theirs, pair_sems.at[0], pair_sems.at[1],
            in_group(partner),
        )

    def y_send(j):
        there = pl.ds(aligned(j * size + (1 - bit) * side), side)
        return remote(
            half_sum.at[there], across_y.at[j], y_sems.at[0, j], y_sems.at[1, j], in_group(beside)
        )

    def z_send(j, s):
        there = pl.ds(aligned(lax.rem(at_line + s, line) * part), part)
        return remote(
            y_sum.at[j].at[there], landed.at[j, s - 1],
            z_sems.at[0, j, s - 1], z_sems.at[1, j, s - 1], in_group(along(s)),
        )

    def own_rows(j):
        return pl.ds(aligned(kept + j * size + bit * side + at_line * part), part)

    def own_side(j):
        return pl.ds(aligned(kept + j * size + bit * side), side)

    def other_side(j):
        return pl.ds(aligned(kept + j * size + (1 - bit) * side), side)

    def gather(j, s):
        return remote(
            total.at[j], result.at[own_rows(j)],
            gather_sems.at[0, j, s - 1], gather_sems.at[1, j, s - 1], in_group(along(s)),
        )

    def y_share(j):
        return remote(
            result.at[own_side(j)], result.at[own_side(j)],
            share_y_sems.at[0, j], share_y_sems.at[1, j], in_group(beside),
        )

    def back(j, i):
        there = own_side(j) if i == 0 else other_side(j)
        return remote(
            result.at[there], result.at[there],
            back_sems.at[0, j, i], back_sems.at[1, j, i], in_group(partner),
        )

    def piece(index):
        row = aligned(lax.rem(index, 8) * small_rows, 8)
        col = aligned((index // 8) * small_cols, LANES)
        return pl.ds(row, small_rows), pl.ds(col, small_cols)

    def small_out(s):
        return remote(
            small.at[piece(lax.rem(place + s, devices))], small_landed.at[s - 1],
            small_sems.at[0, s - 1], small_sems.at[1, s - 1],
            in_group(lax.rem(place + s, devices)),
        )

    def small_share(s):
        return remote(
            small_total, small_result.at[piece(place)],
            share_sems.at[0, s - 1], share_sems.at[1, s - 1],
            in_group(lax.rem(place + s, devices)),
        )

    def send_low():
        return remote(lows, lows_landed, cross_sems.at[0, 0], cross_sems.at[1, 0], across)

    def send_high(i):
        return remote(
            dx_high.at[i], dx_landed.at[i], cross_sems.at[0, 1 + i], cross_sems.at[1, 1 + i], across
        )

    def greet(barrier, other):
        pl.semaphore_signal(
            barrier, inc=1, device_id=other, device_id_type=pl.DeviceIdType.MESH
        )

    def load(source, target, i):
        return pltpu.make_async_copy(source, target, load_sems.at[i])

    @pl.when(step == 0)
    def _():
        barrier = pltpu.get_barrier_semaphore()
        for s in range(1, devices):
            greet(barrier, in_group(lax.rem(place + s, devices)))

        def pack(up, down):
            mine[0:chunk] = (up * scale).astype(BF)
            down = (down * scale).astype(BF)
            mine[chunk:width, 0:chunk] = down[0:chunk]
            mine[chunk:width, chunk:width] = down[chunk:width]

        @pl.when(is_encoder)
        def _():
            loads = [load(enc_up, ups.at[0], 0), load(enc_down, downs.at[0], 1)]
            for copy in loads:
                copy.start()
            for copy in loads:
                copy.wait()
            pack(ups[0], downs[0])
            pl.semaphore_wait(barrier, devices - 1)
            greet(barrier, across)

        @pl.when(jnp.logical_not(is_encoder))
        def _():
            loads = [
                load(long_up, ups.at[0], 0), load(long_down, downs.at[0], 1),
                load(short_up, ups.at[1], 2), load(short_down, downs.at[1], 3),
            ]
            for copy in loads:
                copy.start()
            for copy in loads:
                copy.wait()
            pack(ups[0] + ups[1], downs[0] + downs[1])
            pl.semaphore_wait(barrier, devices)
            greet(barrier, across)

        swap().start()

        @pl.when(jnp.logical_not(is_encoder))
        def _():
            low = width // 2
            lows[0, 0:TGT] = y0_ref[:, 0:low]
            lows[0, TGT : 2 * TGT] = y1_ref[:, 0:low]
            lows[1] = dt_ref[:, 0:low]
            send_low().start()
            small[0:PRE_PAD] = dpk_ref[...] * scale
            small[PRE_PAD : 2 * PRE_PAD] = dpv_ref[...] * scale

        swap().wait()
        half_sum[...] = (
            mine[pl.ds(kept, half)].astype(F32) + theirs[...].astype(F32)
        ).astype(BF)
        for j in range(slices):
            y_send(j).start()

    @pl.when(is_encoder & (step < pairs))
    def _():
        at = aligned(step * LANES, LANES)
        lanes = pl.ds(at, LANES)
        prefix_totals = attend_back_pair(
            q_ref, [k_ref], [v_ref], o_ref, inv_ref, [g0_ref, g1_ref, g2_ref], pk_ref, pv_ref,
            (pl_ref, ps_ref), dq.at[:, lanes], dk.at[:, lanes], dv.at[:, lanes], enc_segs,
        )
        small[0:PRE_PAD, lanes] = prefix_totals[0] * scale
        small[PRE_PAD : 2 * PRE_PAD, lanes] = prefix_totals[1] * scale

    for j in range(slices):

        @pl.when(step == j)
        def _(j=j):
            y_send(j).wait()
            own = pl.ds(aligned(j * size + bit * side), side)
            y_sum[j] = (half_sum[own].astype(F32) + across_y[j].astype(F32)).astype(BF)
            for s in range(1, line):
                z_send(j, s).start()

        @pl.when(step == j + 1)
        def _(j=j):
            summed = y_sum[j, pl.ds(aligned(at_line * part), part)].astype(F32)
            for s in range(1, line):
                z_send(j, s).wait()
                summed = summed + landed[j, s - 1].astype(F32)
            total[j] = summed.astype(BF)
            result[own_rows(j)] = total[j]
            for s in range(1, line):
                gather(j, s).start()

        @pl.when(step == j + 2)
        def _(j=j):
            for s in range(1, line):
                gather(j, s).wait()
            y_share(j).start()
            back(j, 0).start()

        @pl.when(step == j + 3)
        def _(j=j):
            y_share(j).wait()
            back(j, 1).start()

    @pl.when(step == pairs - 1)
    def _():
        @pl.when(is_encoder)
        def _():
            down_row = jnp.concatenate([enc_downb[...], jnp.zeros_like(enc_downb)], 1)
            small[PRE : PRE + 1] = enc_upb[...] * scale
            small[PRE + 1 : PRE + 2] = down_row * scale

        @pl.when(jnp.logical_not(is_encoder))
        def _():
            down_row = long_downb[...] + short_downb[...]
            down_row = jnp.concatenate([down_row, jnp.zeros_like(down_row)], 1)
            small[PRE : PRE + 1] = (long_upb[...] + short_upb[...]) * scale
            small[PRE + 1 : PRE + 2] = down_row * scale

        for s in range(1, devices):
            small_out(s).start()

    @pl.when(is_encoder & (step == pairs))
    def _():
        pl.semaphore_wait(pltpu.get_barrier_semaphore(), 1)

    for i in range(4):

        @pl.when(is_encoder & (step == pairs + i))
        def _(i=i):
            acc = jnp.concatenate([dfirst0_ref[...], dfirst1_ref[...], dfirst2_ref[...]], 0)
            for n, grad in enumerate((dq, dk, dv)):
                acc = acc + nt(grad[...], wqkv_ref[:, n * width : (n + 1) * width])
            if i < 2:
                dx_high[i] = acc.astype(BF)
                send_high(i).start()
            else:
                dx_low[:, (i - 2) * tile : (i - 1) * tile] = acc.astype(BF)

    @pl.when(step == pairs + 1)
    def _():
        own_rows_, own_cols = piece(place)
        summed = small[own_rows_, own_cols]
        for s in range(1, devices):
            small_out(s).wait()
            summed = summed + small_landed[s - 1]
        small_total[...] = summed
        small_result[own_rows_, own_cols] = summed
        for s in range(1, devices):
            small_share(s).start()

    @pl.when(step == pairs + 3)
    def _():
        for j in range(slices):
            for i in range(2):
                back(j, i).wait()
        o_sums_ref[...] = result[...]
        for s in range(1, devices):
            small_share(s).wait()
        o_small_ref[...] = small_result[...]

        @pl.when(is_encoder)
        def _():
            source_ref[...] = dx_low[...]
            send_low().wait_recv()
            y_ref[...] = lows_landed[0]
            target_ref[...] = lows_landed[1]
            for i in range(2):
                send_high(i).wait_send()

        @pl.when(jnp.logical_not(is_encoder))
        def _():
            low = width // 2
            y_ref[0:TGT] = y0_ref[:, low:width]
            y_ref[TGT : 2 * TGT] = y1_ref[:, low:width]
            target_ref[...] = dt_ref[:, low:width]
            send_low().wait_send()
            for i in range(2):
                send_high(i).wait_recv()
                source_ref[:, i * tile : (i + 1) * tile] = dx_landed[i]


def finish(saved, datts, dfirsts, w, adapters, dec_prefix, ys, dt):
    qkv, att, inv, weights = saved
    devices = lax.axis_size("dp")
    line = devices // 4
    slices = 16 // line
    rows, width = att.shape
    targets = dt.shape[0]
    pairs, tile = 8, 256
    half = width // 2
    side = half // slices // 2
    part = side // line
    small_rows, small_cols = small_shape(devices)

    def pair(offset):
        return pl.BlockSpec((rows, LANES), lambda i: (0, jnp.minimum(i, pairs - 1) + offset))

    def at(i):
        return jnp.where(i < pairs + 2, 2 + jnp.maximum(i - pairs, 0), i - pairs - 2)

    def once(shape):
        return pl.BlockSpec(shape, lambda i: (0,) * len(shape), pipeline_mode=pl.Buffered(1))

    anywhere = pl.BlockSpec(memory_space=pl.ANY)
    prefix_pair = pl.BlockSpec((PRE_PAD, LANES), lambda i: (0, jnp.minimum(i, pairs - 1)))
    vmem = pltpu.VMEM
    dma = pltpu.SemaphoreType.DMA
    flat = [a for group in adapters for a in group]
    return pl.pallas_call(
        functools.partial(finish_kernel, devices=devices),
        grid=(pairs + 4,),
        in_specs=[pair(0), pair(8), pair(16), pair(0), pair(0)]
        + [pl.BlockSpec((ENC_ROWS, LANES), lambda i: (0, jnp.minimum(i, pairs - 1)))] * 3
        + [prefix_pair] * 2
        + [
            pl.BlockSpec((2,) + p.shape[1:], lambda i: (jnp.minimum(i, pairs - 1), 0, 0))
            for p in weights
        ]
        + [
            pl.BlockSpec((ENC_ROWS, tile), lambda i: (0, at(i))),
        ]
        * 3
        + [
            pl.BlockSpec((tile, 3 * width), lambda i: (at(i), 0)),
        ]
        + [anywhere if a.shape[0] > 1 else once(a.shape) for a in flat]
        + [once(a.shape) for a in (*dec_prefix, *ys, dt)],
        out_specs=[
            once((rows, half)), once((targets, half)), once((targets, half)), once((width, width)),
            once((2 * PRE_PAD, width)),
        ],
        out_shape=[
            jax.ShapeDtypeStruct((rows, half), BF),
            jax.ShapeDtypeStruct((targets, half), BF),
            jax.ShapeDtypeStruct((targets, half), BF),
            jax.ShapeDtypeStruct((width, width), BF),
            jax.ShapeDtypeStruct((2 * PRE_PAD, width), F32),
        ],
        scratch_shapes=[
            vmem((rows, width), BF), vmem((rows, width), BF), vmem((rows, width), BF),
            vmem((2 * PRE_PAD, width), F32),
            vmem((2, chunk, width), F32), vmem((2, width, chunk), F32),
            vmem((width, width), BF), vmem((half, width), BF), vmem((half, width), BF),
            vmem((slices, side, width), BF), vmem((slices, side, width), BF),
            vmem((slices, line - 1, part, width), BF), vmem((slices, part, width), BF),
            vmem((width, width), BF),
            vmem((devices - 1, small_rows, small_cols), F32), vmem((small_rows, small_cols), F32),
            vmem((2 * PRE_PAD, width), F32),
            vmem((rows, half), BF), vmem((2, rows, tile), BF), vmem((2, rows, tile), BF),
            vmem((2, targets, half), BF), vmem((2, targets, half), BF),
            dma((4,)), dma((2,)), dma((2, slices)), dma((2, slices, line - 1)),
            dma((2, slices, line - 1)), dma((2, slices)), dma((2, slices, 2)),
            dma((2, devices - 1)), dma((2, devices - 1)), dma((2, 3)),
        ],
        compiler_params=pltpu.CompilerParams(
            vmem_limit_bytes=60 * 2**20, collective_id=0, has_side_effects=True
        ),
        name="finish",
    )(
        qkv, qkv, qkv, att, inv, *datts, *w["prefix"], *weights,
        *dfirsts, w["qkv"], *flat, *dec_prefix, *ys, dt,
    )


def blank_kernel(*refs):
    pass


def blanks(shapes):
    return pl.pallas_call(
        blank_kernel,
        out_shape=list(shapes),
        out_specs=[pl.BlockSpec(memory_space=pl.ANY)] * len(shapes),
        name="blank",
    )()


def on_section(is_encoder, encoder_work, decoder_work, *operands):
    enc_shapes, _ = jax.eval_shape(encoder_work, *operands)
    dec_shapes, _ = jax.eval_shape(decoder_work, *operands)

    def blank_like(shapes):
        leaves, tree = jax.tree.flatten(shapes)
        if not leaves:
            return shapes
        return jax.tree.unflatten(tree, blanks(leaves))

    def encoder_branch(*a):
        own, shared = encoder_work(*a)
        return own, blank_like(dec_shapes), shared

    def decoder_branch(*a):
        own, shared = decoder_work(*a)
        return blank_like(enc_shapes), own, shared

    return lax.cond(is_encoder, encoder_branch, decoder_branch, *operands)


def to_decoder(block):
    return lax.ppermute(block, "section", [(0, 1)])


def to_encoder(block):
    return lax.ppermute(block, "section", [(1, 0)])


def per_device(
    sources, targets, cotangent, source_lengths, target_lengths,
    attn_qkv, attn_out, ffn_in, ffn_out, norm_gains, prefix_pairs,
    adapt_down, adapt_down_bias, adapt_up, adapt_up_bias,
    cross_query, cross_pairs, cross_out, cross_gain,
):
    is_encoder = lax.axis_index("section") == 0
    prefix = jnp.pad(prefix_pairs[0], ((0, 0), (0, PRE_PAD - PRE), (0, 0)))
    w = dict(
        qkv=attn_qkv[0], out=attn_out[0], ffn_in=ffn_in[0], ffn_out=ffn_out[0],
        gains=norm_gains[0], prefix=(prefix[0], prefix[1]),
        down=adapt_down[0], down_bias=adapt_down_bias,
        up=adapt_up[0], up_bias=adapt_up_bias,
    )
    cross = dict(query=cross_query, pairs=cross_pairs, out=cross_out, gain=cross_gain[None])

    def at_encoder(work, *operands):
        return on_section(is_encoder, lambda *a: (work(*a), ()), lambda *a: ((), ()), *operands)[0]

    def at_decoder(work, *operands):
        return on_section(is_encoder, lambda *a: ((), ()), lambda *a: (work(*a), ()), *operands)[1]

    def at_both(enc_work, dec_work, *operands):
        return on_section(
            is_encoder, lambda *a: (enc_work(*a), ()), lambda *a: (dec_work(*a), ()), *operands
        )[:2]

    def encoder_start():
        qkv = product(sources, w["qkv"])
        att, inv, *weights = attend(
            source_lengths, *self_columns(qkv), w["prefix"], enc_segs, False
        )
        return (qkv, att, inv, weights), enc_ffn(sources, att, w, 2)

    (saved, part2), (cq, kept) = at_both(
        encoder_start, lambda: decoder_self(targets, target_lengths, w, cross)
    )
    mem2 = to_decoder(part2[0])
    part1 = at_encoder(lambda saved: enc_ffn(sources, saved[1], w, 1), saved)
    mem1 = to_decoder(part1[0])

    def decoder_short(saved, mem2, cq):
        kv2 = product(mem2, cross["pairs"])
        return kv2, cross_forward(source_lengths, cq, [kv2], 1)

    part0, (kv2, short) = at_both(
        lambda saved, mem2, cq: enc_ffn(sources, saved[1], w, 0), decoder_short, saved, mem2, cq
    )
    mem0 = to_decoder(part0[0])
    kv1 = at_decoder(lambda mem1: product(mem1, cross["pairs"]), mem1)

    def decoder_long(mem0, kv1, kv2, cq, kept):
        kvs = [product(mem0, cross["pairs"]), kv1, kv2]
        long = cross_forward(source_lengths, cq, kvs, 0)
        y, dsecond, dcatt, *adapter = dec_ffn(
            target_lengths, kept[4], long[0], cotangent, w, cross, 0
        )
        dcq, dck, dcv = cross_backward(cq, kvs, long, dcatt, 0)
        cuts = ((0, ENC_ROWS), (ENC_ROWS, ENC_ROWS), (2 * ENC_ROWS, SRC_LONG - 2 * ENC_ROWS))
        return back_product([dck, dcv], cross["pairs"], cuts=cuts), y, dsecond, dcq, adapter

    dmems, *long = at_decoder(decoder_long, mem0, kv1, kv2, cq, kept)
    dmem0, dmem1, dmem2 = [to_encoder(block) for block in dmems]

    def decoder_short_back(kv2, cq, kept, short):
        y, dsecond, dcatt, *adapter = dec_ffn(
            target_lengths, kept[4], short[0], cotangent, w, cross, 1
        )
        dcq, dck, dcv = cross_backward(cq, [kv2], short, dcatt, 1)
        return back_product([dck, dcv], cross["pairs"])[0], y, dsecond, dcq, adapter

    dmem_short, *short = at_decoder(decoder_short_back, kv2, cq, kept, short)
    dmem_short = to_encoder(dmem_short)

    def decoder_end(kept, *grads):
        return decoder_self_back(kept, grads[:2], grads[2:], w, cross)

    (long_y, long_second, long_cq, long_adapter) = long
    (short_y, short_second, short_cq, short_adapter) = short
    dt, dec_prefix = at_decoder(
        decoder_end, kept, long_second, short_second, long_cq, short_cq
    )
    dmem0, dt = lax.optimization_barrier((dmem0, dt))
    back0 = at_encoder(lambda dmem0, part0: enc_ffn_back([dmem0], part0, w), dmem0, part0)
    back1 = at_encoder(lambda dmem1, part1: enc_ffn_back([dmem1], part1, w), dmem1, part1)

    def encoder_end(dmem2, dmem_short, part0, part1, part2, back0, back1):
        back2 = enc_ffn_back([dmem2, dmem_short], part2, w)
        parts, backs = (part0, part1, part2), (back0, back1, back2)
        adapter = adapter_grads(
            [p[4] for p in parts], [p[3] for p in parts],
            [b[2] for b in backs], [b[3] for b in backs],
        )
        return back2, adapter

    back2, enc_adapter = at_encoder(
        encoder_end, dmem2, dmem_short, part0, part1, part2, back0, back1
    )
    backs = (back0, back1, back2)
    source_grad, y, target_grad, sums, small = finish(
        saved, [b[1] for b in backs], [b[0] for b in backs], w,
        [enc_adapter, long_adapter, short_adapter], dec_prefix, [long_y, short_y], dt,
    )
    sums = sums.astype(F32)
    return (
        y,
        source_grad,
        target_grad,
        jnp.stack([small[:PRE], small[PRE_PAD : PRE_PAD + PRE]])[None],
        jnp.concatenate([sums[chunk:, :chunk], sums[chunk:, chunk:]], 0)[None],
        small[PRE + 1 : PRE + 2, :chunk],
        sums[None, :chunk],
        small[PRE : PRE + 1],
    )


def solution(mesh):
    layer2, layer3, rows = P("section", None), P("section", None, None), P("dp", None)
    return jax.shard_map(
        per_device,
        mesh=mesh,
        in_specs=(
            rows, rows, rows, rows, rows,
            layer3, layer3, layer3, layer3, layer3,
            P("section", None, None, None),
            layer3, layer2, layer3, layer2,
            P(), P(), P(), P(),
        ),
        out_specs=(
            P("dp", "section"), P("dp", "section"), P("dp", "section"),
            P("section", None, None, None), layer3, layer2, layer3, layer2,
        ),
        check_vma=False,
    )
```

```python
import functools

import jax
import jax.numpy as jnp
from jax import lax
from jax.experimental import pallas as pl
from jax.experimental.pallas import tpu as pltpu
from jax.sharding import PartitionSpec as P

HD = 64
PRE = 30
PRE_PAD = 32
SRC_LONG = 768
SRC_SHORT = 96
TGT = 256
LANES = 128

BF = jnp.bfloat16
F32 = jnp.float32
norm_eps = 1e-05
big_negative = -1e30
adapter_scale = 4.0
chunk = 512
wide = 1024
ENC_ROWS = (SRC_LONG + SRC_SHORT) // 3
vmem_bytes = 56 * 2**20

phi_poly = (
    0.797869713181688,
    0.036392283539041996,
    -8.782472977701046e-05,
    -3.669384069669515e-05,
    1.4250308145882202e-06,
)


def nn(left, right):
    return lax.dot_general(left, right, (((1,), (0,)), ((), ())), preferred_element_type=F32)


def nt(left, right):
    return lax.dot_general(left, right, (((1,), (1,)), ((), ())), preferred_element_type=F32)


def tn(left, right):
    return lax.dot_general(left, right, (((0,), (0,)), ((), ())), preferred_element_type=F32)


def gelu_pair(values):
    square = values * values
    poly = phi_poly[4]
    for coefficient in phi_poly[3::-1]:
        poly = poly * square + coefficient
    half = 0.5 * jnp.tanh(values * poly) + 0.5
    density = jnp.exp(square * -0.5) * 0.3989422804014327
    return values * half, half + values * density


def row_tiles(rows, most=288):
    count = -(-rows // most)
    size = rows // count
    return [(i * size, size) for i in range(count)]


def norm_rows(values):
    centered = values - jnp.mean(values, axis=-1, keepdims=True)
    scale = lax.rsqrt(jnp.mean(centered * centered, axis=-1, keepdims=True) + norm_eps)
    return centered * scale, scale


def norm_rows_back(hat, scale, grad_hat):
    mean_grad = jnp.mean(grad_hat, axis=-1, keepdims=True)
    mean_dot = jnp.mean(grad_hat * hat, axis=-1, keepdims=True)
    return scale * (grad_hat - mean_grad - hat * mean_dot)


def params(limit=vmem_bytes):
    return pltpu.CompilerParams(vmem_limit_bytes=limit)


def whole(shape):
    return pl.BlockSpec(shape, lambda *g: (0,) * len(shape))


def product_kernel(x_ref, w_ref, o_ref):
    o_ref[...] = nn(x_ref[...], w_ref[...]).astype(BF)


def product(x, w, tile=1024):
    rows, depth = x.shape
    width = w.shape[1]
    return pl.pallas_call(
        product_kernel,
        grid=(width // tile,),
        in_specs=[whole((rows, depth)), pl.BlockSpec((depth, tile), lambda i: (0, i))],
        out_specs=pl.BlockSpec((rows, tile), lambda i: (0, i)),
        out_shape=jax.ShapeDtypeStruct((rows, width), BF),
        compiler_params=params(),
        name="product",
    )(x, w)


def back_product_kernel(*refs, parts, residual, cuts):
    grads = refs[:parts]
    w_ref = refs[parts]
    outs = refs[-len(cuts) :]
    total = None
    width = grads[0].shape[1]
    for i, grad in enumerate(grads):
        term = nt(grad[...], w_ref[:, i * width : (i + 1) * width])
        total = term if total is None else total + term
    if residual:
        total = total + refs[parts + 1][...]
    for (start, size), o_ref in zip(cuts, outs):
        o_ref[...] = total[start : start + size].astype(BF)


def back_product(grads, w, residual=None, tile=512, cuts=None):
    rows, width = grads[0].shape
    depth = w.shape[0]
    parts = len(grads)
    cuts = cuts or ((0, rows),)
    specs = [whole((rows, width))] * parts + [
        pl.BlockSpec((tile, parts * width), lambda i: (i, 0))
    ]
    args = list(grads) + [w]
    if residual is not None:
        specs.append(pl.BlockSpec((rows, tile), lambda i: (0, i)))
        args.append(residual)
    return pl.pallas_call(
        functools.partial(
            back_product_kernel, parts=parts, residual=residual is not None, cuts=cuts
        ),
        grid=(depth // tile,),
        in_specs=specs,
        out_specs=[pl.BlockSpec((size, tile), lambda i: (0, i)) for _, size in cuts],
        out_shape=[jax.ShapeDtypeStruct((size, depth), BF) for _, size in cuts],
        compiler_params=params(),
        name="back_product",
    )(*args)


def head_lanes(head):
    lane = lax.broadcasted_iota(jnp.int32, (1, LANES), 1)
    own = (lane < HD) if head == 0 else (lane >= HD)
    first = HD if head == 0 else 0
    return own, lane == first, lane == first + 1


def bf(value):
    return jnp.asarray(value, BF)


def rows_of(refs, start, count):
    parts = []
    for ref in refs:
        size = ref.shape[0]
        low, high = max(start, 0), min(start + count, size)
        if low < high:
            parts.append(ref[low:high])
        start -= size
    return parts


def stacked(refs, prefix_ref, start, count):
    parts = rows_of(refs, start, count)
    if prefix_ref is not None:
        parts.append(prefix_ref[...])
    return parts[0] if len(parts) == 1 else jnp.concatenate(parts, 0)


def attend_pair(*refs, segs, prefix, causal, pieces, which):
    len_ref, q_ref = refs[:2]
    k_refs, v_refs = refs[2 : 2 + pieces], refs[2 + pieces : 2 + 2 * pieces]
    at = 2 + 2 * pieces
    pk_ref = pv_ref = None
    if prefix:
        pk_ref, pv_ref = refs[at : at + 2]
        at += 2
    o_ref, inv_ref = refs[at : at + 2]
    p_refs = refs[at + 2 :]
    for seg, (q0, nq, k0, nk) in enumerate(segs):
        keys = stacked(k_refs, pk_ref, k0, nk)
        values = stacked(v_refs, pv_ref, k0, nk)
        count = keys.shape[0]
        row = lax.broadcasted_iota(jnp.int32, (count, 1), 0)
        seen = row < jnp.minimum(len_ref[0, which + seg], nk)
        if prefix:
            seen = seen | ((row >= nk) & (row < nk + PRE))
        queries = q_ref[q0 : q0 + nq] * bf(HD**-0.5)
        out = inv = None
        for head in range(2):
            own, first, _ = head_lanes(head)
            k_own = jnp.where(own, keys, jnp.where(first & ~seen, bf(big_negative), bf(0)))
            q_own = jnp.where(own, queries, jnp.where(first, bf(1), bf(0)))
            v_own = jnp.where(own, values, bf(1))
            scores = nt(k_own, q_own)
            if causal:
                key_at = lax.broadcasted_iota(jnp.int32, scores.shape, 0)
                query_at = lax.broadcasted_iota(jnp.int32, scores.shape, 1)
                allowed = (key_at <= query_at) | (key_at >= nk)
                scores = jnp.where(allowed, scores, big_negative)
            peak = jnp.max(scores, axis=0, keepdims=True)
            weights = jnp.exp(scores - peak).astype(BF)
            p_refs[seg][head] = weights
            mixed = tn(weights, v_own)
            inverse = 1.0 / pltpu.roll(mixed, HD, 1)
            mixed = mixed * inverse
            out = mixed if out is None else jnp.where(own, mixed, out)
            inv = inverse if inv is None else jnp.where(own, inverse, inv)
        o_ref[q0 : q0 + nq] = out.astype(BF)
        inv_ref[q0 : q0 + nq] = inv


def lane_views(refs, group, j):
    views = []
    for ref in refs:
        if len(ref.shape) == 2:
            views.append(ref.at[:, j * LANES : (j + 1) * LANES])
        else:
            views.append(ref.at[2 * j : 2 * j + 2])
    return views


def attend_kernel(len_ref, *refs, group, **kw):
    for j in range(group):
        attend_pair(len_ref, *lane_views(refs, group, j), **kw)


def column_spec(rows, offset, row_block=0, group=1):
    return pl.BlockSpec((rows, group * LANES), lambda h: (row_block, h + offset // group))


def attend(lengths, q, keys, values, prefixes, segs, causal, which=0, group=1):
    pairs = 8
    q_rows = q[1]
    prefix = prefixes is not None
    extra = PRE_PAD if prefix else 0
    specs = [pl.BlockSpec(memory_space=pltpu.SMEM)]
    args = [lengths]
    for array, rows, block, offset in [q, *keys, *values]:
        specs.append(column_spec(rows, offset, block, group))
        args.append(array)
    if prefix:
        specs += [column_spec(PRE_PAD, 0, 0, group)] * 2
        args += list(prefixes)
    weight_shapes = [(2 * pairs, nk + extra, nq) for _, nq, _, nk in segs]
    return pl.pallas_call(
        functools.partial(
            attend_kernel, group=group, segs=segs, prefix=prefix, causal=causal, pieces=len(keys), which=which
        ),
        grid=(pairs // group,),
        in_specs=specs,
        out_specs=[column_spec(q_rows, 0, 0, group)] * 2
        + [pl.BlockSpec((2 * group,) + s[1:], lambda h: (h, 0, 0)) for s in weight_shapes],
        out_shape=[
            jax.ShapeDtypeStruct((q_rows, pairs * LANES), BF),
            jax.ShapeDtypeStruct((q_rows, pairs * LANES), F32),
        ]
        + [jax.ShapeDtypeStruct(s, BF) for s in weight_shapes],
        compiler_params=params(),
        name="attend",
    )(*args)


def attend_back_pair(
    q_ref, k_refs, v_refs, o_ref, inv_ref, g_refs, pk_ref, pv_ref, p_refs, dq_ref, dk_ref, dv_ref, segs
):
    prefix_totals = [None, None]
    scale = HD**-0.5
    for seg, (q0, nq, k0, nk) in enumerate(segs):
        keys = stacked(k_refs, pk_ref, k0, nk)
        values = stacked(v_refs, pv_ref, k0, nk)
        queries = q_ref[q0 : q0 + nq]
        grads = stacked(g_refs, None, q0, nq).astype(F32) * inv_ref[q0 : q0 + nq]
        grads_low = grads.astype(BF)
        dots = grads * o_ref[q0 : q0 + nq].astype(F32)
        dq = dk = dv = None
        for head in range(2):
            own, first, second = head_lanes(head)
            row_dot = -jnp.sum(jnp.where(own, dots, 0.0), axis=1, keepdims=True)
            high = row_dot.astype(BF)
            rest = (row_dot - high.astype(F32)).astype(BF)
            g_own = jnp.where(
                own, grads_low, jnp.where(first, high, jnp.where(second, rest, bf(0)))
            )
            v_own = jnp.where(own, values, jnp.where(first | second, bf(1), bf(0)))
            weights = p_refs[seg][head]
            score_grad = (weights.astype(F32) * nt(v_own, g_own)).astype(BF)
            dv_head = nn(weights, grads_low)
            dk_head = nn(score_grad, queries)
            dq_head = tn(score_grad, keys)
            dq = dq_head if dq is None else jnp.where(own, dq_head, dq)
            dk = dk_head if dk is None else jnp.where(own, dk_head, dk)
            dv = dv_head if dv is None else jnp.where(own, dv_head, dv)
        dk = dk * scale
        dq_ref[q0 : q0 + nq] = (dq * scale).astype(BF)
        at = k0 - segs[0][2]
        dk_ref[at : at + nk] = dk[:nk].astype(BF)
        dv_ref[at : at + nk] = dv[:nk].astype(BF)
        if pk_ref is not None:
            for i, grad in enumerate((dk, dv)):
                part = grad[nk:]
                prefix_totals[i] = part if seg == 0 else prefix_totals[i] + part
    return prefix_totals


def attend_back_kernel(*refs, group, **kw):
    for j in range(group):
        attend_back_views(*lane_views(refs, group, j), **kw)


def attend_back_views(*refs, segs, prefix, pieces):
    q_ref, o_ref, inv_ref, g_ref = refs[:4]
    k_refs, v_refs = refs[4 : 4 + pieces], refs[4 + pieces : 4 + 2 * pieces]
    at = 4 + 2 * pieces
    pk_ref = pv_ref = None
    if prefix:
        pk_ref, pv_ref = refs[at : at + 2]
        at += 2
    outs = refs[at + len(segs) :]
    totals = attend_back_pair(
        q_ref, k_refs, v_refs, o_ref, inv_ref, [g_ref], pk_ref, pv_ref,
        refs[at : at + len(segs)], *outs[:3], segs,
    )
    if prefix:
        outs[3][...] = totals[0]
        outs[4][...] = totals[1]


def attend_back(q, keys, values, prefixes, attended, inverse, grad, weights, segs, group=2):
    pairs = 8
    q_rows = q[1]
    k_rows = sum(nk for _, _, _, nk in segs)
    prefix = prefixes is not None
    specs, args = [], []
    own = [(a, q_rows, 0, 0) for a in (attended, inverse, grad)]
    for array, rows, block, offset in [q, *own, *keys, *values]:
        specs.append(column_spec(rows, offset, block, group))
        args.append(array)
    if prefix:
        specs += [column_spec(PRE_PAD, 0, 0, group)] * 2
        args += list(prefixes)
    specs += [pl.BlockSpec((2 * group,) + w.shape[1:], lambda h: (h, 0, 0)) for w in weights]
    args += list(weights)
    out_specs = [column_spec(n, 0, 0, group) for n in (q_rows, k_rows, k_rows)]
    out_shape = [
        jax.ShapeDtypeStruct((q_rows, pairs * LANES), BF),
        jax.ShapeDtypeStruct((k_rows, pairs * LANES), BF),
        jax.ShapeDtypeStruct((k_rows, pairs * LANES), BF),
    ]
    if prefix:
        out_specs += [column_spec(PRE_PAD, 0, 0, group)] * 2
        out_shape += [jax.ShapeDtypeStruct((PRE_PAD, pairs * LANES), F32)] * 2
    return pl.pallas_call(
        functools.partial(
            attend_back_kernel, group=group, segs=segs, prefix=prefix, pieces=len(keys)
        ),
        grid=(pairs // group,),
        in_specs=specs,
        out_specs=out_specs,
        out_shape=out_shape,
        compiler_params=params(),
        name="attend_back",
    )(*args)


def ffn_step(low_ref, acc_ref, in_ref, out_ref, slope_ref, act_ref, bias_ref, scale):
    for start, size in row_tiles(low_ref.shape[0]):
        rows = slice(start, start + size)
        hidden = nn(low_ref[rows], in_ref[...])
        if bias_ref is not None:
            hidden = hidden + bias_ref[...]
        active, slope = gelu_pair(hidden)
        slope_ref[rows] = slope.astype(BF)
        active = active.astype(BF)
        if act_ref is not None:
            act_ref[rows] = active
        term = nn(active, out_ref[...])
        acc_ref[rows] += term if scale is None else scale * term


def enc_ffn_kernel(
    x_ref, att_ref, wo_ref, gain_ref, in_ref, out_ref, down_ref, downb_ref, up_ref, upb_ref,
    mem_ref, slope_ref, pre_slope_ref, act_ref, low_ref, scales_ref, acc_ref,
):
    step = pl.program_id(0)
    last = pl.num_programs(0) - 1

    @pl.when(step == 0)
    def _():
        first = x_ref[...].astype(F32) + nn(att_ref[...], wo_ref[...])
        hat, scale = norm_rows(first)
        normed = hat * gain_ref[0:1]
        acc_ref[...] = normed
        low_ref[...] = normed.astype(BF)
        scales_ref[:, 0:1] = scale

    @pl.when((step > 0) & (step < last))
    def _():
        ffn_step(low_ref, acc_ref, in_ref, out_ref, slope_ref, None, None, None)

    @pl.when(step == last)
    def _():
        ffn_step(
            low_ref, acc_ref, down_ref, up_ref, pre_slope_ref, act_ref, downb_ref, adapter_scale
        )
        hat, scale = norm_rows(acc_ref[...] + adapter_scale * upb_ref[...])
        mem_ref[...] = (hat * gain_ref[1:2]).astype(BF)
        scales_ref[:, 1:2] = scale


def enc_ffn(x, att, w, part):
    width = x.shape[1]
    rows = ENC_ROWS
    hidden = w["ffn_in"].shape[1]
    steps = hidden // wide

    def at(i):
        return jnp.clip(i - 1, 0, steps - 1)

    return pl.pallas_call(
        enc_ffn_kernel,
        grid=(steps + 2,),
        in_specs=[
            pl.BlockSpec((rows, width), lambda i: (part, 0)),
            pl.BlockSpec((rows, width), lambda i: (part, 0)),
            whole((width, width)),
            whole((2, width)),
            pl.BlockSpec((width, wide), lambda i: (0, at(i))),
            pl.BlockSpec((wide, width), lambda i: (at(i), 0)),
            whole((width, chunk)),
            whole((1, chunk)),
            whole((chunk, width)),
            whole((1, width)),
        ],
        out_specs=[
            whole((rows, width)),
            pl.BlockSpec((rows, wide), lambda i: (0, at(i))),
            whole((rows, chunk)),
            whole((rows, chunk)),
            whole((rows, width)),
            whole((rows, LANES)),
        ],
        out_shape=[
            jax.ShapeDtypeStruct((rows, width), BF),
            jax.ShapeDtypeStruct((rows, hidden), BF),
            jax.ShapeDtypeStruct((rows, chunk), BF),
            jax.ShapeDtypeStruct((rows, chunk), BF),
            jax.ShapeDtypeStruct((rows, width), BF),
            jax.ShapeDtypeStruct((rows, LANES), F32),
        ],
        scratch_shapes=[pltpu.VMEM((rows, width), F32)],
        compiler_params=params(),
        name="enc_ffn",
    )(
        x, att, w["out"], w["gains"], w["ffn_in"], w["ffn_out"],
        w["down"], w["down_bias"], w["up"], w["up_bias"],
    )


def ffn_back_step(grad_ref, acc_ref, in_ref, out_ref, slope_ref):
    for start, size in row_tiles(grad_ref.shape[0]):
        rows = slice(start, start + size)
        pre = (nt(grad_ref[rows], out_ref[...]) * slope_ref[rows].astype(F32)).astype(BF)
        acc_ref[rows] += nt(pre, in_ref[...])


def adapter_back(grad_ref, acc_ref, low_ref, act_ref, slope_ref, down_ref, up_ref, outs, pre_ref):
    ddown_ref, ddownb_ref, dup_ref, dupb_ref = outs
    total = None
    for start, size in row_tiles(grad_ref.shape[0]):
        rows = slice(start, start + size)
        back = adapter_scale * nt(grad_ref[rows], up_ref[...])
        pre = (back * slope_ref[rows].astype(F32)).astype(BF)
        pre_ref[rows] = pre
        sums = jnp.sum(pre.astype(F32), axis=0, keepdims=True)
        total = sums if total is None else total + sums
        acc_ref[rows] += nt(pre, down_ref[...])
    ddownb_ref[...] = total
    ddown_ref[...] = tn(low_ref[...], pre_ref[...])
    dup_ref[...] = adapter_scale * tn(act_ref[...], grad_ref[...])
    dupb_ref[...] = adapter_scale * jnp.sum(grad_ref[...].astype(F32), axis=0, keepdims=True)


def enc_ffn_back_kernel(
    *refs, pieces,
):
    enc_ffn_back_body(refs[:pieces], *refs[pieces:])


def enc_ffn_back_body(
    dmem_refs, mem_ref, low_ref, scales_ref, gain_ref, slope_ref, pre_slope_ref,
    in_ref, out_ref, down_ref, up_ref, wo_ref,
    dfirst_ref, datt_ref, grad_ref, pre_ref,
    acc_ref,
):
    step = pl.program_id(0)
    last = pl.num_programs(0) - 1

    @pl.when(step == 0)
    def _():
        gain = gain_ref[1:2]
        hat = mem_ref[...].astype(F32) / gain
        grad = norm_rows_back(hat, scales_ref[:, 1:2], stacked(dmem_refs, None, 0, ENC_ROWS).astype(F32) * gain)
        low = grad.astype(BF)
        grad_ref[...] = low
        back = adapter_scale * nt(low, up_ref[...])
        pre = (back * pre_slope_ref[...].astype(F32)).astype(BF)
        pre_ref[...] = pre
        acc_ref[...] = grad + nt(pre, down_ref[...])

    ffn_back_step(grad_ref, acc_ref, in_ref, out_ref, slope_ref)

    @pl.when(step == last)
    def _():
        gain = gain_ref[0:1]
        hat = low_ref[...].astype(F32) / gain
        grad = norm_rows_back(hat, scales_ref[:, 0:1], acc_ref[...] * gain)
        dfirst_ref[...] = grad
        datt_ref[...] = nt(grad.astype(BF), wo_ref[...]).astype(BF)


def enc_ffn_back(dmems, saved, w):
    mem, slope, pre_slope, act, low, scales = saved
    rows, width = mem.shape
    hidden = w["ffn_in"].shape[1]
    steps = hidden // wide
    return pl.pallas_call(
        functools.partial(enc_ffn_back_kernel, pieces=len(dmems)),
        grid=(steps,),
        in_specs=[whole(d.shape) for d in dmems]
        + [
            whole((rows, width)),
            whole((rows, width)),
            whole((rows, LANES)),
            whole((2, width)),
            pl.BlockSpec((rows, wide), lambda i: (0, i)),
            whole((rows, chunk)),
            pl.BlockSpec((width, wide), lambda i: (0, i)),
            pl.BlockSpec((wide, width), lambda i: (i, 0)),
            whole((width, chunk)),
            whole((chunk, width)),
            whole((width, width)),
        ],
        out_specs=[
            whole((rows, width)),
            whole((rows, width)),
            whole((rows, width)),
            whole((rows, chunk)),
        ],
        out_shape=[
            jax.ShapeDtypeStruct((rows, width), F32),
            jax.ShapeDtypeStruct((rows, width), BF),
            jax.ShapeDtypeStruct((rows, width), BF),
            jax.ShapeDtypeStruct((rows, chunk), BF),
        ],
        scratch_shapes=[pltpu.VMEM((rows, width), F32)],
        compiler_params=params(),
        name="enc_ffn_back",
    )(
        *dmems, mem, low, scales, w["gains"], slope, pre_slope,
        w["ffn_in"], w["ffn_out"], w["down"], w["up"], w["out"],
    )


def adapter_grads_kernel(*refs, parts):
    groups = [refs[n * parts : (n + 1) * parts] for n in range(4)]
    low, act, grad, pre = [jnp.concatenate([r[...] for r in g], 0) for g in groups]
    ddown_ref, ddownb_ref, dup_ref, dupb_ref = refs[4 * parts :]
    ddown_ref[...] = tn(low, pre)
    ddownb_ref[...] = jnp.sum(pre.astype(F32), axis=0, keepdims=True)
    dup_ref[...] = adapter_scale * tn(act, grad)
    dupb_ref[...] = adapter_scale * jnp.sum(grad.astype(F32), axis=0, keepdims=True)


def adapter_grads(lows, acts, grads, pres):
    width = lows[0].shape[1]
    return pl.pallas_call(
        functools.partial(adapter_grads_kernel, parts=len(lows)),
        out_shape=[
            jax.ShapeDtypeStruct((width, chunk), F32),
            jax.ShapeDtypeStruct((1, chunk), F32),
            jax.ShapeDtypeStruct((chunk, width), F32),
            jax.ShapeDtypeStruct((1, width), F32),
        ],
        compiler_params=params(),
        name="adapter_grads",
    )(*lows, *acts, *grads, *pres)


def dec_mid_kernel(x_ref, att_ref, wo_ref, gain_ref, wq_ref, n_ref, scale_ref, cq_ref):
    for start, size in row_tiles(x_ref.shape[0], 256):
        rows = slice(start, start + size)
        first = x_ref[rows].astype(F32) + nn(att_ref[rows], wo_ref[...])
        hat, scale = norm_rows(first)
        normed = hat * gain_ref[0:1]
        n_ref[rows] = normed
        scale_ref[rows, 0:1] = scale
        cq_ref[rows] = nn(normed.astype(BF), wq_ref[...]).astype(BF)


def dec_mid(x, att, w, cross):
    rows, width = x.shape
    return pl.pallas_call(
        dec_mid_kernel,
        out_shape=[
            jax.ShapeDtypeStruct((rows, width), F32),
            jax.ShapeDtypeStruct((rows, LANES), F32),
            jax.ShapeDtypeStruct((rows, width), BF),
        ],
        compiler_params=params(),
        name="dec_mid",
    )(x, att, w["out"], w["gains"], cross["query"])


def dec_ffn_kernel(
    len_ref, n_ref, catt_ref, cot_ref, wco_ref, cgain_ref, gain_ref,
    in_ref, out_ref, down_ref, downb_ref, up_ref, upb_ref,
    y_ref, dsecond_ref, dcatt_ref, ddown_ref, ddownb_ref, dup_ref, dupb_ref,
    acc_ref, low_ref, grad_ref, slope_ref, pre_slope_ref, act_ref, pre_ref, scale_ref,
    *, steps, which,
):
    step = pl.program_id(0)
    tiles = row_tiles(n_ref.shape[0], TGT)

    @pl.when(step == 0)
    def _():
        for start, size in tiles:
            rows = slice(start, start + size)
            second = n_ref[rows] + nn(catt_ref[rows], wco_ref[...])
            hat, scale = norm_rows(second)
            middle = hat * cgain_ref[...]
            acc_ref[rows] = middle
            low_ref[rows] = middle.astype(BF)
            scale_ref[rows, 0:1] = scale

    @pl.when((step > 0) & (step <= steps))
    def _():
        ffn_step(low_ref, acc_ref, in_ref, out_ref, slope_ref.at[step - 1], None, None, None)

    @pl.when(step == steps + 1)
    def _():
        ffn_step(
            low_ref, acc_ref, down_ref, up_ref, pre_slope_ref, act_ref, downb_ref,
            adapter_scale,
        )
        for start, size in tiles:
            rows = slice(start, start + size)
            gain = gain_ref[1:2]
            hat, scale = norm_rows(acc_ref[rows] + adapter_scale * upb_ref[...])
            valid = lax.broadcasted_iota(jnp.int32, (size, 1), 0) < len_ref[0, which]
            y_ref[rows] = jnp.where(valid, hat * gain, 0.0).astype(BF)
            cot = jnp.where(valid, cot_ref[rows].astype(F32), 0.0)
            grad = norm_rows_back(hat, scale, cot * gain)
            acc_ref[rows] = grad
            grad_ref[rows] = grad.astype(BF)
        adapter_back(
            grad_ref, acc_ref, low_ref, act_ref, pre_slope_ref, down_ref, up_ref,
            (ddown_ref, ddownb_ref, dup_ref, dupb_ref), pre_ref,
        )

    @pl.when(step > steps + 1)
    def _():
        ffn_back_step(grad_ref, acc_ref, in_ref, out_ref, slope_ref.at[2 * steps + 1 - step])

    @pl.when(step == 2 * steps + 1)
    def _():
        for start, size in tiles:
            rows = slice(start, start + size)
            gain = cgain_ref[...]
            hat = low_ref[rows].astype(F32) / gain
            grad = norm_rows_back(hat, scale_ref[rows, 0:1], acc_ref[rows] * gain)
            dsecond_ref[rows] = grad
            dcatt_ref[rows] = nt(grad.astype(BF), wco_ref[...]).astype(BF)


def dec_ffn(lengths, n, catt, cot, w, cross, which):
    rows, width = catt.shape
    hidden = w["ffn_in"].shape[1]
    steps = hidden // wide

    def at(i):
        return jnp.where(i <= steps, jnp.clip(i - 1, 0, steps - 1), jnp.clip(2 * steps + 1 - i, 0, steps - 1))

    return pl.pallas_call(
        functools.partial(dec_ffn_kernel, steps=steps, which=which),
        grid=(2 * steps + 2,),
        in_specs=[
            pl.BlockSpec(memory_space=pltpu.SMEM),
            pl.BlockSpec((rows, width), lambda i: (which, 0)),
            whole((rows, width)),
            pl.BlockSpec((rows, width), lambda i: (which, 0)),
            whole((width, width)),
            whole((1, width)),
            whole((2, width)),
            pl.BlockSpec((width, wide), lambda i: (0, at(i))),
            pl.BlockSpec((wide, width), lambda i: (at(i), 0)),
            whole((width, chunk)),
            whole((1, chunk)),
            whole((chunk, width)),
            whole((1, width)),
        ],
        out_specs=[
            whole((rows, width)),
            whole((rows, width)),
            whole((rows, width)),
            whole((width, chunk)),
            whole((1, chunk)),
            whole((chunk, width)),
            whole((1, width)),
        ],
        out_shape=[
            jax.ShapeDtypeStruct((rows, width), BF),
            jax.ShapeDtypeStruct((rows, width), F32),
            jax.ShapeDtypeStruct((rows, width), BF),
            jax.ShapeDtypeStruct((width, chunk), F32),
            jax.ShapeDtypeStruct((1, chunk), F32),
            jax.ShapeDtypeStruct((chunk, width), F32),
            jax.ShapeDtypeStruct((1, width), F32),
        ],
        scratch_shapes=[
            pltpu.VMEM((rows, width), F32),
            pltpu.VMEM((rows, width), BF),
            pltpu.VMEM((rows, width), BF),
            pltpu.VMEM((steps, rows, wide), BF),
            pltpu.VMEM((rows, chunk), BF),
            pltpu.VMEM((rows, chunk), BF),
            pltpu.VMEM((rows, chunk), BF),
            pltpu.VMEM((rows, LANES), F32),
        ],
        compiler_params=params(),
        name="dec_ffn",
    )(
        lengths, n, catt, cot, cross["out"], cross["gain"], w["gains"],
        w["ffn_in"], w["ffn_out"], w["down"], w["down_bias"], w["up"], w["up_bias"],
    )


def dec_mid_back_kernel(
    dsecond0_ref, dsecond1_ref, dcq0_ref, dcq1_ref, wq_ref, n_ref, scale_ref, gain_ref, wo_ref,
    dfirst_ref, datt_ref,
):
    for pair, (dsecond_ref, dcq_ref) in enumerate(
        ((dsecond0_ref, dcq0_ref), (dsecond1_ref, dcq1_ref))
    ):
        rows = slice(pair * TGT, (pair + 1) * TGT)
        gain = gain_ref[0:1]
        total = dsecond_ref[...] + nt(dcq_ref[...], wq_ref[...])
        grad = norm_rows_back(n_ref[rows] / gain, scale_ref[rows, 0:1], total * gain)
        dfirst_ref[rows] = grad
        datt_ref[rows] = nt(grad.astype(BF), wo_ref[...]).astype(BF)


def dec_mid_back(dseconds, dcqs, n, scale, w, cross):
    rows, width = n.shape
    return pl.pallas_call(
        dec_mid_back_kernel,
        out_shape=[
            jax.ShapeDtypeStruct((rows, width), F32),
            jax.ShapeDtypeStruct((rows, width), BF),
        ],
        compiler_params=params(),
        name="dec_mid_back",
    )(*dseconds, *dcqs, cross["query"], n, scale, w["gains"], w["out"])


enc_segs = ((0, SRC_LONG, 0, SRC_LONG), (SRC_LONG, SRC_SHORT, SRC_LONG, SRC_SHORT))
dec_segs = ((0, TGT, 0, TGT), (TGT, TGT, TGT, TGT))
cross_segs = (((0, TGT, 0, SRC_LONG),), ((0, TGT, SRC_LONG % ENC_ROWS, SRC_SHORT),))


def self_columns(qkv):
    rows = qkv.shape[0]
    return (qkv, rows, 0, 0), [(qkv, rows, 0, 8)], [(qkv, rows, 0, 16)]


def cross_columns(cq, kvs, which):
    return (
        (cq, TGT, which, 0),
        [(kv, ENC_ROWS, 0, 0) for kv in kvs],
        [(kv, ENC_ROWS, 0, 8) for kv in kvs],
    )


def decoder_self(t, lengths, w, cross):
    qkv = product(t, w["qkv"])
    att, inv, *weights = attend(lengths, *self_columns(qkv), w["prefix"], dec_segs, True, group=2)
    n, scale, cq = dec_mid(t, att, w, cross)
    return cq, (qkv, att, inv, weights, n, scale)


def cross_forward(lengths, cq, kvs, which):
    return attend(
        lengths, *cross_columns(cq, kvs, which), None, cross_segs[which], False, which, group=2
    )


def cross_backward(cq, kvs, forward, dcatt, which):
    catt, inv, *weights = forward
    return attend_back(
        *cross_columns(cq, kvs, which), None, catt, inv, dcatt, weights, cross_segs[which]
    )


def decoder_self_back(kept, dseconds, dcqs, w, cross):
    qkv, att, inv, weights, n, scale = kept
    dfirst, datt = dec_mid_back(dseconds, dcqs, n, scale, w, cross)
    dq, dk, dv, *dprefix = attend_back(
        *self_columns(qkv), w["prefix"], att, inv, datt, weights, dec_segs
    )
    return back_product([dq, dk, dv], w["qkv"], dfirst)[0], dprefix


def small_shape(devices):
    return 8, 8 * (2 * chunk) // devices


def finish_kernel(
    q_ref, k_ref, v_ref, o_ref, inv_ref, g0_ref, g1_ref, g2_ref, pk_ref, pv_ref, pl_ref, ps_ref,
    dfirst0_ref, dfirst1_ref, dfirst2_ref, wqkv_ref,
    enc_down, enc_downb, enc_up, enc_upb, long_down, long_downb, long_up, long_upb,
    short_down, short_downb, short_up, short_upb, dpk_ref, dpv_ref,
    y0_ref, y1_ref, dt_ref,
    source_ref, y_ref, target_ref, o_up_ref, o_down_ref, o_small_ref,
    dq, dk, dv, small, ups, downs, mine, theirs, half_sum, across_y, y_sum, landed, total, result,
    small_landed, small_total, small_result, dx_low, dx_high, dx_landed, lows, lows_landed,
    load_sems, pair_sems, y_sems, z_sems, gather_sems, share_y_sems, back_sems,
    small_sems, share_sems, cross_sems,
    *, devices,
):
    step = pl.program_id(0)
    pairs = 8
    section = lax.axis_index("section")
    is_encoder = section == 0
    chips = devices // 2
    line = chips // 2
    slices = 16 // line
    rows = 2 * chunk
    half = rows // 2
    size = half // slices
    side = size // 2
    part = side // line
    place = lax.axis_index("dp")
    core, chip = lax.rem(place, 2), place // 2
    bit, at_line = lax.rem(chip, 2), chip // 2
    partner = place + 1 - 2 * core
    beside = place + 2 - 4 * bit
    small_rows, small_cols = small_shape(devices)
    tile = 256
    width = 2 * chunk
    scale = 1.0 / devices

    def aligned(value, unit=16):
        return pl.multiple_of(value, unit)

    def along(distance):
        return (lax.rem(at_line + distance, line) * 2 + bit) * 2 + core

    def remote(source, target, send_sem, recv_sem, other):
        return pltpu.make_async_remote_copy(
            src_ref=source, dst_ref=target, send_sem=send_sem, recv_sem=recv_sem,
            device_id=other, device_id_type=pl.DeviceIdType.MESH,
        )

    def in_group(other):
        return {"dp": other}

    across = {"section": 1 - section}
    kept = aligned(core * half)
    given = aligned((1 - core) * half)

    def swap():
        return remote(
            mine.at[pl.ds(given, half)], theirs, pair_sems.at[0], pair_sems.at[1],
            in_group(partner),
        )

    def y_send(j):
        there = pl.ds(aligned(j * size + (1 - bit) * side), side)
        return remote(
            half_sum.at[there], across_y.at[j], y_sems.at[0, j], y_sems.at[1, j], in_group(beside)
        )

    def z_send(j, s):
        there = pl.ds(aligned(lax.rem(at_line + s, line) * part), part)
        return remote(
            y_sum.at[j].at[there], landed.at[j, s - 1],
            z_sems.at[0, j, s - 1], z_sems.at[1, j, s - 1], in_group(along(s)),
        )

    def own_rows(j):
        return pl.ds(aligned(kept + j * size + bit * side + at_line * part), part)

    def own_side(j):
        return pl.ds(aligned(kept + j * size + bit * side), side)

    def other_side(j):
        return pl.ds(aligned(kept + j * size + (1 - bit) * side), side)

    def gather(j, s):
        return remote(
            total.at[j], result.at[own_rows(j)],
            gather_sems.at[0, j, s - 1], gather_sems.at[1, j, s - 1], in_group(along(s)),
        )

    def y_share(j):
        return remote(
            result.at[own_side(j)], result.at[own_side(j)],
            share_y_sems.at[0, j], share_y_sems.at[1, j], in_group(beside),
        )

    def back(j, i):
        there = own_side(j) if i == 0 else other_side(j)
        return remote(
            result.at[there], result.at[there],
            back_sems.at[0, j, i], back_sems.at[1, j, i], in_group(partner),
        )

    def piece(index):
        row = aligned(lax.rem(index, 8) * small_rows, 8)
        col = aligned((index // 8) * small_cols, LANES)
        return pl.ds(row, small_rows), pl.ds(col, small_cols)

    def small_out(s):
        return remote(
            small.at[piece(lax.rem(place + s, devices))], small_landed.at[s - 1],
            small_sems.at[0, s - 1], small_sems.at[1, s - 1],
            in_group(lax.rem(place + s, devices)),
        )

    def small_share(s):
        return remote(
            small_total, small_result.at[piece(place)],
            share_sems.at[0, s - 1], share_sems.at[1, s - 1],
            in_group(lax.rem(place + s, devices)),
        )

    def send_low():
        return remote(lows, lows_landed, cross_sems.at[0, 0], cross_sems.at[1, 0], across)

    def send_high(i):
        return remote(
            dx_high.at[i], dx_landed.at[i], cross_sems.at[0, 1 + i], cross_sems.at[1, 1 + i], across
        )

    def greet(barrier, other):
        pl.semaphore_signal(
            barrier, inc=1, device_id=other, device_id_type=pl.DeviceIdType.MESH
        )

    def load(source, target, i):
        return pltpu.make_async_copy(source, target, load_sems.at[i])

    enc_loads = [load(enc_up, ups.at[0], 0), load(enc_down, downs.at[0], 1)]
    dec_loads = [
        load(long_up, ups.at[0], 0), load(long_down, downs.at[0], 1),
        load(short_up, ups.at[1], 2), load(short_down, downs.at[1], 3),
    ]

    @pl.when(step == 0)
    def _():
        barrier = pltpu.get_barrier_semaphore()
        for s in range(1, devices):
            greet(barrier, in_group(lax.rem(place + s, devices)))

        @pl.when(is_encoder)
        def _():
            for copy in enc_loads:
                copy.start()

        @pl.when(jnp.logical_not(is_encoder))
        def _():
            for copy in dec_loads:
                copy.start()

    @pl.when(is_encoder & (step < pairs))
    def _():
        at = aligned(step * LANES, LANES)
        lanes = pl.ds(at, LANES)
        prefix_totals = attend_back_pair(
            q_ref, [k_ref], [v_ref], o_ref, inv_ref, [g0_ref, g1_ref, g2_ref], pk_ref, pv_ref,
            (pl_ref, ps_ref), dq.at[:, lanes], dk.at[:, lanes], dv.at[:, lanes], enc_segs,
        )
        small[0:PRE_PAD, lanes] = prefix_totals[0] * scale
        small[PRE_PAD : 2 * PRE_PAD, lanes] = prefix_totals[1] * scale

    @pl.when(step == 0)
    def _():
        barrier = pltpu.get_barrier_semaphore()

        def pack(up, down):
            mine[0:chunk] = (up * scale).astype(BF)
            down = (down * scale).astype(BF)
            mine[chunk:width, 0:chunk] = down[0:chunk]
            mine[chunk:width, chunk:width] = down[chunk:width]

        @pl.when(is_encoder)
        def _():
            for copy in enc_loads:
                copy.wait()
            pack(ups[0], downs[0])
            pl.semaphore_wait(barrier, devices - 1)
            greet(barrier, across)

        @pl.when(jnp.logical_not(is_encoder))
        def _():
            for copy in dec_loads:
                copy.wait()
            pack(ups[0] + ups[1], downs[0] + downs[1])
            pl.semaphore_wait(barrier, devices)
            greet(barrier, across)

        swap().start()

        @pl.when(jnp.logical_not(is_encoder))
        def _():
            low = width // 2
            lows[0, 0:TGT] = y0_ref[:, 0:low]
            lows[0, TGT : 2 * TGT] = y1_ref[:, 0:low]
            lows[1] = dt_ref[:, 0:low]
            send_low().start()
            small[0:PRE_PAD] = dpk_ref[...] * scale
            small[PRE_PAD : 2 * PRE_PAD] = dpv_ref[...] * scale

    @pl.when(step == 1)
    def _():
        swap().wait()
        half_sum[...] = (
            mine[pl.ds(kept, half)].astype(F32) + theirs[...].astype(F32)
        ).astype(BF)
        for j in range(min(2, slices)):
            y_send(j).start()

    for j in range(slices):

        @pl.when(step == 2 + j)
        def _(j=j):
            y_send(j).wait()
            if j + 2 < slices:
                y_send(j + 2).start()
            own = pl.ds(aligned(j * size + bit * side), side)
            y_sum[j] = (half_sum[own].astype(F32) + across_y[j].astype(F32)).astype(BF)
            for s in range(1, line):
                z_send(j, s).start()

        @pl.when(step == 4 + j)
        def _(j=j):
            summed = y_sum[j, pl.ds(aligned(at_line * part), part)].astype(F32)
            for s in range(1, line):
                z_send(j, s).wait()
                summed = summed + landed[j, s - 1].astype(F32)
            total[j] = summed.astype(BF)
            result[own_rows(j)] = total[j]
            for s in range(1, line):
                gather(j, s).start()

        @pl.when(step == 6 + j)
        def _(j=j):
            for s in range(1, line):
                gather(j, s).wait()
            y_share(j).start()
            back(j, 0).start()

        @pl.when(step == 8 + j)
        def _(j=j):
            y_share(j).wait()
            back(j, 1).start()

    @pl.when(step == pairs - 1)
    def _():
        @pl.when(is_encoder)
        def _():
            down_row = jnp.concatenate([enc_downb[...], jnp.zeros_like(enc_downb)], 1)
            small[PRE : PRE + 1] = enc_upb[...] * scale
            small[PRE + 1 : PRE + 2] = down_row * scale

        @pl.when(jnp.logical_not(is_encoder))
        def _():
            down_row = long_downb[...] + short_downb[...]
            down_row = jnp.concatenate([down_row, jnp.zeros_like(down_row)], 1)
            small[PRE : PRE + 1] = (long_upb[...] + short_upb[...]) * scale
            small[PRE + 1 : PRE + 2] = down_row * scale

        for s in range(1, devices):
            small_out(s).start()

    @pl.when(is_encoder & (step == pairs))
    def _():
        pl.semaphore_wait(pltpu.get_barrier_semaphore(), 1)

    for i in range(4):

        @pl.when(is_encoder & (step == pairs + i))
        def _(i=i):
            acc = jnp.concatenate([dfirst0_ref[...], dfirst1_ref[...], dfirst2_ref[...]], 0)
            for n, grad in enumerate((dq, dk, dv)):
                acc = acc + nt(grad[...], wqkv_ref[:, n * width : (n + 1) * width])
            if i < 2:
                dx_high[i] = acc.astype(BF)
                send_high(i).start()
            else:
                dx_low[:, (i - 2) * tile : (i - 1) * tile] = acc.astype(BF)

    @pl.when(step == pairs + 1)
    def _():
        own_rows_, own_cols = piece(place)
        summed = small[own_rows_, own_cols]
        for s in range(1, devices):
            small_out(s).wait()
            summed = summed + small_landed[s - 1]
        small_total[...] = summed
        small_result[own_rows_, own_cols] = summed
        for s in range(1, devices):
            small_share(s).start()

    @pl.when(step == pairs + 3)
    def _():
        for j in range(slices):
            for i in range(2):
                back(j, i).wait()
        o_up_ref[...] = result[0:chunk]
        o_down_ref[0:chunk] = result[chunk:width, 0:chunk]
        o_down_ref[chunk:width] = result[chunk:width, chunk:width]
        for s in range(1, devices):
            small_share(s).wait()
        o_small_ref[...] = small_result[...]

        @pl.when(is_encoder)
        def _():
            source_ref[...] = dx_low[...]
            send_low().wait_recv()
            y_ref[...] = lows_landed[0]
            target_ref[...] = lows_landed[1]
            for i in range(2):
                send_high(i).wait_send()

        @pl.when(jnp.logical_not(is_encoder))
        def _():
            low = width // 2
            y_ref[0:TGT] = y0_ref[:, low:width]
            y_ref[TGT : 2 * TGT] = y1_ref[:, low:width]
            target_ref[...] = dt_ref[:, low:width]
            send_low().wait_send()
            for i in range(2):
                send_high(i).wait_recv()
                source_ref[:, i * tile : (i + 1) * tile] = dx_landed[i]


def finish(saved, datts, dfirsts, w, adapters, dec_prefix, ys, dt):
    qkv, att, inv, weights = saved
    devices = lax.axis_size("dp")
    line = devices // 4
    slices = 16 // line
    rows, width = att.shape
    targets = dt.shape[0]
    pairs, tile = 8, 256
    half = width // 2
    side = half // slices // 2
    part = side // line
    small_rows, small_cols = small_shape(devices)

    def mine(value):
        return jnp.where(lax.axis_index("section") == 0, value, 0)

    def head(i):
        return mine(jnp.minimum(i, pairs - 1))

    def pair(offset):
        return pl.BlockSpec((rows, LANES), lambda i: (0, head(i) + offset))

    def at(i):
        return mine(jnp.where(i < pairs + 2, 2 + jnp.maximum(i - pairs, 0), i - pairs - 2))

    def once(shape):
        return pl.BlockSpec(shape, lambda i: (0,) * len(shape), pipeline_mode=pl.Buffered(1))

    anywhere = pl.BlockSpec(memory_space=pl.ANY)
    prefix_pair = pl.BlockSpec((PRE_PAD, LANES), lambda i: (0, head(i)))
    vmem = pltpu.VMEM
    dma = pltpu.SemaphoreType.DMA
    flat = [a for group in adapters for a in group]
    return pl.pallas_call(
        functools.partial(finish_kernel, devices=devices),
        grid=(pairs + 4,),
        in_specs=[pair(0), pair(8), pair(16), pair(0), pair(0)]
        + [pl.BlockSpec((ENC_ROWS, LANES), lambda i: (0, head(i)))] * 3
        + [prefix_pair] * 2
        + [
            pl.BlockSpec((2,) + p.shape[1:], lambda i: (head(i), 0, 0))
            for p in weights
        ]
        + [
            pl.BlockSpec((ENC_ROWS, tile), lambda i: (0, at(i))),
        ]
        * 3
        + [
            pl.BlockSpec((tile, 3 * width), lambda i: (at(i), 0)),
        ]
        + [anywhere if a.shape[0] > 1 else once(a.shape) for a in flat]
        + [once(a.shape) for a in (*dec_prefix, *ys, dt)],
        out_specs=[
            once((rows, half)), once((targets, half)), once((targets, half)),
            once((chunk, width)), once((width, chunk)),
            once((2 * PRE_PAD, width)),
        ],
        out_shape=[
            jax.ShapeDtypeStruct((rows, half), BF),
            jax.ShapeDtypeStruct((targets, half), BF),
            jax.ShapeDtypeStruct((targets, half), BF),
            jax.ShapeDtypeStruct((chunk, width), BF),
            jax.ShapeDtypeStruct((width, chunk), BF),
            jax.ShapeDtypeStruct((2 * PRE_PAD, width), F32),
        ],
        scratch_shapes=[
            vmem((rows, width), BF), vmem((rows, width), BF), vmem((rows, width), BF),
            vmem((2 * PRE_PAD, width), F32),
            vmem((2, chunk, width), F32), vmem((2, width, chunk), F32),
            vmem((width, width), BF), vmem((half, width), BF), vmem((half, width), BF),
            vmem((slices, side, width), BF), vmem((slices, side, width), BF),
            vmem((slices, line - 1, part, width), BF), vmem((slices, part, width), BF),
            vmem((width, width), BF),
            vmem((devices - 1, small_rows, small_cols), F32), vmem((small_rows, small_cols), F32),
            vmem((2 * PRE_PAD, width), F32),
            vmem((rows, half), BF), vmem((2, rows, tile), BF), vmem((2, rows, tile), BF),
            vmem((2, targets, half), BF), vmem((2, targets, half), BF),
            dma((4,)), dma((2,)), dma((2, slices)), dma((2, slices, line - 1)),
            dma((2, slices, line - 1)), dma((2, slices)), dma((2, slices, 2)),
            dma((2, devices - 1)), dma((2, devices - 1)), dma((2, 3)),
        ],
        compiler_params=pltpu.CompilerParams(
            vmem_limit_bytes=60 * 2**20, collective_id=0, has_side_effects=True
        ),
        name="finish",
    )(
        qkv, qkv, qkv, att, inv, *datts, *w["prefix"], *weights,
        *dfirsts, w["qkv"], *flat, *dec_prefix, *ys, dt,
    )


def blank_kernel(*refs):
    pass


def blanks(shapes):
    return pl.pallas_call(
        blank_kernel,
        out_shape=list(shapes),
        out_specs=[pl.BlockSpec(memory_space=pl.ANY)] * len(shapes),
        name="blank",
    )()


def on_section(is_encoder, encoder_work, decoder_work, *operands):
    enc_shapes, _ = jax.eval_shape(encoder_work, *operands)
    dec_shapes, _ = jax.eval_shape(decoder_work, *operands)

    def blank_like(shapes):
        leaves, tree = jax.tree.flatten(shapes)
        if not leaves:
            return shapes
        return jax.tree.unflatten(tree, blanks(leaves))

    def encoder_branch(*a):
        own, shared = encoder_work(*a)
        return own, blank_like(dec_shapes), shared

    def decoder_branch(*a):
        own, shared = decoder_work(*a)
        return blank_like(enc_shapes), own, shared

    return lax.cond(is_encoder, encoder_branch, decoder_branch, *operands)


def to_decoder(block):
    return lax.ppermute(block, "section", [(0, 1)])


def to_encoder(block):
    return lax.ppermute(block, "section", [(1, 0)])


def per_device(
    sources, targets, cotangent, source_lengths, target_lengths,
    attn_qkv, attn_out, ffn_in, ffn_out, norm_gains, prefix_pairs,
    adapt_down, adapt_down_bias, adapt_up, adapt_up_bias,
    cross_query, cross_pairs, cross_out, cross_gain,
):
    is_encoder = lax.axis_index("section") == 0
    prefix = jnp.pad(prefix_pairs[0], ((0, 0), (0, PRE_PAD - PRE), (0, 0)))
    w = dict(
        qkv=attn_qkv[0], out=attn_out[0], ffn_in=ffn_in[0], ffn_out=ffn_out[0],
        gains=norm_gains[0], prefix=(prefix[0], prefix[1]),
        down=adapt_down[0], down_bias=adapt_down_bias,
        up=adapt_up[0], up_bias=adapt_up_bias,
    )
    cross = dict(query=cross_query, pairs=cross_pairs, out=cross_out, gain=cross_gain[None])

    def at_encoder(work, *operands):
        return on_section(is_encoder, lambda *a: (work(*a), ()), lambda *a: ((), ()), *operands)[0]

    def at_decoder(work, *operands):
        return on_section(is_encoder, lambda *a: ((), ()), lambda *a: (work(*a), ()), *operands)[1]

    def at_both(enc_work, dec_work, *operands):
        return on_section(
            is_encoder, lambda *a: (enc_work(*a), ()), lambda *a: (dec_work(*a), ()), *operands
        )[:2]

    def encoder_start():
        qkv = product(sources, w["qkv"])
        att, inv, *weights = attend(
            source_lengths, *self_columns(qkv), w["prefix"], enc_segs, False
        )
        return (qkv, att, inv, weights), enc_ffn(sources, att, w, 2)

    (saved, part2), (cq, kept) = at_both(
        encoder_start, lambda: decoder_self(targets, target_lengths, w, cross)
    )
    mem2 = to_decoder(part2[0])
    part1 = at_encoder(lambda saved: enc_ffn(sources, saved[1], w, 1), saved)
    mem1 = to_decoder(part1[0])

    def decoder_short(saved, mem2, cq):
        kv2 = product(mem2, cross["pairs"])
        return kv2, cross_forward(source_lengths, cq, [kv2], 1)

    part0, (kv2, short) = at_both(
        lambda saved, mem2, cq: enc_ffn(sources, saved[1], w, 0), decoder_short, saved, mem2, cq
    )
    mem0 = to_decoder(part0[0])
    kv1 = at_decoder(lambda mem1: product(mem1, cross["pairs"]), mem1)

    def decoder_long(mem0, kv1, kv2, cq, kept):
        kvs = [product(mem0, cross["pairs"]), kv1, kv2]
        long = cross_forward(source_lengths, cq, kvs, 0)
        y, dsecond, dcatt, *adapter = dec_ffn(
            target_lengths, kept[4], long[0], cotangent, w, cross, 0
        )
        dcq, dck, dcv = cross_backward(cq, kvs, long, dcatt, 0)
        cuts = ((0, ENC_ROWS), (ENC_ROWS, ENC_ROWS), (2 * ENC_ROWS, SRC_LONG - 2 * ENC_ROWS))
        return back_product([dck, dcv], cross["pairs"], cuts=cuts), y, dsecond, dcq, adapter

    dmems, *long = at_decoder(decoder_long, mem0, kv1, kv2, cq, kept)
    dmem0, dmem1, dmem2 = [to_encoder(block) for block in dmems]

    def decoder_short_back(kv2, cq, kept, short):
        y, dsecond, dcatt, *adapter = dec_ffn(
            target_lengths, kept[4], short[0], cotangent, w, cross, 1
        )
        dcq, dck, dcv = cross_backward(cq, [kv2], short, dcatt, 1)
        return back_product([dck, dcv], cross["pairs"])[0], y, dsecond, dcq, adapter

    dmem_short, *short = at_decoder(decoder_short_back, kv2, cq, kept, short)
    dmem_short = to_encoder(dmem_short)

    def decoder_end(kept, *grads):
        return decoder_self_back(kept, grads[:2], grads[2:], w, cross)

    (long_y, long_second, long_cq, long_adapter) = long
    (short_y, short_second, short_cq, short_adapter) = short
    dt, dec_prefix = at_decoder(
        decoder_end, kept, long_second, short_second, long_cq, short_cq
    )
    dmem0, dt = lax.optimization_barrier((dmem0, dt))
    back0 = at_encoder(lambda dmem0, part0: enc_ffn_back([dmem0], part0, w), dmem0, part0)
    back1 = at_encoder(lambda dmem1, part1: enc_ffn_back([dmem1], part1, w), dmem1, part1)

    def encoder_end(dmem2, dmem_short, part0, part1, part2, back0, back1):
        back2 = enc_ffn_back([dmem2, dmem_short], part2, w)
        parts, backs = (part0, part1, part2), (back0, back1, back2)
        adapter = adapter_grads(
            [p[4] for p in parts], [p[3] for p in parts],
            [b[2] for b in backs], [b[3] for b in backs],
        )
        return back2, adapter

    back2, enc_adapter = at_encoder(
        encoder_end, dmem2, dmem_short, part0, part1, part2, back0, back1
    )
    backs = (back0, back1, back2)
    source_grad, y, target_grad, up, down, small = finish(
        saved, [b[1] for b in backs], [b[0] for b in backs], w,
        [enc_adapter, long_adapter, short_adapter], dec_prefix, [long_y, short_y], dt,
    )
    return (
        y,
        source_grad,
        target_grad,
        jnp.stack([small[:PRE], small[PRE_PAD : PRE_PAD + PRE]])[None],
        down.astype(F32)[None],
        small[PRE + 1 : PRE + 2, :chunk],
        up.astype(F32)[None],
        small[PRE : PRE + 1],
    )


def solution(mesh):
    layer2, layer3, rows = P("section", None), P("section", None, None), P("dp", None)
    return jax.shard_map(
        per_device,
        mesh=mesh,
        in_specs=(
            rows, rows, rows, rows, rows,
            layer3, layer3, layer3, layer3, layer3,
            P("section", None, None, None),
            layer3, layer2, layer3, layer2,
            P(), P(), P(), P(),
        ),
        out_specs=(
            P("dp", "section"), P("dp", "section"), P("dp", "section"),
            P("section", None, None, None), layer3, layer2, layer3, layer2,
        ),
        check_vma=False,
    )
```

```python
import functools

import jax
import jax.numpy as jnp
from jax import lax
from jax.experimental import pallas as pl
from jax.experimental.pallas import tpu as pltpu
from jax.sharding import PartitionSpec as P

HD = 64
PRE = 30
PRE_PAD = 32
SRC_LONG = 768
SRC_SHORT = 96
TGT = 256
LANES = 128

BF = jnp.bfloat16
F32 = jnp.float32
norm_eps = 1e-05
big_negative = -1e30
adapter_scale = 4.0
chunk = 512
wide = 1024
ENC_ROWS = (SRC_LONG + SRC_SHORT) // 3
vmem_bytes = 56 * 2**20

phi_poly = (
    0.797869713181688,
    0.036392283539041996,
    -8.782472977701046e-05,
    -3.669384069669515e-05,
    1.4250308145882202e-06,
)


def nn(left, right):
    return lax.dot_general(left, right, (((1,), (0,)), ((), ())), preferred_element_type=F32)


def nt(left, right):
    return lax.dot_general(left, right, (((1,), (1,)), ((), ())), preferred_element_type=F32)


def tn(left, right):
    return lax.dot_general(left, right, (((0,), (0,)), ((), ())), preferred_element_type=F32)


def gelu_pair(values):
    square = values * values
    poly = phi_poly[4]
    for coefficient in phi_poly[3::-1]:
        poly = poly * square + coefficient
    half = 0.5 * jnp.tanh(values * poly) + 0.5
    density = jnp.exp(square * -0.5) * 0.3989422804014327
    return values * half, half + values * density


def row_tiles(rows, most=288):
    count = -(-rows // most)
    size = rows // count
    return [(i * size, size) for i in range(count)]


def norm_rows(values):
    centered = values - jnp.mean(values, axis=-1, keepdims=True)
    scale = lax.rsqrt(jnp.mean(centered * centered, axis=-1, keepdims=True) + norm_eps)
    return centered * scale, scale


def norm_rows_back(hat, scale, grad_hat):
    mean_grad = jnp.mean(grad_hat, axis=-1, keepdims=True)
    mean_dot = jnp.mean(grad_hat * hat, axis=-1, keepdims=True)
    return scale * (grad_hat - mean_grad - hat * mean_dot)


def params(limit=vmem_bytes):
    return pltpu.CompilerParams(vmem_limit_bytes=limit)


def whole(shape):
    return pl.BlockSpec(shape, lambda *g: (0,) * len(shape))


def product_kernel(x_ref, w_ref, o_ref):
    o_ref[...] = nn(x_ref[...], w_ref[...]).astype(BF)


def product(x, w, tile=1024):
    rows, depth = x.shape
    width = w.shape[1]
    return pl.pallas_call(
        product_kernel,
        grid=(width // tile,),
        in_specs=[whole((rows, depth)), pl.BlockSpec((depth, tile), lambda i: (0, i))],
        out_specs=pl.BlockSpec((rows, tile), lambda i: (0, i)),
        out_shape=jax.ShapeDtypeStruct((rows, width), BF),
        compiler_params=params(),
        name="product",
    )(x, w)


def back_product_kernel(*refs, parts, residual, cuts):
    grads = refs[:parts]
    w_ref = refs[parts]
    outs = refs[-len(cuts) :]
    total = None
    width = grads[0].shape[1]
    for i, grad in enumerate(grads):
        term = nt(grad[...], w_ref[:, i * width : (i + 1) * width])
        total = term if total is None else total + term
    if residual:
        total = total + refs[parts + 1][...]
    for (start, size), o_ref in zip(cuts, outs):
        o_ref[...] = total[start : start + size].astype(BF)


def back_product(grads, w, residual=None, tile=512, cuts=None):
    rows, width = grads[0].shape
    depth = w.shape[0]
    parts = len(grads)
    cuts = cuts or ((0, rows),)
    specs = [whole((rows, width))] * parts + [
        pl.BlockSpec((tile, parts * width), lambda i: (i, 0))
    ]
    args = list(grads) + [w]
    if residual is not None:
        specs.append(pl.BlockSpec((rows, tile), lambda i: (0, i)))
        args.append(residual)
    return pl.pallas_call(
        functools.partial(
            back_product_kernel, parts=parts, residual=residual is not None, cuts=cuts
        ),
        grid=(depth // tile,),
        in_specs=specs,
        out_specs=[pl.BlockSpec((size, tile), lambda i: (0, i)) for _, size in cuts],
        out_shape=[jax.ShapeDtypeStruct((size, depth), BF) for _, size in cuts],
        compiler_params=params(),
        name="back_product",
    )(*args)


def head_lanes(head):
    lane = lax.broadcasted_iota(jnp.int32, (1, LANES), 1)
    own = (lane < HD) if head == 0 else (lane >= HD)
    first = HD if head == 0 else 0
    return own, lane == first, lane == first + 1


def bf(value):
    return jnp.asarray(value, BF)


def rows_of(refs, start, count):
    parts = []
    for ref in refs:
        size = ref.shape[0]
        low, high = max(start, 0), min(start + count, size)
        if low < high:
            parts.append(ref[low:high])
        start -= size
    return parts


def stacked(refs, prefix_ref, start, count):
    parts = rows_of(refs, start, count)
    if prefix_ref is not None:
        parts.append(prefix_ref[...])
    return parts[0] if len(parts) == 1 else jnp.concatenate(parts, 0)


def attend_pair(*refs, segs, prefix, causal, pieces, which, checked):
    len_ref, q_ref = refs[:2]
    k_refs, v_refs = refs[2 : 2 + pieces], refs[2 + pieces : 2 + 2 * pieces]
    at = 2 + 2 * pieces
    pk_ref = pv_ref = None
    if prefix:
        pk_ref, pv_ref = refs[at : at + 2]
        at += 2
    o_ref, inv_ref = refs[at : at + 2]
    p_refs = refs[at + 2 :]

    def work(peaked):
        for seg, (q0, nq, k0, nk) in enumerate(segs):
            keys = stacked(k_refs, pk_ref, k0, nk)
            values = stacked(v_refs, pv_ref, k0, nk)
            count = keys.shape[0]
            row = lax.broadcasted_iota(jnp.int32, (count, 1), 0)
            seen = row < jnp.minimum(len_ref[0, which + seg], nk)
            if prefix:
                seen = seen | ((row >= nk) & (row < nk + PRE))
            queries = q_ref[q0 : q0 + nq] * bf(HD**-0.5)
            out = inv = None
            across = nq >= 4 * LANES
            outs, invs = [], []
            if across:
                turned = values.T
                ones = jnp.ones((16, count), BF)
            for head in range(2):
                own, first, _ = head_lanes(head)
                k_own = jnp.where(own, keys, jnp.where(first & ~seen, bf(big_negative), bf(0)))
                q_own = jnp.where(own, queries, jnp.where(first, bf(1), bf(0)))
                scores = nt(k_own, q_own)
                if causal:
                    key_at = lax.broadcasted_iota(jnp.int32, scores.shape, 0)
                    query_at = lax.broadcasted_iota(jnp.int32, scores.shape, 1)
                    allowed = (key_at <= query_at) | (key_at >= nk)
                    scores = jnp.where(allowed, scores, big_negative)
                if peaked:
                    scores = scores - jnp.max(scores, axis=0, keepdims=True)
                weights = jnp.exp(scores).astype(BF)
                p_refs[seg][head] = weights
                if across:
                    rows = jnp.concatenate([turned[head * HD : (head + 1) * HD], ones], 0)
                    mixed = nn(rows, weights)
                    inverse = 1.0 / mixed[HD : HD + 1]
                    outs.append(mixed[:HD] * inverse)
                    invs.append(jnp.broadcast_to(inverse, (HD, nq)))
                    continue
                mixed = tn(weights, jnp.where(own, values, bf(1)))
                inverse = 1.0 / pltpu.roll(mixed, HD, 1)
                mixed = mixed * inverse
                out = mixed if out is None else jnp.where(own, mixed, out)
                inv = inverse if inv is None else jnp.where(own, inverse, inv)
            if across:
                out = jnp.concatenate(outs, 0).T
                inv = jnp.concatenate(invs, 0).T
            o_ref[q0 : q0 + nq] = out.astype(BF)
            inv_ref[q0 : q0 + nq] = inv

    if not checked:
        work(True)
        return

    limit = 50.0**2
    head_row = lax.broadcasted_iota(jnp.int32, (LANES, LANES), 0) // HD
    head_col = lax.broadcasted_iota(jnp.int32, (LANES, LANES), 1) // HD
    same_head = jnp.where(head_row == head_col, 1.0, 0.0).astype(BF)

    def largest(array):
        square = (array.astype(F32) * array.astype(F32)).astype(BF)
        return jnp.max(nn(square, same_head), axis=0, keepdims=True)

    key_peak = largest(k_refs[0][...])
    for ref in k_refs[1:]:
        key_peak = jnp.maximum(key_peak, largest(ref[...]))
    if prefix:
        key_peak = jnp.maximum(key_peak, largest(pk_ref[...]))
    small = jnp.max(largest(q_ref[...]) * key_peak) * (1.0 / HD) <= limit

    @pl.when(small)
    def _():
        work(False)

    @pl.when(jnp.logical_not(small))
    def _():
        work(True)


def lane_views(refs, group, j):
    views = []
    for ref in refs:
        if len(ref.shape) == 2:
            views.append(ref.at[:, j * LANES : (j + 1) * LANES])
        else:
            views.append(ref.at[2 * j : 2 * j + 2])
    return views


def attend_kernel(len_ref, *refs, group, **kw):
    for j in range(group):
        attend_pair(len_ref, *lane_views(refs, group, j), **kw)


def column_spec(rows, offset, row_block=0, group=1):
    return pl.BlockSpec((rows, group * LANES), lambda h: (row_block, h + offset // group))


def attend(lengths, q, keys, values, prefixes, segs, causal, which=0, group=1, checked=False):
    pairs = 8
    q_rows = q[1]
    prefix = prefixes is not None
    extra = PRE_PAD if prefix else 0
    specs = [pl.BlockSpec(memory_space=pltpu.SMEM)]
    args = [lengths]
    for array, rows, block, offset in [q, *keys, *values]:
        specs.append(column_spec(rows, offset, block, group))
        args.append(array)
    if prefix:
        specs += [column_spec(PRE_PAD, 0, 0, group)] * 2
        args += list(prefixes)
    weight_shapes = [(2 * pairs, nk + extra, nq) for _, nq, _, nk in segs]
    return pl.pallas_call(
        functools.partial(
            attend_kernel, group=group, segs=segs, prefix=prefix, causal=causal, pieces=len(keys), which=which,
            checked=checked,
        ),
        grid=(pairs // group,),
        in_specs=specs,
        out_specs=[column_spec(q_rows, 0, 0, group)] * 2
        + [pl.BlockSpec((2 * group,) + s[1:], lambda h: (h, 0, 0)) for s in weight_shapes],
        out_shape=[
            jax.ShapeDtypeStruct((q_rows, pairs * LANES), BF),
            jax.ShapeDtypeStruct((q_rows, pairs * LANES), F32),
        ]
        + [jax.ShapeDtypeStruct(s, BF) for s in weight_shapes],
        compiler_params=params(),
        name="attend",
    )(*args)


def attend_back_pair(
    q_ref, k_refs, v_refs, o_ref, inv_ref, g_refs, pk_ref, pv_ref, p_refs, dq_ref, dk_ref, dv_ref, segs
):
    prefix_totals = [None, None]
    scale = HD**-0.5
    for seg, (q0, nq, k0, nk) in enumerate(segs):
        keys = stacked(k_refs, pk_ref, k0, nk)
        values = stacked(v_refs, pv_ref, k0, nk)
        queries = q_ref[q0 : q0 + nq]
        grads = stacked(g_refs, None, q0, nq).astype(F32) * inv_ref[q0 : q0 + nq]
        grads_low = grads.astype(BF)
        dots = grads * o_ref[q0 : q0 + nq].astype(F32)
        dq = dk = dv = None
        across = nq >= LANES and keys.shape[0] >= 4 * LANES
        turned_grads = []
        if across:
            turned = keys.T
        for head in range(2):
            own, first, second = head_lanes(head)
            row_dot = -jnp.sum(jnp.where(own, dots, 0.0), axis=1, keepdims=True)
            high = row_dot.astype(BF)
            rest = (row_dot - high.astype(F32)).astype(BF)
            g_own = jnp.where(
                own, grads_low, jnp.where(first, high, jnp.where(second, rest, bf(0)))
            )
            v_own = jnp.where(own, values, jnp.where(first | second, bf(1), bf(0)))
            weights = p_refs[seg][head]
            score_grad = (weights.astype(F32) * nt(v_own, g_own)).astype(BF)
            dv_head = nn(weights, grads_low)
            dk_head = nn(score_grad, queries)
            dq_head = None if across else tn(score_grad, keys)
            if across:
                turned_grads.append(nn(turned[head * HD : (head + 1) * HD], score_grad))
            if not across:
                dq = dq_head if dq is None else jnp.where(own, dq_head, dq)
            dk = dk_head if dk is None else jnp.where(own, dk_head, dk)
            dv = dv_head if dv is None else jnp.where(own, dv_head, dv)
        if across:
            dq = jnp.concatenate(turned_grads, 0).T
        dk = dk * scale
        dq_ref[q0 : q0 + nq] = (dq * scale).astype(BF)
        at = k0 - segs[0][2]
        dk_ref[at : at + nk] = dk[:nk].astype(BF)
        dv_ref[at : at + nk] = dv[:nk].astype(BF)
        if pk_ref is not None:
            for i, grad in enumerate((dk, dv)):
                part = grad[nk:]
                prefix_totals[i] = part if seg == 0 else prefix_totals[i] + part
    return prefix_totals


def attend_back_kernel(*refs, group, **kw):
    for j in range(group):
        attend_back_views(*lane_views(refs, group, j), **kw)


def attend_back_views(*refs, segs, prefix, pieces):
    q_ref, o_ref, inv_ref, g_ref = refs[:4]
    k_refs, v_refs = refs[4 : 4 + pieces], refs[4 + pieces : 4 + 2 * pieces]
    at = 4 + 2 * pieces
    pk_ref = pv_ref = None
    if prefix:
        pk_ref, pv_ref = refs[at : at + 2]
        at += 2
    outs = refs[at + len(segs) :]
    totals = attend_back_pair(
        q_ref, k_refs, v_refs, o_ref, inv_ref, [g_ref], pk_ref, pv_ref,
        refs[at : at + len(segs)], *outs[:3], segs,
    )
    if prefix:
        outs[3][...] = totals[0]
        outs[4][...] = totals[1]


def attend_back(q, keys, values, prefixes, attended, inverse, grad, weights, segs, group=2):
    pairs = 8
    q_rows = q[1]
    k_rows = sum(nk for _, _, _, nk in segs)
    prefix = prefixes is not None
    specs, args = [], []
    own = [(a, q_rows, 0, 0) for a in (attended, inverse, grad)]
    for array, rows, block, offset in [q, *own, *keys, *values]:
        specs.append(column_spec(rows, offset, block, group))
        args.append(array)
    if prefix:
        specs += [column_spec(PRE_PAD, 0, 0, group)] * 2
        args += list(prefixes)
    specs += [pl.BlockSpec((2 * group,) + w.shape[1:], lambda h: (h, 0, 0)) for w in weights]
    args += list(weights)
    out_specs = [column_spec(n, 0, 0, group) for n in (q_rows, k_rows, k_rows)]
    out_shape = [
        jax.ShapeDtypeStruct((q_rows, pairs * LANES), BF),
        jax.ShapeDtypeStruct((k_rows, pairs * LANES), BF),
        jax.ShapeDtypeStruct((k_rows, pairs * LANES), BF),
    ]
    if prefix:
        out_specs += [column_spec(PRE_PAD, 0, 0, group)] * 2
        out_shape += [jax.ShapeDtypeStruct((PRE_PAD, pairs * LANES), F32)] * 2
    return pl.pallas_call(
        functools.partial(
            attend_back_kernel, group=group, segs=segs, prefix=prefix, pieces=len(keys)
        ),
        grid=(pairs // group,),
        in_specs=specs,
        out_specs=out_specs,
        out_shape=out_shape,
        compiler_params=params(),
        name="attend_back",
    )(*args)


class Weights:
    def __init__(self, sources, targets, sems):
        self.sources, self.targets, self.sems = sources, targets, sems

    def copy(self, name, part=None):
        source, target = self.sources[name], self.targets[name]
        first = list(self.sources).index(name)
        sem = self.sems.at[first, 0 if part is None else part]
        if part is not None:
            cut = pl.ds(pl.multiple_of(part * wide, wide), wide)
            index = (slice(None), cut) if name == "in" else (cut, slice(None))
            source, target = source.at[index], target.at[index]
        return pltpu.make_async_copy(source, target, sem)

    def wait(self, name, part=None):
        self.copy(name, part).wait()

    def part(self, name, part):
        cut = pl.ds(pl.multiple_of(part * wide, wide), wide)
        index = (slice(None), cut) if name == "in" else (cut, slice(None))
        return self.targets[name].at[index]


def weight_scratch(arrays, parts):
    return [pltpu.VMEM(a.shape, BF) for a in arrays] + [
        pltpu.SemaphoreType.DMA((len(arrays), parts))
    ]


def ffn_step(low_ref, acc_ref, in_ref, out_ref, slope_ref, act_ref, bias_ref, scale):
    for start, size in row_tiles(low_ref.shape[0]):
        rows = slice(start, start + size)
        hidden = nn(low_ref[rows], in_ref[...])
        if bias_ref is not None:
            hidden = hidden + bias_ref[...]
        active, slope = gelu_pair(hidden)
        slope_ref[rows] = slope.astype(BF)
        active = active.astype(BF)
        if act_ref is not None:
            act_ref[rows] = active
        term = nn(active, out_ref[...])
        acc_ref[rows] += term if scale is None else scale * term


def enc_ffn_kernel(
    x_ref, att_ref, gain_ref, downb_ref, upb_ref, wo_hbm, in_hbm, out_hbm, down_hbm, up_hbm,
    mem_ref, slope_ref, pre_slope_ref, act_ref, low_ref, scales_ref,
    acc_ref, wo_ref, in_ref, out_ref, down_ref, up_ref, sems,
):
    weights = Weights(
        {"wo": wo_hbm, "in": in_hbm, "out": out_hbm, "down": down_hbm, "up": up_hbm},
        {"wo": wo_ref, "in": in_ref, "out": out_ref, "down": down_ref, "up": up_ref},
        sems,
    )

    weights.copy("wo").start()
    for part in range(in_ref.shape[1] // wide):
        weights.copy("in", part).start()
        weights.copy("out", part).start()
    weights.copy("down").start()
    weights.copy("up").start()
    weights.wait("wo")
    first = x_ref[...].astype(F32) + nn(att_ref[...], wo_ref[...])
    hat, scale = norm_rows(first)
    normed = hat * gain_ref[0:1]
    acc_ref[...] = normed
    low_ref[...] = normed.astype(BF)
    scales_ref[:, 0:1] = scale

    for part in range(in_ref.shape[1] // wide):
        weights.wait("in", part)
        weights.wait("out", part)
        cols = slice(part * wide, (part + 1) * wide)
        ffn_step(
            low_ref, acc_ref, in_ref.at[:, cols], out_ref.at[cols], slope_ref.at[:, cols],
            None, None, None,
        )

    weights.wait("down")
    weights.wait("up")
    ffn_step(low_ref, acc_ref, down_ref, up_ref, pre_slope_ref, act_ref, downb_ref, adapter_scale)
    hat, scale = norm_rows(acc_ref[...] + adapter_scale * upb_ref[...])
    mem_ref[...] = (hat * gain_ref[1:2]).astype(BF)
    scales_ref[:, 1:2] = scale


def enc_ffn(x, att, w, part):
    width = x.shape[1]
    rows = ENC_ROWS
    hidden = w["ffn_in"].shape[1]
    steps = hidden // wide
    weights = [w["out"], w["ffn_in"], w["ffn_out"], w["down"], w["up"]]
    return pl.pallas_call(
        enc_ffn_kernel,
        grid=(1,),
        in_specs=[
            pl.BlockSpec((rows, width), lambda i: (part, 0)),
            pl.BlockSpec((rows, width), lambda i: (part, 0)),
            whole((2, width)),
            whole((1, chunk)),
            whole((1, width)),
        ]
        + [pl.BlockSpec(memory_space=pl.ANY)] * len(weights),
        out_specs=[
            whole((rows, width)),
            whole((rows, hidden)),
            whole((rows, chunk)),
            whole((rows, chunk)),
            whole((rows, width)),
            whole((rows, LANES)),
        ],
        out_shape=[
            jax.ShapeDtypeStruct((rows, width), BF),
            jax.ShapeDtypeStruct((rows, hidden), BF),
            jax.ShapeDtypeStruct((rows, chunk), BF),
            jax.ShapeDtypeStruct((rows, chunk), BF),
            jax.ShapeDtypeStruct((rows, width), BF),
            jax.ShapeDtypeStruct((rows, LANES), F32),
        ],
        scratch_shapes=[pltpu.VMEM((rows, width), F32)] + weight_scratch(weights, steps),
        compiler_params=params(),
        name="enc_ffn",
    )(x, att, w["gains"], w["down_bias"], w["up_bias"], *weights)


def ffn_back_step(grad_ref, acc_ref, in_ref, out_ref, slope_ref):
    for start, size in row_tiles(grad_ref.shape[0]):
        rows = slice(start, start + size)
        pre = (nt(grad_ref[rows], out_ref[...]) * slope_ref[rows].astype(F32)).astype(BF)
        acc_ref[rows] += nt(pre, in_ref[...])


def adapter_back(grad_ref, acc_ref, low_ref, act_ref, slope_ref, down_ref, up_ref, outs, pre_ref):
    ddown_ref, ddownb_ref, dup_ref, dupb_ref = outs
    total = None
    for start, size in row_tiles(grad_ref.shape[0]):
        rows = slice(start, start + size)
        back = adapter_scale * nt(grad_ref[rows], up_ref[...])
        pre = (back * slope_ref[rows].astype(F32)).astype(BF)
        pre_ref[rows] = pre
        sums = jnp.sum(pre.astype(F32), axis=0, keepdims=True)
        total = sums if total is None else total + sums
        acc_ref[rows] += nt(pre, down_ref[...])
    ddownb_ref[...] = total
    ddown_ref[...] = tn(low_ref[...], pre_ref[...])
    dup_ref[...] = adapter_scale * tn(act_ref[...], grad_ref[...])
    dupb_ref[...] = adapter_scale * jnp.sum(grad_ref[...].astype(F32), axis=0, keepdims=True)


def enc_ffn_back_kernel(*refs, pieces):
    enc_ffn_back_body(refs[:pieces], *refs[pieces:])


def enc_ffn_back_body(
    dmem_refs, mem_ref, low_ref, scales_ref, gain_ref, slope_ref, pre_slope_ref,
    up_hbm, down_hbm, in_hbm, out_hbm, wo_hbm,
    dfirst_ref, datt_ref, grad_ref, pre_ref,
    acc_ref, up_ref, down_ref, in_ref, out_ref, wo_ref, sems,
):
    weights = Weights(
        {"up": up_hbm, "down": down_hbm, "in": in_hbm, "out": out_hbm, "wo": wo_hbm},
        {"up": up_ref, "down": down_ref, "in": in_ref, "out": out_ref, "wo": wo_ref},
        sems,
    )

    weights.copy("up").start()
    weights.copy("down").start()
    for part in range(in_ref.shape[1] // wide):
        weights.copy("out", part).start()
        weights.copy("in", part).start()
    weights.copy("wo").start()
    gain = gain_ref[1:2]
    hat = mem_ref[...].astype(F32) / gain
    dmem = stacked(dmem_refs, None, 0, ENC_ROWS).astype(F32)
    grad = norm_rows_back(hat, scales_ref[:, 1:2], dmem * gain)
    low = grad.astype(BF)
    grad_ref[...] = low
    weights.wait("up")
    back = adapter_scale * nt(low, up_ref[...])
    pre = (back * pre_slope_ref[...].astype(F32)).astype(BF)
    pre_ref[...] = pre
    weights.wait("down")
    acc_ref[...] = grad + nt(pre, down_ref[...])

    for part in range(in_ref.shape[1] // wide):
        weights.wait("out", part)
        weights.wait("in", part)
        cols = slice(part * wide, (part + 1) * wide)
        ffn_back_step(
            grad_ref, acc_ref, in_ref.at[:, cols], out_ref.at[cols], slope_ref.at[:, cols]
        )

    gain = gain_ref[0:1]
    hat = low_ref[...].astype(F32) / gain
    grad = norm_rows_back(hat, scales_ref[:, 0:1], acc_ref[...] * gain)
    dfirst_ref[...] = grad
    weights.wait("wo")
    datt_ref[...] = nt(grad.astype(BF), wo_ref[...]).astype(BF)


def enc_ffn_back(dmems, saved, w):
    mem, slope, pre_slope, act, low, scales = saved
    rows, width = mem.shape
    hidden = w["ffn_in"].shape[1]
    steps = hidden // wide
    weights = [w["up"], w["down"], w["ffn_in"], w["ffn_out"], w["out"]]
    return pl.pallas_call(
        functools.partial(enc_ffn_back_kernel, pieces=len(dmems)),
        grid=(1,),
        in_specs=[whole(d.shape) for d in dmems]
        + [
            whole((rows, width)),
            whole((rows, width)),
            whole((rows, LANES)),
            whole((2, width)),
            whole((rows, hidden)),
            whole((rows, chunk)),
        ]
        + [pl.BlockSpec(memory_space=pl.ANY)] * len(weights),
        out_specs=[
            whole((rows, width)),
            whole((rows, width)),
            whole((rows, width)),
            whole((rows, chunk)),
        ],
        out_shape=[
            jax.ShapeDtypeStruct((rows, width), F32),
            jax.ShapeDtypeStruct((rows, width), BF),
            jax.ShapeDtypeStruct((rows, width), BF),
            jax.ShapeDtypeStruct((rows, chunk), BF),
        ],
        scratch_shapes=[pltpu.VMEM((rows, width), F32)] + weight_scratch(weights, steps),
        compiler_params=params(),
        name="enc_ffn_back",
    )(*dmems, mem, low, scales, w["gains"], slope, pre_slope, *weights)


def adapter_grads_kernel(*refs, parts):
    groups = [refs[n * parts : (n + 1) * parts] for n in range(4)]
    low, act, grad, pre = [jnp.concatenate([r[...] for r in g], 0) for g in groups]
    ddown_ref, ddownb_ref, dup_ref, dupb_ref = refs[4 * parts :]
    ddown_ref[...] = tn(low, pre)
    ddownb_ref[...] = jnp.sum(pre.astype(F32), axis=0, keepdims=True)
    dup_ref[...] = adapter_scale * tn(act, grad)
    dupb_ref[...] = adapter_scale * jnp.sum(grad.astype(F32), axis=0, keepdims=True)


def adapter_grads(lows, acts, grads, pres):
    width = lows[0].shape[1]
    return pl.pallas_call(
        functools.partial(adapter_grads_kernel, parts=len(lows)),
        out_shape=[
            jax.ShapeDtypeStruct((width, chunk), F32),
            jax.ShapeDtypeStruct((1, chunk), F32),
            jax.ShapeDtypeStruct((chunk, width), F32),
            jax.ShapeDtypeStruct((1, width), F32),
        ],
        compiler_params=params(),
        name="adapter_grads",
    )(*lows, *acts, *grads, *pres)


def dec_mid_kernel(x_ref, att_ref, wo_ref, gain_ref, wq_ref, n_ref, scale_ref, cq_ref):
    for start, size in row_tiles(x_ref.shape[0], 256):
        rows = slice(start, start + size)
        first = x_ref[rows].astype(F32) + nn(att_ref[rows], wo_ref[...])
        hat, scale = norm_rows(first)
        normed = hat * gain_ref[0:1]
        n_ref[rows] = normed
        scale_ref[rows, 0:1] = scale
        cq_ref[rows] = nn(normed.astype(BF), wq_ref[...]).astype(BF)


def dec_mid(x, att, w, cross):
    rows, width = x.shape
    return pl.pallas_call(
        dec_mid_kernel,
        out_shape=[
            jax.ShapeDtypeStruct((rows, width), F32),
            jax.ShapeDtypeStruct((rows, LANES), F32),
            jax.ShapeDtypeStruct((rows, width), BF),
        ],
        compiler_params=params(),
        name="dec_mid",
    )(x, att, w["out"], w["gains"], cross["query"])


def dec_ffn_kernel(
    len_ref, n_ref, catt_ref, cot_ref, cgain_ref, gain_ref, downb_ref, upb_ref,
    wco_hbm, in_hbm, out_hbm, down_hbm, up_hbm,
    y_ref, dsecond_ref, dcatt_ref, ddown_ref, ddownb_ref, dup_ref, dupb_ref,
    acc_ref, low_ref, grad_ref, slope_ref, pre_slope_ref, act_ref, pre_ref, scale_ref,
    wco_ref, in_ref, out_ref, down_ref, up_ref, sems,
    *, steps, which,
):
    step = pl.program_id(0)
    weights = Weights(
        {"wco": wco_hbm, "in": in_hbm, "out": out_hbm, "down": down_hbm, "up": up_hbm},
        {"wco": wco_ref, "in": in_ref, "out": out_ref, "down": down_ref, "up": up_ref},
        sems,
    )

    @pl.when(step == 0)
    def _():
        weights.copy("wco").start()
        for part in range(steps):
            weights.copy("in", part).start()
            weights.copy("out", part).start()
        weights.copy("down").start()
        weights.copy("up").start()
        weights.wait("wco")
        second = n_ref[...] + nn(catt_ref[...], wco_ref[...])
        hat, scale = norm_rows(second)
        middle = hat * cgain_ref[...]
        acc_ref[...] = middle
        low_ref[...] = middle.astype(BF)
        scale_ref[:, 0:1] = scale

    @pl.when(step < steps)
    def _():
        weights.wait("in", step)
        weights.wait("out", step)
        ffn_step(
            low_ref, acc_ref, weights.part("in", step), weights.part("out", step),
            slope_ref.at[step], None, None, None,
        )

    @pl.when(step == steps)
    def _():
        weights.wait("down")
        weights.wait("up")
        ffn_step(
            low_ref, acc_ref, down_ref, up_ref, pre_slope_ref, act_ref, downb_ref, adapter_scale
        )
        gain = gain_ref[1:2]
        hat, scale = norm_rows(acc_ref[...] + adapter_scale * upb_ref[...])
        row = lax.broadcasted_iota(jnp.int32, (low_ref.shape[0], 1), 0)
        valid = row < len_ref[0, which]
        y_ref[...] = jnp.where(valid, hat * gain, 0.0).astype(BF)
        cot = jnp.where(valid, cot_ref[...].astype(F32), 0.0)
        grad = norm_rows_back(hat, scale, cot * gain)
        acc_ref[...] = grad
        grad_ref[...] = grad.astype(BF)
        adapter_back(
            grad_ref, acc_ref, low_ref, act_ref, pre_slope_ref, down_ref, up_ref,
            (ddown_ref, ddownb_ref, dup_ref, dupb_ref), pre_ref,
        )

    @pl.when(step > steps)
    def _():
        part = step - steps - 1
        ffn_back_step(
            grad_ref, acc_ref, weights.part("in", part), weights.part("out", part),
            slope_ref.at[part],
        )

    @pl.when(step == 2 * steps)
    def _():
        gain = cgain_ref[...]
        hat = low_ref[...].astype(F32) / gain
        grad = norm_rows_back(hat, scale_ref[:, 0:1], acc_ref[...] * gain)
        dsecond_ref[...] = grad
        dcatt_ref[...] = nt(grad.astype(BF), wco_ref[...]).astype(BF)


def dec_ffn(lengths, n, catt, cot, w, cross, which):
    rows, width = catt.shape
    hidden = w["ffn_in"].shape[1]
    steps = hidden // wide
    weights = [cross["out"], w["ffn_in"], w["ffn_out"], w["down"], w["up"]]
    return pl.pallas_call(
        functools.partial(dec_ffn_kernel, steps=steps, which=which),
        grid=(2 * steps + 1,),
        in_specs=[
            pl.BlockSpec(memory_space=pltpu.SMEM),
            pl.BlockSpec((rows, width), lambda i: (which, 0)),
            whole((rows, width)),
            pl.BlockSpec((rows, width), lambda i: (which, 0)),
            whole((1, width)),
            whole((2, width)),
            whole((1, chunk)),
            whole((1, width)),
        ]
        + [pl.BlockSpec(memory_space=pl.ANY)] * len(weights),
        out_specs=[
            whole((rows, width)),
            whole((rows, width)),
            whole((rows, width)),
            whole((width, chunk)),
            whole((1, chunk)),
            whole((chunk, width)),
            whole((1, width)),
        ],
        out_shape=[
            jax.ShapeDtypeStruct((rows, width), BF),
            jax.ShapeDtypeStruct((rows, width), F32),
            jax.ShapeDtypeStruct((rows, width), BF),
            jax.ShapeDtypeStruct((width, chunk), F32),
            jax.ShapeDtypeStruct((1, chunk), F32),
            jax.ShapeDtypeStruct((chunk, width), F32),
            jax.ShapeDtypeStruct((1, width), F32),
        ],
        scratch_shapes=[
            pltpu.VMEM((rows, width), F32),
            pltpu.VMEM((rows, width), BF),
            pltpu.VMEM((rows, width), BF),
            pltpu.VMEM((steps, rows, wide), BF),
            pltpu.VMEM((rows, chunk), BF),
            pltpu.VMEM((rows, chunk), BF),
            pltpu.VMEM((rows, chunk), BF),
            pltpu.VMEM((rows, LANES), F32),
        ]
        + weight_scratch(weights, steps),
        compiler_params=params(),
        name="dec_ffn",
    )(
        lengths, n, catt, cot, cross["gain"], w["gains"], w["down_bias"], w["up_bias"], *weights
    )


def dec_mid_back_kernel(
    dsecond0_ref, dsecond1_ref, dcq0_ref, dcq1_ref, wq_ref, n_ref, scale_ref, gain_ref, wo_ref,
    dfirst_ref, datt_ref,
):
    for pair, (dsecond_ref, dcq_ref) in enumerate(
        ((dsecond0_ref, dcq0_ref), (dsecond1_ref, dcq1_ref))
    ):
        rows = slice(pair * TGT, (pair + 1) * TGT)
        gain = gain_ref[0:1]
        total = dsecond_ref[...] + nt(dcq_ref[...], wq_ref[...])
        grad = norm_rows_back(n_ref[rows] / gain, scale_ref[rows, 0:1], total * gain)
        dfirst_ref[rows] = grad
        datt_ref[rows] = nt(grad.astype(BF), wo_ref[...]).astype(BF)


def dec_mid_back(dseconds, dcqs, n, scale, w, cross):
    rows, width = n.shape
    return pl.pallas_call(
        dec_mid_back_kernel,
        out_shape=[
            jax.ShapeDtypeStruct((rows, width), F32),
            jax.ShapeDtypeStruct((rows, width), BF),
        ],
        compiler_params=params(),
        name="dec_mid_back",
    )(*dseconds, *dcqs, cross["query"], n, scale, w["gains"], w["out"])


enc_segs = ((0, SRC_LONG, 0, SRC_LONG), (SRC_LONG, SRC_SHORT, SRC_LONG, SRC_SHORT))
dec_segs = ((0, TGT, 0, TGT), (TGT, TGT, TGT, TGT))
cross_segs = (((0, TGT, 0, SRC_LONG),), ((0, TGT, SRC_LONG % ENC_ROWS, SRC_SHORT),))


def self_columns(qkv):
    rows = qkv.shape[0]
    return (qkv, rows, 0, 0), [(qkv, rows, 0, 8)], [(qkv, rows, 0, 16)]


def cross_columns(cq, kvs, which):
    return (
        (cq, TGT, which, 0),
        [(kv, ENC_ROWS, 0, 0) for kv in kvs],
        [(kv, ENC_ROWS, 0, 8) for kv in kvs],
    )


def decoder_self(t, lengths, w, cross):
    qkv = product(t, w["qkv"])
    att, inv, *weights = attend(lengths, *self_columns(qkv), w["prefix"], dec_segs, True, group=2)
    n, scale, cq = dec_mid(t, att, w, cross)
    return cq, (qkv, att, inv, weights, n, scale)


def cross_forward(lengths, cq, kvs, which):
    return attend(
        lengths, *cross_columns(cq, kvs, which), None, cross_segs[which], False, which, group=2
    )


def cross_backward(cq, kvs, forward, dcatt, which):
    catt, inv, *weights = forward
    return attend_back(
        *cross_columns(cq, kvs, which), None, catt, inv, dcatt, weights, cross_segs[which]
    )


def decoder_self_back(kept, dseconds, dcqs, w, cross):
    qkv, att, inv, weights, n, scale = kept
    dfirst, datt = dec_mid_back(dseconds, dcqs, n, scale, w, cross)
    dq, dk, dv, *dprefix = attend_back(
        *self_columns(qkv), w["prefix"], att, inv, datt, weights, dec_segs
    )
    return back_product([dq, dk, dv], w["qkv"], dfirst)[0], dprefix


def small_shape(devices):
    return 8, 8 * (2 * chunk) // devices


def finish_kernel(
    q_ref, k_ref, v_ref, o_ref, inv_ref, g0_ref, g1_ref, g2_ref, pk_ref, pv_ref, pl_ref, ps_ref,
    dfirst0_ref, dfirst1_ref, dfirst2_ref, wqkv_ref,
    enc_down, enc_downb, enc_up, enc_upb, long_down, long_downb, long_up, long_upb,
    short_down, short_downb, short_up, short_upb, dpk_ref, dpv_ref,
    y0_ref, y1_ref, dt_ref,
    source_ref, y_ref, target_ref, o_up_ref, o_down_ref, o_prefix_ref, o_upb_ref, o_downb_ref,
    dq, dk, dv, small, ups, downs, mine, theirs, half_sum, across_y, y_sum, landed, total, result,
    small_landed, small_total, small_result, dx_low, dx_high, dx_landed, lows, lows_landed,
    load_sems, pair_sems, y_sems, z_sems, gather_sems, share_y_sems, back_sems,
    small_sems, share_sems, cross_sems,
    *, devices,
):
    step = pl.program_id(0)
    pairs = 8
    section = lax.axis_index("section")
    is_encoder = section == 0
    chips = devices // 2
    line = chips // 2
    slices = 16 // line
    rows = 2 * chunk
    half = rows // 2
    size = half // slices
    side = size // 2
    part = side // line
    place = lax.axis_index("dp")
    core, chip = lax.rem(place, 2), place // 2
    bit, at_line = lax.rem(chip, 2), chip // 2
    partner = place + 1 - 2 * core
    beside = place + 2 - 4 * bit
    small_rows, small_cols = small_shape(devices)
    tile = 256
    width = 2 * chunk
    scale = 1.0 / devices

    def aligned(value, unit=16):
        return pl.multiple_of(value, unit)

    def along(distance):
        return (lax.rem(at_line + distance, line) * 2 + bit) * 2 + core

    def remote(source, target, send_sem, recv_sem, other):
        return pltpu.make_async_remote_copy(
            src_ref=source, dst_ref=target, send_sem=send_sem, recv_sem=recv_sem,
            device_id=other, device_id_type=pl.DeviceIdType.MESH,
        )

    def in_group(other):
        return {"dp": other}

    across = {"section": 1 - section}
    kept = aligned(core * half)
    given = aligned((1 - core) * half)

    def swap():
        return remote(
            mine.at[pl.ds(given, half)], theirs, pair_sems.at[0], pair_sems.at[1],
            in_group(partner),
        )

    def y_send(j):
        there = pl.ds(aligned(j * size + (1 - bit) * side), side)
        return remote(
            half_sum.at[there], across_y.at[j], y_sems.at[0, j], y_sems.at[1, j], in_group(beside)
        )

    def z_send(j, s):
        there = pl.ds(aligned(lax.rem(at_line + s, line) * part), part)
        return remote(
            y_sum.at[j].at[there], landed.at[j, s - 1],
            z_sems.at[0, j, s - 1], z_sems.at[1, j, s - 1], in_group(along(s)),
        )

    def own_rows(j):
        return pl.ds(aligned(kept + j * size + bit * side + at_line * part), part)

    def own_side(j):
        return pl.ds(aligned(kept + j * size + bit * side), side)

    def other_side(j):
        return pl.ds(aligned(kept + j * size + (1 - bit) * side), side)

    def gather(j, s):
        return remote(
            total.at[j], result.at[own_rows(j)],
            gather_sems.at[0, j, s - 1], gather_sems.at[1, j, s - 1], in_group(along(s)),
        )

    def y_share(j):
        return remote(
            result.at[own_side(j)], result.at[own_side(j)],
            share_y_sems.at[0, j], share_y_sems.at[1, j], in_group(beside),
        )

    def back(j, i):
        there = own_side(j) if i == 0 else other_side(j)
        return remote(
            result.at[there], result.at[there],
            back_sems.at[0, j, i], back_sems.at[1, j, i], in_group(partner),
        )

    def piece(index):
        row = aligned(lax.rem(index, 8) * small_rows, 8)
        col = aligned((index // 8) * small_cols, LANES)
        return pl.ds(row, small_rows), pl.ds(col, small_cols)

    def small_out(s):
        return remote(
            small.at[piece(lax.rem(place + s, devices))], small_landed.at[s - 1],
            small_sems.at[0, s - 1], small_sems.at[1, s - 1],
            in_group(lax.rem(place + s, devices)),
        )

    def small_share(s):
        return remote(
            small_total, small_result.at[piece(place)],
            share_sems.at[0, s - 1], share_sems.at[1, s - 1],
            in_group(lax.rem(place + s, devices)),
        )

    def send_low():
        return remote(lows, lows_landed, cross_sems.at[0, 0], cross_sems.at[1, 0], across)

    def send_high(i):
        return remote(
            dx_high.at[i], dx_landed.at[i], cross_sems.at[0, 1 + i], cross_sems.at[1, 1 + i], across
        )

    def greet(barrier, other):
        pl.semaphore_signal(
            barrier, inc=1, device_id=other, device_id_type=pl.DeviceIdType.MESH
        )

    def load(source, target, i):
        return pltpu.make_async_copy(source, target, load_sems.at[i])

    enc_loads = [load(enc_up, ups.at[0], 0), load(enc_down, downs.at[0], 1)]
    dec_loads = [
        load(long_up, ups.at[0], 0), load(long_down, downs.at[0], 1),
        load(short_up, ups.at[1], 2), load(short_down, downs.at[1], 3),
    ]

    @pl.when(step == 0)
    def _():
        barrier = pltpu.get_barrier_semaphore()
        for s in range(1, devices):
            greet(barrier, in_group(lax.rem(place + s, devices)))

        @pl.when(is_encoder)
        def _():
            for copy in enc_loads:
                copy.start()

        @pl.when(jnp.logical_not(is_encoder))
        def _():
            for copy in dec_loads:
                copy.start()

    @pl.when(is_encoder & (step < pairs))
    def _():
        at = aligned(step * LANES, LANES)
        lanes = pl.ds(at, LANES)
        prefix_totals = attend_back_pair(
            q_ref, [k_ref], [v_ref], o_ref, inv_ref, [g0_ref, g1_ref, g2_ref], pk_ref, pv_ref,
            (pl_ref, ps_ref), dq.at[:, lanes], dk.at[:, lanes], dv.at[:, lanes], enc_segs,
        )
        small[0:PRE_PAD, lanes] = prefix_totals[0] * scale
        small[PRE_PAD : 2 * PRE_PAD, lanes] = prefix_totals[1] * scale

    @pl.when(step == 0)
    def _():
        barrier = pltpu.get_barrier_semaphore()

        def pack(up, down):
            mine[0:chunk] = (up * scale).astype(BF)
            down = (down * scale).astype(BF)
            mine[chunk:width, 0:chunk] = down[0:chunk]
            mine[chunk:width, chunk:width] = down[chunk:width]

        @pl.when(is_encoder)
        def _():
            for copy in enc_loads:
                copy.wait()
            pack(ups[0], downs[0])
            pl.semaphore_wait(barrier, devices - 1)
            greet(barrier, across)

        @pl.when(jnp.logical_not(is_encoder))
        def _():
            for copy in dec_loads:
                copy.wait()
            pack(ups[0] + ups[1], downs[0] + downs[1])
            pl.semaphore_wait(barrier, devices)
            greet(barrier, across)

        swap().start()

        @pl.when(jnp.logical_not(is_encoder))
        def _():
            low = width // 2
            lows[0, 0:TGT] = y0_ref[:, 0:low]
            lows[0, TGT : 2 * TGT] = y1_ref[:, 0:low]
            lows[1] = dt_ref[:, 0:low]
            send_low().start()
            small[0:PRE_PAD] = dpk_ref[...] * scale
            small[PRE_PAD : 2 * PRE_PAD] = dpv_ref[...] * scale

    @pl.when(step == 1)
    def _():
        swap().wait()
        half_sum[...] = (
            mine[pl.ds(kept, half)].astype(F32) + theirs[...].astype(F32)
        ).astype(BF)
        for j in range(min(2, slices)):
            y_send(j).start()

    for j in range(slices):

        @pl.when(step == 2 + j)
        def _(j=j):
            y_send(j).wait()
            if j + 2 < slices:
                y_send(j + 2).start()
            own = pl.ds(aligned(j * size + bit * side), side)
            y_sum[j] = (half_sum[own].astype(F32) + across_y[j].astype(F32)).astype(BF)
            for s in range(1, line):
                z_send(j, s).start()

        @pl.when(step == 4 + j)
        def _(j=j):
            summed = y_sum[j, pl.ds(aligned(at_line * part), part)].astype(F32)
            for s in range(1, line):
                z_send(j, s).wait()
                summed = summed + landed[j, s - 1].astype(F32)
            total[j] = summed.astype(BF)
            result[own_rows(j)] = total[j]
            for s in range(1, line):
                gather(j, s).start()

        @pl.when(step == 6 + j)
        def _(j=j):
            for s in range(1, line):
                gather(j, s).wait()
            y_share(j).start()
            back(j, 0).start()

        @pl.when(step == 8 + j)
        def _(j=j):
            y_share(j).wait()
            back(j, 1).start()

    @pl.when(step == pairs - 1)
    def _():
        @pl.when(is_encoder)
        def _():
            down_row = jnp.concatenate([enc_downb[...], jnp.zeros_like(enc_downb)], 1)
            small[PRE : PRE + 1] = enc_upb[...] * scale
            small[PRE + 1 : PRE + 2] = down_row * scale

        @pl.when(jnp.logical_not(is_encoder))
        def _():
            down_row = long_downb[...] + short_downb[...]
            down_row = jnp.concatenate([down_row, jnp.zeros_like(down_row)], 1)
            small[PRE : PRE + 1] = (long_upb[...] + short_upb[...]) * scale
            small[PRE + 1 : PRE + 2] = down_row * scale

        for s in range(1, devices):
            small_out(s).start()

    @pl.when(is_encoder & (step == pairs))
    def _():
        pl.semaphore_wait(pltpu.get_barrier_semaphore(), 1)

    for i in range(4):

        @pl.when(is_encoder & (step == pairs + i))
        def _(i=i):
            acc = jnp.concatenate([dfirst0_ref[...], dfirst1_ref[...], dfirst2_ref[...]], 0)
            for n, grad in enumerate((dq, dk, dv)):
                acc = acc + nt(grad[...], wqkv_ref[:, n * width : (n + 1) * width])
            if i < 2:
                dx_high[i] = acc.astype(BF)
                send_high(i).start()
            else:
                dx_low[:, (i - 2) * tile : (i - 1) * tile] = acc.astype(BF)

    @pl.when(step == pairs + 1)
    def _():
        own_rows_, own_cols = piece(place)
        summed = small[own_rows_, own_cols]
        for s in range(1, devices):
            small_out(s).wait()
            summed = summed + small_landed[s - 1]
        small_total[...] = summed
        small_result[own_rows_, own_cols] = summed
        for s in range(1, devices):
            small_share(s).start()

    @pl.when(step == pairs + 3)
    def _():
        for j in range(slices):
            for i in range(2):
                back(j, i).wait()
        o_up_ref[...] = result[0:chunk]
        o_down_ref[0:chunk] = result[chunk:width, 0:chunk]
        o_down_ref[chunk:width] = result[chunk:width, chunk:width]
        for s in range(1, devices):
            small_share(s).wait()
        o_prefix_ref[0] = small_result[0:PRE]
        o_prefix_ref[1] = small_result[PRE_PAD : PRE_PAD + PRE]
        o_upb_ref[...] = small_result[PRE : PRE + 1]
        o_downb_ref[...] = small_result[PRE + 1 : PRE + 2, 0:chunk]

        @pl.when(is_encoder)
        def _():
            source_ref[...] = dx_low[...]
            send_low().wait_recv()
            y_ref[...] = lows_landed[0]
            target_ref[...] = lows_landed[1]
            for i in range(2):
                send_high(i).wait_send()

        @pl.when(jnp.logical_not(is_encoder))
        def _():
            low = width // 2
            y_ref[0:TGT] = y0_ref[:, low:width]
            y_ref[TGT : 2 * TGT] = y1_ref[:, low:width]
            target_ref[...] = dt_ref[:, low:width]
            send_low().wait_send()
            for i in range(2):
                send_high(i).wait_recv()
                source_ref[:, i * tile : (i + 1) * tile] = dx_landed[i]


def finish(saved, datts, dfirsts, w, adapters, dec_prefix, ys, dt):
    qkv, att, inv, weights = saved
    devices = lax.axis_size("dp")
    line = devices // 4
    slices = 16 // line
    rows, width = att.shape
    targets = dt.shape[0]
    pairs, tile = 8, 256
    half = width // 2
    side = half // slices // 2
    part = side // line
    small_rows, small_cols = small_shape(devices)

    def mine(value):
        return jnp.where(lax.axis_index("section") == 0, value, 0)

    def head(i):
        return mine(jnp.minimum(i, pairs - 1))

    def pair(offset):
        return pl.BlockSpec((rows, LANES), lambda i: (0, head(i) + offset))

    def at(i):
        return mine(jnp.where(i < pairs + 2, 2 + jnp.maximum(i - pairs, 0), i - pairs - 2))

    def once(shape):
        return pl.BlockSpec(shape, lambda i: (0,) * len(shape), pipeline_mode=pl.Buffered(1))

    anywhere = pl.BlockSpec(memory_space=pl.ANY)
    prefix_pair = pl.BlockSpec((PRE_PAD, LANES), lambda i: (0, head(i)))
    vmem = pltpu.VMEM
    dma = pltpu.SemaphoreType.DMA
    flat = [a for group in adapters for a in group]
    return pl.pallas_call(
        functools.partial(finish_kernel, devices=devices),
        grid=(pairs + 4,),
        in_specs=[pair(0), pair(8), pair(16), pair(0), pair(0)]
        + [pl.BlockSpec((ENC_ROWS, LANES), lambda i: (0, head(i)))] * 3
        + [prefix_pair] * 2
        + [
            pl.BlockSpec((2,) + p.shape[1:], lambda i: (head(i), 0, 0))
            for p in weights
        ]
        + [
            pl.BlockSpec((ENC_ROWS, tile), lambda i: (0, at(i))),
        ]
        * 3
        + [
            pl.BlockSpec((tile, 3 * width), lambda i: (at(i), 0)),
        ]
        + [anywhere if a.shape[0] > 1 else once(a.shape) for a in flat]
        + [once(a.shape) for a in (*dec_prefix, *ys, dt)],
        out_specs=[
            once((rows, half)), once((targets, half)), once((targets, half)),
            once((chunk, width)), once((width, chunk)),
            once((2, PRE, width)), once((1, width)), once((1, chunk)),
        ],
        out_shape=[
            jax.ShapeDtypeStruct((rows, half), BF),
            jax.ShapeDtypeStruct((targets, half), BF),
            jax.ShapeDtypeStruct((targets, half), BF),
            jax.ShapeDtypeStruct((chunk, width), BF),
            jax.ShapeDtypeStruct((width, chunk), BF),
            jax.ShapeDtypeStruct((2, PRE, width), F32),
            jax.ShapeDtypeStruct((1, width), F32),
            jax.ShapeDtypeStruct((1, chunk), F32),
        ],
        scratch_shapes=[
            vmem((rows, width), BF), vmem((rows, width), BF), vmem((rows, width), BF),
            vmem((2 * PRE_PAD, width), F32),
            vmem((2, chunk, width), F32), vmem((2, width, chunk), F32),
            vmem((width, width), BF), vmem((half, width), BF), vmem((half, width), BF),
            vmem((slices, side, width), BF), vmem((slices, side, width), BF),
            vmem((slices, line - 1, part, width), BF), vmem((slices, part, width), BF),
            vmem((width, width), BF),
            vmem((devices - 1, small_rows, small_cols), F32), vmem((small_rows, small_cols), F32),
            vmem((2 * PRE_PAD, width), F32),
            vmem((rows, half), BF), vmem((2, rows, tile), BF), vmem((2, rows, tile), BF),
            vmem((2, targets, half), BF), vmem((2, targets, half), BF),
            dma((4,)), dma((2,)), dma((2, slices)), dma((2, slices, line - 1)),
            dma((2, slices, line - 1)), dma((2, slices)), dma((2, slices, 2)),
            dma((2, devices - 1)), dma((2, devices - 1)), dma((2, 3)),
        ],
        compiler_params=pltpu.CompilerParams(
            vmem_limit_bytes=60 * 2**20, collective_id=0, has_side_effects=True
        ),
        name="finish",
    )(
        qkv, qkv, qkv, att, inv, *datts, *w["prefix"], *weights,
        *dfirsts, w["qkv"], *flat, *dec_prefix, *ys, dt,
    )


def blank_kernel(*refs):
    pass


def blanks(shapes):
    return pl.pallas_call(
        blank_kernel,
        out_shape=list(shapes),
        out_specs=[pl.BlockSpec(memory_space=pl.ANY)] * len(shapes),
        name="blank",
    )()


def on_section(is_encoder, encoder_work, decoder_work, *operands):
    enc_shapes, _ = jax.eval_shape(encoder_work, *operands)
    dec_shapes, _ = jax.eval_shape(decoder_work, *operands)

    def blank_like(shapes):
        leaves, tree = jax.tree.flatten(shapes)
        if not leaves:
            return shapes
        return jax.tree.unflatten(tree, blanks(leaves))

    def encoder_branch(*a):
        own, shared = encoder_work(*a)
        return own, blank_like(dec_shapes), shared

    def decoder_branch(*a):
        own, shared = decoder_work(*a)
        return blank_like(enc_shapes), own, shared

    return lax.cond(is_encoder, encoder_branch, decoder_branch, *operands)


def to_decoder(block):
    return lax.ppermute(block, "section", [(0, 1)])


def to_encoder(block):
    return lax.ppermute(block, "section", [(1, 0)])


def per_device(
    sources, targets, cotangent, source_lengths, target_lengths,
    attn_qkv, attn_out, ffn_in, ffn_out, norm_gains, prefix_pairs,
    adapt_down, adapt_down_bias, adapt_up, adapt_up_bias,
    cross_query, cross_pairs, cross_out, cross_gain,
):
    is_encoder = lax.axis_index("section") == 0
    prefix = jnp.pad(prefix_pairs[0], ((0, 0), (0, PRE_PAD - PRE), (0, 0)))
    w = dict(
        qkv=attn_qkv[0], out=attn_out[0], ffn_in=ffn_in[0], ffn_out=ffn_out[0],
        gains=norm_gains[0], prefix=(prefix[0], prefix[1]),
        down=adapt_down[0], down_bias=adapt_down_bias,
        up=adapt_up[0], up_bias=adapt_up_bias,
    )
    cross = dict(query=cross_query, pairs=cross_pairs, out=cross_out, gain=cross_gain[None])

    def at_encoder(work, *operands):
        return on_section(is_encoder, lambda *a: (work(*a), ()), lambda *a: ((), ()), *operands)[0]

    def at_decoder(work, *operands):
        return on_section(is_encoder, lambda *a: ((), ()), lambda *a: (work(*a), ()), *operands)[1]

    def at_both(enc_work, dec_work, *operands):
        return on_section(
            is_encoder, lambda *a: (enc_work(*a), ()), lambda *a: (dec_work(*a), ()), *operands
        )[:2]

    def encoder_start():
        qkv = product(sources, w["qkv"])
        att, inv, *weights = attend(
            source_lengths, *self_columns(qkv), w["prefix"], enc_segs, False, checked=True
        )
        return (qkv, att, inv, weights), enc_ffn(sources, att, w, 2)

    (saved, part2), (cq, kept) = at_both(
        encoder_start, lambda: decoder_self(targets, target_lengths, w, cross)
    )
    mem2 = to_decoder(part2[0])
    part1 = at_encoder(lambda saved: enc_ffn(sources, saved[1], w, 1), saved)
    mem1 = to_decoder(part1[0])

    def decoder_short(saved, mem2, cq):
        kv2 = product(mem2, cross["pairs"])
        return kv2, cross_forward(source_lengths, cq, [kv2], 1)

    part0, (kv2, short) = at_both(
        lambda saved, mem2, cq: enc_ffn(sources, saved[1], w, 0), decoder_short, saved, mem2, cq
    )
    mem0 = to_decoder(part0[0])
    kv1 = at_decoder(lambda mem1: product(mem1, cross["pairs"]), mem1)

    def decoder_long(mem0, kv1, kv2, cq, kept):
        kvs = [product(mem0, cross["pairs"]), kv1, kv2]
        long = cross_forward(source_lengths, cq, kvs, 0)
        y, dsecond, dcatt, *adapter = dec_ffn(
            target_lengths, kept[4], long[0], cotangent, w, cross, 0
        )
        dcq, dck, dcv = cross_backward(cq, kvs, long, dcatt, 0)
        cuts = ((0, ENC_ROWS), (ENC_ROWS, ENC_ROWS), (2 * ENC_ROWS, SRC_LONG - 2 * ENC_ROWS))
        return back_product([dck, dcv], cross["pairs"], cuts=cuts), y, dsecond, dcq, adapter

    dmems, *long = at_decoder(decoder_long, mem0, kv1, kv2, cq, kept)
    dmem0, dmem1, dmem2 = [to_encoder(block) for block in dmems]

    def decoder_short_back(kv2, cq, kept, short):
        y, dsecond, dcatt, *adapter = dec_ffn(
            target_lengths, kept[4], short[0], cotangent, w, cross, 1
        )
        dcq, dck, dcv = cross_backward(cq, [kv2], short, dcatt, 1)
        return back_product([dck, dcv], cross["pairs"])[0], y, dsecond, dcq, adapter

    dmem_short, *short = at_decoder(decoder_short_back, kv2, cq, kept, short)
    dmem_short = to_encoder(dmem_short)

    def decoder_end(kept, *grads):
        return decoder_self_back(kept, grads[:2], grads[2:], w, cross)

    (long_y, long_second, long_cq, long_adapter) = long
    (short_y, short_second, short_cq, short_adapter) = short
    dt, dec_prefix = at_decoder(
        decoder_end, kept, long_second, short_second, long_cq, short_cq
    )
    dmem0, dt = lax.optimization_barrier((dmem0, dt))
    back0 = at_encoder(lambda dmem0, part0: enc_ffn_back([dmem0], part0, w), dmem0, part0)
    back1 = at_encoder(lambda dmem1, part1: enc_ffn_back([dmem1], part1, w), dmem1, part1)

    def encoder_end(dmem2, dmem_short, part0, part1, part2, back0, back1):
        back2 = enc_ffn_back([dmem2, dmem_short], part2, w)
        parts, backs = (part0, part1, part2), (back0, back1, back2)
        adapter = adapter_grads(
            [p[4] for p in parts], [p[3] for p in parts],
            [b[2] for b in backs], [b[3] for b in backs],
        )
        return back2, adapter

    back2, enc_adapter = at_encoder(
        encoder_end, dmem2, dmem_short, part0, part1, part2, back0, back1
    )
    backs = (back0, back1, back2)
    source_grad, y, target_grad, up, down, prefix_grad, up_bias, down_bias = finish(
        saved, [b[1] for b in backs], [b[0] for b in backs], w,
        [enc_adapter, long_adapter, short_adapter], dec_prefix, [long_y, short_y], dt,
    )
    return (
        y,
        source_grad,
        target_grad,
        prefix_grad[None],
        down.astype(F32)[None],
        down_bias,
        up.astype(F32)[None],
        up_bias,
    )


def solution(mesh):
    layer2, layer3, rows = P("section", None), P("section", None, None), P("dp", None)
    return jax.shard_map(
        per_device,
        mesh=mesh,
        in_specs=(
            rows, rows, rows, rows, rows,
            layer3, layer3, layer3, layer3, layer3,
            P("section", None, None, None),
            layer3, layer2, layer3, layer2,
            P(), P(), P(), P(),
        ),
        out_specs=(
            P("dp", "section"), P("dp", "section"), P("dp", "section"),
            P("section", None, None, None), layer3, layer2, layer3, layer2,
        ),
        check_vma=False,
    )
```

```python
import functools

import jax
import jax.numpy as jnp
from jax import lax
from jax.experimental import pallas as pl
from jax.experimental.pallas import tpu as pltpu
from jax.sharding import PartitionSpec as P

HD = 64
PRE = 30
PRE_PAD = 32
SRC_LONG = 768
SRC_SHORT = 96
TGT = 256
LANES = 128

BF = jnp.bfloat16
F32 = jnp.float32
norm_eps = 1e-05
big_negative = -1e30
adapter_scale = 4.0
chunk = 512
wide = 1024
ENC_ROWS = (SRC_LONG + SRC_SHORT) // 3
vmem_bytes = 56 * 2**20

phi_poly = (
    0.797869713181688,
    0.036392283539041996,
    -8.782472977701046e-05,
    -3.669384069669515e-05,
    1.4250308145882202e-06,
)


def nn(left, right):
    return lax.dot_general(left, right, (((1,), (0,)), ((), ())), preferred_element_type=F32)


def nt(left, right):
    return lax.dot_general(left, right, (((1,), (1,)), ((), ())), preferred_element_type=F32)


def tn(left, right):
    return lax.dot_general(left, right, (((0,), (0,)), ((), ())), preferred_element_type=F32)


def gelu_pair(values):
    square = values * values
    poly = phi_poly[4]
    for coefficient in phi_poly[3::-1]:
        poly = poly * square + coefficient
    half = 0.5 * jnp.tanh(values * poly) + 0.5
    density = jnp.exp(square * -0.5) * 0.3989422804014327
    return values * half, half + values * density


def row_tiles(rows, most=288):
    count = -(-rows // most)
    size = rows // count
    return [(i * size, size) for i in range(count)]


def norm_rows(values):
    centered = values - jnp.mean(values, axis=-1, keepdims=True)
    scale = lax.rsqrt(jnp.mean(centered * centered, axis=-1, keepdims=True) + norm_eps)
    return centered * scale, scale


def norm_rows_back(hat, scale, grad_hat):
    mean_grad = jnp.mean(grad_hat, axis=-1, keepdims=True)
    mean_dot = jnp.mean(grad_hat * hat, axis=-1, keepdims=True)
    return scale * (grad_hat - mean_grad - hat * mean_dot)


def params(limit=vmem_bytes):
    return pltpu.CompilerParams(vmem_limit_bytes=limit)


def whole(shape):
    return pl.BlockSpec(shape, lambda *g: (0,) * len(shape))


def product_kernel(x_ref, w_ref, o_ref):
    o_ref[...] = nn(x_ref[...], w_ref[...]).astype(BF)


def product(x, w, tile=1024):
    rows, depth = x.shape
    width = w.shape[1]
    return pl.pallas_call(
        product_kernel,
        grid=(width // tile,),
        in_specs=[whole((rows, depth)), pl.BlockSpec((depth, tile), lambda i: (0, i))],
        out_specs=pl.BlockSpec((rows, tile), lambda i: (0, i)),
        out_shape=jax.ShapeDtypeStruct((rows, width), BF),
        compiler_params=params(),
        name="product",
    )(x, w)


def back_product_kernel(*refs, parts, residual, cuts):
    grads = refs[:parts]
    w_ref = refs[parts]
    outs = refs[-len(cuts) :]
    total = None
    width = grads[0].shape[1]
    for i, grad in enumerate(grads):
        term = nt(grad[...], w_ref[:, i * width : (i + 1) * width])
        total = term if total is None else total + term
    if residual:
        total = total + refs[parts + 1][...]
    for (start, size), o_ref in zip(cuts, outs):
        o_ref[...] = total[start : start + size].astype(BF)


def back_product(grads, w, residual=None, tile=512, cuts=None):
    rows, width = grads[0].shape
    depth = w.shape[0]
    parts = len(grads)
    cuts = cuts or ((0, rows),)
    specs = [whole((rows, width))] * parts + [
        pl.BlockSpec((tile, parts * width), lambda i: (i, 0))
    ]
    args = list(grads) + [w]
    if residual is not None:
        specs.append(pl.BlockSpec((rows, tile), lambda i: (0, i)))
        args.append(residual)
    return pl.pallas_call(
        functools.partial(
            back_product_kernel, parts=parts, residual=residual is not None, cuts=cuts
        ),
        grid=(depth // tile,),
        in_specs=specs,
        out_specs=[pl.BlockSpec((size, tile), lambda i: (0, i)) for _, size in cuts],
        out_shape=[jax.ShapeDtypeStruct((size, depth), BF) for _, size in cuts],
        compiler_params=params(),
        name="back_product",
    )(*args)


def head_lanes(head):
    lane = lax.broadcasted_iota(jnp.int32, (1, LANES), 1)
    own = (lane < HD) if head == 0 else (lane >= HD)
    first = HD if head == 0 else 0
    return own, lane == first, lane == first + 1


def bf(value):
    return jnp.asarray(value, BF)


def rows_of(refs, start, count):
    parts = []
    for ref in refs:
        size = ref.shape[0]
        low, high = max(start, 0), min(start + count, size)
        if low < high:
            parts.append(ref[low:high])
        start -= size
    return parts


def stacked(refs, prefix_ref, start, count):
    parts = rows_of(refs, start, count)
    if prefix_ref is not None:
        parts.append(prefix_ref[...])
    return parts[0] if len(parts) == 1 else jnp.concatenate(parts, 0)


def attend_pair(*refs, segs, prefix, causal, pieces, which, checked):
    len_ref, q_ref = refs[:2]
    k_refs, v_refs = refs[2 : 2 + pieces], refs[2 + pieces : 2 + 2 * pieces]
    at = 2 + 2 * pieces
    pk_ref = pv_ref = None
    if prefix:
        pk_ref, pv_ref = refs[at : at + 2]
        at += 2
    o_ref, inv_ref = refs[at : at + 2]
    p_refs = refs[at + 2 :]

    def work(peaked):
        for seg, (q0, nq, k0, nk) in enumerate(segs):
            keys = stacked(k_refs, pk_ref, k0, nk)
            values = stacked(v_refs, pv_ref, k0, nk)
            count = keys.shape[0]
            row = lax.broadcasted_iota(jnp.int32, (count, 1), 0)
            seen = row < jnp.minimum(len_ref[0, which + seg], nk)
            if prefix:
                seen = seen | ((row >= nk) & (row < nk + PRE))
            queries = q_ref[q0 : q0 + nq] * bf(HD**-0.5)
            out = inv = None
            across = nq >= 4 * LANES
            outs, invs = [], []
            if across:
                turned = values.T
                ones = jnp.ones((16, count), BF)
            for head in range(2):
                own, first, _ = head_lanes(head)
                k_own = jnp.where(own, keys, jnp.where(first & ~seen, bf(big_negative), bf(0)))
                q_own = jnp.where(own, queries, jnp.where(first, bf(1), bf(0)))
                scores = nt(k_own, q_own)
                if causal:
                    key_at = lax.broadcasted_iota(jnp.int32, scores.shape, 0)
                    query_at = lax.broadcasted_iota(jnp.int32, scores.shape, 1)
                    allowed = (key_at <= query_at) | (key_at >= nk)
                    scores = jnp.where(allowed, scores, big_negative)
                if peaked:
                    scores = scores - jnp.max(scores, axis=0, keepdims=True)
                weights = jnp.exp(scores).astype(BF)
                p_refs[seg][head] = weights
                if across:
                    rows = jnp.concatenate([turned[head * HD : (head + 1) * HD], ones], 0)
                    mixed = nn(rows, weights)
                    inverse = 1.0 / mixed[HD : HD + 1]
                    outs.append(mixed[:HD] * inverse)
                    invs.append(jnp.broadcast_to(inverse, (HD, nq)))
                    continue
                mixed = tn(weights, jnp.where(own, values, bf(1)))
                inverse = 1.0 / pltpu.roll(mixed, HD, 1)
                mixed = mixed * inverse
                out = mixed if out is None else jnp.where(own, mixed, out)
                inv = inverse if inv is None else jnp.where(own, inverse, inv)
            if across:
                out = jnp.concatenate(outs, 0).T
                inv = jnp.concatenate(invs, 0).T
            o_ref[q0 : q0 + nq] = out.astype(BF)
            inv_ref[q0 : q0 + nq] = inv

    if not checked:
        work(True)
        return

    limit = 50.0**2
    head_row = lax.broadcasted_iota(jnp.int32, (LANES, LANES), 0) // HD
    head_col = lax.broadcasted_iota(jnp.int32, (LANES, LANES), 1) // HD
    same_head = jnp.where(head_row == head_col, 1.0, 0.0).astype(BF)

    def largest(array):
        square = (array.astype(F32) * array.astype(F32)).astype(BF)
        return jnp.max(nn(square, same_head), axis=0, keepdims=True)

    key_peak = largest(k_refs[0][...])
    for ref in k_refs[1:]:
        key_peak = jnp.maximum(key_peak, largest(ref[...]))
    if prefix:
        key_peak = jnp.maximum(key_peak, largest(pk_ref[...]))
    small = jnp.max(largest(q_ref[...]) * key_peak) * (1.0 / HD) <= limit

    @pl.when(small)
    def _():
        work(False)

    @pl.when(jnp.logical_not(small))
    def _():
        work(True)


def lane_views(refs, group, j):
    views = []
    for ref in refs:
        if len(ref.shape) == 2:
            views.append(ref.at[:, j * LANES : (j + 1) * LANES])
        else:
            views.append(ref.at[2 * j : 2 * j + 2])
    return views


def attend_kernel(len_ref, *refs, group, **kw):
    for j in range(group):
        attend_pair(len_ref, *lane_views(refs, group, j), **kw)


def column_spec(rows, offset, row_block=0, group=1):
    return pl.BlockSpec((rows, group * LANES), lambda h: (row_block, h + offset // group))


def attend(lengths, q, keys, values, prefixes, segs, causal, which=0, group=1, checked=False):
    pairs = 8
    q_rows = q[1]
    prefix = prefixes is not None
    extra = PRE_PAD if prefix else 0
    specs = [pl.BlockSpec(memory_space=pltpu.SMEM)]
    args = [lengths]
    for array, rows, block, offset in [q, *keys, *values]:
        specs.append(column_spec(rows, offset, block, group))
        args.append(array)
    if prefix:
        specs += [column_spec(PRE_PAD, 0, 0, group)] * 2
        args += list(prefixes)
    weight_shapes = [(2 * pairs, nk + extra, nq) for _, nq, _, nk in segs]
    return pl.pallas_call(
        functools.partial(
            attend_kernel, group=group, segs=segs, prefix=prefix, causal=causal, pieces=len(keys), which=which,
            checked=checked,
        ),
        grid=(pairs // group,),
        in_specs=specs,
        out_specs=[column_spec(q_rows, 0, 0, group)] * 2
        + [pl.BlockSpec((2 * group,) + s[1:], lambda h: (h, 0, 0)) for s in weight_shapes],
        out_shape=[
            jax.ShapeDtypeStruct((q_rows, pairs * LANES), BF),
            jax.ShapeDtypeStruct((q_rows, pairs * LANES), F32),
        ]
        + [jax.ShapeDtypeStruct(s, BF) for s in weight_shapes],
        compiler_params=params(),
        name="attend",
    )(*args)


def attend_back_pair(
    q_ref, k_refs, v_refs, o_ref, inv_ref, g_refs, pk_ref, pv_ref, p_refs, dq_ref, dk_ref, dv_ref, segs
):
    prefix_totals = [None, None]
    scale = HD**-0.5
    for seg, (q0, nq, k0, nk) in enumerate(segs):
        keys = stacked(k_refs, pk_ref, k0, nk)
        values = stacked(v_refs, pv_ref, k0, nk)
        queries = q_ref[q0 : q0 + nq]
        grads = stacked(g_refs, None, q0, nq).astype(F32) * inv_ref[q0 : q0 + nq]
        grads_low = grads.astype(BF)
        dots = grads * o_ref[q0 : q0 + nq].astype(F32)
        dq = dk = dv = None
        across = nq >= LANES and keys.shape[0] >= 4 * LANES
        turned_grads = []
        if across:
            turned = keys.T
        for head in range(2):
            own, first, second = head_lanes(head)
            row_dot = -jnp.sum(jnp.where(own, dots, 0.0), axis=1, keepdims=True)
            high = row_dot.astype(BF)
            rest = (row_dot - high.astype(F32)).astype(BF)
            g_own = jnp.where(
                own, grads_low, jnp.where(first, high, jnp.where(second, rest, bf(0)))
            )
            v_own = jnp.where(own, values, jnp.where(first | second, bf(1), bf(0)))
            weights = p_refs[seg][head]
            score_grad = (weights.astype(F32) * nt(v_own, g_own)).astype(BF)
            dv_head = nn(weights, grads_low)
            dk_head = nn(score_grad, queries)
            dq_head = None if across else tn(score_grad, keys)
            if across:
                turned_grads.append(nn(turned[head * HD : (head + 1) * HD], score_grad))
            if not across:
                dq = dq_head if dq is None else jnp.where(own, dq_head, dq)
            dk = dk_head if dk is None else jnp.where(own, dk_head, dk)
            dv = dv_head if dv is None else jnp.where(own, dv_head, dv)
        if across:
            dq = jnp.concatenate(turned_grads, 0).T
        dk = dk * scale
        dq_ref[q0 : q0 + nq] = (dq * scale).astype(BF)
        at = k0 - segs[0][2]
        dk_ref[at : at + nk] = dk[:nk].astype(BF)
        dv_ref[at : at + nk] = dv[:nk].astype(BF)
        if pk_ref is not None:
            for i, grad in enumerate((dk, dv)):
                part = grad[nk:]
                prefix_totals[i] = part if seg == 0 else prefix_totals[i] + part
    return prefix_totals


def attend_back_kernel(*refs, group, **kw):
    for j in range(group):
        attend_back_views(*lane_views(refs, group, j), **kw)


def attend_back_views(*refs, segs, prefix, pieces):
    q_ref, o_ref, inv_ref, g_ref = refs[:4]
    k_refs, v_refs = refs[4 : 4 + pieces], refs[4 + pieces : 4 + 2 * pieces]
    at = 4 + 2 * pieces
    pk_ref = pv_ref = None
    if prefix:
        pk_ref, pv_ref = refs[at : at + 2]
        at += 2
    outs = refs[at + len(segs) :]
    totals = attend_back_pair(
        q_ref, k_refs, v_refs, o_ref, inv_ref, [g_ref], pk_ref, pv_ref,
        refs[at : at + len(segs)], *outs[:3], segs,
    )
    if prefix:
        outs[3][...] = totals[0]
        outs[4][...] = totals[1]


def attend_back(q, keys, values, prefixes, attended, inverse, grad, weights, segs, group=2):
    pairs = 8
    q_rows = q[1]
    k_rows = sum(nk for _, _, _, nk in segs)
    prefix = prefixes is not None
    specs, args = [], []
    own = [(a, q_rows, 0, 0) for a in (attended, inverse, grad)]
    for array, rows, block, offset in [q, *own, *keys, *values]:
        specs.append(column_spec(rows, offset, block, group))
        args.append(array)
    if prefix:
        specs += [column_spec(PRE_PAD, 0, 0, group)] * 2
        args += list(prefixes)
    specs += [pl.BlockSpec((2 * group,) + w.shape[1:], lambda h: (h, 0, 0)) for w in weights]
    args += list(weights)
    out_specs = [column_spec(n, 0, 0, group) for n in (q_rows, k_rows, k_rows)]
    out_shape = [
        jax.ShapeDtypeStruct((q_rows, pairs * LANES), BF),
        jax.ShapeDtypeStruct((k_rows, pairs * LANES), BF),
        jax.ShapeDtypeStruct((k_rows, pairs * LANES), BF),
    ]
    if prefix:
        out_specs += [column_spec(PRE_PAD, 0, 0, group)] * 2
        out_shape += [jax.ShapeDtypeStruct((PRE_PAD, pairs * LANES), F32)] * 2
    return pl.pallas_call(
        functools.partial(
            attend_back_kernel, group=group, segs=segs, prefix=prefix, pieces=len(keys)
        ),
        grid=(pairs // group,),
        in_specs=specs,
        out_specs=out_specs,
        out_shape=out_shape,
        compiler_params=params(),
        name="attend_back",
    )(*args)


class Weights:
    def __init__(self, sources, targets, sems):
        self.sources, self.targets, self.sems = sources, targets, sems

    def copy(self, name, part=None):
        source, target = self.sources[name], self.targets[name]
        first = list(self.sources).index(name)
        sem = self.sems.at[first, 0 if part is None else part]
        if part is not None:
            cut = pl.ds(pl.multiple_of(part * wide, wide), wide)
            index = (slice(None), cut) if name == "in" else (cut, slice(None))
            source, target = source.at[index], target.at[index]
        return pltpu.make_async_copy(source, target, sem)

    def wait(self, name, part=None):
        self.copy(name, part).wait()

    def part(self, name, part):
        cut = pl.ds(pl.multiple_of(part * wide, wide), wide)
        index = (slice(None), cut) if name == "in" else (cut, slice(None))
        return self.targets[name].at[index]


def weight_scratch(arrays, parts):
    return [pltpu.VMEM(a.shape, BF) for a in arrays] + [
        pltpu.SemaphoreType.DMA((len(arrays), parts))
    ]


def ffn_step(low_ref, acc_ref, in_ref, out_ref, slope_ref, act_ref, bias_ref, scale):
    for start, size in row_tiles(low_ref.shape[0]):
        rows = slice(start, start + size)
        hidden = nn(low_ref[rows], in_ref[...])
        if bias_ref is not None:
            hidden = hidden + bias_ref[...]
        active, slope = gelu_pair(hidden)
        slope_ref[rows] = slope.astype(BF)
        active = active.astype(BF)
        if act_ref is not None:
            act_ref[rows] = active
        term = nn(active, out_ref[...])
        acc_ref[rows] += term if scale is None else scale * term


def enc_ffn_kernel(
    x_ref, att_ref, gain_ref, downb_ref, upb_ref, wo_hbm, in_hbm, out_hbm, down_hbm, up_hbm,
    mem_ref, slope_ref, pre_slope_ref, act_ref, low_ref, scales_ref,
    acc_ref, wo_ref, in_ref, out_ref, down_ref, up_ref, sems,
):
    weights = Weights(
        {"wo": wo_hbm, "in": in_hbm, "out": out_hbm, "down": down_hbm, "up": up_hbm},
        {"wo": wo_ref, "in": in_ref, "out": out_ref, "down": down_ref, "up": up_ref},
        sems,
    )

    weights.copy("wo").start()
    for part in range(in_ref.shape[1] // wide):
        weights.copy("in", part).start()
        weights.copy("out", part).start()
    weights.copy("down").start()
    weights.copy("up").start()
    weights.wait("wo")
    first = x_ref[...].astype(F32) + nn(att_ref[...], wo_ref[...])
    hat, scale = norm_rows(first)
    normed = hat * gain_ref[0:1]
    acc_ref[...] = normed
    low_ref[...] = normed.astype(BF)
    scales_ref[:, 0:1] = scale

    def one_part(part, carry):
        weights.wait("in", part)
        weights.wait("out", part)
        cols = pl.ds(pl.multiple_of(part * wide, wide), wide)
        ffn_step(
            low_ref, acc_ref, in_ref.at[:, cols], out_ref.at[cols], slope_ref.at[:, cols],
            None, None, None,
        )
        return carry

    lax.fori_loop(0, in_ref.shape[1] // wide, one_part, 0)

    weights.wait("down")
    weights.wait("up")
    ffn_step(low_ref, acc_ref, down_ref, up_ref, pre_slope_ref, act_ref, downb_ref, adapter_scale)
    hat, scale = norm_rows(acc_ref[...] + adapter_scale * upb_ref[...])
    mem_ref[...] = (hat * gain_ref[1:2]).astype(BF)
    scales_ref[:, 1:2] = scale


def enc_ffn(x, att, w, part):
    width = x.shape[1]
    rows = ENC_ROWS
    hidden = w["ffn_in"].shape[1]
    steps = hidden // wide
    weights = [w["out"], w["ffn_in"], w["ffn_out"], w["down"], w["up"]]
    return pl.pallas_call(
        enc_ffn_kernel,
        grid=(1,),
        in_specs=[
            pl.BlockSpec((rows, width), lambda i: (part, 0)),
            pl.BlockSpec((rows, width), lambda i: (part, 0)),
            whole((2, width)),
            whole((1, chunk)),
            whole((1, width)),
        ]
        + [pl.BlockSpec(memory_space=pl.ANY)] * len(weights),
        out_specs=[
            whole((rows, width)),
            whole((rows, hidden)),
            whole((rows, chunk)),
            whole((rows, chunk)),
            whole((rows, width)),
            whole((rows, LANES)),
        ],
        out_shape=[
            jax.ShapeDtypeStruct((rows, width), BF),
            jax.ShapeDtypeStruct((rows, hidden), BF),
            jax.ShapeDtypeStruct((rows, chunk), BF),
            jax.ShapeDtypeStruct((rows, chunk), BF),
            jax.ShapeDtypeStruct((rows, width), BF),
            jax.ShapeDtypeStruct((rows, LANES), F32),
        ],
        scratch_shapes=[pltpu.VMEM((rows, width), F32)] + weight_scratch(weights, steps),
        compiler_params=params(),
        name="enc_ffn",
    )(x, att, w["gains"], w["down_bias"], w["up_bias"], *weights)


def ffn_back_step(grad_ref, acc_ref, in_ref, out_ref, slope_ref):
    for start, size in row_tiles(grad_ref.shape[0]):
        rows = slice(start, start + size)
        pre = (nt(grad_ref[rows], out_ref[...]) * slope_ref[rows].astype(F32)).astype(BF)
        acc_ref[rows] += nt(pre, in_ref[...])


def adapter_back(grad_ref, acc_ref, low_ref, act_ref, slope_ref, down_ref, up_ref, outs, pre_ref):
    ddown_ref, ddownb_ref, dup_ref, dupb_ref = outs
    total = None
    for start, size in row_tiles(grad_ref.shape[0]):
        rows = slice(start, start + size)
        back = adapter_scale * nt(grad_ref[rows], up_ref[...])
        pre = (back * slope_ref[rows].astype(F32)).astype(BF)
        pre_ref[rows] = pre
        sums = jnp.sum(pre.astype(F32), axis=0, keepdims=True)
        total = sums if total is None else total + sums
        acc_ref[rows] += nt(pre, down_ref[...])
    ddownb_ref[...] = total
    ddown_ref[...] = tn(low_ref[...], pre_ref[...])
    dup_ref[...] = adapter_scale * tn(act_ref[...], grad_ref[...])
    dupb_ref[...] = adapter_scale * jnp.sum(grad_ref[...].astype(F32), axis=0, keepdims=True)


def enc_ffn_back_kernel(*refs, pieces):
    enc_ffn_back_body(refs[:pieces], *refs[pieces:])


def enc_ffn_back_body(
    dmem_refs, mem_ref, low_ref, scales_ref, gain_ref, slope_ref, pre_slope_ref,
    up_hbm, down_hbm, in_hbm, out_hbm, wo_hbm,
    dfirst_ref, datt_ref, grad_ref, pre_ref,
    acc_ref, up_ref, down_ref, in_ref, out_ref, wo_ref, sems,
):
    weights = Weights(
        {"up": up_hbm, "down": down_hbm, "in": in_hbm, "out": out_hbm, "wo": wo_hbm},
        {"up": up_ref, "down": down_ref, "in": in_ref, "out": out_ref, "wo": wo_ref},
        sems,
    )

    weights.copy("up").start()
    weights.copy("down").start()
    for part in range(in_ref.shape[1] // wide):
        weights.copy("out", part).start()
        weights.copy("in", part).start()
    weights.copy("wo").start()
    gain = gain_ref[1:2]
    hat = mem_ref[...].astype(F32) / gain
    dmem = stacked(dmem_refs, None, 0, ENC_ROWS).astype(F32)
    grad = norm_rows_back(hat, scales_ref[:, 1:2], dmem * gain)
    low = grad.astype(BF)
    grad_ref[...] = low
    weights.wait("up")
    back = adapter_scale * nt(low, up_ref[...])
    pre = (back * pre_slope_ref[...].astype(F32)).astype(BF)
    pre_ref[...] = pre
    weights.wait("down")
    acc_ref[...] = grad + nt(pre, down_ref[...])

    def one_part(part, carry):
        weights.wait("out", part)
        weights.wait("in", part)
        cols = pl.ds(pl.multiple_of(part * wide, wide), wide)
        ffn_back_step(
            grad_ref, acc_ref, in_ref.at[:, cols], out_ref.at[cols], slope_ref.at[:, cols]
        )
        return carry

    lax.fori_loop(0, in_ref.shape[1] // wide, one_part, 0)

    gain = gain_ref[0:1]
    hat = low_ref[...].astype(F32) / gain
    grad = norm_rows_back(hat, scales_ref[:, 0:1], acc_ref[...] * gain)
    dfirst_ref[...] = grad
    weights.wait("wo")
    datt_ref[...] = nt(grad.astype(BF), wo_ref[...]).astype(BF)


def enc_ffn_back(dmems, saved, w):
    mem, slope, pre_slope, act, low, scales = saved
    rows, width = mem.shape
    hidden = w["ffn_in"].shape[1]
    steps = hidden // wide
    weights = [w["up"], w["down"], w["ffn_in"], w["ffn_out"], w["out"]]
    return pl.pallas_call(
        functools.partial(enc_ffn_back_kernel, pieces=len(dmems)),
        grid=(1,),
        in_specs=[whole(d.shape) for d in dmems]
        + [
            whole((rows, width)),
            whole((rows, width)),
            whole((rows, LANES)),
            whole((2, width)),
            whole((rows, hidden)),
            whole((rows, chunk)),
        ]
        + [pl.BlockSpec(memory_space=pl.ANY)] * len(weights),
        out_specs=[
            whole((rows, width)),
            whole((rows, width)),
            whole((rows, width)),
            whole((rows, chunk)),
        ],
        out_shape=[
            jax.ShapeDtypeStruct((rows, width), F32),
            jax.ShapeDtypeStruct((rows, width), BF),
            jax.ShapeDtypeStruct((rows, width), BF),
            jax.ShapeDtypeStruct((rows, chunk), BF),
        ],
        scratch_shapes=[pltpu.VMEM((rows, width), F32)] + weight_scratch(weights, steps),
        compiler_params=params(),
        name="enc_ffn_back",
    )(*dmems, mem, low, scales, w["gains"], slope, pre_slope, *weights)


def adapter_grads_kernel(*refs, parts):
    groups = [refs[n * parts : (n + 1) * parts] for n in range(4)]
    low, act, grad, pre = [jnp.concatenate([r[...] for r in g], 0) for g in groups]
    ddown_ref, ddownb_ref, dup_ref, dupb_ref = refs[4 * parts :]
    ddown_ref[...] = tn(low, pre)
    ddownb_ref[...] = jnp.sum(pre.astype(F32), axis=0, keepdims=True)
    dup_ref[...] = adapter_scale * tn(act, grad)
    dupb_ref[...] = adapter_scale * jnp.sum(grad.astype(F32), axis=0, keepdims=True)


def adapter_grads(lows, acts, grads, pres):
    width = lows[0].shape[1]
    return pl.pallas_call(
        functools.partial(adapter_grads_kernel, parts=len(lows)),
        out_shape=[
            jax.ShapeDtypeStruct((width, chunk), F32),
            jax.ShapeDtypeStruct((1, chunk), F32),
            jax.ShapeDtypeStruct((chunk, width), F32),
            jax.ShapeDtypeStruct((1, width), F32),
        ],
        compiler_params=params(),
        name="adapter_grads",
    )(*lows, *acts, *grads, *pres)


def dec_mid_kernel(x_ref, att_ref, wo_ref, gain_ref, wq_ref, n_ref, scale_ref, cq_ref):
    for start, size in row_tiles(x_ref.shape[0], 256):
        rows = slice(start, start + size)
        first = x_ref[rows].astype(F32) + nn(att_ref[rows], wo_ref[...])
        hat, scale = norm_rows(first)
        normed = hat * gain_ref[0:1]
        n_ref[rows] = normed
        scale_ref[rows, 0:1] = scale
        cq_ref[rows] = nn(normed.astype(BF), wq_ref[...]).astype(BF)


def dec_mid(x, att, w, cross):
    rows, width = x.shape
    return pl.pallas_call(
        dec_mid_kernel,
        out_shape=[
            jax.ShapeDtypeStruct((rows, width), F32),
            jax.ShapeDtypeStruct((rows, LANES), F32),
            jax.ShapeDtypeStruct((rows, width), BF),
        ],
        compiler_params=params(),
        name="dec_mid",
    )(x, att, w["out"], w["gains"], cross["query"])


def dec_ffn_kernel(
    len_ref, n_ref, catt_ref, cot_ref, cgain_ref, gain_ref, downb_ref, upb_ref,
    wco_hbm, in_hbm, out_hbm, down_hbm, up_hbm,
    y_ref, dsecond_ref, dcatt_ref, ddown_ref, ddownb_ref, dup_ref, dupb_ref,
    acc_ref, low_ref, grad_ref, slope_ref, pre_slope_ref, act_ref, pre_ref, scale_ref,
    wco_ref, in_ref, out_ref, down_ref, up_ref, sems,
    *, steps, which,
):
    step = pl.program_id(0)
    weights = Weights(
        {"wco": wco_hbm, "in": in_hbm, "out": out_hbm, "down": down_hbm, "up": up_hbm},
        {"wco": wco_ref, "in": in_ref, "out": out_ref, "down": down_ref, "up": up_ref},
        sems,
    )

    @pl.when(step == 0)
    def _():
        weights.copy("wco").start()
        for part in range(steps):
            weights.copy("in", part).start()
            weights.copy("out", part).start()
        weights.copy("down").start()
        weights.copy("up").start()
        weights.wait("wco")
        second = n_ref[...] + nn(catt_ref[...], wco_ref[...])
        hat, scale = norm_rows(second)
        middle = hat * cgain_ref[...]
        acc_ref[...] = middle
        low_ref[...] = middle.astype(BF)
        scale_ref[:, 0:1] = scale

    @pl.when(step < steps)
    def _():
        weights.wait("in", step)
        weights.wait("out", step)
        ffn_step(
            low_ref, acc_ref, weights.part("in", step), weights.part("out", step),
            slope_ref.at[step], None, None, None,
        )

    @pl.when(step == steps)
    def _():
        weights.wait("down")
        weights.wait("up")
        ffn_step(
            low_ref, acc_ref, down_ref, up_ref, pre_slope_ref, act_ref, downb_ref, adapter_scale
        )
        gain = gain_ref[1:2]
        hat, scale = norm_rows(acc_ref[...] + adapter_scale * upb_ref[...])
        row = lax.broadcasted_iota(jnp.int32, (low_ref.shape[0], 1), 0)
        valid = row < len_ref[0, which]
        y_ref[...] = jnp.where(valid, hat * gain, 0.0).astype(BF)
        cot = jnp.where(valid, cot_ref[...].astype(F32), 0.0)
        grad = norm_rows_back(hat, scale, cot * gain)
        acc_ref[...] = grad
        grad_ref[...] = grad.astype(BF)
        adapter_back(
            grad_ref, acc_ref, low_ref, act_ref, pre_slope_ref, down_ref, up_ref,
            (ddown_ref, ddownb_ref, dup_ref, dupb_ref), pre_ref,
        )

    @pl.when(step > steps)
    def _():
        part = step - steps - 1
        ffn_back_step(
            grad_ref, acc_ref, weights.part("in", part), weights.part("out", part),
            slope_ref.at[part],
        )

    @pl.when(step == 2 * steps)
    def _():
        gain = cgain_ref[...]
        hat = low_ref[...].astype(F32) / gain
        grad = norm_rows_back(hat, scale_ref[:, 0:1], acc_ref[...] * gain)
        dsecond_ref[...] = grad
        dcatt_ref[...] = nt(grad.astype(BF), wco_ref[...]).astype(BF)


def dec_ffn(lengths, n, catt, cot, w, cross, which):
    rows, width = catt.shape
    hidden = w["ffn_in"].shape[1]
    steps = hidden // wide
    weights = [cross["out"], w["ffn_in"], w["ffn_out"], w["down"], w["up"]]
    return pl.pallas_call(
        functools.partial(dec_ffn_kernel, steps=steps, which=which),
        grid=(2 * steps + 1,),
        in_specs=[
            pl.BlockSpec(memory_space=pltpu.SMEM),
            pl.BlockSpec((rows, width), lambda i: (which, 0)),
            whole((rows, width)),
            pl.BlockSpec((rows, width), lambda i: (which, 0)),
            whole((1, width)),
            whole((2, width)),
            whole((1, chunk)),
            whole((1, width)),
        ]
        + [pl.BlockSpec(memory_space=pl.ANY)] * len(weights),
        out_specs=[
            whole((rows, width)),
            whole((rows, width)),
            whole((rows, width)),
            whole((width, chunk)),
            whole((1, chunk)),
            whole((chunk, width)),
            whole((1, width)),
        ],
        out_shape=[
            jax.ShapeDtypeStruct((rows, width), BF),
            jax.ShapeDtypeStruct((rows, width), F32),
            jax.ShapeDtypeStruct((rows, width), BF),
            jax.ShapeDtypeStruct((width, chunk), F32),
            jax.ShapeDtypeStruct((1, chunk), F32),
            jax.ShapeDtypeStruct((chunk, width), F32),
            jax.ShapeDtypeStruct((1, width), F32),
        ],
        scratch_shapes=[
            pltpu.VMEM((rows, width), F32),
            pltpu.VMEM((rows, width), BF),
            pltpu.VMEM((rows, width), BF),
            pltpu.VMEM((steps, rows, wide), BF),
            pltpu.VMEM((rows, chunk), BF),
            pltpu.VMEM((rows, chunk), BF),
            pltpu.VMEM((rows, chunk), BF),
            pltpu.VMEM((rows, LANES), F32),
        ]
        + weight_scratch(weights, steps),
        compiler_params=params(),
        name="dec_ffn",
    )(
        lengths, n, catt, cot, cross["gain"], w["gains"], w["down_bias"], w["up_bias"], *weights
    )


def dec_mid_back_kernel(
    dsecond0_ref, dsecond1_ref, dcq0_ref, dcq1_ref, wq_ref, n_ref, scale_ref, gain_ref, wo_ref,
    dfirst_ref, datt_ref,
):
    for pair, (dsecond_ref, dcq_ref) in enumerate(
        ((dsecond0_ref, dcq0_ref), (dsecond1_ref, dcq1_ref))
    ):
        rows = slice(pair * TGT, (pair + 1) * TGT)
        gain = gain_ref[0:1]
        total = dsecond_ref[...] + nt(dcq_ref[...], wq_ref[...])
        grad = norm_rows_back(n_ref[rows] / gain, scale_ref[rows, 0:1], total * gain)
        dfirst_ref[rows] = grad
        datt_ref[rows] = nt(grad.astype(BF), wo_ref[...]).astype(BF)


def dec_mid_back(dseconds, dcqs, n, scale, w, cross):
    rows, width = n.shape
    return pl.pallas_call(
        dec_mid_back_kernel,
        out_shape=[
            jax.ShapeDtypeStruct((rows, width), F32),
            jax.ShapeDtypeStruct((rows, width), BF),
        ],
        compiler_params=params(),
        name="dec_mid_back",
    )(*dseconds, *dcqs, cross["query"], n, scale, w["gains"], w["out"])


enc_segs = ((0, SRC_LONG, 0, SRC_LONG), (SRC_LONG, SRC_SHORT, SRC_LONG, SRC_SHORT))
dec_segs = ((0, TGT, 0, TGT), (TGT, TGT, TGT, TGT))
cross_segs = (((0, TGT, 0, SRC_LONG),), ((0, TGT, SRC_LONG % ENC_ROWS, SRC_SHORT),))


def self_columns(qkv):
    rows = qkv.shape[0]
    return (qkv, rows, 0, 0), [(qkv, rows, 0, 8)], [(qkv, rows, 0, 16)]


def cross_columns(cq, kvs, which):
    return (
        (cq, TGT, which, 0),
        [(kv, ENC_ROWS, 0, 0) for kv in kvs],
        [(kv, ENC_ROWS, 0, 8) for kv in kvs],
    )


def decoder_self(t, lengths, w, cross):
    qkv = product(t, w["qkv"])
    att, inv, *weights = attend(lengths, *self_columns(qkv), w["prefix"], dec_segs, True, group=2)
    n, scale, cq = dec_mid(t, att, w, cross)
    return cq, (qkv, att, inv, weights, n, scale)


def cross_forward(lengths, cq, kvs, which):
    return attend(
        lengths, *cross_columns(cq, kvs, which), None, cross_segs[which], False, which, group=2
    )


def cross_backward(cq, kvs, forward, dcatt, which):
    catt, inv, *weights = forward
    return attend_back(
        *cross_columns(cq, kvs, which), None, catt, inv, dcatt, weights, cross_segs[which]
    )


def decoder_self_back(kept, dseconds, dcqs, w, cross):
    qkv, att, inv, weights, n, scale = kept
    dfirst, datt = dec_mid_back(dseconds, dcqs, n, scale, w, cross)
    dq, dk, dv, *dprefix = attend_back(
        *self_columns(qkv), w["prefix"], att, inv, datt, weights, dec_segs
    )
    return back_product([dq, dk, dv], w["qkv"], dfirst)[0], dprefix


def small_shape(devices):
    return 8, 8 * (2 * chunk) // devices


def finish_kernel(
    q_ref, k_ref, v_ref, o_ref, inv_ref, g0_ref, g1_ref, g2_ref, pk_ref, pv_ref, pl_ref, ps_ref,
    dfirst0_ref, dfirst1_ref, dfirst2_ref, wqkv_ref,
    enc_down, enc_downb, enc_up, enc_upb, long_down, long_downb, long_up, long_upb,
    short_down, short_downb, short_up, short_upb, dpk_ref, dpv_ref,
    y0_ref, y1_ref, dt_ref,
    source_ref, y_ref, target_ref, o_up_ref, o_down_ref, o_prefix_ref, o_upb_ref, o_downb_ref,
    dq, dk, dv, small, ups, downs, mine, theirs, half_sum, across_y, y_sum, landed, total, result,
    small_landed, small_total, small_result, dx, dx_landed, lows, lows_landed,
    load_sems, pair_sems, y_sems, z_sems, gather_sems, share_y_sems, back_sems,
    small_sems, share_sems, cross_sems,
    *, devices,
):
    step = pl.program_id(0)
    pairs = 8
    section = lax.axis_index("section")
    is_encoder = section == 0
    chips = devices // 2
    line = chips // 2
    slices = 16 // line
    rows = 2 * chunk
    half = rows // 2
    size = half // slices
    side = size // 2
    part = side // line
    place = lax.axis_index("dp")
    core, chip = lax.rem(place, 2), place // 2
    bit, at_line = lax.rem(chip, 2), chip // 2
    partner = place + 1 - 2 * core
    beside = place + 2 - 4 * bit
    small_rows, small_cols = small_shape(devices)
    tile = 256
    width = 2 * chunk
    scale = 1.0 / devices

    def aligned(value, unit=16):
        return pl.multiple_of(value, unit)

    def along(distance):
        return (lax.rem(at_line + distance, line) * 2 + bit) * 2 + core

    def remote(source, target, send_sem, recv_sem, other):
        return pltpu.make_async_remote_copy(
            src_ref=source, dst_ref=target, send_sem=send_sem, recv_sem=recv_sem,
            device_id=other, device_id_type=pl.DeviceIdType.MESH,
        )

    def in_group(other):
        return {"dp": other}

    across = {"section": 1 - section}
    kept = aligned(core * half)
    given = aligned((1 - core) * half)

    def swap():
        return remote(
            mine.at[pl.ds(given, half)], theirs, pair_sems.at[0], pair_sems.at[1],
            in_group(partner),
        )

    def y_send(j):
        there = pl.ds(aligned(j * size + (1 - bit) * side), side)
        return remote(
            half_sum.at[there], across_y.at[j], y_sems.at[0, j], y_sems.at[1, j], in_group(beside)
        )

    def z_send(j, s):
        there = pl.ds(aligned(lax.rem(at_line + s, line) * part), part)
        return remote(
            y_sum.at[j].at[there], landed.at[j, s - 1],
            z_sems.at[0, j, s - 1], z_sems.at[1, j, s - 1], in_group(along(s)),
        )

    def own_rows(j):
        return pl.ds(aligned(kept + j * size + bit * side + at_line * part), part)

    def own_side(j):
        return pl.ds(aligned(kept + j * size + bit * side), side)

    def other_side(j):
        return pl.ds(aligned(kept + j * size + (1 - bit) * side), side)

    def gather(j, s):
        return remote(
            total.at[j], result.at[own_rows(j)],
            gather_sems.at[0, j, s - 1], gather_sems.at[1, j, s - 1], in_group(along(s)),
        )

    def y_share(j):
        return remote(
            result.at[own_side(j)], result.at[own_side(j)],
            share_y_sems.at[0, j], share_y_sems.at[1, j], in_group(beside),
        )

    def back(j, i):
        there = own_side(j) if i == 0 else other_side(j)
        return remote(
            result.at[there], result.at[there],
            back_sems.at[0, j, i], back_sems.at[1, j, i], in_group(partner),
        )

    def piece(index):
        row = aligned(lax.rem(index, 8) * small_rows, 8)
        col = aligned((index // 8) * small_cols, LANES)
        return pl.ds(row, small_rows), pl.ds(col, small_cols)

    def small_out(s):
        return remote(
            small.at[piece(lax.rem(place + s, devices))], small_landed.at[s - 1],
            small_sems.at[0, s - 1], small_sems.at[1, s - 1],
            in_group(lax.rem(place + s, devices)),
        )

    def small_share(s):
        return remote(
            small_total, small_result.at[piece(place)],
            share_sems.at[0, s - 1], share_sems.at[1, s - 1],
            in_group(lax.rem(place + s, devices)),
        )

    def send_low():
        return remote(lows, lows_landed, cross_sems.at[0, 0], cross_sems.at[1, 0], across)

    def send_high(i):
        return remote(
            dx.at[i], dx_landed.at[i], cross_sems.at[0, 1 + i], cross_sems.at[1, 1 + i], across
        )

    def greet(barrier, other):
        pl.semaphore_signal(
            barrier, inc=1, device_id=other, device_id_type=pl.DeviceIdType.MESH
        )

    def load(source, target, i):
        return pltpu.make_async_copy(source, target, load_sems.at[i])

    enc_loads = [load(enc_up, ups.at[0], 0), load(enc_down, downs.at[0], 1)]
    dec_loads = [
        load(long_up, ups.at[0], 0), load(long_down, downs.at[0], 1),
        load(short_up, ups.at[1], 2), load(short_down, downs.at[1], 3),
    ]

    @pl.when(step == 0)
    def _():
        barrier = pltpu.get_barrier_semaphore()
        for s in range(1, devices):
            greet(barrier, in_group(lax.rem(place + s, devices)))

        @pl.when(is_encoder)
        def _():
            for copy in enc_loads:
                copy.start()

        @pl.when(jnp.logical_not(is_encoder))
        def _():
            for copy in dec_loads:
                copy.start()

    @pl.when(is_encoder & (step < pairs))
    def _():
        at = aligned(step * LANES, LANES)
        lanes = pl.ds(at, LANES)
        prefix_totals = attend_back_pair(
            q_ref, [k_ref], [v_ref], o_ref, inv_ref, [g0_ref, g1_ref, g2_ref], pk_ref, pv_ref,
            (pl_ref, ps_ref), dq.at[:, lanes], dk.at[:, lanes], dv.at[:, lanes], enc_segs,
        )
        small[0:PRE_PAD, lanes] = prefix_totals[0] * scale
        small[PRE_PAD : 2 * PRE_PAD, lanes] = prefix_totals[1] * scale

    @pl.when(step == 0)
    def _():
        barrier = pltpu.get_barrier_semaphore()

        def pack(up, down):
            mine[0:chunk] = (up * scale).astype(BF)
            down = (down * scale).astype(BF)
            mine[chunk:width, 0:chunk] = down[0:chunk]
            mine[chunk:width, chunk:width] = down[chunk:width]

        @pl.when(is_encoder)
        def _():
            for copy in enc_loads:
                copy.wait()
            pack(ups[0], downs[0])
            pl.semaphore_wait(barrier, devices - 1)
            greet(barrier, across)

        @pl.when(jnp.logical_not(is_encoder))
        def _():
            for copy in dec_loads:
                copy.wait()
            pack(ups[0] + ups[1], downs[0] + downs[1])
            pl.semaphore_wait(barrier, devices)
            greet(barrier, across)

        swap().start()

        @pl.when(jnp.logical_not(is_encoder))
        def _():
            low = width // 2
            lows[0, 0:TGT] = y0_ref[:, 0:low]
            lows[0, TGT : 2 * TGT] = y1_ref[:, 0:low]
            lows[1] = dt_ref[:, 0:low]
            send_low().start()
            small[0:PRE_PAD] = dpk_ref[...] * scale
            small[PRE_PAD : 2 * PRE_PAD] = dpv_ref[...] * scale

    @pl.when(step == 1)
    def _():
        swap().wait()
        half_sum[...] = (
            mine[pl.ds(kept, half)].astype(F32) + theirs[...].astype(F32)
        ).astype(BF)
        for j in range(min(2, slices)):
            y_send(j).start()

    for j in range(slices):

        @pl.when(step == 2 + j)
        def _(j=j):
            y_send(j).wait()
            if j + 2 < slices:
                y_send(j + 2).start()
            own = pl.ds(aligned(j * size + bit * side), side)
            y_sum[j] = (half_sum[own].astype(F32) + across_y[j].astype(F32)).astype(BF)
            for s in range(1, line):
                z_send(j, s).start()

        @pl.when(step == 4 + j)
        def _(j=j):
            summed = y_sum[j, pl.ds(aligned(at_line * part), part)].astype(F32)
            for s in range(1, line):
                z_send(j, s).wait()
                summed = summed + landed[j, s - 1].astype(F32)
            total[j] = summed.astype(BF)
            result[own_rows(j)] = total[j]
            for s in range(1, line):
                gather(j, s).start()

        @pl.when(step == 6 + j)
        def _(j=j):
            for s in range(1, line):
                gather(j, s).wait()
            y_share(j).start()
            back(j, 0).start()

        @pl.when(step == 8 + j)
        def _(j=j):
            y_share(j).wait()
            back(j, 1).start()

    @pl.when(step == pairs - 1)
    def _():
        @pl.when(is_encoder)
        def _():
            down_row = jnp.concatenate([enc_downb[...], jnp.zeros_like(enc_downb)], 1)
            small[PRE : PRE + 1] = enc_upb[...] * scale
            small[PRE + 1 : PRE + 2] = down_row * scale

        @pl.when(jnp.logical_not(is_encoder))
        def _():
            down_row = long_downb[...] + short_downb[...]
            down_row = jnp.concatenate([down_row, jnp.zeros_like(down_row)], 1)
            small[PRE : PRE + 1] = (long_upb[...] + short_upb[...]) * scale
            small[PRE + 1 : PRE + 2] = down_row * scale

        for s in range(1, devices):
            small_out(s).start()

    @pl.when(is_encoder & (step == pairs))
    def _():
        pl.semaphore_wait(pltpu.get_barrier_semaphore(), 1)

    @pl.when(is_encoder & (step >= pairs))
    def _():
        acc = jnp.concatenate([dfirst0_ref[...], dfirst1_ref[...], dfirst2_ref[...]], 0)
        for n, grad in enumerate((dq, dk, dv)):
            acc = acc + nt(grad[...], wqkv_ref[:, n * width : (n + 1) * width])
        dx[step - pairs] = acc.astype(BF)

    for i in range(2):

        @pl.when(is_encoder & (step == pairs + i))
        def _(i=i):
            send_high(i).start()

    @pl.when(step == pairs + 1)
    def _():
        own_rows_, own_cols = piece(place)
        summed = small[own_rows_, own_cols]
        for s in range(1, devices):
            small_out(s).wait()
            summed = summed + small_landed[s - 1]
        small_total[...] = summed
        small_result[own_rows_, own_cols] = summed
        for s in range(1, devices):
            small_share(s).start()

    @pl.when(step == pairs + 3)
    def _():
        for j in range(slices):
            for i in range(2):
                back(j, i).wait()
        o_up_ref[...] = result[0:chunk]
        o_down_ref[0:chunk] = result[chunk:width, 0:chunk]
        o_down_ref[chunk:width] = result[chunk:width, chunk:width]
        for s in range(1, devices):
            small_share(s).wait()
        o_prefix_ref[0] = small_result[0:PRE]
        o_prefix_ref[1] = small_result[PRE_PAD : PRE_PAD + PRE]
        o_upb_ref[...] = small_result[PRE : PRE + 1]
        o_downb_ref[...] = small_result[PRE + 1 : PRE + 2, 0:chunk]

        @pl.when(is_encoder)
        def _():
            for i in range(2):
                source_ref[:, i * tile : (i + 1) * tile] = dx[2 + i]
            send_low().wait_recv()
            y_ref[...] = lows_landed[0]
            target_ref[...] = lows_landed[1]
            for i in range(2):
                send_high(i).wait_send()

        @pl.when(jnp.logical_not(is_encoder))
        def _():
            low = width // 2
            y_ref[0:TGT] = y0_ref[:, low:width]
            y_ref[TGT : 2 * TGT] = y1_ref[:, low:width]
            target_ref[...] = dt_ref[:, low:width]
            send_low().wait_send()
            for i in range(2):
                send_high(i).wait_recv()
                source_ref[:, i * tile : (i + 1) * tile] = dx_landed[i]


def finish(saved, datts, dfirsts, w, adapters, dec_prefix, ys, dt):
    qkv, att, inv, weights = saved
    devices = lax.axis_size("dp")
    line = devices // 4
    slices = 16 // line
    rows, width = att.shape
    targets = dt.shape[0]
    pairs, tile = 8, 256
    half = width // 2
    side = half // slices // 2
    part = side // line
    small_rows, small_cols = small_shape(devices)

    def mine(value):
        return jnp.where(lax.axis_index("section") == 0, value, 0)

    def head(i):
        return mine(jnp.minimum(i, pairs - 1))

    def pair(offset):
        return pl.BlockSpec((rows, LANES), lambda i: (0, head(i) + offset))

    def at(i):
        return mine(jnp.where(i < pairs + 2, 2 + jnp.maximum(i - pairs, 0), i - pairs - 2))

    def once(shape):
        return pl.BlockSpec(shape, lambda i: (0,) * len(shape), pipeline_mode=pl.Buffered(1))

    anywhere = pl.BlockSpec(memory_space=pl.ANY)
    prefix_pair = pl.BlockSpec((PRE_PAD, LANES), lambda i: (0, head(i)))
    vmem = pltpu.VMEM
    dma = pltpu.SemaphoreType.DMA
    flat = [a for group in adapters for a in group]
    return pl.pallas_call(
        functools.partial(finish_kernel, devices=devices),
        grid=(pairs + 4,),
        in_specs=[pair(0), pair(8), pair(16), pair(0), pair(0)]
        + [pl.BlockSpec((ENC_ROWS, LANES), lambda i: (0, head(i)))] * 3
        + [prefix_pair] * 2
        + [
            pl.BlockSpec((2,) + p.shape[1:], lambda i: (head(i), 0, 0))
            for p in weights
        ]
        + [
            pl.BlockSpec((ENC_ROWS, tile), lambda i: (0, at(i))),
        ]
        * 3
        + [
            pl.BlockSpec((tile, 3 * width), lambda i: (at(i), 0)),
        ]
        + [anywhere if a.shape[0] > 1 else once(a.shape) for a in flat]
        + [once(a.shape) for a in (*dec_prefix, *ys, dt)],
        out_specs=[
            once((rows, half)), once((targets, half)), once((targets, half)),
            once((chunk, width)), once((width, chunk)),
            once((2, PRE, width)), once((1, width)), once((1, chunk)),
        ],
        out_shape=[
            jax.ShapeDtypeStruct((rows, half), BF),
            jax.ShapeDtypeStruct((targets, half), BF),
            jax.ShapeDtypeStruct((targets, half), BF),
            jax.ShapeDtypeStruct((chunk, width), BF),
            jax.ShapeDtypeStruct((width, chunk), BF),
            jax.ShapeDtypeStruct((2, PRE, width), F32),
            jax.ShapeDtypeStruct((1, width), F32),
            jax.ShapeDtypeStruct((1, chunk), F32),
        ],
        scratch_shapes=[
            vmem((rows, width), BF), vmem((rows, width), BF), vmem((rows, width), BF),
            vmem((2 * PRE_PAD, width), F32),
            vmem((2, chunk, width), F32), vmem((2, width, chunk), F32),
            vmem((width, width), BF), vmem((half, width), BF), vmem((half, width), BF),
            vmem((slices, side, width), BF), vmem((slices, side, width), BF),
            vmem((slices, line - 1, part, width), BF), vmem((slices, part, width), BF),
            vmem((width, width), BF),
            vmem((devices - 1, small_rows, small_cols), F32), vmem((small_rows, small_cols), F32),
            vmem((2 * PRE_PAD, width), F32),
            vmem((4, rows, tile), BF), vmem((2, rows, tile), BF),
            vmem((2, targets, half), BF), vmem((2, targets, half), BF),
            dma((4,)), dma((2,)), dma((2, slices)), dma((2, slices, line - 1)),
            dma((2, slices, line - 1)), dma((2, slices)), dma((2, slices, 2)),
            dma((2, devices - 1)), dma((2, devices - 1)), dma((2, 3)),
        ],
        compiler_params=pltpu.CompilerParams(
            vmem_limit_bytes=60 * 2**20, collective_id=0, has_side_effects=True
        ),
        name="finish",
    )(
        qkv, qkv, qkv, att, inv, *datts, *w["prefix"], *weights,
        *dfirsts, w["qkv"], *flat, *dec_prefix, *ys, dt,
    )


def blank_kernel(*refs):
    pass


def blanks(shapes):
    return pl.pallas_call(
        blank_kernel,
        out_shape=list(shapes),
        out_specs=[pl.BlockSpec(memory_space=pl.ANY)] * len(shapes),
        name="blank",
    )()


def on_section(is_encoder, encoder_work, decoder_work, *operands):
    enc_shapes, _ = jax.eval_shape(encoder_work, *operands)
    dec_shapes, _ = jax.eval_shape(decoder_work, *operands)

    def blank_like(shapes):
        leaves, tree = jax.tree.flatten(shapes)
        if not leaves:
            return shapes
        return jax.tree.unflatten(tree, blanks(leaves))

    def encoder_branch(*a):
        own, shared = encoder_work(*a)
        return own, blank_like(dec_shapes), shared

    def decoder_branch(*a):
        own, shared = decoder_work(*a)
        return blank_like(enc_shapes), own, shared

    return lax.cond(is_encoder, encoder_branch, decoder_branch, *operands)


def to_decoder(block):
    return lax.ppermute(block, "section", [(0, 1)])


def to_encoder(block):
    return lax.ppermute(block, "section", [(1, 0)])


def per_device(
    sources, targets, cotangent, source_lengths, target_lengths,
    attn_qkv, attn_out, ffn_in, ffn_out, norm_gains, prefix_pairs,
    adapt_down, adapt_down_bias, adapt_up, adapt_up_bias,
    cross_query, cross_pairs, cross_out, cross_gain,
):
    is_encoder = lax.axis_index("section") == 0
    prefix = jnp.pad(prefix_pairs[0], ((0, 0), (0, PRE_PAD - PRE), (0, 0)))
    w = dict(
        qkv=attn_qkv[0], out=attn_out[0], ffn_in=ffn_in[0], ffn_out=ffn_out[0],
        gains=norm_gains[0], prefix=(prefix[0], prefix[1]),
        down=adapt_down[0], down_bias=adapt_down_bias,
        up=adapt_up[0], up_bias=adapt_up_bias,
    )
    cross = dict(query=cross_query, pairs=cross_pairs, out=cross_out, gain=cross_gain[None])

    def at_encoder(work, *operands):
        return on_section(is_encoder, lambda *a: (work(*a), ()), lambda *a: ((), ()), *operands)[0]

    def at_decoder(work, *operands):
        return on_section(is_encoder, lambda *a: ((), ()), lambda *a: (work(*a), ()), *operands)[1]

    def at_both(enc_work, dec_work, *operands):
        return on_section(
            is_encoder, lambda *a: (enc_work(*a), ()), lambda *a: (dec_work(*a), ()), *operands
        )[:2]

    def encoder_start():
        qkv = product(sources, w["qkv"])
        att, inv, *weights = attend(
            source_lengths, *self_columns(qkv), w["prefix"], enc_segs, False, checked=True
        )
        return (qkv, att, inv, weights), enc_ffn(sources, att, w, 2)

    (saved, part2), (cq, kept) = at_both(
        encoder_start, lambda: decoder_self(targets, target_lengths, w, cross)
    )
    mem2 = to_decoder(part2[0])
    part1 = at_encoder(lambda saved: enc_ffn(sources, saved[1], w, 1), saved)
    mem1 = to_decoder(part1[0])

    def decoder_short(saved, mem2, cq, kept):
        kv2 = product(mem2, cross["pairs"])
        forward = cross_forward(source_lengths, cq, [kv2], 1)
        return kv2, forward, dec_ffn(
            target_lengths, kept[4], forward[0], cotangent, w, cross, 1
        )

    part0, (kv2, short, short_ffn) = at_both(
        lambda saved, *a: enc_ffn(sources, saved[1], w, 0),
        decoder_short, saved, mem2, cq, kept,
    )
    mem0 = to_decoder(part0[0])
    kv1 = at_decoder(lambda mem1: product(mem1, cross["pairs"]), mem1)

    def decoder_long(mem0, kv1, kv2, cq, kept):
        kvs = [product(mem0, cross["pairs"]), kv1, kv2]
        long = cross_forward(source_lengths, cq, kvs, 0)
        y, dsecond, dcatt, *adapter = dec_ffn(
            target_lengths, kept[4], long[0], cotangent, w, cross, 0
        )
        dcq, dck, dcv = cross_backward(cq, kvs, long, dcatt, 0)
        cuts = ((0, ENC_ROWS), (ENC_ROWS, ENC_ROWS), (2 * ENC_ROWS, SRC_LONG - 2 * ENC_ROWS))
        return back_product([dck, dcv], cross["pairs"], cuts=cuts), y, dsecond, dcq, adapter

    dmems, *long = at_decoder(decoder_long, mem0, kv1, kv2, cq, kept)
    dmem0, dmem1, dmem2 = [to_encoder(block) for block in dmems]

    def decoder_short_back(kv2, cq, short, dcatt):
        dcq, dck, dcv = cross_backward(cq, [kv2], short, dcatt, 1)
        return back_product([dck, dcv], cross["pairs"])[0], dcq

    short_y, short_second, short_dcatt, *short_adapter = short_ffn
    dmem_short, short_cq = at_decoder(decoder_short_back, kv2, cq, short, short_dcatt)
    dmem_short = to_encoder(dmem_short)

    def decoder_end(kept, *grads):
        return decoder_self_back(kept, grads[:2], grads[2:], w, cross)

    (long_y, long_second, long_cq, long_adapter) = long
    dt, dec_prefix = at_decoder(
        decoder_end, kept, long_second, short_second, long_cq, short_cq
    )
    dmem0, dt = lax.optimization_barrier((dmem0, dt))
    back0 = at_encoder(lambda dmem0, part0: enc_ffn_back([dmem0], part0, w), dmem0, part0)
    back1 = at_encoder(lambda dmem1, part1: enc_ffn_back([dmem1], part1, w), dmem1, part1)

    def encoder_end(dmem2, dmem_short, part0, part1, part2, back0, back1):
        back2 = enc_ffn_back([dmem2, dmem_short], part2, w)
        parts, backs = (part0, part1, part2), (back0, back1, back2)
        adapter = adapter_grads(
            [p[4] for p in parts], [p[3] for p in parts],
            [b[2] for b in backs], [b[3] for b in backs],
        )
        return back2, adapter

    back2, enc_adapter = at_encoder(
        encoder_end, dmem2, dmem_short, part0, part1, part2, back0, back1
    )
    backs = (back0, back1, back2)
    source_grad, y, target_grad, up, down, prefix_grad, up_bias, down_bias = finish(
        saved, [b[1] for b in backs], [b[0] for b in backs], w,
        [enc_adapter, long_adapter, short_adapter], dec_prefix, [long_y, short_y], dt,
    )
    return (
        y,
        source_grad,
        target_grad,
        prefix_grad[None],
        down.astype(F32)[None],
        down_bias,
        up.astype(F32)[None],
        up_bias,
    )


def solution(mesh):
    layer2, layer3, rows = P("section", None), P("section", None, None), P("dp", None)
    return jax.shard_map(
        per_device,
        mesh=mesh,
        in_specs=(
            rows, rows, rows, rows, rows,
            layer3, layer3, layer3, layer3, layer3,
            P("section", None, None, None),
            layer3, layer2, layer3, layer2,
            P(), P(), P(), P(),
        ),
        out_specs=(
            P("dp", "section"), P("dp", "section"), P("dp", "section"),
            P("section", None, None, None), layer3, layer2, layer3, layer2,
        ),
        check_vma=False,
    )
```

```python
import functools

import jax
import jax.numpy as jnp
from jax import lax
from jax.experimental import pallas as pl
from jax.experimental.pallas import tpu as pltpu
from jax.sharding import PartitionSpec as P

HD = 64
PRE = 30
PRE_PAD = 32
SRC_LONG = 768
SRC_SHORT = 96
TGT = 256
LANES = 128

BF = jnp.bfloat16
F32 = jnp.float32
norm_eps = 1e-05
big_negative = -1e30
adapter_scale = 4.0
chunk = 512
wide = 1024
ENC_ROWS = (SRC_LONG + SRC_SHORT) // 3
vmem_bytes = 56 * 2**20

phi_poly = (
    0.797869713181688,
    0.036392283539041996,
    -8.782472977701046e-05,
    -3.669384069669515e-05,
    1.4250308145882202e-06,
)


def nn(left, right):
    return lax.dot_general(left, right, (((1,), (0,)), ((), ())), preferred_element_type=F32)


def nt(left, right):
    return lax.dot_general(left, right, (((1,), (1,)), ((), ())), preferred_element_type=F32)


def tn(left, right):
    return lax.dot_general(left, right, (((0,), (0,)), ((), ())), preferred_element_type=F32)


def gelu_pair(values):
    square = values * values
    poly = phi_poly[4]
    for coefficient in phi_poly[3::-1]:
        poly = poly * square + coefficient
    half = 0.5 * jnp.tanh(values * poly) + 0.5
    density = jnp.exp(square * -0.5) * 0.3989422804014327
    return values * half, half + values * density


def row_tiles(rows, most=288):
    count = -(-rows // most)
    size = rows // count
    return [(i * size, size) for i in range(count)]


def norm_rows(values):
    centered = values - jnp.mean(values, axis=-1, keepdims=True)
    scale = lax.rsqrt(jnp.mean(centered * centered, axis=-1, keepdims=True) + norm_eps)
    return centered * scale, scale


def norm_rows_back(hat, scale, grad_hat):
    mean_grad = jnp.mean(grad_hat, axis=-1, keepdims=True)
    mean_dot = jnp.mean(grad_hat * hat, axis=-1, keepdims=True)
    return scale * (grad_hat - mean_grad - hat * mean_dot)


def params(limit=vmem_bytes):
    return pltpu.CompilerParams(vmem_limit_bytes=limit)


def whole(shape):
    return pl.BlockSpec(shape, lambda *g: (0,) * len(shape))


def product_kernel(x_ref, w_ref, o_ref):
    o_ref[...] = nn(x_ref[...], w_ref[...]).astype(BF)


def product(x, w, tile=1024):
    rows, depth = x.shape
    width = w.shape[1]
    return pl.pallas_call(
        product_kernel,
        grid=(width // tile,),
        in_specs=[whole((rows, depth)), pl.BlockSpec((depth, tile), lambda i: (0, i))],
        out_specs=pl.BlockSpec((rows, tile), lambda i: (0, i)),
        out_shape=jax.ShapeDtypeStruct((rows, width), BF),
        compiler_params=params(),
        name="product",
    )(x, w)


def back_product_kernel(*refs, parts, residual, cuts):
    grads = refs[:parts]
    w_ref = refs[parts]
    outs = refs[-len(cuts) :]
    total = None
    width = grads[0].shape[1]
    for i, grad in enumerate(grads):
        term = nt(grad[...], w_ref[:, i * width : (i + 1) * width])
        total = term if total is None else total + term
    if residual:
        total = total + refs[parts + 1][...]
    for (start, size), o_ref in zip(cuts, outs):
        o_ref[...] = total[start : start + size].astype(BF)


def back_product(grads, w, residual=None, tile=512, cuts=None):
    rows, width = grads[0].shape
    depth = w.shape[0]
    parts = len(grads)
    cuts = cuts or ((0, rows),)
    specs = [whole((rows, width))] * parts + [
        pl.BlockSpec((tile, parts * width), lambda i: (i, 0))
    ]
    args = list(grads) + [w]
    if residual is not None:
        specs.append(pl.BlockSpec((rows, tile), lambda i: (0, i)))
        args.append(residual)
    return pl.pallas_call(
        functools.partial(
            back_product_kernel, parts=parts, residual=residual is not None, cuts=cuts
        ),
        grid=(depth // tile,),
        in_specs=specs,
        out_specs=[pl.BlockSpec((size, tile), lambda i: (0, i)) for _, size in cuts],
        out_shape=[jax.ShapeDtypeStruct((size, depth), BF) for _, size in cuts],
        compiler_params=params(),
        name="back_product",
    )(*args)


def head_lanes(head):
    lane = lax.broadcasted_iota(jnp.int32, (1, LANES), 1)
    own = (lane < HD) if head == 0 else (lane >= HD)
    first = HD if head == 0 else 0
    return own, lane == first, lane == first + 1


def bf(value):
    return jnp.asarray(value, BF)


def rows_of(refs, start, count):
    parts = []
    for ref in refs:
        size = ref.shape[0]
        low, high = max(start, 0), min(start + count, size)
        if low < high:
            parts.append(ref[low:high])
        start -= size
    return parts


def stacked(refs, prefix_ref, start, count):
    parts = rows_of(refs, start, count)
    if prefix_ref is not None:
        parts.append(prefix_ref[...])
    return parts[0] if len(parts) == 1 else jnp.concatenate(parts, 0)


def attend_pair(*refs, segs, prefix, causal, pieces, which, checked):
    len_ref, q_ref = refs[:2]
    k_refs, v_refs = refs[2 : 2 + pieces], refs[2 + pieces : 2 + 2 * pieces]
    at = 2 + 2 * pieces
    pk_ref = pv_ref = None
    if prefix:
        pk_ref, pv_ref = refs[at : at + 2]
        at += 2
    o_ref, inv_ref = refs[at : at + 2]
    p_refs = refs[at + 2 :]

    def work(peaked):
        for seg, (q0, nq, k0, nk) in enumerate(segs):
            keys = stacked(k_refs, pk_ref, k0, nk)
            values = stacked(v_refs, pv_ref, k0, nk)
            count = keys.shape[0]
            row = lax.broadcasted_iota(jnp.int32, (count, 1), 0)
            seen = row < jnp.minimum(len_ref[0, which + seg], nk)
            if prefix:
                seen = seen | ((row >= nk) & (row < nk + PRE))
            queries = q_ref[q0 : q0 + nq] * bf(HD**-0.5)
            out = inv = None
            across = nq >= 4 * LANES
            outs, invs = [], []
            if across:
                turned = values.T
                ones = jnp.ones((16, count), BF)
            for head in range(2):
                own, first, _ = head_lanes(head)
                k_own = jnp.where(own, keys, jnp.where(first & ~seen, bf(big_negative), bf(0)))
                q_own = jnp.where(own, queries, jnp.where(first, bf(1), bf(0)))
                scores = nt(k_own, q_own)
                if causal:
                    key_at = lax.broadcasted_iota(jnp.int32, scores.shape, 0)
                    query_at = lax.broadcasted_iota(jnp.int32, scores.shape, 1)
                    allowed = (key_at <= query_at) | (key_at >= nk)
                    scores = jnp.where(allowed, scores, big_negative)
                if peaked:
                    scores = scores - jnp.max(scores, axis=0, keepdims=True)
                weights = jnp.exp(scores).astype(BF)
                p_refs[seg][head] = weights
                if across:
                    rows = jnp.concatenate([turned[head * HD : (head + 1) * HD], ones], 0)
                    mixed = nn(rows, weights)
                    inverse = 1.0 / mixed[HD : HD + 1]
                    outs.append(mixed[:HD] * inverse)
                    invs.append(jnp.broadcast_to(inverse, (HD, nq)))
                    continue
                mixed = tn(weights, jnp.where(own, values, bf(1)))
                inverse = 1.0 / pltpu.roll(mixed, HD, 1)
                mixed = mixed * inverse
                out = mixed if out is None else jnp.where(own, mixed, out)
                inv = inverse if inv is None else jnp.where(own, inverse, inv)
            if across:
                out = jnp.concatenate(outs, 0).T
                inv = jnp.concatenate(invs, 0).T
            o_ref[q0 : q0 + nq] = out.astype(BF)
            inv_ref[q0 : q0 + nq] = inv

    if not checked:
        work(True)
        return

    limit = 50.0**2
    head_row = lax.broadcasted_iota(jnp.int32, (LANES, LANES), 0) // HD
    head_col = lax.broadcasted_iota(jnp.int32, (LANES, LANES), 1) // HD
    same_head = jnp.where(head_row == head_col, 1.0, 0.0).astype(BF)

    def largest(array):
        square = (array.astype(F32) * array.astype(F32)).astype(BF)
        return jnp.max(nn(square, same_head), axis=0, keepdims=True)

    key_peak = largest(k_refs[0][...])
    for ref in k_refs[1:]:
        key_peak = jnp.maximum(key_peak, largest(ref[...]))
    if prefix:
        key_peak = jnp.maximum(key_peak, largest(pk_ref[...]))
    small = jnp.max(largest(q_ref[...]) * key_peak) * (1.0 / HD) <= limit

    @pl.when(small)
    def _():
        work(False)

    @pl.when(jnp.logical_not(small))
    def _():
        work(True)


def lane_views(refs, group, j):
    views = []
    for ref in refs:
        if len(ref.shape) == 2:
            views.append(ref.at[:, j * LANES : (j + 1) * LANES])
        else:
            views.append(ref.at[2 * j : 2 * j + 2])
    return views


def attend_kernel(len_ref, *refs, group, **kw):
    for j in range(group):
        attend_pair(len_ref, *lane_views(refs, group, j), **kw)


def column_spec(rows, offset, row_block=0, group=1):
    return pl.BlockSpec((rows, group * LANES), lambda h: (row_block, h + offset // group))


def attend(lengths, q, keys, values, prefixes, segs, causal, which=0, group=1, checked=False):
    pairs = 8
    q_rows = q[1]
    prefix = prefixes is not None
    extra = PRE_PAD if prefix else 0
    specs = [pl.BlockSpec(memory_space=pltpu.SMEM)]
    args = [lengths]
    for array, rows, block, offset in [q, *keys, *values]:
        specs.append(column_spec(rows, offset, block, group))
        args.append(array)
    if prefix:
        specs += [column_spec(PRE_PAD, 0, 0, group)] * 2
        args += list(prefixes)
    weight_shapes = [(2 * pairs, nk + extra, nq) for _, nq, _, nk in segs]
    return pl.pallas_call(
        functools.partial(
            attend_kernel, group=group, segs=segs, prefix=prefix, causal=causal, pieces=len(keys), which=which,
            checked=checked,
        ),
        grid=(pairs // group,),
        in_specs=specs,
        out_specs=[column_spec(q_rows, 0, 0, group)] * 2
        + [pl.BlockSpec((2 * group,) + s[1:], lambda h: (h, 0, 0)) for s in weight_shapes],
        out_shape=[
            jax.ShapeDtypeStruct((q_rows, pairs * LANES), BF),
            jax.ShapeDtypeStruct((q_rows, pairs * LANES), F32),
        ]
        + [jax.ShapeDtypeStruct(s, BF) for s in weight_shapes],
        compiler_params=params(),
        name="attend",
    )(*args)


def attend_back_pair(
    q_ref, k_refs, v_refs, o_ref, inv_ref, g_refs, pk_ref, pv_ref, p_refs, dq_ref, dk_ref, dv_ref, segs
):
    prefix_totals = [None, None]
    scale = HD**-0.5
    for seg, (q0, nq, k0, nk) in enumerate(segs):
        keys = stacked(k_refs, pk_ref, k0, nk)
        values = stacked(v_refs, pv_ref, k0, nk)
        queries = q_ref[q0 : q0 + nq]
        grads = stacked(g_refs, None, q0, nq).astype(F32) * inv_ref[q0 : q0 + nq]
        grads_low = grads.astype(BF)
        dots = grads * o_ref[q0 : q0 + nq].astype(F32)
        dq = dk = dv = None
        across = nq >= LANES and keys.shape[0] >= 4 * LANES
        turned_grads = []
        if across:
            turned = keys.T
        for head in range(2):
            own, first, second = head_lanes(head)
            row_dot = -jnp.sum(jnp.where(own, dots, 0.0), axis=1, keepdims=True)
            high = row_dot.astype(BF)
            rest = (row_dot - high.astype(F32)).astype(BF)
            g_own = jnp.where(
                own, grads_low, jnp.where(first, high, jnp.where(second, rest, bf(0)))
            )
            v_own = jnp.where(own, values, jnp.where(first | second, bf(1), bf(0)))
            weights = p_refs[seg][head]
            score_grad = (weights.astype(F32) * nt(v_own, g_own)).astype(BF)
            dv_head = nn(weights, grads_low)
            dk_head = nn(score_grad, queries)
            dq_head = None if across else tn(score_grad, keys)
            if across:
                turned_grads.append(nn(turned[head * HD : (head + 1) * HD], score_grad))
            if not across:
                dq = dq_head if dq is None else jnp.where(own, dq_head, dq)
            dk = dk_head if dk is None else jnp.where(own, dk_head, dk)
            dv = dv_head if dv is None else jnp.where(own, dv_head, dv)
        if across:
            dq = jnp.concatenate(turned_grads, 0).T
        dk = dk * scale
        dq_ref[q0 : q0 + nq] = (dq * scale).astype(BF)
        at = k0 - segs[0][2]
        dk_ref[at : at + nk] = dk[:nk].astype(BF)
        dv_ref[at : at + nk] = dv[:nk].astype(BF)
        if pk_ref is not None:
            for i, grad in enumerate((dk, dv)):
                part = grad[nk:]
                prefix_totals[i] = part if seg == 0 else prefix_totals[i] + part
    return prefix_totals


def attend_back_kernel(*refs, group, **kw):
    for j in range(group):
        attend_back_views(*lane_views(refs, group, j), **kw)


def attend_back_views(*refs, segs, prefix, pieces):
    q_ref, o_ref, inv_ref, g_ref = refs[:4]
    k_refs, v_refs = refs[4 : 4 + pieces], refs[4 + pieces : 4 + 2 * pieces]
    at = 4 + 2 * pieces
    pk_ref = pv_ref = None
    if prefix:
        pk_ref, pv_ref = refs[at : at + 2]
        at += 2
    outs = refs[at + len(segs) :]
    totals = attend_back_pair(
        q_ref, k_refs, v_refs, o_ref, inv_ref, [g_ref], pk_ref, pv_ref,
        refs[at : at + len(segs)], *outs[:3], segs,
    )
    if prefix:
        outs[3][...] = totals[0]
        outs[4][...] = totals[1]


def attend_back(q, keys, values, prefixes, attended, inverse, grad, weights, segs, group=2):
    pairs = 8
    q_rows = q[1]
    k_rows = sum(nk for _, _, _, nk in segs)
    prefix = prefixes is not None
    specs, args = [], []
    own = [(a, q_rows, 0, 0) for a in (attended, inverse, grad)]
    for array, rows, block, offset in [q, *own, *keys, *values]:
        specs.append(column_spec(rows, offset, block, group))
        args.append(array)
    if prefix:
        specs += [column_spec(PRE_PAD, 0, 0, group)] * 2
        args += list(prefixes)
    specs += [pl.BlockSpec((2 * group,) + w.shape[1:], lambda h: (h, 0, 0)) for w in weights]
    args += list(weights)
    out_specs = [column_spec(n, 0, 0, group) for n in (q_rows, k_rows, k_rows)]
    out_shape = [
        jax.ShapeDtypeStruct((q_rows, pairs * LANES), BF),
        jax.ShapeDtypeStruct((k_rows, pairs * LANES), BF),
        jax.ShapeDtypeStruct((k_rows, pairs * LANES), BF),
    ]
    if prefix:
        out_specs += [column_spec(PRE_PAD, 0, 0, group)] * 2
        out_shape += [jax.ShapeDtypeStruct((PRE_PAD, pairs * LANES), F32)] * 2
    return pl.pallas_call(
        functools.partial(
            attend_back_kernel, group=group, segs=segs, prefix=prefix, pieces=len(keys)
        ),
        grid=(pairs // group,),
        in_specs=specs,
        out_specs=out_specs,
        out_shape=out_shape,
        compiler_params=params(),
        name="attend_back",
    )(*args)


class Weights:
    def __init__(self, sources, targets, sems):
        self.sources, self.targets, self.sems = sources, targets, sems

    def copy(self, name, part=None):
        source, target = self.sources[name], self.targets[name]
        first = list(self.sources).index(name)
        sem = self.sems.at[first, 0 if part is None else part]
        if part is not None:
            cut = pl.ds(pl.multiple_of(part * wide, wide), wide)
            index = (slice(None), cut) if name == "in" else (cut, slice(None))
            source, target = source.at[index], target.at[index]
        return pltpu.make_async_copy(source, target, sem)

    def wait(self, name, part=None):
        self.copy(name, part).wait()

    def part(self, name, part):
        cut = pl.ds(pl.multiple_of(part * wide, wide), wide)
        index = (slice(None), cut) if name == "in" else (cut, slice(None))
        return self.targets[name].at[index]


def weight_scratch(arrays, parts):
    return [pltpu.VMEM(a.shape, BF) for a in arrays] + [
        pltpu.SemaphoreType.DMA((len(arrays), parts))
    ]


def ffn_step(low_ref, acc_ref, in_ref, out_ref, slope_ref, act_ref, bias_ref, scale):
    for start, size in row_tiles(low_ref.shape[0]):
        rows = slice(start, start + size)
        hidden = nn(low_ref[rows], in_ref[...])
        if bias_ref is not None:
            hidden = hidden + bias_ref[...]
        active, slope = gelu_pair(hidden)
        slope_ref[rows] = slope.astype(BF)
        active = active.astype(BF)
        if act_ref is not None:
            act_ref[rows] = active
        term = nn(active, out_ref[...])
        acc_ref[rows] += term if scale is None else scale * term


def enc_ffn_kernel(
    x_ref, att_ref, gain_ref, downb_ref, upb_ref, wo_hbm, in_hbm, out_hbm, down_hbm, up_hbm,
    mem_ref, slope_ref, pre_slope_ref, act_ref, low_ref, scales_ref,
    acc_ref, wo_ref, in_ref, out_ref, down_ref, up_ref, sems,
):
    weights = Weights(
        {"wo": wo_hbm, "in": in_hbm, "out": out_hbm, "down": down_hbm, "up": up_hbm},
        {"wo": wo_ref, "in": in_ref, "out": out_ref, "down": down_ref, "up": up_ref},
        sems,
    )

    weights.copy("wo").start()
    for part in range(in_ref.shape[1] // wide):
        weights.copy("in", part).start()
        weights.copy("out", part).start()
    weights.copy("down").start()
    weights.copy("up").start()
    weights.wait("wo")
    first = x_ref[...].astype(F32) + nn(att_ref[...], wo_ref[...])
    hat, scale = norm_rows(first)
    normed = hat * gain_ref[0:1]
    acc_ref[...] = normed
    low_ref[...] = normed.astype(BF)
    scales_ref[:, 0:1] = scale

    def one_part(part, carry):
        weights.wait("in", part)
        weights.wait("out", part)
        cols = pl.ds(pl.multiple_of(part * wide, wide), wide)
        ffn_step(
            low_ref, acc_ref, in_ref.at[:, cols], out_ref.at[cols], slope_ref.at[:, cols],
            None, None, None,
        )
        return carry

    lax.fori_loop(0, in_ref.shape[1] // wide, one_part, 0)

    weights.wait("down")
    weights.wait("up")
    ffn_step(low_ref, acc_ref, down_ref, up_ref, pre_slope_ref, act_ref, downb_ref, adapter_scale)
    hat, scale = norm_rows(acc_ref[...] + adapter_scale * upb_ref[...])
    mem_ref[...] = (hat * gain_ref[1:2]).astype(BF)
    scales_ref[:, 1:2] = scale


def enc_ffn(x, att, w, part):
    width = x.shape[1]
    rows = ENC_ROWS
    hidden = w["ffn_in"].shape[1]
    steps = hidden // wide
    weights = [w["out"], w["ffn_in"], w["ffn_out"], w["down"], w["up"]]
    return pl.pallas_call(
        enc_ffn_kernel,
        grid=(1,),
        in_specs=[
            pl.BlockSpec((rows, width), lambda i: (part, 0)),
            pl.BlockSpec((rows, width), lambda i: (part, 0)),
            whole((2, width)),
            whole((1, chunk)),
            whole((1, width)),
        ]
        + [pl.BlockSpec(memory_space=pl.ANY)] * len(weights),
        out_specs=[
            whole((rows, width)),
            whole((rows, hidden)),
            whole((rows, chunk)),
            whole((rows, chunk)),
            whole((rows, width)),
            whole((rows, LANES)),
        ],
        out_shape=[
            jax.ShapeDtypeStruct((rows, width), BF),
            jax.ShapeDtypeStruct((rows, hidden), BF),
            jax.ShapeDtypeStruct((rows, chunk), BF),
            jax.ShapeDtypeStruct((rows, chunk), BF),
            jax.ShapeDtypeStruct((rows, width), BF),
            jax.ShapeDtypeStruct((rows, LANES), F32),
        ],
        scratch_shapes=[pltpu.VMEM((rows, width), F32)] + weight_scratch(weights, steps),
        compiler_params=params(),
        name="enc_ffn",
    )(x, att, w["gains"], w["down_bias"], w["up_bias"], *weights)


def ffn_back_step(grad_ref, acc_ref, in_ref, out_ref, slope_ref):
    for start, size in row_tiles(grad_ref.shape[0]):
        rows = slice(start, start + size)
        pre = (nt(grad_ref[rows], out_ref[...]) * slope_ref[rows].astype(F32)).astype(BF)
        acc_ref[rows] += nt(pre, in_ref[...])


def adapter_back(grad_ref, acc_ref, low_ref, act_ref, slope_ref, down_ref, up_ref, outs, pre_ref):
    ddown_ref, ddownb_ref, dup_ref, dupb_ref = outs
    total = None
    for start, size in row_tiles(grad_ref.shape[0]):
        rows = slice(start, start + size)
        back = adapter_scale * nt(grad_ref[rows], up_ref[...])
        pre = (back * slope_ref[rows].astype(F32)).astype(BF)
        pre_ref[rows] = pre
        sums = jnp.sum(pre.astype(F32), axis=0, keepdims=True)
        total = sums if total is None else total + sums
        acc_ref[rows] += nt(pre, down_ref[...])
    ddownb_ref[...] = total
    ddown_ref[...] = tn(low_ref[...], pre_ref[...])
    dup_ref[...] = adapter_scale * tn(act_ref[...], grad_ref[...])
    dupb_ref[...] = adapter_scale * jnp.sum(grad_ref[...].astype(F32), axis=0, keepdims=True)


def enc_ffn_back_kernel(*refs, pieces):
    enc_ffn_back_body(refs[:pieces], *refs[pieces:])


def enc_ffn_back_body(
    dmem_refs, mem_ref, low_ref, scales_ref, gain_ref, slope_ref, pre_slope_ref,
    up_hbm, down_hbm, in_hbm, out_hbm, wo_hbm,
    dfirst_ref, datt_ref, grad_ref, pre_ref,
    acc_ref, up_ref, down_ref, in_ref, out_ref, wo_ref, sems,
):
    weights = Weights(
        {"up": up_hbm, "down": down_hbm, "in": in_hbm, "out": out_hbm, "wo": wo_hbm},
        {"up": up_ref, "down": down_ref, "in": in_ref, "out": out_ref, "wo": wo_ref},
        sems,
    )

    weights.copy("up").start()
    weights.copy("down").start()
    for part in range(in_ref.shape[1] // wide):
        weights.copy("out", part).start()
        weights.copy("in", part).start()
    weights.copy("wo").start()
    gain = gain_ref[1:2]
    hat = mem_ref[...].astype(F32) / gain
    dmem = stacked(dmem_refs, None, 0, ENC_ROWS).astype(F32)
    grad = norm_rows_back(hat, scales_ref[:, 1:2], dmem * gain)
    low = grad.astype(BF)
    grad_ref[...] = low
    weights.wait("up")
    back = adapter_scale * nt(low, up_ref[...])
    pre = (back * pre_slope_ref[...].astype(F32)).astype(BF)
    pre_ref[...] = pre
    weights.wait("down")
    acc_ref[...] = grad + nt(pre, down_ref[...])

    def one_part(part, carry):
        weights.wait("out", part)
        weights.wait("in", part)
        cols = pl.ds(pl.multiple_of(part * wide, wide), wide)
        ffn_back_step(
            grad_ref, acc_ref, in_ref.at[:, cols], out_ref.at[cols], slope_ref.at[:, cols]
        )
        return carry

    lax.fori_loop(0, in_ref.shape[1] // wide, one_part, 0)

    gain = gain_ref[0:1]
    hat = low_ref[...].astype(F32) / gain
    grad = norm_rows_back(hat, scales_ref[:, 0:1], acc_ref[...] * gain)
    dfirst_ref[...] = grad
    weights.wait("wo")
    datt_ref[...] = nt(grad.astype(BF), wo_ref[...]).astype(BF)


def enc_ffn_back(dmems, saved, w):
    mem, slope, pre_slope, act, low, scales = saved
    rows, width = mem.shape
    hidden = w["ffn_in"].shape[1]
    steps = hidden // wide
    weights = [w["up"], w["down"], w["ffn_in"], w["ffn_out"], w["out"]]
    return pl.pallas_call(
        functools.partial(enc_ffn_back_kernel, pieces=len(dmems)),
        grid=(1,),
        in_specs=[whole(d.shape) for d in dmems]
        + [
            whole((rows, width)),
            whole((rows, width)),
            whole((rows, LANES)),
            whole((2, width)),
            whole((rows, hidden)),
            whole((rows, chunk)),
        ]
        + [pl.BlockSpec(memory_space=pl.ANY)] * len(weights),
        out_specs=[
            whole((rows, width)),
            whole((rows, width)),
            whole((rows, width)),
            whole((rows, chunk)),
        ],
        out_shape=[
            jax.ShapeDtypeStruct((rows, width), F32),
            jax.ShapeDtypeStruct((rows, width), BF),
            jax.ShapeDtypeStruct((rows, width), BF),
            jax.ShapeDtypeStruct((rows, chunk), BF),
        ],
        scratch_shapes=[pltpu.VMEM((rows, width), F32)] + weight_scratch(weights, steps),
        compiler_params=params(),
        name="enc_ffn_back",
    )(*dmems, mem, low, scales, w["gains"], slope, pre_slope, *weights)


def adapter_grads_kernel(*refs, parts):
    groups = [refs[n * parts : (n + 1) * parts] for n in range(4)]
    low, act, grad, pre = [jnp.concatenate([r[...] for r in g], 0) for g in groups]
    ddown_ref, ddownb_ref, dup_ref, dupb_ref = refs[4 * parts :]
    ddown_ref[...] = tn(low, pre)
    ddownb_ref[...] = jnp.sum(pre.astype(F32), axis=0, keepdims=True)
    dup_ref[...] = adapter_scale * tn(act, grad)
    dupb_ref[...] = adapter_scale * jnp.sum(grad.astype(F32), axis=0, keepdims=True)


def adapter_grads(lows, acts, grads, pres):
    width = lows[0].shape[1]
    return pl.pallas_call(
        functools.partial(adapter_grads_kernel, parts=len(lows)),
        out_shape=[
            jax.ShapeDtypeStruct((width, chunk), F32),
            jax.ShapeDtypeStruct((1, chunk), F32),
            jax.ShapeDtypeStruct((chunk, width), F32),
            jax.ShapeDtypeStruct((1, width), F32),
        ],
        compiler_params=params(),
        name="adapter_grads",
    )(*lows, *acts, *grads, *pres)


def dec_mid_kernel(x_ref, att_ref, wo_ref, gain_ref, wq_ref, n_ref, scale_ref, cq_ref):
    for start, size in row_tiles(x_ref.shape[0], 256):
        rows = slice(start, start + size)
        first = x_ref[rows].astype(F32) + nn(att_ref[rows], wo_ref[...])
        hat, scale = norm_rows(first)
        normed = hat * gain_ref[0:1]
        n_ref[rows] = normed
        scale_ref[rows, 0:1] = scale
        cq_ref[rows] = nn(normed.astype(BF), wq_ref[...]).astype(BF)


def dec_mid(x, att, w, cross):
    rows, width = x.shape
    return pl.pallas_call(
        dec_mid_kernel,
        out_shape=[
            jax.ShapeDtypeStruct((rows, width), F32),
            jax.ShapeDtypeStruct((rows, LANES), F32),
            jax.ShapeDtypeStruct((rows, width), BF),
        ],
        compiler_params=params(),
        name="dec_mid",
    )(x, att, w["out"], w["gains"], cross["query"])


def dec_ffn_kernel(
    len_ref, n_ref, catt_ref, cot_ref, cgain_ref, gain_ref, downb_ref, upb_ref,
    wco_hbm, in_hbm, out_hbm, down_hbm, up_hbm,
    y_ref, dsecond_ref, dcatt_ref, ddown_ref, ddownb_ref, dup_ref, dupb_ref,
    acc_ref, low_ref, grad_ref, slope_ref, pre_slope_ref, act_ref, pre_ref, scale_ref,
    wco_ref, in_ref, out_ref, down_ref, up_ref, sems,
    *, steps, which,
):
    weights = Weights(
        {"wco": wco_hbm, "in": in_hbm, "out": out_hbm, "down": down_hbm, "up": up_hbm},
        {"wco": wco_ref, "in": in_ref, "out": out_ref, "down": down_ref, "up": up_ref},
        sems,
    )

    weights.copy("wco").start()
    for part in range(steps):
        weights.copy("in", part).start()
        weights.copy("out", part).start()
    weights.copy("down").start()
    weights.copy("up").start()
    weights.wait("wco")
    second = n_ref[...] + nn(catt_ref[...], wco_ref[...])
    hat, scale = norm_rows(second)
    middle = hat * cgain_ref[...]
    acc_ref[...] = middle
    low_ref[...] = middle.astype(BF)
    scale_ref[:, 0:1] = scale

    def forward(part, carry):
        weights.wait("in", part)
        weights.wait("out", part)
        ffn_step(
            low_ref, acc_ref, weights.part("in", part), weights.part("out", part),
            slope_ref.at[part], None, None, None,
        )
        return carry

    lax.fori_loop(0, steps, forward, 0)

    weights.wait("down")
    weights.wait("up")
    ffn_step(
        low_ref, acc_ref, down_ref, up_ref, pre_slope_ref, act_ref, downb_ref, adapter_scale
    )
    gain = gain_ref[1:2]
    hat, scale = norm_rows(acc_ref[...] + adapter_scale * upb_ref[...])
    row = lax.broadcasted_iota(jnp.int32, (low_ref.shape[0], 1), 0)
    valid = row < len_ref[0, which]
    y_ref[...] = jnp.where(valid, hat * gain, 0.0).astype(BF)
    cot = jnp.where(valid, cot_ref[...].astype(F32), 0.0)
    grad = norm_rows_back(hat, scale, cot * gain)
    acc_ref[...] = grad
    grad_ref[...] = grad.astype(BF)
    adapter_back(
        grad_ref, acc_ref, low_ref, act_ref, pre_slope_ref, down_ref, up_ref,
        (ddown_ref, ddownb_ref, dup_ref, dupb_ref), pre_ref,
    )

    def backward(part, carry):
        ffn_back_step(
            grad_ref, acc_ref, weights.part("in", part), weights.part("out", part),
            slope_ref.at[part],
        )
        return carry

    lax.fori_loop(0, steps, backward, 0)

    gain = cgain_ref[...]
    hat = low_ref[...].astype(F32) / gain
    grad = norm_rows_back(hat, scale_ref[:, 0:1], acc_ref[...] * gain)
    dsecond_ref[...] = grad
    dcatt_ref[...] = nt(grad.astype(BF), wco_ref[...]).astype(BF)


def dec_ffn(lengths, n, catt, cot, w, cross, which):
    rows, width = catt.shape
    hidden = w["ffn_in"].shape[1]
    steps = hidden // wide
    weights = [cross["out"], w["ffn_in"], w["ffn_out"], w["down"], w["up"]]
    return pl.pallas_call(
        functools.partial(dec_ffn_kernel, steps=steps, which=which),
        grid=(1,),
        in_specs=[
            pl.BlockSpec(memory_space=pltpu.SMEM),
            pl.BlockSpec((rows, width), lambda i: (which, 0)),
            whole((rows, width)),
            pl.BlockSpec((rows, width), lambda i: (which, 0)),
            whole((1, width)),
            whole((2, width)),
            whole((1, chunk)),
            whole((1, width)),
        ]
        + [pl.BlockSpec(memory_space=pl.ANY)] * len(weights),
        out_specs=[
            whole((rows, width)),
            whole((rows, width)),
            whole((rows, width)),
            whole((width, chunk)),
            whole((1, chunk)),
            whole((chunk, width)),
            whole((1, width)),
        ],
        out_shape=[
            jax.ShapeDtypeStruct((rows, width), BF),
            jax.ShapeDtypeStruct((rows, width), F32),
            jax.ShapeDtypeStruct((rows, width), BF),
            jax.ShapeDtypeStruct((width, chunk), F32),
            jax.ShapeDtypeStruct((1, chunk), F32),
            jax.ShapeDtypeStruct((chunk, width), F32),
            jax.ShapeDtypeStruct((1, width), F32),
        ],
        scratch_shapes=[
            pltpu.VMEM((rows, width), F32),
            pltpu.VMEM((rows, width), BF),
            pltpu.VMEM((rows, width), BF),
            pltpu.VMEM((steps, rows, wide), BF),
            pltpu.VMEM((rows, chunk), BF),
            pltpu.VMEM((rows, chunk), BF),
            pltpu.VMEM((rows, chunk), BF),
            pltpu.VMEM((rows, LANES), F32),
        ]
        + weight_scratch(weights, steps),
        compiler_params=params(),
        name="dec_ffn",
    )(
        lengths, n, catt, cot, cross["gain"], w["gains"], w["down_bias"], w["up_bias"], *weights
    )


def dec_mid_back_kernel(
    dsecond0_ref, dsecond1_ref, dcq0_ref, dcq1_ref, wq_ref, n_ref, scale_ref, gain_ref, wo_ref,
    dfirst_ref, datt_ref,
):
    for pair, (dsecond_ref, dcq_ref) in enumerate(
        ((dsecond0_ref, dcq0_ref), (dsecond1_ref, dcq1_ref))
    ):
        rows = slice(pair * TGT, (pair + 1) * TGT)
        gain = gain_ref[0:1]
        total = dsecond_ref[...] + nt(dcq_ref[...], wq_ref[...])
        grad = norm_rows_back(n_ref[rows] / gain, scale_ref[rows, 0:1], total * gain)
        dfirst_ref[rows] = grad
        datt_ref[rows] = nt(grad.astype(BF), wo_ref[...]).astype(BF)


def dec_mid_back(dseconds, dcqs, n, scale, w, cross):
    rows, width = n.shape
    return pl.pallas_call(
        dec_mid_back_kernel,
        out_shape=[
            jax.ShapeDtypeStruct((rows, width), F32),
            jax.ShapeDtypeStruct((rows, width), BF),
        ],
        compiler_params=params(),
        name="dec_mid_back",
    )(*dseconds, *dcqs, cross["query"], n, scale, w["gains"], w["out"])


enc_segs = ((0, SRC_LONG, 0, SRC_LONG), (SRC_LONG, SRC_SHORT, SRC_LONG, SRC_SHORT))
dec_segs = ((0, TGT, 0, TGT), (TGT, TGT, TGT, TGT))
cross_segs = (((0, TGT, 0, SRC_LONG),), ((0, TGT, SRC_LONG % ENC_ROWS, SRC_SHORT),))


def self_columns(qkv):
    rows = qkv.shape[0]
    return (qkv, rows, 0, 0), [(qkv, rows, 0, 8)], [(qkv, rows, 0, 16)]


def cross_columns(cq, kvs, which):
    return (
        (cq, TGT, which, 0),
        [(kv, ENC_ROWS, 0, 0) for kv in kvs],
        [(kv, ENC_ROWS, 0, 8) for kv in kvs],
    )


def decoder_self(t, lengths, w, cross):
    qkv = product(t, w["qkv"])
    att, inv, *weights = attend(lengths, *self_columns(qkv), w["prefix"], dec_segs, True, group=2)
    n, scale, cq = dec_mid(t, att, w, cross)
    return cq, (qkv, att, inv, weights, n, scale)


def cross_forward(lengths, cq, kvs, which):
    return attend(
        lengths, *cross_columns(cq, kvs, which), None, cross_segs[which], False, which, group=2
    )


def cross_backward(cq, kvs, forward, dcatt, which):
    catt, inv, *weights = forward
    return attend_back(
        *cross_columns(cq, kvs, which), None, catt, inv, dcatt, weights, cross_segs[which]
    )


def decoder_self_back(kept, dseconds, dcqs, w, cross):
    qkv, att, inv, weights, n, scale = kept
    dfirst, datt = dec_mid_back(dseconds, dcqs, n, scale, w, cross)
    dq, dk, dv, *dprefix = attend_back(
        *self_columns(qkv), w["prefix"], att, inv, datt, weights, dec_segs
    )
    return back_product([dq, dk, dv], w["qkv"], dfirst)[0], dprefix


def small_shape(devices):
    return 8, 8 * (2 * chunk) // devices


def finish_kernel(
    q_ref, k_ref, v_ref, o_ref, inv_ref, g0_ref, g1_ref, g2_ref, pk_ref, pv_ref, pl_ref, ps_ref,
    dfirst0_ref, dfirst1_ref, dfirst2_ref, wqkv_ref,
    enc_down, enc_downb, enc_up, enc_upb, long_down, long_downb, long_up, long_upb,
    short_down, short_downb, short_up, short_upb, dpk_ref, dpv_ref,
    y0_ref, y1_ref, dt_ref,
    source_ref, y_ref, target_ref, o_up_ref, o_down_ref, o_prefix_ref, o_upb_ref, o_downb_ref,
    dq, dk, dv, small, ups, downs, mine, theirs, half_sum, across_y, y_sum, landed, total, result,
    small_landed, small_total, small_result, dx, dx_landed, lows, lows_landed,
    load_sems, pair_sems, y_sems, z_sems, gather_sems, share_y_sems, back_sems,
    small_sems, share_sems, cross_sems,
    *, devices,
):
    step = pl.program_id(0)
    pairs = 8
    section = lax.axis_index("section")
    is_encoder = section == 0
    chips = devices // 2
    line = chips // 2
    slices = 16 // line
    rows = 2 * chunk
    half = rows // 2
    size = half // slices
    side = size // 2
    part = side // line
    place = lax.axis_index("dp")
    core, chip = lax.rem(place, 2), place // 2
    bit, at_line = lax.rem(chip, 2), chip // 2
    partner = place + 1 - 2 * core
    beside = place + 2 - 4 * bit
    small_rows, small_cols = small_shape(devices)
    tile = 256
    width = 2 * chunk
    scale = 1.0 / devices

    def aligned(value, unit=16):
        return pl.multiple_of(value, unit)

    def along(distance):
        return (lax.rem(at_line + distance, line) * 2 + bit) * 2 + core

    def remote(source, target, send_sem, recv_sem, other):
        return pltpu.make_async_remote_copy(
            src_ref=source, dst_ref=target, send_sem=send_sem, recv_sem=recv_sem,
            device_id=other, device_id_type=pl.DeviceIdType.MESH,
        )

    def in_group(other):
        return {"dp": other}

    across = {"section": 1 - section}
    kept = aligned(core * half)
    given = aligned((1 - core) * half)

    def swap():
        return remote(
            mine.at[pl.ds(given, half)], theirs, pair_sems.at[0], pair_sems.at[1],
            in_group(partner),
        )

    def y_send(j):
        there = pl.ds(aligned(j * size + (1 - bit) * side), side)
        return remote(
            half_sum.at[there], across_y.at[j], y_sems.at[0, j], y_sems.at[1, j], in_group(beside)
        )

    def z_send(j, s):
        there = pl.ds(aligned(lax.rem(at_line + s, line) * part), part)
        return remote(
            y_sum.at[j].at[there], landed.at[j, s - 1],
            z_sems.at[0, j, s - 1], z_sems.at[1, j, s - 1], in_group(along(s)),
        )

    def own_rows(j):
        return pl.ds(aligned(kept + j * size + bit * side + at_line * part), part)

    def own_side(j):
        return pl.ds(aligned(kept + j * size + bit * side), side)

    def other_side(j):
        return pl.ds(aligned(kept + j * size + (1 - bit) * side), side)

    def gather(j, s):
        return remote(
            total.at[j], result.at[own_rows(j)],
            gather_sems.at[0, j, s - 1], gather_sems.at[1, j, s - 1], in_group(along(s)),
        )

    def y_share(j):
        return remote(
            result.at[own_side(j)], result.at[own_side(j)],
            share_y_sems.at[0, j], share_y_sems.at[1, j], in_group(beside),
        )

    def back(j, i):
        there = own_side(j) if i == 0 else other_side(j)
        return remote(
            result.at[there], result.at[there],
            back_sems.at[0, j, i], back_sems.at[1, j, i], in_group(partner),
        )

    def piece(index):
        row = aligned(lax.rem(index, 8) * small_rows, 8)
        col = aligned((index // 8) * small_cols, LANES)
        return pl.ds(row, small_rows), pl.ds(col, small_cols)

    def small_out(s):
        return remote(
            small.at[piece(lax.rem(place + s, devices))], small_landed.at[s - 1],
            small_sems.at[0, s - 1], small_sems.at[1, s - 1],
            in_group(lax.rem(place + s, devices)),
        )

    def small_share(s):
        return remote(
            small_total, small_result.at[piece(place)],
            share_sems.at[0, s - 1], share_sems.at[1, s - 1],
            in_group(lax.rem(place + s, devices)),
        )

    def send_low():
        return remote(lows, lows_landed, cross_sems.at[0, 0], cross_sems.at[1, 0], across)

    def send_high(i):
        return remote(
            dx.at[i], dx_landed.at[i], cross_sems.at[0, 1 + i], cross_sems.at[1, 1 + i], across
        )

    def greet(barrier, other):
        pl.semaphore_signal(
            barrier, inc=1, device_id=other, device_id_type=pl.DeviceIdType.MESH
        )

    def load(source, target, i):
        return pltpu.make_async_copy(source, target, load_sems.at[i])

    enc_loads = [load(enc_up, ups.at[0], 0), load(enc_down, downs.at[0], 1)]
    dec_loads = [
        load(long_up, ups.at[0], 0), load(long_down, downs.at[0], 1),
        load(short_up, ups.at[1], 2), load(short_down, downs.at[1], 3),
    ]

    @pl.when(step == 0)
    def _():
        barrier = pltpu.get_barrier_semaphore()
        for s in range(1, devices):
            greet(barrier, in_group(lax.rem(place + s, devices)))

        @pl.when(is_encoder)
        def _():
            for copy in enc_loads:
                copy.start()

        @pl.when(jnp.logical_not(is_encoder))
        def _():
            for copy in dec_loads:
                copy.start()

    @pl.when(is_encoder & (step < pairs))
    def _():
        at = aligned(step * LANES, LANES)
        lanes = pl.ds(at, LANES)
        prefix_totals = attend_back_pair(
            q_ref, [k_ref], [v_ref], o_ref, inv_ref, [g0_ref, g1_ref, g2_ref], pk_ref, pv_ref,
            (pl_ref, ps_ref), dq.at[:, lanes], dk.at[:, lanes], dv.at[:, lanes], enc_segs,
        )
        small[0:PRE_PAD, lanes] = prefix_totals[0] * scale
        small[PRE_PAD : 2 * PRE_PAD, lanes] = prefix_totals[1] * scale

    @pl.when(step == 0)
    def _():
        barrier = pltpu.get_barrier_semaphore()

        def pack(up, down):
            mine[0:chunk] = (up * scale).astype(BF)
            down = (down * scale).astype(BF)
            mine[chunk:width, 0:chunk] = down[0:chunk]
            mine[chunk:width, chunk:width] = down[chunk:width]

        @pl.when(is_encoder)
        def _():
            for copy in enc_loads:
                copy.wait()
            pack(ups[0], downs[0])
            pl.semaphore_wait(barrier, devices - 1)
            greet(barrier, across)

        @pl.when(jnp.logical_not(is_encoder))
        def _():
            for copy in dec_loads:
                copy.wait()
            pack(ups[0] + ups[1], downs[0] + downs[1])
            pl.semaphore_wait(barrier, devices)
            greet(barrier, across)

        swap().start()

        @pl.when(jnp.logical_not(is_encoder))
        def _():
            low = width // 2
            lows[0, 0:TGT] = y0_ref[:, 0:low]
            lows[0, TGT : 2 * TGT] = y1_ref[:, 0:low]
            lows[1] = dt_ref[:, 0:low]
            send_low().start()
            small[0:PRE_PAD] = dpk_ref[...] * scale
            small[PRE_PAD : 2 * PRE_PAD] = dpv_ref[...] * scale

    @pl.when(step == 1)
    def _():
        swap().wait()
        half_sum[...] = (
            mine[pl.ds(kept, half)].astype(F32) + theirs[...].astype(F32)
        ).astype(BF)
        for j in range(min(2, slices)):
            y_send(j).start()

    for j in range(slices):

        @pl.when(step == 2 + j)
        def _(j=j):
            y_send(j).wait()
            if j + 2 < slices:
                y_send(j + 2).start()
            own = pl.ds(aligned(j * size + bit * side), side)
            y_sum[j] = (half_sum[own].astype(F32) + across_y[j].astype(F32)).astype(BF)
            for s in range(1, line):
                z_send(j, s).start()

        @pl.when(step == 4 + j)
        def _(j=j):
            summed = y_sum[j, pl.ds(aligned(at_line * part), part)].astype(F32)
            for s in range(1, line):
                z_send(j, s).wait()
                summed = summed + landed[j, s - 1].astype(F32)
            total[j] = summed.astype(BF)
            result[own_rows(j)] = total[j]
            for s in range(1, line):
                gather(j, s).start()

        @pl.when(step == 6 + j)
        def _(j=j):
            for s in range(1, line):
                gather(j, s).wait()
            y_share(j).start()
            back(j, 0).start()

        @pl.when(step == 8 + j)
        def _(j=j):
            y_share(j).wait()
            back(j, 1).start()

    @pl.when(step == pairs - 1)
    def _():
        @pl.when(is_encoder)
        def _():
            down_row = jnp.concatenate([enc_downb[...], jnp.zeros_like(enc_downb)], 1)
            small[PRE : PRE + 1] = enc_upb[...] * scale
            small[PRE + 1 : PRE + 2] = down_row * scale

        @pl.when(jnp.logical_not(is_encoder))
        def _():
            down_row = long_downb[...] + short_downb[...]
            down_row = jnp.concatenate([down_row, jnp.zeros_like(down_row)], 1)
            small[PRE : PRE + 1] = (long_upb[...] + short_upb[...]) * scale
            small[PRE + 1 : PRE + 2] = down_row * scale

        for s in range(1, devices):
            small_out(s).start()

    @pl.when(is_encoder & (step == pairs))
    def _():
        pl.semaphore_wait(pltpu.get_barrier_semaphore(), 1)

    @pl.when(is_encoder & (step >= pairs))
    def _():
        acc = jnp.concatenate([dfirst0_ref[...], dfirst1_ref[...], dfirst2_ref[...]], 0)
        for n, grad in enumerate((dq, dk, dv)):
            acc = acc + nt(grad[...], wqkv_ref[:, n * width : (n + 1) * width])
        dx[step - pairs] = acc.astype(BF)

    for i in range(2):

        @pl.when(is_encoder & (step == pairs + i))
        def _(i=i):
            send_high(i).start()

    @pl.when(step == pairs + 1)
    def _():
        own_rows_, own_cols = piece(place)
        summed = small[own_rows_, own_cols]
        for s in range(1, devices):
            small_out(s).wait()
            summed = summed + small_landed[s - 1]
        small_total[...] = summed
        small_result[own_rows_, own_cols] = summed
        for s in range(1, devices):
            small_share(s).start()

    @pl.when(step == pairs + 3)
    def _():
        for j in range(slices):
            for i in range(2):
                back(j, i).wait()
        o_up_ref[...] = result[0:chunk]
        o_down_ref[0:chunk] = result[chunk:width, 0:chunk]
        o_down_ref[chunk:width] = result[chunk:width, chunk:width]
        for s in range(1, devices):
            small_share(s).wait()
        o_prefix_ref[0] = small_result[0:PRE]
        o_prefix_ref[1] = small_result[PRE_PAD : PRE_PAD + PRE]
        o_upb_ref[...] = small_result[PRE : PRE + 1]
        o_downb_ref[...] = small_result[PRE + 1 : PRE + 2, 0:chunk]

        @pl.when(is_encoder)
        def _():
            for i in range(2):
                source_ref[:, i * tile : (i + 1) * tile] = dx[2 + i]
            send_low().wait_recv()
            y_ref[...] = lows_landed[0]
            target_ref[...] = lows_landed[1]
            for i in range(2):
                send_high(i).wait_send()

        @pl.when(jnp.logical_not(is_encoder))
        def _():
            low = width // 2
            y_ref[0:TGT] = y0_ref[:, low:width]
            y_ref[TGT : 2 * TGT] = y1_ref[:, low:width]
            target_ref[...] = dt_ref[:, low:width]
            send_low().wait_send()
            for i in range(2):
                send_high(i).wait_recv()
                source_ref[:, i * tile : (i + 1) * tile] = dx_landed[i]


def finish(saved, datts, dfirsts, w, adapters, dec_prefix, ys, dt):
    qkv, att, inv, weights = saved
    devices = lax.axis_size("dp")
    line = devices // 4
    slices = 16 // line
    rows, width = att.shape
    targets = dt.shape[0]
    pairs, tile = 8, 256
    half = width // 2
    side = half // slices // 2
    part = side // line
    small_rows, small_cols = small_shape(devices)

    def mine(value):
        return jnp.where(lax.axis_index("section") == 0, value, 0)

    def head(i):
        return mine(jnp.minimum(i, pairs - 1))

    def pair(offset):
        return pl.BlockSpec((rows, LANES), lambda i: (0, head(i) + offset))

    def at(i):
        return mine(jnp.where(i < pairs + 2, 2 + jnp.maximum(i - pairs, 0), i - pairs - 2))

    def once(shape):
        return pl.BlockSpec(shape, lambda i: (0,) * len(shape), pipeline_mode=pl.Buffered(1))

    anywhere = pl.BlockSpec(memory_space=pl.ANY)
    prefix_pair = pl.BlockSpec((PRE_PAD, LANES), lambda i: (0, head(i)))
    vmem = pltpu.VMEM
    dma = pltpu.SemaphoreType.DMA
    flat = [a for group in adapters for a in group]
    return pl.pallas_call(
        functools.partial(finish_kernel, devices=devices),
        grid=(pairs + 4,),
        in_specs=[pair(0), pair(8), pair(16), pair(0), pair(0)]
        + [pl.BlockSpec((ENC_ROWS, LANES), lambda i: (0, head(i)))] * 3
        + [prefix_pair] * 2
        + [
            pl.BlockSpec((2,) + p.shape[1:], lambda i: (head(i), 0, 0))
            for p in weights
        ]
        + [
            pl.BlockSpec((ENC_ROWS, tile), lambda i: (0, at(i))),
        ]
        * 3
        + [
            pl.BlockSpec((tile, 3 * width), lambda i: (at(i), 0)),
        ]
        + [anywhere if a.shape[0] > 1 else once(a.shape) for a in flat]
        + [once(a.shape) for a in (*dec_prefix, *ys, dt)],
        out_specs=[
            once((rows, half)), once((targets, half)), once((targets, half)),
            once((chunk, width)), once((width, chunk)),
            once((2, PRE, width)), once((1, width)), once((1, chunk)),
        ],
        out_shape=[
            jax.ShapeDtypeStruct((rows, half), BF),
            jax.ShapeDtypeStruct((targets, half), BF),
            jax.ShapeDtypeStruct((targets, half), BF),
            jax.ShapeDtypeStruct((chunk, width), BF),
            jax.ShapeDtypeStruct((width, chunk), BF),
            jax.ShapeDtypeStruct((2, PRE, width), F32),
            jax.ShapeDtypeStruct((1, width), F32),
            jax.ShapeDtypeStruct((1, chunk), F32),
        ],
        scratch_shapes=[
            vmem((rows, width), BF), vmem((rows, width), BF), vmem((rows, width), BF),
            vmem((2 * PRE_PAD, width), F32),
            vmem((2, chunk, width), F32), vmem((2, width, chunk), F32),
            vmem((width, width), BF), vmem((half, width), BF), vmem((half, width), BF),
            vmem((slices, side, width), BF), vmem((slices, side, width), BF),
            vmem((slices, line - 1, part, width), BF), vmem((slices, part, width), BF),
            vmem((width, width), BF),
            vmem((devices - 1, small_rows, small_cols), F32), vmem((small_rows, small_cols), F32),
            vmem((2 * PRE_PAD, width), F32),
            vmem((4, rows, tile), BF), vmem((2, rows, tile), BF),
            vmem((2, targets, half), BF), vmem((2, targets, half), BF),
            dma((4,)), dma((2,)), dma((2, slices)), dma((2, slices, line - 1)),
            dma((2, slices, line - 1)), dma((2, slices)), dma((2, slices, 2)),
            dma((2, devices - 1)), dma((2, devices - 1)), dma((2, 3)),
        ],
        compiler_params=pltpu.CompilerParams(
            vmem_limit_bytes=60 * 2**20, collective_id=0, has_side_effects=True
        ),
        name="finish",
    )(
        qkv, qkv, qkv, att, inv, *datts, *w["prefix"], *weights,
        *dfirsts, w["qkv"], *flat, *dec_prefix, *ys, dt,
    )


def blank_kernel(*refs):
    pass


def blanks(shapes):
    return pl.pallas_call(
        blank_kernel,
        out_shape=list(shapes),
        out_specs=[pl.BlockSpec(memory_space=pl.ANY)] * len(shapes),
        name="blank",
    )()


def on_section(is_encoder, encoder_work, decoder_work, *operands):
    enc_shapes, _ = jax.eval_shape(encoder_work, *operands)
    dec_shapes, _ = jax.eval_shape(decoder_work, *operands)

    def blank_like(shapes):
        leaves, tree = jax.tree.flatten(shapes)
        if not leaves:
            return shapes
        return jax.tree.unflatten(tree, blanks(leaves))

    def encoder_branch(*a):
        own, shared = encoder_work(*a)
        return own, blank_like(dec_shapes), shared

    def decoder_branch(*a):
        own, shared = decoder_work(*a)
        return blank_like(enc_shapes), own, shared

    return lax.cond(is_encoder, encoder_branch, decoder_branch, *operands)


def to_decoder(block):
    return lax.ppermute(block, "section", [(0, 1)])


def to_encoder(block):
    return lax.ppermute(block, "section", [(1, 0)])


def per_device(
    sources, targets, cotangent, source_lengths, target_lengths,
    attn_qkv, attn_out, ffn_in, ffn_out, norm_gains, prefix_pairs,
    adapt_down, adapt_down_bias, adapt_up, adapt_up_bias,
    cross_query, cross_pairs, cross_out, cross_gain,
):
    is_encoder = lax.axis_index("section") == 0
    prefix = jnp.pad(prefix_pairs[0], ((0, 0), (0, PRE_PAD - PRE), (0, 0)))
    w = dict(
        qkv=attn_qkv[0], out=attn_out[0], ffn_in=ffn_in[0], ffn_out=ffn_out[0],
        gains=norm_gains[0], prefix=(prefix[0], prefix[1]),
        down=adapt_down[0], down_bias=adapt_down_bias,
        up=adapt_up[0], up_bias=adapt_up_bias,
    )
    cross = dict(query=cross_query, pairs=cross_pairs, out=cross_out, gain=cross_gain[None])

    def at_encoder(work, *operands):
        return on_section(is_encoder, lambda *a: (work(*a), ()), lambda *a: ((), ()), *operands)[0]

    def at_decoder(work, *operands):
        return on_section(is_encoder, lambda *a: ((), ()), lambda *a: (work(*a), ()), *operands)[1]

    def at_both(enc_work, dec_work, *operands):
        return on_section(
            is_encoder, lambda *a: (enc_work(*a), ()), lambda *a: (dec_work(*a), ()), *operands
        )[:2]

    def encoder_start():
        qkv = product(sources, w["qkv"])
        att, inv, *weights = attend(
            source_lengths, *self_columns(qkv), w["prefix"], enc_segs, False, checked=True
        )
        return (qkv, att, inv, weights), enc_ffn(sources, att, w, 2)

    (saved, part2), (cq, kept) = at_both(
        encoder_start, lambda: decoder_self(targets, target_lengths, w, cross)
    )
    mem2 = to_decoder(part2[0])
    part1 = at_encoder(lambda saved: enc_ffn(sources, saved[1], w, 1), saved)
    mem1 = to_decoder(part1[0])

    def decoder_short(mem2, cq, kept):
        kv2 = product(mem2, cross["pairs"])
        forward = cross_forward(source_lengths, cq, [kv2], 1)
        return kv2, forward, dec_ffn(
            target_lengths, kept[4], forward[0], cotangent, w, cross, 1
        )

    part0 = at_encoder(lambda saved: enc_ffn(sources, saved[1], w, 0), saved)
    mem2, last = lax.optimization_barrier((mem2, part0[0]))
    mem0 = to_decoder(last)
    kv2, short, short_ffn = at_decoder(decoder_short, mem2, cq, kept)
    mem1, kv2 = lax.optimization_barrier((mem1, kv2))
    kv1 = at_decoder(lambda mem1: product(mem1, cross["pairs"]), mem1)

    def decoder_long(mem0, kv1, kv2, cq, kept):
        kvs = [product(mem0, cross["pairs"]), kv1, kv2]
        long = cross_forward(source_lengths, cq, kvs, 0)
        y, dsecond, dcatt, *adapter = dec_ffn(
            target_lengths, kept[4], long[0], cotangent, w, cross, 0
        )
        dcq, dck, dcv = cross_backward(cq, kvs, long, dcatt, 0)
        cuts = ((0, ENC_ROWS), (ENC_ROWS, ENC_ROWS), (2 * ENC_ROWS, SRC_LONG - 2 * ENC_ROWS))
        return back_product([dck, dcv], cross["pairs"], cuts=cuts), y, dsecond, dcq, adapter

    dmems, *long = at_decoder(decoder_long, mem0, kv1, kv2, cq, kept)
    dmem0, dmem1, dmem2 = [to_encoder(block) for block in dmems]

    def decoder_short_back(kv2, cq, short, dcatt):
        dcq, dck, dcv = cross_backward(cq, [kv2], short, dcatt, 1)
        return back_product([dck, dcv], cross["pairs"])[0], dcq

    short_y, short_second, short_dcatt, *short_adapter = short_ffn
    dmem_short, short_cq = at_decoder(decoder_short_back, kv2, cq, short, short_dcatt)
    dmem_short = to_encoder(dmem_short)

    def decoder_end(kept, *grads):
        return decoder_self_back(kept, grads[:2], grads[2:], w, cross)

    (long_y, long_second, long_cq, long_adapter) = long
    dt, dec_prefix = at_decoder(
        decoder_end, kept, long_second, short_second, long_cq, short_cq
    )
    dmem0, dt = lax.optimization_barrier((dmem0, dt))
    back0 = at_encoder(lambda dmem0, part0: enc_ffn_back([dmem0], part0, w), dmem0, part0)
    back1 = at_encoder(lambda dmem1, part1: enc_ffn_back([dmem1], part1, w), dmem1, part1)

    def encoder_end(dmem2, dmem_short, part0, part1, part2, back0, back1):
        back2 = enc_ffn_back([dmem2, dmem_short], part2, w)
        parts, backs = (part0, part1, part2), (back0, back1, back2)
        adapter = adapter_grads(
            [p[4] for p in parts], [p[3] for p in parts],
            [b[2] for b in backs], [b[3] for b in backs],
        )
        return back2, adapter

    back2, enc_adapter = at_encoder(
        encoder_end, dmem2, dmem_short, part0, part1, part2, back0, back1
    )
    backs = (back0, back1, back2)
    source_grad, y, target_grad, up, down, prefix_grad, up_bias, down_bias = finish(
        saved, [b[1] for b in backs], [b[0] for b in backs], w,
        [enc_adapter, long_adapter, short_adapter], dec_prefix, [long_y, short_y], dt,
    )
    return (
        y,
        source_grad,
        target_grad,
        prefix_grad[None],
        down.astype(F32)[None],
        down_bias,
        up.astype(F32)[None],
        up_bias,
    )


def solution(mesh):
    layer2, layer3, rows = P("section", None), P("section", None, None), P("dp", None)
    return jax.shard_map(
        per_device,
        mesh=mesh,
        in_specs=(
            rows, rows, rows, rows, rows,
            layer3, layer3, layer3, layer3, layer3,
            P("section", None, None, None),
            layer3, layer2, layer3, layer2,
            P(), P(), P(), P(),
        ),
        out_specs=(
            P("dp", "section"), P("dp", "section"), P("dp", "section"),
            P("section", None, None, None), layer3, layer2, layer3, layer2,
        ),
        check_vma=False,
    )
```

```python
import functools

import jax
import jax.numpy as jnp
from jax import lax
from jax.experimental import pallas as pl
from jax.experimental.pallas import tpu as pltpu
from jax.sharding import PartitionSpec as P

HD = 64
PRE = 30
PRE_PAD = 32
SRC_LONG = 768
SRC_SHORT = 96
TGT = 256
LANES = 128

BF = jnp.bfloat16
F32 = jnp.float32
norm_eps = 1e-05
big_negative = -1e30
adapter_scale = 4.0
chunk = 512
wide = 1024
ENC_ROWS = (SRC_LONG + SRC_SHORT) // 3
vmem_bytes = 56 * 2**20

phi_poly = (
    0.797869713181688,
    0.036392283539041996,
    -8.782472977701046e-05,
    -3.669384069669515e-05,
    1.4250308145882202e-06,
)


def nn(left, right):
    return lax.dot_general(left, right, (((1,), (0,)), ((), ())), preferred_element_type=F32)


def nt(left, right):
    return lax.dot_general(left, right, (((1,), (1,)), ((), ())), preferred_element_type=F32)


def tn(left, right):
    return lax.dot_general(left, right, (((0,), (0,)), ((), ())), preferred_element_type=F32)


def gelu_pair(values):
    square = values * values
    poly = phi_poly[4]
    for coefficient in phi_poly[3::-1]:
        poly = poly * square + coefficient
    half = 0.5 * jnp.tanh(values * poly) + 0.5
    density = jnp.exp(square * -0.5) * 0.3989422804014327
    return values * half, half + values * density


def row_tiles(rows, most=288):
    count = -(-rows // most)
    size = rows // count
    return [(i * size, size) for i in range(count)]


def norm_rows(values):
    centered = values - jnp.mean(values, axis=-1, keepdims=True)
    scale = lax.rsqrt(jnp.mean(centered * centered, axis=-1, keepdims=True) + norm_eps)
    return centered * scale, scale


def norm_rows_back(hat, scale, grad_hat):
    mean_grad = jnp.mean(grad_hat, axis=-1, keepdims=True)
    mean_dot = jnp.mean(grad_hat * hat, axis=-1, keepdims=True)
    return scale * (grad_hat - mean_grad - hat * mean_dot)


def params(limit=vmem_bytes):
    return pltpu.CompilerParams(vmem_limit_bytes=limit)


def whole(shape):
    return pl.BlockSpec(shape, lambda *g: (0,) * len(shape))


def product_kernel(x_ref, w_ref, o_ref):
    o_ref[...] = nn(x_ref[...], w_ref[...]).astype(BF)


def product(x, w, tile=1024):
    rows, depth = x.shape
    width = w.shape[1]
    return pl.pallas_call(
        product_kernel,
        grid=(width // tile,),
        in_specs=[whole((rows, depth)), pl.BlockSpec((depth, tile), lambda i: (0, i))],
        out_specs=pl.BlockSpec((rows, tile), lambda i: (0, i)),
        out_shape=jax.ShapeDtypeStruct((rows, width), BF),
        compiler_params=params(),
        name="product",
    )(x, w)


def back_product_kernel(*refs, parts, residual, cuts):
    grads = refs[:parts]
    w_ref = refs[parts]
    outs = refs[-len(cuts) :]
    total = None
    width = grads[0].shape[1]
    for i, grad in enumerate(grads):
        term = nt(grad[...], w_ref[:, i * width : (i + 1) * width])
        total = term if total is None else total + term
    if residual:
        total = total + refs[parts + 1][...]
    for (start, size), o_ref in zip(cuts, outs):
        o_ref[...] = total[start : start + size].astype(BF)


def back_product(grads, w, residual=None, tile=512, cuts=None):
    rows, width = grads[0].shape
    depth = w.shape[0]
    parts = len(grads)
    cuts = cuts or ((0, rows),)
    specs = [whole((rows, width))] * parts + [
        pl.BlockSpec((tile, parts * width), lambda i: (i, 0))
    ]
    args = list(grads) + [w]
    if residual is not None:
        specs.append(pl.BlockSpec((rows, tile), lambda i: (0, i)))
        args.append(residual)
    return pl.pallas_call(
        functools.partial(
            back_product_kernel, parts=parts, residual=residual is not None, cuts=cuts
        ),
        grid=(depth // tile,),
        in_specs=specs,
        out_specs=[pl.BlockSpec((size, tile), lambda i: (0, i)) for _, size in cuts],
        out_shape=[jax.ShapeDtypeStruct((size, depth), BF) for _, size in cuts],
        compiler_params=params(),
        name="back_product",
    )(*args)


def head_lanes(head):
    lane = lax.broadcasted_iota(jnp.int32, (1, LANES), 1)
    own = (lane < HD) if head == 0 else (lane >= HD)
    first = HD if head == 0 else 0
    return own, lane == first, lane == first + 1


def bf(value):
    return jnp.asarray(value, BF)


def rows_of(refs, start, count):
    parts = []
    for ref in refs:
        size = ref.shape[0]
        low, high = max(start, 0), min(start + count, size)
        if low < high:
            parts.append(ref[low:high])
        start -= size
    return parts


def stacked(refs, prefix_ref, start, count):
    parts = rows_of(refs, start, count)
    if prefix_ref is not None:
        parts.append(prefix_ref[...])
    return parts[0] if len(parts) == 1 else jnp.concatenate(parts, 0)


def attend_pair(*refs, segs, prefix, causal, pieces, which, checked):
    len_ref, q_ref = refs[:2]
    k_refs, v_refs = refs[2 : 2 + pieces], refs[2 + pieces : 2 + 2 * pieces]
    at = 2 + 2 * pieces
    pk_ref = pv_ref = None
    if prefix:
        pk_ref, pv_ref = refs[at : at + 2]
        at += 2
    o_ref, inv_ref = refs[at : at + 2]
    p_refs = refs[at + 2 :]

    def work(peaked):
        for seg, (q0, nq, k0, nk) in enumerate(segs):
            keys = stacked(k_refs, pk_ref, k0, nk)
            values = stacked(v_refs, pv_ref, k0, nk)
            count = keys.shape[0]
            row = lax.broadcasted_iota(jnp.int32, (count, 1), 0)
            seen = row < jnp.minimum(len_ref[0, which + seg], nk)
            if prefix:
                seen = seen | ((row >= nk) & (row < nk + PRE))
            queries = q_ref[q0 : q0 + nq] * bf(HD**-0.5)
            out = inv = None
            across = nq >= 4 * LANES
            outs, invs = [], []
            if across:
                turned = values.T
                ones = jnp.ones((16, count), BF)
            for head in range(2):
                own, first, _ = head_lanes(head)
                k_own = jnp.where(own, keys, jnp.where(first & ~seen, bf(big_negative), bf(0)))
                q_own = jnp.where(own, queries, jnp.where(first, bf(1), bf(0)))
                scores = nt(k_own, q_own)
                if causal:
                    key_at = lax.broadcasted_iota(jnp.int32, scores.shape, 0)
                    query_at = lax.broadcasted_iota(jnp.int32, scores.shape, 1)
                    allowed = (key_at <= query_at) | (key_at >= nk)
                    scores = jnp.where(allowed, scores, big_negative)
                if peaked:
                    scores = scores - jnp.max(scores, axis=0, keepdims=True)
                weights = jnp.exp(scores).astype(BF)
                p_refs[seg][head] = weights
                if across:
                    rows = jnp.concatenate([turned[head * HD : (head + 1) * HD], ones], 0)
                    mixed = nn(rows, weights)
                    inverse = 1.0 / mixed[HD : HD + 1]
                    outs.append(mixed[:HD] * inverse)
                    invs.append(jnp.broadcast_to(inverse, (HD, nq)))
                    continue
                mixed = tn(weights, jnp.where(own, values, bf(1)))
                inverse = 1.0 / pltpu.roll(mixed, HD, 1)
                mixed = mixed * inverse
                out = mixed if out is None else jnp.where(own, mixed, out)
                inv = inverse if inv is None else jnp.where(own, inverse, inv)
            if across:
                out = jnp.concatenate(outs, 0).T
                inv = jnp.concatenate(invs, 0).T
            o_ref[q0 : q0 + nq] = out.astype(BF)
            inv_ref[q0 : q0 + nq] = inv

    if not checked:
        work(True)
        return

    limit = 50.0**2
    head_row = lax.broadcasted_iota(jnp.int32, (LANES, LANES), 0) // HD
    head_col = lax.broadcasted_iota(jnp.int32, (LANES, LANES), 1) // HD
    same_head = jnp.where(head_row == head_col, 1.0, 0.0).astype(BF)

    def largest(array):
        square = (array.astype(F32) * array.astype(F32)).astype(BF)
        return jnp.max(nn(square, same_head), axis=0, keepdims=True)

    key_peak = largest(k_refs[0][...])
    for ref in k_refs[1:]:
        key_peak = jnp.maximum(key_peak, largest(ref[...]))
    if prefix:
        key_peak = jnp.maximum(key_peak, largest(pk_ref[...]))
    small = jnp.max(largest(q_ref[...]) * key_peak) * (1.0 / HD) <= limit

    @pl.when(small)
    def _():
        work(False)

    @pl.when(jnp.logical_not(small))
    def _():
        work(True)


def lane_views(refs, group, j):
    views = []
    for ref in refs:
        if len(ref.shape) == 2:
            views.append(ref.at[:, j * LANES : (j + 1) * LANES])
        else:
            views.append(ref.at[2 * j : 2 * j + 2])
    return views


def attend_kernel(len_ref, *refs, group, **kw):
    for j in range(group):
        attend_pair(len_ref, *lane_views(refs, group, j), **kw)


def column_spec(rows, offset, row_block=0, group=1):
    return pl.BlockSpec((rows, group * LANES), lambda h: (row_block, h + offset // group))


def attend(lengths, q, keys, values, prefixes, segs, causal, which=0, group=1, checked=False):
    pairs = 8
    q_rows = q[1]
    prefix = prefixes is not None
    extra = PRE_PAD if prefix else 0
    specs = [pl.BlockSpec(memory_space=pltpu.SMEM)]
    args = [lengths]
    for array, rows, block, offset in [q, *keys, *values]:
        specs.append(column_spec(rows, offset, block, group))
        args.append(array)
    if prefix:
        specs += [column_spec(PRE_PAD, 0, 0, group)] * 2
        args += list(prefixes)
    weight_shapes = [(2 * pairs, nk + extra, nq) for _, nq, _, nk in segs]
    return pl.pallas_call(
        functools.partial(
            attend_kernel, group=group, segs=segs, prefix=prefix, causal=causal, pieces=len(keys), which=which,
            checked=checked,
        ),
        grid=(pairs // group,),
        in_specs=specs,
        out_specs=[column_spec(q_rows, 0, 0, group)] * 2
        + [pl.BlockSpec((2 * group,) + s[1:], lambda h: (h, 0, 0)) for s in weight_shapes],
        out_shape=[
            jax.ShapeDtypeStruct((q_rows, pairs * LANES), BF),
            jax.ShapeDtypeStruct((q_rows, pairs * LANES), F32),
        ]
        + [jax.ShapeDtypeStruct(s, BF) for s in weight_shapes],
        compiler_params=params(),
        name="attend",
    )(*args)


def attend_back_pair(
    q_ref, k_refs, v_refs, o_ref, inv_ref, g_refs, pk_ref, pv_ref, p_refs, dq_ref, dk_ref, dv_ref, segs
):
    prefix_totals = [None, None]
    scale = HD**-0.5
    for seg, (q0, nq, k0, nk) in enumerate(segs):
        keys = stacked(k_refs, pk_ref, k0, nk)
        values = stacked(v_refs, pv_ref, k0, nk)
        queries = q_ref[q0 : q0 + nq]
        grads = stacked(g_refs, None, q0, nq).astype(F32) * inv_ref[q0 : q0 + nq]
        grads_low = grads.astype(BF)
        dots = grads * o_ref[q0 : q0 + nq].astype(F32)
        dq = dk = dv = None
        across = nq >= LANES and keys.shape[0] >= 4 * LANES
        turned_grads = []
        if across:
            turned = keys.T
        for head in range(2):
            own, first, second = head_lanes(head)
            row_dot = -jnp.sum(jnp.where(own, dots, 0.0), axis=1, keepdims=True)
            high = row_dot.astype(BF)
            rest = (row_dot - high.astype(F32)).astype(BF)
            g_own = jnp.where(
                own, grads_low, jnp.where(first, high, jnp.where(second, rest, bf(0)))
            )
            v_own = jnp.where(own, values, jnp.where(first | second, bf(1), bf(0)))
            weights = p_refs[seg][head]
            score_grad = (weights.astype(F32) * nt(v_own, g_own)).astype(BF)
            dv_head = nn(weights, grads_low)
            dk_head = nn(score_grad, queries)
            dq_head = None if across else tn(score_grad, keys)
            if across:
                turned_grads.append(nn(turned[head * HD : (head + 1) * HD], score_grad))
            if not across:
                dq = dq_head if dq is None else jnp.where(own, dq_head, dq)
            dk = dk_head if dk is None else jnp.where(own, dk_head, dk)
            dv = dv_head if dv is None else jnp.where(own, dv_head, dv)
        if across:
            dq = jnp.concatenate(turned_grads, 0).T
        dk = dk * scale
        dq_ref[q0 : q0 + nq] = (dq * scale).astype(BF)
        at = k0 - segs[0][2]
        dk_ref[at : at + nk] = dk[:nk].astype(BF)
        dv_ref[at : at + nk] = dv[:nk].astype(BF)
        if pk_ref is not None:
            for i, grad in enumerate((dk, dv)):
                part = grad[nk:]
                prefix_totals[i] = part if seg == 0 else prefix_totals[i] + part
    return prefix_totals


def attend_back_kernel(*refs, group, **kw):
    for j in range(group):
        attend_back_views(*lane_views(refs, group, j), **kw)


def attend_back_views(*refs, segs, prefix, pieces):
    q_ref, o_ref, inv_ref, g_ref = refs[:4]
    k_refs, v_refs = refs[4 : 4 + pieces], refs[4 + pieces : 4 + 2 * pieces]
    at = 4 + 2 * pieces
    pk_ref = pv_ref = None
    if prefix:
        pk_ref, pv_ref = refs[at : at + 2]
        at += 2
    outs = refs[at + len(segs) :]
    totals = attend_back_pair(
        q_ref, k_refs, v_refs, o_ref, inv_ref, [g_ref], pk_ref, pv_ref,
        refs[at : at + len(segs)], *outs[:3], segs,
    )
    if prefix:
        outs[3][...] = totals[0]
        outs[4][...] = totals[1]


def attend_back(q, keys, values, prefixes, attended, inverse, grad, weights, segs, group=2):
    pairs = 8
    q_rows = q[1]
    k_rows = sum(nk for _, _, _, nk in segs)
    prefix = prefixes is not None
    specs, args = [], []
    own = [(a, q_rows, 0, 0) for a in (attended, inverse, grad)]
    for array, rows, block, offset in [q, *own, *keys, *values]:
        specs.append(column_spec(rows, offset, block, group))
        args.append(array)
    if prefix:
        specs += [column_spec(PRE_PAD, 0, 0, group)] * 2
        args += list(prefixes)
    specs += [pl.BlockSpec((2 * group,) + w.shape[1:], lambda h: (h, 0, 0)) for w in weights]
    args += list(weights)
    out_specs = [column_spec(n, 0, 0, group) for n in (q_rows, k_rows, k_rows)]
    out_shape = [
        jax.ShapeDtypeStruct((q_rows, pairs * LANES), BF),
        jax.ShapeDtypeStruct((k_rows, pairs * LANES), BF),
        jax.ShapeDtypeStruct((k_rows, pairs * LANES), BF),
    ]
    if prefix:
        out_specs += [column_spec(PRE_PAD, 0, 0, group)] * 2
        out_shape += [jax.ShapeDtypeStruct((PRE_PAD, pairs * LANES), F32)] * 2
    return pl.pallas_call(
        functools.partial(
            attend_back_kernel, group=group, segs=segs, prefix=prefix, pieces=len(keys)
        ),
        grid=(pairs // group,),
        in_specs=specs,
        out_specs=out_specs,
        out_shape=out_shape,
        compiler_params=params(),
        name="attend_back",
    )(*args)


class Weights:
    def __init__(self, sources, targets, sems):
        self.sources, self.targets, self.sems = sources, targets, sems

    def copy(self, name, part=None):
        source, target = self.sources[name], self.targets[name]
        first = list(self.sources).index(name)
        sem = self.sems.at[first, 0 if part is None else part]
        if part is not None:
            cut = pl.ds(pl.multiple_of(part * wide, wide), wide)
            index = (slice(None), cut) if name == "in" else (cut, slice(None))
            source, target = source.at[index], target.at[index]
        return pltpu.make_async_copy(source, target, sem)

    def wait(self, name, part=None):
        self.copy(name, part).wait()

    def part(self, name, part):
        cut = pl.ds(pl.multiple_of(part * wide, wide), wide)
        index = (slice(None), cut) if name == "in" else (cut, slice(None))
        return self.targets[name].at[index]


def weight_scratch(arrays, parts):
    return [pltpu.VMEM(a.shape, BF) for a in arrays] + [
        pltpu.SemaphoreType.DMA((len(arrays), parts))
    ]


def ffn_step(low_ref, acc_ref, in_ref, out_ref, slope_ref, act_ref, bias_ref, scale):
    for start, size in row_tiles(low_ref.shape[0]):
        rows = slice(start, start + size)
        hidden = nn(low_ref[rows], in_ref[...])
        if bias_ref is not None:
            hidden = hidden + bias_ref[...]
        active, slope = gelu_pair(hidden)
        slope_ref[rows] = slope.astype(BF)
        active = active.astype(BF)
        if act_ref is not None:
            act_ref[rows] = active
        term = nn(active, out_ref[...])
        acc_ref[rows] += term if scale is None else scale * term


def enc_ffn_kernel(
    x_ref, att_ref, gain_ref, downb_ref, upb_ref, wo_hbm, in_hbm, out_hbm, down_hbm, up_hbm,
    mem_ref, slope_ref, pre_slope_ref, act_ref, low_ref, scales_ref,
    acc_ref, wo_ref, in_ref, out_ref, down_ref, up_ref, sems,
):
    weights = Weights(
        {"wo": wo_hbm, "in": in_hbm, "out": out_hbm, "down": down_hbm, "up": up_hbm},
        {"wo": wo_ref, "in": in_ref, "out": out_ref, "down": down_ref, "up": up_ref},
        sems,
    )

    weights.copy("wo").start()
    for part in range(in_ref.shape[1] // wide):
        weights.copy("in", part).start()
        weights.copy("out", part).start()
    weights.copy("down").start()
    weights.copy("up").start()
    weights.wait("wo")
    first = x_ref[...].astype(F32) + nn(att_ref[...], wo_ref[...])
    hat, scale = norm_rows(first)
    normed = hat * gain_ref[0:1]
    acc_ref[...] = normed
    low_ref[...] = normed.astype(BF)
    scales_ref[:, 0:1] = scale

    def one_part(part, carry):
        weights.wait("in", part)
        weights.wait("out", part)
        cols = pl.ds(pl.multiple_of(part * wide, wide), wide)
        ffn_step(
            low_ref, acc_ref, in_ref.at[:, cols], out_ref.at[cols], slope_ref.at[:, cols],
            None, None, None,
        )
        return carry

    lax.fori_loop(0, in_ref.shape[1] // wide, one_part, 0)

    weights.wait("down")
    weights.wait("up")
    ffn_step(low_ref, acc_ref, down_ref, up_ref, pre_slope_ref, act_ref, downb_ref, adapter_scale)
    hat, scale = norm_rows(acc_ref[...] + adapter_scale * upb_ref[...])
    mem_ref[...] = (hat * gain_ref[1:2]).astype(BF)
    scales_ref[:, 1:2] = scale


def enc_ffn(x, att, w, part):
    width = x.shape[1]
    rows = ENC_ROWS
    hidden = w["ffn_in"].shape[1]
    steps = hidden // wide
    weights = [w["out"], w["ffn_in"], w["ffn_out"], w["down"], w["up"]]
    return pl.pallas_call(
        enc_ffn_kernel,
        grid=(1,),
        in_specs=[
            pl.BlockSpec((rows, width), lambda i: (part, 0)),
            pl.BlockSpec((rows, width), lambda i: (part, 0)),
            whole((2, width)),
            whole((1, chunk)),
            whole((1, width)),
        ]
        + [pl.BlockSpec(memory_space=pl.ANY)] * len(weights),
        out_specs=[
            whole((rows, width)),
            whole((rows, hidden)),
            whole((rows, chunk)),
            whole((rows, chunk)),
            whole((rows, width)),
            whole((rows, LANES)),
        ],
        out_shape=[
            jax.ShapeDtypeStruct((rows, width), BF),
            jax.ShapeDtypeStruct((rows, hidden), BF),
            jax.ShapeDtypeStruct((rows, chunk), BF),
            jax.ShapeDtypeStruct((rows, chunk), BF),
            jax.ShapeDtypeStruct((rows, width), BF),
            jax.ShapeDtypeStruct((rows, LANES), F32),
        ],
        scratch_shapes=[pltpu.VMEM((rows, width), F32)] + weight_scratch(weights, steps),
        compiler_params=params(),
        name="enc_ffn",
    )(x, att, w["gains"], w["down_bias"], w["up_bias"], *weights)


def ffn_back_step(grad_ref, acc_ref, in_ref, out_ref, slope_ref):
    for start, size in row_tiles(grad_ref.shape[0]):
        rows = slice(start, start + size)
        pre = (nt(grad_ref[rows], out_ref[...]) * slope_ref[rows].astype(F32)).astype(BF)
        acc_ref[rows] += nt(pre, in_ref[...])


def adapter_back(grad_ref, acc_ref, low_ref, act_ref, slope_ref, down_ref, up_ref, outs, pre_ref):
    ddown_ref, ddownb_ref, dup_ref, dupb_ref = outs
    total = None
    for start, size in row_tiles(grad_ref.shape[0]):
        rows = slice(start, start + size)
        back = adapter_scale * nt(grad_ref[rows], up_ref[...])
        pre = (back * slope_ref[rows].astype(F32)).astype(BF)
        pre_ref[rows] = pre
        sums = jnp.sum(pre.astype(F32), axis=0, keepdims=True)
        total = sums if total is None else total + sums
        acc_ref[rows] += nt(pre, down_ref[...])
    ddownb_ref[...] = total
    ddown_ref[...] = tn(low_ref[...], pre_ref[...])
    dup_ref[...] = adapter_scale * tn(act_ref[...], grad_ref[...])
    dupb_ref[...] = adapter_scale * jnp.sum(grad_ref[...].astype(F32), axis=0, keepdims=True)


def enc_ffn_back_kernel(*refs, pieces):
    enc_ffn_back_body(refs[:pieces], *refs[pieces:])


def enc_ffn_back_body(
    dmem_refs, mem_ref, low_ref, scales_ref, gain_ref, slope_ref, pre_slope_ref,
    up_hbm, down_hbm, in_hbm, out_hbm, wo_hbm,
    dfirst_ref, datt_ref, grad_ref, pre_ref,
    acc_ref, up_ref, down_ref, in_ref, out_ref, wo_ref, sems,
):
    weights = Weights(
        {"up": up_hbm, "down": down_hbm, "in": in_hbm, "out": out_hbm, "wo": wo_hbm},
        {"up": up_ref, "down": down_ref, "in": in_ref, "out": out_ref, "wo": wo_ref},
        sems,
    )

    weights.copy("up").start()
    weights.copy("down").start()
    for part in range(in_ref.shape[1] // wide):
        weights.copy("out", part).start()
        weights.copy("in", part).start()
    weights.copy("wo").start()
    gain = gain_ref[1:2]
    hat = mem_ref[...].astype(F32) / gain
    dmem = stacked(dmem_refs, None, 0, ENC_ROWS).astype(F32)
    grad = norm_rows_back(hat, scales_ref[:, 1:2], dmem * gain)
    low = grad.astype(BF)
    grad_ref[...] = low
    weights.wait("up")
    back = adapter_scale * nt(low, up_ref[...])
    pre = (back * pre_slope_ref[...].astype(F32)).astype(BF)
    pre_ref[...] = pre
    weights.wait("down")
    acc_ref[...] = grad + nt(pre, down_ref[...])

    def one_part(part, carry):
        weights.wait("out", part)
        weights.wait("in", part)
        cols = pl.ds(pl.multiple_of(part * wide, wide), wide)
        ffn_back_step(
            grad_ref, acc_ref, in_ref.at[:, cols], out_ref.at[cols], slope_ref.at[:, cols]
        )
        return carry

    lax.fori_loop(0, in_ref.shape[1] // wide, one_part, 0)

    gain = gain_ref[0:1]
    hat = low_ref[...].astype(F32) / gain
    grad = norm_rows_back(hat, scales_ref[:, 0:1], acc_ref[...] * gain)
    dfirst_ref[...] = grad
    weights.wait("wo")
    datt_ref[...] = nt(grad.astype(BF), wo_ref[...]).astype(BF)


def enc_ffn_back(dmems, saved, w):
    mem, slope, pre_slope, act, low, scales = saved
    rows, width = mem.shape
    hidden = w["ffn_in"].shape[1]
    steps = hidden // wide
    weights = [w["up"], w["down"], w["ffn_in"], w["ffn_out"], w["out"]]
    return pl.pallas_call(
        functools.partial(enc_ffn_back_kernel, pieces=len(dmems)),
        grid=(1,),
        in_specs=[whole(d.shape) for d in dmems]
        + [
            whole((rows, width)),
            whole((rows, width)),
            whole((rows, LANES)),
            whole((2, width)),
            whole((rows, hidden)),
            whole((rows, chunk)),
        ]
        + [pl.BlockSpec(memory_space=pl.ANY)] * len(weights),
        out_specs=[
            whole((rows, width)),
            whole((rows, width)),
            whole((rows, width)),
            whole((rows, chunk)),
        ],
        out_shape=[
            jax.ShapeDtypeStruct((rows, width), F32),
            jax.ShapeDtypeStruct((rows, width), BF),
            jax.ShapeDtypeStruct((rows, width), BF),
            jax.ShapeDtypeStruct((rows, chunk), BF),
        ],
        scratch_shapes=[pltpu.VMEM((rows, width), F32)] + weight_scratch(weights, steps),
        compiler_params=params(),
        name="enc_ffn_back",
    )(*dmems, mem, low, scales, w["gains"], slope, pre_slope, *weights)


def dec_mid_kernel(x_ref, att_ref, wo_ref, gain_ref, wq_ref, n_ref, scale_ref, cq_ref):
    for start, size in row_tiles(x_ref.shape[0], 256):
        rows = slice(start, start + size)
        first = x_ref[rows].astype(F32) + nn(att_ref[rows], wo_ref[...])
        hat, scale = norm_rows(first)
        normed = hat * gain_ref[0:1]
        n_ref[rows] = normed
        scale_ref[rows, 0:1] = scale
        cq_ref[rows] = nn(normed.astype(BF), wq_ref[...]).astype(BF)


def dec_mid(x, att, w, cross):
    rows, width = x.shape
    return pl.pallas_call(
        dec_mid_kernel,
        out_shape=[
            jax.ShapeDtypeStruct((rows, width), F32),
            jax.ShapeDtypeStruct((rows, LANES), F32),
            jax.ShapeDtypeStruct((rows, width), BF),
        ],
        compiler_params=params(),
        name="dec_mid",
    )(x, att, w["out"], w["gains"], cross["query"])


def dec_ffn_kernel(
    len_ref, n_ref, catt_ref, cot_ref, cgain_ref, gain_ref, downb_ref, upb_ref,
    wco_hbm, in_hbm, out_hbm, down_hbm, up_hbm,
    y_ref, dsecond_ref, dcatt_ref, ddown_ref, ddownb_ref, dup_ref, dupb_ref,
    acc_ref, low_ref, grad_ref, slope_ref, pre_slope_ref, act_ref, pre_ref, scale_ref,
    wco_ref, in_ref, out_ref, down_ref, up_ref, sems,
    *, steps, which,
):
    weights = Weights(
        {"wco": wco_hbm, "in": in_hbm, "out": out_hbm, "down": down_hbm, "up": up_hbm},
        {"wco": wco_ref, "in": in_ref, "out": out_ref, "down": down_ref, "up": up_ref},
        sems,
    )

    weights.copy("wco").start()
    for part in range(steps):
        weights.copy("in", part).start()
        weights.copy("out", part).start()
    weights.copy("down").start()
    weights.copy("up").start()
    weights.wait("wco")
    second = n_ref[...] + nn(catt_ref[...], wco_ref[...])
    hat, scale = norm_rows(second)
    middle = hat * cgain_ref[...]
    acc_ref[...] = middle
    low_ref[...] = middle.astype(BF)
    scale_ref[:, 0:1] = scale

    def forward(part, carry):
        weights.wait("in", part)
        weights.wait("out", part)
        ffn_step(
            low_ref, acc_ref, weights.part("in", part), weights.part("out", part),
            slope_ref.at[part], None, None, None,
        )
        return carry

    lax.fori_loop(0, steps, forward, 0)

    weights.wait("down")
    weights.wait("up")
    ffn_step(
        low_ref, acc_ref, down_ref, up_ref, pre_slope_ref, act_ref, downb_ref, adapter_scale
    )
    gain = gain_ref[1:2]
    hat, scale = norm_rows(acc_ref[...] + adapter_scale * upb_ref[...])
    row = lax.broadcasted_iota(jnp.int32, (low_ref.shape[0], 1), 0)
    valid = row < len_ref[0, which]
    y_ref[...] = jnp.where(valid, hat * gain, 0.0).astype(BF)
    cot = jnp.where(valid, cot_ref[...].astype(F32), 0.0)
    grad = norm_rows_back(hat, scale, cot * gain)
    acc_ref[...] = grad
    grad_ref[...] = grad.astype(BF)
    adapter_back(
        grad_ref, acc_ref, low_ref, act_ref, pre_slope_ref, down_ref, up_ref,
        (ddown_ref, ddownb_ref, dup_ref, dupb_ref), pre_ref,
    )

    def backward(part, carry):
        ffn_back_step(
            grad_ref, acc_ref, weights.part("in", part), weights.part("out", part),
            slope_ref.at[part],
        )
        return carry

    lax.fori_loop(0, steps, backward, 0)

    gain = cgain_ref[...]
    hat = low_ref[...].astype(F32) / gain
    grad = norm_rows_back(hat, scale_ref[:, 0:1], acc_ref[...] * gain)
    dsecond_ref[...] = grad
    dcatt_ref[...] = nt(grad.astype(BF), wco_ref[...]).astype(BF)


def dec_ffn(lengths, n, catt, cot, w, cross, which):
    rows, width = catt.shape
    hidden = w["ffn_in"].shape[1]
    steps = hidden // wide
    weights = [cross["out"], w["ffn_in"], w["ffn_out"], w["down"], w["up"]]
    return pl.pallas_call(
        functools.partial(dec_ffn_kernel, steps=steps, which=which),
        grid=(1,),
        in_specs=[
            pl.BlockSpec(memory_space=pltpu.SMEM),
            pl.BlockSpec((rows, width), lambda i: (which, 0)),
            whole((rows, width)),
            pl.BlockSpec((rows, width), lambda i: (which, 0)),
            whole((1, width)),
            whole((2, width)),
            whole((1, chunk)),
            whole((1, width)),
        ]
        + [pl.BlockSpec(memory_space=pl.ANY)] * len(weights),
        out_specs=[
            whole((rows, width)),
            whole((rows, width)),
            whole((rows, width)),
            whole((width, chunk)),
            whole((1, chunk)),
            whole((chunk, width)),
            whole((1, width)),
        ],
        out_shape=[
            jax.ShapeDtypeStruct((rows, width), BF),
            jax.ShapeDtypeStruct((rows, width), F32),
            jax.ShapeDtypeStruct((rows, width), BF),
            jax.ShapeDtypeStruct((width, chunk), F32),
            jax.ShapeDtypeStruct((1, chunk), F32),
            jax.ShapeDtypeStruct((chunk, width), F32),
            jax.ShapeDtypeStruct((1, width), F32),
        ],
        scratch_shapes=[
            pltpu.VMEM((rows, width), F32),
            pltpu.VMEM((rows, width), BF),
            pltpu.VMEM((rows, width), BF),
            pltpu.VMEM((steps, rows, wide), BF),
            pltpu.VMEM((rows, chunk), BF),
            pltpu.VMEM((rows, chunk), BF),
            pltpu.VMEM((rows, chunk), BF),
            pltpu.VMEM((rows, LANES), F32),
        ]
        + weight_scratch(weights, steps),
        compiler_params=params(),
        name="dec_ffn",
    )(
        lengths, n, catt, cot, cross["gain"], w["gains"], w["down_bias"], w["up_bias"], *weights
    )


def dec_mid_back_kernel(
    dsecond0_ref, dsecond1_ref, dcq0_ref, dcq1_ref, wq_ref, n_ref, scale_ref, gain_ref, wo_ref,
    dfirst_ref, datt_ref,
):
    for pair, (dsecond_ref, dcq_ref) in enumerate(
        ((dsecond0_ref, dcq0_ref), (dsecond1_ref, dcq1_ref))
    ):
        rows = slice(pair * TGT, (pair + 1) * TGT)
        gain = gain_ref[0:1]
        total = dsecond_ref[...] + nt(dcq_ref[...], wq_ref[...])
        grad = norm_rows_back(n_ref[rows] / gain, scale_ref[rows, 0:1], total * gain)
        dfirst_ref[rows] = grad
        datt_ref[rows] = nt(grad.astype(BF), wo_ref[...]).astype(BF)


def dec_mid_back(dseconds, dcqs, n, scale, w, cross):
    rows, width = n.shape
    return pl.pallas_call(
        dec_mid_back_kernel,
        out_shape=[
            jax.ShapeDtypeStruct((rows, width), F32),
            jax.ShapeDtypeStruct((rows, width), BF),
        ],
        compiler_params=params(),
        name="dec_mid_back",
    )(*dseconds, *dcqs, cross["query"], n, scale, w["gains"], w["out"])


enc_segs = ((0, SRC_LONG, 0, SRC_LONG), (SRC_LONG, SRC_SHORT, SRC_LONG, SRC_SHORT))
dec_segs = ((0, TGT, 0, TGT), (TGT, TGT, TGT, TGT))
cross_segs = (((0, TGT, 0, SRC_LONG),), ((0, TGT, SRC_LONG % ENC_ROWS, SRC_SHORT),))


def self_columns(qkv):
    rows = qkv.shape[0]
    return (qkv, rows, 0, 0), [(qkv, rows, 0, 8)], [(qkv, rows, 0, 16)]


def cross_columns(cq, kvs, which):
    return (
        (cq, TGT, which, 0),
        [(kv, ENC_ROWS, 0, 0) for kv in kvs],
        [(kv, ENC_ROWS, 0, 8) for kv in kvs],
    )


def decoder_self(t, lengths, w, cross):
    qkv = product(t, w["qkv"])
    att, inv, *weights = attend(lengths, *self_columns(qkv), w["prefix"], dec_segs, True, group=2)
    n, scale, cq = dec_mid(t, att, w, cross)
    return cq, (qkv, att, inv, weights, n, scale)


def cross_forward(lengths, cq, kvs, which):
    return attend(
        lengths, *cross_columns(cq, kvs, which), None, cross_segs[which], False, which, group=2
    )


def cross_backward(cq, kvs, forward, dcatt, which):
    catt, inv, *weights = forward
    return attend_back(
        *cross_columns(cq, kvs, which), None, catt, inv, dcatt, weights, cross_segs[which]
    )


def decoder_self_back(kept, dseconds, dcqs, w, cross):
    qkv, att, inv, weights, n, scale = kept
    dfirst, datt = dec_mid_back(dseconds, dcqs, n, scale, w, cross)
    dq, dk, dv, *dprefix = attend_back(
        *self_columns(qkv), w["prefix"], att, inv, datt, weights, dec_segs
    )
    return back_product([dq, dk, dv], w["qkv"], dfirst)[0], dprefix


def small_shape(devices):
    return 8, 8 * (2 * chunk) // devices


def finish_kernel(
    q_ref, k_ref, v_ref, o_ref, inv_ref, g0_ref, g1_ref, g2_ref, pk_ref, pv_ref, pl_ref, ps_ref,
    dfirst0_ref, dfirst1_ref, dfirst2_ref, wqkv_ref,
    low0, low1, low2, act0, act1, act2, grad0, grad1, grad2, pre0, pre1, pre2,
    long_down, long_downb, long_up, long_upb,
    short_down, short_downb, short_up, short_upb, dpk_ref, dpv_ref,
    y0_ref, y1_ref, dt_ref,
    source_ref, y_ref, target_ref, o_up_ref, o_down_ref, o_prefix_ref, o_upb_ref, o_downb_ref,
    dq, dk, dv, small, lows_all, acts_all, grads_all, pres_all, ups, downs, mine, theirs, half_sum, across_y, y_sum, landed, total, result,
    small_landed, small_total, small_result, dx, dx_landed, lows, lows_landed,
    load_sems, pair_sems, y_sems, z_sems, gather_sems, share_y_sems, back_sems,
    small_sems, share_sems, cross_sems,
    *, devices,
):
    step = pl.program_id(0)
    pairs = 8
    section = lax.axis_index("section")
    is_encoder = section == 0
    chips = devices // 2
    line = chips // 2
    slices = 16 // line
    rows = 2 * chunk
    half = rows // 2
    size = half // slices
    side = size // 2
    part = side // line
    place = lax.axis_index("dp")
    core, chip = lax.rem(place, 2), place // 2
    bit, at_line = lax.rem(chip, 2), chip // 2
    partner = place + 1 - 2 * core
    beside = place + 2 - 4 * bit
    small_rows, small_cols = small_shape(devices)
    tile = 256
    width = 2 * chunk
    scale = 1.0 / devices

    def aligned(value, unit=16):
        return pl.multiple_of(value, unit)

    def along(distance):
        return (lax.rem(at_line + distance, line) * 2 + bit) * 2 + core

    def remote(source, target, send_sem, recv_sem, other):
        return pltpu.make_async_remote_copy(
            src_ref=source, dst_ref=target, send_sem=send_sem, recv_sem=recv_sem,
            device_id=other, device_id_type=pl.DeviceIdType.MESH,
        )

    def in_group(other):
        return {"dp": other}

    across = {"section": 1 - section}
    kept = aligned(core * half)
    given = aligned((1 - core) * half)

    def swap():
        return remote(
            mine.at[pl.ds(given, half)], theirs, pair_sems.at[0], pair_sems.at[1],
            in_group(partner),
        )

    def y_send(j):
        there = pl.ds(aligned(j * size + (1 - bit) * side), side)
        return remote(
            half_sum.at[there], across_y.at[j], y_sems.at[0, j], y_sems.at[1, j], in_group(beside)
        )

    def z_send(j, s):
        there = pl.ds(aligned(lax.rem(at_line + s, line) * part), part)
        return remote(
            y_sum.at[j].at[there], landed.at[j, s - 1],
            z_sems.at[0, j, s - 1], z_sems.at[1, j, s - 1], in_group(along(s)),
        )

    def own_rows(j):
        return pl.ds(aligned(kept + j * size + bit * side + at_line * part), part)

    def own_side(j):
        return pl.ds(aligned(kept + j * size + bit * side), side)

    def other_side(j):
        return pl.ds(aligned(kept + j * size + (1 - bit) * side), side)

    def gather(j, s):
        return remote(
            total.at[j], result.at[own_rows(j)],
            gather_sems.at[0, j, s - 1], gather_sems.at[1, j, s - 1], in_group(along(s)),
        )

    def y_share(j):
        return remote(
            result.at[own_side(j)], result.at[own_side(j)],
            share_y_sems.at[0, j], share_y_sems.at[1, j], in_group(beside),
        )

    def back(j, i):
        there = own_side(j) if i == 0 else other_side(j)
        return remote(
            result.at[there], result.at[there],
            back_sems.at[0, j, i], back_sems.at[1, j, i], in_group(partner),
        )

    def piece(index):
        row = aligned(lax.rem(index, 8) * small_rows, 8)
        col = aligned((index // 8) * small_cols, LANES)
        return pl.ds(row, small_rows), pl.ds(col, small_cols)

    def small_out(s):
        return remote(
            small.at[piece(lax.rem(place + s, devices))], small_landed.at[s - 1],
            small_sems.at[0, s - 1], small_sems.at[1, s - 1],
            in_group(lax.rem(place + s, devices)),
        )

    def small_share(s):
        return remote(
            small_total, small_result.at[piece(place)],
            share_sems.at[0, s - 1], share_sems.at[1, s - 1],
            in_group(lax.rem(place + s, devices)),
        )

    def send_low():
        return remote(lows, lows_landed, cross_sems.at[0, 0], cross_sems.at[1, 0], across)

    def send_high(i):
        return remote(
            dx.at[i], dx_landed.at[i], cross_sems.at[0, 1 + i], cross_sems.at[1, 1 + i], across
        )

    def greet(barrier, other):
        pl.semaphore_signal(
            barrier, inc=1, device_id=other, device_id_type=pl.DeviceIdType.MESH
        )

    def load(source, target, i):
        return pltpu.make_async_copy(source, target, load_sems.at[i])

    enc_loads = [
        load(source, target.at[i * ENC_ROWS : (i + 1) * ENC_ROWS], 3 * n + i)
        for n, (target, sources) in enumerate((
            (lows_all, (low0, low1, low2)), (acts_all, (act0, act1, act2)),
            (grads_all, (grad0, grad1, grad2)), (pres_all, (pre0, pre1, pre2)),
        ))
        for i, source in enumerate(sources)
    ]
    dec_loads = [
        load(long_up, ups.at[0], 0), load(long_down, downs.at[0], 1),
        load(short_up, ups.at[1], 2), load(short_down, downs.at[1], 3),
    ]

    @pl.when(step == 0)
    def _():
        barrier = pltpu.get_barrier_semaphore()
        for s in range(1, devices):
            greet(barrier, in_group(lax.rem(place + s, devices)))

        @pl.when(is_encoder)
        def _():
            for copy in enc_loads:
                copy.start()

        @pl.when(jnp.logical_not(is_encoder))
        def _():
            for copy in dec_loads:
                copy.start()

    @pl.when(is_encoder & (step < pairs))
    def _():
        at = aligned(step * LANES, LANES)
        lanes = pl.ds(at, LANES)
        prefix_totals = attend_back_pair(
            q_ref, [k_ref], [v_ref], o_ref, inv_ref, [g0_ref, g1_ref, g2_ref], pk_ref, pv_ref,
            (pl_ref, ps_ref), dq.at[:, lanes], dk.at[:, lanes], dv.at[:, lanes], enc_segs,
        )
        small[0:PRE_PAD, lanes] = prefix_totals[0] * scale
        small[PRE_PAD : 2 * PRE_PAD, lanes] = prefix_totals[1] * scale

    @pl.when(step == 0)
    def _():
        barrier = pltpu.get_barrier_semaphore()

        def pack(up, down):
            mine[0:chunk] = (up * scale).astype(BF)
            down = (down * scale).astype(BF)
            mine[chunk:width, 0:chunk] = down[0:chunk]
            mine[chunk:width, chunk:width] = down[chunk:width]

        @pl.when(is_encoder)
        def _():
            for copy in enc_loads:
                copy.wait()
            pack(
                adapter_scale * tn(acts_all[...], grads_all[...]),
                tn(lows_all[...], pres_all[...]),
            )
            pl.semaphore_wait(barrier, devices - 1)
            greet(barrier, across)

        @pl.when(jnp.logical_not(is_encoder))
        def _():
            for copy in dec_loads:
                copy.wait()
            pack(ups[0] + ups[1], downs[0] + downs[1])
            pl.semaphore_wait(barrier, devices)
            greet(barrier, across)

        swap().start()

        @pl.when(jnp.logical_not(is_encoder))
        def _():
            low = width // 2
            lows[0, 0:TGT] = y0_ref[:, 0:low]
            lows[0, TGT : 2 * TGT] = y1_ref[:, 0:low]
            lows[1] = dt_ref[:, 0:low]
            send_low().start()
            small[0:PRE_PAD] = dpk_ref[...] * scale
            small[PRE_PAD : 2 * PRE_PAD] = dpv_ref[...] * scale

    @pl.when(step == 1)
    def _():
        swap().wait()
        half_sum[...] = (
            mine[pl.ds(kept, half)].astype(F32) + theirs[...].astype(F32)
        ).astype(BF)
        for j in range(min(2, slices)):
            y_send(j).start()

    for j in range(slices):

        @pl.when(step == 2 + j)
        def _(j=j):
            y_send(j).wait()
            if j + 2 < slices:
                y_send(j + 2).start()
            own = pl.ds(aligned(j * size + bit * side), side)
            y_sum[j] = (half_sum[own].astype(F32) + across_y[j].astype(F32)).astype(BF)
            for s in range(1, line):
                z_send(j, s).start()

        @pl.when(step == 4 + j)
        def _(j=j):
            summed = y_sum[j, pl.ds(aligned(at_line * part), part)].astype(F32)
            for s in range(1, line):
                z_send(j, s).wait()
                summed = summed + landed[j, s - 1].astype(F32)
            total[j] = summed.astype(BF)
            result[own_rows(j)] = total[j]
            for s in range(1, line):
                gather(j, s).start()

        @pl.when(step == 6 + j)
        def _(j=j):
            for s in range(1, line):
                gather(j, s).wait()
            y_share(j).start()
            back(j, 0).start()

        @pl.when(step == 8 + j)
        def _(j=j):
            y_share(j).wait()
            back(j, 1).start()

    @pl.when(step == pairs - 1)
    def _():
        @pl.when(is_encoder)
        def _():
            up_row = jnp.sum(grads_all[...].astype(F32), axis=0, keepdims=True)
            down_row = jnp.sum(pres_all[...].astype(F32), axis=0, keepdims=True)
            down_row = jnp.concatenate([down_row, jnp.zeros_like(down_row)], 1)
            small[PRE : PRE + 1] = up_row * (adapter_scale * scale)
            small[PRE + 1 : PRE + 2] = down_row * scale

        @pl.when(jnp.logical_not(is_encoder))
        def _():
            down_row = long_downb[...] + short_downb[...]
            down_row = jnp.concatenate([down_row, jnp.zeros_like(down_row)], 1)
            small[PRE : PRE + 1] = (long_upb[...] + short_upb[...]) * scale
            small[PRE + 1 : PRE + 2] = down_row * scale

        for s in range(1, devices):
            small_out(s).start()

    @pl.when(is_encoder & (step == pairs))
    def _():
        pl.semaphore_wait(pltpu.get_barrier_semaphore(), 1)

    @pl.when(is_encoder & (step >= pairs))
    def _():
        acc = jnp.concatenate([dfirst0_ref[...], dfirst1_ref[...], dfirst2_ref[...]], 0)
        for n, grad in enumerate((dq, dk, dv)):
            acc = acc + nt(grad[...], wqkv_ref[:, n * width : (n + 1) * width])
        dx[step - pairs] = acc.astype(BF)

    for i in range(2):

        @pl.when(is_encoder & (step == pairs + i))
        def _(i=i):
            send_high(i).start()

    @pl.when(step == pairs + 1)
    def _():
        own_rows_, own_cols = piece(place)
        summed = small[own_rows_, own_cols]
        for s in range(1, devices):
            small_out(s).wait()
            summed = summed + small_landed[s - 1]
        small_total[...] = summed
        small_result[own_rows_, own_cols] = summed
        for s in range(1, devices):
            small_share(s).start()

    @pl.when(step == pairs + 3)
    def _():
        for j in range(slices):
            for i in range(2):
                back(j, i).wait()
        o_up_ref[...] = result[0:chunk]
        o_down_ref[0:chunk] = result[chunk:width, 0:chunk]
        o_down_ref[chunk:width] = result[chunk:width, chunk:width]
        for s in range(1, devices):
            small_share(s).wait()
        o_prefix_ref[0] = small_result[0:PRE]
        o_prefix_ref[1] = small_result[PRE_PAD : PRE_PAD + PRE]
        o_upb_ref[...] = small_result[PRE : PRE + 1]
        o_downb_ref[...] = small_result[PRE + 1 : PRE + 2, 0:chunk]

        @pl.when(is_encoder)
        def _():
            for i in range(2):
                source_ref[:, i * tile : (i + 1) * tile] = dx[2 + i]
            send_low().wait_recv()
            y_ref[...] = lows_landed[0]
            target_ref[...] = lows_landed[1]
            for i in range(2):
                send_high(i).wait_send()

        @pl.when(jnp.logical_not(is_encoder))
        def _():
            low = width // 2
            y_ref[0:TGT] = y0_ref[:, low:width]
            y_ref[TGT : 2 * TGT] = y1_ref[:, low:width]
            target_ref[...] = dt_ref[:, low:width]
            send_low().wait_send()
            for i in range(2):
                send_high(i).wait_recv()
                source_ref[:, i * tile : (i + 1) * tile] = dx_landed[i]


def finish(saved, datts, dfirsts, w, traces, adapters, dec_prefix, ys, dt):
    qkv, att, inv, weights = saved
    devices = lax.axis_size("dp")
    line = devices // 4
    slices = 16 // line
    rows, width = att.shape
    targets = dt.shape[0]
    pairs, tile = 8, 256
    half = width // 2
    side = half // slices // 2
    part = side // line
    small_rows, small_cols = small_shape(devices)

    def mine(value):
        return jnp.where(lax.axis_index("section") == 0, value, 0)

    def head(i):
        return mine(jnp.minimum(i, pairs - 1))

    def pair(offset):
        return pl.BlockSpec((rows, LANES), lambda i: (0, head(i) + offset))

    def at(i):
        return mine(jnp.where(i < pairs + 2, 2 + jnp.maximum(i - pairs, 0), i - pairs - 2))

    def once(shape):
        return pl.BlockSpec(shape, lambda i: (0,) * len(shape), pipeline_mode=pl.Buffered(1))

    anywhere = pl.BlockSpec(memory_space=pl.ANY)
    prefix_pair = pl.BlockSpec((PRE_PAD, LANES), lambda i: (0, head(i)))
    vmem = pltpu.VMEM
    dma = pltpu.SemaphoreType.DMA
    flat = [a for group in [*traces, *adapters] for a in group]
    return pl.pallas_call(
        functools.partial(finish_kernel, devices=devices),
        grid=(pairs + 4,),
        in_specs=[pair(0), pair(8), pair(16), pair(0), pair(0)]
        + [pl.BlockSpec((ENC_ROWS, LANES), lambda i: (0, head(i)))] * 3
        + [prefix_pair] * 2
        + [
            pl.BlockSpec((2,) + p.shape[1:], lambda i: (head(i), 0, 0))
            for p in weights
        ]
        + [
            pl.BlockSpec((ENC_ROWS, tile), lambda i: (0, at(i))),
        ]
        * 3
        + [
            pl.BlockSpec((tile, 3 * width), lambda i: (at(i), 0)),
        ]
        + [anywhere if a.shape[0] > 1 else once(a.shape) for a in flat]
        + [once(a.shape) for a in (*dec_prefix, *ys, dt)],
        out_specs=[
            once((rows, half)), once((targets, half)), once((targets, half)),
            once((chunk, width)), once((width, chunk)),
            once((2, PRE, width)), once((1, width)), once((1, chunk)),
        ],
        out_shape=[
            jax.ShapeDtypeStruct((rows, half), BF),
            jax.ShapeDtypeStruct((targets, half), BF),
            jax.ShapeDtypeStruct((targets, half), BF),
            jax.ShapeDtypeStruct((chunk, width), BF),
            jax.ShapeDtypeStruct((width, chunk), BF),
            jax.ShapeDtypeStruct((2, PRE, width), F32),
            jax.ShapeDtypeStruct((1, width), F32),
            jax.ShapeDtypeStruct((1, chunk), F32),
        ],
        scratch_shapes=[
            vmem((rows, width), BF), vmem((rows, width), BF), vmem((rows, width), BF),
            vmem((2 * PRE_PAD, width), F32),
            vmem((rows, width), BF), vmem((rows, chunk), BF),
            vmem((rows, width), BF), vmem((rows, chunk), BF),
            vmem((2, chunk, width), F32), vmem((2, width, chunk), F32),
            vmem((width, width), BF), vmem((half, width), BF), vmem((half, width), BF),
            vmem((slices, side, width), BF), vmem((slices, side, width), BF),
            vmem((slices, line - 1, part, width), BF), vmem((slices, part, width), BF),
            vmem((width, width), BF),
            vmem((devices - 1, small_rows, small_cols), F32), vmem((small_rows, small_cols), F32),
            vmem((2 * PRE_PAD, width), F32),
            vmem((4, rows, tile), BF), vmem((2, rows, tile), BF),
            vmem((2, targets, half), BF), vmem((2, targets, half), BF),
            dma((12,)), dma((2,)), dma((2, slices)), dma((2, slices, line - 1)),
            dma((2, slices, line - 1)), dma((2, slices)), dma((2, slices, 2)),
            dma((2, devices - 1)), dma((2, devices - 1)), dma((2, 3)),
        ],
        compiler_params=pltpu.CompilerParams(
            vmem_limit_bytes=60 * 2**20, collective_id=0, has_side_effects=True
        ),
        name="finish",
    )(
        qkv, qkv, qkv, att, inv, *datts, *w["prefix"], *weights,
        *dfirsts, w["qkv"], *flat, *dec_prefix, *ys, dt,
    )


def blank_kernel(*refs):
    pass


def blanks(shapes):
    return pl.pallas_call(
        blank_kernel,
        out_shape=list(shapes),
        out_specs=[pl.BlockSpec(memory_space=pl.ANY)] * len(shapes),
        name="blank",
    )()


def on_section(is_encoder, encoder_work, decoder_work, *operands):
    enc_shapes, _ = jax.eval_shape(encoder_work, *operands)
    dec_shapes, _ = jax.eval_shape(decoder_work, *operands)

    def blank_like(shapes):
        leaves, tree = jax.tree.flatten(shapes)
        if not leaves:
            return shapes
        return jax.tree.unflatten(tree, blanks(leaves))

    def encoder_branch(*a):
        own, shared = encoder_work(*a)
        return own, blank_like(dec_shapes), shared

    def decoder_branch(*a):
        own, shared = decoder_work(*a)
        return blank_like(enc_shapes), own, shared

    return lax.cond(is_encoder, encoder_branch, decoder_branch, *operands)


def to_decoder(block):
    return lax.ppermute(block, "section", [(0, 1)])


def to_encoder(block):
    return lax.ppermute(block, "section", [(1, 0)])


def per_device(
    sources, targets, cotangent, source_lengths, target_lengths,
    attn_qkv, attn_out, ffn_in, ffn_out, norm_gains, prefix_pairs,
    adapt_down, adapt_down_bias, adapt_up, adapt_up_bias,
    cross_query, cross_pairs, cross_out, cross_gain,
):
    is_encoder = lax.axis_index("section") == 0
    prefix = jnp.pad(prefix_pairs[0], ((0, 0), (0, PRE_PAD - PRE), (0, 0)))
    w = dict(
        qkv=attn_qkv[0], out=attn_out[0], ffn_in=ffn_in[0], ffn_out=ffn_out[0],
        gains=norm_gains[0], prefix=(prefix[0], prefix[1]),
        down=adapt_down[0], down_bias=adapt_down_bias,
        up=adapt_up[0], up_bias=adapt_up_bias,
    )
    cross = dict(query=cross_query, pairs=cross_pairs, out=cross_out, gain=cross_gain[None])

    def at_encoder(work, *operands):
        return on_section(is_encoder, lambda *a: (work(*a), ()), lambda *a: ((), ()), *operands)[0]

    def at_decoder(work, *operands):
        return on_section(is_encoder, lambda *a: ((), ()), lambda *a: (work(*a), ()), *operands)[1]

    def at_both(enc_work, dec_work, *operands):
        return on_section(
            is_encoder, lambda *a: (enc_work(*a), ()), lambda *a: (dec_work(*a), ()), *operands
        )[:2]

    def encoder_start():
        qkv = product(sources, w["qkv"])
        att, inv, *weights = attend(
            source_lengths, *self_columns(qkv), w["prefix"], enc_segs, False, checked=True
        )
        return (qkv, att, inv, weights), enc_ffn(sources, att, w, 2)

    (saved, part2), (cq, kept) = at_both(
        encoder_start, lambda: decoder_self(targets, target_lengths, w, cross)
    )
    mem2 = to_decoder(part2[0])
    part1 = at_encoder(lambda saved: enc_ffn(sources, saved[1], w, 1), saved)
    mem1 = to_decoder(part1[0])

    def decoder_short(mem2, cq, kept):
        kv2 = product(mem2, cross["pairs"])
        forward = cross_forward(source_lengths, cq, [kv2], 1)
        return kv2, forward, dec_ffn(
            target_lengths, kept[4], forward[0], cotangent, w, cross, 1
        )

    part0 = at_encoder(lambda saved: enc_ffn(sources, saved[1], w, 0), saved)
    mem2, last = lax.optimization_barrier((mem2, part0[0]))
    mem0 = to_decoder(last)
    kv2, short, short_ffn = at_decoder(decoder_short, mem2, cq, kept)
    mem1, kv2 = lax.optimization_barrier((mem1, kv2))
    kv1 = at_decoder(lambda mem1: product(mem1, cross["pairs"]), mem1)

    def decoder_long(mem0, kv1, kv2, cq, kept):
        kvs = [product(mem0, cross["pairs"]), kv1, kv2]
        long = cross_forward(source_lengths, cq, kvs, 0)
        y, dsecond, dcatt, *adapter = dec_ffn(
            target_lengths, kept[4], long[0], cotangent, w, cross, 0
        )
        dcq, dck, dcv = cross_backward(cq, kvs, long, dcatt, 0)
        cuts = ((0, ENC_ROWS), (ENC_ROWS, ENC_ROWS), (2 * ENC_ROWS, SRC_LONG - 2 * ENC_ROWS))
        return back_product([dck, dcv], cross["pairs"], cuts=cuts), y, dsecond, dcq, adapter

    dmems, *long = at_decoder(decoder_long, mem0, kv1, kv2, cq, kept)

    def decoder_short_back(kv2, cq, short, dcatt):
        dcq, dck, dcv = cross_backward(cq, [kv2], short, dcatt, 1)
        return back_product([dck, dcv], cross["pairs"])[0], dcq

    short_y, short_second, short_dcatt, *short_adapter = short_ffn
    short_dcatt, first = lax.optimization_barrier((short_dcatt, dmems[0]))
    dmem_short, short_cq = at_decoder(decoder_short_back, kv2, cq, short, short_dcatt)
    dmem0 = to_encoder(first)
    others = lax.optimization_barrier((dmems[1], dmems[2], dmem_short))
    dmem1, dmem2, dmem_short = [to_encoder(block) for block in others]

    def decoder_end(kept, *grads):
        return decoder_self_back(kept, grads[:2], grads[2:], w, cross)

    (long_y, long_second, long_cq, long_adapter) = long
    dt, dec_prefix = at_decoder(
        decoder_end, kept, long_second, short_second, long_cq, short_cq
    )
    dmem0, dt = lax.optimization_barrier((dmem0, dt))
    def back_part(blocks, part, before):
        if before is not None:
            mem, _ = lax.optimization_barrier((part[0], before[1]))
            part = (mem, *part[1:])
        return at_encoder(lambda blocks, part: enc_ffn_back(blocks, part, w), blocks, part)

    back0 = back_part([dmem0], part0, None)
    back1 = back_part([dmem1], part1, back0)
    back2 = back_part([dmem2, dmem_short], part2, back1)
    parts = (part0, part1, part2)
    backs = (back0, back1, back2)
    source_grad, y, target_grad, up, down, prefix_grad, up_bias, down_bias = finish(
        saved, [b[1] for b in backs], [b[0] for b in backs], w,
        [
            [p[4] for p in parts], [p[3] for p in parts],
            [b[2] for b in backs], [b[3] for b in backs],
        ],
        [long_adapter, short_adapter], dec_prefix, [long_y, short_y], dt,
    )
    return (
        y,
        source_grad,
        target_grad,
        prefix_grad[None],
        down.astype(F32)[None],
        down_bias,
        up.astype(F32)[None],
        up_bias,
    )


def solution(mesh):
    layer2, layer3, rows = P("section", None), P("section", None, None), P("dp", None)
    return jax.shard_map(
        per_device,
        mesh=mesh,
        in_specs=(
            rows, rows, rows, rows, rows,
            layer3, layer3, layer3, layer3, layer3,
            P("section", None, None, None),
            layer3, layer2, layer3, layer2,
            P(), P(), P(), P(),
        ),
        out_specs=(
            P("dp", "section"), P("dp", "section"), P("dp", "section"),
            P("section", None, None, None), layer3, layer2, layer3, layer2,
        ),
        check_vma=False,
    )
```

```python
import functools

import jax
import jax.numpy as jnp
from jax import lax
from jax.experimental import pallas as pl
from jax.experimental.pallas import tpu as pltpu
from jax.sharding import PartitionSpec as P

HD = 64
PRE = 30
PRE_PAD = 32
SRC_LONG = 768
SRC_SHORT = 96
TGT = 256
LANES = 128

BF = jnp.bfloat16
F32 = jnp.float32
norm_eps = 1e-05
big_negative = -1e30
adapter_scale = 4.0
chunk = 512
wide = 1024
ENC_ROWS = (SRC_LONG + SRC_SHORT) // 3
vmem_bytes = 56 * 2**20

phi_poly = (
    0.797869713181688,
    0.036392283539041996,
    -8.782472977701046e-05,
    -3.669384069669515e-05,
    1.4250308145882202e-06,
)


def nn(left, right):
    return lax.dot_general(left, right, (((1,), (0,)), ((), ())), preferred_element_type=F32)


def nt(left, right):
    return lax.dot_general(left, right, (((1,), (1,)), ((), ())), preferred_element_type=F32)


def tn(left, right):
    return lax.dot_general(left, right, (((0,), (0,)), ((), ())), preferred_element_type=F32)


def gelu_pair(values):
    square = values * values
    poly = phi_poly[4]
    for coefficient in phi_poly[3::-1]:
        poly = poly * square + coefficient
    half = 0.5 * jnp.tanh(values * poly) + 0.5
    density = jnp.exp(square * -0.5) * 0.3989422804014327
    return values * half, half + values * density


def row_tiles(rows, most=432):
    count = -(-rows // most)
    size = rows // count
    return [(i * size, size) for i in range(count)]


def norm_rows(values):
    centered = values - jnp.mean(values, axis=-1, keepdims=True)
    scale = lax.rsqrt(jnp.mean(centered * centered, axis=-1, keepdims=True) + norm_eps)
    return centered * scale, scale


def norm_rows_back(hat, scale, grad_hat):
    mean_grad = jnp.mean(grad_hat, axis=-1, keepdims=True)
    mean_dot = jnp.mean(grad_hat * hat, axis=-1, keepdims=True)
    return scale * (grad_hat - mean_grad - hat * mean_dot)


def params(limit=vmem_bytes):
    return pltpu.CompilerParams(vmem_limit_bytes=limit)


def whole(shape):
    return pl.BlockSpec(shape, lambda *g: (0,) * len(shape))


def single(shape):
    return pl.BlockSpec(shape, lambda *g: (0,) * len(shape), pipeline_mode=pl.Buffered(1))


def product_kernel(x_ref, w_ref, o_ref):
    o_ref[...] = nn(x_ref[...], w_ref[...]).astype(BF)


def product(x, w, tile=1024):
    rows, depth = x.shape
    width = w.shape[1]
    return pl.pallas_call(
        product_kernel,
        grid=(width // tile,),
        in_specs=[whole((rows, depth)), pl.BlockSpec((depth, tile), lambda i: (0, i))],
        out_specs=pl.BlockSpec((rows, tile), lambda i: (0, i)),
        out_shape=jax.ShapeDtypeStruct((rows, width), BF),
        compiler_params=params(),
        name="product",
    )(x, w)


def back_product_kernel(*refs, parts, residual, cuts):
    grads = refs[:parts]
    w_ref = refs[parts]
    outs = refs[-len(cuts) :]
    total = None
    width = grads[0].shape[1]
    for i, grad in enumerate(grads):
        term = nt(grad[...], w_ref[:, i * width : (i + 1) * width])
        total = term if total is None else total + term
    if residual:
        total = total + refs[parts + 1][...]
    for (start, size), o_ref in zip(cuts, outs):
        o_ref[...] = total[start : start + size].astype(BF)


def back_product(grads, w, residual=None, tile=512, cuts=None):
    rows, width = grads[0].shape
    depth = w.shape[0]
    parts = len(grads)
    cuts = cuts or ((0, rows),)
    specs = [whole((rows, width))] * parts + [
        pl.BlockSpec((tile, parts * width), lambda i: (i, 0))
    ]
    args = list(grads) + [w]
    if residual is not None:
        specs.append(pl.BlockSpec((rows, tile), lambda i: (0, i)))
        args.append(residual)
    return pl.pallas_call(
        functools.partial(
            back_product_kernel, parts=parts, residual=residual is not None, cuts=cuts
        ),
        grid=(depth // tile,),
        in_specs=specs,
        out_specs=[pl.BlockSpec((size, tile), lambda i: (0, i)) for _, size in cuts],
        out_shape=[jax.ShapeDtypeStruct((size, depth), BF) for _, size in cuts],
        compiler_params=params(),
        name="back_product",
    )(*args)


def head_lanes(head):
    lane = lax.broadcasted_iota(jnp.int32, (1, LANES), 1)
    own = (lane < HD) if head == 0 else (lane >= HD)
    first = HD if head == 0 else 0
    return own, lane == first, lane == first + 1


def bf(value):
    return jnp.asarray(value, BF)


def rows_of(refs, start, count):
    parts = []
    for ref in refs:
        size = ref.shape[0]
        low, high = max(start, 0), min(start + count, size)
        if low < high:
            parts.append(ref[low:high])
        start -= size
    return parts


def stacked(refs, prefix_ref, start, count):
    parts = rows_of(refs, start, count)
    if prefix_ref is not None:
        parts.append(prefix_ref[...])
    return parts[0] if len(parts) == 1 else jnp.concatenate(parts, 0)


def attend_pair(*refs, segs, prefix, causal, pieces, which, checked):
    len_ref, q_ref = refs[:2]
    k_refs, v_refs = refs[2 : 2 + pieces], refs[2 + pieces : 2 + 2 * pieces]
    at = 2 + 2 * pieces
    pk_ref = pv_ref = None
    if prefix:
        pk_ref, pv_ref = refs[at : at + 2]
        at += 2
    o_ref, inv_ref = refs[at : at + 2]
    p_refs = refs[at + 2 :]

    def work(peaked):
        for seg, (q0, nq, k0, nk) in enumerate(segs):
            keys = stacked(k_refs, pk_ref, k0, nk)
            values = stacked(v_refs, pv_ref, k0, nk)
            count = keys.shape[0]
            row = lax.broadcasted_iota(jnp.int32, (count, 1), 0)
            seen = row < jnp.minimum(len_ref[0, which + seg], nk)
            if prefix:
                seen = seen | ((row >= nk) & (row < nk + PRE))
            queries = q_ref[q0 : q0 + nq] * bf(HD**-0.5)
            out = inv = None
            across = nq >= 4 * LANES
            outs, invs = [], []
            if across:
                turned = values.T
                ones = jnp.ones((16, count), BF)
            for head in range(2):
                own, first, _ = head_lanes(head)
                k_own = jnp.where(own, keys, jnp.where(first & ~seen, bf(big_negative), bf(0)))
                q_own = jnp.where(own, queries, jnp.where(first, bf(1), bf(0)))
                scores = nt(k_own, q_own)
                if causal:
                    key_at = lax.broadcasted_iota(jnp.int32, scores.shape, 0)
                    query_at = lax.broadcasted_iota(jnp.int32, scores.shape, 1)
                    allowed = (key_at <= query_at) | (key_at >= nk)
                    scores = jnp.where(allowed, scores, big_negative)
                if peaked:
                    scores = scores - jnp.max(scores, axis=0, keepdims=True)
                weights = jnp.exp(scores).astype(BF)
                p_refs[seg][head] = weights
                if across:
                    rows = jnp.concatenate([turned[head * HD : (head + 1) * HD], ones], 0)
                    mixed = nn(rows, weights)
                    inverse = 1.0 / mixed[HD : HD + 1]
                    outs.append(mixed[:HD] * inverse)
                    invs.append(jnp.broadcast_to(inverse, (HD, nq)))
                    continue
                mixed = tn(weights, jnp.where(own, values, bf(1)))
                inverse = 1.0 / pltpu.roll(mixed, HD, 1)
                mixed = mixed * inverse
                out = mixed if out is None else jnp.where(own, mixed, out)
                inv = inverse if inv is None else jnp.where(own, inverse, inv)
            if across:
                out = jnp.concatenate(outs, 0).T
                inv = jnp.concatenate(invs, 0).T
            o_ref[q0 : q0 + nq] = out.astype(BF)
            inv_ref[q0 : q0 + nq] = inv

    if not checked:
        work(True)
        return

    limit = 50.0**2
    head_row = lax.broadcasted_iota(jnp.int32, (LANES, LANES), 0) // HD
    head_col = lax.broadcasted_iota(jnp.int32, (LANES, LANES), 1) // HD
    same_head = jnp.where(head_row == head_col, 1.0, 0.0).astype(BF)

    def largest(array):
        square = (array.astype(F32) * array.astype(F32)).astype(BF)
        return jnp.max(nn(square, same_head), axis=0, keepdims=True)

    key_peak = largest(k_refs[0][...])
    for ref in k_refs[1:]:
        key_peak = jnp.maximum(key_peak, largest(ref[...]))
    if prefix:
        key_peak = jnp.maximum(key_peak, largest(pk_ref[...]))
    small = jnp.max(largest(q_ref[...]) * key_peak) * (1.0 / HD) <= limit

    @pl.when(small)
    def _():
        work(False)

    @pl.when(jnp.logical_not(small))
    def _():
        work(True)


def lane_views(refs, group, j):
    views = []
    for ref in refs:
        if len(ref.shape) == 2:
            views.append(ref.at[:, j * LANES : (j + 1) * LANES])
        else:
            views.append(ref.at[2 * j : 2 * j + 2])
    return views


def attend_kernel(len_ref, *refs, group, **kw):
    for j in range(group):
        attend_pair(len_ref, *lane_views(refs, group, j), **kw)


def column_spec(rows, offset, row_block=0, group=1):
    return pl.BlockSpec((rows, group * LANES), lambda h: (row_block, h + offset // group))


def attend(lengths, q, keys, values, prefixes, segs, causal, which=0, group=1, checked=False):
    pairs = 8
    q_rows = q[1]
    prefix = prefixes is not None
    extra = PRE_PAD if prefix else 0
    specs = [pl.BlockSpec(memory_space=pltpu.SMEM)]
    args = [lengths]
    for array, rows, block, offset in [q, *keys, *values]:
        specs.append(column_spec(rows, offset, block, group))
        args.append(array)
    if prefix:
        specs += [column_spec(PRE_PAD, 0, 0, group)] * 2
        args += list(prefixes)
    weight_shapes = [(2 * pairs, nk + extra, nq) for _, nq, _, nk in segs]
    return pl.pallas_call(
        functools.partial(
            attend_kernel, group=group, segs=segs, prefix=prefix, causal=causal, pieces=len(keys), which=which,
            checked=checked,
        ),
        grid=(pairs // group,),
        in_specs=specs,
        out_specs=[column_spec(q_rows, 0, 0, group)] * 2
        + [pl.BlockSpec((2 * group,) + s[1:], lambda h: (h, 0, 0)) for s in weight_shapes],
        out_shape=[
            jax.ShapeDtypeStruct((q_rows, pairs * LANES), BF),
            jax.ShapeDtypeStruct((q_rows, pairs * LANES), F32),
        ]
        + [jax.ShapeDtypeStruct(s, BF) for s in weight_shapes],
        compiler_params=params(),
        name="attend",
    )(*args)


def attend_back_pair(
    q_ref, k_refs, v_refs, o_ref, inv_ref, g_refs, pk_ref, pv_ref, p_refs, dq_ref, dk_ref, dv_ref, segs
):
    prefix_totals = [None, None]
    scale = HD**-0.5
    for seg, (q0, nq, k0, nk) in enumerate(segs):
        keys = stacked(k_refs, pk_ref, k0, nk)
        values = stacked(v_refs, pv_ref, k0, nk)
        queries = q_ref[q0 : q0 + nq]
        grads = stacked(g_refs, None, q0, nq).astype(F32) * inv_ref[q0 : q0 + nq]
        grads_low = grads.astype(BF)
        dots = grads * o_ref[q0 : q0 + nq].astype(F32)
        dq = dk = dv = None
        across = nq >= LANES and keys.shape[0] >= 4 * LANES
        turned_grads = []
        if across:
            turned = keys.T
        for head in range(2):
            own, first, second = head_lanes(head)
            row_dot = -jnp.sum(jnp.where(own, dots, 0.0), axis=1, keepdims=True)
            high = row_dot.astype(BF)
            rest = (row_dot - high.astype(F32)).astype(BF)
            g_own = jnp.where(
                own, grads_low, jnp.where(first, high, jnp.where(second, rest, bf(0)))
            )
            v_own = jnp.where(own, values, jnp.where(first | second, bf(1), bf(0)))
            weights = p_refs[seg][head]
            score_grad = (weights.astype(F32) * nt(v_own, g_own)).astype(BF)
            dv_head = nn(weights, grads_low)
            dk_head = nn(score_grad, queries)
            dq_head = None if across else tn(score_grad, keys)
            if across:
                turned_grads.append(nn(turned[head * HD : (head + 1) * HD], score_grad))
            if not across:
                dq = dq_head if dq is None else jnp.where(own, dq_head, dq)
            dk = dk_head if dk is None else jnp.where(own, dk_head, dk)
            dv = dv_head if dv is None else jnp.where(own, dv_head, dv)
        if across:
            dq = jnp.concatenate(turned_grads, 0).T
        dk = dk * scale
        dq_ref[q0 : q0 + nq] = (dq * scale).astype(BF)
        at = k0 - segs[0][2]
        dk_ref[at : at + nk] = dk[:nk].astype(BF)
        dv_ref[at : at + nk] = dv[:nk].astype(BF)
        if pk_ref is not None:
            for i, grad in enumerate((dk, dv)):
                part = grad[nk:]
                prefix_totals[i] = part if seg == 0 else prefix_totals[i] + part
    return prefix_totals


def attend_back_kernel(*refs, group, **kw):
    for j in range(group):
        attend_back_views(*lane_views(refs, group, j), **kw)


def attend_back_views(*refs, segs, prefix, pieces):
    q_ref, o_ref, inv_ref, g_ref = refs[:4]
    k_refs, v_refs = refs[4 : 4 + pieces], refs[4 + pieces : 4 + 2 * pieces]
    at = 4 + 2 * pieces
    pk_ref = pv_ref = None
    if prefix:
        pk_ref, pv_ref = refs[at : at + 2]
        at += 2
    outs = refs[at + len(segs) :]
    totals = attend_back_pair(
        q_ref, k_refs, v_refs, o_ref, inv_ref, [g_ref], pk_ref, pv_ref,
        refs[at : at + len(segs)], *outs[:3], segs,
    )
    if prefix:
        outs[3][...] = totals[0]
        outs[4][...] = totals[1]


def attend_back(q, keys, values, prefixes, attended, inverse, grad, weights, segs, group=2):
    pairs = 8
    q_rows = q[1]
    k_rows = sum(nk for _, _, _, nk in segs)
    prefix = prefixes is not None
    specs, args = [], []
    own = [(a, q_rows, 0, 0) for a in (attended, inverse, grad)]
    for array, rows, block, offset in [q, *own, *keys, *values]:
        specs.append(column_spec(rows, offset, block, group))
        args.append(array)
    if prefix:
        specs += [column_spec(PRE_PAD, 0, 0, group)] * 2
        args += list(prefixes)
    specs += [pl.BlockSpec((2 * group,) + w.shape[1:], lambda h: (h, 0, 0)) for w in weights]
    args += list(weights)
    out_specs = [column_spec(n, 0, 0, group) for n in (q_rows, k_rows, k_rows)]
    out_shape = [
        jax.ShapeDtypeStruct((q_rows, pairs * LANES), BF),
        jax.ShapeDtypeStruct((k_rows, pairs * LANES), BF),
        jax.ShapeDtypeStruct((k_rows, pairs * LANES), BF),
    ]
    if prefix:
        out_specs += [column_spec(PRE_PAD, 0, 0, group)] * 2
        out_shape += [jax.ShapeDtypeStruct((PRE_PAD, pairs * LANES), F32)] * 2
    return pl.pallas_call(
        functools.partial(
            attend_back_kernel, group=group, segs=segs, prefix=prefix, pieces=len(keys)
        ),
        grid=(pairs // group,),
        in_specs=specs,
        out_specs=out_specs,
        out_shape=out_shape,
        compiler_params=params(),
        name="attend_back",
    )(*args)


class Weights:
    def __init__(self, sources, targets, sems):
        self.sources, self.targets, self.sems = sources, targets, sems

    def copy(self, name, part=None):
        source, target = self.sources[name], self.targets[name]
        first = list(self.sources).index(name)
        sem = self.sems.at[first, 0 if part is None else part]
        if part is not None:
            cut = pl.ds(pl.multiple_of(part * wide, wide), wide)
            index = (slice(None), cut) if name == "in" else (cut, slice(None))
            source, target = source.at[index], target.at[index]
        return pltpu.make_async_copy(source, target, sem)

    def wait(self, name, part=None):
        self.copy(name, part).wait()

    def part(self, name, part):
        cut = pl.ds(pl.multiple_of(part * wide, wide), wide)
        index = (slice(None), cut) if name == "in" else (cut, slice(None))
        return self.targets[name].at[index]


def weight_scratch(arrays, parts):
    return [pltpu.VMEM(a.shape, BF) for a in arrays] + [
        pltpu.SemaphoreType.DMA((len(arrays), parts))
    ]


def ffn_step(low_ref, acc_ref, in_ref, out_ref, slope_ref, act_ref, bias_ref, scale):
    for start, size in row_tiles(low_ref.shape[0]):
        rows = slice(start, start + size)
        hidden = nn(low_ref[rows], in_ref[...])
        if bias_ref is not None:
            hidden = hidden + bias_ref[...]
        active, slope = gelu_pair(hidden)
        slope_ref[rows] = slope.astype(BF)
        active = active.astype(BF)
        if act_ref is not None:
            act_ref[rows] = active
        term = nn(active, out_ref[...])
        acc_ref[rows] += term if scale is None else scale * term


def enc_ffn_kernel(
    x_ref, att_ref, gain_ref, downb_ref, upb_ref, wo_hbm, in_hbm, out_hbm, down_hbm, up_hbm,
    mem_ref, slope_ref, pre_slope_ref, act_ref, low_ref, scales_ref,
    acc_ref, wo_ref, in_ref, out_ref, down_ref, up_ref, sems,
):
    weights = Weights(
        {"wo": wo_hbm, "in": in_hbm, "out": out_hbm, "down": down_hbm, "up": up_hbm},
        {"wo": wo_ref, "in": in_ref, "out": out_ref, "down": down_ref, "up": up_ref},
        sems,
    )

    weights.copy("wo").start()
    for part in range(in_ref.shape[1] // wide):
        weights.copy("in", part).start()
        weights.copy("out", part).start()
    weights.copy("down").start()
    weights.copy("up").start()
    weights.wait("wo")
    for start, size in row_tiles(x_ref.shape[0]):
        rows = slice(start, start + size)
        first = x_ref[rows].astype(F32) + nn(att_ref[rows], wo_ref[...])
        hat, scale = norm_rows(first)
        normed = hat * gain_ref[0:1]
        acc_ref[rows] = normed
        low_ref[rows] = normed.astype(BF)
        scales_ref[rows, 0:1] = scale

    def one_part(part, carry):
        weights.wait("in", part)
        weights.wait("out", part)
        cols = pl.ds(pl.multiple_of(part * wide, wide), wide)
        ffn_step(
            low_ref, acc_ref, in_ref.at[:, cols], out_ref.at[cols], slope_ref.at[:, cols],
            None, None, None,
        )
        return carry

    lax.fori_loop(0, in_ref.shape[1] // wide, one_part, 0)

    weights.wait("down")
    weights.wait("up")
    ffn_step(low_ref, acc_ref, down_ref, up_ref, pre_slope_ref, act_ref, downb_ref, adapter_scale)
    for start, size in row_tiles(x_ref.shape[0]):
        rows = slice(start, start + size)
        hat, scale = norm_rows(acc_ref[rows] + adapter_scale * upb_ref[...])
        mem_ref[rows] = (hat * gain_ref[1:2]).astype(BF)
        scales_ref[rows, 1:2] = scale


def enc_ffn(x, att, w):
    rows, width = x.shape
    hidden = w["ffn_in"].shape[1]
    steps = hidden // wide
    weights = [w["out"], w["ffn_in"], w["ffn_out"], w["down"], w["up"]]
    return pl.pallas_call(
        enc_ffn_kernel,
        grid=(1,),
        in_specs=[
            single((rows, width)),
            single((rows, width)),
            single((2, width)),
            single((1, chunk)),
            single((1, width)),
        ]
        + [pl.BlockSpec(memory_space=pl.ANY)] * len(weights),
        out_specs=[
            single((rows, width)),
            single((rows, hidden)),
            single((rows, chunk)),
            single((rows, chunk)),
            single((rows, width)),
            single((rows, LANES)),
        ],
        out_shape=[
            jax.ShapeDtypeStruct((rows, width), BF),
            jax.ShapeDtypeStruct((rows, hidden), BF),
            jax.ShapeDtypeStruct((rows, chunk), BF),
            jax.ShapeDtypeStruct((rows, chunk), BF),
            jax.ShapeDtypeStruct((rows, width), BF),
            jax.ShapeDtypeStruct((rows, LANES), F32),
        ],
        scratch_shapes=[pltpu.VMEM((rows, width), F32)] + weight_scratch(weights, steps),
        compiler_params=params(),
        name="enc_ffn",
    )(x, att, w["gains"], w["down_bias"], w["up_bias"], *weights)


def ffn_back_step(grad_ref, acc_ref, in_ref, out_ref, slope_ref):
    for start, size in row_tiles(grad_ref.shape[0]):
        rows = slice(start, start + size)
        pre = (nt(grad_ref[rows], out_ref[...]) * slope_ref[rows].astype(F32)).astype(BF)
        acc_ref[rows] += nt(pre, in_ref[...])


def adapter_back(grad_ref, acc_ref, low_ref, act_ref, slope_ref, down_ref, up_ref, outs, pre_ref):
    ddown_ref, ddownb_ref, dup_ref, dupb_ref = outs
    total = None
    for start, size in row_tiles(grad_ref.shape[0]):
        rows = slice(start, start + size)
        back = adapter_scale * nt(grad_ref[rows], up_ref[...])
        pre = (back * slope_ref[rows].astype(F32)).astype(BF)
        pre_ref[rows] = pre
        sums = jnp.sum(pre.astype(F32), axis=0, keepdims=True)
        total = sums if total is None else total + sums
        acc_ref[rows] += nt(pre, down_ref[...])
    ddownb_ref[...] = total
    ddown_ref[...] = tn(low_ref[...], pre_ref[...])
    dup_ref[...] = adapter_scale * tn(act_ref[...], grad_ref[...])
    dupb_ref[...] = adapter_scale * jnp.sum(grad_ref[...].astype(F32), axis=0, keepdims=True)


def enc_ffn_back_kernel(*refs, pieces):
    enc_ffn_back_body(refs[:pieces], *refs[pieces:])


def enc_ffn_back_body(
    dmem_refs, mem_ref, low_ref, scales_ref, gain_ref, slope_ref, pre_slope_ref,
    up_hbm, down_hbm, in_hbm, out_hbm, wo_hbm,
    dfirst_ref, datt_ref, grad_ref, pre_ref,
    acc_ref, up_ref, down_ref, in_ref, out_ref, wo_ref, sems,
):
    weights = Weights(
        {"up": up_hbm, "down": down_hbm, "in": in_hbm, "out": out_hbm, "wo": wo_hbm},
        {"up": up_ref, "down": down_ref, "in": in_ref, "out": out_ref, "wo": wo_ref},
        sems,
    )

    weights.copy("up").start()
    weights.copy("down").start()
    for part in range(in_ref.shape[1] // wide):
        weights.copy("out", part).start()
        weights.copy("in", part).start()
    weights.copy("wo").start()
    weights.wait("up")
    weights.wait("down")
    for start, size in row_tiles(mem_ref.shape[0]):
        rows = slice(start, start + size)
        gain = gain_ref[1:2]
        hat = mem_ref[rows].astype(F32) / gain
        dmem = stacked(dmem_refs, None, start, size).astype(F32)
        grad = norm_rows_back(hat, scales_ref[rows, 1:2], dmem * gain)
        low = grad.astype(BF)
        grad_ref[rows] = low
        back = adapter_scale * nt(low, up_ref[...])
        pre = (back * pre_slope_ref[rows].astype(F32)).astype(BF)
        pre_ref[rows] = pre
        acc_ref[rows] = grad + nt(pre, down_ref[...])

    def one_part(part, carry):
        weights.wait("out", part)
        weights.wait("in", part)
        cols = pl.ds(pl.multiple_of(part * wide, wide), wide)
        ffn_back_step(
            grad_ref, acc_ref, in_ref.at[:, cols], out_ref.at[cols], slope_ref.at[:, cols]
        )
        return carry

    lax.fori_loop(0, in_ref.shape[1] // wide, one_part, 0)

    weights.wait("wo")
    for start, size in row_tiles(mem_ref.shape[0]):
        rows = slice(start, start + size)
        gain = gain_ref[0:1]
        hat = low_ref[rows].astype(F32) / gain
        grad = norm_rows_back(hat, scales_ref[rows, 0:1], acc_ref[rows] * gain)
        dfirst_ref[rows] = grad
        datt_ref[rows] = nt(grad.astype(BF), wo_ref[...]).astype(BF)


def enc_ffn_back(dmems, saved, w):
    mem, slope, pre_slope, act, low, scales = saved
    rows, width = mem.shape
    hidden = w["ffn_in"].shape[1]
    steps = hidden // wide
    weights = [w["up"], w["down"], w["ffn_in"], w["ffn_out"], w["out"]]
    return pl.pallas_call(
        functools.partial(enc_ffn_back_kernel, pieces=len(dmems)),
        grid=(1,),
        in_specs=[single(d.shape) for d in dmems]
        + [
            single((rows, width)),
            single((rows, width)),
            single((rows, LANES)),
            single((2, width)),
            single((rows, hidden)),
            single((rows, chunk)),
        ]
        + [pl.BlockSpec(memory_space=pl.ANY)] * len(weights),
        out_specs=[
            single((rows, width)),
            single((rows, width)),
            single((rows, width)),
            single((rows, chunk)),
        ],
        out_shape=[
            jax.ShapeDtypeStruct((rows, width), F32),
            jax.ShapeDtypeStruct((rows, width), BF),
            jax.ShapeDtypeStruct((rows, width), BF),
            jax.ShapeDtypeStruct((rows, chunk), BF),
        ],
        scratch_shapes=[pltpu.VMEM((rows, width), F32)] + weight_scratch(weights, steps),
        compiler_params=params(),
        name="enc_ffn_back",
    )(*dmems, mem, low, scales, w["gains"], slope, pre_slope, *weights)


def dec_mid_kernel(x_ref, att_ref, wo_ref, gain_ref, wq_ref, n_ref, scale_ref, cq_ref):
    for start, size in row_tiles(x_ref.shape[0], 256):
        rows = slice(start, start + size)
        first = x_ref[rows].astype(F32) + nn(att_ref[rows], wo_ref[...])
        hat, scale = norm_rows(first)
        normed = hat * gain_ref[0:1]
        n_ref[rows] = normed
        scale_ref[rows, 0:1] = scale
        cq_ref[rows] = nn(normed.astype(BF), wq_ref[...]).astype(BF)


def dec_mid(x, att, w, cross):
    rows, width = x.shape
    return pl.pallas_call(
        dec_mid_kernel,
        out_shape=[
            jax.ShapeDtypeStruct((rows, width), F32),
            jax.ShapeDtypeStruct((rows, LANES), F32),
            jax.ShapeDtypeStruct((rows, width), BF),
        ],
        compiler_params=params(),
        name="dec_mid",
    )(x, att, w["out"], w["gains"], cross["query"])


def dec_ffn_kernel(
    len_ref, n_ref, catt_ref, cot_ref, cgain_ref, gain_ref, downb_ref, upb_ref,
    wco_hbm, in_hbm, out_hbm, down_hbm, up_hbm,
    y_ref, dsecond_ref, dcatt_ref, ddown_ref, ddownb_ref, dup_ref, dupb_ref,
    acc_ref, low_ref, grad_ref, slope_ref, pre_slope_ref, act_ref, pre_ref, scale_ref,
    wco_ref, in_ref, out_ref, down_ref, up_ref, sems,
    *, steps, which,
):
    weights = Weights(
        {"wco": wco_hbm, "in": in_hbm, "out": out_hbm, "down": down_hbm, "up": up_hbm},
        {"wco": wco_ref, "in": in_ref, "out": out_ref, "down": down_ref, "up": up_ref},
        sems,
    )

    weights.copy("wco").start()
    for part in range(steps):
        weights.copy("in", part).start()
        weights.copy("out", part).start()
    weights.copy("down").start()
    weights.copy("up").start()
    weights.wait("wco")
    second = n_ref[...] + nn(catt_ref[...], wco_ref[...])
    hat, scale = norm_rows(second)
    middle = hat * cgain_ref[...]
    acc_ref[...] = middle
    low_ref[...] = middle.astype(BF)
    scale_ref[:, 0:1] = scale

    def forward(part, carry):
        weights.wait("in", part)
        weights.wait("out", part)
        ffn_step(
            low_ref, acc_ref, weights.part("in", part), weights.part("out", part),
            slope_ref.at[part], None, None, None,
        )
        return carry

    lax.fori_loop(0, steps, forward, 0)

    weights.wait("down")
    weights.wait("up")
    ffn_step(
        low_ref, acc_ref, down_ref, up_ref, pre_slope_ref, act_ref, downb_ref, adapter_scale
    )
    gain = gain_ref[1:2]
    hat, scale = norm_rows(acc_ref[...] + adapter_scale * upb_ref[...])
    row = lax.broadcasted_iota(jnp.int32, (low_ref.shape[0], 1), 0)
    valid = row < len_ref[0, which]
    y_ref[...] = jnp.where(valid, hat * gain, 0.0).astype(BF)
    cot = jnp.where(valid, cot_ref[...].astype(F32), 0.0)
    grad = norm_rows_back(hat, scale, cot * gain)
    acc_ref[...] = grad
    grad_ref[...] = grad.astype(BF)
    adapter_back(
        grad_ref, acc_ref, low_ref, act_ref, pre_slope_ref, down_ref, up_ref,
        (ddown_ref, ddownb_ref, dup_ref, dupb_ref), pre_ref,
    )

    def backward(part, carry):
        ffn_back_step(
            grad_ref, acc_ref, weights.part("in", part), weights.part("out", part),
            slope_ref.at[part],
        )
        return carry

    lax.fori_loop(0, steps, backward, 0)

    gain = cgain_ref[...]
    hat = low_ref[...].astype(F32) / gain
    grad = norm_rows_back(hat, scale_ref[:, 0:1], acc_ref[...] * gain)
    dsecond_ref[...] = grad
    dcatt_ref[...] = nt(grad.astype(BF), wco_ref[...]).astype(BF)


def dec_ffn(lengths, n, catt, cot, w, cross, which):
    rows, width = catt.shape
    hidden = w["ffn_in"].shape[1]
    steps = hidden // wide
    weights = [cross["out"], w["ffn_in"], w["ffn_out"], w["down"], w["up"]]
    return pl.pallas_call(
        functools.partial(dec_ffn_kernel, steps=steps, which=which),
        grid=(1,),
        in_specs=[
            pl.BlockSpec(memory_space=pltpu.SMEM),
            pl.BlockSpec((rows, width), lambda i: (which, 0)),
            whole((rows, width)),
            pl.BlockSpec((rows, width), lambda i: (which, 0)),
            whole((1, width)),
            whole((2, width)),
            whole((1, chunk)),
            whole((1, width)),
        ]
        + [pl.BlockSpec(memory_space=pl.ANY)] * len(weights),
        out_specs=[
            whole((rows, width)),
            whole((rows, width)),
            whole((rows, width)),
            whole((width, chunk)),
            whole((1, chunk)),
            whole((chunk, width)),
            whole((1, width)),
        ],
        out_shape=[
            jax.ShapeDtypeStruct((rows, width), BF),
            jax.ShapeDtypeStruct((rows, width), F32),
            jax.ShapeDtypeStruct((rows, width), BF),
            jax.ShapeDtypeStruct((width, chunk), F32),
            jax.ShapeDtypeStruct((1, chunk), F32),
            jax.ShapeDtypeStruct((chunk, width), F32),
            jax.ShapeDtypeStruct((1, width), F32),
        ],
        scratch_shapes=[
            pltpu.VMEM((rows, width), F32),
            pltpu.VMEM((rows, width), BF),
            pltpu.VMEM((rows, width), BF),
            pltpu.VMEM((steps, rows, wide), BF),
            pltpu.VMEM((rows, chunk), BF),
            pltpu.VMEM((rows, chunk), BF),
            pltpu.VMEM((rows, chunk), BF),
            pltpu.VMEM((rows, LANES), F32),
        ]
        + weight_scratch(weights, steps),
        compiler_params=params(),
        name="dec_ffn",
    )(
        lengths, n, catt, cot, cross["gain"], w["gains"], w["down_bias"], w["up_bias"], *weights
    )


def dec_mid_back_kernel(
    dsecond0_ref, dsecond1_ref, dcq0_ref, dcq1_ref, wq_ref, n_ref, scale_ref, gain_ref, wo_ref,
    dfirst_ref, datt_ref,
):
    for pair, (dsecond_ref, dcq_ref) in enumerate(
        ((dsecond0_ref, dcq0_ref), (dsecond1_ref, dcq1_ref))
    ):
        rows = slice(pair * TGT, (pair + 1) * TGT)
        gain = gain_ref[0:1]
        total = dsecond_ref[...] + nt(dcq_ref[...], wq_ref[...])
        grad = norm_rows_back(n_ref[rows] / gain, scale_ref[rows, 0:1], total * gain)
        dfirst_ref[rows] = grad
        datt_ref[rows] = nt(grad.astype(BF), wo_ref[...]).astype(BF)


def dec_mid_back(dseconds, dcqs, n, scale, w, cross):
    rows, width = n.shape
    return pl.pallas_call(
        dec_mid_back_kernel,
        out_shape=[
            jax.ShapeDtypeStruct((rows, width), F32),
            jax.ShapeDtypeStruct((rows, width), BF),
        ],
        compiler_params=params(),
        name="dec_mid_back",
    )(*dseconds, *dcqs, cross["query"], n, scale, w["gains"], w["out"])


enc_segs = ((0, SRC_LONG, 0, SRC_LONG), (SRC_LONG, SRC_SHORT, SRC_LONG, SRC_SHORT))
dec_segs = ((0, TGT, 0, TGT), (TGT, TGT, TGT, TGT))
cross_segs = (((0, TGT, 0, SRC_LONG),), ((0, TGT, 0, SRC_SHORT),))


def self_columns(qkv):
    rows = qkv.shape[0]
    return (qkv, rows, 0, 0), [(qkv, rows, 0, 8)], [(qkv, rows, 0, 16)]


def cross_columns(cq, block, kv, which):
    keys = (SRC_LONG, SRC_SHORT)[which]
    return (cq, TGT, block, 0), [(kv, keys, 0, 0)], [(kv, keys, 0, 8)]


def decoder_self(t, lengths, w, cross):
    qkv = product(t, w["qkv"])
    att, inv, *weights = attend(lengths, *self_columns(qkv), w["prefix"], dec_segs, True, group=2)
    n, scale, cq = dec_mid(t, att, w, cross)
    return cq, (qkv, att, inv, weights, n, scale)


def cross_forward(lengths, cq, block, kv, which):
    return attend(
        lengths, *cross_columns(cq, block, kv, which), None, cross_segs[which], False, which, group=2
    )


def cross_backward(cq, block, kv, forward, dcatt, which):
    catt, inv, *weights = forward
    return attend_back(
        *cross_columns(cq, block, kv, which), None, catt, inv, dcatt, weights, cross_segs[which]
    )


def decoder_self_back(kept, dseconds, dcqs, w, cross):
    qkv, att, inv, weights, n, scale = kept
    dfirst, datt = dec_mid_back(dseconds, dcqs, n, scale, w, cross)
    dq, dk, dv, *dprefix = attend_back(
        *self_columns(qkv), w["prefix"], att, inv, datt, weights, dec_segs
    )
    return back_product([dq, dk, dv], w["qkv"], dfirst)[0], dprefix


def small_shape(devices):
    return 8, 8 * (2 * chunk) // devices


def finish_kernel(
    q_ref, k_ref, v_ref, o_ref, inv_ref, g0_ref, g1_ref, g2_ref, pk_ref, pv_ref, pl_ref, ps_ref,
    dfirst0_ref, dfirst1_ref, dfirst2_ref, wqkv_ref,
    low_all, act_all, grad_all, pre_all,
    long_down, long_downb, long_up, long_upb,
    short_down, short_downb, short_up, short_upb, dpk_ref, dpv_ref,
    y0_ref, y1_ref, dt_ref,
    source_ref, y_ref, target_ref, o_up_ref, o_down_ref, o_prefix_ref, o_upb_ref, o_downb_ref,
    dq, dk, dv, small, lows_all, acts_all, grads_all, pres_all, ups, downs, mine, theirs, half_sum, across_y, y_sum, landed, total, result,
    small_landed, small_total, small_result, dx, dx_landed, lows, lows_landed,
    load_sems, pair_sems, y_sems, z_sems, gather_sems, share_y_sems, back_sems,
    small_sems, share_sems, cross_sems,
    *, devices,
):
    step = pl.program_id(0)
    pairs = 8
    section = lax.axis_index("section")
    is_encoder = section == 0
    chips = devices // 2
    line = chips // 2
    slices = 16 // line
    rows = 2 * chunk
    half = rows // 2
    size = half // slices
    side = size // 2
    part = side // line
    place = lax.axis_index("dp")
    core, chip = lax.rem(place, 2), place // 2
    bit, at_line = lax.rem(chip, 2), chip // 2
    partner = place + 1 - 2 * core
    beside = place + 2 - 4 * bit
    small_rows, small_cols = small_shape(devices)
    tile = 256
    width = 2 * chunk
    scale = 1.0 / devices

    def aligned(value, unit=16):
        return pl.multiple_of(value, unit)

    def along(distance):
        return (lax.rem(at_line + distance, line) * 2 + bit) * 2 + core

    def remote(source, target, send_sem, recv_sem, other):
        return pltpu.make_async_remote_copy(
            src_ref=source, dst_ref=target, send_sem=send_sem, recv_sem=recv_sem,
            device_id=other, device_id_type=pl.DeviceIdType.MESH,
        )

    def in_group(other):
        return {"dp": other}

    across = {"section": 1 - section}
    kept = aligned(core * half)
    given = aligned((1 - core) * half)

    def swap():
        return remote(
            mine.at[pl.ds(given, half)], theirs, pair_sems.at[0], pair_sems.at[1],
            in_group(partner),
        )

    def y_send(j):
        there = pl.ds(aligned(j * size + (1 - bit) * side), side)
        return remote(
            half_sum.at[there], across_y.at[j], y_sems.at[0, j], y_sems.at[1, j], in_group(beside)
        )

    def z_send(j, s):
        there = pl.ds(aligned(lax.rem(at_line + s, line) * part), part)
        return remote(
            y_sum.at[j].at[there], landed.at[j, s - 1],
            z_sems.at[0, j, s - 1], z_sems.at[1, j, s - 1], in_group(along(s)),
        )

    def own_rows(j):
        return pl.ds(aligned(kept + j * size + bit * side + at_line * part), part)

    def own_side(j):
        return pl.ds(aligned(kept + j * size + bit * side), side)

    def other_side(j):
        return pl.ds(aligned(kept + j * size + (1 - bit) * side), side)

    def gather(j, s):
        return remote(
            total.at[j], result.at[own_rows(j)],
            gather_sems.at[0, j, s - 1], gather_sems.at[1, j, s - 1], in_group(along(s)),
        )

    def y_share(j):
        return remote(
            result.at[own_side(j)], result.at[own_side(j)],
            share_y_sems.at[0, j], share_y_sems.at[1, j], in_group(beside),
        )

    def back(j, i):
        there = own_side(j) if i == 0 else other_side(j)
        return remote(
            result.at[there], result.at[there],
            back_sems.at[0, j, i], back_sems.at[1, j, i], in_group(partner),
        )

    def piece(index):
        row = aligned(lax.rem(index, 8) * small_rows, 8)
        col = aligned((index // 8) * small_cols, LANES)
        return pl.ds(row, small_rows), pl.ds(col, small_cols)

    def small_out(s):
        return remote(
            small.at[piece(lax.rem(place + s, devices))], small_landed.at[s - 1],
            small_sems.at[0, s - 1], small_sems.at[1, s - 1],
            in_group(lax.rem(place + s, devices)),
        )

    def small_share(s):
        return remote(
            small_total, small_result.at[piece(place)],
            share_sems.at[0, s - 1], share_sems.at[1, s - 1],
            in_group(lax.rem(place + s, devices)),
        )

    def send_low():
        return remote(lows, lows_landed, cross_sems.at[0, 0], cross_sems.at[1, 0], across)

    def send_high(i):
        return remote(
            dx.at[i], dx_landed.at[i], cross_sems.at[0, 1 + i], cross_sems.at[1, 1 + i], across
        )

    def greet(barrier, other):
        pl.semaphore_signal(
            barrier, inc=1, device_id=other, device_id_type=pl.DeviceIdType.MESH
        )

    def load(source, target, i):
        return pltpu.make_async_copy(source, target, load_sems.at[i])

    enc_loads = [
        load(low_all, lows_all, 0), load(act_all, acts_all, 1),
        load(grad_all, grads_all, 2), load(pre_all, pres_all, 3),
    ]
    dec_loads = [
        load(long_up, ups.at[0], 0), load(long_down, downs.at[0], 1),
        load(short_up, ups.at[1], 2), load(short_down, downs.at[1], 3),
    ]

    @pl.when(step == 0)
    def _():
        barrier = pltpu.get_barrier_semaphore()
        for s in range(1, devices):
            greet(barrier, in_group(lax.rem(place + s, devices)))

        @pl.when(is_encoder)
        def _():
            for copy in enc_loads:
                copy.start()

        @pl.when(jnp.logical_not(is_encoder))
        def _():
            for copy in dec_loads:
                copy.start()

    @pl.when(is_encoder & (step < pairs))
    def _():
        at = aligned(step * LANES, LANES)
        lanes = pl.ds(at, LANES)
        prefix_totals = attend_back_pair(
            q_ref, [k_ref], [v_ref], o_ref, inv_ref, [g0_ref, g1_ref, g2_ref], pk_ref, pv_ref,
            (pl_ref, ps_ref), dq.at[:, lanes], dk.at[:, lanes], dv.at[:, lanes], enc_segs,
        )
        small[0:PRE_PAD, lanes] = prefix_totals[0] * scale
        small[PRE_PAD : 2 * PRE_PAD, lanes] = prefix_totals[1] * scale

    @pl.when(step == 0)
    def _():
        barrier = pltpu.get_barrier_semaphore()

        def pack(up, down):
            mine[0:chunk] = (up * scale).astype(BF)
            down = (down * scale).astype(BF)
            mine[chunk:width, 0:chunk] = down[0:chunk]
            mine[chunk:width, chunk:width] = down[chunk:width]

        @pl.when(is_encoder)
        def _():
            for copy in enc_loads:
                copy.wait()
            pack(
                adapter_scale * tn(acts_all[...], grads_all[...]),
                tn(lows_all[...], pres_all[...]),
            )
            pl.semaphore_wait(barrier, devices - 1)
            greet(barrier, across)

        @pl.when(jnp.logical_not(is_encoder))
        def _():
            for copy in dec_loads:
                copy.wait()
            pack(ups[0] + ups[1], downs[0] + downs[1])
            pl.semaphore_wait(barrier, devices)
            greet(barrier, across)

        swap().start()

        @pl.when(jnp.logical_not(is_encoder))
        def _():
            low = width // 2
            lows[0, 0:TGT] = y0_ref[:, 0:low]
            lows[0, TGT : 2 * TGT] = y1_ref[:, 0:low]
            lows[1] = dt_ref[:, 0:low]
            send_low().start()
            small[0:PRE_PAD] = dpk_ref[...] * scale
            small[PRE_PAD : 2 * PRE_PAD] = dpv_ref[...] * scale

    @pl.when(step == 1)
    def _():
        swap().wait()
        half_sum[...] = (
            mine[pl.ds(kept, half)].astype(F32) + theirs[...].astype(F32)
        ).astype(BF)
        for j in range(min(2, slices)):
            y_send(j).start()

    for j in range(slices):

        @pl.when(step == 2 + j)
        def _(j=j):
            y_send(j).wait()
            if j + 2 < slices:
                y_send(j + 2).start()
            own = pl.ds(aligned(j * size + bit * side), side)
            y_sum[j] = (half_sum[own].astype(F32) + across_y[j].astype(F32)).astype(BF)
            for s in range(1, line):
                z_send(j, s).start()

        @pl.when(step == 4 + j)
        def _(j=j):
            summed = y_sum[j, pl.ds(aligned(at_line * part), part)].astype(F32)
            for s in range(1, line):
                z_send(j, s).wait()
                summed = summed + landed[j, s - 1].astype(F32)
            total[j] = summed.astype(BF)
            result[own_rows(j)] = total[j]
            for s in range(1, line):
                gather(j, s).start()

        @pl.when(step == 6 + j)
        def _(j=j):
            for s in range(1, line):
                gather(j, s).wait()
            y_share(j).start()
            back(j, 0).start()

        @pl.when(step == 8 + j)
        def _(j=j):
            y_share(j).wait()
            back(j, 1).start()

    @pl.when(step == pairs - 1)
    def _():
        @pl.when(is_encoder)
        def _():
            up_row = jnp.sum(grads_all[...].astype(F32), axis=0, keepdims=True)
            down_row = jnp.sum(pres_all[...].astype(F32), axis=0, keepdims=True)
            down_row = jnp.concatenate([down_row, jnp.zeros_like(down_row)], 1)
            small[PRE : PRE + 1] = up_row * (adapter_scale * scale)
            small[PRE + 1 : PRE + 2] = down_row * scale

        @pl.when(jnp.logical_not(is_encoder))
        def _():
            down_row = long_downb[...] + short_downb[...]
            down_row = jnp.concatenate([down_row, jnp.zeros_like(down_row)], 1)
            small[PRE : PRE + 1] = (long_upb[...] + short_upb[...]) * scale
            small[PRE + 1 : PRE + 2] = down_row * scale

        for s in range(1, devices):
            small_out(s).start()

    @pl.when(is_encoder & (step == pairs))
    def _():
        pl.semaphore_wait(pltpu.get_barrier_semaphore(), 1)

    @pl.when(is_encoder & (step >= pairs))
    def _():
        acc = jnp.concatenate([dfirst0_ref[...], dfirst1_ref[...], dfirst2_ref[...]], 0)
        for n, grad in enumerate((dq, dk, dv)):
            acc = acc + nt(grad[...], wqkv_ref[:, n * width : (n + 1) * width])
        dx[step - pairs] = acc.astype(BF)

    for i in range(2):

        @pl.when(is_encoder & (step == pairs + i))
        def _(i=i):
            send_high(i).start()

    @pl.when(step == pairs + 1)
    def _():
        own_rows_, own_cols = piece(place)
        summed = small[own_rows_, own_cols]
        for s in range(1, devices):
            small_out(s).wait()
            summed = summed + small_landed[s - 1]
        small_total[...] = summed
        small_result[own_rows_, own_cols] = summed
        for s in range(1, devices):
            small_share(s).start()

    @pl.when(step == pairs + 3)
    def _():
        for j in range(slices):
            for i in range(2):
                back(j, i).wait()
        o_up_ref[...] = result[0:chunk]
        o_down_ref[0:chunk] = result[chunk:width, 0:chunk]
        o_down_ref[chunk:width] = result[chunk:width, chunk:width]
        for s in range(1, devices):
            small_share(s).wait()
        o_prefix_ref[0] = small_result[0:PRE]
        o_prefix_ref[1] = small_result[PRE_PAD : PRE_PAD + PRE]
        o_upb_ref[...] = small_result[PRE : PRE + 1]
        o_downb_ref[...] = small_result[PRE + 1 : PRE + 2, 0:chunk]

        @pl.when(is_encoder)
        def _():
            for i in range(2):
                source_ref[:, i * tile : (i + 1) * tile] = dx[2 + i]
            send_low().wait_recv()
            y_ref[...] = lows_landed[0]
            target_ref[...] = lows_landed[1]
            for i in range(2):
                send_high(i).wait_send()

        @pl.when(jnp.logical_not(is_encoder))
        def _():
            low = width // 2
            y_ref[0:TGT] = y0_ref[:, low:width]
            y_ref[TGT : 2 * TGT] = y1_ref[:, low:width]
            target_ref[...] = dt_ref[:, low:width]
            send_low().wait_send()
            for i in range(2):
                send_high(i).wait_recv()
                source_ref[:, i * tile : (i + 1) * tile] = dx_landed[i]


def finish(saved, datt, dfirst, w, traces, adapters, dec_prefix, ys, dt):
    qkv, att, inv, weights = saved
    devices = lax.axis_size("dp")
    line = devices // 4
    slices = 16 // line
    rows, width = att.shape
    targets = dt.shape[0]
    pairs, tile = 8, 256
    half = width // 2
    side = half // slices // 2
    part = side // line
    small_rows, small_cols = small_shape(devices)

    def mine(value):
        return jnp.where(lax.axis_index("section") == 0, value, 0)

    def head(i):
        return mine(jnp.minimum(i, pairs - 1))

    def pair(offset):
        return pl.BlockSpec((rows, LANES), lambda i: (0, head(i) + offset))

    def at(i):
        return mine(jnp.where(i < pairs + 2, 2 + jnp.maximum(i - pairs, 0), i - pairs - 2))

    def once(shape):
        return pl.BlockSpec(shape, lambda i: (0,) * len(shape), pipeline_mode=pl.Buffered(1))

    anywhere = pl.BlockSpec(memory_space=pl.ANY)
    prefix_pair = pl.BlockSpec((PRE_PAD, LANES), lambda i: (0, head(i)))
    vmem = pltpu.VMEM
    dma = pltpu.SemaphoreType.DMA
    flat = [*traces] + [a for group in adapters for a in group]
    return pl.pallas_call(
        functools.partial(finish_kernel, devices=devices),
        grid=(pairs + 4,),
        in_specs=[pair(0), pair(8), pair(16), pair(0), pair(0)]
        + [pl.BlockSpec((ENC_ROWS, LANES), lambda i, n=n: (n, head(i))) for n in range(3)]
        + [prefix_pair] * 2
        + [
            pl.BlockSpec((2,) + p.shape[1:], lambda i: (head(i), 0, 0))
            for p in weights
        ]
        + [pl.BlockSpec((ENC_ROWS, tile), lambda i, n=n: (n, at(i))) for n in range(3)]
        + [
            pl.BlockSpec((tile, 3 * width), lambda i: (at(i), 0)),
        ]
        + [anywhere if a.shape[0] > 1 else once(a.shape) for a in flat]
        + [once(a.shape) for a in (*dec_prefix, *ys, dt)],
        out_specs=[
            once((rows, half)), once((targets, half)), once((targets, half)),
            once((chunk, width)), once((width, chunk)),
            once((2, PRE, width)), once((1, width)), once((1, chunk)),
        ],
        out_shape=[
            jax.ShapeDtypeStruct((rows, half), BF),
            jax.ShapeDtypeStruct((targets, half), BF),
            jax.ShapeDtypeStruct((targets, half), BF),
            jax.ShapeDtypeStruct((chunk, width), BF),
            jax.ShapeDtypeStruct((width, chunk), BF),
            jax.ShapeDtypeStruct((2, PRE, width), F32),
            jax.ShapeDtypeStruct((1, width), F32),
            jax.ShapeDtypeStruct((1, chunk), F32),
        ],
        scratch_shapes=[
            vmem((rows, width), BF), vmem((rows, width), BF), vmem((rows, width), BF),
            vmem((2 * PRE_PAD, width), F32),
            vmem((rows, width), BF), vmem((rows, chunk), BF),
            vmem((rows, width), BF), vmem((rows, chunk), BF),
            vmem((2, chunk, width), F32), vmem((2, width, chunk), F32),
            vmem((width, width), BF), vmem((half, width), BF), vmem((half, width), BF),
            vmem((slices, side, width), BF), vmem((slices, side, width), BF),
            vmem((slices, line - 1, part, width), BF), vmem((slices, part, width), BF),
            vmem((width, width), BF),
            vmem((devices - 1, small_rows, small_cols), F32), vmem((small_rows, small_cols), F32),
            vmem((2 * PRE_PAD, width), F32),
            vmem((4, rows, tile), BF), vmem((2, rows, tile), BF),
            vmem((2, targets, half), BF), vmem((2, targets, half), BF),
            dma((4,)), dma((2,)), dma((2, slices)), dma((2, slices, line - 1)),
            dma((2, slices, line - 1)), dma((2, slices)), dma((2, slices, 2)),
            dma((2, devices - 1)), dma((2, devices - 1)), dma((2, 3)),
        ],
        compiler_params=pltpu.CompilerParams(
            vmem_limit_bytes=60 * 2**20, collective_id=0, has_side_effects=True
        ),
        name="finish",
    )(
        qkv, qkv, qkv, att, inv, datt, datt, datt, *w["prefix"], *weights,
        dfirst, dfirst, dfirst, w["qkv"], *flat, *dec_prefix, *ys, dt,
    )


def blank_kernel(*refs):
    pass


def blanks(shapes):
    return pl.pallas_call(
        blank_kernel,
        out_shape=list(shapes),
        out_specs=[pl.BlockSpec(memory_space=pl.ANY)] * len(shapes),
        name="blank",
    )()


def on_section(is_encoder, encoder_work, decoder_work, *operands):
    enc_shapes, _ = jax.eval_shape(encoder_work, *operands)
    dec_shapes, _ = jax.eval_shape(decoder_work, *operands)

    def blank_like(shapes):
        leaves, tree = jax.tree.flatten(shapes)
        if not leaves:
            return shapes
        return jax.tree.unflatten(tree, blanks(leaves))

    def encoder_branch(*a):
        own, shared = encoder_work(*a)
        return own, blank_like(dec_shapes), shared

    def decoder_branch(*a):
        own, shared = decoder_work(*a)
        return blank_like(enc_shapes), own, shared

    return lax.cond(is_encoder, encoder_branch, decoder_branch, *operands)


def to_decoder(block):
    return lax.ppermute(block, "section", [(0, 1)])


def to_encoder(block):
    return lax.ppermute(block, "section", [(1, 0)])


def per_device(
    sources, targets, cotangent, source_lengths, target_lengths,
    attn_qkv, attn_out, ffn_in, ffn_out, norm_gains, prefix_pairs,
    adapt_down, adapt_down_bias, adapt_up, adapt_up_bias,
    cross_query, cross_pairs, cross_out, cross_gain,
):
    is_encoder = lax.axis_index("section") == 0
    prefix = jnp.pad(prefix_pairs[0], ((0, 0), (0, PRE_PAD - PRE), (0, 0)))
    w = dict(
        qkv=attn_qkv[0], out=attn_out[0], ffn_in=ffn_in[0], ffn_out=ffn_out[0],
        gains=norm_gains[0], prefix=(prefix[0], prefix[1]),
        down=adapt_down[0], down_bias=adapt_down_bias,
        up=adapt_up[0], up_bias=adapt_up_bias,
    )
    cross = dict(query=cross_query, pairs=cross_pairs, out=cross_out, gain=cross_gain[None])

    def at_encoder(work, *operands):
        return on_section(is_encoder, lambda *a: (work(*a), ()), lambda *a: ((), ()), *operands)[0]

    def at_decoder(work, *operands):
        return on_section(is_encoder, lambda *a: ((), ()), lambda *a: (work(*a), ()), *operands)[1]

    def at_both(enc_work, dec_work, *operands):
        return on_section(
            is_encoder, lambda *a: (enc_work(*a), ()), lambda *a: (dec_work(*a), ()), *operands
        )[:2]

    def tie(*arrays):
        return lax.optimization_barrier(arrays)

    def encoder_self():
        qkv = product(sources, w["qkv"])
        att, inv, *weights = attend(
            source_lengths, *self_columns(qkv), w["prefix"], enc_segs, False, checked=True
        )
        return qkv, att, inv, weights

    saved, (cq, kept) = at_both(
        encoder_self, lambda: decoder_self(targets, target_lengths, w, cross)
    )
    long_queries = to_encoder(cq[:TGT])
    part = at_encoder(lambda saved: enc_ffn(sources, saved[1], w), saved)
    mem_short = to_decoder(part[0][SRC_LONG:])

    def encoder_cross(mem, long_queries):
        kv = product(mem, cross["pairs"])
        return kv, cross_forward(source_lengths, long_queries, 0, kv, 0)

    long_kv, long = at_encoder(encoder_cross, part[0], long_queries)
    mem_short, catt = tie(mem_short, long[0])
    catt_here = to_decoder(catt)

    def decoder_short(mem_short, cq, kept):
        kv = product(mem_short, cross["pairs"])
        forward = cross_forward(source_lengths, cq, 1, kv, 1)
        return kv, forward, dec_ffn(
            target_lengths, kept[4], forward[0], cotangent, w, cross, 1
        )

    short_kv, short, short_ffn = at_decoder(decoder_short, mem_short, cq, kept)
    short_y, short_second, short_dcatt, *short_adapter = short_ffn
    catt_here, short_y = tie(catt_here, short_y)
    long_y, long_second, long_dcatt, *long_adapter = at_decoder(
        lambda catt, kept: dec_ffn(target_lengths, kept[4], catt, cotangent, w, cross, 0),
        catt_here, kept,
    )
    short_dcatt, long_dcatt = tie(short_dcatt, long_dcatt)
    dcatt_here = to_encoder(long_dcatt)

    def decoder_short_back(kv, cq, short, dcatt):
        dcq, dck, dcv = cross_backward(cq, 1, kv, short, dcatt, 1)
        return back_product([dck, dcv], cross["pairs"])[0], dcq

    dmem_short, short_cq = at_decoder(decoder_short_back, short_kv, cq, short, short_dcatt)
    dcatt_here, dmem_short = tie(dcatt_here, to_encoder(dmem_short))
    long_dcq, dck, dcv = at_encoder(
        lambda queries, kv, long, dcatt: cross_backward(queries, 0, kv, long, dcatt, 0),
        long_queries, long_kv, long, dcatt_here,
    )
    long_cq = to_decoder(long_dcq)

    def encoder_back(dck, dcv, dmem_short, part):
        dmem = back_product([dck, dcv], cross["pairs"])[0]
        return enc_ffn_back([dmem, dmem_short], part, w)

    dfirst, datt, grad, pre = at_encoder(encoder_back, dck, dcv, dmem_short, part)

    def decoder_end(kept, *grads):
        return decoder_self_back(kept, grads[:2], grads[2:], w, cross)

    long_cq, datt = tie(long_cq, datt)
    dt, dec_prefix = at_decoder(
        decoder_end, kept, long_second, short_second, long_cq, short_cq
    )
    source_grad, y, target_grad, up, down, prefix_grad, up_bias, down_bias = finish(
        saved, datt, dfirst, w, [part[4], part[3], grad, pre],
        [long_adapter, short_adapter], dec_prefix, [long_y, short_y], dt,
    )
    return (
        y,
        source_grad,
        target_grad,
        prefix_grad[None],
        down.astype(F32)[None],
        down_bias,
        up.astype(F32)[None],
        up_bias,
    )


def solution(mesh):
    layer2, layer3, rows = P("section", None), P("section", None, None), P("dp", None)
    return jax.shard_map(
        per_device,
        mesh=mesh,
        in_specs=(
            rows, rows, rows, rows, rows,
            layer3, layer3, layer3, layer3, layer3,
            P("section", None, None, None),
            layer3, layer2, layer3, layer2,
            P(), P(), P(), P(),
        ),
        out_specs=(
            P("dp", "section"), P("dp", "section"), P("dp", "section"),
            P("section", None, None, None), layer3, layer2, layer3, layer2,
        ),
        check_vma=False,
    )
```

```python
import functools

import jax
import jax.numpy as jnp
from jax import lax
from jax.experimental import pallas as pl
from jax.experimental.pallas import tpu as pltpu
from jax.sharding import PartitionSpec as P

HD = 64
PRE = 30
PRE_PAD = 32
SRC_LONG = 768
SRC_SHORT = 96
TGT = 256
LANES = 128

BF = jnp.bfloat16
F32 = jnp.float32
norm_eps = 1e-05
big_negative = -1e30
adapter_scale = 4.0
chunk = 512
wide = 1024
ENC_ROWS = (SRC_LONG + SRC_SHORT) // 3
vmem_bytes = 56 * 2**20

phi_poly = (
    0.797869713181688,
    0.036392283539041996,
    -8.782472977701046e-05,
    -3.669384069669515e-05,
    1.4250308145882202e-06,
)


def nn(left, right):
    return lax.dot_general(left, right, (((1,), (0,)), ((), ())), preferred_element_type=F32)


def nt(left, right):
    return lax.dot_general(left, right, (((1,), (1,)), ((), ())), preferred_element_type=F32)


def tn(left, right):
    return lax.dot_general(left, right, (((0,), (0,)), ((), ())), preferred_element_type=F32)


def gelu_pair(values):
    square = values * values
    poly = phi_poly[4]
    for coefficient in phi_poly[3::-1]:
        poly = poly * square + coefficient
    half = 0.5 * jnp.tanh(values * poly) + 0.5
    density = jnp.exp(square * -0.5) * 0.3989422804014327
    return values * half, half + values * density


def row_tiles(rows, most=864):
    count = -(-rows // most)
    size = rows // count
    return [(i * size, size) for i in range(count)]


def norm_rows(values):
    centered = values - jnp.mean(values, axis=-1, keepdims=True)
    scale = lax.rsqrt(jnp.mean(centered * centered, axis=-1, keepdims=True) + norm_eps)
    return centered * scale, scale


def norm_rows_back(hat, scale, grad_hat):
    mean_grad = jnp.mean(grad_hat, axis=-1, keepdims=True)
    mean_dot = jnp.mean(grad_hat * hat, axis=-1, keepdims=True)
    return scale * (grad_hat - mean_grad - hat * mean_dot)


def params(limit=vmem_bytes):
    return pltpu.CompilerParams(vmem_limit_bytes=limit)


def whole(shape):
    return pl.BlockSpec(shape, lambda *g: (0,) * len(shape))


def single(shape):
    return pl.BlockSpec(shape, lambda *g: (0,) * len(shape), pipeline_mode=pl.Buffered(1))


def product_kernel(x_ref, w_ref, o_ref):
    o_ref[...] = nn(x_ref[...], w_ref[...]).astype(BF)


def product(x, w, tile=1024, rows=None):
    depth = x.shape[1]
    rows = rows or x.shape[0]
    width = w.shape[1]
    return pl.pallas_call(
        product_kernel,
        grid=(width // tile,),
        in_specs=[whole((rows, depth)), pl.BlockSpec((depth, tile), lambda i: (0, i))],
        out_specs=pl.BlockSpec((rows, tile), lambda i: (0, i)),
        out_shape=jax.ShapeDtypeStruct((rows, width), BF),
        compiler_params=params(),
        name="product",
    )(x, w)


def back_product_kernel(*refs, parts, residual, cuts):
    grads = refs[:parts]
    w_ref = refs[parts]
    outs = refs[-len(cuts) :]
    total = None
    width = grads[0].shape[1]
    for i, grad in enumerate(grads):
        term = nt(grad[...], w_ref[:, i * width : (i + 1) * width])
        total = term if total is None else total + term
    if residual:
        total = total + refs[parts + 1][...]
    for (start, size), o_ref in zip(cuts, outs):
        o_ref[...] = total[start : start + size].astype(BF)


def back_product(grads, w, residual=None, tile=512, cuts=None):
    rows, width = grads[0].shape
    depth = w.shape[0]
    parts = len(grads)
    cuts = cuts or ((0, rows),)
    specs = [whole((rows, width))] * parts + [
        pl.BlockSpec((tile, parts * width), lambda i: (i, 0))
    ]
    args = list(grads) + [w]
    if residual is not None:
        specs.append(pl.BlockSpec((rows, tile), lambda i: (0, i)))
        args.append(residual)
    return pl.pallas_call(
        functools.partial(
            back_product_kernel, parts=parts, residual=residual is not None, cuts=cuts
        ),
        grid=(depth // tile,),
        in_specs=specs,
        out_specs=[pl.BlockSpec((size, tile), lambda i: (0, i)) for _, size in cuts],
        out_shape=[jax.ShapeDtypeStruct((size, depth), BF) for _, size in cuts],
        compiler_params=params(),
        name="back_product",
    )(*args)


def head_lanes(head):
    lane = lax.broadcasted_iota(jnp.int32, (1, LANES), 1)
    own = (lane < HD) if head == 0 else (lane >= HD)
    first = HD if head == 0 else 0
    return own, lane == first, lane == first + 1


def bf(value):
    return jnp.asarray(value, BF)


def rows_of(refs, start, count):
    parts = []
    for ref in refs:
        size = ref.shape[0]
        low, high = max(start, 0), min(start + count, size)
        if low < high:
            parts.append(ref[low:high])
        start -= size
    return parts


def stacked(refs, prefix_ref, start, count):
    parts = rows_of(refs, start, count)
    if prefix_ref is not None:
        parts.append(prefix_ref[...])
    return parts[0] if len(parts) == 1 else jnp.concatenate(parts, 0)


def attend_pair(*refs, segs, prefix, causal, pieces, which, checked):
    len_ref, q_ref = refs[:2]
    k_refs, v_refs = refs[2 : 2 + pieces], refs[2 + pieces : 2 + 2 * pieces]
    at = 2 + 2 * pieces
    pk_ref = pv_ref = None
    if prefix:
        pk_ref, pv_ref = refs[at : at + 2]
        at += 2
    o_ref, inv_ref = refs[at : at + 2]
    p_refs = refs[at + 2 :]

    def work(peaked):
        for seg, (q0, nq, k0, nk) in enumerate(segs):
            keys = stacked(k_refs, pk_ref, k0, nk)
            values = stacked(v_refs, pv_ref, k0, nk)
            count = keys.shape[0]
            row = lax.broadcasted_iota(jnp.int32, (count, 1), 0)
            seen = row < jnp.minimum(len_ref[0, which + seg], nk)
            if prefix:
                seen = seen | ((row >= nk) & (row < nk + PRE))
            queries = q_ref[q0 : q0 + nq] * bf(HD**-0.5)
            out = inv = None
            across = nq >= 4 * LANES
            outs, invs = [], []
            if across:
                turned = values.T
                ones = jnp.ones((16, count), BF)
            for head in range(2):
                own, first, _ = head_lanes(head)
                k_own = jnp.where(own, keys, jnp.where(first & ~seen, bf(big_negative), bf(0)))
                q_own = jnp.where(own, queries, jnp.where(first, bf(1), bf(0)))
                scores = nt(k_own, q_own)
                if causal:
                    key_at = lax.broadcasted_iota(jnp.int32, scores.shape, 0)
                    query_at = lax.broadcasted_iota(jnp.int32, scores.shape, 1)
                    allowed = (key_at <= query_at) | (key_at >= nk)
                    scores = jnp.where(allowed, scores, big_negative)
                if peaked:
                    scores = scores - jnp.max(scores, axis=0, keepdims=True)
                weights = jnp.exp(scores).astype(BF)
                p_refs[seg][head] = weights
                if across:
                    rows = jnp.concatenate([turned[head * HD : (head + 1) * HD], ones], 0)
                    mixed = nn(rows, weights)
                    inverse = 1.0 / mixed[HD : HD + 1]
                    outs.append(mixed[:HD] * inverse)
                    invs.append(jnp.broadcast_to(inverse, (HD, nq)))
                    continue
                mixed = tn(weights, jnp.where(own, values, bf(1)))
                inverse = 1.0 / pltpu.roll(mixed, HD, 1)
                mixed = mixed * inverse
                out = mixed if out is None else jnp.where(own, mixed, out)
                inv = inverse if inv is None else jnp.where(own, inverse, inv)
            if across:
                out = jnp.concatenate(outs, 0).T
                inv = jnp.concatenate(invs, 0).T
            o_ref[q0 : q0 + nq] = out.astype(BF)
            inv_ref[q0 : q0 + nq] = inv

    if not checked:
        work(True)
        return

    limit = 50.0**2
    head_row = lax.broadcasted_iota(jnp.int32, (LANES, LANES), 0) // HD
    head_col = lax.broadcasted_iota(jnp.int32, (LANES, LANES), 1) // HD
    same_head = jnp.where(head_row == head_col, 1.0, 0.0).astype(BF)

    def largest(array):
        square = (array.astype(F32) * array.astype(F32)).astype(BF)
        return jnp.max(nn(square, same_head), axis=0, keepdims=True)

    key_peak = largest(k_refs[0][...])
    for ref in k_refs[1:]:
        key_peak = jnp.maximum(key_peak, largest(ref[...]))
    if prefix:
        key_peak = jnp.maximum(key_peak, largest(pk_ref[...]))
    small = jnp.max(largest(q_ref[...]) * key_peak) * (1.0 / HD) <= limit

    @pl.when(small)
    def _():
        work(False)

    @pl.when(jnp.logical_not(small))
    def _():
        work(True)


def lane_views(refs, group, j):
    views = []
    for ref in refs:
        if len(ref.shape) == 2:
            views.append(ref.at[:, j * LANES : (j + 1) * LANES])
        else:
            views.append(ref.at[2 * j : 2 * j + 2])
    return views


def attend_kernel(len_ref, *refs, group, **kw):
    for j in range(group):
        attend_pair(len_ref, *lane_views(refs, group, j), **kw)


def column_spec(rows, offset, row_block=0, group=1):
    return pl.BlockSpec((rows, group * LANES), lambda h: (row_block, h + offset // group))


def attend(lengths, q, keys, values, prefixes, segs, causal, which=0, group=1, checked=False):
    pairs = 8
    q_rows = q[1]
    prefix = prefixes is not None
    extra = PRE_PAD if prefix else 0
    specs = [pl.BlockSpec(memory_space=pltpu.SMEM)]
    args = [lengths]
    for array, rows, block, offset in [q, *keys, *values]:
        specs.append(column_spec(rows, offset, block, group))
        args.append(array)
    if prefix:
        specs += [column_spec(PRE_PAD, 0, 0, group)] * 2
        args += list(prefixes)
    weight_shapes = [(2 * pairs, nk + extra, nq) for _, nq, _, nk in segs]
    return pl.pallas_call(
        functools.partial(
            attend_kernel, group=group, segs=segs, prefix=prefix, causal=causal, pieces=len(keys), which=which,
            checked=checked,
        ),
        grid=(pairs // group,),
        in_specs=specs,
        out_specs=[column_spec(q_rows, 0, 0, group)] * 2
        + [pl.BlockSpec((2 * group,) + s[1:], lambda h: (h, 0, 0)) for s in weight_shapes],
        out_shape=[
            jax.ShapeDtypeStruct((q_rows, pairs * LANES), BF),
            jax.ShapeDtypeStruct((q_rows, pairs * LANES), F32),
        ]
        + [jax.ShapeDtypeStruct(s, BF) for s in weight_shapes],
        compiler_params=params(),
        name="attend",
    )(*args)


def attend_back_pair(
    q_ref, k_refs, v_refs, o_ref, inv_ref, g_refs, pk_ref, pv_ref, p_refs, dq_ref, dk_ref, dv_ref, segs
):
    prefix_totals = [None, None]
    scale = HD**-0.5
    for seg, (q0, nq, k0, nk) in enumerate(segs):
        keys = stacked(k_refs, pk_ref, k0, nk)
        values = stacked(v_refs, pv_ref, k0, nk)
        queries = q_ref[q0 : q0 + nq]
        grads = stacked(g_refs, None, q0, nq).astype(F32) * inv_ref[q0 : q0 + nq]
        grads_low = grads.astype(BF)
        dots = grads * o_ref[q0 : q0 + nq].astype(F32)
        dq = dk = dv = None
        across = nq >= LANES and keys.shape[0] >= 4 * LANES
        turned_grads = []
        if across:
            turned = keys.T
        for head in range(2):
            own, first, second = head_lanes(head)
            row_dot = -jnp.sum(jnp.where(own, dots, 0.0), axis=1, keepdims=True)
            high = row_dot.astype(BF)
            rest = (row_dot - high.astype(F32)).astype(BF)
            g_own = jnp.where(
                own, grads_low, jnp.where(first, high, jnp.where(second, rest, bf(0)))
            )
            v_own = jnp.where(own, values, jnp.where(first | second, bf(1), bf(0)))
            weights = p_refs[seg][head]
            score_grad = (weights.astype(F32) * nt(v_own, g_own)).astype(BF)
            dv_head = nn(weights, grads_low)
            dk_head = nn(score_grad, queries)
            dq_head = None if across else tn(score_grad, keys)
            if across:
                turned_grads.append(nn(turned[head * HD : (head + 1) * HD], score_grad))
            if not across:
                dq = dq_head if dq is None else jnp.where(own, dq_head, dq)
            dk = dk_head if dk is None else jnp.where(own, dk_head, dk)
            dv = dv_head if dv is None else jnp.where(own, dv_head, dv)
        if across:
            dq = jnp.concatenate(turned_grads, 0).T
        dk = dk * scale
        dq_ref[q0 : q0 + nq] = (dq * scale).astype(BF)
        at = k0 - segs[0][2]
        dk_ref[at : at + nk] = dk[:nk].astype(BF)
        dv_ref[at : at + nk] = dv[:nk].astype(BF)
        if pk_ref is not None:
            for i, grad in enumerate((dk, dv)):
                part = grad[nk:]
                prefix_totals[i] = part if seg == 0 else prefix_totals[i] + part
    return prefix_totals


def attend_back_kernel(*refs, group, **kw):
    for j in range(group):
        attend_back_views(*lane_views(refs, group, j), **kw)


def attend_back_views(*refs, segs, prefix, pieces):
    q_ref, o_ref, inv_ref, g_ref = refs[:4]
    k_refs, v_refs = refs[4 : 4 + pieces], refs[4 + pieces : 4 + 2 * pieces]
    at = 4 + 2 * pieces
    pk_ref = pv_ref = None
    if prefix:
        pk_ref, pv_ref = refs[at : at + 2]
        at += 2
    outs = refs[at + len(segs) :]
    totals = attend_back_pair(
        q_ref, k_refs, v_refs, o_ref, inv_ref, [g_ref], pk_ref, pv_ref,
        refs[at : at + len(segs)], *outs[:3], segs,
    )
    if prefix:
        outs[3][...] = totals[0]
        outs[4][...] = totals[1]


def attend_back(q, keys, values, prefixes, attended, inverse, grad, weights, segs, group=2):
    pairs = 8
    q_rows = q[1]
    k_rows = sum(nk for _, _, _, nk in segs)
    prefix = prefixes is not None
    specs, args = [], []
    own = [(a, q_rows, 0, 0) for a in (attended, inverse, grad)]
    for array, rows, block, offset in [q, *own, *keys, *values]:
        specs.append(column_spec(rows, offset, block, group))
        args.append(array)
    if prefix:
        specs += [column_spec(PRE_PAD, 0, 0, group)] * 2
        args += list(prefixes)
    specs += [pl.BlockSpec((2 * group,) + w.shape[1:], lambda h: (h, 0, 0)) for w in weights]
    args += list(weights)
    out_specs = [column_spec(n, 0, 0, group) for n in (q_rows, k_rows, k_rows)]
    out_shape = [
        jax.ShapeDtypeStruct((q_rows, pairs * LANES), BF),
        jax.ShapeDtypeStruct((k_rows, pairs * LANES), BF),
        jax.ShapeDtypeStruct((k_rows, pairs * LANES), BF),
    ]
    if prefix:
        out_specs += [column_spec(PRE_PAD, 0, 0, group)] * 2
        out_shape += [jax.ShapeDtypeStruct((PRE_PAD, pairs * LANES), F32)] * 2
    return pl.pallas_call(
        functools.partial(
            attend_back_kernel, group=group, segs=segs, prefix=prefix, pieces=len(keys)
        ),
        grid=(pairs // group,),
        in_specs=specs,
        out_specs=out_specs,
        out_shape=out_shape,
        compiler_params=params(),
        name="attend_back",
    )(*args)


class Weights:
    def __init__(self, sources, targets, sems):
        self.sources, self.targets, self.sems = sources, targets, sems

    def copy(self, name, part=None):
        source, target = self.sources[name], self.targets[name]
        first = list(self.sources).index(name)
        sem = self.sems.at[first, 0 if part is None else part]
        if part is not None:
            cut = pl.ds(pl.multiple_of(part * wide, wide), wide)
            index = (slice(None), cut) if name == "in" else (cut, slice(None))
            source, target = source.at[index], target.at[index]
        return pltpu.make_async_copy(source, target, sem)

    def wait(self, name, part=None):
        self.copy(name, part).wait()

    def part(self, name, part):
        cut = pl.ds(pl.multiple_of(part * wide, wide), wide)
        index = (slice(None), cut) if name == "in" else (cut, slice(None))
        return self.targets[name].at[index]


def weight_scratch(arrays, parts):
    return [pltpu.VMEM(a.shape, BF) for a in arrays] + [
        pltpu.SemaphoreType.DMA((len(arrays), parts))
    ]


def ffn_step(low_ref, acc_ref, in_ref, out_ref, slope_ref, act_ref, bias_ref, scale):
    for start, size in row_tiles(low_ref.shape[0]):
        rows = slice(start, start + size)
        hidden = nn(low_ref[rows], in_ref[...])
        if bias_ref is not None:
            hidden = hidden + bias_ref[...]
        active, slope = gelu_pair(hidden)
        slope_ref[rows] = slope.astype(BF)
        active = active.astype(BF)
        if act_ref is not None:
            act_ref[rows] = active
        term = nn(active, out_ref[...])
        acc_ref[rows] += term if scale is None else scale * term


def enc_ffn_kernel(
    x_ref, att_ref, gain_ref, downb_ref, upb_ref, wo_hbm, in_hbm, out_hbm, down_hbm, up_hbm,
    mem_ref, slope_ref, pre_slope_ref, act_ref, low_ref, scales_ref,
    acc_ref, wo_ref, in_ref, out_ref, down_ref, up_ref, sems,
):
    weights = Weights(
        {"wo": wo_hbm, "in": in_hbm, "out": out_hbm, "down": down_hbm, "up": up_hbm},
        {"wo": wo_ref, "in": in_ref, "out": out_ref, "down": down_ref, "up": up_ref},
        sems,
    )

    weights.copy("wo").start()
    for part in range(in_ref.shape[1] // wide):
        weights.copy("in", part).start()
        weights.copy("out", part).start()
    weights.copy("down").start()
    weights.copy("up").start()
    weights.wait("wo")
    for start, size in row_tiles(x_ref.shape[0]):
        rows = slice(start, start + size)
        first = x_ref[rows].astype(F32) + nn(att_ref[rows], wo_ref[...])
        hat, scale = norm_rows(first)
        normed = hat * gain_ref[0:1]
        acc_ref[rows] = normed
        low_ref[rows] = normed.astype(BF)
        scales_ref[rows, 0:1] = scale

    def one_part(part, carry):
        weights.wait("in", part)
        weights.wait("out", part)
        cols = pl.ds(pl.multiple_of(part * wide, wide), wide)
        ffn_step(
            low_ref, acc_ref, in_ref.at[:, cols], out_ref.at[cols], slope_ref.at[:, cols],
            None, None, None,
        )
        return carry

    lax.fori_loop(0, in_ref.shape[1] // wide, one_part, 0)

    weights.wait("down")
    weights.wait("up")
    ffn_step(low_ref, acc_ref, down_ref, up_ref, pre_slope_ref, act_ref, downb_ref, adapter_scale)
    for start, size in row_tiles(x_ref.shape[0]):
        rows = slice(start, start + size)
        hat, scale = norm_rows(acc_ref[rows] + adapter_scale * upb_ref[...])
        mem_ref[rows] = (hat * gain_ref[1:2]).astype(BF)
        scales_ref[rows, 1:2] = scale


def enc_ffn(x, att, w):
    rows, width = x.shape
    hidden = w["ffn_in"].shape[1]
    steps = hidden // wide
    weights = [w["out"], w["ffn_in"], w["ffn_out"], w["down"], w["up"]]
    return pl.pallas_call(
        enc_ffn_kernel,
        grid=(1,),
        in_specs=[
            single((rows, width)),
            single((rows, width)),
            single((2, width)),
            single((1, chunk)),
            single((1, width)),
        ]
        + [pl.BlockSpec(memory_space=pl.ANY)] * len(weights),
        out_specs=[
            single((rows, width)),
            single((rows, hidden)),
            single((rows, chunk)),
            single((rows, chunk)),
            single((rows, width)),
            single((rows, LANES)),
        ],
        out_shape=[
            jax.ShapeDtypeStruct((rows, width), BF),
            jax.ShapeDtypeStruct((rows, hidden), BF),
            jax.ShapeDtypeStruct((rows, chunk), BF),
            jax.ShapeDtypeStruct((rows, chunk), BF),
            jax.ShapeDtypeStruct((rows, width), BF),
            jax.ShapeDtypeStruct((rows, LANES), F32),
        ],
        scratch_shapes=[pltpu.VMEM((rows, width), F32)] + weight_scratch(weights, steps),
        compiler_params=params(),
        name="enc_ffn",
    )(x, att, w["gains"], w["down_bias"], w["up_bias"], *weights)


def ffn_back_step(grad_ref, acc_ref, in_ref, out_ref, slope_ref):
    for start, size in row_tiles(grad_ref.shape[0]):
        rows = slice(start, start + size)
        pre = (nt(grad_ref[rows], out_ref[...]) * slope_ref[rows].astype(F32)).astype(BF)
        acc_ref[rows] += nt(pre, in_ref[...])


def adapter_back(grad_ref, acc_ref, low_ref, act_ref, slope_ref, down_ref, up_ref, outs, pre_ref):
    ddown_ref, ddownb_ref, dup_ref, dupb_ref = outs
    total = None
    for start, size in row_tiles(grad_ref.shape[0]):
        rows = slice(start, start + size)
        back = adapter_scale * nt(grad_ref[rows], up_ref[...])
        pre = (back * slope_ref[rows].astype(F32)).astype(BF)
        pre_ref[rows] = pre
        sums = jnp.sum(pre.astype(F32), axis=0, keepdims=True)
        total = sums if total is None else total + sums
        acc_ref[rows] += nt(pre, down_ref[...])
    ddownb_ref[...] = total
    ddown_ref[...] = tn(low_ref[...], pre_ref[...])
    dup_ref[...] = adapter_scale * tn(act_ref[...], grad_ref[...])
    dupb_ref[...] = adapter_scale * jnp.sum(grad_ref[...].astype(F32), axis=0, keepdims=True)


def enc_ffn_back_kernel(*refs, pieces):
    enc_ffn_back_body(refs[:pieces], *refs[pieces:])


def enc_ffn_back_body(
    dmem_refs, mem_ref, low_ref, scales_ref, gain_ref, slope_ref, pre_slope_ref,
    up_hbm, down_hbm, in_hbm, out_hbm, wo_hbm,
    dfirst_ref, datt_ref, grad_ref, pre_ref,
    acc_ref, up_ref, down_ref, in_ref, out_ref, wo_ref, sems,
):
    weights = Weights(
        {"up": up_hbm, "down": down_hbm, "in": in_hbm, "out": out_hbm, "wo": wo_hbm},
        {"up": up_ref, "down": down_ref, "in": in_ref, "out": out_ref, "wo": wo_ref},
        sems,
    )

    weights.copy("up").start()
    weights.copy("down").start()
    for part in range(in_ref.shape[1] // wide):
        weights.copy("out", part).start()
        weights.copy("in", part).start()
    weights.copy("wo").start()
    weights.wait("up")
    weights.wait("down")
    for start, size in row_tiles(mem_ref.shape[0]):
        rows = slice(start, start + size)
        gain = gain_ref[1:2]
        hat = mem_ref[rows].astype(F32) / gain
        dmem = stacked(dmem_refs, None, start, size).astype(F32)
        grad = norm_rows_back(hat, scales_ref[rows, 1:2], dmem * gain)
        low = grad.astype(BF)
        grad_ref[rows] = low
        back = adapter_scale * nt(low, up_ref[...])
        pre = (back * pre_slope_ref[rows].astype(F32)).astype(BF)
        pre_ref[rows] = pre
        acc_ref[rows] = grad + nt(pre, down_ref[...])

    def one_part(part, carry):
        weights.wait("out", part)
        weights.wait("in", part)
        cols = pl.ds(pl.multiple_of(part * wide, wide), wide)
        ffn_back_step(
            grad_ref, acc_ref, in_ref.at[:, cols], out_ref.at[cols], slope_ref.at[:, cols]
        )
        return carry

    lax.fori_loop(0, in_ref.shape[1] // wide, one_part, 0)

    weights.wait("wo")
    for start, size in row_tiles(mem_ref.shape[0]):
        rows = slice(start, start + size)
        gain = gain_ref[0:1]
        hat = low_ref[rows].astype(F32) / gain
        grad = norm_rows_back(hat, scales_ref[rows, 0:1], acc_ref[rows] * gain)
        dfirst_ref[rows] = grad
        datt_ref[rows] = nt(grad.astype(BF), wo_ref[...]).astype(BF)


def enc_ffn_back(dmems, saved, w):
    mem, slope, pre_slope, act, low, scales = saved
    rows, width = mem.shape
    hidden = w["ffn_in"].shape[1]
    steps = hidden // wide
    weights = [w["up"], w["down"], w["ffn_in"], w["ffn_out"], w["out"]]
    return pl.pallas_call(
        functools.partial(enc_ffn_back_kernel, pieces=len(dmems)),
        grid=(1,),
        in_specs=[single(d.shape) for d in dmems]
        + [
            single((rows, width)),
            single((rows, width)),
            single((rows, LANES)),
            single((2, width)),
            single((rows, hidden)),
            single((rows, chunk)),
        ]
        + [pl.BlockSpec(memory_space=pl.ANY)] * len(weights),
        out_specs=[
            single((rows, width)),
            single((rows, width)),
            single((rows, width)),
            single((rows, chunk)),
        ],
        out_shape=[
            jax.ShapeDtypeStruct((rows, width), F32),
            jax.ShapeDtypeStruct((rows, width), BF),
            jax.ShapeDtypeStruct((rows, width), BF),
            jax.ShapeDtypeStruct((rows, chunk), BF),
        ],
        scratch_shapes=[pltpu.VMEM((rows, width), F32)] + weight_scratch(weights, steps),
        compiler_params=params(),
        name="enc_ffn_back",
    )(*dmems, mem, low, scales, w["gains"], slope, pre_slope, *weights)


def dec_mid_kernel(x_ref, att_ref, wo_ref, gain_ref, wq_ref, n_ref, scale_ref, *cq_refs):
    for (start, size), cq_ref in zip(row_tiles(x_ref.shape[0], TGT), cq_refs):
        rows = slice(start, start + size)
        first = x_ref[rows].astype(F32) + nn(att_ref[rows], wo_ref[...])
        hat, scale = norm_rows(first)
        normed = hat * gain_ref[0:1]
        n_ref[rows] = normed
        scale_ref[rows, 0:1] = scale
        cq_ref[...] = nn(normed.astype(BF), wq_ref[...]).astype(BF)


def dec_mid(x, att, w, cross):
    rows, width = x.shape
    return pl.pallas_call(
        dec_mid_kernel,
        out_shape=[
            jax.ShapeDtypeStruct((rows, width), F32),
            jax.ShapeDtypeStruct((rows, LANES), F32),
        ]
        + [jax.ShapeDtypeStruct((TGT, width), BF)] * (rows // TGT),
        compiler_params=params(),
        name="dec_mid",
    )(x, att, w["out"], w["gains"], cross["query"])


def dec_ffn_kernel(
    len_ref, n_ref, catt_ref, cot_ref, cgain_ref, gain_ref, downb_ref, upb_ref,
    wco_hbm, in_hbm, out_hbm, down_hbm, up_hbm,
    y_ref, dsecond_ref, dcatt_ref, ddown_ref, ddownb_ref, dup_ref, dupb_ref,
    acc_ref, low_ref, grad_ref, slope_ref, pre_slope_ref, act_ref, pre_ref, scale_ref,
    wco_ref, in_ref, out_ref, down_ref, up_ref, sems,
    *, steps, which,
):
    weights = Weights(
        {"wco": wco_hbm, "in": in_hbm, "out": out_hbm, "down": down_hbm, "up": up_hbm},
        {"wco": wco_ref, "in": in_ref, "out": out_ref, "down": down_ref, "up": up_ref},
        sems,
    )

    weights.copy("wco").start()
    for part in range(steps):
        weights.copy("in", part).start()
        weights.copy("out", part).start()
    weights.copy("down").start()
    weights.copy("up").start()
    weights.wait("wco")
    second = n_ref[...] + nn(catt_ref[...], wco_ref[...])
    hat, scale = norm_rows(second)
    middle = hat * cgain_ref[...]
    acc_ref[...] = middle
    low_ref[...] = middle.astype(BF)
    scale_ref[:, 0:1] = scale

    def forward(part, carry):
        weights.wait("in", part)
        weights.wait("out", part)
        ffn_step(
            low_ref, acc_ref, weights.part("in", part), weights.part("out", part),
            slope_ref.at[part], None, None, None,
        )
        return carry

    lax.fori_loop(0, steps, forward, 0)

    weights.wait("down")
    weights.wait("up")
    ffn_step(
        low_ref, acc_ref, down_ref, up_ref, pre_slope_ref, act_ref, downb_ref, adapter_scale
    )
    gain = gain_ref[1:2]
    hat, scale = norm_rows(acc_ref[...] + adapter_scale * upb_ref[...])
    row = lax.broadcasted_iota(jnp.int32, (low_ref.shape[0], 1), 0)
    valid = row < len_ref[0, which]
    y_ref[...] = jnp.where(valid, hat * gain, 0.0).astype(BF)
    cot = jnp.where(valid, cot_ref[...].astype(F32), 0.0)
    grad = norm_rows_back(hat, scale, cot * gain)
    acc_ref[...] = grad
    grad_ref[...] = grad.astype(BF)
    adapter_back(
        grad_ref, acc_ref, low_ref, act_ref, pre_slope_ref, down_ref, up_ref,
        (ddown_ref, ddownb_ref, dup_ref, dupb_ref), pre_ref,
    )

    def backward(part, carry):
        ffn_back_step(
            grad_ref, acc_ref, weights.part("in", part), weights.part("out", part),
            slope_ref.at[part],
        )
        return carry

    lax.fori_loop(0, steps, backward, 0)

    gain = cgain_ref[...]
    hat = low_ref[...].astype(F32) / gain
    grad = norm_rows_back(hat, scale_ref[:, 0:1], acc_ref[...] * gain)
    dsecond_ref[...] = grad
    dcatt_ref[...] = nt(grad.astype(BF), wco_ref[...]).astype(BF)


def dec_ffn(lengths, n, catt, cot, w, cross, which):
    rows, width = catt.shape
    hidden = w["ffn_in"].shape[1]
    steps = hidden // wide
    weights = [cross["out"], w["ffn_in"], w["ffn_out"], w["down"], w["up"]]
    return pl.pallas_call(
        functools.partial(dec_ffn_kernel, steps=steps, which=which),
        grid=(1,),
        in_specs=[
            pl.BlockSpec(memory_space=pltpu.SMEM),
            pl.BlockSpec((rows, width), lambda i: (which, 0)),
            whole((rows, width)),
            pl.BlockSpec((rows, width), lambda i: (which, 0)),
            whole((1, width)),
            whole((2, width)),
            whole((1, chunk)),
            whole((1, width)),
        ]
        + [pl.BlockSpec(memory_space=pl.ANY)] * len(weights),
        out_specs=[
            whole((rows, width)),
            whole((rows, width)),
            whole((rows, width)),
            whole((width, chunk)),
            whole((1, chunk)),
            whole((chunk, width)),
            whole((1, width)),
        ],
        out_shape=[
            jax.ShapeDtypeStruct((rows, width), BF),
            jax.ShapeDtypeStruct((rows, width), F32),
            jax.ShapeDtypeStruct((rows, width), BF),
            jax.ShapeDtypeStruct((width, chunk), F32),
            jax.ShapeDtypeStruct((1, chunk), F32),
            jax.ShapeDtypeStruct((chunk, width), F32),
            jax.ShapeDtypeStruct((1, width), F32),
        ],
        scratch_shapes=[
            pltpu.VMEM((rows, width), F32),
            pltpu.VMEM((rows, width), BF),
            pltpu.VMEM((rows, width), BF),
            pltpu.VMEM((steps, rows, wide), BF),
            pltpu.VMEM((rows, chunk), BF),
            pltpu.VMEM((rows, chunk), BF),
            pltpu.VMEM((rows, chunk), BF),
            pltpu.VMEM((rows, LANES), F32),
        ]
        + weight_scratch(weights, steps),
        compiler_params=params(),
        name="dec_ffn",
    )(
        lengths, n, catt, cot, cross["gain"], w["gains"], w["down_bias"], w["up_bias"], *weights
    )


def dec_mid_back_kernel(
    dsecond0_ref, dsecond1_ref, dcq0_ref, dcq1_ref, wq_ref, n_ref, scale_ref, gain_ref, wo_ref,
    dfirst_ref, datt_ref,
):
    for pair, (dsecond_ref, dcq_ref) in enumerate(
        ((dsecond0_ref, dcq0_ref), (dsecond1_ref, dcq1_ref))
    ):
        rows = slice(pair * TGT, (pair + 1) * TGT)
        gain = gain_ref[0:1]
        total = dsecond_ref[...] + nt(dcq_ref[...], wq_ref[...])
        grad = norm_rows_back(n_ref[rows] / gain, scale_ref[rows, 0:1], total * gain)
        dfirst_ref[rows] = grad
        datt_ref[rows] = nt(grad.astype(BF), wo_ref[...]).astype(BF)


def dec_mid_back(dseconds, dcqs, n, scale, w, cross):
    rows, width = n.shape
    return pl.pallas_call(
        dec_mid_back_kernel,
        out_shape=[
            jax.ShapeDtypeStruct((rows, width), F32),
            jax.ShapeDtypeStruct((rows, width), BF),
        ],
        compiler_params=params(),
        name="dec_mid_back",
    )(*dseconds, *dcqs, cross["query"], n, scale, w["gains"], w["out"])


enc_segs = ((0, SRC_LONG, 0, SRC_LONG), (SRC_LONG, SRC_SHORT, SRC_LONG, SRC_SHORT))
dec_segs = ((0, TGT, 0, TGT), (TGT, TGT, TGT, TGT))
cross_segs = (((0, TGT, 0, SRC_LONG),), ((0, TGT, 0, SRC_SHORT),))


def self_columns(qkv):
    rows = qkv.shape[0]
    return (qkv, rows, 0, 0), [(qkv, rows, 0, 8)], [(qkv, rows, 0, 16)]


def cross_columns(cq, kv, which):
    keys = (SRC_LONG, SRC_SHORT)[which]
    return (cq, TGT, 0, 0), [(kv, keys, 0, 0)], [(kv, keys, 0, 8)]


def decoder_self(t, lengths, w, cross):
    qkv = product(t, w["qkv"])
    att, inv, *weights = attend(lengths, *self_columns(qkv), w["prefix"], dec_segs, True, group=2)
    n, scale, *cq = dec_mid(t, att, w, cross)
    return cq, (qkv, att, inv, weights, n, scale)


def cross_forward(lengths, cq, kv, which):
    return attend(
        lengths, *cross_columns(cq, kv, which), None, cross_segs[which], False, which, group=2
    )


def cross_backward(cq, kv, forward, dcatt, which):
    catt, inv, *weights = forward
    return attend_back(
        *cross_columns(cq, kv, which), None, catt, inv, dcatt, weights, cross_segs[which]
    )


def decoder_self_back(kept, dseconds, dcqs, w, cross):
    qkv, att, inv, weights, n, scale = kept
    dfirst, datt = dec_mid_back(dseconds, dcqs, n, scale, w, cross)
    dq, dk, dv, *dprefix = attend_back(
        *self_columns(qkv), w["prefix"], att, inv, datt, weights, dec_segs, group=1
    )
    return back_product([dq, dk, dv], w["qkv"], dfirst)[0], dprefix


def small_shape(devices):
    return 8, 8 * (2 * chunk) // devices


def finish_kernel(
    q_ref, k_ref, v_ref, o_ref, inv_ref, g0_ref, g1_ref, g2_ref, pk_ref, pv_ref, pl_ref, ps_ref,
    dfirst0_ref, dfirst1_ref, dfirst2_ref, wqkv_ref,
    low_all, act_all, grad_all, pre_all,
    long_down, long_downb, long_up, long_upb,
    short_down, short_downb, short_up, short_upb, dpk_ref, dpv_ref,
    y0_ref, y1_ref, dt_ref,
    source_ref, y_ref, target_ref, o_up_ref, o_down_ref, o_prefix_ref, o_upb_ref, o_downb_ref,
    dq, dk, dv, small, lows_all, acts_all, grads_all, pres_all, ups, downs, mine, theirs, half_sum, across_y, y_sum, landed, total, result,
    small_landed, small_total, small_result, dx, dx_landed, lows, lows_landed,
    load_sems, pair_sems, y_sems, z_sems, gather_sems, share_y_sems, back_sems,
    small_sems, share_sems, cross_sems,
    *, devices,
):
    step = pl.program_id(0)
    pairs = 8
    section = lax.axis_index("section")
    is_encoder = section == 0
    chips = devices // 2
    line = chips // 2
    slices = 16 // line
    rows = 2 * chunk
    half = rows // 2
    size = half // slices
    side = size // 2
    part = side // line
    place = lax.axis_index("dp")
    core, chip = lax.rem(place, 2), place // 2
    bit, at_line = lax.rem(chip, 2), chip // 2
    partner = place + 1 - 2 * core
    beside = place + 2 - 4 * bit
    small_rows, small_cols = small_shape(devices)
    tile = 256
    width = 2 * chunk
    scale = 1.0 / devices

    def aligned(value, unit=16):
        return pl.multiple_of(value, unit)

    def along(distance):
        return (lax.rem(at_line + distance, line) * 2 + bit) * 2 + core

    def remote(source, target, send_sem, recv_sem, other):
        return pltpu.make_async_remote_copy(
            src_ref=source, dst_ref=target, send_sem=send_sem, recv_sem=recv_sem,
            device_id=other, device_id_type=pl.DeviceIdType.MESH,
        )

    def in_group(other):
        return {"dp": other}

    across = {"section": 1 - section}
    kept = aligned(core * half)
    given = aligned((1 - core) * half)

    def swap():
        return remote(
            mine.at[pl.ds(given, half)], theirs, pair_sems.at[0], pair_sems.at[1],
            in_group(partner),
        )

    def y_send(j):
        there = pl.ds(aligned(j * size + (1 - bit) * side), side)
        return remote(
            half_sum.at[there], across_y.at[j], y_sems.at[0, j], y_sems.at[1, j], in_group(beside)
        )

    def z_send(j, s):
        there = pl.ds(aligned(lax.rem(at_line + s, line) * part), part)
        return remote(
            y_sum.at[j].at[there], landed.at[j, s - 1],
            z_sems.at[0, j, s - 1], z_sems.at[1, j, s - 1], in_group(along(s)),
        )

    def own_rows(j):
        return pl.ds(aligned(kept + j * size + bit * side + at_line * part), part)

    def own_side(j):
        return pl.ds(aligned(kept + j * size + bit * side), side)

    def other_side(j):
        return pl.ds(aligned(kept + j * size + (1 - bit) * side), side)

    def gather(j, s):
        return remote(
            total.at[j], result.at[own_rows(j)],
            gather_sems.at[0, j, s - 1], gather_sems.at[1, j, s - 1], in_group(along(s)),
        )

    def y_share(j):
        return remote(
            result.at[own_side(j)], result.at[own_side(j)],
            share_y_sems.at[0, j], share_y_sems.at[1, j], in_group(beside),
        )

    def back(j, i):
        there = own_side(j) if i == 0 else other_side(j)
        return remote(
            result.at[there], result.at[there],
            back_sems.at[0, j, i], back_sems.at[1, j, i], in_group(partner),
        )

    def piece(index):
        row = aligned(lax.rem(index, 8) * small_rows, 8)
        col = aligned((index // 8) * small_cols, LANES)
        return pl.ds(row, small_rows), pl.ds(col, small_cols)

    def small_out(s):
        return remote(
            small.at[piece(lax.rem(place + s, devices))], small_landed.at[s - 1],
            small_sems.at[0, s - 1], small_sems.at[1, s - 1],
            in_group(lax.rem(place + s, devices)),
        )

    def small_share(s):
        return remote(
            small_total, small_result.at[piece(place)],
            share_sems.at[0, s - 1], share_sems.at[1, s - 1],
            in_group(lax.rem(place + s, devices)),
        )

    def send_low():
        return remote(lows, lows_landed, cross_sems.at[0, 0], cross_sems.at[1, 0], across)

    def send_high(i):
        return remote(
            dx.at[i], dx_landed.at[i], cross_sems.at[0, 1 + i], cross_sems.at[1, 1 + i], across
        )

    def greet(barrier, other):
        pl.semaphore_signal(
            barrier, inc=1, device_id=other, device_id_type=pl.DeviceIdType.MESH
        )

    def load(source, target, i):
        return pltpu.make_async_copy(source, target, load_sems.at[i])

    enc_loads = [
        load(low_all, lows_all, 0), load(act_all, acts_all, 1),
        load(grad_all, grads_all, 2), load(pre_all, pres_all, 3),
    ]
    dec_loads = [
        load(long_up, ups.at[0], 0), load(long_down, downs.at[0], 1),
        load(short_up, ups.at[1], 2), load(short_down, downs.at[1], 3),
    ]

    @pl.when(step == 0)
    def _():
        barrier = pltpu.get_barrier_semaphore()
        for s in range(1, devices):
            greet(barrier, in_group(lax.rem(place + s, devices)))

        @pl.when(is_encoder)
        def _():
            for copy in enc_loads:
                copy.start()

        @pl.when(jnp.logical_not(is_encoder))
        def _():
            for copy in dec_loads:
                copy.start()

    @pl.when(is_encoder & (step < pairs))
    def _():
        at = aligned(step * LANES, LANES)
        lanes = pl.ds(at, LANES)
        prefix_totals = attend_back_pair(
            q_ref, [k_ref], [v_ref], o_ref, inv_ref, [g0_ref, g1_ref, g2_ref], pk_ref, pv_ref,
            (pl_ref, ps_ref), dq.at[:, lanes], dk.at[:, lanes], dv.at[:, lanes], enc_segs,
        )
        small[0:PRE_PAD, lanes] = prefix_totals[0] * scale
        small[PRE_PAD : 2 * PRE_PAD, lanes] = prefix_totals[1] * scale

    @pl.when(step == 0)
    def _():
        barrier = pltpu.get_barrier_semaphore()

        def pack(up, down):
            mine[0:chunk] = (up * scale).astype(BF)
            down = (down * scale).astype(BF)
            mine[chunk:width, 0:chunk] = down[0:chunk]
            mine[chunk:width, chunk:width] = down[chunk:width]

        @pl.when(is_encoder)
        def _():
            for copy in enc_loads:
                copy.wait()
            pack(
                adapter_scale * tn(acts_all[...], grads_all[...]),
                tn(lows_all[...], pres_all[...]),
            )
            pl.semaphore_wait(barrier, devices - 1)
            greet(barrier, across)

        @pl.when(jnp.logical_not(is_encoder))
        def _():
            for copy in dec_loads:
                copy.wait()
            pack(ups[0] + ups[1], downs[0] + downs[1])
            pl.semaphore_wait(barrier, devices)
            greet(barrier, across)

        swap().start()

        @pl.when(jnp.logical_not(is_encoder))
        def _():
            low = width // 2
            lows[0, 0:TGT] = y0_ref[:, 0:low]
            lows[0, TGT : 2 * TGT] = y1_ref[:, 0:low]
            lows[1] = dt_ref[:, 0:low]
            send_low().start()
            small[0:PRE_PAD] = dpk_ref[...] * scale
            small[PRE_PAD : 2 * PRE_PAD] = dpv_ref[...] * scale

    @pl.when(step == 1)
    def _():
        swap().wait()
        half_sum[...] = (
            mine[pl.ds(kept, half)].astype(F32) + theirs[...].astype(F32)
        ).astype(BF)
        for j in range(min(2, slices)):
            y_send(j).start()

    for j in range(slices):

        @pl.when(step == 2 + j)
        def _(j=j):
            y_send(j).wait()
            if j + 2 < slices:
                y_send(j + 2).start()
            own = pl.ds(aligned(j * size + bit * side), side)
            y_sum[j] = (half_sum[own].astype(F32) + across_y[j].astype(F32)).astype(BF)
            for s in range(1, line):
                z_send(j, s).start()

        @pl.when(step == 4 + j)
        def _(j=j):
            summed = y_sum[j, pl.ds(aligned(at_line * part), part)].astype(F32)
            for s in range(1, line):
                z_send(j, s).wait()
                summed = summed + landed[j, s - 1].astype(F32)
            total[j] = summed.astype(BF)
            result[own_rows(j)] = total[j]
            for s in range(1, line):
                gather(j, s).start()

        @pl.when(step == 6 + j)
        def _(j=j):
            for s in range(1, line):
                gather(j, s).wait()
            y_share(j).start()
            back(j, 0).start()

        @pl.when(step == 8 + j)
        def _(j=j):
            y_share(j).wait()
            back(j, 1).start()

    @pl.when(step == pairs - 1)
    def _():
        @pl.when(is_encoder)
        def _():
            up_row = jnp.sum(grads_all[...].astype(F32), axis=0, keepdims=True)
            down_row = jnp.sum(pres_all[...].astype(F32), axis=0, keepdims=True)
            down_row = jnp.concatenate([down_row, jnp.zeros_like(down_row)], 1)
            small[PRE : PRE + 1] = up_row * (adapter_scale * scale)
            small[PRE + 1 : PRE + 2] = down_row * scale

        @pl.when(jnp.logical_not(is_encoder))
        def _():
            down_row = long_downb[...] + short_downb[...]
            down_row = jnp.concatenate([down_row, jnp.zeros_like(down_row)], 1)
            small[PRE : PRE + 1] = (long_upb[...] + short_upb[...]) * scale
            small[PRE + 1 : PRE + 2] = down_row * scale

        for s in range(1, devices):
            small_out(s).start()

    @pl.when(is_encoder & (step == pairs))
    def _():
        pl.semaphore_wait(pltpu.get_barrier_semaphore(), 1)

    @pl.when(is_encoder & (step >= pairs))
    def _():
        acc = jnp.concatenate([dfirst0_ref[...], dfirst1_ref[...], dfirst2_ref[...]], 0)
        for n, grad in enumerate((dq, dk, dv)):
            acc = acc + nt(grad[...], wqkv_ref[:, n * width : (n + 1) * width])
        dx[step - pairs] = acc.astype(BF)

    for i in range(2):

        @pl.when(is_encoder & (step == pairs + i))
        def _(i=i):
            send_high(i).start()

    @pl.when(step == pairs + 1)
    def _():
        own_rows_, own_cols = piece(place)
        summed = small[own_rows_, own_cols]
        for s in range(1, devices):
            small_out(s).wait()
            summed = summed + small_landed[s - 1]
        small_total[...] = summed
        small_result[own_rows_, own_cols] = summed
        for s in range(1, devices):
            small_share(s).start()

    @pl.when(step == pairs + 3)
    def _():
        for j in range(slices):
            for i in range(2):
                back(j, i).wait()
        o_up_ref[...] = result[0:chunk]
        o_down_ref[0:chunk] = result[chunk:width, 0:chunk]
        o_down_ref[chunk:width] = result[chunk:width, chunk:width]
        for s in range(1, devices):
            small_share(s).wait()
        o_prefix_ref[0] = small_result[0:PRE]
        o_prefix_ref[1] = small_result[PRE_PAD : PRE_PAD + PRE]
        o_upb_ref[...] = small_result[PRE : PRE + 1]
        o_downb_ref[...] = small_result[PRE + 1 : PRE + 2, 0:chunk]

        @pl.when(is_encoder)
        def _():
            for i in range(2):
                source_ref[:, i * tile : (i + 1) * tile] = dx[2 + i]
            send_low().wait_recv()
            y_ref[...] = lows_landed[0]
            target_ref[...] = lows_landed[1]
            for i in range(2):
                send_high(i).wait_send()

        @pl.when(jnp.logical_not(is_encoder))
        def _():
            low = width // 2
            y_ref[0:TGT] = y0_ref[:, low:width]
            y_ref[TGT : 2 * TGT] = y1_ref[:, low:width]
            target_ref[...] = dt_ref[:, low:width]
            send_low().wait_send()
            for i in range(2):
                send_high(i).wait_recv()
                source_ref[:, i * tile : (i + 1) * tile] = dx_landed[i]


def finish(saved, datt, dfirst, w, traces, adapters, dec_prefix, ys, dt):
    qkv, att, inv, weights = saved
    devices = lax.axis_size("dp")
    line = devices // 4
    slices = 16 // line
    rows, width = att.shape
    targets = dt.shape[0]
    pairs, tile = 8, 256
    half = width // 2
    side = half // slices // 2
    part = side // line
    small_rows, small_cols = small_shape(devices)

    def mine(value):
        return jnp.where(lax.axis_index("section") == 0, value, 0)

    def head(i):
        return mine(jnp.minimum(i, pairs - 1))

    def pair(offset):
        return pl.BlockSpec((rows, LANES), lambda i: (0, head(i) + offset))

    def at(i):
        return mine(jnp.where(i < pairs + 2, 2 + jnp.maximum(i - pairs, 0), i - pairs - 2))

    def once(shape):
        return pl.BlockSpec(shape, lambda i: (0,) * len(shape), pipeline_mode=pl.Buffered(1))

    anywhere = pl.BlockSpec(memory_space=pl.ANY)
    prefix_pair = pl.BlockSpec((PRE_PAD, LANES), lambda i: (0, head(i)))
    vmem = pltpu.VMEM
    dma = pltpu.SemaphoreType.DMA
    flat = [*traces] + [a for group in adapters for a in group]
    return pl.pallas_call(
        functools.partial(finish_kernel, devices=devices),
        grid=(pairs + 4,),
        in_specs=[pair(0), pair(8), pair(16), pair(0), pair(0)]
        + [pl.BlockSpec((ENC_ROWS, LANES), lambda i, n=n: (n, head(i))) for n in range(3)]
        + [prefix_pair] * 2
        + [
            pl.BlockSpec((2,) + p.shape[1:], lambda i: (head(i), 0, 0))
            for p in weights
        ]
        + [pl.BlockSpec((ENC_ROWS, tile), lambda i, n=n: (n, at(i))) for n in range(3)]
        + [
            pl.BlockSpec((tile, 3 * width), lambda i: (at(i), 0)),
        ]
        + [anywhere if a.shape[0] > 1 else once(a.shape) for a in flat]
        + [once(a.shape) for a in (*dec_prefix, *ys, dt)],
        out_specs=[
            once((rows, half)), once((targets, half)), once((targets, half)),
            once((chunk, width)), once((width, chunk)),
            once((2, PRE, width)), once((1, width)), once((1, chunk)),
        ],
        out_shape=[
            jax.ShapeDtypeStruct((rows, half), BF),
            jax.ShapeDtypeStruct((targets, half), BF),
            jax.ShapeDtypeStruct((targets, half), BF),
            jax.ShapeDtypeStruct((chunk, width), BF),
            jax.ShapeDtypeStruct((width, chunk), BF),
            jax.ShapeDtypeStruct((2, PRE, width), F32),
            jax.ShapeDtypeStruct((1, width), F32),
            jax.ShapeDtypeStruct((1, chunk), F32),
        ],
        scratch_shapes=[
            vmem((rows, width), BF), vmem((rows, width), BF), vmem((rows, width), BF),
            vmem((2 * PRE_PAD, width), F32),
            vmem((rows, width), BF), vmem((rows, chunk), BF),
            vmem((rows, width), BF), vmem((rows, chunk), BF),
            vmem((2, chunk, width), F32), vmem((2, width, chunk), F32),
            vmem((width, width), BF), vmem((half, width), BF), vmem((half, width), BF),
            vmem((slices, side, width), BF), vmem((slices, side, width), BF),
            vmem((slices, line - 1, part, width), BF), vmem((slices, part, width), BF),
            vmem((width, width), BF),
            vmem((devices - 1, small_rows, small_cols), F32), vmem((small_rows, small_cols), F32),
            vmem((2 * PRE_PAD, width), F32),
            vmem((4, rows, tile), BF), vmem((2, rows, tile), BF),
            vmem((2, targets, half), BF), vmem((2, targets, half), BF),
            dma((4,)), dma((2,)), dma((2, slices)), dma((2, slices, line - 1)),
            dma((2, slices, line - 1)), dma((2, slices)), dma((2, slices, 2)),
            dma((2, devices - 1)), dma((2, devices - 1)), dma((2, 3)),
        ],
        compiler_params=pltpu.CompilerParams(
            vmem_limit_bytes=60 * 2**20, collective_id=0, has_side_effects=True
        ),
        name="finish",
    )(
        qkv, qkv, qkv, att, inv, datt, datt, datt, *w["prefix"], *weights,
        dfirst, dfirst, dfirst, w["qkv"], *flat, *dec_prefix, *ys, dt,
    )


def blank_kernel(*refs):
    pass


def blanks(shapes):
    return pl.pallas_call(
        blank_kernel,
        out_shape=list(shapes),
        out_specs=[pl.BlockSpec(memory_space=pl.ANY)] * len(shapes),
        name="blank",
    )()


def on_section(is_encoder, encoder_work, decoder_work, *operands):
    enc_shapes, _ = jax.eval_shape(encoder_work, *operands)
    dec_shapes, _ = jax.eval_shape(decoder_work, *operands)

    def blank_like(shapes):
        leaves, tree = jax.tree.flatten(shapes)
        if not leaves:
            return shapes
        return jax.tree.unflatten(tree, blanks(leaves))

    def encoder_branch(*a):
        own, shared = encoder_work(*a)
        return own, blank_like(dec_shapes), shared

    def decoder_branch(*a):
        own, shared = decoder_work(*a)
        return blank_like(enc_shapes), own, shared

    return lax.cond(is_encoder, encoder_branch, decoder_branch, *operands)


def to_decoder(block):
    return lax.ppermute(block, "section", [(0, 1)])


def to_encoder(block):
    return lax.ppermute(block, "section", [(1, 0)])


def per_device(
    sources, targets, cotangent, source_lengths, target_lengths,
    attn_qkv, attn_out, ffn_in, ffn_out, norm_gains, prefix_pairs,
    adapt_down, adapt_down_bias, adapt_up, adapt_up_bias,
    cross_query, cross_pairs, cross_out, cross_gain,
):
    is_encoder = lax.axis_index("section") == 0
    prefix = jnp.pad(prefix_pairs[0], ((0, 0), (0, PRE_PAD - PRE), (0, 0)))
    w = dict(
        qkv=attn_qkv[0], out=attn_out[0], ffn_in=ffn_in[0], ffn_out=ffn_out[0],
        gains=norm_gains[0], prefix=(prefix[0], prefix[1]),
        down=adapt_down[0], down_bias=adapt_down_bias,
        up=adapt_up[0], up_bias=adapt_up_bias,
    )
    cross = dict(query=cross_query, pairs=cross_pairs, out=cross_out, gain=cross_gain[None])

    def at_encoder(work, *operands):
        return on_section(is_encoder, lambda *a: (work(*a), ()), lambda *a: ((), ()), *operands)[0]

    def at_decoder(work, *operands):
        return on_section(is_encoder, lambda *a: ((), ()), lambda *a: (work(*a), ()), *operands)[1]

    def at_both(enc_work, dec_work, *operands):
        return on_section(
            is_encoder, lambda *a: (enc_work(*a), ()), lambda *a: (dec_work(*a), ()), *operands
        )[:2]

    def tie(*arrays):
        return lax.optimization_barrier(arrays)

    def encoder_self():
        qkv = product(sources, w["qkv"])
        att, inv, *weights = attend(
            source_lengths, *self_columns(qkv), w["prefix"], enc_segs, False, checked=True
        )
        return qkv, att, inv, weights

    saved, (cq, kept) = at_both(
        encoder_self, lambda: decoder_self(targets, target_lengths, w, cross)
    )
    long_queries = to_encoder(cq[0])
    short_queries = cq[1]
    part = at_encoder(lambda saved: enc_ffn(sources, saved[1], w), saved)
    mem_short = to_decoder(part[0][SRC_LONG:])

    def encoder_cross(mem, long_queries):
        kv = product(mem, cross["pairs"], rows=SRC_LONG)
        return kv, cross_forward(source_lengths, long_queries, kv, 0)

    long_kv, long = at_encoder(encoder_cross, part[0], long_queries)
    mem_short, catt = tie(mem_short, long[0])
    catt_here = to_decoder(catt)

    def decoder_short(mem_short, cq, kept):
        kv = product(mem_short, cross["pairs"])
        forward = cross_forward(source_lengths, cq, kv, 1)
        return kv, forward, dec_ffn(
            target_lengths, kept[4], forward[0], cotangent, w, cross, 1
        )

    short_kv, short, short_ffn = at_decoder(decoder_short, mem_short, short_queries, kept)
    short_y, short_second, short_dcatt, *short_adapter = short_ffn
    catt_here, short_y = tie(catt_here, short_y)
    long_y, long_second, long_dcatt, *long_adapter = at_decoder(
        lambda catt, kept: dec_ffn(target_lengths, kept[4], catt, cotangent, w, cross, 0),
        catt_here, kept,
    )
    short_dcatt, long_dcatt = tie(short_dcatt, long_dcatt)
    dcatt_here = to_encoder(long_dcatt)

    def decoder_short_back(kv, cq, short, dcatt):
        dcq, dck, dcv = cross_backward(cq, kv, short, dcatt, 1)
        return back_product([dck, dcv], cross["pairs"])[0], dcq

    dmem_short, short_cq = at_decoder(decoder_short_back, short_kv, short_queries, short, short_dcatt)
    dcatt_here, dmem_short = tie(dcatt_here, to_encoder(dmem_short))
    long_dcq, dck, dcv = at_encoder(
        lambda queries, kv, long, dcatt: cross_backward(queries, kv, long, dcatt, 0),
        long_queries, long_kv, long, dcatt_here,
    )
    long_cq = to_decoder(long_dcq)

    def encoder_back(dck, dcv, dmem_short, part):
        dmem = back_product([dck, dcv], cross["pairs"])[0]
        return enc_ffn_back([dmem, dmem_short], part, w)

    dfirst, datt, grad, pre = at_encoder(encoder_back, dck, dcv, dmem_short, part)

    def decoder_end(kept, *grads):
        return decoder_self_back(kept, grads[:2], grads[2:], w, cross)

    long_cq, datt = tie(long_cq, datt)
    dt, dec_prefix = at_decoder(
        decoder_end, kept, long_second, short_second, long_cq, short_cq
    )
    source_grad, y, target_grad, up, down, prefix_grad, up_bias, down_bias = finish(
        saved, datt, dfirst, w, [part[4], part[3], grad, pre],
        [long_adapter, short_adapter], dec_prefix, [long_y, short_y], dt,
    )
    return (
        y,
        source_grad,
        target_grad,
        prefix_grad[None],
        down.astype(F32)[None],
        down_bias,
        up.astype(F32)[None],
        up_bias,
    )


def solution(mesh):
    layer2, layer3, rows = P("section", None), P("section", None, None), P("dp", None)
    return jax.shard_map(
        per_device,
        mesh=mesh,
        in_specs=(
            rows, rows, rows, rows, rows,
            layer3, layer3, layer3, layer3, layer3,
            P("section", None, None, None),
            layer3, layer2, layer3, layer2,
            P(), P(), P(), P(),
        ),
        out_specs=(
            P("dp", "section"), P("dp", "section"), P("dp", "section"),
            P("section", None, None, None), layer3, layer2, layer3, layer2,
        ),
        check_vma=False,
    )
```

```python
import functools

import jax
import jax.numpy as jnp
from jax import lax
from jax.experimental import pallas as pl
from jax.experimental.pallas import tpu as pltpu
from jax.sharding import PartitionSpec as P

HD = 64
PRE = 30
PRE_PAD = 32
SRC_LONG = 768
SRC_SHORT = 96
TGT = 256
LANES = 128

BF = jnp.bfloat16
F32 = jnp.float32
norm_eps = 1e-05
big_negative = -1e30
adapter_scale = 4.0
chunk = 512
wide = 1024
ENC_ROWS = (SRC_LONG + SRC_SHORT) // 3
vmem_bytes = 56 * 2**20

phi_poly = (
    0.797869713181688,
    0.036392283539041996,
    -8.782472977701046e-05,
    -3.669384069669515e-05,
    1.4250308145882202e-06,
)


def nn(left, right):
    return lax.dot_general(left, right, (((1,), (0,)), ((), ())), preferred_element_type=F32)


def nt(left, right):
    return lax.dot_general(left, right, (((1,), (1,)), ((), ())), preferred_element_type=F32)


def tn(left, right):
    return lax.dot_general(left, right, (((0,), (0,)), ((), ())), preferred_element_type=F32)


def gelu_pair(values):
    square = values * values
    poly = phi_poly[4]
    for coefficient in phi_poly[3::-1]:
        poly = poly * square + coefficient
    half = 0.5 * jnp.tanh(values * poly) + 0.5
    density = jnp.exp(square * -0.5) * 0.3989422804014327
    return values * half, half + values * density


def row_tiles(rows, most=864):
    count = -(-rows // most)
    size = rows // count
    return [(i * size, size) for i in range(count)]


def norm_rows(values):
    centered = values - jnp.mean(values, axis=-1, keepdims=True)
    scale = lax.rsqrt(jnp.mean(centered * centered, axis=-1, keepdims=True) + norm_eps)
    return centered * scale, scale


def norm_rows_back(hat, scale, grad_hat):
    mean_grad = jnp.mean(grad_hat, axis=-1, keepdims=True)
    mean_dot = jnp.mean(grad_hat * hat, axis=-1, keepdims=True)
    return scale * (grad_hat - mean_grad - hat * mean_dot)


def params(limit=vmem_bytes):
    return pltpu.CompilerParams(vmem_limit_bytes=limit)


def whole(shape):
    return pl.BlockSpec(shape, lambda *g: (0,) * len(shape))


def single(shape):
    return pl.BlockSpec(shape, lambda *g: (0,) * len(shape), pipeline_mode=pl.Buffered(1))


def product_kernel(x_ref, w_ref, o_ref):
    o_ref[...] = nn(x_ref[...], w_ref[...]).astype(BF)


def product(x, w, tile=1024, rows=None):
    depth = x.shape[1]
    rows = rows or x.shape[0]
    width = w.shape[1]
    return pl.pallas_call(
        product_kernel,
        grid=(width // tile,),
        in_specs=[whole((rows, depth)), pl.BlockSpec((depth, tile), lambda i: (0, i))],
        out_specs=pl.BlockSpec((rows, tile), lambda i: (0, i)),
        out_shape=jax.ShapeDtypeStruct((rows, width), BF),
        compiler_params=params(),
        name="product",
    )(x, w)


def back_product_kernel(*refs, parts, residual, cuts):
    grads = refs[:parts]
    w_ref = refs[parts]
    outs = refs[-len(cuts) :]
    total = None
    width = grads[0].shape[1]
    for i, grad in enumerate(grads):
        term = nt(grad[...], w_ref[:, i * width : (i + 1) * width])
        total = term if total is None else total + term
    if residual:
        total = total + refs[parts + 1][...]
    for (start, size), o_ref in zip(cuts, outs):
        o_ref[...] = total[start : start + size].astype(BF)


def back_product(grads, w, residual=None, tile=512, cuts=None):
    rows, width = grads[0].shape
    depth = w.shape[0]
    parts = len(grads)
    cuts = cuts or ((0, rows),)
    specs = [whole((rows, width))] * parts + [
        pl.BlockSpec((tile, parts * width), lambda i: (i, 0))
    ]
    args = list(grads) + [w]
    if residual is not None:
        specs.append(pl.BlockSpec((rows, tile), lambda i: (0, i)))
        args.append(residual)
    return pl.pallas_call(
        functools.partial(
            back_product_kernel, parts=parts, residual=residual is not None, cuts=cuts
        ),
        grid=(depth // tile,),
        in_specs=specs,
        out_specs=[pl.BlockSpec((size, tile), lambda i: (0, i)) for _, size in cuts],
        out_shape=[jax.ShapeDtypeStruct((size, depth), BF) for _, size in cuts],
        compiler_params=params(),
        name="back_product",
    )(*args)


def head_lanes(head):
    lane = lax.broadcasted_iota(jnp.int32, (1, LANES), 1)
    own = (lane < HD) if head == 0 else (lane >= HD)
    first = HD if head == 0 else 0
    return own, lane == first, lane == first + 1


def bf(value):
    return jnp.asarray(value, BF)


def rows_of(refs, start, count):
    parts = []
    for ref in refs:
        size = ref.shape[0]
        low, high = max(start, 0), min(start + count, size)
        if low < high:
            parts.append(ref[low:high])
        start -= size
    return parts


def stacked(refs, prefix_ref, start, count):
    parts = rows_of(refs, start, count)
    if prefix_ref is not None:
        parts.append(prefix_ref[...])
    return parts[0] if len(parts) == 1 else jnp.concatenate(parts, 0)


def attend_pair(*refs, segs, prefix, causal, pieces, which, checked):
    len_ref, q_ref = refs[:2]
    k_refs, v_refs = refs[2 : 2 + pieces], refs[2 + pieces : 2 + 2 * pieces]
    at = 2 + 2 * pieces
    pk_ref = pv_ref = None
    if prefix:
        pk_ref, pv_ref = refs[at : at + 2]
        at += 2
    o_ref, inv_ref = refs[at : at + 2]
    p_refs = refs[at + 2 :]

    def work(peaked):
        for seg, (q0, nq, k0, nk) in enumerate(segs):
            keys = stacked(k_refs, pk_ref, k0, nk)
            values = stacked(v_refs, pv_ref, k0, nk)
            count = keys.shape[0]
            row = lax.broadcasted_iota(jnp.int32, (count, 1), 0)
            seen = row < jnp.minimum(len_ref[0, which + seg], nk)
            if prefix:
                seen = seen | ((row >= nk) & (row < nk + PRE))
            queries = q_ref[q0 : q0 + nq] * bf(HD**-0.5)
            out = inv = None
            across = nq >= 4 * LANES
            outs, invs = [], []
            if across:
                turned = values.T
                ones = jnp.ones((16, count), BF)
            for head in range(2):
                own, first, _ = head_lanes(head)
                k_own = jnp.where(own, keys, jnp.where(first & ~seen, bf(big_negative), bf(0)))
                q_own = jnp.where(own, queries, jnp.where(first, bf(1), bf(0)))
                scores = nt(k_own, q_own)
                if causal:
                    key_at = lax.broadcasted_iota(jnp.int32, scores.shape, 0)
                    query_at = lax.broadcasted_iota(jnp.int32, scores.shape, 1)
                    allowed = (key_at <= query_at) | (key_at >= nk)
                    scores = jnp.where(allowed, scores, big_negative)
                if peaked:
                    scores = scores - jnp.max(scores, axis=0, keepdims=True)
                weights = jnp.exp(scores).astype(BF)
                p_refs[seg][head] = weights
                if across:
                    rows = jnp.concatenate([turned[head * HD : (head + 1) * HD], ones], 0)
                    mixed = nn(rows, weights)
                    inverse = 1.0 / mixed[HD : HD + 1]
                    outs.append(mixed[:HD] * inverse)
                    invs.append(jnp.broadcast_to(inverse, (HD, nq)))
                    continue
                mixed = tn(weights, jnp.where(own, values, bf(1)))
                inverse = 1.0 / pltpu.roll(mixed, HD, 1)
                mixed = mixed * inverse
                out = mixed if out is None else jnp.where(own, mixed, out)
                inv = inverse if inv is None else jnp.where(own, inverse, inv)
            if across:
                out = jnp.concatenate(outs, 0).T
                inv = jnp.concatenate(invs, 0).T
            o_ref[q0 : q0 + nq] = out.astype(BF)
            inv_ref[q0 : q0 + nq] = inv

    if not checked:
        work(True)
        return

    limit = 50.0**2
    head_row = lax.broadcasted_iota(jnp.int32, (LANES, LANES), 0) // HD
    head_col = lax.broadcasted_iota(jnp.int32, (LANES, LANES), 1) // HD
    same_head = jnp.where(head_row == head_col, 1.0, 0.0).astype(BF)

    def largest(array):
        square = (array.astype(F32) * array.astype(F32)).astype(BF)
        return jnp.max(nn(square, same_head), axis=0, keepdims=True)

    key_peak = largest(k_refs[0][...])
    for ref in k_refs[1:]:
        key_peak = jnp.maximum(key_peak, largest(ref[...]))
    if prefix:
        key_peak = jnp.maximum(key_peak, largest(pk_ref[...]))
    small = jnp.max(largest(q_ref[...]) * key_peak) * (1.0 / HD) <= limit

    @pl.when(small)
    def _():
        work(False)

    @pl.when(jnp.logical_not(small))
    def _():
        work(True)


def lane_views(refs, group, j):
    views = []
    for ref in refs:
        if len(ref.shape) == 2:
            views.append(ref.at[:, j * LANES : (j + 1) * LANES])
        else:
            views.append(ref.at[2 * j : 2 * j + 2])
    return views


def attend_kernel(len_ref, *refs, group, **kw):
    for j in range(group):
        attend_pair(len_ref, *lane_views(refs, group, j), **kw)


def column_spec(rows, offset, row_block=0, group=1):
    return pl.BlockSpec((rows, group * LANES), lambda h: (row_block, h + offset // group))


def attend(lengths, q, keys, values, prefixes, segs, causal, which=0, group=1, checked=False):
    pairs = 8
    q_rows = q[1]
    prefix = prefixes is not None
    extra = PRE_PAD if prefix else 0
    specs = [pl.BlockSpec(memory_space=pltpu.SMEM)]
    args = [lengths]
    for array, rows, block, offset in [q, *keys, *values]:
        specs.append(column_spec(rows, offset, block, group))
        args.append(array)
    if prefix:
        specs += [column_spec(PRE_PAD, 0, 0, group)] * 2
        args += list(prefixes)
    weight_shapes = [(2 * pairs, nk + extra, nq) for _, nq, _, nk in segs]
    return pl.pallas_call(
        functools.partial(
            attend_kernel, group=group, segs=segs, prefix=prefix, causal=causal, pieces=len(keys), which=which,
            checked=checked,
        ),
        grid=(pairs // group,),
        in_specs=specs,
        out_specs=[column_spec(q_rows, 0, 0, group)] * 2
        + [pl.BlockSpec((2 * group,) + s[1:], lambda h: (h, 0, 0)) for s in weight_shapes],
        out_shape=[
            jax.ShapeDtypeStruct((q_rows, pairs * LANES), BF),
            jax.ShapeDtypeStruct((q_rows, pairs * LANES), F32),
        ]
        + [jax.ShapeDtypeStruct(s, BF) for s in weight_shapes],
        compiler_params=params(),
        name="attend",
    )(*args)


def attend_back_pair(
    q_ref, k_refs, v_refs, o_ref, inv_ref, g_refs, pk_ref, pv_ref, p_refs, dq_ref, dk_ref, dv_ref, segs
):
    prefix_totals = [None, None]
    scale = HD**-0.5
    for seg, (q0, nq, k0, nk) in enumerate(segs):
        keys = stacked(k_refs, pk_ref, k0, nk)
        values = stacked(v_refs, pv_ref, k0, nk)
        queries = q_ref[q0 : q0 + nq]
        grads = stacked(g_refs, None, q0, nq).astype(F32) * inv_ref[q0 : q0 + nq]
        grads_low = grads.astype(BF)
        dots = grads * o_ref[q0 : q0 + nq].astype(F32)
        dq = dk = dv = None
        across = nq >= LANES and keys.shape[0] >= 4 * LANES
        turned_grads = []
        if across:
            turned = keys.T
        for head in range(2):
            own, first, second = head_lanes(head)
            row_dot = -jnp.sum(jnp.where(own, dots, 0.0), axis=1, keepdims=True)
            high = row_dot.astype(BF)
            rest = (row_dot - high.astype(F32)).astype(BF)
            g_own = jnp.where(
                own, grads_low, jnp.where(first, high, jnp.where(second, rest, bf(0)))
            )
            v_own = jnp.where(own, values, jnp.where(first | second, bf(1), bf(0)))
            weights = p_refs[seg][head]
            score_grad = (weights.astype(F32) * nt(v_own, g_own)).astype(BF)
            dv_head = nn(weights, grads_low)
            dk_head = nn(score_grad, queries)
            dq_head = None if across else tn(score_grad, keys)
            if across:
                turned_grads.append(nn(turned[head * HD : (head + 1) * HD], score_grad))
            if not across:
                dq = dq_head if dq is None else jnp.where(own, dq_head, dq)
            dk = dk_head if dk is None else jnp.where(own, dk_head, dk)
            dv = dv_head if dv is None else jnp.where(own, dv_head, dv)
        if across:
            dq = jnp.concatenate(turned_grads, 0).T
        dk = dk * scale
        dq_ref[q0 : q0 + nq] = (dq * scale).astype(BF)
        at = k0 - segs[0][2]
        dk_ref[at : at + nk] = dk[:nk].astype(BF)
        dv_ref[at : at + nk] = dv[:nk].astype(BF)
        if pk_ref is not None:
            for i, grad in enumerate((dk, dv)):
                part = grad[nk:]
                prefix_totals[i] = part if seg == 0 else prefix_totals[i] + part
    return prefix_totals


def attend_back_kernel(*refs, group, **kw):
    for j in range(group):
        attend_back_views(*lane_views(refs, group, j), **kw)


def attend_back_views(*refs, segs, prefix, pieces):
    q_ref, o_ref, inv_ref, g_ref = refs[:4]
    k_refs, v_refs = refs[4 : 4 + pieces], refs[4 + pieces : 4 + 2 * pieces]
    at = 4 + 2 * pieces
    pk_ref = pv_ref = None
    if prefix:
        pk_ref, pv_ref = refs[at : at + 2]
        at += 2
    outs = refs[at + len(segs) :]
    totals = attend_back_pair(
        q_ref, k_refs, v_refs, o_ref, inv_ref, [g_ref], pk_ref, pv_ref,
        refs[at : at + len(segs)], *outs[:3], segs,
    )
    if prefix:
        outs[3][...] = totals[0]
        outs[4][...] = totals[1]


def attend_back(q, keys, values, prefixes, attended, inverse, grad, weights, segs, group=2):
    pairs = 8
    q_rows = q[1]
    k_rows = sum(nk for _, _, _, nk in segs)
    prefix = prefixes is not None
    specs, args = [], []
    own = [(a, q_rows, 0, 0) for a in (attended, inverse, grad)]
    for array, rows, block, offset in [q, *own, *keys, *values]:
        specs.append(column_spec(rows, offset, block, group))
        args.append(array)
    if prefix:
        specs += [column_spec(PRE_PAD, 0, 0, group)] * 2
        args += list(prefixes)
    specs += [pl.BlockSpec((2 * group,) + w.shape[1:], lambda h: (h, 0, 0)) for w in weights]
    args += list(weights)
    out_specs = [column_spec(n, 0, 0, group) for n in (q_rows, k_rows, k_rows)]
    out_shape = [
        jax.ShapeDtypeStruct((q_rows, pairs * LANES), BF),
        jax.ShapeDtypeStruct((k_rows, pairs * LANES), BF),
        jax.ShapeDtypeStruct((k_rows, pairs * LANES), BF),
    ]
    if prefix:
        out_specs += [column_spec(PRE_PAD, 0, 0, group)] * 2
        out_shape += [jax.ShapeDtypeStruct((PRE_PAD, pairs * LANES), F32)] * 2
    return pl.pallas_call(
        functools.partial(
            attend_back_kernel, group=group, segs=segs, prefix=prefix, pieces=len(keys)
        ),
        grid=(pairs // group,),
        in_specs=specs,
        out_specs=out_specs,
        out_shape=out_shape,
        compiler_params=params(),
        name="attend_back",
    )(*args)


class Weights:
    def __init__(self, sources, targets, sems):
        self.sources, self.targets, self.sems = sources, targets, sems

    def copy(self, name, part=None):
        source, target = self.sources[name], self.targets[name]
        first = list(self.sources).index(name)
        sem = self.sems.at[first, 0 if part is None else part]
        if part is not None:
            cut = pl.ds(pl.multiple_of(part * wide, wide), wide)
            index = (slice(None), cut) if name == "in" else (cut, slice(None))
            source, target = source.at[index], target.at[index]
        return pltpu.make_async_copy(source, target, sem)

    def wait(self, name, part=None):
        self.copy(name, part).wait()

    def part(self, name, part):
        cut = pl.ds(pl.multiple_of(part * wide, wide), wide)
        index = (slice(None), cut) if name == "in" else (cut, slice(None))
        return self.targets[name].at[index]


def weight_scratch(arrays, parts):
    return [pltpu.VMEM(a.shape, BF) for a in arrays] + [
        pltpu.SemaphoreType.DMA((len(arrays), parts))
    ]


def ffn_step(low_ref, acc_ref, in_ref, out_ref, slope_ref, act_ref, bias_ref, scale):
    for start, size in row_tiles(low_ref.shape[0]):
        rows = slice(start, start + size)
        hidden = nn(low_ref[rows], in_ref[...])
        if bias_ref is not None:
            hidden = hidden + bias_ref[...]
        active, slope = gelu_pair(hidden)
        slope_ref[rows] = slope.astype(BF)
        active = active.astype(BF)
        if act_ref is not None:
            act_ref[rows] = active
        term = nn(active, out_ref[...])
        acc_ref[rows] += term if scale is None else scale * term


def enc_ffn_kernel(
    x_ref, att_ref, gain_ref, downb_ref, upb_ref, wo_hbm, in_hbm, out_hbm, down_hbm, up_hbm,
    mem_ref, slope_ref, pre_slope_ref, act_ref, low_ref, scales_ref,
    acc_ref, wo_ref, in_ref, out_ref, down_ref, up_ref, sems,
):
    weights = Weights(
        {"wo": wo_hbm, "in": in_hbm, "out": out_hbm, "down": down_hbm, "up": up_hbm},
        {"wo": wo_ref, "in": in_ref, "out": out_ref, "down": down_ref, "up": up_ref},
        sems,
    )

    weights.copy("wo").start()
    for part in range(in_ref.shape[1] // wide):
        weights.copy("in", part).start()
        weights.copy("out", part).start()
    weights.copy("down").start()
    weights.copy("up").start()
    weights.wait("wo")
    for start, size in row_tiles(x_ref.shape[0]):
        rows = slice(start, start + size)
        first = x_ref[rows].astype(F32) + nn(att_ref[rows], wo_ref[...])
        hat, scale = norm_rows(first)
        normed = hat * gain_ref[0:1]
        acc_ref[rows] = normed
        low_ref[rows] = normed.astype(BF)
        scales_ref[rows, 0:1] = scale

    def one_part(part, carry):
        weights.wait("in", part)
        weights.wait("out", part)
        cols = pl.ds(pl.multiple_of(part * wide, wide), wide)
        ffn_step(
            low_ref, acc_ref, in_ref.at[:, cols], out_ref.at[cols], slope_ref.at[:, cols],
            None, None, None,
        )
        return carry

    lax.fori_loop(0, in_ref.shape[1] // wide, one_part, 0)

    weights.wait("down")
    weights.wait("up")
    ffn_step(low_ref, acc_ref, down_ref, up_ref, pre_slope_ref, act_ref, downb_ref, adapter_scale)
    for start, size in row_tiles(x_ref.shape[0]):
        rows = slice(start, start + size)
        hat, scale = norm_rows(acc_ref[rows] + adapter_scale * upb_ref[...])
        mem_ref[rows] = (hat * gain_ref[1:2]).astype(BF)
        scales_ref[rows, 1:2] = scale


def enc_ffn(x, att, w):
    rows, width = x.shape
    hidden = w["ffn_in"].shape[1]
    steps = hidden // wide
    weights = [w["out"], w["ffn_in"], w["ffn_out"], w["down"], w["up"]]
    return pl.pallas_call(
        enc_ffn_kernel,
        grid=(1,),
        in_specs=[
            single((rows, width)),
            single((rows, width)),
            single((2, width)),
            single((1, chunk)),
            single((1, width)),
        ]
        + [pl.BlockSpec(memory_space=pl.ANY)] * len(weights),
        out_specs=[
            single((rows, width)),
            single((rows, hidden)),
            single((rows, chunk)),
            single((rows, chunk)),
            single((rows, width)),
            single((rows, LANES)),
        ],
        out_shape=[
            jax.ShapeDtypeStruct((rows, width), BF),
            jax.ShapeDtypeStruct((rows, hidden), BF),
            jax.ShapeDtypeStruct((rows, chunk), BF),
            jax.ShapeDtypeStruct((rows, chunk), BF),
            jax.ShapeDtypeStruct((rows, width), BF),
            jax.ShapeDtypeStruct((rows, LANES), F32),
        ],
        scratch_shapes=[pltpu.VMEM((rows, width), F32)] + weight_scratch(weights, steps),
        compiler_params=params(),
        name="enc_ffn",
    )(x, att, w["gains"], w["down_bias"], w["up_bias"], *weights)


def ffn_back_step(grad_ref, acc_ref, in_ref, out_ref, slope_ref):
    for start, size in row_tiles(grad_ref.shape[0]):
        rows = slice(start, start + size)
        pre = (nt(grad_ref[rows], out_ref[...]) * slope_ref[rows].astype(F32)).astype(BF)
        acc_ref[rows] += nt(pre, in_ref[...])


def adapter_back(grad_ref, acc_ref, low_ref, act_ref, slope_ref, down_ref, up_ref, outs, pre_ref):
    ddown_ref, ddownb_ref, dup_ref, dupb_ref = outs
    total = None
    for start, size in row_tiles(grad_ref.shape[0]):
        rows = slice(start, start + size)
        back = adapter_scale * nt(grad_ref[rows], up_ref[...])
        pre = (back * slope_ref[rows].astype(F32)).astype(BF)
        pre_ref[rows] = pre
        sums = jnp.sum(pre.astype(F32), axis=0, keepdims=True)
        total = sums if total is None else total + sums
        acc_ref[rows] += nt(pre, down_ref[...])
    ddownb_ref[...] = total
    ddown_ref[...] = tn(low_ref[...], pre_ref[...])
    dup_ref[...] = adapter_scale * tn(act_ref[...], grad_ref[...])
    dupb_ref[...] = adapter_scale * jnp.sum(grad_ref[...].astype(F32), axis=0, keepdims=True)


def enc_ffn_back_kernel(*refs, pieces):
    enc_ffn_back_body(refs[:pieces], *refs[pieces:])


def enc_ffn_back_body(
    dmem_refs, mem_ref, low_ref, scales_ref, gain_ref, slope_ref, pre_slope_ref,
    up_hbm, down_hbm, in_hbm, out_hbm, wo_hbm,
    dfirst_ref, datt_ref, grad_ref, pre_ref,
    acc_ref, up_ref, down_ref, in_ref, out_ref, wo_ref, sems,
):
    weights = Weights(
        {"up": up_hbm, "down": down_hbm, "in": in_hbm, "out": out_hbm, "wo": wo_hbm},
        {"up": up_ref, "down": down_ref, "in": in_ref, "out": out_ref, "wo": wo_ref},
        sems,
    )

    weights.copy("up").start()
    weights.copy("down").start()
    for part in range(in_ref.shape[1] // wide):
        weights.copy("out", part).start()
        weights.copy("in", part).start()
    weights.copy("wo").start()
    weights.wait("up")
    weights.wait("down")
    for start, size in row_tiles(mem_ref.shape[0]):
        rows = slice(start, start + size)
        gain = gain_ref[1:2]
        hat = mem_ref[rows].astype(F32) / gain
        dmem = stacked(dmem_refs, None, start, size).astype(F32)
        grad = norm_rows_back(hat, scales_ref[rows, 1:2], dmem * gain)
        low = grad.astype(BF)
        grad_ref[rows] = low
        back = adapter_scale * nt(low, up_ref[...])
        pre = (back * pre_slope_ref[rows].astype(F32)).astype(BF)
        pre_ref[rows] = pre
        acc_ref[rows] = grad + nt(pre, down_ref[...])

    def one_part(part, carry):
        weights.wait("out", part)
        weights.wait("in", part)
        cols = pl.ds(pl.multiple_of(part * wide, wide), wide)
        ffn_back_step(
            grad_ref, acc_ref, in_ref.at[:, cols], out_ref.at[cols], slope_ref.at[:, cols]
        )
        return carry

    lax.fori_loop(0, in_ref.shape[1] // wide, one_part, 0)

    weights.wait("wo")
    for start, size in row_tiles(mem_ref.shape[0]):
        rows = slice(start, start + size)
        gain = gain_ref[0:1]
        hat = low_ref[rows].astype(F32) / gain
        grad = norm_rows_back(hat, scales_ref[rows, 0:1], acc_ref[rows] * gain)
        dfirst_ref[rows] = grad
        datt_ref[rows] = nt(grad.astype(BF), wo_ref[...]).astype(BF)


def enc_ffn_back(dmems, saved, w):
    mem, slope, pre_slope, act, low, scales = saved
    rows, width = mem.shape
    hidden = w["ffn_in"].shape[1]
    steps = hidden // wide
    weights = [w["up"], w["down"], w["ffn_in"], w["ffn_out"], w["out"]]
    return pl.pallas_call(
        functools.partial(enc_ffn_back_kernel, pieces=len(dmems)),
        grid=(1,),
        in_specs=[single(d.shape) for d in dmems]
        + [
            single((rows, width)),
            single((rows, width)),
            single((rows, LANES)),
            single((2, width)),
            single((rows, hidden)),
            single((rows, chunk)),
        ]
        + [pl.BlockSpec(memory_space=pl.ANY)] * len(weights),
        out_specs=[
            single((rows, width)),
            single((rows, width)),
            single((rows, width)),
            single((rows, chunk)),
        ],
        out_shape=[
            jax.ShapeDtypeStruct((rows, width), F32),
            jax.ShapeDtypeStruct((rows, width), BF),
            jax.ShapeDtypeStruct((rows, width), BF),
            jax.ShapeDtypeStruct((rows, chunk), BF),
        ],
        scratch_shapes=[pltpu.VMEM((rows, width), F32)] + weight_scratch(weights, steps),
        compiler_params=params(),
        name="enc_ffn_back",
    )(*dmems, mem, low, scales, w["gains"], slope, pre_slope, *weights)


def dec_mid_kernel(x_ref, att_ref, wo_ref, gain_ref, wq_ref, n_ref, scale_ref, *cq_refs):
    for (start, size), cq_ref in zip(row_tiles(x_ref.shape[0], TGT), cq_refs):
        rows = slice(start, start + size)
        first = x_ref[rows].astype(F32) + nn(att_ref[rows], wo_ref[...])
        hat, scale = norm_rows(first)
        normed = hat * gain_ref[0:1]
        n_ref[rows] = normed
        scale_ref[rows, 0:1] = scale
        cq_ref[...] = nn(normed.astype(BF), wq_ref[...]).astype(BF)


def dec_mid(x, att, w, cross):
    rows, width = x.shape
    return pl.pallas_call(
        dec_mid_kernel,
        out_shape=[
            jax.ShapeDtypeStruct((rows, width), F32),
            jax.ShapeDtypeStruct((rows, LANES), F32),
        ]
        + [jax.ShapeDtypeStruct((TGT, width), BF)] * (rows // TGT),
        compiler_params=params(),
        name="dec_mid",
    )(x, att, w["out"], w["gains"], cross["query"])


def dec_ffn_kernel(
    len_ref, n_ref, catt_ref, cot_ref, cgain_ref, gain_ref, downb_ref, upb_ref,
    wco_hbm, in_hbm, out_hbm, down_hbm, up_hbm,
    y_ref, dsecond_ref, dcatt_ref, ddown_ref, ddownb_ref, dup_ref, dupb_ref,
    acc_ref, low_ref, grad_ref, slope_ref, pre_slope_ref, act_ref, pre_ref, scale_ref,
    wco_ref, in_ref, out_ref, down_ref, up_ref, sems,
    *, steps, which,
):
    weights = Weights(
        {"wco": wco_hbm, "in": in_hbm, "out": out_hbm, "down": down_hbm, "up": up_hbm},
        {"wco": wco_ref, "in": in_ref, "out": out_ref, "down": down_ref, "up": up_ref},
        sems,
    )

    weights.copy("wco").start()
    for part in range(steps):
        weights.copy("in", part).start()
        weights.copy("out", part).start()
    weights.copy("down").start()
    weights.copy("up").start()
    weights.wait("wco")
    second = n_ref[...] + nn(catt_ref[...], wco_ref[...])
    hat, scale = norm_rows(second)
    middle = hat * cgain_ref[...]
    acc_ref[...] = middle
    low_ref[...] = middle.astype(BF)
    scale_ref[:, 0:1] = scale

    def forward(part, carry):
        weights.wait("in", part)
        weights.wait("out", part)
        ffn_step(
            low_ref, acc_ref, weights.part("in", part), weights.part("out", part),
            slope_ref.at[part], None, None, None,
        )
        return carry

    lax.fori_loop(0, steps, forward, 0)

    weights.wait("down")
    weights.wait("up")
    ffn_step(
        low_ref, acc_ref, down_ref, up_ref, pre_slope_ref, act_ref, downb_ref, adapter_scale
    )
    gain = gain_ref[1:2]
    hat, scale = norm_rows(acc_ref[...] + adapter_scale * upb_ref[...])
    row = lax.broadcasted_iota(jnp.int32, (low_ref.shape[0], 1), 0)
    valid = row < len_ref[0, which]
    y_ref[...] = jnp.where(valid, hat * gain, 0.0).astype(BF)
    cot = jnp.where(valid, cot_ref[...].astype(F32), 0.0)
    grad = norm_rows_back(hat, scale, cot * gain)
    acc_ref[...] = grad
    grad_ref[...] = grad.astype(BF)
    adapter_back(
        grad_ref, acc_ref, low_ref, act_ref, pre_slope_ref, down_ref, up_ref,
        (ddown_ref, ddownb_ref, dup_ref, dupb_ref), pre_ref,
    )

    def backward(part, carry):
        ffn_back_step(
            grad_ref, acc_ref, weights.part("in", part), weights.part("out", part),
            slope_ref.at[part],
        )
        return carry

    lax.fori_loop(0, steps, backward, 0)

    gain = cgain_ref[...]
    hat = low_ref[...].astype(F32) / gain
    grad = norm_rows_back(hat, scale_ref[:, 0:1], acc_ref[...] * gain)
    dsecond_ref[...] = grad
    dcatt_ref[...] = nt(grad.astype(BF), wco_ref[...]).astype(BF)


def dec_ffn(lengths, n, catt, cot, w, cross, which):
    rows, width = catt.shape
    hidden = w["ffn_in"].shape[1]
    steps = hidden // wide
    weights = [cross["out"], w["ffn_in"], w["ffn_out"], w["down"], w["up"]]
    return pl.pallas_call(
        functools.partial(dec_ffn_kernel, steps=steps, which=which),
        grid=(1,),
        in_specs=[
            pl.BlockSpec(memory_space=pltpu.SMEM),
            pl.BlockSpec((rows, width), lambda i: (which, 0)),
            whole((rows, width)),
            pl.BlockSpec((rows, width), lambda i: (which, 0)),
            whole((1, width)),
            whole((2, width)),
            whole((1, chunk)),
            whole((1, width)),
        ]
        + [pl.BlockSpec(memory_space=pl.ANY)] * len(weights),
        out_specs=[
            whole((rows, width)),
            whole((rows, width)),
            whole((rows, width)),
            whole((width, chunk)),
            whole((1, chunk)),
            whole((chunk, width)),
            whole((1, width)),
        ],
        out_shape=[
            jax.ShapeDtypeStruct((rows, width), BF),
            jax.ShapeDtypeStruct((rows, width), F32),
            jax.ShapeDtypeStruct((rows, width), BF),
            jax.ShapeDtypeStruct((width, chunk), F32),
            jax.ShapeDtypeStruct((1, chunk), F32),
            jax.ShapeDtypeStruct((chunk, width), F32),
            jax.ShapeDtypeStruct((1, width), F32),
        ],
        scratch_shapes=[
            pltpu.VMEM((rows, width), F32),
            pltpu.VMEM((rows, width), BF),
            pltpu.VMEM((rows, width), BF),
            pltpu.VMEM((steps, rows, wide), BF),
            pltpu.VMEM((rows, chunk), BF),
            pltpu.VMEM((rows, chunk), BF),
            pltpu.VMEM((rows, chunk), BF),
            pltpu.VMEM((rows, LANES), F32),
        ]
        + weight_scratch(weights, steps),
        compiler_params=params(),
        name="dec_ffn",
    )(
        lengths, n, catt, cot, cross["gain"], w["gains"], w["down_bias"], w["up_bias"], *weights
    )


def dec_mid_back_kernel(
    dsecond0_ref, dsecond1_ref, dcq0_ref, dcq1_ref, wq_ref, n_ref, scale_ref, gain_ref, wo_ref,
    dfirst_ref, datt_ref,
):
    for pair, (dsecond_ref, dcq_ref) in enumerate(
        ((dsecond0_ref, dcq0_ref), (dsecond1_ref, dcq1_ref))
    ):
        rows = slice(pair * TGT, (pair + 1) * TGT)
        gain = gain_ref[0:1]
        total = dsecond_ref[...] + nt(dcq_ref[...], wq_ref[...])
        grad = norm_rows_back(n_ref[rows] / gain, scale_ref[rows, 0:1], total * gain)
        dfirst_ref[rows] = grad
        datt_ref[rows] = nt(grad.astype(BF), wo_ref[...]).astype(BF)


def dec_mid_back(dseconds, dcqs, n, scale, w, cross):
    rows, width = n.shape
    return pl.pallas_call(
        dec_mid_back_kernel,
        out_shape=[
            jax.ShapeDtypeStruct((rows, width), F32),
            jax.ShapeDtypeStruct((rows, width), BF),
        ],
        compiler_params=params(),
        name="dec_mid_back",
    )(*dseconds, *dcqs, cross["query"], n, scale, w["gains"], w["out"])


enc_segs = ((0, SRC_LONG, 0, SRC_LONG), (SRC_LONG, SRC_SHORT, SRC_LONG, SRC_SHORT))
dec_segs = ((0, TGT, 0, TGT), (TGT, TGT, TGT, TGT))
cross_segs = (((0, TGT, 0, SRC_LONG),), ((0, TGT, 0, SRC_SHORT),))


def self_columns(qkv):
    rows = qkv.shape[0]
    return (qkv, rows, 0, 0), [(qkv, rows, 0, 8)], [(qkv, rows, 0, 16)]


def cross_columns(cq, kv, which):
    keys = (SRC_LONG, SRC_SHORT)[which]
    return (cq, TGT, 0, 0), [(kv, keys, 0, 0)], [(kv, keys, 0, 8)]


def decoder_self(t, lengths, w, cross):
    qkv = product(t, w["qkv"])
    att, inv, *weights = attend(lengths, *self_columns(qkv), w["prefix"], dec_segs, True, group=2)
    n, scale, *cq = dec_mid(t, att, w, cross)
    return cq, (qkv, att, inv, weights, n, scale)


def cross_forward(lengths, cq, kv, which):
    return attend(
        lengths, *cross_columns(cq, kv, which), None, cross_segs[which], False, which, group=2
    )


def cross_backward(cq, kv, forward, dcatt, which):
    catt, inv, *weights = forward
    return attend_back(
        *cross_columns(cq, kv, which), None, catt, inv, dcatt, weights, cross_segs[which]
    )


def decoder_self_back(kept, dseconds, dcqs, w, cross):
    qkv, att, inv, weights, n, scale = kept
    dfirst, datt = dec_mid_back(dseconds, dcqs, n, scale, w, cross)
    dq, dk, dv, *dprefix = attend_back(
        *self_columns(qkv), w["prefix"], att, inv, datt, weights, dec_segs, group=1
    )
    return back_product([dq, dk, dv], w["qkv"], dfirst)[0], dprefix


def small_shape(devices):
    return 8, 8 * (2 * chunk) // devices


def finish_kernel(
    q_ref, k_ref, v_ref, o_ref, inv_ref, g0_ref, g1_ref, g2_ref, pk_ref, pv_ref, pl_ref, ps_ref,
    dfirst0_ref, dfirst1_ref, dfirst2_ref, wqkv_ref,
    low_all, act_all, grad_all, pre_all,
    long_down, long_downb, long_up, long_upb,
    short_down, short_downb, short_up, short_upb, dpk_ref, dpv_ref,
    y0_ref, y1_ref, dt_ref,
    source_ref, y_ref, target_ref, o_up_ref, o_down_ref, o_prefix_ref, o_upb_ref, o_downb_ref,
    dq, dk, dv, small, lows_all, acts_all, grads_all, pres_all, ups, downs, mine, theirs, half_sum, across_y, y_sum, landed, total, result,
    small_landed, small_total, small_result, dx, dx_landed, lows, lows_landed,
    load_sems, pair_sems, y_sems, z_sems, gather_sems, share_y_sems, back_sems,
    small_sems, share_sems, cross_sems,
    *, devices,
):
    step = pl.program_id(0)
    pairs = 8
    section = lax.axis_index("section")
    is_encoder = section == 0
    chips = devices // 2
    line = chips // 2
    slices = 16 // line
    rows = 2 * chunk
    half = rows // 2
    size = half // slices
    side = size // 2
    part = side // line
    place = lax.axis_index("dp")
    core, chip = lax.rem(place, 2), place // 2
    bit, at_line = lax.rem(chip, 2), chip // 2
    partner = place + 1 - 2 * core
    beside = place + 2 - 4 * bit
    small_rows, small_cols = small_shape(devices)
    tile = 256
    width = 2 * chunk
    scale = 1.0 / devices

    def aligned(value, unit=16):
        return pl.multiple_of(value, unit)

    def along(distance):
        return (lax.rem(at_line + distance, line) * 2 + bit) * 2 + core

    def remote(source, target, send_sem, recv_sem, other):
        return pltpu.make_async_remote_copy(
            src_ref=source, dst_ref=target, send_sem=send_sem, recv_sem=recv_sem,
            device_id=other, device_id_type=pl.DeviceIdType.MESH,
        )

    def in_group(other):
        return {"dp": other}

    across = {"section": 1 - section}
    kept = aligned(core * half)
    given = aligned((1 - core) * half)

    def swap():
        return remote(
            mine.at[pl.ds(given, half)], theirs, pair_sems.at[0], pair_sems.at[1],
            in_group(partner),
        )

    def y_send(j):
        there = pl.ds(aligned(j * size + (1 - bit) * side), side)
        return remote(
            half_sum.at[there], across_y.at[j], y_sems.at[0, j], y_sems.at[1, j], in_group(beside)
        )

    def z_send(j, s):
        there = pl.ds(aligned(lax.rem(at_line + s, line) * part), part)
        return remote(
            y_sum.at[j].at[there], landed.at[j, s - 1],
            z_sems.at[0, j, s - 1], z_sems.at[1, j, s - 1], in_group(along(s)),
        )

    def own_rows(j):
        return pl.ds(aligned(kept + j * size + bit * side + at_line * part), part)

    def own_side(j):
        return pl.ds(aligned(kept + j * size + bit * side), side)

    def other_side(j):
        return pl.ds(aligned(kept + j * size + (1 - bit) * side), side)

    def gather(j, s):
        return remote(
            total.at[j], result.at[own_rows(j)],
            gather_sems.at[0, j, s - 1], gather_sems.at[1, j, s - 1], in_group(along(s)),
        )

    def y_share(j):
        return remote(
            result.at[own_side(j)], result.at[own_side(j)],
            share_y_sems.at[0, j], share_y_sems.at[1, j], in_group(beside),
        )

    def back(j, i):
        there = own_side(j) if i == 0 else other_side(j)
        return remote(
            result.at[there], result.at[there],
            back_sems.at[0, j, i], back_sems.at[1, j, i], in_group(partner),
        )

    def piece(index):
        row = aligned(lax.rem(index, 8) * small_rows, 8)
        col = aligned((index // 8) * small_cols, LANES)
        return pl.ds(row, small_rows), pl.ds(col, small_cols)

    def small_out(s):
        return remote(
            small.at[piece(lax.rem(place + s, devices))], small_landed.at[s - 1],
            small_sems.at[0, s - 1], small_sems.at[1, s - 1],
            in_group(lax.rem(place + s, devices)),
        )

    def small_share(s):
        return remote(
            small_total, small_result.at[piece(place)],
            share_sems.at[0, s - 1], share_sems.at[1, s - 1],
            in_group(lax.rem(place + s, devices)),
        )

    def send_low():
        return remote(lows, lows_landed, cross_sems.at[0, 0], cross_sems.at[1, 0], across)

    def send_high(i):
        return remote(
            dx.at[i], dx_landed.at[i], cross_sems.at[0, 1 + i], cross_sems.at[1, 1 + i], across
        )

    def greet(barrier, other):
        pl.semaphore_signal(
            barrier, inc=1, device_id=other, device_id_type=pl.DeviceIdType.MESH
        )

    def load(source, target, i):
        return pltpu.make_async_copy(source, target, load_sems.at[i])

    enc_loads = [
        load(low_all, lows_all, 0), load(act_all, acts_all, 1),
        load(grad_all, grads_all, 2), load(pre_all, pres_all, 3),
    ]
    dec_loads = [
        load(long_up, ups.at[0], 0), load(long_down, downs.at[0], 1),
        load(short_up, ups.at[1], 2), load(short_down, downs.at[1], 3),
    ]

    @pl.when(step == 0)
    def _():
        barrier = pltpu.get_barrier_semaphore()
        for s in range(1, devices):
            greet(barrier, in_group(lax.rem(place + s, devices)))

        @pl.when(is_encoder)
        def _():
            for copy in enc_loads:
                copy.start()

        @pl.when(jnp.logical_not(is_encoder))
        def _():
            for copy in dec_loads:
                copy.start()

    @pl.when(is_encoder & (step < pairs))
    def _():
        at = aligned(step * LANES, LANES)
        lanes = pl.ds(at, LANES)
        prefix_totals = attend_back_pair(
            q_ref, [k_ref], [v_ref], o_ref, inv_ref, [g0_ref, g1_ref, g2_ref], pk_ref, pv_ref,
            (pl_ref, ps_ref), dq.at[:, lanes], dk.at[:, lanes], dv.at[:, lanes], enc_segs,
        )
        small[0:PRE_PAD, lanes] = prefix_totals[0] * scale
        small[PRE_PAD : 2 * PRE_PAD, lanes] = prefix_totals[1] * scale

    @pl.when(step == 0)
    def _():
        barrier = pltpu.get_barrier_semaphore()

        def pack(up, down):
            mine[0:chunk] = (up * scale).astype(BF)
            down = (down * scale).astype(BF)
            mine[chunk:width, 0:chunk] = down[0:chunk]
            mine[chunk:width, chunk:width] = down[chunk:width]

        @pl.when(is_encoder)
        def _():
            for copy in enc_loads:
                copy.wait()
            pack(
                adapter_scale * tn(acts_all[...], grads_all[...]),
                tn(lows_all[...], pres_all[...]),
            )
            pl.semaphore_wait(barrier, devices - 1)
            greet(barrier, across)

        @pl.when(jnp.logical_not(is_encoder))
        def _():
            for copy in dec_loads:
                copy.wait()
            pack(ups[0] + ups[1], downs[0] + downs[1])
            pl.semaphore_wait(barrier, devices)
            greet(barrier, across)

        swap().start()

        @pl.when(jnp.logical_not(is_encoder))
        def _():
            low = width // 2
            lows[0, 0:TGT] = y0_ref[:, 0:low]
            lows[0, TGT : 2 * TGT] = y1_ref[:, 0:low]
            lows[1] = dt_ref[:, 0:low]
            send_low().start()
            small[0:PRE_PAD] = dpk_ref[...] * scale
            small[PRE_PAD : 2 * PRE_PAD] = dpv_ref[...] * scale

    @pl.when(step == 1)
    def _():
        swap().wait()
        half_sum[...] = (
            mine[pl.ds(kept, half)].astype(F32) + theirs[...].astype(F32)
        ).astype(BF)
        for j in range(min(2, slices)):
            y_send(j).start()

    for j in range(slices):

        @pl.when(step == 2 + j)
        def _(j=j):
            y_send(j).wait()
            if j + 2 < slices:
                y_send(j + 2).start()
            own = pl.ds(aligned(j * size + bit * side), side)
            y_sum[j] = (half_sum[own].astype(F32) + across_y[j].astype(F32)).astype(BF)
            for s in range(1, line):
                z_send(j, s).start()

        @pl.when(step == 4 + j)
        def _(j=j):
            summed = y_sum[j, pl.ds(aligned(at_line * part), part)].astype(F32)
            for s in range(1, line):
                z_send(j, s).wait()
                summed = summed + landed[j, s - 1].astype(F32)
            total[j] = summed.astype(BF)
            result[own_rows(j)] = total[j]
            for s in range(1, line):
                gather(j, s).start()

        @pl.when(step == 6 + j)
        def _(j=j):
            for s in range(1, line):
                gather(j, s).wait()
            y_share(j).start()
            back(j, 0).start()

        @pl.when(step == 8 + j)
        def _(j=j):
            y_share(j).wait()
            back(j, 1).start()

    @pl.when(step == pairs - 1)
    def _():
        @pl.when(is_encoder)
        def _():
            up_row = jnp.sum(grads_all[...].astype(F32), axis=0, keepdims=True)
            down_row = jnp.sum(pres_all[...].astype(F32), axis=0, keepdims=True)
            down_row = jnp.concatenate([down_row, jnp.zeros_like(down_row)], 1)
            small[PRE : PRE + 1] = up_row * (adapter_scale * scale)
            small[PRE + 1 : PRE + 2] = down_row * scale

        @pl.when(jnp.logical_not(is_encoder))
        def _():
            down_row = long_downb[...] + short_downb[...]
            down_row = jnp.concatenate([down_row, jnp.zeros_like(down_row)], 1)
            small[PRE : PRE + 1] = (long_upb[...] + short_upb[...]) * scale
            small[PRE + 1 : PRE + 2] = down_row * scale

        for s in range(1, devices):
            small_out(s).start()

    @pl.when(is_encoder & (step == pairs))
    def _():
        pl.semaphore_wait(pltpu.get_barrier_semaphore(), 1)

    @pl.when(is_encoder & (step >= pairs))
    def _():
        acc = jnp.concatenate([dfirst0_ref[...], dfirst1_ref[...], dfirst2_ref[...]], 0)
        for n, grad in enumerate((dq, dk, dv)):
            acc = acc + nt(grad[...], wqkv_ref[:, n * width : (n + 1) * width])
        dx[step - pairs] = acc.astype(BF)

    for i in range(2):

        @pl.when(is_encoder & (step == pairs + i))
        def _(i=i):
            send_high(i).start()

    @pl.when(step == pairs + 1)
    def _():
        own_rows_, own_cols = piece(place)
        summed = small[own_rows_, own_cols]
        for s in range(1, devices):
            small_out(s).wait()
            summed = summed + small_landed[s - 1]
        small_total[...] = summed
        small_result[own_rows_, own_cols] = summed
        for s in range(1, devices):
            small_share(s).start()

    @pl.when(step == pairs + 3)
    def _():
        for j in range(slices):
            for i in range(2):
                back(j, i).wait()
        o_up_ref[...] = result[0:chunk]
        o_down_ref[0:chunk] = result[chunk:width, 0:chunk]
        o_down_ref[chunk:width] = result[chunk:width, chunk:width]
        for s in range(1, devices):
            small_share(s).wait()
        o_prefix_ref[0] = small_result[0:PRE]
        o_prefix_ref[1] = small_result[PRE_PAD : PRE_PAD + PRE]
        o_upb_ref[...] = small_result[PRE : PRE + 1]
        o_downb_ref[...] = small_result[PRE + 1 : PRE + 2, 0:chunk]

        @pl.when(is_encoder)
        def _():
            for i in range(2):
                source_ref[:, i * tile : (i + 1) * tile] = dx[2 + i]
            send_low().wait_recv()
            y_ref[...] = lows_landed[0]
            target_ref[...] = lows_landed[1]
            for i in range(2):
                send_high(i).wait_send()

        @pl.when(jnp.logical_not(is_encoder))
        def _():
            low = width // 2
            y_ref[0:TGT] = y0_ref[:, low:width]
            y_ref[TGT : 2 * TGT] = y1_ref[:, low:width]
            target_ref[...] = dt_ref[:, low:width]
            send_low().wait_send()
            for i in range(2):
                send_high(i).wait_recv()
                source_ref[:, i * tile : (i + 1) * tile] = dx_landed[i]


def finish(saved, datt, dfirst, w, traces, adapters, dec_prefix, ys, dt):
    qkv, att, inv, weights = saved
    devices = lax.axis_size("dp")
    line = devices // 4
    slices = 16 // line
    rows, width = att.shape
    targets = dt.shape[0]
    pairs, tile = 8, 256
    half = width // 2
    side = half // slices // 2
    part = side // line
    small_rows, small_cols = small_shape(devices)

    def mine(value):
        return jnp.where(lax.axis_index("section") == 0, value, 0)

    def head(i):
        return mine(jnp.minimum(i, pairs - 1))

    def pair(offset):
        return pl.BlockSpec((rows, LANES), lambda i: (0, head(i) + offset))

    def at(i):
        return mine(jnp.where(i < pairs + 2, 2 + jnp.maximum(i - pairs, 0), i - pairs - 2))

    def once(shape):
        return pl.BlockSpec(shape, lambda i: (0,) * len(shape), pipeline_mode=pl.Buffered(1))

    anywhere = pl.BlockSpec(memory_space=pl.ANY)
    prefix_pair = pl.BlockSpec((PRE_PAD, LANES), lambda i: (0, head(i)))
    vmem = pltpu.VMEM
    dma = pltpu.SemaphoreType.DMA
    flat = [*traces] + [a for group in adapters for a in group]
    return pl.pallas_call(
        functools.partial(finish_kernel, devices=devices),
        grid=(pairs + 4,),
        in_specs=[pair(0), pair(8), pair(16), pair(0), pair(0)]
        + [pl.BlockSpec((ENC_ROWS, LANES), lambda i, n=n: (n, head(i))) for n in range(3)]
        + [prefix_pair] * 2
        + [
            pl.BlockSpec((2,) + p.shape[1:], lambda i: (head(i), 0, 0))
            for p in weights
        ]
        + [pl.BlockSpec((ENC_ROWS, tile), lambda i, n=n: (n, at(i))) for n in range(3)]
        + [
            pl.BlockSpec((tile, 3 * width), lambda i: (at(i), 0)),
        ]
        + [anywhere if a.shape[0] > 1 else once(a.shape) for a in flat]
        + [once(a.shape) for a in (*dec_prefix, *ys, dt)],
        out_specs=[
            once((rows, half)), once((targets, half)), once((targets, half)),
            once((chunk, width)), once((width, chunk)),
            once((2, PRE, width)), once((1, width)), once((1, chunk)),
        ],
        out_shape=[
            jax.ShapeDtypeStruct((rows, half), BF),
            jax.ShapeDtypeStruct((targets, half), BF),
            jax.ShapeDtypeStruct((targets, half), BF),
            jax.ShapeDtypeStruct((chunk, width), BF),
            jax.ShapeDtypeStruct((width, chunk), BF),
            jax.ShapeDtypeStruct((2, PRE, width), F32),
            jax.ShapeDtypeStruct((1, width), F32),
            jax.ShapeDtypeStruct((1, chunk), F32),
        ],
        scratch_shapes=[
            vmem((rows, width), BF), vmem((rows, width), BF), vmem((rows, width), BF),
            vmem((2 * PRE_PAD, width), F32),
            vmem((rows, width), BF), vmem((rows, chunk), BF),
            vmem((rows, width), BF), vmem((rows, chunk), BF),
            vmem((2, chunk, width), F32), vmem((2, width, chunk), F32),
            vmem((width, width), BF), vmem((half, width), BF), vmem((half, width), BF),
            vmem((slices, side, width), BF), vmem((slices, side, width), BF),
            vmem((slices, line - 1, part, width), BF), vmem((slices, part, width), BF),
            vmem((width, width), BF),
            vmem((devices - 1, small_rows, small_cols), F32), vmem((small_rows, small_cols), F32),
            vmem((2 * PRE_PAD, width), F32),
            vmem((4, rows, tile), BF), vmem((2, rows, tile), BF),
            vmem((2, targets, half), BF), vmem((2, targets, half), BF),
            dma((4,)), dma((2,)), dma((2, slices)), dma((2, slices, line - 1)),
            dma((2, slices, line - 1)), dma((2, slices)), dma((2, slices, 2)),
            dma((2, devices - 1)), dma((2, devices - 1)), dma((2, 3)),
        ],
        compiler_params=pltpu.CompilerParams(
            vmem_limit_bytes=60 * 2**20, collective_id=0, has_side_effects=True
        ),
        name="finish",
    )(
        qkv, qkv, qkv, att, inv, datt, datt, datt, *w["prefix"], *weights,
        dfirst, dfirst, dfirst, w["qkv"], *flat, *dec_prefix, *ys, dt,
    )


def blank_kernel(*refs):
    pass


def blanks(shapes):
    return pl.pallas_call(
        blank_kernel,
        out_shape=list(shapes),
        out_specs=[pl.BlockSpec(memory_space=pl.ANY)] * len(shapes),
        name="blank",
    )()


def on_section(is_encoder, encoder_work, decoder_work, *operands):
    enc_shapes, _ = jax.eval_shape(encoder_work, *operands)
    dec_shapes, _ = jax.eval_shape(decoder_work, *operands)

    def blank_like(shapes):
        leaves, tree = jax.tree.flatten(shapes)
        if not leaves:
            return shapes
        return jax.tree.unflatten(tree, blanks(leaves))

    def encoder_branch(*a):
        own, shared = encoder_work(*a)
        return own, blank_like(dec_shapes), shared

    def decoder_branch(*a):
        own, shared = decoder_work(*a)
        return blank_like(enc_shapes), own, shared

    return lax.cond(is_encoder, encoder_branch, decoder_branch, *operands)


def to_decoder(block):
    return lax.ppermute(block, "section", [(0, 1)])


def to_encoder(block):
    return lax.ppermute(block, "section", [(1, 0)])


def per_device(
    sources, targets, cotangent, source_lengths, target_lengths,
    attn_qkv, attn_out, ffn_in, ffn_out, norm_gains, prefix_pairs,
    adapt_down, adapt_down_bias, adapt_up, adapt_up_bias,
    cross_query, cross_pairs, cross_out, cross_gain,
):
    is_encoder = lax.axis_index("section") == 0
    prefix = jnp.pad(prefix_pairs[0], ((0, 0), (0, PRE_PAD - PRE), (0, 0)))
    w = dict(
        qkv=attn_qkv[0], out=attn_out[0], ffn_in=ffn_in[0], ffn_out=ffn_out[0],
        gains=norm_gains[0], prefix=(prefix[0], prefix[1]),
        down=adapt_down[0], down_bias=adapt_down_bias,
        up=adapt_up[0], up_bias=adapt_up_bias,
    )
    cross = dict(query=cross_query, pairs=cross_pairs, out=cross_out, gain=cross_gain[None])

    def at_encoder(work, *operands):
        return on_section(is_encoder, lambda *a: (work(*a), ()), lambda *a: ((), ()), *operands)[0]

    def at_decoder(work, *operands):
        return on_section(is_encoder, lambda *a: ((), ()), lambda *a: (work(*a), ()), *operands)[1]

    def at_both(enc_work, dec_work, *operands):
        return on_section(
            is_encoder, lambda *a: (enc_work(*a), ()), lambda *a: (dec_work(*a), ()), *operands
        )[:2]

    def tie(*arrays):
        return lax.optimization_barrier(arrays)

    def encoder_self():
        qkv = product(sources, w["qkv"])
        att, inv, *weights = attend(
            source_lengths, *self_columns(qkv), w["prefix"], enc_segs, False, checked=True
        )
        return qkv, att, inv, weights

    saved, (cq, kept) = at_both(
        encoder_self, lambda: decoder_self(targets, target_lengths, w, cross)
    )
    long_queries = to_encoder(cq[0])
    short_queries = cq[1]
    part = at_encoder(lambda saved: enc_ffn(sources, saved[1], w), saved)
    mem_short = to_decoder(part[0][SRC_LONG:])

    def encoder_cross(mem, long_queries):
        kv = product(mem, cross["pairs"], rows=SRC_LONG)
        return kv, cross_forward(source_lengths, long_queries, kv, 0)

    long_kv, long = at_encoder(encoder_cross, part[0], long_queries)
    mem_short, catt = tie(mem_short, long[0])
    catt_here = to_decoder(catt)

    def decoder_short(mem_short, cq, kept):
        kv = product(mem_short, cross["pairs"])
        forward = cross_forward(source_lengths, cq, kv, 1)
        return kv, forward, dec_ffn(
            target_lengths, kept[4], forward[0], cotangent, w, cross, 1
        )

    short_kv, short, short_ffn = at_decoder(decoder_short, mem_short, short_queries, kept)
    short_y, short_second, short_dcatt, *short_adapter = short_ffn
    catt_here, short_y = tie(catt_here, short_y)
    long_y, long_second, long_dcatt, *long_adapter = at_decoder(
        lambda catt, kept: dec_ffn(target_lengths, kept[4], catt, cotangent, w, cross, 0),
        catt_here, kept,
    )
    short_dcatt, long_dcatt = tie(short_dcatt, long_dcatt)
    dcatt_here = to_encoder(long_dcatt)

    def decoder_short_back(kv, cq, short, dcatt):
        dcq, dck, dcv = cross_backward(cq, kv, short, dcatt, 1)
        return back_product([dck, dcv], cross["pairs"])[0], dcq

    dmem_short, short_cq = at_decoder(decoder_short_back, short_kv, short_queries, short, short_dcatt)
    dcatt_here, dmem_short = tie(dcatt_here, dmem_short)
    dmem_short = to_encoder(dmem_short)
    long_dcq, dck, dcv = at_encoder(
        lambda queries, kv, long, dcatt: cross_backward(queries, kv, long, dcatt, 0),
        long_queries, long_kv, long, dcatt_here,
    )
    long_cq = to_decoder(long_dcq)

    dmem_long = at_encoder(
        lambda *grads: back_product(grads, cross["pairs"])[0], dck, dcv
    )
    dmem_short, dmem_long = tie(dmem_short, dmem_long)
    dfirst, datt, grad, pre = at_encoder(
        lambda dmem_long, dmem_short, part: enc_ffn_back([dmem_long, dmem_short], part, w),
        dmem_long, dmem_short, part,
    )

    def decoder_end(kept, *grads):
        return decoder_self_back(kept, grads[:2], grads[2:], w, cross)

    long_cq, datt = tie(long_cq, datt)
    dt, dec_prefix = at_decoder(
        decoder_end, kept, long_second, short_second, long_cq, short_cq
    )
    source_grad, y, target_grad, up, down, prefix_grad, up_bias, down_bias = finish(
        saved, datt, dfirst, w, [part[4], part[3], grad, pre],
        [long_adapter, short_adapter], dec_prefix, [long_y, short_y], dt,
    )
    return (
        y,
        source_grad,
        target_grad,
        prefix_grad[None],
        down.astype(F32)[None],
        down_bias,
        up.astype(F32)[None],
        up_bias,
    )


def solution(mesh):
    layer2, layer3, rows = P("section", None), P("section", None, None), P("dp", None)
    return jax.shard_map(
        per_device,
        mesh=mesh,
        in_specs=(
            rows, rows, rows, rows, rows,
            layer3, layer3, layer3, layer3, layer3,
            P("section", None, None, None),
            layer3, layer2, layer3, layer2,
            P(), P(), P(), P(),
        ),
        out_specs=(
            P("dp", "section"), P("dp", "section"), P("dp", "section"),
            P("section", None, None, None), layer3, layer2, layer3, layer2,
        ),
        check_vma=False,
    )
```

```python
import functools

import jax
import jax.numpy as jnp
from jax import lax
from jax.experimental import pallas as pl
from jax.experimental.pallas import tpu as pltpu
from jax.sharding import PartitionSpec as P

HD = 64
PRE = 30
PRE_PAD = 32
SRC_LONG = 768
SRC_SHORT = 96
TGT = 256
LANES = 128

BF = jnp.bfloat16
F32 = jnp.float32
norm_eps = 1e-05
big_negative = -1e30
adapter_scale = 4.0
chunk = 512
wide = 1024
ENC_ROWS = (SRC_LONG + SRC_SHORT) // 3
vmem_bytes = 56 * 2**20

phi_poly = (
    0.797869713181688,
    0.036392283539041996,
    -8.782472977701046e-05,
    -3.669384069669515e-05,
    1.4250308145882202e-06,
)


def nn(left, right):
    return lax.dot_general(left, right, (((1,), (0,)), ((), ())), preferred_element_type=F32)


def nt(left, right):
    return lax.dot_general(left, right, (((1,), (1,)), ((), ())), preferred_element_type=F32)


def tn(left, right):
    return lax.dot_general(left, right, (((0,), (0,)), ((), ())), preferred_element_type=F32)


def gelu_pair(values):
    square = values * values
    poly = phi_poly[4]
    for coefficient in phi_poly[3::-1]:
        poly = poly * square + coefficient
    half = 0.5 * jnp.tanh(values * poly) + 0.5
    density = jnp.exp(square * -0.5) * 0.3989422804014327
    return values * half, half + values * density


def row_tiles(rows, most=864):
    count = -(-rows // most)
    size = rows // count
    return [(i * size, size) for i in range(count)]


def norm_rows(values):
    centered = values - jnp.mean(values, axis=-1, keepdims=True)
    scale = lax.rsqrt(jnp.mean(centered * centered, axis=-1, keepdims=True) + norm_eps)
    return centered * scale, scale


def norm_rows_back(hat, scale, grad_hat):
    mean_grad = jnp.mean(grad_hat, axis=-1, keepdims=True)
    mean_dot = jnp.mean(grad_hat * hat, axis=-1, keepdims=True)
    return scale * (grad_hat - mean_grad - hat * mean_dot)


def params(limit=vmem_bytes):
    return pltpu.CompilerParams(vmem_limit_bytes=limit)


def whole(shape):
    return pl.BlockSpec(shape, lambda *g: (0,) * len(shape))


def single(shape):
    return pl.BlockSpec(shape, lambda *g: (0,) * len(shape), pipeline_mode=pl.Buffered(1))


def product_kernel(x_ref, w_ref, o_ref):
    o_ref[...] = nn(x_ref[...], w_ref[...]).astype(BF)


def product(x, w, tile=1024, rows=None):
    depth = x.shape[1]
    rows = rows or x.shape[0]
    width = w.shape[1]
    return pl.pallas_call(
        product_kernel,
        grid=(width // tile,),
        in_specs=[whole((rows, depth)), pl.BlockSpec((depth, tile), lambda i: (0, i))],
        out_specs=pl.BlockSpec((rows, tile), lambda i: (0, i)),
        out_shape=jax.ShapeDtypeStruct((rows, width), BF),
        compiler_params=params(),
        name="product",
    )(x, w)


def back_product_kernel(*refs, parts, residual, cuts):
    grads = refs[:parts]
    w_ref = refs[parts]
    outs = refs[-len(cuts) :]
    total = None
    width = grads[0].shape[1]
    for i, grad in enumerate(grads):
        term = nt(grad[...], w_ref[:, i * width : (i + 1) * width])
        total = term if total is None else total + term
    if residual:
        total = total + refs[parts + 1][...]
    for (start, size), o_ref in zip(cuts, outs):
        o_ref[...] = total[start : start + size].astype(BF)


def back_product(grads, w, residual=None, tile=512, cuts=None):
    rows, width = grads[0].shape
    depth = w.shape[0]
    parts = len(grads)
    cuts = cuts or ((0, rows),)
    specs = [whole((rows, width))] * parts + [
        pl.BlockSpec((tile, parts * width), lambda i: (i, 0))
    ]
    args = list(grads) + [w]
    if residual is not None:
        specs.append(pl.BlockSpec((rows, tile), lambda i: (0, i)))
        args.append(residual)
    return pl.pallas_call(
        functools.partial(
            back_product_kernel, parts=parts, residual=residual is not None, cuts=cuts
        ),
        grid=(depth // tile,),
        in_specs=specs,
        out_specs=[pl.BlockSpec((size, tile), lambda i: (0, i)) for _, size in cuts],
        out_shape=[jax.ShapeDtypeStruct((size, depth), BF) for _, size in cuts],
        compiler_params=params(),
        name="back_product",
    )(*args)


def head_lanes(head):
    lane = lax.broadcasted_iota(jnp.int32, (1, LANES), 1)
    own = (lane < HD) if head == 0 else (lane >= HD)
    first = HD if head == 0 else 0
    return own, lane == first, lane == first + 1


def bf(value):
    return jnp.asarray(value, BF)


def rows_of(refs, start, count):
    parts = []
    for ref in refs:
        size = ref.shape[0]
        low, high = max(start, 0), min(start + count, size)
        if low < high:
            parts.append(ref[low:high])
        start -= size
    return parts


def stacked(refs, prefix_ref, start, count):
    parts = rows_of(refs, start, count)
    if prefix_ref is not None:
        parts.append(prefix_ref[...])
    return parts[0] if len(parts) == 1 else jnp.concatenate(parts, 0)


def attend_pair(*refs, segs, prefix, causal, pieces, which, checked):
    len_ref, q_ref = refs[:2]
    k_refs, v_refs = refs[2 : 2 + pieces], refs[2 + pieces : 2 + 2 * pieces]
    at = 2 + 2 * pieces
    pk_ref = pv_ref = None
    if prefix:
        pk_ref, pv_ref = refs[at : at + 2]
        at += 2
    o_ref, inv_ref = refs[at : at + 2]
    p_refs = refs[at + 2 :]

    def work(peaked):
        for seg, (q0, nq, k0, nk) in enumerate(segs):
            keys = stacked(k_refs, pk_ref, k0, nk)
            values = stacked(v_refs, pv_ref, k0, nk)
            count = keys.shape[0]
            row = lax.broadcasted_iota(jnp.int32, (count, 1), 0)
            seen = row < jnp.minimum(len_ref[0, which + seg], nk)
            if prefix:
                seen = seen | ((row >= nk) & (row < nk + PRE))
            queries = q_ref[q0 : q0 + nq] * bf(HD**-0.5)
            out = inv = None
            across = nq >= 4 * LANES
            outs, invs = [], []
            if across:
                turned = values.T
                ones = jnp.ones((16, count), BF)
            for head in range(2):
                own, first, _ = head_lanes(head)
                k_own = jnp.where(own, keys, jnp.where(first & ~seen, bf(big_negative), bf(0)))
                q_own = jnp.where(own, queries, jnp.where(first, bf(1), bf(0)))
                scores = nt(k_own, q_own)
                if causal:
                    key_at = lax.broadcasted_iota(jnp.int32, scores.shape, 0)
                    query_at = lax.broadcasted_iota(jnp.int32, scores.shape, 1)
                    allowed = (key_at <= query_at) | (key_at >= nk)
                    scores = jnp.where(allowed, scores, big_negative)
                if peaked:
                    scores = scores - jnp.max(scores, axis=0, keepdims=True)
                weights = jnp.exp(scores).astype(BF)
                p_refs[seg][head] = weights
                if across:
                    rows = jnp.concatenate([turned[head * HD : (head + 1) * HD], ones], 0)
                    mixed = nn(rows, weights)
                    inverse = 1.0 / mixed[HD : HD + 1]
                    outs.append(mixed[:HD] * inverse)
                    invs.append(jnp.broadcast_to(inverse, (HD, nq)))
                    continue
                mixed = tn(weights, jnp.where(own, values, bf(1)))
                inverse = 1.0 / pltpu.roll(mixed, HD, 1)
                mixed = mixed * inverse
                out = mixed if out is None else jnp.where(own, mixed, out)
                inv = inverse if inv is None else jnp.where(own, inverse, inv)
            if across:
                out = jnp.concatenate(outs, 0).T
                inv = jnp.concatenate(invs, 0).T
            o_ref[q0 : q0 + nq] = out.astype(BF)
            inv_ref[q0 : q0 + nq] = inv

    if not checked:
        work(True)
        return

    limit = 50.0**2
    head_row = lax.broadcasted_iota(jnp.int32, (LANES, LANES), 0) // HD
    head_col = lax.broadcasted_iota(jnp.int32, (LANES, LANES), 1) // HD
    same_head = jnp.where(head_row == head_col, 1.0, 0.0).astype(BF)

    def largest(array):
        square = (array.astype(F32) * array.astype(F32)).astype(BF)
        return jnp.max(nn(square, same_head), axis=0, keepdims=True)

    key_peak = largest(k_refs[0][...])
    for ref in k_refs[1:]:
        key_peak = jnp.maximum(key_peak, largest(ref[...]))
    if prefix:
        key_peak = jnp.maximum(key_peak, largest(pk_ref[...]))
    small = jnp.max(largest(q_ref[...]) * key_peak) * (1.0 / HD) <= limit

    @pl.when(small)
    def _():
        work(False)

    @pl.when(jnp.logical_not(small))
    def _():
        work(True)


def lane_views(refs, group, j):
    views = []
    for ref in refs:
        if len(ref.shape) == 2:
            views.append(ref.at[:, j * LANES : (j + 1) * LANES])
        else:
            views.append(ref.at[2 * j : 2 * j + 2])
    return views


def attend_kernel(len_ref, *refs, group, **kw):
    for j in range(group):
        attend_pair(len_ref, *lane_views(refs, group, j), **kw)


def column_spec(rows, offset, row_block=0, group=1):
    return pl.BlockSpec((rows, group * LANES), lambda h: (row_block, h + offset // group))


def attend(lengths, q, keys, values, prefixes, segs, causal, which=0, group=1, checked=False):
    pairs = 8
    q_rows = q[1]
    prefix = prefixes is not None
    extra = PRE_PAD if prefix else 0
    specs = [pl.BlockSpec(memory_space=pltpu.SMEM)]
    args = [lengths]
    for array, rows, block, offset in [q, *keys, *values]:
        specs.append(column_spec(rows, offset, block, group))
        args.append(array)
    if prefix:
        specs += [column_spec(PRE_PAD, 0, 0, group)] * 2
        args += list(prefixes)
    weight_shapes = [(2 * pairs, nk + extra, nq) for _, nq, _, nk in segs]
    return pl.pallas_call(
        functools.partial(
            attend_kernel, group=group, segs=segs, prefix=prefix, causal=causal, pieces=len(keys), which=which,
            checked=checked,
        ),
        grid=(pairs // group,),
        in_specs=specs,
        out_specs=[column_spec(q_rows, 0, 0, group)] * 2
        + [pl.BlockSpec((2 * group,) + s[1:], lambda h: (h, 0, 0)) for s in weight_shapes],
        out_shape=[
            jax.ShapeDtypeStruct((q_rows, pairs * LANES), BF),
            jax.ShapeDtypeStruct((q_rows, pairs * LANES), F32),
        ]
        + [jax.ShapeDtypeStruct(s, BF) for s in weight_shapes],
        compiler_params=params(),
        name="attend",
    )(*args)


def attend_back_pair(
    q_ref, k_refs, v_refs, o_ref, inv_ref, g_refs, pk_ref, pv_ref, p_refs, dq_ref, dk_ref, dv_ref, segs
):
    prefix_totals = [None, None]
    scale = HD**-0.5
    for seg, (q0, nq, k0, nk) in enumerate(segs):
        keys = stacked(k_refs, pk_ref, k0, nk)
        values = stacked(v_refs, pv_ref, k0, nk)
        queries = q_ref[q0 : q0 + nq]
        grads = stacked(g_refs, None, q0, nq).astype(F32) * inv_ref[q0 : q0 + nq]
        grads_low = grads.astype(BF)
        dots = grads * o_ref[q0 : q0 + nq].astype(F32)
        dq = dk = dv = None
        across = nq >= LANES and keys.shape[0] >= 4 * LANES
        turned_grads = []
        if across:
            turned = keys.T
        for head in range(2):
            own, first, second = head_lanes(head)
            row_dot = -jnp.sum(jnp.where(own, dots, 0.0), axis=1, keepdims=True)
            high = row_dot.astype(BF)
            rest = (row_dot - high.astype(F32)).astype(BF)
            g_own = jnp.where(
                own, grads_low, jnp.where(first, high, jnp.where(second, rest, bf(0)))
            )
            v_own = jnp.where(own, values, jnp.where(first | second, bf(1), bf(0)))
            weights = p_refs[seg][head]
            score_grad = (weights.astype(F32) * nt(v_own, g_own)).astype(BF)
            dv_head = nn(weights, grads_low)
            dk_head = nn(score_grad, queries)
            dq_head = None if across else tn(score_grad, keys)
            if across:
                turned_grads.append(nn(turned[head * HD : (head + 1) * HD], score_grad))
            if not across:
                dq = dq_head if dq is None else jnp.where(own, dq_head, dq)
            dk = dk_head if dk is None else jnp.where(own, dk_head, dk)
            dv = dv_head if dv is None else jnp.where(own, dv_head, dv)
        if across:
            dq = jnp.concatenate(turned_grads, 0).T
        dk = dk * scale
        dq_ref[q0 : q0 + nq] = (dq * scale).astype(BF)
        at = k0 - segs[0][2]
        dk_ref[at : at + nk] = dk[:nk].astype(BF)
        dv_ref[at : at + nk] = dv[:nk].astype(BF)
        if pk_ref is not None:
            for i, grad in enumerate((dk, dv)):
                part = grad[nk:]
                prefix_totals[i] = part if seg == 0 else prefix_totals[i] + part
    return prefix_totals


def attend_back_kernel(*refs, group, **kw):
    for j in range(group):
        attend_back_views(*lane_views(refs, group, j), **kw)


def attend_back_views(*refs, segs, prefix, pieces):
    q_ref, o_ref, inv_ref, g_ref = refs[:4]
    k_refs, v_refs = refs[4 : 4 + pieces], refs[4 + pieces : 4 + 2 * pieces]
    at = 4 + 2 * pieces
    pk_ref = pv_ref = None
    if prefix:
        pk_ref, pv_ref = refs[at : at + 2]
        at += 2
    outs = refs[at + len(segs) :]
    totals = attend_back_pair(
        q_ref, k_refs, v_refs, o_ref, inv_ref, [g_ref], pk_ref, pv_ref,
        refs[at : at + len(segs)], *outs[:3], segs,
    )
    if prefix:
        outs[3][...] = totals[0]
        outs[4][...] = totals[1]


def attend_back(q, keys, values, prefixes, attended, inverse, grad, weights, segs, group=2):
    pairs = 8
    q_rows = q[1]
    k_rows = sum(nk for _, _, _, nk in segs)
    prefix = prefixes is not None
    specs, args = [], []
    own = [(a, q_rows, 0, 0) for a in (attended, inverse, grad)]
    for array, rows, block, offset in [q, *own, *keys, *values]:
        specs.append(column_spec(rows, offset, block, group))
        args.append(array)
    if prefix:
        specs += [column_spec(PRE_PAD, 0, 0, group)] * 2
        args += list(prefixes)
    specs += [pl.BlockSpec((2 * group,) + w.shape[1:], lambda h: (h, 0, 0)) for w in weights]
    args += list(weights)
    out_specs = [column_spec(n, 0, 0, group) for n in (q_rows, k_rows, k_rows)]
    out_shape = [
        jax.ShapeDtypeStruct((q_rows, pairs * LANES), BF),
        jax.ShapeDtypeStruct((k_rows, pairs * LANES), BF),
        jax.ShapeDtypeStruct((k_rows, pairs * LANES), BF),
    ]
    if prefix:
        out_specs += [column_spec(PRE_PAD, 0, 0, group)] * 2
        out_shape += [jax.ShapeDtypeStruct((PRE_PAD, pairs * LANES), F32)] * 2
    return pl.pallas_call(
        functools.partial(
            attend_back_kernel, group=group, segs=segs, prefix=prefix, pieces=len(keys)
        ),
        grid=(pairs // group,),
        in_specs=specs,
        out_specs=out_specs,
        out_shape=out_shape,
        compiler_params=params(),
        name="attend_back",
    )(*args)


class Weights:
    def __init__(self, sources, targets, sems):
        self.sources, self.targets, self.sems = sources, targets, sems

    def copy(self, name, part=None):
        source, target = self.sources[name], self.targets[name]
        first = list(self.sources).index(name)
        sem = self.sems.at[first, 0 if part is None else part]
        if part is not None:
            cut = pl.ds(pl.multiple_of(part * wide, wide), wide)
            index = (slice(None), cut) if name == "in" else (cut, slice(None))
            source, target = source.at[index], target.at[index]
        return pltpu.make_async_copy(source, target, sem)

    def wait(self, name, part=None):
        self.copy(name, part).wait()

    def part(self, name, part):
        cut = pl.ds(pl.multiple_of(part * wide, wide), wide)
        index = (slice(None), cut) if name == "in" else (cut, slice(None))
        return self.targets[name].at[index]


def weight_scratch(arrays, parts):
    return [pltpu.VMEM(a.shape, BF) for a in arrays] + [
        pltpu.SemaphoreType.DMA((len(arrays), parts))
    ]


def ffn_step(low_ref, acc_ref, in_ref, out_ref, slope_ref, act_ref, bias_ref, scale):
    for start, size in row_tiles(low_ref.shape[0]):
        rows = slice(start, start + size)
        hidden = nn(low_ref[rows], in_ref[...])
        if bias_ref is not None:
            hidden = hidden + bias_ref[...]
        active, slope = gelu_pair(hidden)
        slope_ref[rows] = slope.astype(BF)
        active = active.astype(BF)
        if act_ref is not None:
            act_ref[rows] = active
        term = nn(active, out_ref[...])
        acc_ref[rows] += term if scale is None else scale * term


def enc_ffn_kernel(
    x_ref, att_ref, gain_ref, downb_ref, upb_ref, wo_hbm, in_hbm, out_hbm, down_hbm, up_hbm,
    mem_ref, slope_ref, pre_slope_ref, act_ref, low_ref, scales_ref,
    acc_ref, wo_ref, in_ref, out_ref, down_ref, up_ref, sems,
):
    weights = Weights(
        {"wo": wo_hbm, "in": in_hbm, "out": out_hbm, "down": down_hbm, "up": up_hbm},
        {"wo": wo_ref, "in": in_ref, "out": out_ref, "down": down_ref, "up": up_ref},
        sems,
    )

    weights.copy("wo").start()
    for part in range(in_ref.shape[1] // wide):
        weights.copy("in", part).start()
        weights.copy("out", part).start()
    weights.copy("down").start()
    weights.copy("up").start()
    weights.wait("wo")
    for start, size in row_tiles(x_ref.shape[0]):
        rows = slice(start, start + size)
        first = x_ref[rows].astype(F32) + nn(att_ref[rows], wo_ref[...])
        hat, scale = norm_rows(first)
        normed = hat * gain_ref[0:1]
        acc_ref[rows] = normed
        low_ref[rows] = normed.astype(BF)
        scales_ref[rows, 0:1] = scale

    def one_part(part, carry):
        weights.wait("in", part)
        weights.wait("out", part)
        cols = pl.ds(pl.multiple_of(part * wide, wide), wide)
        ffn_step(
            low_ref, acc_ref, in_ref.at[:, cols], out_ref.at[cols], slope_ref.at[:, cols],
            None, None, None,
        )
        return carry

    lax.fori_loop(0, in_ref.shape[1] // wide, one_part, 0)

    weights.wait("down")
    weights.wait("up")
    ffn_step(low_ref, acc_ref, down_ref, up_ref, pre_slope_ref, act_ref, downb_ref, adapter_scale)
    for start, size in row_tiles(x_ref.shape[0]):
        rows = slice(start, start + size)
        hat, scale = norm_rows(acc_ref[rows] + adapter_scale * upb_ref[...])
        mem_ref[rows] = (hat * gain_ref[1:2]).astype(BF)
        scales_ref[rows, 1:2] = scale


def enc_ffn(x, att, w):
    rows, width = x.shape
    hidden = w["ffn_in"].shape[1]
    steps = hidden // wide
    weights = [w["out"], w["ffn_in"], w["ffn_out"], w["down"], w["up"]]
    return pl.pallas_call(
        enc_ffn_kernel,
        grid=(1,),
        in_specs=[
            single((rows, width)),
            single((rows, width)),
            single((2, width)),
            single((1, chunk)),
            single((1, width)),
        ]
        + [pl.BlockSpec(memory_space=pl.ANY)] * len(weights),
        out_specs=[
            single((rows, width)),
            single((rows, hidden)),
            single((rows, chunk)),
            single((rows, chunk)),
            single((rows, width)),
            single((rows, LANES)),
        ],
        out_shape=[
            jax.ShapeDtypeStruct((rows, width), BF),
            jax.ShapeDtypeStruct((rows, hidden), BF),
            jax.ShapeDtypeStruct((rows, chunk), BF),
            jax.ShapeDtypeStruct((rows, chunk), BF),
            jax.ShapeDtypeStruct((rows, width), BF),
            jax.ShapeDtypeStruct((rows, LANES), F32),
        ],
        scratch_shapes=[pltpu.VMEM((rows, width), F32)] + weight_scratch(weights, steps),
        compiler_params=params(),
        name="enc_ffn",
    )(x, att, w["gains"], w["down_bias"], w["up_bias"], *weights)


def ffn_back_step(grad_ref, acc_ref, in_ref, out_ref, slope_ref):
    for start, size in row_tiles(grad_ref.shape[0]):
        rows = slice(start, start + size)
        pre = (nt(grad_ref[rows], out_ref[...]) * slope_ref[rows].astype(F32)).astype(BF)
        acc_ref[rows] += nt(pre, in_ref[...])


def adapter_back(grad_ref, acc_ref, low_ref, act_ref, slope_ref, down_ref, up_ref, outs, pre_ref):
    ddown_ref, ddownb_ref, dup_ref, dupb_ref = outs
    total = None
    for start, size in row_tiles(grad_ref.shape[0]):
        rows = slice(start, start + size)
        back = adapter_scale * nt(grad_ref[rows], up_ref[...])
        pre = (back * slope_ref[rows].astype(F32)).astype(BF)
        pre_ref[rows] = pre
        sums = jnp.sum(pre.astype(F32), axis=0, keepdims=True)
        total = sums if total is None else total + sums
        acc_ref[rows] += nt(pre, down_ref[...])
    ddownb_ref[...] = total
    ddown_ref[...] = tn(low_ref[...], pre_ref[...])
    dup_ref[...] = adapter_scale * tn(act_ref[...], grad_ref[...])
    dupb_ref[...] = adapter_scale * jnp.sum(grad_ref[...].astype(F32), axis=0, keepdims=True)


def enc_ffn_back_kernel(*refs, pieces):
    enc_ffn_back_body(refs[:pieces], *refs[pieces:])


def enc_ffn_back_body(
    dmem_refs, mem_ref, low_ref, scales_ref, gain_ref, slope_ref, pre_slope_ref,
    up_hbm, down_hbm, in_hbm, out_hbm, wo_hbm,
    dfirst_ref, datt_ref, grad_ref, pre_ref,
    acc_ref, up_ref, down_ref, in_ref, out_ref, wo_ref, sems,
):
    weights = Weights(
        {"up": up_hbm, "down": down_hbm, "in": in_hbm, "out": out_hbm, "wo": wo_hbm},
        {"up": up_ref, "down": down_ref, "in": in_ref, "out": out_ref, "wo": wo_ref},
        sems,
    )

    weights.copy("up").start()
    weights.copy("down").start()
    for part in range(in_ref.shape[1] // wide):
        weights.copy("out", part).start()
        weights.copy("in", part).start()
    weights.copy("wo").start()
    weights.wait("up")
    weights.wait("down")
    for start, size in row_tiles(mem_ref.shape[0]):
        rows = slice(start, start + size)
        gain = gain_ref[1:2]
        hat = mem_ref[rows].astype(F32) / gain
        dmem = stacked(dmem_refs, None, start, size).astype(F32)
        grad = norm_rows_back(hat, scales_ref[rows, 1:2], dmem * gain)
        low = grad.astype(BF)
        grad_ref[rows] = low
        back = adapter_scale * nt(low, up_ref[...])
        pre = (back * pre_slope_ref[rows].astype(F32)).astype(BF)
        pre_ref[rows] = pre
        acc_ref[rows] = grad + nt(pre, down_ref[...])

    def one_part(part, carry):
        weights.wait("out", part)
        weights.wait("in", part)
        cols = pl.ds(pl.multiple_of(part * wide, wide), wide)
        ffn_back_step(
            grad_ref, acc_ref, in_ref.at[:, cols], out_ref.at[cols], slope_ref.at[:, cols]
        )
        return carry

    lax.fori_loop(0, in_ref.shape[1] // wide, one_part, 0)

    weights.wait("wo")
    for start, size in row_tiles(mem_ref.shape[0]):
        rows = slice(start, start + size)
        gain = gain_ref[0:1]
        hat = low_ref[rows].astype(F32) / gain
        grad = norm_rows_back(hat, scales_ref[rows, 0:1], acc_ref[rows] * gain)
        dfirst_ref[rows] = grad
        datt_ref[rows] = nt(grad.astype(BF), wo_ref[...]).astype(BF)


def enc_ffn_back(dmems, saved, w):
    mem, slope, pre_slope, act, low, scales = saved
    rows, width = mem.shape
    hidden = w["ffn_in"].shape[1]
    steps = hidden // wide
    weights = [w["up"], w["down"], w["ffn_in"], w["ffn_out"], w["out"]]
    return pl.pallas_call(
        functools.partial(enc_ffn_back_kernel, pieces=len(dmems)),
        grid=(1,),
        in_specs=[single(d.shape) for d in dmems]
        + [
            single((rows, width)),
            single((rows, width)),
            single((rows, LANES)),
            single((2, width)),
            single((rows, hidden)),
            single((rows, chunk)),
        ]
        + [pl.BlockSpec(memory_space=pl.ANY)] * len(weights),
        out_specs=[
            single((rows, width)),
            single((rows, width)),
            single((rows, width)),
            single((rows, chunk)),
        ],
        out_shape=[
            jax.ShapeDtypeStruct((rows, width), F32),
            jax.ShapeDtypeStruct((rows, width), BF),
            jax.ShapeDtypeStruct((rows, width), BF),
            jax.ShapeDtypeStruct((rows, chunk), BF),
        ],
        scratch_shapes=[pltpu.VMEM((rows, width), F32)] + weight_scratch(weights, steps),
        compiler_params=params(),
        name="enc_ffn_back",
    )(*dmems, mem, low, scales, w["gains"], slope, pre_slope, *weights)


def dec_mid_kernel(x_ref, att_ref, wo_ref, gain_ref, wq_ref, n_ref, scale_ref, *cq_refs):
    for (start, size), cq_ref in zip(row_tiles(x_ref.shape[0], TGT), cq_refs):
        rows = slice(start, start + size)
        first = x_ref[rows].astype(F32) + nn(att_ref[rows], wo_ref[...])
        hat, scale = norm_rows(first)
        normed = hat * gain_ref[0:1]
        n_ref[rows] = normed
        scale_ref[rows, 0:1] = scale
        cq_ref[...] = nn(normed.astype(BF), wq_ref[...]).astype(BF)


def dec_mid(x, att, w, cross):
    rows, width = x.shape
    return pl.pallas_call(
        dec_mid_kernel,
        out_shape=[
            jax.ShapeDtypeStruct((rows, width), F32),
            jax.ShapeDtypeStruct((rows, LANES), F32),
        ]
        + [jax.ShapeDtypeStruct((TGT, width), BF)] * (rows // TGT),
        compiler_params=params(),
        name="dec_mid",
    )(x, att, w["out"], w["gains"], cross["query"])


def dec_ffn_kernel(
    len_ref, n_ref, catt_ref, cot_ref, cgain_ref, gain_ref, downb_ref, upb_ref,
    wco_hbm, in_hbm, out_hbm, down_hbm, up_hbm,
    y_ref, dsecond_ref, dcatt_ref, ddown_ref, ddownb_ref, dup_ref, dupb_ref,
    acc_ref, low_ref, grad_ref, slope_ref, pre_slope_ref, act_ref, pre_ref, scale_ref,
    wco_ref, in_ref, out_ref, down_ref, up_ref, sems,
    *, steps, which,
):
    weights = Weights(
        {"wco": wco_hbm, "in": in_hbm, "out": out_hbm, "down": down_hbm, "up": up_hbm},
        {"wco": wco_ref, "in": in_ref, "out": out_ref, "down": down_ref, "up": up_ref},
        sems,
    )

    weights.copy("wco").start()
    for part in range(steps):
        weights.copy("in", part).start()
        weights.copy("out", part).start()
    weights.copy("down").start()
    weights.copy("up").start()
    weights.wait("wco")
    second = n_ref[...] + nn(catt_ref[...], wco_ref[...])
    hat, scale = norm_rows(second)
    middle = hat * cgain_ref[...]
    acc_ref[...] = middle
    low_ref[...] = middle.astype(BF)
    scale_ref[:, 0:1] = scale

    def forward(part, carry):
        weights.wait("in", part)
        weights.wait("out", part)
        ffn_step(
            low_ref, acc_ref, weights.part("in", part), weights.part("out", part),
            slope_ref.at[part], None, None, None,
        )
        return carry

    lax.fori_loop(0, steps, forward, 0)

    weights.wait("down")
    weights.wait("up")
    ffn_step(
        low_ref, acc_ref, down_ref, up_ref, pre_slope_ref, act_ref, downb_ref, adapter_scale
    )
    gain = gain_ref[1:2]
    hat, scale = norm_rows(acc_ref[...] + adapter_scale * upb_ref[...])
    row = lax.broadcasted_iota(jnp.int32, (low_ref.shape[0], 1), 0)
    valid = row < len_ref[0, which]
    y_ref[...] = jnp.where(valid, hat * gain, 0.0).astype(BF)
    cot = jnp.where(valid, cot_ref[...].astype(F32), 0.0)
    grad = norm_rows_back(hat, scale, cot * gain)
    acc_ref[...] = grad
    grad_ref[...] = grad.astype(BF)
    adapter_back(
        grad_ref, acc_ref, low_ref, act_ref, pre_slope_ref, down_ref, up_ref,
        (ddown_ref, ddownb_ref, dup_ref, dupb_ref), pre_ref,
    )

    def backward(part, carry):
        ffn_back_step(
            grad_ref, acc_ref, weights.part("in", part), weights.part("out", part),
            slope_ref.at[part],
        )
        return carry

    lax.fori_loop(0, steps, backward, 0)

    gain = cgain_ref[...]
    hat = low_ref[...].astype(F32) / gain
    grad = norm_rows_back(hat, scale_ref[:, 0:1], acc_ref[...] * gain)
    dsecond_ref[...] = grad
    dcatt_ref[...] = nt(grad.astype(BF), wco_ref[...]).astype(BF)


def dec_ffn(lengths, n, catt, cot, w, cross, which):
    rows, width = catt.shape
    hidden = w["ffn_in"].shape[1]
    steps = hidden // wide
    weights = [cross["out"], w["ffn_in"], w["ffn_out"], w["down"], w["up"]]
    return pl.pallas_call(
        functools.partial(dec_ffn_kernel, steps=steps, which=which),
        grid=(1,),
        in_specs=[
            pl.BlockSpec(memory_space=pltpu.SMEM),
            pl.BlockSpec((rows, width), lambda i: (which, 0)),
            whole((rows, width)),
            pl.BlockSpec((rows, width), lambda i: (which, 0)),
            whole((1, width)),
            whole((2, width)),
            whole((1, chunk)),
            whole((1, width)),
        ]
        + [pl.BlockSpec(memory_space=pl.ANY)] * len(weights),
        out_specs=[
            whole((rows, width)),
            whole((rows, width)),
            whole((rows, width)),
            whole((width, chunk)),
            whole((1, chunk)),
            whole((chunk, width)),
            whole((1, width)),
        ],
        out_shape=[
            jax.ShapeDtypeStruct((rows, width), BF),
            jax.ShapeDtypeStruct((rows, width), F32),
            jax.ShapeDtypeStruct((rows, width), BF),
            jax.ShapeDtypeStruct((width, chunk), F32),
            jax.ShapeDtypeStruct((1, chunk), F32),
            jax.ShapeDtypeStruct((chunk, width), F32),
            jax.ShapeDtypeStruct((1, width), F32),
        ],
        scratch_shapes=[
            pltpu.VMEM((rows, width), F32),
            pltpu.VMEM((rows, width), BF),
            pltpu.VMEM((rows, width), BF),
            pltpu.VMEM((steps, rows, wide), BF),
            pltpu.VMEM((rows, chunk), BF),
            pltpu.VMEM((rows, chunk), BF),
            pltpu.VMEM((rows, chunk), BF),
            pltpu.VMEM((rows, LANES), F32),
        ]
        + weight_scratch(weights, steps),
        compiler_params=params(),
        name="dec_ffn",
    )(
        lengths, n, catt, cot, cross["gain"], w["gains"], w["down_bias"], w["up_bias"], *weights
    )


def dec_mid_back_kernel(
    dsecond0_ref, dsecond1_ref, dcq0_ref, dcq1_ref, wq_ref, n_ref, scale_ref, gain_ref, wo_ref,
    dfirst_ref, datt_ref,
):
    for pair, (dsecond_ref, dcq_ref) in enumerate(
        ((dsecond0_ref, dcq0_ref), (dsecond1_ref, dcq1_ref))
    ):
        rows = slice(pair * TGT, (pair + 1) * TGT)
        gain = gain_ref[0:1]
        total = dsecond_ref[...] + nt(dcq_ref[...], wq_ref[...])
        grad = norm_rows_back(n_ref[rows] / gain, scale_ref[rows, 0:1], total * gain)
        dfirst_ref[rows] = grad
        datt_ref[rows] = nt(grad.astype(BF), wo_ref[...]).astype(BF)


def dec_mid_back(dseconds, dcqs, n, scale, w, cross):
    rows, width = n.shape
    return pl.pallas_call(
        dec_mid_back_kernel,
        out_shape=[
            jax.ShapeDtypeStruct((rows, width), F32),
            jax.ShapeDtypeStruct((rows, width), BF),
        ],
        compiler_params=params(),
        name="dec_mid_back",
    )(*dseconds, *dcqs, cross["query"], n, scale, w["gains"], w["out"])


enc_segs = ((0, SRC_LONG, 0, SRC_LONG), (SRC_LONG, SRC_SHORT, SRC_LONG, SRC_SHORT))
dec_segs = ((0, TGT, 0, TGT), (TGT, TGT, TGT, TGT))
cross_segs = (((0, TGT, 0, SRC_LONG),), ((0, TGT, 0, SRC_SHORT),))


def self_columns(qkv):
    rows = qkv.shape[0]
    return (qkv, rows, 0, 0), [(qkv, rows, 0, 8)], [(qkv, rows, 0, 16)]


def cross_columns(cq, kv, which):
    keys = (SRC_LONG, SRC_SHORT)[which]
    return (cq, TGT, 0, 0), [(kv, keys, 0, 0)], [(kv, keys, 0, 8)]


def decoder_self(t, lengths, w, cross):
    qkv = product(t, w["qkv"])
    att, inv, *weights = attend(lengths, *self_columns(qkv), w["prefix"], dec_segs, True, group=2)
    n, scale, *cq = dec_mid(t, att, w, cross)
    return cq, (qkv, att, inv, weights, n, scale)


def cross_forward(lengths, cq, kv, which):
    return attend(
        lengths, *cross_columns(cq, kv, which), None, cross_segs[which], False, which, group=2
    )


def cross_backward(cq, kv, forward, dcatt, which):
    catt, inv, *weights = forward
    return attend_back(
        *cross_columns(cq, kv, which), None, catt, inv, dcatt, weights, cross_segs[which]
    )


def decoder_self_back(kept, dseconds, dcqs, w, cross):
    qkv, att, inv, weights, n, scale = kept
    dfirst, datt = dec_mid_back(dseconds, dcqs, n, scale, w, cross)
    dq, dk, dv, *dprefix = attend_back(
        *self_columns(qkv), w["prefix"], att, inv, datt, weights, dec_segs, group=1
    )
    return back_product([dq, dk, dv], w["qkv"], dfirst)[0], dprefix


def small_shape(devices):
    return 8, 8 * (2 * chunk) // devices


def finish_kernel(
    q_ref, k_ref, v_ref, o_ref, inv_ref, g0_ref, g1_ref, g2_ref, pk_ref, pv_ref, pl_ref, ps_ref,
    dfirst0_ref, dfirst1_ref, dfirst2_ref, wqkv_ref,
    low_all, act_all, grad_all, pre_all,
    long_down, long_downb, long_up, long_upb,
    short_down, short_downb, short_up, short_upb, dpk_ref, dpv_ref,
    y0_hbm, y1_hbm, dt_hbm,
    source_ref, y_ref, target_ref, o_up_ref, o_down_ref, o_prefix_ref, o_upb_ref, o_downb_ref,
    dq, dk, dv, small, y0_ref, y1_ref, dt_ref, lows_all, acts_all, grads_all, pres_all, ups, downs, mine, theirs, half_sum, across_y, y_sum, landed, total, result,
    small_landed, small_total, small_result, dx, dx_landed, lows, lows_landed,
    load_sems, pair_sems, y_sems, z_sems, gather_sems, share_y_sems, back_sems,
    small_sems, share_sems, cross_sems,
    *, devices,
):
    step = pl.program_id(0)
    pairs = 8
    section = lax.axis_index("section")
    is_encoder = section == 0
    chips = devices // 2
    line = chips // 2
    slices = 16 // line
    rows = 2 * chunk
    half = rows // 2
    size = half // slices
    side = size // 2
    part = side // line
    place = lax.axis_index("dp")
    core, chip = lax.rem(place, 2), place // 2
    bit, at_line = lax.rem(chip, 2), chip // 2
    partner = place + 1 - 2 * core
    beside = place + 2 - 4 * bit
    small_rows, small_cols = small_shape(devices)
    tile = 256
    width = 2 * chunk
    scale = 1.0 / devices

    def aligned(value, unit=16):
        return pl.multiple_of(value, unit)

    def along(distance):
        return (lax.rem(at_line + distance, line) * 2 + bit) * 2 + core

    def remote(source, target, send_sem, recv_sem, other):
        return pltpu.make_async_remote_copy(
            src_ref=source, dst_ref=target, send_sem=send_sem, recv_sem=recv_sem,
            device_id=other, device_id_type=pl.DeviceIdType.MESH,
        )

    def in_group(other):
        return {"dp": other}

    across = {"section": 1 - section}
    kept = aligned(core * half)
    given = aligned((1 - core) * half)

    def swap():
        return remote(
            mine.at[pl.ds(given, half)], theirs, pair_sems.at[0], pair_sems.at[1],
            in_group(partner),
        )

    def y_send(j):
        there = pl.ds(aligned(j * size + (1 - bit) * side), side)
        return remote(
            half_sum.at[there], across_y.at[j], y_sems.at[0, j], y_sems.at[1, j], in_group(beside)
        )

    def z_send(j, s):
        there = pl.ds(aligned(lax.rem(at_line + s, line) * part), part)
        return remote(
            y_sum.at[j].at[there], landed.at[j, s - 1],
            z_sems.at[0, j, s - 1], z_sems.at[1, j, s - 1], in_group(along(s)),
        )

    def own_rows(j):
        return pl.ds(aligned(kept + j * size + bit * side + at_line * part), part)

    def own_side(j):
        return pl.ds(aligned(kept + j * size + bit * side), side)

    def other_side(j):
        return pl.ds(aligned(kept + j * size + (1 - bit) * side), side)

    def gather(j, s):
        return remote(
            total.at[j], result.at[own_rows(j)],
            gather_sems.at[0, j, s - 1], gather_sems.at[1, j, s - 1], in_group(along(s)),
        )

    def y_share(j):
        return remote(
            result.at[own_side(j)], result.at[own_side(j)],
            share_y_sems.at[0, j], share_y_sems.at[1, j], in_group(beside),
        )

    def back(j, i):
        there = own_side(j) if i == 0 else other_side(j)
        return remote(
            result.at[there], result.at[there],
            back_sems.at[0, j, i], back_sems.at[1, j, i], in_group(partner),
        )

    def piece(index):
        row = aligned(lax.rem(index, 8) * small_rows, 8)
        col = aligned((index // 8) * small_cols, LANES)
        return pl.ds(row, small_rows), pl.ds(col, small_cols)

    def small_out(s):
        return remote(
            small.at[piece(lax.rem(place + s, devices))], small_landed.at[s - 1],
            small_sems.at[0, s - 1], small_sems.at[1, s - 1],
            in_group(lax.rem(place + s, devices)),
        )

    def small_share(s):
        return remote(
            small_total, small_result.at[piece(place)],
            share_sems.at[0, s - 1], share_sems.at[1, s - 1],
            in_group(lax.rem(place + s, devices)),
        )

    def send_low():
        return remote(lows, lows_landed, cross_sems.at[0, 0], cross_sems.at[1, 0], across)

    def send_high(i):
        return remote(
            dx.at[i], dx_landed.at[i], cross_sems.at[0, 1 + i], cross_sems.at[1, 1 + i], across
        )

    def greet(barrier, other):
        pl.semaphore_signal(
            barrier, inc=1, device_id=other, device_id_type=pl.DeviceIdType.MESH
        )

    def load(source, target, i):
        return pltpu.make_async_copy(source, target, load_sems.at[i])

    enc_loads = [
        load(low_all, lows_all, 0), load(act_all, acts_all, 1),
        load(grad_all, grads_all, 2), load(pre_all, pres_all, 3),
    ]
    dec_loads = [
        load(long_up, ups.at[0], 0), load(long_down, downs.at[0], 1),
        load(short_up, ups.at[1], 2), load(short_down, downs.at[1], 3),
        load(y0_hbm, y0_ref, 4), load(y1_hbm, y1_ref, 5), load(dt_hbm, dt_ref, 6),
    ]

    @pl.when(step == 0)
    def _():
        barrier = pltpu.get_barrier_semaphore()
        for s in range(1, devices):
            greet(barrier, in_group(lax.rem(place + s, devices)))

        @pl.when(is_encoder)
        def _():
            for copy in enc_loads:
                copy.start()

        @pl.when(jnp.logical_not(is_encoder))
        def _():
            for copy in dec_loads:
                copy.start()

    @pl.when(is_encoder & (step < pairs))
    def _():
        at = aligned(step * LANES, LANES)
        lanes = pl.ds(at, LANES)
        prefix_totals = attend_back_pair(
            q_ref, [k_ref], [v_ref], o_ref, inv_ref, [g0_ref, g1_ref, g2_ref], pk_ref, pv_ref,
            (pl_ref, ps_ref), dq.at[:, lanes], dk.at[:, lanes], dv.at[:, lanes], enc_segs,
        )
        small[0:PRE_PAD, lanes] = prefix_totals[0] * scale
        small[PRE_PAD : 2 * PRE_PAD, lanes] = prefix_totals[1] * scale

    @pl.when(step == 0)
    def _():
        barrier = pltpu.get_barrier_semaphore()

        def pack(up, down):
            mine[0:chunk] = (up * scale).astype(BF)
            down = (down * scale).astype(BF)
            mine[chunk:width, 0:chunk] = down[0:chunk]
            mine[chunk:width, chunk:width] = down[chunk:width]

        @pl.when(is_encoder)
        def _():
            for copy in enc_loads:
                copy.wait()
            pack(
                adapter_scale * tn(acts_all[...], grads_all[...]),
                tn(lows_all[...], pres_all[...]),
            )
            pl.semaphore_wait(barrier, devices - 1)
            greet(barrier, across)

        @pl.when(jnp.logical_not(is_encoder))
        def _():
            for copy in dec_loads:
                copy.wait()
            pack(ups[0] + ups[1], downs[0] + downs[1])
            pl.semaphore_wait(barrier, devices)
            greet(barrier, across)

        swap().start()

        @pl.when(jnp.logical_not(is_encoder))
        def _():
            low = width // 2
            lows[0, 0:TGT] = y0_ref[:, 0:low]
            lows[0, TGT : 2 * TGT] = y1_ref[:, 0:low]
            lows[1] = dt_ref[:, 0:low]
            send_low().start()
            small[0:PRE_PAD] = dpk_ref[...] * scale
            small[PRE_PAD : 2 * PRE_PAD] = dpv_ref[...] * scale

    @pl.when(step == 1)
    def _():
        swap().wait()
        half_sum[...] = (
            mine[pl.ds(kept, half)].astype(F32) + theirs[...].astype(F32)
        ).astype(BF)
        for j in range(min(2, slices)):
            y_send(j).start()

    for j in range(slices):

        @pl.when(step == 2 + j)
        def _(j=j):
            y_send(j).wait()
            if j + 2 < slices:
                y_send(j + 2).start()
            own = pl.ds(aligned(j * size + bit * side), side)
            y_sum[j] = (half_sum[own].astype(F32) + across_y[j].astype(F32)).astype(BF)
            for s in range(1, line):
                z_send(j, s).start()

        @pl.when(step == 4 + j)
        def _(j=j):
            summed = y_sum[j, pl.ds(aligned(at_line * part), part)].astype(F32)
            for s in range(1, line):
                z_send(j, s).wait()
                summed = summed + landed[j, s - 1].astype(F32)
            total[j] = summed.astype(BF)
            result[own_rows(j)] = total[j]
            for s in range(1, line):
                gather(j, s).start()

        @pl.when(step == 6 + j)
        def _(j=j):
            for s in range(1, line):
                gather(j, s).wait()
            y_share(j).start()
            back(j, 0).start()

        @pl.when(step == 8 + j)
        def _(j=j):
            y_share(j).wait()
            back(j, 1).start()

    @pl.when(step == pairs - 1)
    def _():
        @pl.when(is_encoder)
        def _():
            up_row = jnp.sum(grads_all[...].astype(F32), axis=0, keepdims=True)
            down_row = jnp.sum(pres_all[...].astype(F32), axis=0, keepdims=True)
            down_row = jnp.concatenate([down_row, jnp.zeros_like(down_row)], 1)
            small[PRE : PRE + 1] = up_row * (adapter_scale * scale)
            small[PRE + 1 : PRE + 2] = down_row * scale

        @pl.when(jnp.logical_not(is_encoder))
        def _():
            down_row = long_downb[...] + short_downb[...]
            down_row = jnp.concatenate([down_row, jnp.zeros_like(down_row)], 1)
            small[PRE : PRE + 1] = (long_upb[...] + short_upb[...]) * scale
            small[PRE + 1 : PRE + 2] = down_row * scale

        for s in range(1, devices):
            small_out(s).start()

    @pl.when(is_encoder & (step == pairs))
    def _():
        pl.semaphore_wait(pltpu.get_barrier_semaphore(), 1)

    @pl.when(is_encoder & (step >= pairs))
    def _():
        acc = jnp.concatenate([dfirst0_ref[...], dfirst1_ref[...], dfirst2_ref[...]], 0)
        for n, grad in enumerate((dq, dk, dv)):
            acc = acc + nt(grad[...], wqkv_ref[:, n * width : (n + 1) * width])
        dx[step - pairs] = acc.astype(BF)

    for i in range(2):

        @pl.when(is_encoder & (step == pairs + i))
        def _(i=i):
            send_high(i).start()

    @pl.when(step == pairs + 1)
    def _():
        own_rows_, own_cols = piece(place)
        summed = small[own_rows_, own_cols]
        for s in range(1, devices):
            small_out(s).wait()
            summed = summed + small_landed[s - 1]
        small_total[...] = summed
        small_result[own_rows_, own_cols] = summed
        for s in range(1, devices):
            small_share(s).start()

    @pl.when(step == pairs + 3)
    def _():
        for j in range(slices):
            for i in range(2):
                back(j, i).wait()
        o_up_ref[...] = result[0:chunk]
        o_down_ref[0:chunk] = result[chunk:width, 0:chunk]
        o_down_ref[chunk:width] = result[chunk:width, chunk:width]
        for s in range(1, devices):
            small_share(s).wait()
        o_prefix_ref[:, 0] = small_result[0:PRE]
        o_prefix_ref[:, 1] = small_result[PRE_PAD : PRE_PAD + PRE]
        o_upb_ref[...] = small_result[PRE : PRE + 1]
        o_downb_ref[...] = small_result[PRE + 1 : PRE + 2, 0:chunk]

        @pl.when(is_encoder)
        def _():
            for i in range(2):
                source_ref[:, i * tile : (i + 1) * tile] = dx[2 + i]
            send_low().wait_recv()
            y_ref[...] = lows_landed[0]
            target_ref[...] = lows_landed[1]
            for i in range(2):
                send_high(i).wait_send()

        @pl.when(jnp.logical_not(is_encoder))
        def _():
            low = width // 2
            y_ref[0:TGT] = y0_ref[:, low:width]
            y_ref[TGT : 2 * TGT] = y1_ref[:, low:width]
            target_ref[...] = dt_ref[:, low:width]
            send_low().wait_send()
            for i in range(2):
                send_high(i).wait_recv()
                source_ref[:, i * tile : (i + 1) * tile] = dx_landed[i]


def finish(saved, datt, dfirst, w, traces, adapters, dec_prefix, ys, dt):
    qkv, att, inv, weights = saved
    devices = lax.axis_size("dp")
    line = devices // 4
    slices = 16 // line
    rows, width = att.shape
    targets = dt.shape[0]
    pairs, tile = 8, 256
    half = width // 2
    side = half // slices // 2
    part = side // line
    small_rows, small_cols = small_shape(devices)

    def mine(value):
        return jnp.where(lax.axis_index("section") == 0, value, 0)

    def head(i):
        return mine(jnp.minimum(i, pairs - 1))

    def pair(offset):
        return pl.BlockSpec((rows, LANES), lambda i: (0, head(i) + offset))

    def at(i):
        return mine(jnp.where(i < pairs + 2, 2 + jnp.maximum(i - pairs, 0), i - pairs - 2))

    def once(shape):
        return pl.BlockSpec(shape, lambda i: (0,) * len(shape), pipeline_mode=pl.Buffered(1))

    anywhere = pl.BlockSpec(memory_space=pl.ANY)
    prefix_pair = pl.BlockSpec((PRE_PAD, LANES), lambda i: (0, head(i)))
    vmem = pltpu.VMEM
    dma = pltpu.SemaphoreType.DMA
    flat = [*traces] + [a for group in adapters for a in group]
    return pl.pallas_call(
        functools.partial(finish_kernel, devices=devices),
        grid=(pairs + 4,),
        in_specs=[pair(0), pair(8), pair(16), pair(0), pair(0)]
        + [pl.BlockSpec((ENC_ROWS, LANES), lambda i, n=n: (n, head(i))) for n in range(3)]
        + [prefix_pair] * 2
        + [
            pl.BlockSpec((2,) + p.shape[1:], lambda i: (head(i), 0, 0))
            for p in weights
        ]
        + [pl.BlockSpec((ENC_ROWS, tile), lambda i, n=n: (n, at(i))) for n in range(3)]
        + [
            pl.BlockSpec((tile, 3 * width), lambda i: (at(i), 0)),
        ]
        + [anywhere if a.shape[0] > 1 else once(a.shape) for a in flat]
        + [once(a.shape) for a in dec_prefix]
        + [anywhere] * 3,
        out_specs=[
            once((rows, half)), once((targets, half)), once((targets, half)),
            once((chunk, width)), once((width, chunk)),
            once((PRE, 2, width)), once((1, width)), once((1, chunk)),
        ],
        out_shape=[
            jax.ShapeDtypeStruct((rows, half), BF),
            jax.ShapeDtypeStruct((targets, half), BF),
            jax.ShapeDtypeStruct((targets, half), BF),
            jax.ShapeDtypeStruct((chunk, width), BF),
            jax.ShapeDtypeStruct((width, chunk), BF),
            jax.ShapeDtypeStruct((PRE, 2, width), F32),
            jax.ShapeDtypeStruct((1, width), F32),
            jax.ShapeDtypeStruct((1, chunk), F32),
        ],
        scratch_shapes=[
            vmem((rows, width), BF), vmem((rows, width), BF), vmem((rows, width), BF),
            vmem((2 * PRE_PAD, width), F32),
            vmem((TGT, width), BF), vmem((TGT, width), BF), vmem((targets, width), BF),
            vmem((rows, width), BF), vmem((rows, chunk), BF),
            vmem((rows, width), BF), vmem((rows, chunk), BF),
            vmem((2, chunk, width), F32), vmem((2, width, chunk), F32),
            vmem((width, width), BF), vmem((half, width), BF), vmem((half, width), BF),
            vmem((slices, side, width), BF), vmem((slices, side, width), BF),
            vmem((slices, line - 1, part, width), BF), vmem((slices, part, width), BF),
            vmem((width, width), BF),
            vmem((devices - 1, small_rows, small_cols), F32), vmem((small_rows, small_cols), F32),
            vmem((2 * PRE_PAD, width), F32),
            vmem((4, rows, tile), BF), vmem((2, rows, tile), BF),
            vmem((2, targets, half), BF), vmem((2, targets, half), BF),
            dma((7,)), dma((2,)), dma((2, slices)), dma((2, slices, line - 1)),
            dma((2, slices, line - 1)), dma((2, slices)), dma((2, slices, 2)),
            dma((2, devices - 1)), dma((2, devices - 1)), dma((2, 3)),
        ],
        compiler_params=pltpu.CompilerParams(
            vmem_limit_bytes=60 * 2**20, collective_id=0, has_side_effects=True
        ),
        name="finish",
    )(
        qkv, qkv, qkv, att, inv, datt, datt, datt, *w["prefix"], *weights,
        dfirst, dfirst, dfirst, w["qkv"], *flat, *dec_prefix, *ys, dt,
    )


def blank_kernel(*refs):
    pass


def blanks(shapes):
    return pl.pallas_call(
        blank_kernel,
        out_shape=list(shapes),
        out_specs=[pl.BlockSpec(memory_space=pl.ANY)] * len(shapes),
        name="blank",
    )()


def on_section(is_encoder, encoder_work, decoder_work, *operands):
    enc_shapes, _ = jax.eval_shape(encoder_work, *operands)
    dec_shapes, _ = jax.eval_shape(decoder_work, *operands)

    def blank_like(shapes):
        leaves, tree = jax.tree.flatten(shapes)
        if not leaves:
            return shapes
        return jax.tree.unflatten(tree, blanks(leaves))

    def encoder_branch(*a):
        own, shared = encoder_work(*a)
        return own, blank_like(dec_shapes), shared

    def decoder_branch(*a):
        own, shared = decoder_work(*a)
        return blank_like(enc_shapes), own, shared

    return lax.cond(is_encoder, encoder_branch, decoder_branch, *operands)


def to_decoder(block):
    return lax.ppermute(block, "section", [(0, 1)])


def to_encoder(block):
    return lax.ppermute(block, "section", [(1, 0)])


def per_device(
    sources, targets, cotangent, source_lengths, target_lengths,
    attn_qkv, attn_out, ffn_in, ffn_out, norm_gains, prefix_pairs,
    adapt_down, adapt_down_bias, adapt_up, adapt_up_bias,
    cross_query, cross_pairs, cross_out, cross_gain,
):
    is_encoder = lax.axis_index("section") == 0
    prefix = jnp.pad(prefix_pairs[0], ((0, 0), (0, PRE_PAD - PRE), (0, 0)))
    w = dict(
        qkv=attn_qkv[0], out=attn_out[0], ffn_in=ffn_in[0], ffn_out=ffn_out[0],
        gains=norm_gains[0], prefix=(prefix[0], prefix[1]),
        down=adapt_down[0], down_bias=adapt_down_bias,
        up=adapt_up[0], up_bias=adapt_up_bias,
    )
    cross = dict(query=cross_query, pairs=cross_pairs, out=cross_out, gain=cross_gain[None])

    def at_encoder(work, *operands):
        return on_section(is_encoder, lambda *a: (work(*a), ()), lambda *a: ((), ()), *operands)[0]

    def at_decoder(work, *operands):
        return on_section(is_encoder, lambda *a: ((), ()), lambda *a: (work(*a), ()), *operands)[1]

    def at_both(enc_work, dec_work, *operands):
        return on_section(
            is_encoder, lambda *a: (enc_work(*a), ()), lambda *a: (dec_work(*a), ()), *operands
        )[:2]

    def tie(*arrays):
        return lax.optimization_barrier(arrays)

    def encoder_self():
        qkv = product(sources, w["qkv"])
        att, inv, *weights = attend(
            source_lengths, *self_columns(qkv), w["prefix"], enc_segs, False, checked=True
        )
        return qkv, att, inv, weights

    saved, (cq, kept) = at_both(
        encoder_self, lambda: decoder_self(targets, target_lengths, w, cross)
    )
    long_queries = to_encoder(cq[0])
    short_queries = cq[1]
    part = at_encoder(lambda saved: enc_ffn(sources, saved[1], w), saved)
    mem_short = to_decoder(part[0][SRC_LONG:])

    def encoder_cross(mem, long_queries):
        kv = product(mem, cross["pairs"], rows=SRC_LONG)
        return kv, cross_forward(source_lengths, long_queries, kv, 0)

    long_kv, long = at_encoder(encoder_cross, part[0], long_queries)
    mem_short, catt = tie(mem_short, long[0])
    catt_here = to_decoder(catt)

    def decoder_short(mem_short, cq, kept):
        kv = product(mem_short, cross["pairs"])
        forward = cross_forward(source_lengths, cq, kv, 1)
        return kv, forward, dec_ffn(
            target_lengths, kept[4], forward[0], cotangent, w, cross, 1
        )

    short_kv, short, short_ffn = at_decoder(decoder_short, mem_short, short_queries, kept)
    short_y, short_second, short_dcatt, *short_adapter = short_ffn
    catt_here, short_y = tie(catt_here, short_y)
    long_y, long_second, long_dcatt, *long_adapter = at_decoder(
        lambda catt, kept: dec_ffn(target_lengths, kept[4], catt, cotangent, w, cross, 0),
        catt_here, kept,
    )
    short_dcatt, long_dcatt = tie(short_dcatt, long_dcatt)
    dcatt_here = to_encoder(long_dcatt)

    def decoder_short_back(kv, cq, short, dcatt):
        dcq, dck, dcv = cross_backward(cq, kv, short, dcatt, 1)
        return back_product([dck, dcv], cross["pairs"])[0], dcq

    dmem_short, short_cq = at_decoder(decoder_short_back, short_kv, short_queries, short, short_dcatt)
    dcatt_here, dmem_short = tie(dcatt_here, dmem_short)
    dmem_short = to_encoder(dmem_short)
    long_dcq, dck, dcv = at_encoder(
        lambda queries, kv, long, dcatt: cross_backward(queries, kv, long, dcatt, 0),
        long_queries, long_kv, long, dcatt_here,
    )
    long_cq = to_decoder(long_dcq)

    dmem_long = at_encoder(
        lambda *grads: back_product(grads, cross["pairs"])[0], dck, dcv
    )
    dmem_short, dmem_long = tie(dmem_short, dmem_long)
    dfirst, datt, grad, pre = at_encoder(
        lambda dmem_long, dmem_short, part: enc_ffn_back([dmem_long, dmem_short], part, w),
        dmem_long, dmem_short, part,
    )

    def decoder_end(kept, *grads):
        return decoder_self_back(kept, grads[:2], grads[2:], w, cross)

    long_cq, datt = tie(long_cq, datt)
    dt, dec_prefix = at_decoder(
        decoder_end, kept, long_second, short_second, long_cq, short_cq
    )
    source_grad, y, target_grad, up, down, prefix_grad, up_bias, down_bias = finish(
        saved, datt, dfirst, w, [part[4], part[3], grad, pre],
        [long_adapter, short_adapter], dec_prefix, [long_y, short_y], dt,
    )
    return (
        y,
        source_grad,
        target_grad,
        jnp.swapaxes(prefix_grad, 0, 1)[None],
        down.astype(F32)[None],
        down_bias,
        up.astype(F32)[None],
        up_bias,
    )


def solution(mesh):
    layer2, layer3, rows = P("section", None), P("section", None, None), P("dp", None)
    return jax.shard_map(
        per_device,
        mesh=mesh,
        in_specs=(
            rows, rows, rows, rows, rows,
            layer3, layer3, layer3, layer3, layer3,
            P("section", None, None, None),
            layer3, layer2, layer3, layer2,
            P(), P(), P(), P(),
        ),
        out_specs=(
            P("dp", "section"), P("dp", "section"), P("dp", "section"),
            P("section", None, None, None), layer3, layer2, layer3, layer2,
        ),
        check_vma=False,
    )
```

```python
import functools

import jax
import jax.numpy as jnp
from jax import lax
from jax.experimental import pallas as pl
from jax.experimental.pallas import tpu as pltpu
from jax.sharding import PartitionSpec as P

HD = 64
PRE = 30
PRE_PAD = 32
SRC_LONG = 768
SRC_SHORT = 96
TGT = 256
LANES = 128

BF = jnp.bfloat16
F32 = jnp.float32
norm_eps = 1e-05
big_negative = -1e30
adapter_scale = 4.0
chunk = 512
wide = 1024
ENC_ROWS = (SRC_LONG + SRC_SHORT) // 3
vmem_bytes = 56 * 2**20

phi_poly = (
    0.797869713181688,
    0.036392283539041996,
    -8.782472977701046e-05,
    -3.669384069669515e-05,
    1.4250308145882202e-06,
)


def nn(left, right):
    return lax.dot_general(left, right, (((1,), (0,)), ((), ())), preferred_element_type=F32)


def nt(left, right):
    return lax.dot_general(left, right, (((1,), (1,)), ((), ())), preferred_element_type=F32)


def tn(left, right):
    return lax.dot_general(left, right, (((0,), (0,)), ((), ())), preferred_element_type=F32)


def gelu_pair(values):
    square = values * values
    poly = phi_poly[4]
    for coefficient in phi_poly[3::-1]:
        poly = poly * square + coefficient
    half = 0.5 * jnp.tanh(values * poly) + 0.5
    density = jnp.exp(square * -0.5) * 0.3989422804014327
    return values * half, half + values * density


def row_tiles(rows, most=864):
    count = -(-rows // most)
    size = rows // count
    return [(i * size, size) for i in range(count)]


def norm_rows(values):
    centered = values - jnp.mean(values, axis=-1, keepdims=True)
    scale = lax.rsqrt(jnp.mean(centered * centered, axis=-1, keepdims=True) + norm_eps)
    return centered * scale, scale


def norm_rows_back(hat, scale, grad_hat):
    mean_grad = jnp.mean(grad_hat, axis=-1, keepdims=True)
    mean_dot = jnp.mean(grad_hat * hat, axis=-1, keepdims=True)
    return scale * (grad_hat - mean_grad - hat * mean_dot)


def params(limit=vmem_bytes):
    return pltpu.CompilerParams(vmem_limit_bytes=limit)


def whole(shape):
    return pl.BlockSpec(shape, lambda *g: (0,) * len(shape))


def single(shape):
    return pl.BlockSpec(shape, lambda *g: (0,) * len(shape), pipeline_mode=pl.Buffered(1))


def product_kernel(x_ref, w_ref, o_ref):
    o_ref[...] = nn(x_ref[...], w_ref[...]).astype(BF)


def product(x, w, tile=1024, rows=None):
    depth = x.shape[1]
    rows = rows or x.shape[0]
    width = w.shape[1]
    return pl.pallas_call(
        product_kernel,
        grid=(width // tile,),
        in_specs=[whole((rows, depth)), pl.BlockSpec((depth, tile), lambda i: (0, i))],
        out_specs=pl.BlockSpec((rows, tile), lambda i: (0, i)),
        out_shape=jax.ShapeDtypeStruct((rows, width), BF),
        compiler_params=params(),
        name="product",
    )(x, w)


def back_product_kernel(*refs, parts, residual, cuts):
    grads = refs[:parts]
    w_ref = refs[parts]
    outs = refs[-len(cuts) :]
    total = None
    width = grads[0].shape[1]
    for i, grad in enumerate(grads):
        term = nt(grad[...], w_ref[:, i * width : (i + 1) * width])
        total = term if total is None else total + term
    if residual:
        total = total + refs[parts + 1][...]
    for (start, size), o_ref in zip(cuts, outs):
        o_ref[...] = total[start : start + size].astype(BF)


def back_product(grads, w, residual=None, tile=512, cuts=None):
    rows, width = grads[0].shape
    depth = w.shape[0]
    parts = len(grads)
    cuts = cuts or ((0, rows),)
    specs = [whole((rows, width))] * parts + [
        pl.BlockSpec((tile, parts * width), lambda i: (i, 0))
    ]
    args = list(grads) + [w]
    if residual is not None:
        specs.append(pl.BlockSpec((rows, tile), lambda i: (0, i)))
        args.append(residual)
    return pl.pallas_call(
        functools.partial(
            back_product_kernel, parts=parts, residual=residual is not None, cuts=cuts
        ),
        grid=(depth // tile,),
        in_specs=specs,
        out_specs=[pl.BlockSpec((size, tile), lambda i: (0, i)) for _, size in cuts],
        out_shape=[jax.ShapeDtypeStruct((size, depth), BF) for _, size in cuts],
        compiler_params=params(),
        name="back_product",
    )(*args)


def head_lanes(head):
    lane = lax.broadcasted_iota(jnp.int32, (1, LANES), 1)
    own = (lane < HD) if head == 0 else (lane >= HD)
    first = HD if head == 0 else 0
    return own, lane == first, lane == first + 1


def bf(value):
    return jnp.asarray(value, BF)


def rows_of(refs, start, count):
    parts = []
    for ref in refs:
        size = ref.shape[0]
        low, high = max(start, 0), min(start + count, size)
        if low < high:
            parts.append(ref[low:high])
        start -= size
    return parts


def stacked(refs, prefix_ref, start, count):
    parts = rows_of(refs, start, count)
    if prefix_ref is not None:
        parts.append(prefix_ref[...])
    return parts[0] if len(parts) == 1 else jnp.concatenate(parts, 0)


def attend_pair(*refs, segs, prefix, causal, pieces, which, checked):
    len_ref, q_ref = refs[:2]
    k_refs, v_refs = refs[2 : 2 + pieces], refs[2 + pieces : 2 + 2 * pieces]
    at = 2 + 2 * pieces
    pk_ref = pv_ref = None
    if prefix:
        pk_ref, pv_ref = refs[at : at + 2]
        at += 2
    o_ref, inv_ref = refs[at : at + 2]
    p_refs = refs[at + 2 :]

    def work(peaked):
        for seg, (q0, nq, k0, nk) in enumerate(segs):
            keys = stacked(k_refs, pk_ref, k0, nk)
            values = stacked(v_refs, pv_ref, k0, nk)
            count = keys.shape[0]
            row = lax.broadcasted_iota(jnp.int32, (count, 1), 0)
            seen = row < jnp.minimum(len_ref[0, which + seg], nk)
            if prefix:
                seen = seen | ((row >= nk) & (row < nk + PRE))
            queries = q_ref[q0 : q0 + nq] * bf(HD**-0.5)
            out = inv = None
            across = nq >= 4 * LANES
            outs, invs = [], []
            if across:
                turned = values.T
                ones = jnp.ones((16, count), BF)
            for head in range(2):
                own, first, _ = head_lanes(head)
                k_own = jnp.where(own, keys, jnp.where(first & ~seen, bf(big_negative), bf(0)))
                q_own = jnp.where(own, queries, jnp.where(first, bf(1), bf(0)))
                scores = nt(k_own, q_own)
                if causal:
                    key_at = lax.broadcasted_iota(jnp.int32, scores.shape, 0)
                    query_at = lax.broadcasted_iota(jnp.int32, scores.shape, 1)
                    allowed = (key_at <= query_at) | (key_at >= nk)
                    scores = jnp.where(allowed, scores, big_negative)
                if peaked:
                    scores = scores - jnp.max(scores, axis=0, keepdims=True)
                weights = jnp.exp(scores).astype(BF)
                p_refs[seg][head] = weights
                if across:
                    rows = jnp.concatenate([turned[head * HD : (head + 1) * HD], ones], 0)
                    mixed = nn(rows, weights)
                    inverse = 1.0 / mixed[HD : HD + 1]
                    outs.append(mixed[:HD] * inverse)
                    invs.append(jnp.broadcast_to(inverse, (HD, nq)))
                    continue
                mixed = tn(weights, jnp.where(own, values, bf(1)))
                inverse = 1.0 / pltpu.roll(mixed, HD, 1)
                mixed = mixed * inverse
                out = mixed if out is None else jnp.where(own, mixed, out)
                inv = inverse if inv is None else jnp.where(own, inverse, inv)
            if across:
                out = jnp.concatenate(outs, 0).T
                inv = jnp.concatenate(invs, 0).T
            o_ref[q0 : q0 + nq] = out.astype(BF)
            inv_ref[q0 : q0 + nq] = inv

    if not checked:
        work(True)
        return

    limit = 50.0**2
    head_row = lax.broadcasted_iota(jnp.int32, (LANES, LANES), 0) // HD
    head_col = lax.broadcasted_iota(jnp.int32, (LANES, LANES), 1) // HD
    same_head = jnp.where(head_row == head_col, 1.0, 0.0).astype(BF)

    def largest(array):
        square = (array.astype(F32) * array.astype(F32)).astype(BF)
        return jnp.max(nn(square, same_head), axis=0, keepdims=True)

    key_peak = largest(k_refs[0][...])
    for ref in k_refs[1:]:
        key_peak = jnp.maximum(key_peak, largest(ref[...]))
    if prefix:
        key_peak = jnp.maximum(key_peak, largest(pk_ref[...]))
    small = jnp.max(largest(q_ref[...]) * key_peak) * (1.0 / HD) <= limit

    @pl.when(small)
    def _():
        work(False)

    @pl.when(jnp.logical_not(small))
    def _():
        work(True)


def lane_views(refs, group, j):
    views = []
    for ref in refs:
        if len(ref.shape) == 2:
            views.append(ref.at[:, j * LANES : (j + 1) * LANES])
        else:
            views.append(ref.at[2 * j : 2 * j + 2])
    return views


def attend_kernel(len_ref, *refs, group, **kw):
    for j in range(group):
        attend_pair(len_ref, *lane_views(refs, group, j), **kw)


def column_spec(rows, offset, row_block=0, group=1):
    return pl.BlockSpec((rows, group * LANES), lambda h: (row_block, h + offset // group))


def attend(lengths, q, keys, values, prefixes, segs, causal, which=0, group=1, checked=False):
    pairs = 8
    q_rows = q[1]
    prefix = prefixes is not None
    extra = PRE_PAD if prefix else 0
    specs = [pl.BlockSpec(memory_space=pltpu.SMEM)]
    args = [lengths]
    for array, rows, block, offset in [q, *keys, *values]:
        specs.append(column_spec(rows, offset, block, group))
        args.append(array)
    if prefix:
        specs += [column_spec(PRE_PAD, 0, 0, group)] * 2
        args += list(prefixes)
    weight_shapes = [(2 * pairs, nk + extra, nq) for _, nq, _, nk in segs]
    return pl.pallas_call(
        functools.partial(
            attend_kernel, group=group, segs=segs, prefix=prefix, causal=causal, pieces=len(keys), which=which,
            checked=checked,
        ),
        grid=(pairs // group,),
        in_specs=specs,
        out_specs=[column_spec(q_rows, 0, 0, group)] * 2
        + [pl.BlockSpec((2 * group,) + s[1:], lambda h: (h, 0, 0)) for s in weight_shapes],
        out_shape=[
            jax.ShapeDtypeStruct((q_rows, pairs * LANES), BF),
            jax.ShapeDtypeStruct((q_rows, pairs * LANES), F32),
        ]
        + [jax.ShapeDtypeStruct(s, BF) for s in weight_shapes],
        compiler_params=params(),
        name="attend",
    )(*args)


def attend_back_pair(
    q_ref, k_refs, v_refs, o_ref, inv_ref, g_refs, pk_ref, pv_ref, p_refs, dq_ref, dk_ref, dv_ref, segs
):
    prefix_totals = [None, None]
    scale = HD**-0.5
    for seg, (q0, nq, k0, nk) in enumerate(segs):
        keys = stacked(k_refs, pk_ref, k0, nk)
        values = stacked(v_refs, pv_ref, k0, nk)
        queries = q_ref[q0 : q0 + nq]
        grads = stacked(g_refs, None, q0, nq).astype(F32) * inv_ref[q0 : q0 + nq]
        grads_low = grads.astype(BF)
        dots = grads * o_ref[q0 : q0 + nq].astype(F32)
        dq = dk = dv = None
        across = nq >= LANES and keys.shape[0] >= 4 * LANES
        turned_grads = []
        if across:
            turned = keys.T
        for head in range(2):
            own, first, second = head_lanes(head)
            row_dot = -jnp.sum(jnp.where(own, dots, 0.0), axis=1, keepdims=True)
            high = row_dot.astype(BF)
            rest = (row_dot - high.astype(F32)).astype(BF)
            g_own = jnp.where(
                own, grads_low, jnp.where(first, high, jnp.where(second, rest, bf(0)))
            )
            v_own = jnp.where(own, values, jnp.where(first | second, bf(1), bf(0)))
            weights = p_refs[seg][head]
            score_grad = (weights.astype(F32) * nt(v_own, g_own)).astype(BF)
            dv_head = nn(weights, grads_low)
            dk_head = nn(score_grad, queries)
            dq_head = None if across else tn(score_grad, keys)
            if across:
                turned_grads.append(nn(turned[head * HD : (head + 1) * HD], score_grad))
            if not across:
                dq = dq_head if dq is None else jnp.where(own, dq_head, dq)
            dk = dk_head if dk is None else jnp.where(own, dk_head, dk)
            dv = dv_head if dv is None else jnp.where(own, dv_head, dv)
        if across:
            dq = jnp.concatenate(turned_grads, 0).T
        dk = dk * scale
        dq_ref[q0 : q0 + nq] = (dq * scale).astype(BF)
        at = k0 - segs[0][2]
        dk_ref[at : at + nk] = dk[:nk].astype(BF)
        dv_ref[at : at + nk] = dv[:nk].astype(BF)
        if pk_ref is not None:
            for i, grad in enumerate((dk, dv)):
                part = grad[nk:]
                prefix_totals[i] = part if seg == 0 else prefix_totals[i] + part
    return prefix_totals


def attend_back_kernel(*refs, group, **kw):
    for j in range(group):
        attend_back_views(*lane_views(refs, group, j), **kw)


def attend_back_views(*refs, segs, prefix, pieces):
    q_ref, o_ref, inv_ref, g_ref = refs[:4]
    k_refs, v_refs = refs[4 : 4 + pieces], refs[4 + pieces : 4 + 2 * pieces]
    at = 4 + 2 * pieces
    pk_ref = pv_ref = None
    if prefix:
        pk_ref, pv_ref = refs[at : at + 2]
        at += 2
    outs = refs[at + len(segs) :]
    totals = attend_back_pair(
        q_ref, k_refs, v_refs, o_ref, inv_ref, [g_ref], pk_ref, pv_ref,
        refs[at : at + len(segs)], *outs[:3], segs,
    )
    if prefix:
        outs[3][...] = totals[0]
        outs[4][...] = totals[1]


def attend_back(q, keys, values, prefixes, attended, inverse, grad, weights, segs, group=2):
    pairs = 8
    q_rows = q[1]
    k_rows = sum(nk for _, _, _, nk in segs)
    prefix = prefixes is not None
    specs, args = [], []
    own = [(a, q_rows, 0, 0) for a in (attended, inverse, grad)]
    for array, rows, block, offset in [q, *own, *keys, *values]:
        specs.append(column_spec(rows, offset, block, group))
        args.append(array)
    if prefix:
        specs += [column_spec(PRE_PAD, 0, 0, group)] * 2
        args += list(prefixes)
    specs += [pl.BlockSpec((2 * group,) + w.shape[1:], lambda h: (h, 0, 0)) for w in weights]
    args += list(weights)
    out_specs = [column_spec(n, 0, 0, group) for n in (q_rows, k_rows, k_rows)]
    out_shape = [
        jax.ShapeDtypeStruct((q_rows, pairs * LANES), BF),
        jax.ShapeDtypeStruct((k_rows, pairs * LANES), BF),
        jax.ShapeDtypeStruct((k_rows, pairs * LANES), BF),
    ]
    if prefix:
        out_specs += [column_spec(PRE_PAD, 0, 0, group)] * 2
        out_shape += [jax.ShapeDtypeStruct((PRE_PAD, pairs * LANES), F32)] * 2
    return pl.pallas_call(
        functools.partial(
            attend_back_kernel, group=group, segs=segs, prefix=prefix, pieces=len(keys)
        ),
        grid=(pairs // group,),
        in_specs=specs,
        out_specs=out_specs,
        out_shape=out_shape,
        compiler_params=params(),
        name="attend_back",
    )(*args)


class Weights:
    def __init__(self, sources, targets, sems):
        self.sources, self.targets, self.sems = sources, targets, sems

    def copy(self, name, part=None):
        source, target = self.sources[name], self.targets[name]
        first = list(self.sources).index(name)
        sem = self.sems.at[first, 0 if part is None else part]
        if part is not None:
            cut = pl.ds(pl.multiple_of(part * wide, wide), wide)
            index = (slice(None), cut) if name == "in" else (cut, slice(None))
            source, target = source.at[index], target.at[index]
        return pltpu.make_async_copy(source, target, sem)

    def wait(self, name, part=None):
        self.copy(name, part).wait()

    def part(self, name, part):
        cut = pl.ds(pl.multiple_of(part * wide, wide), wide)
        index = (slice(None), cut) if name == "in" else (cut, slice(None))
        return self.targets[name].at[index]


def weight_scratch(arrays, parts):
    return [pltpu.VMEM(a.shape, BF) for a in arrays] + [
        pltpu.SemaphoreType.DMA((len(arrays), parts))
    ]


def ffn_step(low_ref, acc_ref, in_ref, out_ref, slope_ref, act_ref, bias_ref, scale):
    for start, size in row_tiles(low_ref.shape[0]):
        rows = slice(start, start + size)
        hidden = nn(low_ref[rows], in_ref[...])
        if bias_ref is not None:
            hidden = hidden + bias_ref[...]
        active, slope = gelu_pair(hidden)
        slope_ref[rows] = slope.astype(BF)
        active = active.astype(BF)
        if act_ref is not None:
            act_ref[rows] = active
        term = nn(active, out_ref[...])
        acc_ref[rows] += term if scale is None else scale * term


def enc_ffn_kernel(
    x_ref, att_ref, gain_ref, downb_ref, upb_ref, wo_hbm, in_hbm, out_hbm, down_hbm, up_hbm,
    mem_ref, slope_ref, pre_slope_ref, act_ref, low_ref, scales_ref,
    acc_ref, wo_ref, in_ref, out_ref, down_ref, up_ref, sems,
):
    weights = Weights(
        {"wo": wo_hbm, "in": in_hbm, "out": out_hbm, "down": down_hbm, "up": up_hbm},
        {"wo": wo_ref, "in": in_ref, "out": out_ref, "down": down_ref, "up": up_ref},
        sems,
    )

    weights.copy("wo").start()
    for part in range(in_ref.shape[1] // wide):
        weights.copy("in", part).start()
        weights.copy("out", part).start()
    weights.copy("down").start()
    weights.copy("up").start()
    weights.wait("wo")
    for start, size in row_tiles(x_ref.shape[0]):
        rows = slice(start, start + size)
        first = x_ref[rows].astype(F32) + nn(att_ref[rows], wo_ref[...])
        hat, scale = norm_rows(first)
        normed = hat * gain_ref[0:1]
        acc_ref[rows] = normed
        low_ref[rows] = normed.astype(BF)
        scales_ref[rows, 0:1] = scale

    def one_part(part, carry):
        weights.wait("in", part)
        weights.wait("out", part)
        cols = pl.ds(pl.multiple_of(part * wide, wide), wide)
        ffn_step(
            low_ref, acc_ref, in_ref.at[:, cols], out_ref.at[cols], slope_ref.at[:, cols],
            None, None, None,
        )
        return carry

    lax.fori_loop(0, in_ref.shape[1] // wide, one_part, 0)

    weights.wait("down")
    weights.wait("up")
    ffn_step(low_ref, acc_ref, down_ref, up_ref, pre_slope_ref, act_ref, downb_ref, adapter_scale)
    for start, size in row_tiles(x_ref.shape[0]):
        rows = slice(start, start + size)
        hat, scale = norm_rows(acc_ref[rows] + adapter_scale * upb_ref[...])
        mem_ref[rows] = (hat * gain_ref[1:2]).astype(BF)
        scales_ref[rows, 1:2] = scale


def enc_ffn(x, att, w):
    rows, width = x.shape
    hidden = w["ffn_in"].shape[1]
    steps = hidden // wide
    weights = [w["out"], w["ffn_in"], w["ffn_out"], w["down"], w["up"]]
    return pl.pallas_call(
        enc_ffn_kernel,
        grid=(1,),
        in_specs=[
            single((rows, width)),
            single((rows, width)),
            single((2, width)),
            single((1, chunk)),
            single((1, width)),
        ]
        + [pl.BlockSpec(memory_space=pl.ANY)] * len(weights),
        out_specs=[
            single((rows, width)),
            single((rows, hidden)),
            single((rows, chunk)),
            single((rows, chunk)),
            single((rows, width)),
            single((rows, LANES)),
        ],
        out_shape=[
            jax.ShapeDtypeStruct((rows, width), BF),
            jax.ShapeDtypeStruct((rows, hidden), BF),
            jax.ShapeDtypeStruct((rows, chunk), BF),
            jax.ShapeDtypeStruct((rows, chunk), BF),
            jax.ShapeDtypeStruct((rows, width), BF),
            jax.ShapeDtypeStruct((rows, LANES), F32),
        ],
        scratch_shapes=[pltpu.VMEM((rows, width), F32)] + weight_scratch(weights, steps),
        compiler_params=params(),
        name="enc_ffn",
    )(x, att, w["gains"], w["down_bias"], w["up_bias"], *weights)


def ffn_back_step(grad_ref, acc_ref, in_ref, out_ref, slope_ref):
    for start, size in row_tiles(grad_ref.shape[0]):
        rows = slice(start, start + size)
        pre = (nt(grad_ref[rows], out_ref[...]) * slope_ref[rows].astype(F32)).astype(BF)
        acc_ref[rows] += nt(pre, in_ref[...])


def adapter_back(grad_ref, acc_ref, low_ref, act_ref, slope_ref, down_ref, up_ref, outs, pre_ref):
    ddown_ref, ddownb_ref, dup_ref, dupb_ref = outs
    total = None
    for start, size in row_tiles(grad_ref.shape[0]):
        rows = slice(start, start + size)
        back = adapter_scale * nt(grad_ref[rows], up_ref[...])
        pre = (back * slope_ref[rows].astype(F32)).astype(BF)
        pre_ref[rows] = pre
        sums = jnp.sum(pre.astype(F32), axis=0, keepdims=True)
        total = sums if total is None else total + sums
        acc_ref[rows] += nt(pre, down_ref[...])
    ddownb_ref[...] = total
    ddown_ref[...] = tn(low_ref[...], pre_ref[...])
    dup_ref[...] = adapter_scale * tn(act_ref[...], grad_ref[...])
    dupb_ref[...] = adapter_scale * jnp.sum(grad_ref[...].astype(F32), axis=0, keepdims=True)


def enc_ffn_back_kernel(*refs, pieces):
    enc_ffn_back_body(refs[:pieces], *refs[pieces:])


def enc_ffn_back_body(
    dmem_refs, mem_ref, low_ref, scales_ref, gain_ref, slope_ref, pre_slope_ref,
    up_hbm, down_hbm, in_hbm, out_hbm, wo_hbm,
    dfirst_ref, datt_ref, grad_ref, pre_ref,
    acc_ref, up_ref, down_ref, in_ref, out_ref, wo_ref, sems,
):
    weights = Weights(
        {"up": up_hbm, "down": down_hbm, "in": in_hbm, "out": out_hbm, "wo": wo_hbm},
        {"up": up_ref, "down": down_ref, "in": in_ref, "out": out_ref, "wo": wo_ref},
        sems,
    )

    weights.copy("up").start()
    weights.copy("down").start()
    for part in range(in_ref.shape[1] // wide):
        weights.copy("out", part).start()
        weights.copy("in", part).start()
    weights.copy("wo").start()
    weights.wait("up")
    weights.wait("down")
    for start, size in row_tiles(mem_ref.shape[0]):
        rows = slice(start, start + size)
        gain = gain_ref[1:2]
        hat = mem_ref[rows].astype(F32) / gain
        dmem = stacked(dmem_refs, None, start, size).astype(F32)
        grad = norm_rows_back(hat, scales_ref[rows, 1:2], dmem * gain)
        low = grad.astype(BF)
        grad_ref[rows] = low
        back = adapter_scale * nt(low, up_ref[...])
        pre = (back * pre_slope_ref[rows].astype(F32)).astype(BF)
        pre_ref[rows] = pre
        acc_ref[rows] = grad + nt(pre, down_ref[...])

    def one_part(part, carry):
        weights.wait("out", part)
        weights.wait("in", part)
        cols = pl.ds(pl.multiple_of(part * wide, wide), wide)
        ffn_back_step(
            grad_ref, acc_ref, in_ref.at[:, cols], out_ref.at[cols], slope_ref.at[:, cols]
        )
        return carry

    lax.fori_loop(0, in_ref.shape[1] // wide, one_part, 0)

    weights.wait("wo")
    for start, size in row_tiles(mem_ref.shape[0]):
        rows = slice(start, start + size)
        gain = gain_ref[0:1]
        hat = low_ref[rows].astype(F32) / gain
        grad = norm_rows_back(hat, scales_ref[rows, 0:1], acc_ref[rows] * gain)
        dfirst_ref[rows] = grad
        datt_ref[rows] = nt(grad.astype(BF), wo_ref[...]).astype(BF)


def enc_ffn_back(dmems, saved, w):
    mem, slope, pre_slope, act, low, scales = saved
    rows, width = mem.shape
    hidden = w["ffn_in"].shape[1]
    steps = hidden // wide
    weights = [w["up"], w["down"], w["ffn_in"], w["ffn_out"], w["out"]]
    return pl.pallas_call(
        functools.partial(enc_ffn_back_kernel, pieces=len(dmems)),
        grid=(1,),
        in_specs=[single(d.shape) for d in dmems]
        + [
            single((rows, width)),
            single((rows, width)),
            single((rows, LANES)),
            single((2, width)),
            single((rows, hidden)),
            single((rows, chunk)),
        ]
        + [pl.BlockSpec(memory_space=pl.ANY)] * len(weights),
        out_specs=[
            single((rows, width)),
            single((rows, width)),
            single((rows, width)),
            single((rows, chunk)),
        ],
        out_shape=[
            jax.ShapeDtypeStruct((rows, width), F32),
            jax.ShapeDtypeStruct((rows, width), BF),
            jax.ShapeDtypeStruct((rows, width), BF),
            jax.ShapeDtypeStruct((rows, chunk), BF),
        ],
        scratch_shapes=[pltpu.VMEM((rows, width), F32)] + weight_scratch(weights, steps),
        compiler_params=params(),
        name="enc_ffn_back",
    )(*dmems, mem, low, scales, w["gains"], slope, pre_slope, *weights)


def dec_mid_kernel(x_ref, att_ref, wo_ref, gain_ref, wq_ref, n_ref, scale_ref, *cq_refs):
    for (start, size), cq_ref in zip(row_tiles(x_ref.shape[0], TGT), cq_refs):
        rows = slice(start, start + size)
        first = x_ref[rows].astype(F32) + nn(att_ref[rows], wo_ref[...])
        hat, scale = norm_rows(first)
        normed = hat * gain_ref[0:1]
        n_ref[rows] = normed
        scale_ref[rows, 0:1] = scale
        cq_ref[...] = nn(normed.astype(BF), wq_ref[...]).astype(BF)


def dec_mid(x, att, w, cross):
    rows, width = x.shape
    return pl.pallas_call(
        dec_mid_kernel,
        out_shape=[
            jax.ShapeDtypeStruct((rows, width), F32),
            jax.ShapeDtypeStruct((rows, LANES), F32),
        ]
        + [jax.ShapeDtypeStruct((TGT, width), BF)] * (rows // TGT),
        compiler_params=params(),
        name="dec_mid",
    )(x, att, w["out"], w["gains"], cross["query"])


def dec_ffn_kernel(
    len_ref, n_ref, catt_ref, cot_ref, cgain_ref, gain_ref, downb_ref, upb_ref,
    wco_hbm, in_hbm, out_hbm, down_hbm, up_hbm,
    y_ref, dsecond_ref, dcatt_ref, ddown_ref, ddownb_ref, dup_ref, dupb_ref,
    acc_ref, low_ref, grad_ref, slope_ref, pre_slope_ref, act_ref, pre_ref, scale_ref,
    wco_ref, in_ref, out_ref, down_ref, up_ref, sems,
    *, steps, which,
):
    weights = Weights(
        {"wco": wco_hbm, "in": in_hbm, "out": out_hbm, "down": down_hbm, "up": up_hbm},
        {"wco": wco_ref, "in": in_ref, "out": out_ref, "down": down_ref, "up": up_ref},
        sems,
    )

    weights.copy("wco").start()
    for part in range(steps):
        weights.copy("in", part).start()
        weights.copy("out", part).start()
    weights.copy("down").start()
    weights.copy("up").start()
    weights.wait("wco")
    second = n_ref[...] + nn(catt_ref[...], wco_ref[...])
    hat, scale = norm_rows(second)
    middle = hat * cgain_ref[...]
    acc_ref[...] = middle
    low_ref[...] = middle.astype(BF)
    scale_ref[:, 0:1] = scale

    def forward(part, carry):
        weights.wait("in", part)
        weights.wait("out", part)
        ffn_step(
            low_ref, acc_ref, weights.part("in", part), weights.part("out", part),
            slope_ref.at[part], None, None, None,
        )
        return carry

    lax.fori_loop(0, steps, forward, 0)

    weights.wait("down")
    weights.wait("up")
    ffn_step(
        low_ref, acc_ref, down_ref, up_ref, pre_slope_ref, act_ref, downb_ref, adapter_scale
    )
    gain = gain_ref[1:2]
    hat, scale = norm_rows(acc_ref[...] + adapter_scale * upb_ref[...])
    row = lax.broadcasted_iota(jnp.int32, (low_ref.shape[0], 1), 0)
    valid = row < len_ref[0, which]
    y_ref[...] = jnp.where(valid, hat * gain, 0.0).astype(BF)
    cot = jnp.where(valid, cot_ref[...].astype(F32), 0.0)
    grad = norm_rows_back(hat, scale, cot * gain)
    acc_ref[...] = grad
    grad_ref[...] = grad.astype(BF)
    adapter_back(
        grad_ref, acc_ref, low_ref, act_ref, pre_slope_ref, down_ref, up_ref,
        (ddown_ref, ddownb_ref, dup_ref, dupb_ref), pre_ref,
    )

    def backward(part, carry):
        ffn_back_step(
            grad_ref, acc_ref, weights.part("in", part), weights.part("out", part),
            slope_ref.at[part],
        )
        return carry

    lax.fori_loop(0, steps, backward, 0)

    gain = cgain_ref[...]
    hat = low_ref[...].astype(F32) / gain
    grad = norm_rows_back(hat, scale_ref[:, 0:1], acc_ref[...] * gain)
    dsecond_ref[...] = grad
    dcatt_ref[...] = nt(grad.astype(BF), wco_ref[...]).astype(BF)


def dec_ffn(lengths, n, catt, cot, w, cross, which):
    rows, width = catt.shape
    hidden = w["ffn_in"].shape[1]
    steps = hidden // wide
    weights = [cross["out"], w["ffn_in"], w["ffn_out"], w["down"], w["up"]]
    return pl.pallas_call(
        functools.partial(dec_ffn_kernel, steps=steps, which=which),
        grid=(1,),
        in_specs=[
            pl.BlockSpec(memory_space=pltpu.SMEM),
            pl.BlockSpec((rows, width), lambda i: (which, 0)),
            whole((rows, width)),
            pl.BlockSpec((rows, width), lambda i: (which, 0)),
            whole((1, width)),
            whole((2, width)),
            whole((1, chunk)),
            whole((1, width)),
        ]
        + [pl.BlockSpec(memory_space=pl.ANY)] * len(weights),
        out_specs=[
            whole((rows, width)),
            whole((rows, width)),
            whole((rows, width)),
            whole((width, chunk)),
            whole((1, chunk)),
            whole((chunk, width)),
            whole((1, width)),
        ],
        out_shape=[
            jax.ShapeDtypeStruct((rows, width), BF),
            jax.ShapeDtypeStruct((rows, width), F32),
            jax.ShapeDtypeStruct((rows, width), BF),
            jax.ShapeDtypeStruct((width, chunk), F32),
            jax.ShapeDtypeStruct((1, chunk), F32),
            jax.ShapeDtypeStruct((chunk, width), F32),
            jax.ShapeDtypeStruct((1, width), F32),
        ],
        scratch_shapes=[
            pltpu.VMEM((rows, width), F32),
            pltpu.VMEM((rows, width), BF),
            pltpu.VMEM((rows, width), BF),
            pltpu.VMEM((steps, rows, wide), BF),
            pltpu.VMEM((rows, chunk), BF),
            pltpu.VMEM((rows, chunk), BF),
            pltpu.VMEM((rows, chunk), BF),
            pltpu.VMEM((rows, LANES), F32),
        ]
        + weight_scratch(weights, steps),
        compiler_params=params(),
        name="dec_ffn",
    )(
        lengths, n, catt, cot, cross["gain"], w["gains"], w["down_bias"], w["up_bias"], *weights
    )


def dec_mid_back_kernel(
    dsecond0_ref, dsecond1_ref, dcq0_ref, dcq1_ref, wq_ref, n_ref, scale_ref, gain_ref, wo_ref,
    dfirst_ref, datt_ref,
):
    for pair, (dsecond_ref, dcq_ref) in enumerate(
        ((dsecond0_ref, dcq0_ref), (dsecond1_ref, dcq1_ref))
    ):
        rows = slice(pair * TGT, (pair + 1) * TGT)
        gain = gain_ref[0:1]
        total = dsecond_ref[...] + nt(dcq_ref[...], wq_ref[...])
        grad = norm_rows_back(n_ref[rows] / gain, scale_ref[rows, 0:1], total * gain)
        dfirst_ref[rows] = grad
        datt_ref[rows] = nt(grad.astype(BF), wo_ref[...]).astype(BF)


def dec_mid_back(dseconds, dcqs, n, scale, w, cross):
    rows, width = n.shape
    return pl.pallas_call(
        dec_mid_back_kernel,
        out_shape=[
            jax.ShapeDtypeStruct((rows, width), F32),
            jax.ShapeDtypeStruct((rows, width), BF),
        ],
        compiler_params=params(),
        name="dec_mid_back",
    )(*dseconds, *dcqs, cross["query"], n, scale, w["gains"], w["out"])


enc_segs = ((0, SRC_LONG, 0, SRC_LONG), (SRC_LONG, SRC_SHORT, SRC_LONG, SRC_SHORT))
dec_segs = ((0, TGT, 0, TGT), (TGT, TGT, TGT, TGT))
cross_segs = (((0, TGT, 0, SRC_LONG),), ((0, TGT, 0, SRC_SHORT),))


def self_columns(qkv):
    rows = qkv.shape[0]
    return (qkv, rows, 0, 0), [(qkv, rows, 0, 8)], [(qkv, rows, 0, 16)]


def cross_columns(cq, kv, which):
    keys = (SRC_LONG, SRC_SHORT)[which]
    return (cq, TGT, 0, 0), [(kv, keys, 0, 0)], [(kv, keys, 0, 8)]


def decoder_self(t, lengths, w, cross):
    qkv = product(t, w["qkv"])
    att, inv, *weights = attend(lengths, *self_columns(qkv), w["prefix"], dec_segs, True, group=2)
    n, scale, *cq = dec_mid(t, att, w, cross)
    return cq, (qkv, att, inv, weights, n, scale)


def cross_forward(lengths, cq, kv, which):
    return attend(
        lengths, *cross_columns(cq, kv, which), None, cross_segs[which], False, which,
        group=(2, 4)[which],
    )


def cross_backward(cq, kv, forward, dcatt, which):
    catt, inv, *weights = forward
    return attend_back(
        *cross_columns(cq, kv, which), None, catt, inv, dcatt, weights, cross_segs[which]
    )


def decoder_self_back(kept, dseconds, dcqs, w, cross):
    qkv, att, inv, weights, n, scale = kept
    dfirst, datt = dec_mid_back(dseconds, dcqs, n, scale, w, cross)
    dq, dk, dv, *dprefix = attend_back(
        *self_columns(qkv), w["prefix"], att, inv, datt, weights, dec_segs, group=1
    )
    return back_product([dq, dk, dv], w["qkv"], dfirst)[0], dprefix


def small_shape(devices):
    return 8, 8 * (2 * chunk) // devices


def finish_kernel(
    q_ref, k_ref, v_ref, o_ref, inv_ref, g0_ref, g1_ref, g2_ref, pk_ref, pv_ref, pl_ref, ps_ref,
    dfirst0_ref, dfirst1_ref, dfirst2_ref, wqkv_ref,
    low_all, act_all, grad_all, pre_all,
    long_down, long_downb, long_up, long_upb,
    short_down, short_downb, short_up, short_upb, dpk_ref, dpv_ref,
    y0_hbm, y1_hbm, dt_hbm,
    source_ref, y_ref, target_ref, o_up_ref, o_down_ref, o_prefix_ref, o_upb_ref, o_downb_ref,
    dq, dk, dv, small, y0_ref, y1_ref, dt_ref, lows_all, acts_all, grads_all, pres_all, ups, downs, mine, theirs, half_sum, across_y, y_sum, landed, total, result,
    small_landed, small_total, small_result, dx, dx_landed, lows, lows_landed,
    load_sems, pair_sems, y_sems, z_sems, gather_sems, share_y_sems, back_sems,
    small_sems, share_sems, cross_sems,
    *, devices,
):
    step = pl.program_id(0)
    pairs = 8
    section = lax.axis_index("section")
    is_encoder = section == 0
    chips = devices // 2
    line = chips // 2
    slices = 16 // line
    rows = 2 * chunk
    half = rows // 2
    size = half // slices
    side = size // 2
    part = side // line
    place = lax.axis_index("dp")
    core, chip = lax.rem(place, 2), place // 2
    bit, at_line = lax.rem(chip, 2), chip // 2
    partner = place + 1 - 2 * core
    beside = place + 2 - 4 * bit
    small_rows, small_cols = small_shape(devices)
    tile = 256
    width = 2 * chunk
    scale = 1.0 / devices

    def aligned(value, unit=16):
        return pl.multiple_of(value, unit)

    def along(distance):
        return (lax.rem(at_line + distance, line) * 2 + bit) * 2 + core

    def remote(source, target, send_sem, recv_sem, other):
        return pltpu.make_async_remote_copy(
            src_ref=source, dst_ref=target, send_sem=send_sem, recv_sem=recv_sem,
            device_id=other, device_id_type=pl.DeviceIdType.MESH,
        )

    def in_group(other):
        return {"dp": other}

    across = {"section": 1 - section}
    kept = aligned(core * half)
    given = aligned((1 - core) * half)

    def swap():
        return remote(
            mine.at[pl.ds(given, half)], theirs, pair_sems.at[0], pair_sems.at[1],
            in_group(partner),
        )

    def y_send(j):
        there = pl.ds(aligned(j * size + (1 - bit) * side), side)
        return remote(
            half_sum.at[there], across_y.at[j], y_sems.at[0, j], y_sems.at[1, j], in_group(beside)
        )

    def z_send(j, s):
        there = pl.ds(aligned(lax.rem(at_line + s, line) * part), part)
        return remote(
            y_sum.at[j].at[there], landed.at[j, s - 1],
            z_sems.at[0, j, s - 1], z_sems.at[1, j, s - 1], in_group(along(s)),
        )

    def own_rows(j):
        return pl.ds(aligned(kept + j * size + bit * side + at_line * part), part)

    def own_side(j):
        return pl.ds(aligned(kept + j * size + bit * side), side)

    def other_side(j):
        return pl.ds(aligned(kept + j * size + (1 - bit) * side), side)

    def gather(j, s):
        return remote(
            total.at[j], result.at[own_rows(j)],
            gather_sems.at[0, j, s - 1], gather_sems.at[1, j, s - 1], in_group(along(s)),
        )

    def y_share(j):
        return remote(
            result.at[own_side(j)], result.at[own_side(j)],
            share_y_sems.at[0, j], share_y_sems.at[1, j], in_group(beside),
        )

    def back(j, i):
        there = own_side(j) if i == 0 else other_side(j)
        return remote(
            result.at[there], result.at[there],
            back_sems.at[0, j, i], back_sems.at[1, j, i], in_group(partner),
        )

    def piece(index):
        row = aligned(lax.rem(index, 8) * small_rows, 8)
        col = aligned((index // 8) * small_cols, LANES)
        return pl.ds(row, small_rows), pl.ds(col, small_cols)

    def small_out(s):
        return remote(
            small.at[piece(lax.rem(place + s, devices))], small_landed.at[s - 1],
            small_sems.at[0, s - 1], small_sems.at[1, s - 1],
            in_group(lax.rem(place + s, devices)),
        )

    def small_share(s):
        return remote(
            small_total, small_result.at[piece(place)],
            share_sems.at[0, s - 1], share_sems.at[1, s - 1],
            in_group(lax.rem(place + s, devices)),
        )

    def send_low():
        return remote(lows, lows_landed, cross_sems.at[0, 0], cross_sems.at[1, 0], across)

    def send_high(i):
        return remote(
            dx.at[i], dx_landed.at[i], cross_sems.at[0, 1 + i], cross_sems.at[1, 1 + i], across
        )

    def greet(barrier, other):
        pl.semaphore_signal(
            barrier, inc=1, device_id=other, device_id_type=pl.DeviceIdType.MESH
        )

    def load(source, target, i):
        return pltpu.make_async_copy(source, target, load_sems.at[i])

    enc_loads = [
        load(low_all, lows_all, 0), load(act_all, acts_all, 1),
        load(grad_all, grads_all, 2), load(pre_all, pres_all, 3),
    ]
    dec_loads = [
        load(long_up, ups.at[0], 0), load(long_down, downs.at[0], 1),
        load(short_up, ups.at[1], 2), load(short_down, downs.at[1], 3),
        load(y0_hbm, y0_ref, 4), load(y1_hbm, y1_ref, 5), load(dt_hbm, dt_ref, 6),
    ]

    @pl.when(step == 0)
    def _():
        barrier = pltpu.get_barrier_semaphore()
        for s in range(1, devices):
            greet(barrier, in_group(lax.rem(place + s, devices)))

        @pl.when(is_encoder)
        def _():
            for copy in enc_loads:
                copy.start()

        @pl.when(jnp.logical_not(is_encoder))
        def _():
            for copy in dec_loads:
                copy.start()

    @pl.when(is_encoder & (step < pairs))
    def _():
        at = aligned(step * LANES, LANES)
        lanes = pl.ds(at, LANES)
        prefix_totals = attend_back_pair(
            q_ref, [k_ref], [v_ref], o_ref, inv_ref, [g0_ref, g1_ref, g2_ref], pk_ref, pv_ref,
            (pl_ref, ps_ref), dq.at[:, lanes], dk.at[:, lanes], dv.at[:, lanes], enc_segs,
        )
        small[0:PRE_PAD, lanes] = prefix_totals[0] * scale
        small[PRE_PAD : 2 * PRE_PAD, lanes] = prefix_totals[1] * scale

    @pl.when(step == 0)
    def _():
        barrier = pltpu.get_barrier_semaphore()

        def pack(up, down):
            mine[0:chunk] = (up * scale).astype(BF)
            down = (down * scale).astype(BF)
            mine[chunk:width, 0:chunk] = down[0:chunk]
            mine[chunk:width, chunk:width] = down[chunk:width]

        @pl.when(is_encoder)
        def _():
            for copy in enc_loads:
                copy.wait()
            pack(
                adapter_scale * tn(acts_all[...], grads_all[...]),
                tn(lows_all[...], pres_all[...]),
            )
            pl.semaphore_wait(barrier, devices - 1)
            greet(barrier, across)

        @pl.when(jnp.logical_not(is_encoder))
        def _():
            for copy in dec_loads:
                copy.wait()
            pack(ups[0] + ups[1], downs[0] + downs[1])
            pl.semaphore_wait(barrier, devices)
            greet(barrier, across)

        swap().start()

        @pl.when(jnp.logical_not(is_encoder))
        def _():
            low = width // 2
            lows[0, 0:TGT] = y0_ref[:, 0:low]
            lows[0, TGT : 2 * TGT] = y1_ref[:, 0:low]
            lows[1] = dt_ref[:, 0:low]
            send_low().start()
            small[0:PRE_PAD] = dpk_ref[...] * scale
            small[PRE_PAD : 2 * PRE_PAD] = dpv_ref[...] * scale

    @pl.when(step == 1)
    def _():
        swap().wait()
        half_sum[...] = (
            mine[pl.ds(kept, half)].astype(F32) + theirs[...].astype(F32)
        ).astype(BF)
        for j in range(min(2, slices)):
            y_send(j).start()

    for j in range(slices):

        @pl.when(step == 2 + j)
        def _(j=j):
            y_send(j).wait()
            if j + 2 < slices:
                y_send(j + 2).start()
            own = pl.ds(aligned(j * size + bit * side), side)
            y_sum[j] = (half_sum[own].astype(F32) + across_y[j].astype(F32)).astype(BF)
            for s in range(1, line):
                z_send(j, s).start()

        @pl.when(step == 4 + j)
        def _(j=j):
            summed = y_sum[j, pl.ds(aligned(at_line * part), part)].astype(F32)
            for s in range(1, line):
                z_send(j, s).wait()
                summed = summed + landed[j, s - 1].astype(F32)
            total[j] = summed.astype(BF)
            result[own_rows(j)] = total[j]
            for s in range(1, line):
                gather(j, s).start()

        @pl.when(step == 6 + j)
        def _(j=j):
            for s in range(1, line):
                gather(j, s).wait()
            y_share(j).start()
            back(j, 0).start()

        @pl.when(step == 8 + j)
        def _(j=j):
            y_share(j).wait()
            back(j, 1).start()

    @pl.when(step == pairs - 1)
    def _():
        @pl.when(is_encoder)
        def _():
            up_row = jnp.sum(grads_all[...].astype(F32), axis=0, keepdims=True)
            down_row = jnp.sum(pres_all[...].astype(F32), axis=0, keepdims=True)
            down_row = jnp.concatenate([down_row, jnp.zeros_like(down_row)], 1)
            small[PRE : PRE + 1] = up_row * (adapter_scale * scale)
            small[PRE + 1 : PRE + 2] = down_row * scale

        @pl.when(jnp.logical_not(is_encoder))
        def _():
            down_row = long_downb[...] + short_downb[...]
            down_row = jnp.concatenate([down_row, jnp.zeros_like(down_row)], 1)
            small[PRE : PRE + 1] = (long_upb[...] + short_upb[...]) * scale
            small[PRE + 1 : PRE + 2] = down_row * scale

        for s in range(1, devices):
            small_out(s).start()

    @pl.when(is_encoder & (step == pairs))
    def _():
        pl.semaphore_wait(pltpu.get_barrier_semaphore(), 1)

    @pl.when(is_encoder & (step >= pairs))
    def _():
        acc = jnp.concatenate([dfirst0_ref[...], dfirst1_ref[...], dfirst2_ref[...]], 0)
        for n, grad in enumerate((dq, dk, dv)):
            acc = acc + nt(grad[...], wqkv_ref[:, n * width : (n + 1) * width])
        dx[step - pairs] = acc.astype(BF)

    for i in range(2):

        @pl.when(is_encoder & (step == pairs + i))
        def _(i=i):
            send_high(i).start()

    @pl.when(step == pairs + 1)
    def _():
        own_rows_, own_cols = piece(place)
        summed = small[own_rows_, own_cols]
        for s in range(1, devices):
            small_out(s).wait()
            summed = summed + small_landed[s - 1]
        small_total[...] = summed
        small_result[own_rows_, own_cols] = summed
        for s in range(1, devices):
            small_share(s).start()

    @pl.when(step == pairs + 3)
    def _():
        for j in range(slices):
            for i in range(2):
                back(j, i).wait()
        o_up_ref[...] = result[0:chunk]
        o_down_ref[0:chunk] = result[chunk:width, 0:chunk]
        o_down_ref[chunk:width] = result[chunk:width, chunk:width]
        for s in range(1, devices):
            small_share(s).wait()
        o_prefix_ref[:, 0] = small_result[0:PRE]
        o_prefix_ref[:, 1] = small_result[PRE_PAD : PRE_PAD + PRE]
        o_upb_ref[...] = small_result[PRE : PRE + 1]
        o_downb_ref[...] = small_result[PRE + 1 : PRE + 2, 0:chunk]

        @pl.when(is_encoder)
        def _():
            for i in range(2):
                source_ref[:, i * tile : (i + 1) * tile] = dx[2 + i]
            send_low().wait_recv()
            y_ref[...] = lows_landed[0]
            target_ref[...] = lows_landed[1]
            for i in range(2):
                send_high(i).wait_send()

        @pl.when(jnp.logical_not(is_encoder))
        def _():
            low = width // 2
            y_ref[0:TGT] = y0_ref[:, low:width]
            y_ref[TGT : 2 * TGT] = y1_ref[:, low:width]
            target_ref[...] = dt_ref[:, low:width]
            send_low().wait_send()
            for i in range(2):
                send_high(i).wait_recv()
                source_ref[:, i * tile : (i + 1) * tile] = dx_landed[i]


def finish(saved, datt, dfirst, w, traces, adapters, dec_prefix, ys, dt):
    qkv, att, inv, weights = saved
    devices = lax.axis_size("dp")
    line = devices // 4
    slices = 16 // line
    rows, width = att.shape
    targets = dt.shape[0]
    pairs, tile = 8, 256
    half = width // 2
    side = half // slices // 2
    part = side // line
    small_rows, small_cols = small_shape(devices)

    def mine(value):
        return jnp.where(lax.axis_index("section") == 0, value, 0)

    def head(i):
        return mine(jnp.minimum(i, pairs - 1))

    def pair(offset):
        return pl.BlockSpec((rows, LANES), lambda i: (0, head(i) + offset))

    def at(i):
        return mine(jnp.where(i < pairs + 2, 2 + jnp.maximum(i - pairs, 0), i - pairs - 2))

    def once(shape):
        return pl.BlockSpec(shape, lambda i: (0,) * len(shape), pipeline_mode=pl.Buffered(1))

    anywhere = pl.BlockSpec(memory_space=pl.ANY)
    prefix_pair = pl.BlockSpec((PRE_PAD, LANES), lambda i: (0, head(i)))
    vmem = pltpu.VMEM
    dma = pltpu.SemaphoreType.DMA
    flat = [*traces] + [a for group in adapters for a in group]
    return pl.pallas_call(
        functools.partial(finish_kernel, devices=devices),
        grid=(pairs + 4,),
        in_specs=[pair(0), pair(8), pair(16), pair(0), pair(0)]
        + [pl.BlockSpec((ENC_ROWS, LANES), lambda i, n=n: (n, head(i))) for n in range(3)]
        + [prefix_pair] * 2
        + [
            pl.BlockSpec((2,) + p.shape[1:], lambda i: (head(i), 0, 0))
            for p in weights
        ]
        + [pl.BlockSpec((ENC_ROWS, tile), lambda i, n=n: (n, at(i))) for n in range(3)]
        + [
            pl.BlockSpec((tile, 3 * width), lambda i: (at(i), 0)),
        ]
        + [anywhere if a.shape[0] > 1 else once(a.shape) for a in flat]
        + [once(a.shape) for a in dec_prefix]
        + [anywhere] * 3,
        out_specs=[
            once((rows, half)), once((targets, half)), once((targets, half)),
            once((chunk, width)), once((width, chunk)),
            once((PRE, 2, width)), once((1, width)), once((1, chunk)),
        ],
        out_shape=[
            jax.ShapeDtypeStruct((rows, half), BF),
            jax.ShapeDtypeStruct((targets, half), BF),
            jax.ShapeDtypeStruct((targets, half), BF),
            jax.ShapeDtypeStruct((chunk, width), BF),
            jax.ShapeDtypeStruct((width, chunk), BF),
            jax.ShapeDtypeStruct((PRE, 2, width), F32),
            jax.ShapeDtypeStruct((1, width), F32),
            jax.ShapeDtypeStruct((1, chunk), F32),
        ],
        scratch_shapes=[
            vmem((rows, width), BF), vmem((rows, width), BF), vmem((rows, width), BF),
            vmem((2 * PRE_PAD, width), F32),
            vmem((TGT, width), BF), vmem((TGT, width), BF), vmem((targets, width), BF),
            vmem((rows, width), BF), vmem((rows, chunk), BF),
            vmem((rows, width), BF), vmem((rows, chunk), BF),
            vmem((2, chunk, width), F32), vmem((2, width, chunk), F32),
            vmem((width, width), BF), vmem((half, width), BF), vmem((half, width), BF),
            vmem((slices, side, width), BF), vmem((slices, side, width), BF),
            vmem((slices, line - 1, part, width), BF), vmem((slices, part, width), BF),
            vmem((width, width), BF),
            vmem((devices - 1, small_rows, small_cols), F32), vmem((small_rows, small_cols), F32),
            vmem((2 * PRE_PAD, width), F32),
            vmem((4, rows, tile), BF), vmem((2, rows, tile), BF),
            vmem((2, targets, half), BF), vmem((2, targets, half), BF),
            dma((7,)), dma((2,)), dma((2, slices)), dma((2, slices, line - 1)),
            dma((2, slices, line - 1)), dma((2, slices)), dma((2, slices, 2)),
            dma((2, devices - 1)), dma((2, devices - 1)), dma((2, 3)),
        ],
        compiler_params=pltpu.CompilerParams(
            vmem_limit_bytes=60 * 2**20, collective_id=0, has_side_effects=True
        ),
        name="finish",
    )(
        qkv, qkv, qkv, att, inv, datt, datt, datt, *w["prefix"], *weights,
        dfirst, dfirst, dfirst, w["qkv"], *flat, *dec_prefix, *ys, dt,
    )


def blank_kernel(*refs):
    pass


def blanks(shapes):
    return pl.pallas_call(
        blank_kernel,
        out_shape=list(shapes),
        out_specs=[pl.BlockSpec(memory_space=pl.ANY)] * len(shapes),
        name="blank",
    )()


def on_section(is_encoder, encoder_work, decoder_work, *operands):
    enc_shapes, _ = jax.eval_shape(encoder_work, *operands)
    dec_shapes, _ = jax.eval_shape(decoder_work, *operands)

    def blank_like(shapes):
        leaves, tree = jax.tree.flatten(shapes)
        if not leaves:
            return shapes
        return jax.tree.unflatten(tree, blanks(leaves))

    def encoder_branch(*a):
        own, shared = encoder_work(*a)
        return own, blank_like(dec_shapes), shared

    def decoder_branch(*a):
        own, shared = decoder_work(*a)
        return blank_like(enc_shapes), own, shared

    return lax.cond(is_encoder, encoder_branch, decoder_branch, *operands)


def to_decoder(block):
    return lax.ppermute(block, "section", [(0, 1)])


def to_encoder(block):
    return lax.ppermute(block, "section", [(1, 0)])


def per_device(
    sources, targets, cotangent, source_lengths, target_lengths,
    attn_qkv, attn_out, ffn_in, ffn_out, norm_gains, prefix_pairs,
    adapt_down, adapt_down_bias, adapt_up, adapt_up_bias,
    cross_query, cross_pairs, cross_out, cross_gain,
):
    is_encoder = lax.axis_index("section") == 0
    prefix = jnp.pad(prefix_pairs[0], ((0, 0), (0, PRE_PAD - PRE), (0, 0)))
    w = dict(
        qkv=attn_qkv[0], out=attn_out[0], ffn_in=ffn_in[0], ffn_out=ffn_out[0],
        gains=norm_gains[0], prefix=(prefix[0], prefix[1]),
        down=adapt_down[0], down_bias=adapt_down_bias,
        up=adapt_up[0], up_bias=adapt_up_bias,
    )
    cross = dict(query=cross_query, pairs=cross_pairs, out=cross_out, gain=cross_gain[None])

    def at_encoder(work, *operands):
        return on_section(is_encoder, lambda *a: (work(*a), ()), lambda *a: ((), ()), *operands)[0]

    def at_decoder(work, *operands):
        return on_section(is_encoder, lambda *a: ((), ()), lambda *a: (work(*a), ()), *operands)[1]

    def at_both(enc_work, dec_work, *operands):
        return on_section(
            is_encoder, lambda *a: (enc_work(*a), ()), lambda *a: (dec_work(*a), ()), *operands
        )[:2]

    def tie(*arrays):
        return lax.optimization_barrier(arrays)

    def encoder_self():
        qkv = product(sources, w["qkv"])
        att, inv, *weights = attend(
            source_lengths, *self_columns(qkv), w["prefix"], enc_segs, False, checked=True
        )
        return qkv, att, inv, weights

    saved, (cq, kept) = at_both(
        encoder_self, lambda: decoder_self(targets, target_lengths, w, cross)
    )
    long_queries = to_encoder(cq[0])
    short_queries = cq[1]
    part = at_encoder(lambda saved: enc_ffn(sources, saved[1], w), saved)
    mem_short = to_decoder(part[0][SRC_LONG:])

    def encoder_cross(mem, long_queries):
        kv = product(mem, cross["pairs"], rows=SRC_LONG)
        return kv, cross_forward(source_lengths, long_queries, kv, 0)

    long_kv, long = at_encoder(encoder_cross, part[0], long_queries)
    mem_short, catt = tie(mem_short, long[0])
    catt_here = to_decoder(catt)

    def decoder_short(mem_short, cq, kept):
        kv = product(mem_short, cross["pairs"])
        forward = cross_forward(source_lengths, cq, kv, 1)
        return kv, forward, dec_ffn(
            target_lengths, kept[4], forward[0], cotangent, w, cross, 1
        )

    short_kv, short, short_ffn = at_decoder(decoder_short, mem_short, short_queries, kept)
    short_y, short_second, short_dcatt, *short_adapter = short_ffn
    catt_here, short_y = tie(catt_here, short_y)
    long_y, long_second, long_dcatt, *long_adapter = at_decoder(
        lambda catt, kept: dec_ffn(target_lengths, kept[4], catt, cotangent, w, cross, 0),
        catt_here, kept,
    )
    short_dcatt, long_dcatt = tie(short_dcatt, long_dcatt)
    dcatt_here = to_encoder(long_dcatt)

    def decoder_short_back(kv, cq, short, dcatt):
        dcq, dck, dcv = cross_backward(cq, kv, short, dcatt, 1)
        return back_product([dck, dcv], cross["pairs"])[0], dcq

    dmem_short, short_cq = at_decoder(decoder_short_back, short_kv, short_queries, short, short_dcatt)
    dcatt_here, dmem_short = tie(dcatt_here, dmem_short)
    dmem_short = to_encoder(dmem_short)
    long_dcq, dck, dcv = at_encoder(
        lambda queries, kv, long, dcatt: cross_backward(queries, kv, long, dcatt, 0),
        long_queries, long_kv, long, dcatt_here,
    )
    long_cq = to_decoder(long_dcq)

    dmem_long = at_encoder(
        lambda *grads: back_product(grads, cross["pairs"])[0], dck, dcv
    )
    dmem_short, dmem_long = tie(dmem_short, dmem_long)
    dfirst, datt, grad, pre = at_encoder(
        lambda dmem_long, dmem_short, part: enc_ffn_back([dmem_long, dmem_short], part, w),
        dmem_long, dmem_short, part,
    )

    def decoder_end(kept, *grads):
        return decoder_self_back(kept, grads[:2], grads[2:], w, cross)

    long_cq, datt = tie(long_cq, datt)
    dt, dec_prefix = at_decoder(
        decoder_end, kept, long_second, short_second, long_cq, short_cq
    )
    source_grad, y, target_grad, up, down, prefix_grad, up_bias, down_bias = finish(
        saved, datt, dfirst, w, [part[4], part[3], grad, pre],
        [long_adapter, short_adapter], dec_prefix, [long_y, short_y], dt,
    )
    return (
        y,
        source_grad,
        target_grad,
        jnp.swapaxes(prefix_grad, 0, 1)[None],
        down.astype(F32)[None],
        down_bias,
        up.astype(F32)[None],
        up_bias,
    )


def solution(mesh):
    layer2, layer3, rows = P("section", None), P("section", None, None), P("dp", None)
    return jax.shard_map(
        per_device,
        mesh=mesh,
        in_specs=(
            rows, rows, rows, rows, rows,
            layer3, layer3, layer3, layer3, layer3,
            P("section", None, None, None),
            layer3, layer2, layer3, layer2,
            P(), P(), P(), P(),
        ),
        out_specs=(
            P("dp", "section"), P("dp", "section"), P("dp", "section"),
            P("section", None, None, None), layer3, layer2, layer3, layer2,
        ),
        check_vma=False,
    )
```
